32 devices in a mesh: atoms: 8 (over z, x), feat: 4 (over y, core).
Axes of the slice: x: 2, y: 2, z: 4, core: 2. Of those that a mesh axis runs over, the one named last changes fastest.
Arguments:
- features: bfloat16 [256, 8192], P(None, 'atoms'), may hold values from -18 to 18
- vectors: bfloat16 [3, 256, 8192], P(None, None, 'atoms'), may hold values from -18 to 18
- positions: float32 [3, 8192], P(None, 'atoms'), may hold values from -0.3 to 4.65
- atom_mask: int32 [8192], P('atoms'), may hold values from 0 to 1, as said below
- neighbours: int32 [32, 8192], P(None, 'atoms'), may hold values from 0 to 8191, as said below
- ln_gain: float32 [256], replicated, may hold values from 0.5 to 1.5
- ln_bias: float32 [256], replicated, may hold values from -3 to 3
- w_query: bfloat16 [256, 256], P(None, 'feat'), may hold values from -0.375 to 0.375
- w_key: bfloat16 [256, 256], P(None, 'feat'), may hold values from -0.375 to 0.375
- w_value: bfloat16 [3, 256, 256], P(None, None, 'feat'), may hold values from -0.375 to 0.375
- w_vector: bfloat16 [3, 256, 256], P(None, None, 'feat'), may hold values from -0.375 to 0.375
- w_output: bfloat16 [3, 256, 256], P(None, None, 'feat'), may hold values from -0.1875 to 0.1875
- w_key_filter: bfloat16 [64, 256], P(None, 'feat'), may hold values from -4 to 4
- w_value_filter: bfloat16 [3, 64, 256], P(None, None, 'feat'), may hold values from -4 to 4
- cot_features: bfloat16 [256, 8192], P('feat', 'atoms'), may hold values from -6 to 6
- cot_vectors: bfloat16 [3, 256, 8192], P(None, 'feat', 'atoms'), may hold values from -6 to 6
Outputs:
- layer_features: bfloat16 [256, 8192], P('feat', 'atoms')
- layer_vectors: bfloat16 [3, 256, 8192], P(None, 'feat', 'atoms')
- grad_features: float32 [256, 8192], P('feat', 'atoms')
- grad_vectors: float32 [3, 256, 8192], P(None, 'feat', 'atoms')
- grad_positions: float32 [3, 8192], P(None, 'atoms')
- grad_ln_gain: float32 [256], P('feat')
- grad_ln_bias: float32 [256], P('feat')
- grad_w_query: float32 [256, 256], P(None, 'feat')
- grad_w_key: float32 [256, 256], P(None, 'feat')
- grad_w_value: float32 [3, 256, 256], P(None, None, 'feat')
- grad_w_vector: float32 [3, 256, 256], P(None, None, 'feat')
- grad_w_output: float32 [3, 256, 256], P(None, None, 'feat')
- grad_w_key_filter: float32 [64, 256], P(None, 'feat')
- grad_w_value_filter: float32 [3, 64, 256], P(None, None, 'feat')
- stream_rms: float32 [4], replicated
The draws below stay inside these ranges and needn't reach their ends.
Inputs may be any that keep to these rules, and one draw needn't show every extreme that they name: `atom_mask`: atoms come in blocks of 29 consecutive slots, one molecule each; in each block the first slots are real atoms (mask 1) and the rest padding; the last block, and every block that holds atoms of two consecutive runs of 1024 atoms, is all real. `neighbours`: for a real atom, row 0 is the next real atom of its block, cyclically, and the other rows are real atoms of its own block; every row of a padding slot is the slot itself.
All inputs are finite; a program needn't handle non-finite values.
Results may differ from the reference program's by a relative error of at most 0.011.
Values may be sent and summed in bfloat16 or wider, within the bound.
No kernel may reach another device: no remote copies, remote signals or barrier semaphores. Data moves between devices by JAX's collectives and lax.ppermute only.
A program may use at most 64 MiB of HBM per device.

```python
import math
import jax
import jax.numpy as jnp
from jax import lax

H = 256
HEADS = 8
R = 64
NB = 32
MOL = 29
ATOM_DEV = 1024
ATOMS = 8192


def molecule_sizes(key):
    groups = (ATOMS + MOL - 1) // MOL
    group_ids = jnp.arange(groups, dtype=jnp.int32)
    drawn = jax.random.randint(jax.random.fold_in(key, 71), (groups,), 10, MOL + 1)
    starts = group_ids * MOL
    ends = jnp.minimum(starts + MOL - 1, ATOMS - 1)
    straddles = starts // ATOM_DEV != ends // ATOM_DEV
    drawn = jnp.where((group_ids == groups - 1) | straddles, MOL, drawn)
    return jnp.minimum(drawn, ATOMS - starts).astype(jnp.int32)


def rising(length, factor):
    return jnp.exp(math.log(factor) * jnp.arange(length, dtype=jnp.float32) / (length - 1))


def draw_atom_mask(key, part):
    sizes = molecule_sizes(key)
    atom_ids = jnp.arange(ATOMS, dtype=jnp.int32)
    return (atom_ids % MOL < sizes[atom_ids // MOL]).astype(jnp.int32)


def draw_neighbours(key, part):
    sizes = molecule_sizes(key)
    key = jax.random.fold_in(key, 5)
    atom_ids = jnp.arange(ATOMS, dtype=jnp.int32)
    group_ids = atom_ids // MOL
    slot_ids = atom_ids % MOL
    members = sizes[group_ids]
    first_ids = group_ids * MOL
    real_atom = slot_ids < members
    bounded = jnp.maximum(members, 1)
    chained = first_ids + (slot_ids + 1) % bounded
    picked = first_ids[None, :] + jax.random.randint(key, (NB - 1, ATOMS), 0, bounded[None, :])
    table = jnp.concatenate([chained[None, :], picked], axis=0)
    return jnp.where(real_atom[None, :], table, atom_ids[None, :]).astype(jnp.int32)


def draw_features(key, part):
    key = jax.random.fold_in(key, 11)
    values = jnp.clip(jax.random.normal(key, (H, ATOMS), jnp.float32), -6.0, 6.0) * rising(ATOMS, 3.0)[None, :]
    return values.astype(jnp.bfloat16)


def draw_vectors(key, part):
    key = jax.random.fold_in(key, 13)
    values = jnp.clip(jax.random.normal(key, (3, H, ATOMS), jnp.float32), -6.0, 6.0) * rising(ATOMS, 3.0)[None, None, :]
    return values.astype(jnp.bfloat16)


def draw_positions(key, part):
    key = jax.random.fold_in(key, 17)
    slot_ids = jnp.arange(ATOMS, dtype=jnp.int32) % MOL
    lattice = jnp.stack([slot_ids % 3, slot_ids // 3 % 3, slot_ids // 9]).astype(jnp.float32) * 1.45
    jitter = jax.random.uniform(key, (3, ATOMS), jnp.float32, -0.3, 0.3)
    return lattice + jitter


def block_scale(key, shape, cuts, low, high):
    level, own = 1.0, jax.random.fold_in(key, 6)
    for position, parts in cuts:
        heights = jnp.exp(jax.random.uniform(jax.random.fold_in(own, position), (parts,), jnp.float32, low / len(cuts), high / len(cuts)))
        level = level * jnp.repeat(heights, shape[position] // parts).reshape([-1 if axis == position else 1 for axis in range(len(shape))])
    return level


def scatter_about(stream_key, shape, deviation, limit, split=(), kind=jnp.bfloat16):
    values = jax.random.normal(stream_key, shape, jnp.float32) * deviation
    if len(split) > 0:
        values = block_scale(stream_key, shape, split, -0.22, 0.18) * values
    return jnp.clip(values, min=-limit, max=limit).astype(kind)


def setup_inputs(seed: int = 0) -> dict:
    key_list = jax.random.split(jax.random.key(seed), 17)
    return {
        "features": draw_features(jax.random.fold_in(key_list[16], 71), 0),
        "vectors": draw_vectors(jax.random.fold_in(key_list[16], 71), 0),
        "positions": draw_positions(jax.random.fold_in(key_list[16], 71), 0),
        "atom_mask": draw_atom_mask(jax.random.fold_in(key_list[16], 71), 0),
        "neighbours": draw_neighbours(jax.random.fold_in(key_list[16], 71), 0),
        "ln_gain": jnp.clip(1.0 + 0.1 * jax.random.normal(key_list[5], (H,), jnp.float32), 0.5, 1.5),
        "ln_bias": scatter_about(key_list[6], (H,), 0.5, 3.0, (), jnp.float32),
        "w_query": scatter_about(key_list[7], (H, H), H ** -0.5, 0.375, ((1, 4),)),
        "w_key": scatter_about(key_list[8], (H, H), H ** -0.5, 0.375, ((1, 4),)),
        "w_value": scatter_about(key_list[9], (3, H, H), H ** -0.5, 0.375, ((2, 4),)),
        "w_vector": scatter_about(key_list[10], (3, H, H), H ** -0.5, 0.375, ((2, 4),)),
        "w_output": scatter_about(key_list[11], (3, H, H), (4 * H) ** -0.5, 0.1875, ((2, 4),)),
        "w_key_filter": scatter_about(key_list[12], (R, H), 0.7, 4.0, ((1, 4),)),
        "w_value_filter": scatter_about(key_list[13], (3, R, H), 0.7, 4.0, ((2, 4),)),
        "cot_features": scatter_about(key_list[14], (H, ATOMS), 1.0, 6.0, ((0, 4), (1, 8))),
        "cot_vectors": scatter_about(key_list[15], (3, H, ATOMS), 1.0, 6.0, ((1, 4), (2, 8))),
    }


CUTOFF = 5.0
EPSILON = 1e-05
PRECISE = lax.Precision.HIGHEST

@jax.custom_vjp
def low(v):
    return lax.optimization_barrier(v.astype(jnp.bfloat16)).astype(jnp.float32)

@jax.custom_vjp
def low_back(v):
    return v

def low_keep(v):
    return (low(v), None)

def low_pass(kept, grad):
    return (grad,)

def back_keep(v):
    return (v, None)

def back_low(kept, grad):
    return (low(grad),)
low.defvjp(low_keep, low_pass)
low_back.defvjp(back_keep, back_low)

def radial_basis(distance):
    centers = jnp.linspace(0.0, CUTOFF, R).astype(distance.dtype)
    spacing = CUTOFF / (R - 1)
    shaped = centers.reshape((R,) + (1,) * distance.ndim)
    scaled = (distance[None] - shaped) / spacing
    return jnp.exp(-0.5 * scaled * scaled)

def edge_terms(queries, key_rows, value_rows, vector_rows, dest_pos, source_pos, edge_ok, key_filter_w, value_filter_w):
    offsets = dest_pos[:, None, :] - source_pos
    distance = jnp.sqrt(jnp.maximum(lax.optimization_barrier(jnp.sum(offsets * offsets, axis=0)), 0.01))
    direction = offsets / distance[None]
    envelope = jnp.where(distance < CUTOFF, 0.5 * (jnp.cos(math.pi * distance / CUTOFF) + 1.0), 0.0) * edge_ok
    expanded = radial_basis(distance) * envelope[None]
    key_filter = jax.nn.silu(jnp.einsum('rc,rnb->cnb', key_filter_w, expanded, precision=PRECISE))
    value_filter = jax.nn.silu(jnp.einsum('prc,rnb->pcnb', value_filter_w, expanded, precision=PRECISE))
    channels = queries.shape[0]
    head_size = H // HEADS
    heads_here = channels // head_size
    product = queries[:, None, :] * key_rows * key_filter
    scores = lax.optimization_barrier(jnp.sum(product.reshape((heads_here, head_size) + product.shape[1:]), axis=1))
    attention = jax.nn.silu(scores) * envelope[None]
    attention = jnp.broadcast_to(attention[:, None], (heads_here, head_size) + attention.shape[1:]).reshape(product.shape)
    filtered = value_rows * value_filter
    scalar_sum = lax.optimization_barrier(jnp.sum(filtered[0] * attention, axis=1))
    vector_msg = vector_rows * filtered[1][None] + filtered[2][None] * direction[:, None]
    vector_sum = lax.optimization_barrier(jnp.sum(vector_msg, axis=2))
    return (scalar_sum, vector_sum)

def all_edges(queries, key_rows, value_rows, vectors, positions, key_filter_w, value_filter_w, neighbours, edge_ok):

    def one_block(block_id):
        first_row = block_id * ATOM_DEV
        sources = lax.dynamic_slice_in_dim(neighbours, first_row, ATOM_DEV, 1)
        block_ok = lax.dynamic_slice_in_dim(edge_ok, first_row, ATOM_DEV, 1)
        dest_queries = lax.dynamic_slice_in_dim(queries, first_row, ATOM_DEV, 1)
        dest_pos = lax.dynamic_slice_in_dim(positions, first_row, ATOM_DEV, 1)
        return edge_terms(dest_queries, jnp.take(key_rows, sources, axis=1), jnp.take(value_rows, sources, axis=2), jnp.take(vectors, sources, axis=2), dest_pos, jnp.take(positions, sources, axis=1), block_ok, key_filter_w, value_filter_w)
    scalar_blocks, vector_blocks = lax.map(jax.checkpoint(one_block), jnp.arange(ATOMS // ATOM_DEV, dtype=jnp.int32))
    scalar_sum = jnp.moveaxis(scalar_blocks, 0, 1).reshape(H, ATOMS)
    vector_sum = jnp.moveaxis(vector_blocks, 0, 2).reshape(3, H, ATOMS)
    return (scalar_sum, vector_sum)

def reference(features, vectors, positions, atom_mask, neighbours, ln_gain, ln_bias, w_query, w_key, w_value, w_vector, w_output, w_key_filter, w_value_filter, cot_features, cot_vectors):
    dest_ids = jnp.arange(ATOMS, dtype=jnp.int32)
    edge_ok = (atom_mask[None, :] * (neighbours != dest_ids[None, :]).astype(jnp.int32)).astype(jnp.float32)

    def layer_forward(feat_in, vec_in, pos_in, gain_in, bias_in, query_w, key_w, value_w, vector_w, output_w, kfilter_w, vfilter_w):
        mean_row = lax.optimization_barrier(jnp.mean(feat_in, axis=0))
        centred = feat_in - mean_row[None]
        variance = lax.optimization_barrier(jnp.mean(centred * centred, axis=0))
        normed = centred * lax.rsqrt(variance + EPSILON)[None]
        normal_in = low(normed * gain_in[:, None] + bias_in[:, None])
        queries = low_back(jnp.einsum('hc,ha->ca', query_w, normal_in, precision=PRECISE))
        key_rows = low_back(low(jnp.einsum('hc,ha->ca', key_w, normal_in, precision=PRECISE)))
        value_rows = low_back(low(jnp.einsum('phc,ha->pca', value_w, normal_in, precision=PRECISE)))
        projected = low_back(jnp.einsum('phc,dha->pdca', vector_w, vec_in, precision=PRECISE))
        vec_dot = lax.optimization_barrier(jnp.sum(projected[0] * projected[1], axis=0))
        scalar_sum, vector_sum = all_edges(queries, key_rows, value_rows, vec_in, pos_in, kfilter_w, vfilter_w, neighbours, edge_ok)
        gathered = low(scalar_sum)
        outputs = low_back(jnp.einsum('phc,ha->pca', output_w, gathered, precision=PRECISE))
        delta_x = vec_dot * outputs[1] + outputs[2]
        delta_vec = projected[2] * outputs[0][None] + vector_sum
        return ((feat_in + delta_x, vec_in + delta_vec), (delta_x, delta_vec))
    f32 = jnp.float32
    primal, pull_back, extras = jax.vjp(layer_forward, features.astype(f32), vectors.astype(f32), positions.astype(f32), ln_gain.astype(f32), ln_bias.astype(f32), w_query.astype(f32), w_key.astype(f32), w_value.astype(f32), w_vector.astype(f32), w_output.astype(f32), w_key_filter.astype(f32), w_value_filter.astype(f32), has_aux=True)
    new_features, new_vectors = primal
    delta_x, delta_vec = extras
    gradients = pull_back((cot_features.astype(f32), cot_vectors.astype(f32)))
    mask_rows = atom_mask.astype(f32)
    count = jnp.sum(mask_rows) * H
    squares = jnp.stack([jnp.sum(new_features * new_features * mask_rows[None]), jnp.sum(delta_x * delta_x * mask_rows[None]), jnp.sum(new_vectors * new_vectors * mask_rows[None, None]), jnp.sum(delta_vec * delta_vec * mask_rows[None, None])])
    stream_rms = jnp.sqrt(squares / (count * jnp.array([1.0, 1.0, 3.0, 3.0], jnp.float32)) + 1e-06)
    return (new_features.astype(jnp.bfloat16), new_vectors.astype(jnp.bfloat16), gradients[0], gradients[1], gradients[2], gradients[3], gradients[4], gradients[5], gradients[6], gradients[7], gradients[8], gradients[9], gradients[10], gradients[11], stream_rms)
```

```python
import functools
import math

import jax
import jax.numpy as jnp
from jax import lax
from jax.experimental import pallas as pl
from jax.experimental.pallas import tpu as pltpu
from jax.sharding import PartitionSpec as P

H = 256
HEADS = 8
HEAD = H // HEADS
R = 64
MOL = 29
HALO = 32
CUTOFF = 5.0
EPSILON = 1e-05
F32 = jnp.float32
BF16 = jnp.bfloat16

LANE_GROUPS = 2
ROW_GROUPS = 3
SPAN = 5
OFFSETS = 14
STEPS = SPAN + OFFSETS
SUB = 16
LANES = 128


def place(t, group):
    return (t + SPAN * group) % MOL


def spread(source, first, second, start, molecules, rows):
    low = lax.broadcasted_iota(jnp.int32, (molecules, LANES), 1) < R
    for t in range(STEPS):
        for g in range(ROW_GROUPS):
            a = source[pl.ds(start + place(t, 2 * g), molecules, stride=MOL), :]
            b = source[pl.ds(start + place(t, 2 * g + 1), molecules, stride=MOL), :]
            at = t * rows + g * molecules
            first[at : at + molecules] = jnp.where(low, a, pltpu.roll(b, R, 1))
            if second is not None:
                second[at : at + molecules] = jnp.where(low, pltpu.roll(a, R, 1), b)
        at = t * rows + ROW_GROUPS * molecules
        left = rows - ROW_GROUPS * molecules
        if left:
            first[at : at + left] = jnp.zeros((left, LANES), F32)
            if second is not None:
                second[at : at + left] = jnp.zeros((left, LANES), F32)


def collect(first, second, target, start, molecules, rows):
    low = lax.broadcasted_iota(jnp.int32, (molecules, LANES), 1) < R
    target[...] = jnp.zeros(target.shape, F32)
    for t in range(STEPS):
        for g in range(ROW_GROUPS):
            at = t * rows + g * molecules
            a = first[at : at + molecules]
            if second is None:
                c = jnp.where(low, a, 0.0)
                d = jnp.where(low, pltpu.roll(a, R, 1), 0.0)
            else:
                b = second[at : at + molecules]
                c = jnp.where(low, a, pltpu.roll(b, R, 1))
                d = jnp.where(low, pltpu.roll(a, R, 1), b)
            here = pl.ds(start + place(t, 2 * g), molecules, stride=MOL)
            target[here, :] = target[here, :] + c
            here = pl.ds(start + place(t, 2 * g + 1), molecules, stride=MOL)
            target[here, :] = target[here, :] + d


def row_masks(keep, owned, start, molecules, rows, atoms):
    row = lax.broadcasted_iota(jnp.int32, (rows, LANES), 0)
    lane = lax.broadcasted_iota(jnp.int32, (rows, LANES), 1)
    doubled = (row >= (ROW_GROUPS - 1) * molecules) & (lane >= R)
    keep[...] = jnp.where(doubled, 0.0, 1.0)
    which = row
    for g in range(1, ROW_GROUPS):
        which = jnp.where(row >= g * molecules, row - g * molecules, which)
    first = start - HALO + which * MOL
    owned[...] = jnp.where((first >= 0) & (first < atoms), 1.0, 0.0)


def pick(offset):
    row = lax.broadcasted_iota(jnp.int32, (LANES, LANES), 0)
    lane = lax.broadcasted_iota(jnp.int32, (LANES, LANES), 1)
    base = jnp.where(lane >= R, R, 0)
    return jnp.where(row == base + offset, 1.0, 0.0).astype(BF16)


def dot(a, b):
    return jnp.dot(a, b, preferred_element_type=F32)


def dot_tn(a, b):
    return lax.dot_general(a, b, (((0,), (0,)), ((), ())), preferred_element_type=F32)


def dot_nt(a, b):
    return lax.dot_general(a, b, (((1,), (1,)), ((), ())), preferred_element_type=F32)


def multiplicities(count, keep, counts, i_row, j_row, k, t, rows):
    ci = count[pl.ds(i_row, rows), :]
    cj = count[pl.ds(j_row, rows), :]
    live = jnp.where(t == SPAN - 1, keep[...], 1.0)
    counts[:, :LANES] = dot(ci, pick(k)) * live
    counts[:, LANES:] = dot(cj, pick(MOL - k)) * live


def geometry(pos, i_row, j_row, rows, owned, radial, radial_own, slope, ways, extra):
    lane = lax.broadcasted_iota(jnp.int32, (SUB, LANES), 1)
    centre = jnp.where(lane >= R, lane - R, lane).astype(F32)
    inv_space = (R - 1) / CUTOFF
    for s in range(rows // SUB):
        o = s * SUB
        part = slice(o, o + SUB)
        off = [
            p[pl.ds(i_row + o, SUB), :] - p[pl.ds(j_row + o, SUB), :] for p in pos
        ]
        square = off[0] * off[0] + off[1] * off[1] + off[2] * off[2]
        clamped = jnp.maximum(square, 0.01)
        inverse = lax.rsqrt(clamped)
        distance = clamped * inverse
        z = distance * (math.pi / (2 * CUTOFF))
        z = z * z
        c = 1.0 / 479001600.0
        for term in (-1.0 / 3628800.0, 1.0 / 40320.0, -1.0 / 720.0, 1.0 / 24.0, -0.5, 1.0):
            c = c * z + term
        envelope = jnp.where(distance < CUTOFF, c * c, 0.0)
        bend = (-math.pi / CUTOFF) * jnp.sqrt(envelope * jnp.maximum(1.0 - envelope, 0.0))
        u = distance * inv_space - centre
        bump = jnp.exp(-0.5 * (u * u))
        value = bump * envelope
        radial[part] = value.astype(BF16)
        radial_own[part] = (value * owned[part]).astype(BF16)
        slope[part] = bump * bend - inv_space * (u * value)
        for d in range(3):
            ways[d, part] = off[d] * inverse
        extra[0, part] = jnp.where(square > 0.01, 1.0, 0.0)
        extra[1, part] = inverse
        extra[2, part] = envelope
        extra[3, part] = bend


def add_rows(ref, rows, value):
    ref[rows, :] = ref[rows, :] + value


def vector_kernel(
    molecules, rows, atoms,
    start_ref, pairs_ref, pos_ref, weights_ref,
    out_ref, grad_w_ref,
    w0, w1, w2, v2, c0, c1, c2, count_f, count,
    px, py, pz,
    s0, s1, s2, a0, a1, a2, gv, gx, gy, gz,
    keep, owned, counts, radial, radial_own, slope, ways, extra, pre, grad_pre, grad_ways,
    grad_radial,
):
    start = start_ref[0]
    spread(pairs_ref.at[0], w0, w1, start, molecules, rows)
    spread(pairs_ref.at[1], w2, v2, start, molecules, rows)
    spread(pairs_ref.at[2], c0, c1, start, molecules, rows)
    spread(pairs_ref.at[3], c2, count_f, start, molecules, rows)
    count[...] = count_f[...].astype(BF16)
    for d, p in enumerate((px, py, pz)):
        spread(pos_ref.at[d], p, None, start, molecules, rows)
    row_masks(keep, owned, start, molecules, rows, atoms)
    for total in (s0, s1, s2, a0, a1, a2, gv, gx, gy, gz):
        total[...] = jnp.zeros(total.shape, F32)
    grad_w_ref[...] = jnp.zeros(grad_w_ref.shape, F32)
    w, c, vec_sum, back, g_pos = (w0, w1, w2), (c0, c1, c2), (s0, s1, s2), (a0, a1, a2), (gx, gy, gz)

    def step(n, _):
        k = n // SPAN + 1
        t = n % SPAN
        i_row = pl.multiple_of(t * rows, SUB)
        j_row = pl.multiple_of((t + k) * rows, SUB)
        multiplicities(count, keep, counts, i_row, j_row, k, t, rows)
        geometry((px, py, pz), i_row, j_row, rows, owned, radial, radial_own, slope, ways, extra)
        pre[...] = dot(radial[...], weights_ref[...])
        for s in range(rows // SUB):
            o = s * SUB
            part = slice(o, o + SUB)
            ii = pl.ds(i_row + o, SUB)
            jj = pl.ds(j_row + o, SUB)
            h1, h2 = pre[part, :LANES], pre[part, LANES:]
            t1, t2 = jnp.tanh(h1), jnp.tanh(h2)
            f1, f2 = h1 * (1.0 + t1), h2 * (1.0 + t2)
            d1, d2 = (1.0 + t1) + f1 * (1.0 - t1), (1.0 + t2) + f2 * (1.0 - t2)
            mi, mj = counts[part, :LANES], counts[part, LANES:]
            f1i, f1j, f2i, f2j = f1 * mi, f1 * mj, f2 * mi, f2 * mj
            v2i, v2j = v2[ii, :], v2[jj, :]
            msg_i, msg_j = f2i * v2j, f2j * v2i
            along_i = along_j = across_i = across_j = 0.0
            for d in range(3):
                way = ways[d, part]
                wi, wj = w[d][ii, :], w[d][jj, :]
                ci, cj = c[d][ii, :], c[d][jj, :]
                add_rows(vec_sum[d], ii, f1i * wj + msg_i * way)
                add_rows(vec_sum[d], jj, f1j * wi - msg_j * way)
                add_rows(back[d], jj, f1i * ci)
                add_rows(back[d], ii, f1j * cj)
                grad_ways[d, part] = ci * msg_i - cj * msg_j
                along_i = along_i + ci * way
                along_j = along_j - cj * way
                across_i = across_i + ci * wj
                across_j = across_j + cj * wi
            add_rows(gv, jj, f2i * along_i)
            add_rows(gv, ii, f2j * along_j)
            g1 = mi * across_i + mj * across_j
            g2 = mi * along_i * v2j + mj * along_j * v2i
            grad_pre[part, :LANES] = (g1 * d1).astype(BF16)
            grad_pre[part, LANES:] = (g2 * d2).astype(BF16)
        grad_radial[...] = dot_nt(grad_pre[...], weights_ref[...])
        grad_w_ref[...] = grad_w_ref[...] + dot_tn(radial_own[...], grad_pre[...])
        for s in range(rows // SUB):
            o = s * SUB
            part = slice(o, o + SUB)
            ii = pl.ds(i_row + o, SUB)
            jj = pl.ds(j_row + o, SUB)
            inverse = extra[1, part]
            turn = 0.0
            for d in range(3):
                turn = turn + ways[d, part] * grad_ways[d, part]
            pull = extra[0, part] * (grad_radial[part] * slope[part] - inverse * turn)
            for d in range(3):
                g = grad_ways[d, part] * inverse + ways[d, part] * pull
                add_rows(g_pos[d], ii, g)
                add_rows(g_pos[d], jj, -g)
        return 0

    lax.fori_loop(0, OFFSETS * SPAN, step, 0)
    for n, (a, b) in enumerate(((s0, s1), (s2, gv), (a0, a1), (a2, gx), (gy, gz))):
        collect(a, b, out_ref.at[n], start, molecules, rows)


def scalar_kernel(
    molecules, rows, atoms,
    start_ref, pairs_ref, pos_ref, weights_ref, heads_ref,
    out_ref, grad_w_ref,
    q, key, v0, gs, count_f, count,
    px, py, pz,
    ss, gq, gk, g0, gx, gy, gz,
    keep, owned, counts, radial, radial_own, slope, ways, extra, pre, grad_pre,
    grad_radial, products, sums, gates, bends,
):
    start = start_ref[0]
    spread(pairs_ref.at[0], q, key, start, molecules, rows)
    spread(pairs_ref.at[1], v0, gs, start, molecules, rows)
    spread(pairs_ref.at[2], count_f, None, start, molecules, rows)
    count[...] = count_f[...].astype(BF16)
    for d, p in enumerate((px, py, pz)):
        spread(pos_ref.at[d], p, None, start, molecules, rows)
    row_masks(keep, owned, start, molecules, rows, atoms)
    for total in (ss, gq, gk, g0, gx, gy, gz):
        total[...] = jnp.zeros(total.shape, F32)
    grad_w_ref[...] = jnp.zeros(grad_w_ref.shape, F32)
    g_pos = (gx, gy, gz)

    def step(n, _):
        k = n // SPAN + 1
        t = n % SPAN
        i_row = pl.multiple_of(t * rows, SUB)
        j_row = pl.multiple_of((t + k) * rows, SUB)
        multiplicities(count, keep, counts, i_row, j_row, k, t, rows)
        geometry((px, py, pz), i_row, j_row, rows, owned, radial, radial_own, slope, ways, extra)
        pre[...] = dot(radial[...], weights_ref[...])
        for s in range(rows // SUB):
            o = s * SUB
            part = slice(o, o + SUB)
            ii = pl.ds(i_row + o, SUB)
            jj = pl.ds(j_row + o, SUB)
            hk, h0 = pre[part, :LANES], pre[part, LANES:]
            tk, t0 = jnp.tanh(hk), jnp.tanh(h0)
            fk, f0 = hk * (1.0 + tk), h0 * (1.0 + t0)
            gates[0, part] = fk
            gates[1, part] = f0
            gates[2, part] = (1.0 + tk) + fk * (1.0 - tk)
            gates[3, part] = (1.0 + t0) + f0 * (1.0 - t0)
            products[0, part, :LANES] = (q[ii, :] * key[jj, :] * fk).astype(BF16)
            products[0, part, LANES:] = (q[jj, :] * key[ii, :] * fk).astype(BF16)
            products[1, part, :LANES] = (gs[ii, :] * v0[jj, :] * f0).astype(BF16)
            products[1, part, LANES:] = (gs[jj, :] * v0[ii, :] * f0).astype(BF16)
        sums[0] = dot(products[0], heads_ref[...])
        sums[1] = dot(products[1], heads_ref[...])
        for s in range(rows // SUB):
            o = s * SUB
            part = slice(o, o + SUB)
            ii = pl.ds(i_row + o, SUB)
            jj = pl.ds(j_row + o, SUB)
            fk, f0 = gates[0, part], gates[1, part]
            envelope = extra[2, part]
            grad_k = grad_0 = steep = 0.0
            for side, (here, there) in enumerate(((ii, jj), (jj, ii))):
                lanes = slice(side * LANES, (side + 1) * LANES)
                m = counts[part, lanes]
                half = 0.5 * sums[0, part, lanes]
                g_att = sums[1, part, lanes]
                th = jnp.tanh(half)
                act = half * (1.0 + th)
                steepness = 0.5 * ((1.0 + th) + act * (1.0 - th))
                weight = m * envelope
                att = act * weight
                g_score = g_att * steepness * weight
                steep = steep + m * (g_att * act)
                bv = f0 * att
                dv = fk * g_score
                qh, kt, gh, vt = q[here, :], key[there, :], gs[here, :], v0[there, :]
                add_rows(ss, here, vt * bv)
                add_rows(g0, there, gh * bv)
                add_rows(gq, here, kt * dv)
                add_rows(gk, there, qh * dv)
                grad_k = grad_k + qh * kt * g_score
                grad_0 = grad_0 + gh * vt * att
            grad_pre[part, :LANES] = (grad_k * gates[2, part]).astype(BF16)
            grad_pre[part, LANES:] = (grad_0 * gates[3, part]).astype(BF16)
            bends[part] = steep * extra[3, part] * (1.0 / HEAD)
        grad_radial[...] = dot_nt(grad_pre[...], weights_ref[...])
        grad_w_ref[...] = grad_w_ref[...] + dot_tn(radial_own[...], grad_pre[...])
        for s in range(rows // SUB):
            o = s * SUB
            part = slice(o, o + SUB)
            ii = pl.ds(i_row + o, SUB)
            jj = pl.ds(j_row + o, SUB)
            pull = extra[0, part] * (grad_radial[part] * slope[part] + bends[part])
            for d in range(3):
                g = ways[d, part] * pull
                add_rows(g_pos[d], ii, g)
                add_rows(g_pos[d], jj, -g)
        return 0

    lax.fori_loop(0, OFFSETS * SPAN, step, 0)
    for n, (a, b) in enumerate(((ss, gq), (gk, g0), (gx, gy), (gz, None))):
        collect(a, b, out_ref.at[n], start, molecules, rows)


def whole(memory=pltpu.VMEM):
    return pl.BlockSpec(memory_space=memory)


def edge_call(kernel, atoms, start, inputs, outs, wide, extra_scratch):
    molecules = (atoms + 2 * (MOL - 1)) // MOL
    rows = -(-ROW_GROUPS * molecules // SUB) * SUB
    tall = STEPS * rows
    scratch = [pltpu.VMEM((tall, LANES), kind) for kind in wide]
    scratch += [
        pltpu.VMEM((rows, LANES), F32),
        pltpu.VMEM((rows, LANES), F32),
        pltpu.VMEM((rows, 2 * LANES), F32),
        pltpu.VMEM((rows, LANES), BF16),
        pltpu.VMEM((rows, LANES), BF16),
        pltpu.VMEM((rows, LANES), F32),
        pltpu.VMEM((3, rows, LANES), F32),
        pltpu.VMEM((4, rows, LANES), F32),
        pltpu.VMEM((rows, 2 * LANES), F32),
        pltpu.VMEM((rows, 2 * LANES), BF16),
    ]
    scratch += [pltpu.VMEM(shape(rows), kind) for shape, kind in extra_scratch]
    return pl.pallas_call(
        functools.partial(kernel, molecules, rows, atoms),
        out_shape=outs,
        in_specs=[whole(pltpu.SMEM)] + [whole()] * len(inputs),
        out_specs=[whole()] * len(outs),
        scratch_shapes=scratch,
        compiler_params=pltpu.CompilerParams(vmem_limit_bytes=56 * 1024 * 1024),
    )(start, *inputs)


def block_diagonal(weight):
    zero = jnp.zeros_like(weight)
    return jnp.concatenate(
        [jnp.concatenate([weight, zero], 1), jnp.concatenate([zero, weight], 1)], 0
    )


def both_diagonals(grad):
    parts = []
    for f in range(2):
        block = grad[:, f * LANES : (f + 1) * LANES]
        parts.append(0.5 * (block[:R, :R] + block[R:, R:]))
    return parts


def scatter_sum(part, axis):
    count = lax.axis_size(axis)
    size = part.shape[0] // count
    pieces = part.astype(BF16).reshape((count, size) + part.shape[1:])
    got = lax.all_to_all(pieces, axis, 0, 0)
    return jnp.sum(got.astype(F32), axis=0)


def split3(x):
    a = lax.reduce_precision(x, 8, 7)
    b = lax.reduce_precision(x - a, 8, 7)
    return jnp.concatenate([a, b, x - a - b], axis=0).astype(BF16)


def per_device(
    features, vectors, positions, atom_mask, neighbours, ln_gain, ln_bias,
    w_query, w_key, w_value, w_vector, w_output, w_key_filter, w_value_filter,
    cot_features, cot_vectors,
):
    channels = w_query.shape[1]
    atoms = features.shape[1]
    count = lax.axis_size("atoms")
    chan_first = lax.axis_index("feat") * channels
    row_first = lax.axis_index("atoms") * atoms
    remainder = lax.rem(row_first, MOL)
    start = jnp.reshape(HALO - remainder, (1,)).astype(jnp.int32)
    tall = -(-(HALO + ((atoms + 2 * (MOL - 1)) // MOL) * MOL) // 8) * 8

    dest = row_first + jnp.arange(atoms, dtype=jnp.int32)
    diff = neighbours - dest[None]
    diff = jnp.where(diff < 0, diff + MOL, diff) * atom_mask[None]
    packed = jnp.concatenate(
        [
            features,
            vectors.reshape(3 * H, atoms),
            cot_features,
            cot_vectors.reshape(3 * channels, atoms),
            diff.astype(BF16),
            split3(positions),
        ],
        axis=0,
    )
    forward = [(i, i + 1) for i in range(count - 1)]
    backward = [(i + 1, i) for i in range(count - 1)]
    low = lax.ppermute(packed[:, atoms - HALO :], "atoms", forward)
    high = lax.ppermute(packed[:, :HALO], "atoms", backward)
    ext = jnp.concatenate([low, packed, high], axis=1)
    wide = ext.shape[1]
    at = 0
    ext_parts = []
    for size in (H, 3 * H, channels, 3 * channels, 32, 9):
        ext_parts.append(ext[at : at + size])
        at += size
    x_feat, x_vec, x_cot, x_cotv, x_diff, x_pos = ext_parts
    x_vec = x_vec.reshape(3, H, wide)
    x_cot = x_cot.astype(F32)
    x_cotv = x_cotv.reshape(3, channels, wide)
    x_pos = x_pos.astype(F32)
    pos_ext = x_pos[0:3] + x_pos[3:6] + x_pos[6:9]

    feat_in = x_feat.astype(F32)
    mean_row = jnp.mean(feat_in, axis=0)
    centred = feat_in - mean_row[None]
    variance = jnp.mean(centred * centred, axis=0)
    inv_std = lax.rsqrt(variance + EPSILON)
    normed = centred * inv_std[None]
    normal_in = (normed * ln_gain[:, None] + ln_bias[:, None]).astype(BF16)
    own = slice(HALO, HALO + atoms)

    w_five = jnp.concatenate(
        [w_query, w_key, w_value[0], w_value[1], w_value[2]], axis=1
    )
    rows5 = jnp.einsum("ha,hc->ac", normal_in, w_five, preferred_element_type=F32)
    rows5 = rows5.astype(BF16).astype(F32)
    q_t, k_t, v0_t, v1_t, v2_t = [rows5[:, n * channels : (n + 1) * channels] for n in range(5)]

    projected = jnp.einsum("phc,dha->pdca", w_vector, x_vec, preferred_element_type=F32)
    vec_dot = jnp.sum(projected[0] * projected[1], axis=0)
    grad_out = jnp.stack(
        [jnp.sum(x_cotv.astype(F32) * projected[2], axis=0), x_cot * vec_dot, x_cot]
    ).astype(BF16)
    scalar_part = jnp.einsum("phc,pca->ha", w_output, grad_out, preferred_element_type=F32)
    grad_scalar = scatter_sum(scalar_part, "feat")

    own_vec = lax.dynamic_slice_in_dim(x_vec, chan_first, channels, 1)
    vec_t = jnp.transpose(own_vec.astype(F32), (0, 2, 1))
    cot_t = jnp.transpose(x_cotv.astype(F32), (0, 2, 1))
    gs_t = grad_scalar.T
    sorts = jnp.arange(R, dtype=jnp.int32).astype(F32)
    counts = jnp.sum(
        (x_diff.astype(F32)[:, :, None] == sorts[None, None, :]).astype(F32), axis=0
    )

    def pad(x):
        return jnp.pad(x, ((0, 0), (0, tall - wide), (0, 0)))

    def pair(a, b):
        return jnp.concatenate([a, b], axis=1)

    vec_pairs = pad(
        jnp.stack(
            [
                pair(vec_t[0] * v1_t, vec_t[1] * v1_t),
                pair(vec_t[2] * v1_t, v2_t),
                pair(cot_t[0], cot_t[1]),
                pair(cot_t[2], counts),
            ]
        )
    )
    sca_pairs = pad(jnp.stack([pair(q_t, k_t), pair(v0_t, gs_t), pair(counts, counts)]))
    pos_rows = pad(jnp.broadcast_to(pos_ext[:, :, None], (3, wide, LANES)))
    half = jnp.asarray(0.5, BF16)
    w_vec = jnp.concatenate(
        [block_diagonal(w_value_filter[1] * half), block_diagonal(w_value_filter[2] * half)], 1
    )
    w_sca = jnp.concatenate(
        [block_diagonal(w_key_filter * half), block_diagonal(w_value_filter[0] * half)], 1
    )
    lane = jnp.arange(2 * LANES, dtype=jnp.int32) // HEAD
    heads = (lane[:, None] == lane[None, :]).astype(BF16)
    grad_w_shape = jax.ShapeDtypeStruct((LANES, 2 * LANES), F32)

    vec_out, grad_w_vec_filter = edge_call(
        vector_kernel,
        atoms,
        start,
        (vec_pairs, pos_rows, w_vec),
        [jax.ShapeDtypeStruct((5, tall, LANES), F32), grad_w_shape],
        [F32] * 8 + [BF16] + [F32] * 3 + [F32] * 10,
        [
            (lambda r: (3, r, LANES), F32),
            (lambda r: (r, LANES), F32),
        ],
    )
    sca_out, grad_w_sca_filter = edge_call(
        scalar_kernel,
        atoms,
        start,
        (sca_pairs, pos_rows, w_sca, heads),
        [jax.ShapeDtypeStruct((4, tall, LANES), F32), grad_w_shape],
        [F32] * 5 + [BF16] + [F32] * 3 + [F32] * 7,
        [
            (lambda r: (r, LANES), F32),
            (lambda r: (2, r, 2 * LANES), BF16),
            (lambda r: (2, r, 2 * LANES), F32),
            (lambda r: (4, r, LANES), F32),
            (lambda r: (r, LANES), F32),
        ],
    )

    def parts(out, n):
        block = out[n, own]
        return block[:, :R], block[:, R:]

    s0, s1 = parts(vec_out, 0)
    s2, gv2_t = parts(vec_out, 1)
    a0, a1 = parts(vec_out, 2)
    a2, gx_v = parts(vec_out, 3)
    gy_v, gz_v = parts(vec_out, 4)
    ss_t, gq_t = parts(sca_out, 0)
    gk_t, gv0_t = parts(sca_out, 1)
    gx_s, gy_s = parts(sca_out, 2)
    gz_s, _ = parts(sca_out, 3)
    pos_part = jnp.stack(
        [jnp.sum(gx_v + gx_s, 1), jnp.sum(gy_v + gy_s, 1), jnp.sum(gz_v + gz_s, 1)]
    )

    vec_own_t = vec_t[:, own]
    gv1_t = vec_own_t[0] * a0 + vec_own_t[1] * a1 + vec_own_t[2] * a2
    back = jnp.stack([a0, a1, a2])
    vector_sum = jnp.transpose(jnp.stack([s0, s1, s2]), (0, 2, 1))
    grad_msg_vec = jnp.transpose(back * v1_t[own][None], (0, 2, 1))
    grads_t = jnp.concatenate([gq_t, gk_t, gv0_t, gv1_t, gv2_t], axis=1).astype(BF16)

    scalar_sum = ss_t.T.astype(BF16)
    gathered = lax.all_gather(scalar_sum, "feat", axis=0, tiled=True)
    outputs = jnp.einsum("phc,ha->pca", w_output, gathered, preferred_element_type=F32)
    projected = projected[:, :, :, own]
    vec_dot = vec_dot[:, own]
    grad_out = grad_out[:, :, own]
    delta_x = vec_dot * outputs[1] + outputs[2]
    delta_vec = projected[2] * outputs[0][None] + vector_sum
    own_features = lax.dynamic_slice_in_dim(features, chan_first, channels, 0).astype(F32)
    new_features = own_features + delta_x
    new_vectors = own_vec[:, :, own].astype(F32) + delta_vec
    mask_rows = atom_mask.astype(F32)
    squares = jnp.stack(
        [
            jnp.sum(new_features * new_features * mask_rows[None]),
            jnp.sum(delta_x * delta_x * mask_rows[None]),
            jnp.sum(new_vectors * new_vectors * mask_rows[None, None]),
            jnp.sum(delta_vec * delta_vec * mask_rows[None, None]),
            jnp.sum(mask_rows) * channels,
        ]
    )
    grad_x = cot_features.astype(F32)
    grad_v = cot_vectors.astype(F32)
    grad_dot = grad_x * outputs[1]
    grad_proj = jnp.stack(
        [grad_dot[None] * projected[1], grad_dot[None] * projected[0], grad_v * outputs[0][None]]
    ).astype(BF16)
    grad_w_output = jnp.einsum("ha,pca->phc", gathered, grad_out, preferred_element_type=F32)
    grad_w_vector = jnp.einsum("dha,pdca->phc", vectors, grad_proj, preferred_element_type=F32)
    vector_part = jnp.einsum("phc,pdca->hda", w_vector, grad_proj, preferred_element_type=F32)
    normal_own = normal_in[:, own]
    normed_own = normed[:, own]
    grad_w_five = jnp.einsum("ha,ac->hc", normal_own, grads_t, preferred_element_type=F32)
    normal_part = jnp.einsum("hc,ac->ha", w_five, grads_t, preferred_element_type=F32)
    hat_part = normal_part * ln_gain[:, None]
    small = jnp.concatenate(
        [
            jnp.sum(hat_part, axis=0)[None],
            jnp.sum(hat_part * normed_own, axis=0)[None],
            pos_part,
            jnp.pad(squares[None], ((0, 0), (0, atoms - 5))),
        ],
        axis=0,
    )
    small = jnp.sum(lax.all_gather(small, "feat", axis=0, tiled=False), axis=0)
    both = scatter_sum(
        jnp.concatenate([normal_part[:, None], vector_part], axis=1), "feat"
    )
    grad_normal = both[:, 0]
    grad_vec_proj = jnp.moveaxis(both[:, 1:], 0, 1)
    mean_first = small[0] / H
    mean_second = small[1] / H
    own_gain = lax.dynamic_slice_in_dim(ln_gain, chan_first, channels, 0)
    own_normed = lax.dynamic_slice_in_dim(normed_own, chan_first, channels, 0)
    grad_features = grad_x + inv_std[own][None] * (
        grad_normal * own_gain[:, None] - mean_first[None] - own_normed * mean_second[None]
    )
    grad_gain = jnp.sum(grad_normal * own_normed, axis=1)
    grad_bias = jnp.sum(grad_normal, axis=1)
    grad_vectors = grad_v + grad_vec_proj + grad_msg_vec
    grad_f1, grad_f2 = both_diagonals(grad_w_vec_filter)
    grad_fk, grad_f0 = both_diagonals(grad_w_sca_filter)

    flat = jnp.concatenate(
        [
            grad_w_five,
            grad_w_vector[0],
            grad_w_vector[1],
            grad_w_vector[2],
            grad_w_output[0],
            grad_w_output[1],
            grad_w_output[2],
            jnp.concatenate([grad_fk, grad_f0, grad_f1, grad_f2], axis=0),
            jnp.pad(
                jnp.stack([grad_gain, grad_bias, jnp.pad(small[5, :5], (0, channels - 5))]),
                ((0, H - 3), (0, 0)),
            ),
        ],
        axis=1,
    )
    got = lax.all_to_all(flat.reshape(count, H // count, flat.shape[1]), "atoms", 0, 0)
    summed = lax.all_gather(jnp.sum(got, axis=0), "atoms", axis=0, tiled=True)
    blocks = [summed[:, n * channels : (n + 1) * channels] for n in range(13)]
    filters = blocks[11]
    square_total = blocks[12][2, :4]
    count_total = blocks[12][2, 4]
    stream_rms = jnp.sqrt(
        square_total / (count_total * jnp.array([1.0, 1.0, 3.0, 3.0], F32)) + 1e-06
    )
    return (
        new_features.astype(BF16),
        new_vectors.astype(BF16),
        grad_features,
        grad_vectors,
        small[2:5],
        blocks[12][0],
        blocks[12][1],
        blocks[0],
        blocks[1],
        jnp.stack(blocks[2:5]),
        jnp.stack(blocks[5:8]),
        jnp.stack(blocks[8:11]),
        filters[:R],
        jnp.stack([filters[R : 2 * R], filters[2 * R : 3 * R], filters[3 * R :]]),
        stream_rms,
    )


def solution(mesh):
    in_specs = (
        P(None, "atoms"),
        P(None, None, "atoms"),
        P(None, "atoms"),
        P("atoms"),
        P(None, "atoms"),
        P(),
        P(),
        P(None, "feat"),
        P(None, "feat"),
        P(None, None, "feat"),
        P(None, None, "feat"),
        P(None, None, "feat"),
        P(None, "feat"),
        P(None, None, "feat"),
        P("feat", "atoms"),
        P(None, "feat", "atoms"),
    )
    out_specs = (
        P("feat", "atoms"),
        P(None, "feat", "atoms"),
        P("feat", "atoms"),
        P(None, "feat", "atoms"),
        P(None, "atoms"),
        P("feat"),
        P("feat"),
        P(None, "feat"),
        P(None, "feat"),
        P(None, None, "feat"),
        P(None, None, "feat"),
        P(None, None, "feat"),
        P(None, "feat"),
        P(None, None, "feat"),
        P(),
    )
    return jax.shard_map(
        per_device, mesh=mesh, in_specs=in_specs, out_specs=out_specs, check_vma=False
    )
```

```python
import functools
import math

import jax
import jax.numpy as jnp
from jax import lax
from jax.experimental import pallas as pl
from jax.experimental.pallas import tpu as pltpu
from jax.sharding import PartitionSpec as P

H = 256
HEADS = 8
HEAD = H // HEADS
R = 64
MOL = 29
HALO = 32
CUTOFF = 5.0
EPSILON = 1e-05
F32 = jnp.float32
BF16 = jnp.bfloat16

LANE_GROUPS = 2
ROW_GROUPS = 3
SPAN = 5
OFFSETS = 14
STEPS = SPAN + OFFSETS
SUB = 16
LANES = 128

QK, V0_COUNT, V12, VEC01, VEC2_COUNT, COT01, COT2 = range(7)
GROUP_ROWS = 352
EXTRAS = 16


def place(t, group):
    return (t + SPAN * group) % MOL


def spread(source, first, second, start, molecules, rows):
    low = lax.broadcasted_iota(jnp.int32, (molecules, LANES), 1) < R
    for t in range(STEPS):
        for g in range(ROW_GROUPS):
            a = source[pl.ds(start + place(t, 2 * g), molecules, stride=MOL), :]
            b = source[pl.ds(start + place(t, 2 * g + 1), molecules, stride=MOL), :]
            at = t * rows + g * molecules
            first[at : at + molecules] = jnp.where(low, a, pltpu.roll(b, R, 1))
            if second is not None:
                second[at : at + molecules] = jnp.where(low, pltpu.roll(a, R, 1), b)
        at = t * rows + ROW_GROUPS * molecules
        left = rows - ROW_GROUPS * molecules
        if left:
            first[at : at + left] = jnp.zeros((left, LANES), F32)
            if second is not None:
                second[at : at + left] = jnp.zeros((left, LANES), F32)


def collect(first, second, target, start, molecules, rows):
    low = lax.broadcasted_iota(jnp.int32, (molecules, LANES), 1) < R
    target[...] = jnp.zeros(target.shape, F32)
    for t in range(STEPS):
        for g in range(ROW_GROUPS):
            at = t * rows + g * molecules
            a = first[at : at + molecules]
            if second is None:
                c = jnp.where(low, a, 0.0)
                d = jnp.where(low, pltpu.roll(a, R, 1), 0.0)
            else:
                b = second[at : at + molecules]
                c = jnp.where(low, a, pltpu.roll(b, R, 1))
                d = jnp.where(low, pltpu.roll(a, R, 1), b)
            here = pl.ds(start + place(t, 2 * g), molecules, stride=MOL)
            target[here, :] = target[here, :] + c
            here = pl.ds(start + place(t, 2 * g + 1), molecules, stride=MOL)
            target[here, :] = target[here, :] + d


def row_masks(keep, owned, start, molecules, rows, atoms):
    row = lax.broadcasted_iota(jnp.int32, (rows, LANES), 0)
    lane = lax.broadcasted_iota(jnp.int32, (rows, LANES), 1)
    doubled = (row >= (ROW_GROUPS - 1) * molecules) & (lane >= R)
    keep[...] = jnp.where(doubled, 0.0, 1.0)
    which = row
    for g in range(1, ROW_GROUPS):
        which = jnp.where(row >= g * molecules, row - g * molecules, which)
    first = start - HALO + which * MOL
    owned[...] = jnp.where((first >= 0) & (first < atoms), 1.0, 0.0)


def pick(offset):
    row = lax.broadcasted_iota(jnp.int32, (LANES, LANES), 0)
    lane = lax.broadcasted_iota(jnp.int32, (LANES, LANES), 1)
    base = jnp.where(lane >= R, R, 0)
    return jnp.where(row == base + offset, 1.0, 0.0).astype(BF16)


def dot(a, b):
    return jnp.dot(a, b, preferred_element_type=F32)


def dot_tn(a, b):
    return lax.dot_general(a, b, (((0,), (0,)), ((), ())), preferred_element_type=F32)


def dot_nt(a, b):
    return lax.dot_general(a, b, (((1,), (1,)), ((), ())), preferred_element_type=F32)


def multiplicities(count, keep, counts, i_row, j_row, k, t, rows):
    ci = count[pl.ds(i_row, rows), :]
    cj = count[pl.ds(j_row, rows), :]
    live = jnp.where(t == SPAN - 1, keep[...], 1.0)
    counts[:, :LANES] = dot(ci, pick(k)) * live
    counts[:, LANES:] = dot(cj, pick(MOL - k)) * live


def geometry(pos, i_row, j_row, rows, owned, radial, radial_own, slope, ways, extra):
    lane = lax.broadcasted_iota(jnp.int32, (SUB, LANES), 1)
    centre = jnp.where(lane >= R, lane - R, lane).astype(F32)
    inv_space = (R - 1) / CUTOFF
    for s in range(rows // SUB):
        o = s * SUB
        part = slice(o, o + SUB)
        off = [
            p[pl.ds(i_row + o, SUB), :] - p[pl.ds(j_row + o, SUB), :] for p in pos
        ]
        square = off[0] * off[0] + off[1] * off[1] + off[2] * off[2]
        clamped = jnp.maximum(square, 0.01)
        inverse = lax.rsqrt(clamped)
        distance = clamped * inverse
        z = distance * (math.pi / (2 * CUTOFF))
        z = z * z
        c = 1.0 / 479001600.0
        for term in (-1.0 / 3628800.0, 1.0 / 40320.0, -1.0 / 720.0, 1.0 / 24.0, -0.5, 1.0):
            c = c * z + term
        envelope = jnp.where(distance < CUTOFF, c * c, 0.0)
        bend = (-math.pi / CUTOFF) * jnp.sqrt(envelope * jnp.maximum(1.0 - envelope, 0.0))
        u = distance * inv_space - centre
        bump = jnp.exp(-0.5 * (u * u))
        value = bump * envelope
        radial[part] = value.astype(BF16)
        radial_own[part] = (value * owned[part]).astype(BF16)
        slope[part] = bump * bend - inv_space * (u * value)
        for d in range(3):
            ways[d, part] = off[d] * inverse
        extra[0, part] = jnp.where(square > 0.01, 1.0, 0.0)
        extra[1, part] = inverse
        extra[2, part] = envelope
        extra[3, part] = bend


def set_filters(weights_ref, filter_1, filter_2):
    weights_ref[...] = jnp.zeros(weights_ref.shape, BF16)
    for f, ref in enumerate((filter_1, filter_2)):
        half = ref[...] * jnp.asarray(0.5, BF16)
        for g in range(LANE_GROUPS):
            at = f * LANES + g * R
            weights_ref[g * R : (g + 1) * R, at : at + R] = half


def spread_positions(pos_ref, loose, targets, start, molecules, rows):
    for d, target in enumerate(targets):
        loose[...] = jnp.broadcast_to(pos_ref[:, d : d + 1], loose.shape)
        spread(loose, target, None, start, molecules, rows)


def add_rows(ref, rows, value):
    ref[rows, :] = ref[rows, :] + value


def vector_kernel(
    molecules, rows, atoms,
    scalars, pairs_ref, pos_ref, filter_1, filter_2,
    sums_ref, back_ref, grads_ref, pos_out, grad_w_ref,
    w0, w1, w2, v2, c0, c1, c2, count_f, count,
    px, py, pz,
    s0, s1, s2, a0, a1, a2, gv, gx, gy, gz,
    keep, owned, counts, radial, radial_own, slope, ways, extra, pre, grad_pre,
    weights_ref, loose, loose2, grad_ways, grad_radial,
):
    start = scalars[0]
    set_filters(weights_ref, filter_1, filter_2)
    own = slice(HALO, HALO + atoms)
    v12 = pairs_ref[V12].astype(F32)
    low = lax.broadcasted_iota(jnp.int32, v12.shape, 1) < R
    v11 = jnp.where(low, v12, pltpu.roll(v12, R, 1))
    loose[...] = pairs_ref[VEC01].astype(F32) * v11
    spread(loose, w0, w1, start, molecules, rows)
    third = pairs_ref[VEC2_COUNT].astype(F32)
    loose[...] = jnp.where(low, third * v11, v12)
    spread(loose, w2, v2, start, molecules, rows)
    loose[...] = pairs_ref[COT01].astype(F32)
    spread(loose, c0, c1, start, molecules, rows)
    loose[...] = jnp.where(low, pairs_ref[COT2].astype(F32), third)
    spread(loose, c2, count_f, start, molecules, rows)
    count[...] = count_f[...].astype(BF16)
    spread_positions(pos_ref, loose, (px, py, pz), start, molecules, rows)
    row_masks(keep, owned, start, molecules, rows, atoms)
    for total in (s0, s1, s2, a0, a1, a2, gv, gx, gy, gz):
        total[...] = jnp.zeros(total.shape, F32)
    grad_w_ref[...] = jnp.zeros(grad_w_ref.shape, F32)
    w, c, vec_sum, back, g_pos = (w0, w1, w2), (c0, c1, c2), (s0, s1, s2), (a0, a1, a2), (gx, gy, gz)

    def step(n, _):
        k = n // SPAN + 1
        t = n % SPAN
        i_row = pl.multiple_of(t * rows, SUB)
        j_row = pl.multiple_of((t + k) * rows, SUB)
        multiplicities(count, keep, counts, i_row, j_row, k, t, rows)
        geometry((px, py, pz), i_row, j_row, rows, owned, radial, radial_own, slope, ways, extra)
        pre[...] = dot(radial[...], weights_ref[...])
        for s in range(rows // SUB):
            o = s * SUB
            part = slice(o, o + SUB)
            ii = pl.ds(i_row + o, SUB)
            jj = pl.ds(j_row + o, SUB)
            h1, h2 = pre[part, :LANES], pre[part, LANES:]
            t1, t2 = jnp.tanh(h1), jnp.tanh(h2)
            f1, f2 = h1 * (1.0 + t1), h2 * (1.0 + t2)
            d1, d2 = (1.0 + t1) + f1 * (1.0 - t1), (1.0 + t2) + f2 * (1.0 - t2)
            mi, mj = counts[part, :LANES], counts[part, LANES:]
            f1i, f1j, f2i, f2j = f1 * mi, f1 * mj, f2 * mi, f2 * mj
            v2i, v2j = v2[ii, :], v2[jj, :]
            msg_i, msg_j = f2i * v2j, f2j * v2i
            along_i = along_j = across_i = across_j = 0.0
            for d in range(3):
                way = ways[d, part]
                wi, wj = w[d][ii, :], w[d][jj, :]
                ci, cj = c[d][ii, :], c[d][jj, :]
                add_rows(vec_sum[d], ii, f1i * wj + msg_i * way)
                add_rows(vec_sum[d], jj, f1j * wi - msg_j * way)
                add_rows(back[d], jj, f1i * ci)
                add_rows(back[d], ii, f1j * cj)
                grad_ways[d, part] = ci * msg_i - cj * msg_j
                along_i = along_i + ci * way
                along_j = along_j - cj * way
                across_i = across_i + ci * wj
                across_j = across_j + cj * wi
            add_rows(gv, jj, f2i * along_i)
            add_rows(gv, ii, f2j * along_j)
            g1 = mi * across_i + mj * across_j
            g2 = mi * along_i * v2j + mj * along_j * v2i
            grad_pre[part, :LANES] = (g1 * d1).astype(BF16)
            grad_pre[part, LANES:] = (g2 * d2).astype(BF16)
        grad_radial[...] = dot_nt(grad_pre[...], weights_ref[...])
        grad_w_ref[...] = grad_w_ref[...] + dot_tn(radial_own[...], grad_pre[...])
        for s in range(rows // SUB):
            o = s * SUB
            part = slice(o, o + SUB)
            ii = pl.ds(i_row + o, SUB)
            jj = pl.ds(j_row + o, SUB)
            inverse = extra[1, part]
            turn = 0.0
            for d in range(3):
                turn = turn + ways[d, part] * grad_ways[d, part]
            pull = extra[0, part] * (grad_radial[part] * slope[part] - inverse * turn)
            for d in range(3):
                g = grad_ways[d, part] * inverse + ways[d, part] * pull
                add_rows(g_pos[d], ii, g)
                add_rows(g_pos[d], jj, -g)
        return 0

    lax.fori_loop(0, OFFSETS * SPAN, step, 0)
    low = lax.broadcasted_iota(jnp.int32, (atoms, LANES), 1) < R
    collect(s0, s1, loose, start, molecules, rows)
    both = loose[own].T
    sums_ref[0] = both[:R]
    sums_ref[1] = both[R:]
    collect(s2, gv, loose, start, molecules, rows)
    sums_ref[2] = loose[own].T[:R]
    collect(a0, a1, loose2, start, molecules, rows)
    v12 = pairs_ref[V12, own].astype(F32)
    v11 = jnp.where(low, v12, pltpu.roll(v12, R, 1))
    both = (loose2[own] * v11).T
    back_ref[0] = both[:R]
    back_ref[1] = both[R:]
    partial = loose2[own] * pairs_ref[VEC01, own].astype(F32)
    partial = partial + pltpu.roll(partial, R, 1)
    collect(a2, gx, loose2, start, molecules, rows)
    back_ref[2] = (loose2[own] * v11).T[:R]
    partial = partial + loose2[own] * pairs_ref[VEC2_COUNT, own].astype(F32)
    grads_ref[...] = jnp.where(low, partial, loose[own]).astype(BF16)
    pos_out[...] = jnp.zeros(pos_out.shape, F32)
    pos_out[0:1] = jnp.sum(loose2[own].T[R:], axis=0, keepdims=True)
    collect(gy, gz, loose, start, molecules, rows)
    both = loose[own].T
    pos_out[1:2] = jnp.sum(both[:R], axis=0, keepdims=True)
    pos_out[2:3] = jnp.sum(both[R:], axis=0, keepdims=True)


def scalar_kernel(
    molecules, rows, atoms,
    scalars, pairs_ref, pos_ref, filter_1, filter_2, scalar_parts,
    sum_ref, grads_qk_ref, grads_v0_ref, pos_out, grad_w_ref,
    q, key, v0, gs, count_f, count,
    px, py, pz,
    ss, gq, gk, g0, gx, gy, gz,
    keep, owned, counts, radial, radial_own, slope, ways, extra, pre, grad_pre,
    weights_ref, loose, heads_ref, grad_radial, products, sums, gates, bends,
):
    start = scalars[0]
    set_filters(weights_ref, filter_1, filter_2)
    row = lax.broadcasted_iota(jnp.int32, (2 * LANES, 2 * LANES), 0)
    lane = lax.broadcasted_iota(jnp.int32, (2 * LANES, 2 * LANES), 1)
    heads_ref[...] = jnp.where(row // HEAD == lane // HEAD, 1.0, 0.0).astype(BF16)
    own = slice(HALO, HALO + atoms)
    loose[...] = pairs_ref[QK].astype(F32)
    spread(loose, q, key, start, molecules, rows)
    loose[...] = pairs_ref[V0_COUNT].astype(F32)
    spread(loose, v0, count_f, start, molecules, rows)
    count[...] = count_f[...].astype(BF16)
    summed = scalar_parts[0].astype(F32)
    for f in range(1, scalar_parts.shape[0]):
        summed = summed + scalar_parts[f].astype(F32)
    summed = jnp.concatenate([summed, jnp.zeros_like(summed)], axis=0).T
    loose[own] = summed[:atoms]
    loose[:HALO] = summed[atoms : atoms + HALO]
    loose[HALO + atoms : 2 * HALO + atoms] = summed[atoms + HALO : atoms + 2 * HALO]
    loose[2 * HALO + atoms :] = jnp.zeros((loose.shape[0] - 2 * HALO - atoms, LANES), F32)
    spread(loose, gs, None, start, molecules, rows)
    spread_positions(pos_ref, loose, (px, py, pz), start, molecules, rows)
    row_masks(keep, owned, start, molecules, rows, atoms)
    for total in (ss, gq, gk, g0, gx, gy, gz):
        total[...] = jnp.zeros(total.shape, F32)
    grad_w_ref[...] = jnp.zeros(grad_w_ref.shape, F32)
    g_pos = (gx, gy, gz)

    def step(n, _):
        k = n // SPAN + 1
        t = n % SPAN
        i_row = pl.multiple_of(t * rows, SUB)
        j_row = pl.multiple_of((t + k) * rows, SUB)
        multiplicities(count, keep, counts, i_row, j_row, k, t, rows)
        geometry((px, py, pz), i_row, j_row, rows, owned, radial, radial_own, slope, ways, extra)
        pre[...] = dot(radial[...], weights_ref[...])
        for s in range(rows // SUB):
            o = s * SUB
            part = slice(o, o + SUB)
            ii = pl.ds(i_row + o, SUB)
            jj = pl.ds(j_row + o, SUB)
            hk, h0 = pre[part, :LANES], pre[part, LANES:]
            tk, t0 = jnp.tanh(hk), jnp.tanh(h0)
            fk, f0 = hk * (1.0 + tk), h0 * (1.0 + t0)
            gates[0, part] = fk
            gates[1, part] = f0
            gates[2, part] = (1.0 + tk) + fk * (1.0 - tk)
            gates[3, part] = (1.0 + t0) + f0 * (1.0 - t0)
            products[0, part, :LANES] = (q[ii, :] * key[jj, :] * fk).astype(BF16)
            products[0, part, LANES:] = (q[jj, :] * key[ii, :] * fk).astype(BF16)
            products[1, part, :LANES] = (gs[ii, :] * v0[jj, :] * f0).astype(BF16)
            products[1, part, LANES:] = (gs[jj, :] * v0[ii, :] * f0).astype(BF16)
        sums[0] = dot(products[0], heads_ref[...])
        sums[1] = dot(products[1], heads_ref[...])
        for s in range(rows // SUB):
            o = s * SUB
            part = slice(o, o + SUB)
            ii = pl.ds(i_row + o, SUB)
            jj = pl.ds(j_row + o, SUB)
            fk, f0 = gates[0, part], gates[1, part]
            envelope = extra[2, part]
            grad_k = grad_0 = steep = 0.0
            for side, (here, there) in enumerate(((ii, jj), (jj, ii))):
                lanes = slice(side * LANES, (side + 1) * LANES)
                m = counts[part, lanes]
                half = 0.5 * sums[0, part, lanes]
                g_att = sums[1, part, lanes]
                th = jnp.tanh(half)
                act = half * (1.0 + th)
                steepness = 0.5 * ((1.0 + th) + act * (1.0 - th))
                weight = m * envelope
                att = act * weight
                g_score = g_att * steepness * weight
                steep = steep + m * (g_att * act)
                bv = f0 * att
                dv = fk * g_score
                qh, kt, gh, vt = q[here, :], key[there, :], gs[here, :], v0[there, :]
                add_rows(ss, here, vt * bv)
                add_rows(g0, there, gh * bv)
                add_rows(gq, here, kt * dv)
                add_rows(gk, there, qh * dv)
                grad_k = grad_k + qh * kt * g_score
                grad_0 = grad_0 + gh * vt * att
            grad_pre[part, :LANES] = (grad_k * gates[2, part]).astype(BF16)
            grad_pre[part, LANES:] = (grad_0 * gates[3, part]).astype(BF16)
            bends[part] = steep * extra[3, part] * (1.0 / HEAD)
        grad_radial[...] = dot_nt(grad_pre[...], weights_ref[...])
        grad_w_ref[...] = grad_w_ref[...] + dot_tn(radial_own[...], grad_pre[...])
        for s in range(rows // SUB):
            o = s * SUB
            part = slice(o, o + SUB)
            ii = pl.ds(i_row + o, SUB)
            jj = pl.ds(j_row + o, SUB)
            pull = extra[0, part] * (grad_radial[part] * slope[part] + bends[part])
            for d in range(3):
                g = ways[d, part] * pull
                add_rows(g_pos[d], ii, g)
                add_rows(g_pos[d], jj, -g)
        return 0

    lax.fori_loop(0, OFFSETS * SPAN, step, 0)
    collect(ss, g0, loose, start, molecules, rows)
    sum_ref[...] = loose[own].T[:R].astype(BF16)
    grads_v0_ref[...] = loose[own].astype(BF16)
    collect(gq, gk, loose, start, molecules, rows)
    grads_qk_ref[...] = loose[own].astype(BF16)
    pos_out[...] = jnp.zeros(pos_out.shape, F32)
    collect(gx, gy, loose, start, molecules, rows)
    both = loose[own].T
    pos_out[0:1] = jnp.sum(both[:R], axis=0, keepdims=True)
    pos_out[1:2] = jnp.sum(both[R:], axis=0, keepdims=True)
    collect(gz, None, loose, start, molecules, rows)
    pos_out[2:3] = jnp.sum(loose[own].T[:R], axis=0, keepdims=True)


def whole(memory=pltpu.VMEM):
    return pl.BlockSpec(memory_space=memory)


def params(mib=56):
    return pltpu.CompilerParams(vmem_limit_bytes=mib * 1024 * 1024)


def edge_call(kernel, atoms, tall, inputs, outs, wide, extra_scratch):
    molecules = (atoms + 2 * (MOL - 1)) // MOL
    rows = -(-ROW_GROUPS * molecules // SUB) * SUB
    scratch = [pltpu.VMEM((STEPS * rows, LANES), kind) for kind in wide]
    scratch += [
        pltpu.VMEM((rows, LANES), F32),
        pltpu.VMEM((rows, LANES), F32),
        pltpu.VMEM((rows, 2 * LANES), F32),
        pltpu.VMEM((rows, LANES), BF16),
        pltpu.VMEM((rows, LANES), BF16),
        pltpu.VMEM((rows, LANES), F32),
        pltpu.VMEM((3, rows, LANES), F32),
        pltpu.VMEM((4, rows, LANES), F32),
        pltpu.VMEM((rows, 2 * LANES), F32),
        pltpu.VMEM((rows, 2 * LANES), BF16),
        pltpu.VMEM((LANES, 2 * LANES), BF16),
        pltpu.VMEM((tall, LANES), F32),
    ]
    scratch += [pltpu.VMEM(shape(rows), kind) for shape, kind in extra_scratch]
    outs = [jax.ShapeDtypeStruct(shape, kind) for shape, kind in outs]
    return pl.pallas_call(
        functools.partial(kernel, molecules, rows, atoms),
        out_shape=outs,
        in_specs=[whole(pltpu.SMEM)] + [whole()] * (len(inputs) - 1),
        out_specs=[whole()] * len(outs),
        scratch_shapes=scratch,
        compiler_params=params(),
    )(*inputs)


def offsets_in_block(neighbours, mask, first):
    lane = lax.broadcasted_iota(jnp.int32, neighbours.shape, 1)
    diff = neighbours - (first + lane)
    return jnp.where(diff < 0, diff + MOL, diff) * mask


def pieces(x):
    a = x.astype(BF16)
    rest = x - a.astype(F32)
    b = rest.astype(BF16)
    return a, b, (rest - b.astype(F32)).astype(BF16)


def edge_groups(features, vectors, cot_f, cot_v, neighbours, mask, positions, first):
    diff = offsets_in_block(neighbours[...], mask[...], first).astype(F32).astype(BF16)
    groups = [jnp.concatenate([features[...], cot_f[...], diff], axis=0)]
    for d in range(3):
        rows = [x.astype(F32) for x in pieces(positions[d : d + 1])]
        rows = jnp.concatenate(rows + [jnp.zeros((29, LANES), F32)], axis=0).astype(BF16)
        groups.append(jnp.concatenate([vectors[d], cot_v[d], rows], axis=0))
    return groups


def halo_kernel(atoms, scalars, *refs):
    row_first = scalars[2]
    lane = lax.broadcasted_iota(jnp.int32, (GROUP_ROWS, LANES), 1)
    for end, at, out in ((0, atoms - LANES, refs[14]), (1, 0, refs[15])):
        groups = edge_groups(*refs[7 * end : 7 * end + 7], row_first + at)
        total = None
        for g, group in enumerate(groups):
            by = (HALO * (g + 1) if end == 0 else HALO * g) % LANES
            moved = group.astype(F32)
            moved = pltpu.roll(moved, by, 1) if by else moved
            total = moved if total is None else jnp.where(lane >= HALO * g, moved, total)
        out[...] = total.astype(BF16)


def halo_call(atoms, scalars, arrays):
    specs = []
    for at in (atoms // LANES - 1, 0):
        for x in arrays:
            shape = x.shape[:-1] + (LANES,)
            index = (0,) * (x.ndim - 1) + (at,)
            specs.append(pl.BlockSpec(shape, lambda *_, index=index: index))
    out = jax.ShapeDtypeStruct((GROUP_ROWS, LANES), BF16)
    return pl.pallas_call(
        functools.partial(halo_kernel, atoms),
        grid=(1,),
        out_shape=[out, out],
        in_specs=[whole(pltpu.SMEM)] + specs,
        out_specs=[whole(), whole()],
        compiler_params=params(32),
    )(scalars, *arrays, *arrays)


def column(row):
    return jnp.broadcast_to(row, (8, row.shape[1])).T[:, :1]


def normalised(f):
    mean = jnp.mean(f, axis=0, keepdims=True)
    centred = f - mean
    inv = lax.rsqrt(jnp.mean(centred * centred, axis=0, keepdims=True) + EPSILON)
    return centred * inv, mean, inv


def dense_kernel(
    atoms,
    scalars, features, vectors, cot_f, cot_v, neighbours, mask, positions, low_ref, high_ref,
    gain_ref, bias_ref, w_query, w_key, w_value, w_vector, w_output,
    rows_ref, pos_ref, part_ref, stat_ref,
    w_qk, w_v0, w_v12, w_vec_t, w_out,
):
    chan_first = pl.multiple_of(scalars[1], R)
    row_first = scalars[2]
    gain, bias = column(gain_ref[...]), column(bias_ref[...])
    w_qk[...] = jnp.concatenate([w_query[...], w_key[...]], axis=1)
    w_v0[...] = jnp.concatenate([w_value[0], jnp.zeros_like(w_value[0])], axis=1)
    w_v12[...] = jnp.concatenate([w_value[1], w_value[2]], axis=1)
    w_out[...] = jnp.concatenate([w_output[p] for p in range(3)], axis=1)
    for p in range(3):
        w_vec_t[p * R : (p + 1) * R] = w_vector[p].astype(F32).T.astype(BF16)

    def block(f, v, cf, cv, own_v, diff, pos):
        width = f.shape[1]
        normed, mean, inv = normalised(f)
        turned = (normed * gain + bias).T.astype(BF16)
        kinds = lax.broadcasted_iota(jnp.int32, (32, width), 0).astype(F32)
        counts = jnp.zeros((32, width), F32)
        for s in range(diff.shape[0]):
            counts = counts + jnp.where(diff[s : s + 1] == kinds, 1.0, 0.0)
        none = jnp.zeros((R, width), F32)
        counts = jnp.concatenate([none, counts, none[:32]], axis=0).T
        pairs = [None] * 7
        pairs[QK] = dot(turned, w_qk[...])
        pairs[V0_COUNT] = dot(turned, w_v0[...]) + counts
        pairs[V12] = dot(turned, w_v12[...])
        pairs[VEC01] = jnp.concatenate([own_v[0], own_v[1]], axis=0).T
        pairs[VEC2_COUNT] = jnp.concatenate([own_v[2], none], axis=0).T + counts
        pairs[COT01] = jnp.concatenate([cv[0], cv[1]], axis=0).T
        pairs[COT2] = jnp.concatenate([cv[2], none], axis=0).T
        place3 = jnp.concatenate([pos, jnp.zeros((LANES - 3, width), F32)], axis=0).T
        vec_dot = grad_0 = 0.0
        for d in range(3):
            proj = dot(w_vec_t[...], v[d])
            vec_dot = vec_dot + proj[:R] * proj[R : 2 * R]
            grad_0 = grad_0 + cv[d] * proj[2 * R :]
        grad_out = jnp.concatenate([grad_0, cf * vec_dot, cf], axis=0).astype(BF16)
        part = dot(w_out[...], grad_out)
        return [x.astype(BF16) for x in pairs], place3, part.astype(BF16), mean, inv

    wide = 2 * LANES

    def step(b, _):
        at = pl.multiple_of(b * wide, wide)
        here = pl.ds(at, wide)
        own_v = [vectors[d, pl.ds(chan_first, R), here].astype(F32) for d in range(3)]
        diff = offsets_in_block(neighbours[:, here], mask[:, here], row_first + at)
        pairs, place3, part, mean, inv = block(
            features[:, here].astype(F32),
            [vectors[d, :, here] for d in range(3)],
            cot_f[:, here].astype(F32),
            [cot_v[d, :, here].astype(F32) for d in range(3)],
            own_v,
            diff.astype(F32),
            positions[:, here],
        )
        there = pl.ds(pl.multiple_of(HALO + at, 2 * SUB), wide)
        for n, pair in enumerate(pairs):
            rows_ref[n, there, :] = pair
        pos_ref[there, :] = place3
        part_ref[:, here] = part
        stat_ref[0:1, here] = mean
        stat_ref[1:2, here] = inv
        return 0

    lax.fori_loop(0, atoms // wide, step, 0)

    lane = lax.broadcasted_iota(jnp.int32, (GROUP_ROWS, LANES), 1)
    packed_low, packed_high = low_ref[...].astype(F32), high_ref[...].astype(F32)
    groups = []
    for g in range(4):
        a = pltpu.roll(packed_low, (LANES - HALO * g) % LANES, 1) if g else packed_low
        by = (LANES + HALO - HALO * g) % LANES
        b = pltpu.roll(packed_high, by, 1) if by else packed_high
        both = jnp.where(lane < HALO, a, jnp.where(lane < 2 * HALO, b, 0.0))
        groups.append(both)
    pick_rows = lax.broadcasted_iota(jnp.int32, (H, LANES), 0)
    own_v, pos = [], []
    for d in range(3):
        g = groups[1 + d]
        found = g[:R]
        for f in range(1, H // R):
            found = jnp.where(chan_first == f * R, g[f * R : (f + 1) * R], found)
        own_v.append(found)
        pos.append(g[320:321] + g[321:322] + g[322:323])
    pairs, place3, part, _, _ = block(
        groups[0][:H],
        [groups[1 + d][:H].astype(BF16) for d in range(3)],
        groups[0][H : H + R],
        [groups[1 + d][H : H + R] for d in range(3)],
        own_v,
        groups[0][H + R :],
        jnp.concatenate(pos, axis=0),
    )
    high = HALO + atoms
    tall = rows_ref.shape[1]
    for n, pair in enumerate(pairs):
        rows_ref[n, :HALO] = pair[:HALO]
        rows_ref[n, high : high + HALO] = pair[HALO : 2 * HALO]
        rows_ref[n, high + HALO :] = jnp.zeros((tall - high - HALO, LANES), BF16)
    pos_ref[:HALO] = place3[:HALO]
    pos_ref[high : high + HALO] = place3[HALO : 2 * HALO]
    pos_ref[high + HALO :] = jnp.zeros((tall - high - HALO, LANES), F32)
    part_ref[:, atoms:] = part


def both_diagonals(grad, f):
    at = f * LANES
    return 0.5 * (grad[:R, at : at + R] + grad[R:, at + R : at + LANES])


def layer_kernel(
    atoms,
    scalars, features, stat, vectors, cot_f, cot_v, gathered, sums_ref,
    grads_qk, grads_v0, grads_v12, pos_a, pos_b, mask, gain_ref, bias_ref,
    w_query, w_key, w_value, w_vector, w_output, grad_filters_a, grad_filters_b,
    feat_out, vec_out, send_ref, flat_ref,
    w_five, w_vec, w_vec_t, w_out_t, t_five, t_vec, t_out,
):
    chan_first = pl.multiple_of(scalars[1], R)
    gain, bias = column(gain_ref[...]), column(bias_ref[...])
    none = jnp.zeros((H, R), BF16)
    w_five[...] = jnp.concatenate(
        [w_query[...], w_key[...], none, w_value[0], w_value[1], w_value[2]], axis=1
    )
    w_vec[...] = jnp.concatenate([w_vector[p] for p in range(3)], axis=1)
    for p in range(3):
        w_vec_t[p * R : (p + 1) * R] = w_vector[p].astype(F32).T.astype(BF16)
        w_out_t[p * R : (p + 1) * R] = w_output[p].astype(F32).T.astype(BF16)
    t_five[...] = jnp.zeros(t_five.shape, F32)
    t_vec[...] = jnp.zeros(t_vec.shape, F32)
    t_out[...] = jnp.zeros(t_out.shape, F32)
    wide = 2 * LANES
    split = send_ref.shape[0]

    def step(b, _):
        at = pl.multiple_of(b * wide, wide)
        here = pl.ds(at, wide)
        real = mask[:, here].astype(F32)
        all_sums = gathered[:, here]
        outputs = dot(w_out_t[...], all_sums)
        out_0, out_1, out_2 = outputs[:R], outputs[R : 2 * R], outputs[2 * R :]
        cf = cot_f[:, here].astype(F32)
        grad_dot = cf * out_1
        vec_dot = grad_0 = square_v = square_dv = 0.0
        for d in range(3):
            proj = dot(w_vec_t[...], vectors[d, :, here])
            first, second, third = proj[:R], proj[R : 2 * R], proj[2 * R :]
            cv = cot_v[d, :, here].astype(F32)
            vec_dot = vec_dot + first * second
            grad_0 = grad_0 + cv * third
            delta = third * out_0 + sums_ref[d, :, here]
            moved = vectors[d, pl.ds(chan_first, R), here].astype(F32) + delta
            vec_out[d, :, here] = moved.astype(BF16)
            square_v = square_v + moved * moved
            square_dv = square_dv + delta * delta
            grad_proj = jnp.concatenate(
                [grad_dot * second, grad_dot * first, cv * out_0], axis=0
            ).astype(BF16)
            part = dot(w_vec[...], grad_proj).astype(BF16)
            for f in range(split):
                send_ref[f, (1 + d) * R : (2 + d) * R, here] = part[f * R : (f + 1) * R]
            t_vec[...] = t_vec[...] + dot_nt(vectors[d, :, here], grad_proj)
        delta = vec_dot * out_1 + out_2
        moved = features[pl.ds(chan_first, R), here].astype(F32) + delta
        feat_out[:, here] = moved.astype(BF16)
        grad_out = jnp.concatenate([grad_0, cf * vec_dot, cf], axis=0).astype(BF16)
        t_out[...] = t_out[...] + dot_nt(all_sums, grad_out)
        normed = (features[:, here].astype(F32) - stat[0:1, here]) * stat[1:2, here]
        normal = (normed * gain + bias).astype(BF16)
        grads = jnp.concatenate(
            [grads_qk[here, :], grads_v0[here, :], grads_v12[here, :]], axis=1
        )
        t_five[...] = t_five[...] + dot(normal, grads)
        part = dot_nt(w_five[...], grads)
        rounded = part.astype(BF16)
        for f in range(split):
            send_ref[f, :R, here] = rounded[f * R : (f + 1) * R]
        hat = part * gain
        tops = [
            jnp.sum(hat, axis=0, keepdims=True),
            jnp.sum(hat * normed, axis=0, keepdims=True),
        ]
        exact = [pos_a[d : d + 1, here] + pos_b[d : d + 1, here] for d in range(3)]
        for x in (moved, delta):
            exact.append(jnp.sum(x * x, axis=0, keepdims=True) * real)
        for x in (square_v, square_dv):
            exact.append(jnp.sum(x, axis=0, keepdims=True) * real)
        heads = [x.astype(BF16).astype(F32) for x in exact]
        tops = tops + heads + [x - y for x, y in zip(exact, heads)]
        tops = jnp.concatenate(tops, axis=0).astype(BF16)
        for f in range(split):
            send_ref[f, 4 * R :, here] = tops
        return 0

    lax.fori_loop(0, atoms // wide, step, 0)
    five = t_five[...]
    first = five[:, : 2 * R]
    second = jnp.concatenate([five[:, 3 * R : 4 * R], five[:, 4 * R : 5 * R]], axis=1)
    third = jnp.concatenate([five[:, 5 * R :], t_vec[:, :R]], axis=1)
    grad_a, grad_b = grad_filters_a[...], grad_filters_b[...]
    filters = jnp.concatenate(
        [
            both_diagonals(grad_b, 0),
            both_diagonals(grad_b, 1),
            both_diagonals(grad_a, 0),
            both_diagonals(grad_a, 1),
        ],
        axis=0,
    )
    last = jnp.concatenate([t_out[:, 2 * R :], filters], axis=1)
    for n, pair in enumerate((first, second, third, t_vec[:, R:], t_out[:, : 2 * R], last)):
        flat_ref[:, n * LANES : (n + 1) * LANES] = pair.astype(BF16)


def final_kernel(
    atoms,
    scalars, got, features, stat, gain_ref, cot_f, cot_v, back_ref, mask,
    grad_feat, grad_vec, grad_pos, small_ref,
):
    chan_first = pl.multiple_of(scalars[1], R)
    whole_gain = column(gain_ref[...])
    gain = whole_gain[:R]
    for f in range(1, H // R):
        gain = jnp.where(chan_first == f * R, whole_gain[f * R : (f + 1) * R], gain)

    def summed(rows):
        total = got[0, rows].astype(F32)
        for f in range(1, got.shape[0]):
            total = total + got[f, rows].astype(F32)
        return total

    tops = summed(slice(4 * R, 4 * R + EXTRAS))
    grad_normal = summed(slice(0, R))
    inv = stat[1:2]
    normed = (features[pl.ds(chan_first, R), :].astype(F32) - stat[0:1]) * inv
    inner = grad_normal * gain - tops[0:1] * (1.0 / H) - normed * (tops[1:2] * (1.0 / H))
    grad_feat[...] = cot_f[...].astype(F32) + inv * inner
    for d in range(3):
        part = summed(slice((1 + d) * R, (2 + d) * R))
        grad_vec[d] = cot_v[d].astype(F32) + part + back_ref[d]
    exact = tops[2:9] + tops[9:16]
    grad_pos[...] = exact[:3]
    ones = jnp.ones((8, atoms), BF16)
    small_ref[...] = jnp.zeros(small_ref.shape, F32)
    small_ref[:, :R] = dot_nt(ones, (grad_normal * normed).astype(BF16))
    small_ref[:, R : 2 * R] = dot_nt(ones, grad_normal.astype(BF16))
    totals = jnp.sum(exact[3:7], axis=1, keepdims=True)
    small_ref[0:4, LANES : 2 * LANES] = jnp.broadcast_to(totals, (4, LANES))
    real = jnp.sum(mask[...].astype(F32), axis=1, keepdims=True)
    small_ref[4:5, LANES : 2 * LANES] = jnp.broadcast_to(real, (1, LANES))


def unpack_kernel(
    share,
    got,
    g_gain, g_bias, g_query, g_key, g_value, g_vector, g_output, g_key_f, g_value_f, rms_ref,
):
    total = got[0, share:]
    for n in range(1, got.shape[0]):
        total = total + got[n, share:]
    g_gain[...] = total[0:1, :R]
    g_bias[...] = total[0:1, R : 2 * R]
    numbers = total[:, LANES : LANES + 1]
    size = jnp.where(lax.broadcasted_iota(jnp.int32, (8, 1), 0) < 2, 1.0, 3.0) * H
    rms = jnp.sqrt(numbers / (numbers[4:5] * size) + 1e-06)
    rms_ref[...] = jnp.broadcast_to(rms, (8, LANES)).T[:1, :8]
    plain = [(g_query, None), (g_key, None)]
    plain += [(g, p) for g in (g_value, g_vector, g_output) for p in range(3)]
    for n in range(got.shape[0]):
        rows = slice(n * share, (n + 1) * share)
        for m, (g, p) in enumerate(plain):
            value = got[n, :share, m * R : (m + 1) * R]
            if p is None:
                g[rows] = value
            else:
                g[p, rows] = value
        at = n * share
        value = got[n, :share, 11 * R : 12 * R]
        if at < R:
            g_key_f[at : at + share] = value
        else:
            p = at // R - 1
            g_value_f[p, at % R : at % R + share] = value


def everywhere(x, axis):
    count = lax.axis_size(axis)
    return lax.all_to_all(jnp.broadcast_to(x[None], (count,) + x.shape), axis, 0, 0)


def per_device(
    features, vectors, positions, atom_mask, neighbours, ln_gain, ln_bias,
    w_query, w_key, w_value, w_vector, w_output, w_key_filter, w_value_filter,
    cot_features, cot_vectors,
):
    channels = w_query.shape[1]
    atoms = features.shape[1]
    count = lax.axis_size("atoms")
    split = lax.axis_size("feat")
    chan_first = lax.axis_index("feat") * channels
    row_first = lax.axis_index("atoms") * atoms
    start = HALO - lax.rem(row_first, MOL)
    scalars = jnp.stack([start, chan_first, row_first]).astype(jnp.int32)
    molecules = (atoms + 2 * (MOL - 1)) // MOL
    tall = -(-(HALO + molecules * MOL) // SUB) * SUB
    mask = atom_mask.reshape(1, atoms)
    gain, bias = ln_gain.reshape(1, H), ln_bias.reshape(1, H)

    ends = halo_call(
        atoms,
        scalars,
        (features, vectors, cot_features, cot_vectors, neighbours, mask, positions),
    )
    low = lax.ppermute(ends[0], "atoms", [(i, i + 1) for i in range(count - 1)])
    high = lax.ppermute(ends[1], "atoms", [(i + 1, i) for i in range(count - 1)])

    inputs = (
        scalars, features, vectors, cot_features, cot_vectors, neighbours, mask, positions,
        low, high, gain, bias, w_query, w_key, w_value, w_vector, w_output,
    )
    rows, pos, part, stat = pl.pallas_call(
        functools.partial(dense_kernel, atoms),
        out_shape=[
            jax.ShapeDtypeStruct((7, tall, LANES), BF16),
            jax.ShapeDtypeStruct((tall, LANES), F32),
            jax.ShapeDtypeStruct((H, atoms + LANES), BF16),
            jax.ShapeDtypeStruct((8, atoms), F32),
        ],
        in_specs=[whole(pltpu.SMEM)] + [whole()] * (len(inputs) - 1),
        out_specs=[whole()] * 4,
        scratch_shapes=[
            pltpu.VMEM((H, LANES), BF16),
            pltpu.VMEM((H, LANES), BF16),
            pltpu.VMEM((H, LANES), BF16),
            pltpu.VMEM((3 * R, H), BF16),
            pltpu.VMEM((H, 3 * R), BF16),
        ],
        compiler_params=params(),
    )(*inputs)
    scalar_parts = lax.all_to_all(part.reshape(split, channels, atoms + LANES), "feat", 0, 0)

    sums, back, grads_v12, pos_a, grad_filters_a = edge_call(
        vector_kernel,
        atoms,
        tall,
        (scalars, rows, pos, w_value_filter[1], w_value_filter[2]),
        [
            ((3, R, atoms), F32),
            ((3, R, atoms), F32),
            ((atoms, LANES), BF16),
            ((8, atoms), F32),
            ((LANES, 2 * LANES), F32),
        ],
        [F32] * 8 + [BF16] + [F32] * 13,
        [
            (lambda r: (tall, LANES), F32),
            (lambda r: (3, r, LANES), F32),
            (lambda r: (r, LANES), F32),
        ],
    )
    scalar_sum, grads_qk, grads_v0, pos_b, grad_filters_b = edge_call(
        scalar_kernel,
        atoms,
        tall,
        (scalars, rows, pos, w_key_filter, w_value_filter[0], scalar_parts),
        [
            ((R, atoms), BF16),
            ((atoms, LANES), BF16),
            ((atoms, LANES), BF16),
            ((8, atoms), F32),
            ((LANES, 2 * LANES), F32),
        ],
        [F32] * 5 + [BF16] + [F32] * 10,
        [
            (lambda r: (2 * LANES, 2 * LANES), BF16),
            (lambda r: (r, LANES), F32),
            (lambda r: (2, r, 2 * LANES), BF16),
            (lambda r: (2, r, 2 * LANES), F32),
            (lambda r: (4, r, LANES), F32),
            (lambda r: (r, LANES), F32),
        ],
    )
    gathered = lax.all_gather(scalar_sum, "feat", axis=0, tiled=True)

    inputs = (
        scalars, features, stat, vectors, cot_features, cot_vectors, gathered, sums,
        grads_qk, grads_v0, grads_v12, pos_a, pos_b, mask, gain, bias,
        w_query, w_key, w_value, w_vector, w_output, grad_filters_a, grad_filters_b,
    )
    new_features, new_vectors, send, flat = pl.pallas_call(
        functools.partial(layer_kernel, atoms),
        out_shape=[
            jax.ShapeDtypeStruct((R, atoms), BF16),
            jax.ShapeDtypeStruct((3, R, atoms), BF16),
            jax.ShapeDtypeStruct((split, 4 * R + EXTRAS, atoms), BF16),
            jax.ShapeDtypeStruct((H, 12 * R), BF16),
        ],
        in_specs=[whole(pltpu.SMEM)] + [whole()] * (len(inputs) - 1),
        out_specs=[whole()] * 4,
        scratch_shapes=[
            pltpu.VMEM((H, 6 * R), BF16),
            pltpu.VMEM((H, 3 * R), BF16),
            pltpu.VMEM((3 * R, H), BF16),
            pltpu.VMEM((3 * R, H), BF16),
            pltpu.VMEM((H, 6 * R), F32),
            pltpu.VMEM((H, 3 * R), F32),
            pltpu.VMEM((H, 3 * R), F32),
        ],
        compiler_params=params(),
    )(*inputs)
    got = lax.all_to_all(send, "feat", 0, 0)
    share = H // count
    shares = lax.all_to_all(flat.reshape(count, share, 12 * R), "atoms", 0, 0)

    inputs = (
        scalars, got, features, stat, gain, cot_features, cot_vectors, back, mask,
    )
    grad_features, grad_vectors, grad_positions, small = pl.pallas_call(
        functools.partial(final_kernel, atoms),
        out_shape=[
            jax.ShapeDtypeStruct((R, atoms), F32),
            jax.ShapeDtypeStruct((3, R, atoms), F32),
            jax.ShapeDtypeStruct((3, atoms), F32),
            jax.ShapeDtypeStruct((8, 12 * R), F32),
        ],
        in_specs=[whole(pltpu.SMEM)] + [whole()] * (len(inputs) - 1),
        out_specs=[whole()] * 4,
        compiler_params=params(),
    )(*inputs)
    mine = jnp.concatenate([jnp.sum(shares.astype(F32), axis=0), small], axis=0)
    every = everywhere(mine, "atoms")
    shapes = [
        (1, R), (1, R), (H, R), (H, R), (3, H, R), (3, H, R), (3, H, R), (R, R), (3, R, R), (1, 8),
    ]
    grads = pl.pallas_call(
        functools.partial(unpack_kernel, share),
        out_shape=[jax.ShapeDtypeStruct(shape, F32) for shape in shapes],
        in_specs=[whole()],
        out_specs=[whole()] * len(shapes),
        compiler_params=params(),
    )(every)
    return (
        new_features,
        new_vectors,
        grad_features,
        grad_vectors,
        grad_positions,
        grads[0].reshape(R),
        grads[1].reshape(R),
        grads[2],
        grads[3],
        grads[4],
        grads[5],
        grads[6],
        grads[7],
        grads[8],
        grads[9][0, :4],
    )


def solution(mesh):
    in_specs = (
        P(None, "atoms"),
        P(None, None, "atoms"),
        P(None, "atoms"),
        P("atoms"),
        P(None, "atoms"),
        P(),
        P(),
        P(None, "feat"),
        P(None, "feat"),
        P(None, None, "feat"),
        P(None, None, "feat"),
        P(None, None, "feat"),
        P(None, "feat"),
        P(None, None, "feat"),
        P("feat", "atoms"),
        P(None, "feat", "atoms"),
    )
    out_specs = (
        P("feat", "atoms"),
        P(None, "feat", "atoms"),
        P("feat", "atoms"),
        P(None, "feat", "atoms"),
        P(None, "atoms"),
        P("feat"),
        P("feat"),
        P(None, "feat"),
        P(None, "feat"),
        P(None, None, "feat"),
        P(None, None, "feat"),
        P(None, None, "feat"),
        P(None, "feat"),
        P(None, None, "feat"),
        P(),
    )
    return jax.shard_map(
        per_device, mesh=mesh, in_specs=in_specs, out_specs=out_specs, check_vma=False
    )
```

```python
import functools
import math

import jax
import jax.numpy as jnp
from jax import lax
from jax.experimental import pallas as pl
from jax.experimental.pallas import tpu as pltpu
from jax.sharding import PartitionSpec as P

H = 256
HEADS = 8
HEAD = H // HEADS
R = 64
MOL = 29
HALO = 32
CUTOFF = 5.0
EPSILON = 1e-05
F32 = jnp.float32
BF16 = jnp.bfloat16

LANE_GROUPS = 2
ROW_GROUPS = 3
SPAN = 5
OFFSETS = 14
STEPS = SPAN + OFFSETS
SUB = 16
LANES = 128

QK, V0_COUNT, V12, VEC01, VEC2_COUNT, COT01, COT2 = range(7)
GROUP_ROWS = 352
EXTRAS = 16


def place(t, group):
    return lax.rem(t + SPAN * group, MOL)


def spread(source, first, second, start, molecules, rows):
    low = lax.broadcasted_iota(jnp.int32, (molecules, LANES), 1) < R

    def step(t, _):
        for g in range(ROW_GROUPS):
            a = source[pl.ds(start + place(t, 2 * g), molecules, stride=MOL), :]
            b = source[pl.ds(start + place(t, 2 * g + 1), molecules, stride=MOL), :]
            at = pl.ds(t * rows + g * molecules, molecules)
            if second is None:
                first[at, :] = jnp.where(low, a, b)
                continue
            first[at, :] = jnp.where(low, a, pltpu.roll(b, R, 1))
            second[at, :] = jnp.where(low, pltpu.roll(a, R, 1), b)
        return 0

    lax.fori_loop(0, STEPS, step, 0)


def clear_tails(ref, molecules, rows):
    left = rows - ROW_GROUPS * molecules
    for t in range(STEPS):
        at = t * rows + ROW_GROUPS * molecules
        if left:
            ref[at : at + left] = jnp.zeros((left, LANES), F32)


def collect(first, second, target, start, molecules, rows):
    low = lax.broadcasted_iota(jnp.int32, (molecules, LANES), 1) < R
    target[...] = jnp.zeros(target.shape, F32)

    def step(t, _):
        for g in range(ROW_GROUPS):
            at = pl.ds(t * rows + g * molecules, molecules)
            a = first[at, :]
            b = second[at, :]
            c = jnp.where(low, a, pltpu.roll(b, R, 1))
            d = jnp.where(low, pltpu.roll(a, R, 1), b)
            here = pl.ds(start + place(t, 2 * g), molecules, stride=MOL)
            target[here, :] = target[here, :] + c
            here = pl.ds(start + place(t, 2 * g + 1), molecules, stride=MOL)
            target[here, :] = target[here, :] + d
        return 0

    lax.fori_loop(0, STEPS, step, 0)


def row_masks(owned, start, molecules, rows, atoms):
    row = lax.broadcasted_iota(jnp.int32, (rows, LANES), 0)
    which = row
    for g in range(1, ROW_GROUPS):
        which = jnp.where(row >= g * molecules, row - g * molecules, which)
    first = start - HALO + which * MOL
    owned[...] = jnp.where((first >= 0) & (first < atoms), 1.0, 0.0)


def set_picks(picks):
    row = lax.broadcasted_iota(jnp.int32, (LANES, LANES), 0)
    lane = lax.broadcasted_iota(jnp.int32, (LANES, LANES), 1)
    base = jnp.where(lane >= R, R, 0)
    for n in range(2 * OFFSETS):
        which = 1 + n if n < OFFSETS else 33 + n - OFFSETS
        block = jnp.where(row == base + which, 1.0, 0.0).astype(BF16)
        picks[:, n * LANES : (n + 1) * LANES] = block


def set_multiplicities(count, target, molecules, rows):
    row = lax.broadcasted_iota(jnp.int32, (rows, LANES), 0)
    lane = lax.broadcasted_iota(jnp.int32, (rows, LANES), 1)
    inner = jnp.where(lane >= R, lane - R, lane)
    doubled = (row >= (ROW_GROUPS - 1) * molecules) & (lane >= R)
    for t in range(SPAN):
        value = jnp.where(inner < 32, count[t * rows : (t + 1) * rows], 0.0)
        for k in range(1, OFFSETS + 1):
            there = count[(t + k) * rows : (t + k + 1) * rows]
            value = jnp.where(inner == 32 + k, there, value)
        if t == SPAN - 1:
            value = jnp.where(doubled, 0.0, value)
        target[t * rows : (t + 1) * rows] = value.astype(BF16)


def dot(a, b):
    return jnp.dot(a, b, preferred_element_type=F32)


def dot_tn(a, b):
    return lax.dot_general(a, b, (((0,), (0,)), ((), ())), preferred_element_type=F32)


def dot_nt(a, b):
    return lax.dot_general(a, b, (((1,), (1,)), ((), ())), preferred_element_type=F32)


COSINE = (0.9999999998, -0.04934802137, 0.000405870916, -1.335212003e-06, 2.349373138e-09, -2.43963243e-12)

GEO_ENVELOPE, GEO_SLOPE, GEO_BEND, GEO_OWN, GEO_WAY = 0, 1, 2, 3, 4


def geometry(pos, t, rows, owned, radial, geo, inverses):
    lane = lax.broadcasted_iota(jnp.int32, (SUB, LANES), 1)
    centre = jnp.where(lane >= R, lane - R, lane).astype(F32)
    inv_space = (R - 1) / CUTOFF

    def step(k, _):
        for s in range(rows // SUB):
            o = s * SUB
            here = pl.ds(pl.multiple_of(k * rows + o, SUB), SUB)
            ii = pl.ds(pl.multiple_of(t * rows + o, SUB), SUB)
            jj = pl.ds(pl.multiple_of((t + 1 + k) * rows + o, SUB), SUB)
            off = [p[ii, :] - p[jj, :] for p in pos]
            square = off[0] * off[0] + off[1] * off[1] + off[2] * off[2]
            clamped = jnp.maximum(square, 0.01)
            inverse = lax.rsqrt(clamped)
            c = COSINE[-1]
            for term in COSINE[-2::-1]:
                c = c * clamped + term
            c = jnp.where(clamped < CUTOFF * CUTOFF, c, 0.0)
            envelope = c * c
            y = jnp.maximum(envelope - envelope * envelope, 1e-30)
            free = jnp.where(square > 0.01, 1.0, 0.0)
            bend = ((-math.pi / CUTOFF) * free) * (y * lax.rsqrt(y))
            u = (clamped * inverse) * inv_space - centre
            bump = jnp.exp(-0.5 * (u * u))
            value = bump * envelope
            high = value.astype(BF16)
            radial[here, :LANES] = high
            radial[here, LANES:] = (value - high.astype(F32)).astype(BF16)
            geo[GEO_OWN, here, :] = (value * owned[o : o + SUB]).astype(BF16)
            slope = bump * bend - (inv_space * free) * (u * value)
            geo[GEO_SLOPE, here, :] = slope.astype(BF16)
            geo[GEO_BEND, here, :] = bend.astype(BF16)
            geo[GEO_ENVELOPE, here, :] = envelope.astype(BF16)
            for d in range(3):
                geo[GEO_WAY + d, here, :] = (off[d] * inverse).astype(BF16)
            inverses[0, here, :] = inverse.astype(BF16)
            inverses[1, here, :] = (inverse * free).astype(BF16)
        return 0

    lax.fori_loop(0, OFFSETS, step, 0)


def set_filters(weights_ref, filter_1, filter_2):
    weights_ref[...] = jnp.zeros(weights_ref.shape, BF16)
    for f, ref in enumerate((filter_1, filter_2)):
        half = ref[...] * jnp.asarray(0.5, BF16)
        for part in range(2):
            for g in range(LANE_GROUPS):
                down = part * LANES + g * R
                at = f * LANES + g * R
                weights_ref[down : down + R, at : at + R] = half


def spread_positions(pos_ref, loose, targets, start, molecules, rows):
    for d, target in enumerate(targets):
        clear_tails(target, molecules, rows)
        loose[...] = jnp.broadcast_to(pos_ref[:, d : d + 1], loose.shape)
        spread(loose, target, None, start, molecules, rows)


def add_rows(ref, rows, value):
    ref[rows, :] = ref[rows, :] + value


def gate(h):
    t = jnp.tanh(h)
    u = 1.0 + t
    f = h * u
    return f.astype(BF16), (u + f * (1.0 - t)).astype(BF16)


def total_of(partner, first, t_rows, target):
    target[...] = partner[...].astype(F32)
    target[:t_rows] = target[:t_rows] + first[...]


def carried(rows, t, totals, body):
    def outer(s, _):
        o = pl.multiple_of(s * SUB, SUB)
        base = pl.multiple_of(t * rows + o, SUB)
        ii = pl.ds(base, SUB)
        sums = None
        for k in range(0, OFFSETS, 2):
            pair = []
            for n in (k, k + 1):
                here = pl.ds(o + n * rows, SUB)
                pair.append(body(o, here, ii, pl.ds(base + (1 + n) * rows, SUB), n))
            both = [(x + y).astype(F32) for x, y in zip(*pair)]
            sums = both if sums is None else [x + y for x, y in zip(sums, both)]
        for total, value in zip(totals, sums):
            total[ii, :] = value
        return 0

    lax.fori_loop(0, rows // SUB, outer, 0)


def lanes_of(n):
    return slice(n * LANES, (n + 1) * LANES)


def vector_kernel(
    molecules, rows, atoms,
    scalars, pairs_ref, pos_ref, filter_1, filter_2,
    sums_ref, back_ref, grads_ref, pos_out, grad_w_ref, radial_out, geo_out,
    weights_ref, picks, many, owned, loose, loose2, tall_a, tall_b, counts, pre, grad_pre,
    grad_radial, inverses, grad_ways,
    px, py, pz, w0, w1, w2, v2, c0, c1, c2,
    s0, s1, s2, a0, a1, a2, gv, gx, gy, gz,
    fs0, fs1, fs2, fa0, fa1, fa2, fgv, fgx, fgy, fgz,
):
    t = pl.program_id(0)
    start = scalars[0]
    own = slice(HALO, HALO + atoms)
    radial, geo = radial_out.at[0], geo_out.at[0]
    w, c, g_pos = (w0, w1, w2), (c0, c1, c2), (gx, gy, gz)
    sums, backs = (s0, s1, s2), (a0, a1, a2)

    @pl.when(t == 0)
    def _():
        set_filters(weights_ref, filter_1, filter_2)
        set_picks(picks)
        row_masks(owned, start, molecules, rows, atoms)
        v12 = pairs_ref[V12].astype(F32)
        low = lax.broadcasted_iota(jnp.int32, v12.shape, 1) < R
        v11 = jnp.where(low, v12, pltpu.roll(v12, R, 1))
        clear_tails(tall_a, molecules, rows)
        clear_tails(tall_b, molecules, rows)

        def place_pair(first, second):
            spread(loose, tall_a, tall_b, start, molecules, rows)
            first[...] = tall_a[...].astype(BF16)
            if second is not None:
                second[...] = tall_b[...].astype(BF16)

        loose[...] = pairs_ref[VEC01].astype(F32) * v11
        place_pair(w0, w1)
        third = pairs_ref[VEC2_COUNT].astype(F32)
        loose[...] = jnp.where(low, third * v11, v12)
        place_pair(w2, v2)
        loose[...] = pairs_ref[COT01].astype(F32)
        place_pair(c0, c1)
        loose[...] = jnp.where(low, pairs_ref[COT2].astype(F32), third)
        place_pair(c2, None)
        set_multiplicities(tall_b, many, molecules, rows)
        spread_positions(pos_ref, loose, (px, py, pz), start, molecules, rows)
        for total in (s0, s1, s2, a0, a1, a2, gv, gx, gy, gz):
            total[...] = jnp.zeros(total.shape, BF16)
        grad_w_ref[...] = jnp.zeros(grad_w_ref.shape, F32)

    counts[...] = dot(many[pl.ds(pl.multiple_of(t * rows, SUB), rows), :], picks[...])
    geometry((px, py, pz), t, rows, owned, radial, geo, inverses)
    pre[...] = dot(radial[...], weights_ref[...])

    def channel(o, here, ii, jj, k):
        f1, d1 = gate(pre[here, :LANES])
        f2, d2 = gate(pre[here, LANES:])
        mi = counts[pl.ds(o, SUB), lanes_of(k)].astype(BF16)
        mj = counts[pl.ds(o, SUB), lanes_of(OFFSETS + k)].astype(BF16)
        f1i, f1j, f2i, f2j = f1 * mi, f1 * mj, f2 * mi, f2 * mj
        v2i, v2j = v2[ii, :], v2[jj, :]
        msg_i, msg_j = f2i * v2j, f2j * v2i
        along_i = along_j = across_i = across_j = None
        sum_i, back_i = [], []
        for d in range(3):
            way = geo[GEO_WAY + d, here, :]
            wi, wj = w[d][ii, :], w[d][jj, :]
            ci, cj = c[d][ii, :], c[d][jj, :]
            sum_i.append(f1i * wj + msg_i * way)
            add_rows(sums[d], jj, f1j * wi - msg_j * way)
            add_rows(backs[d], jj, f1i * ci)
            back_i.append(f1j * cj)
            grad_ways[d, here, :] = ci * msg_i - cj * msg_j
            new = (ci * way, cj * way, ci * wj, cj * wi)
            if d == 0:
                along_i, along_j, across_i, across_j = new
            else:
                along_i, along_j = along_i + new[0], along_j + new[1]
                across_i, across_j = across_i + new[2], across_j + new[3]
        add_rows(gv, jj, f2i * along_i)
        g1 = mi * across_i + mj * across_j
        g2 = mi * along_i * v2j - mj * along_j * v2i
        grad_pre[here, :LANES] = g1 * d1
        grad_pre[here, LANES:] = g2 * d2
        return sum_i + back_i + [-(f2j * along_j)]

    carried(rows, t, (fs0, fs1, fs2, fa0, fa1, fa2, fgv), channel)
    grad_radial[...] = dot_nt(grad_pre[...], weights_ref[:LANES])
    grad_w_ref[...] = grad_w_ref[...] + dot_tn(geo[GEO_OWN], grad_pre[...])

    def turn(o, here, ii, jj, k):
        ways = [geo[GEO_WAY + d, here, :] for d in range(3)]
        grads = [grad_ways[d, here, :] for d in range(3)]
        along = ways[0] * grads[0] + ways[1] * grads[1] + ways[2] * grads[2]
        pull = grad_radial[here, :].astype(BF16) * geo[GEO_SLOPE, here, :]
        pull = pull - inverses[1, here, :] * along
        out = []
        for d in range(3):
            g = grads[d] * inverses[0, here, :] + ways[d] * pull
            add_rows(g_pos[d], jj, -g)
            out.append(g)
        return out

    carried(rows, t, (fgx, fgy, fgz), turn)

    @pl.when(t == SPAN - 1)
    def _():
        low = lax.broadcasted_iota(jnp.int32, (atoms, LANES), 1) < R

        def gather_pair(one, two, target):
            total_of(one[0], one[1], SPAN * rows, tall_a)
            total_of(two[0], two[1], SPAN * rows, tall_b)
            collect(tall_a, tall_b, target, start, molecules, rows)

        gather_pair((s0, fs0), (s1, fs1), loose)
        both = loose[own].T
        sums_ref[0] = both[:R]
        sums_ref[1] = both[R:]
        gather_pair((s2, fs2), (gv, fgv), loose)
        both = loose[own].T
        sums_ref[2] = both[:R]
        grads_ref[R:] = both[R:].astype(BF16)
        gather_pair((a0, fa0), (a1, fa1), loose2)
        v12 = pairs_ref[V12, own].astype(F32)
        v11 = jnp.where(low, v12, pltpu.roll(v12, R, 1))
        both = (loose2[own] * v11).T
        back_ref[0] = both[:R]
        back_ref[1] = both[R:]
        partial = loose2[own] * pairs_ref[VEC01, own].astype(F32)
        partial = partial + pltpu.roll(partial, R, 1)
        gather_pair((a2, fa2), (gx, fgx), loose2)
        back_ref[2] = (loose2[own] * v11).T[:R]
        partial = partial + loose2[own] * pairs_ref[VEC2_COUNT, own].astype(F32)
        grads_ref[:R] = partial.T[:R].astype(BF16)
        pos_out[...] = jnp.zeros(pos_out.shape, F32)
        pos_out[0:1] = jnp.sum(loose2[own].T[R:], axis=0, keepdims=True)
        gather_pair((gy, fgy), (gz, fgz), loose)
        both = loose[own].T
        pos_out[1:2] = jnp.sum(both[:R], axis=0, keepdims=True)
        pos_out[2:3] = jnp.sum(both[R:], axis=0, keepdims=True)


def scalar_kernel(
    molecules, rows, atoms,
    scalars, pairs_ref, filter_1, filter_2, scalar_parts, radial_in, geo_in,
    sum_ref, grads_ref, pos_out, grad_w_ref,
    weights_ref, picks, many, heads_ref, loose, tall_a, tall_b, counts, pre, grad_pre,
    grad_radial, products, sums, gates, bends,
    q, key, v0, gs,
    ss, gq, gk, g0, gx, gy, gz,
    fss, fgq, fgk, fg0, fgx, fgy, fgz,
):
    t = pl.program_id(0)
    start = scalars[0]
    own = slice(HALO, HALO + atoms)
    radial, geo = radial_in.at[0], geo_in.at[0]
    g_pos = (gx, gy, gz)

    @pl.when(t == 0)
    def _():
        set_filters(weights_ref, filter_1, filter_2)
        set_picks(picks)
        row = lax.broadcasted_iota(jnp.int32, (2 * LANES, 2 * LANES), 0)
        lane = lax.broadcasted_iota(jnp.int32, (2 * LANES, 2 * LANES), 1)
        heads_ref[...] = jnp.where(row // HEAD == lane // HEAD, 1.0, 0.0).astype(BF16)
        clear_tails(tall_a, molecules, rows)
        clear_tails(tall_b, molecules, rows)

        def place_pair(first, second):
            spread(loose, tall_a, tall_b, start, molecules, rows)
            first[...] = tall_a[...].astype(BF16)
            if second is not None:
                second[...] = tall_b[...].astype(BF16)

        loose[...] = pairs_ref[QK].astype(F32)
        place_pair(q, key)
        loose[...] = pairs_ref[V0_COUNT].astype(F32)
        place_pair(v0, None)
        set_multiplicities(tall_b, many, molecules, rows)
        summed = scalar_parts[0].astype(F32)
        for f in range(1, scalar_parts.shape[0]):
            summed = summed + scalar_parts[f].astype(F32)
        summed = jnp.concatenate([summed, jnp.zeros_like(summed)], axis=0).T
        loose[own] = summed[:atoms]
        loose[:HALO] = summed[atoms : atoms + HALO]
        loose[HALO + atoms : 2 * HALO + atoms] = summed[atoms + HALO : atoms + 2 * HALO]
        loose[2 * HALO + atoms :] = jnp.zeros((loose.shape[0] - 2 * HALO - atoms, LANES), F32)
        place_pair(gs, None)
        for total in (ss, gq, gk, g0, gx, gy, gz):
            total[...] = jnp.zeros(total.shape, BF16)
        grad_w_ref[...] = jnp.zeros(grad_w_ref.shape, F32)

    counts[...] = dot(many[pl.ds(pl.multiple_of(t * rows, SUB), rows), :], picks[...])
    pre[...] = dot(radial[...], weights_ref[...])

    def multiply(k, _):
        for s in range(rows // SUB):
            o = s * SUB
            here = pl.ds(pl.multiple_of(k * rows + o, SUB), SUB)
            ii = pl.ds(pl.multiple_of(t * rows + o, SUB), SUB)
            jj = pl.ds(pl.multiple_of((t + 1 + k) * rows + o, SUB), SUB)
            fk, dk = gate(pre[here, :LANES])
            f0, d0 = gate(pre[here, LANES:])
            gates[0, here, :] = fk
            gates[1, here, :] = f0
            gates[2, here, :] = dk
            gates[3, here, :] = d0
            products[0, here, :LANES] = q[ii, :] * key[jj, :] * fk
            products[0, here, LANES:] = q[jj, :] * key[ii, :] * fk
            products[1, here, :LANES] = gs[ii, :] * v0[jj, :] * f0
            products[1, here, LANES:] = gs[jj, :] * v0[ii, :] * f0
        return 0

    lax.fori_loop(0, OFFSETS, multiply, 0)
    sums[0] = dot(products[0], heads_ref[...])
    sums[1] = dot(products[1], heads_ref[...])

    def channel(o, here, ii, jj, k):
        fk, f0 = gates[0, here, :], gates[1, here, :]
        envelope = geo[GEO_ENVELOPE, here, :]
        kept = []
        grad_k = grad_0 = steep = None
        for side in range(2):
            lanes = slice(side * LANES, (side + 1) * LANES)
            m = counts[pl.ds(o, SUB), lanes_of(side * OFFSETS + k)].astype(BF16)
            half = 0.5 * sums[0, here, lanes]
            g_att = sums[1, here, lanes].astype(BF16)
            act, rise = gate(half)
            weight = m * envelope
            att = act * weight
            g_score = g_att * (0.5 * rise) * weight
            lift = m * (g_att * act)
            bv, dv = f0 * att, fk * g_score
            h, o_ = (ii, jj) if side == 0 else (jj, ii)
            qh, kt, gh, vt = q[h, :], key[o_, :], gs[h, :], v0[o_, :]
            gives = (vt * bv, kt * dv, gh * bv, qh * dv)
            new_k, new_0 = qh * kt * g_score, gh * vt * att
            if side == 0:
                kept = [gives[0], gives[1], None, None]
                add_rows(g0, jj, gives[2])
                add_rows(gk, jj, gives[3])
                grad_k, grad_0, steep = new_k, new_0, lift
            else:
                add_rows(ss, jj, gives[0])
                add_rows(gq, jj, gives[1])
                kept[2], kept[3] = gives[2], gives[3]
                grad_k, grad_0, steep = grad_k + new_k, grad_0 + new_0, steep + lift
        grad_pre[here, :LANES] = grad_k * gates[2, here, :]
        grad_pre[here, LANES:] = grad_0 * gates[3, here, :]
        bends[here, :] = steep * geo[GEO_BEND, here, :] * (1.0 / HEAD)
        return kept

    carried(rows, t, (fss, fgq, fg0, fgk), channel)
    grad_radial[...] = dot_nt(grad_pre[...], weights_ref[:LANES])
    grad_w_ref[...] = grad_w_ref[...] + dot_tn(geo[GEO_OWN], grad_pre[...])

    def turn(o, here, ii, jj, k):
        pull = grad_radial[here, :].astype(BF16) * geo[GEO_SLOPE, here, :] + bends[here, :]
        out = []
        for d in range(3):
            g = geo[GEO_WAY + d, here, :] * pull
            add_rows(g_pos[d], jj, -g)
            out.append(g)
        return out

    carried(rows, t, (fgx, fgy, fgz), turn)

    @pl.when(t == SPAN - 1)
    def _():
        def gather_pair(one, two):
            total_of(one[0], one[1], SPAN * rows, tall_a)
            total_of(two[0], two[1], SPAN * rows, tall_b)
            collect(tall_a, tall_b, loose, start, molecules, rows)
            return loose[own].T

        both = gather_pair((ss, fss), (g0, fg0))
        sum_ref[...] = both[:R].astype(BF16)
        grads_ref[2 * R :] = both[R:].astype(BF16)
        both = gather_pair((gq, fgq), (gk, fgk))
        grads_ref[: 2 * R] = both.astype(BF16)
        pos_out[...] = jnp.zeros(pos_out.shape, F32)
        both = gather_pair((gx, fgx), (gy, fgy))
        pos_out[0:1] = jnp.sum(both[:R], axis=0, keepdims=True)
        pos_out[1:2] = jnp.sum(both[R:], axis=0, keepdims=True)
        both = gather_pair((gz, fgz), (gz, fgz))
        pos_out[2:3] = jnp.sum(both[:R], axis=0, keepdims=True)


def whole(memory=pltpu.VMEM):
    return pl.BlockSpec(memory_space=memory)


def params(mib=60):
    return pltpu.CompilerParams(vmem_limit_bytes=mib * 1024 * 1024)


def edge_sizes(atoms):
    molecules = (atoms + 2 * (MOL - 1)) // MOL
    rows = -(-ROW_GROUPS * molecules // SUB) * SUB
    tall = -(-(HALO + molecules * MOL) // SUB) * SUB
    return molecules, rows, tall


def by_step(shape):
    zeros = (0,) * (len(shape) - 1)
    return pl.BlockSpec((1,) + shape[1:], lambda t: (t,) + zeros)


def fixed(shape):
    zeros = (0,) * len(shape)
    return pl.BlockSpec(shape, lambda t: zeros)


def edge_call(kernel, atoms, inputs, stepped_in, outs, stepped_out, scratch):
    molecules, rows, _ = edge_sizes(atoms)
    return pl.pallas_call(
        functools.partial(kernel, molecules, rows, atoms),
        grid=(SPAN,),
        out_shape=[jax.ShapeDtypeStruct(s, kind) for s, kind in outs + stepped_out],
        in_specs=[whole(pltpu.SMEM)]
        + [fixed(x.shape) for x in inputs[1:]]
        + [by_step(x.shape) for x in stepped_in],
        out_specs=[fixed(s) for s, _ in outs] + [by_step(s) for s, _ in stepped_out],
        scratch_shapes=[pltpu.VMEM(s, kind) for s, kind in scratch],
        compiler_params=params(),
    )(*inputs, *stepped_in)


def shared_scratch(atoms):
    _, rows, tall = edge_sizes(atoms)
    batch = OFFSETS * rows
    high = STEPS * rows
    return {
        "weights": ((2 * LANES, 2 * LANES), BF16),
        "picks": ((LANES, 2 * OFFSETS * LANES), BF16),
        "many": ((SPAN * rows, LANES), BF16),
        "mask": ((rows, LANES), F32),
        "loose": ((tall, LANES), F32),
        "tall": ((high, LANES), F32),
        "low": ((high, LANES), BF16),
        "first": ((SPAN * rows, LANES), F32),
        "counts": ((rows, 2 * OFFSETS * LANES), F32),
        "pre": ((batch, 2 * LANES), F32),
        "grad_pre": ((batch, 2 * LANES), BF16),
        "line": ((batch, LANES), F32),
        "line2": ((2, batch, LANES), BF16),
        "line3": ((3, batch, LANES), BF16),
        "line4": ((4, batch, LANES), BF16),
        "line1": ((batch, LANES), BF16),
        "wide2": ((2, batch, 2 * LANES), BF16),
        "wide2f": ((2, batch, 2 * LANES), F32),
    }


def offsets_in_block(neighbours, mask, first):
    lane = lax.broadcasted_iota(jnp.int32, neighbours.shape, 1)
    diff = neighbours - (first + lane)
    return jnp.where(diff < 0, diff + MOL, diff) * mask


def pieces(x):
    a = x.astype(BF16)
    rest = x - a.astype(F32)
    b = rest.astype(BF16)
    return a, b, (rest - b.astype(F32)).astype(BF16)


def edge_groups(features, vectors, cot_f, cot_v, neighbours, mask, positions, first):
    diff = offsets_in_block(neighbours[...], mask[...], first).astype(F32).astype(BF16)
    groups = [jnp.concatenate([features[...], cot_f[...], diff], axis=0)]
    for d in range(3):
        rows = [x.astype(F32) for x in pieces(positions[d : d + 1])]
        rows = jnp.concatenate(rows + [jnp.zeros((29, LANES), F32)], axis=0).astype(BF16)
        groups.append(jnp.concatenate([vectors[d], cot_v[d], rows], axis=0))
    return groups


def halo_kernel(atoms, scalars, *refs):
    row_first = scalars[2]
    lane = lax.broadcasted_iota(jnp.int32, (GROUP_ROWS, LANES), 1)
    for end, at, out in ((0, atoms - LANES, refs[14]), (1, 0, refs[15])):
        groups = edge_groups(*refs[7 * end : 7 * end + 7], row_first + at)
        total = None
        for g, group in enumerate(groups):
            by = (HALO * (g + 1) if end == 0 else HALO * g) % LANES
            moved = group.astype(F32)
            moved = pltpu.roll(moved, by, 1) if by else moved
            total = moved if total is None else jnp.where(lane >= HALO * g, moved, total)
        out[...] = total.astype(BF16)


def halo_call(atoms, scalars, arrays):
    specs = []
    for at in (atoms // LANES - 1, 0):
        for x in arrays:
            shape = x.shape[:-1] + (LANES,)
            index = (0,) * (x.ndim - 1) + (at,)
            specs.append(pl.BlockSpec(shape, lambda *_, index=index: index))
    out = jax.ShapeDtypeStruct((GROUP_ROWS, LANES), BF16)
    return pl.pallas_call(
        functools.partial(halo_kernel, atoms),
        grid=(1,),
        out_shape=[out, out],
        in_specs=[whole(pltpu.SMEM)] + specs,
        out_specs=[whole(), whole()],
        compiler_params=params(),
    )(scalars, *arrays, *arrays)


def column(row):
    return jnp.broadcast_to(row, (8, row.shape[1])).T[:, :1]


def normalised(f):
    mean = jnp.mean(f, axis=0, keepdims=True)
    centred = f - mean
    inv = lax.rsqrt(jnp.mean(centred * centred, axis=0, keepdims=True) + EPSILON)
    return centred * inv, mean, inv


def dense_kernel(
    atoms,
    scalars, features, vectors, cot_f, cot_v, neighbours, mask, positions, low_ref, high_ref,
    gain_ref, bias_ref, w_query, w_key, w_value, w_vector, w_output,
    rows_ref, pos_ref, part_ref, stat_ref,
    w_qk, w_v0, w_v12, w_vec_t, w_out,
):
    chan_first = pl.multiple_of(scalars[1], R)
    row_first = scalars[2]
    gain, bias = column(gain_ref[...]), column(bias_ref[...])
    w_qk[:R] = w_query[...]
    w_qk[R:] = w_key[...]
    w_v0[:R] = w_value[0]
    w_v0[R:] = jnp.zeros((R, H), BF16)
    w_v12[:R] = w_value[1]
    w_v12[R:] = w_value[2]
    for p in range(3):
        w_vec_t[p * R : (p + 1) * R] = w_vector[p]
    w_out[...] = jnp.concatenate([w_output[p] for p in range(3)], axis=0).astype(F32).T.astype(BF16)

    def block(f, v, cf, cv, own_v, diff, pos):
        width = f.shape[1]
        normed, mean, inv = normalised(f)
        turned = (normed * gain + bias).T.astype(BF16)
        kinds = lax.broadcasted_iota(jnp.int32, (R, width), 0)
        kinds = jnp.where(kinds < 32, kinds, MOL + 32 - kinds).astype(F32)
        counts = jnp.zeros((R, width), F32)
        for s in range(diff.shape[0]):
            counts = counts + jnp.where(diff[s : s + 1] == kinds, 1.0, 0.0)
        none = jnp.zeros((R, width), F32)
        counts = jnp.concatenate([none, counts], axis=0).T
        pairs = [None] * 7
        pairs[QK] = dot_nt(turned, w_qk[...])
        pairs[V0_COUNT] = dot_nt(turned, w_v0[...]) + counts
        pairs[V12] = dot_nt(turned, w_v12[...])
        pairs[VEC01] = jnp.concatenate([own_v[0], own_v[1]], axis=0).T
        pairs[VEC2_COUNT] = jnp.concatenate([own_v[2], none], axis=0).T + counts
        pairs[COT01] = jnp.concatenate([cv[0], cv[1]], axis=0).T
        pairs[COT2] = jnp.concatenate([cv[2], none], axis=0).T
        place3 = jnp.concatenate([pos, jnp.zeros((LANES - 3, width), F32)], axis=0).T
        vec_dot = grad_0 = 0.0
        for d in range(3):
            proj = dot(w_vec_t[...], v[d])
            vec_dot = vec_dot + proj[:R] * proj[R : 2 * R]
            grad_0 = grad_0 + cv[d] * proj[2 * R :]
        grad_out = jnp.concatenate([grad_0, cf * vec_dot, cf], axis=0).astype(BF16)
        part = dot(w_out[...], grad_out)
        return [x.astype(BF16) for x in pairs], place3, part.astype(BF16), mean, inv

    wide = 2 * LANES

    def step(b, _):
        at = pl.multiple_of(b * wide, wide)
        here = pl.ds(at, wide)
        own_v = [vectors[d, pl.ds(chan_first, R), here].astype(F32) for d in range(3)]
        diff = offsets_in_block(neighbours[:, here], mask[:, here], row_first + at)
        pairs, place3, part, mean, inv = block(
            features[:, here].astype(F32),
            [vectors[d, :, here] for d in range(3)],
            cot_f[:, here].astype(F32),
            [cot_v[d, :, here].astype(F32) for d in range(3)],
            own_v,
            diff.astype(F32),
            positions[:, here],
        )
        there = pl.ds(pl.multiple_of(HALO + at, 2 * SUB), wide)
        for n, pair in enumerate(pairs):
            rows_ref[n, there, :] = pair
        pos_ref[there, :] = place3
        part_ref[:, here] = part
        stat_ref[0:1, here] = mean
        stat_ref[1:2, here] = inv
        return 0

    lax.fori_loop(0, atoms // wide, step, 0)

    lane = lax.broadcasted_iota(jnp.int32, (GROUP_ROWS, LANES), 1)
    packed_low, packed_high = low_ref[...].astype(F32), high_ref[...].astype(F32)
    groups = []
    for g in range(4):
        a = pltpu.roll(packed_low, (LANES - HALO * g) % LANES, 1) if g else packed_low
        by = (LANES + HALO - HALO * g) % LANES
        b = pltpu.roll(packed_high, by, 1) if by else packed_high
        both = jnp.where(lane < HALO, a, jnp.where(lane < 2 * HALO, b, 0.0))
        groups.append(both)
    pick_rows = lax.broadcasted_iota(jnp.int32, (H, LANES), 0)
    own_v, pos = [], []
    for d in range(3):
        g = groups[1 + d]
        found = g[:R]
        for f in range(1, H // R):
            found = jnp.where(chan_first == f * R, g[f * R : (f + 1) * R], found)
        own_v.append(found)
        pos.append(g[320:321] + g[321:322] + g[322:323])
    pairs, place3, part, _, _ = block(
        groups[0][:H],
        [groups[1 + d][:H].astype(BF16) for d in range(3)],
        groups[0][H : H + R],
        [groups[1 + d][H : H + R] for d in range(3)],
        own_v,
        groups[0][H + R :],
        jnp.concatenate(pos, axis=0),
    )
    high = HALO + atoms
    tall = rows_ref.shape[1]
    for n, pair in enumerate(pairs):
        rows_ref[n, :HALO] = pair[:HALO]
        rows_ref[n, high : high + HALO] = pair[HALO : 2 * HALO]
        rows_ref[n, high + HALO :] = jnp.zeros((tall - high - HALO, LANES), BF16)
    pos_ref[:HALO] = place3[:HALO]
    pos_ref[high : high + HALO] = place3[HALO : 2 * HALO]
    pos_ref[high + HALO :] = jnp.zeros((tall - high - HALO, LANES), F32)
    part_ref[:, atoms:] = part


def both_diagonals(grad, f):
    at = f * LANES
    return 0.5 * (grad[:R, at : at + R] + grad[R:, at + R : at + LANES])


def layer_kernel(
    atoms,
    scalars, features, stat, vectors, cot_f, cot_v, gathered, sums_ref,
    grads_b, grads_a, pos_a, pos_b, mask, gain_ref, bias_ref,
    w_query, w_key, w_value, w_vector, w_output, grad_filters_a, grad_filters_b,
    feat_out, vec_out, send_ref, flat_ref,
    w_five, w_vec, w_vec_t, w_out_t, t_five, t_vec, t_out,
):
    chan_first = pl.multiple_of(scalars[1], R)
    gain, bias = column(gain_ref[...]), column(bias_ref[...])
    five = [w_query[...], w_key[...]] + [w_value[p] for p in range(3)]
    w_five[...] = jnp.concatenate(five, axis=0).astype(F32).T.astype(BF16)
    for p in range(3):
        w_vec_t[p * R : (p + 1) * R] = w_vector[p]
        w_out_t[p * R : (p + 1) * R] = w_output[p]
    w_vec[...] = w_vec_t[...].astype(F32).T.astype(BF16)
    t_five[...] = jnp.zeros(t_five.shape, F32)
    t_vec[...] = jnp.zeros(t_vec.shape, F32)
    t_out[...] = jnp.zeros(t_out.shape, F32)
    wide = 2 * LANES
    split = send_ref.shape[0]

    def step(b, _):
        at = pl.multiple_of(b * wide, wide)
        here = pl.ds(at, wide)
        real = mask[:, here].astype(F32)
        all_sums = gathered[:, here]
        outputs = dot(w_out_t[...], all_sums)
        out_0, out_1, out_2 = outputs[:R], outputs[R : 2 * R], outputs[2 * R :]
        cf = cot_f[:, here].astype(F32)
        grad_dot = cf * out_1
        vec_dot = grad_0 = square_v = square_dv = 0.0
        for d in range(3):
            proj = dot(w_vec_t[...], vectors[d, :, here])
            first, second, third = proj[:R], proj[R : 2 * R], proj[2 * R :]
            cv = cot_v[d, :, here].astype(F32)
            vec_dot = vec_dot + first * second
            grad_0 = grad_0 + cv * third
            delta = third * out_0 + sums_ref[d, :, here]
            moved = vectors[d, pl.ds(chan_first, R), here].astype(F32) + delta
            vec_out[d, :, here] = moved.astype(BF16)
            square_v = square_v + moved * moved
            square_dv = square_dv + delta * delta
            grad_proj = jnp.concatenate(
                [grad_dot * second, grad_dot * first, cv * out_0], axis=0
            ).astype(BF16)
            part = dot(w_vec[...], grad_proj).astype(BF16)
            for f in range(split):
                send_ref[f, (1 + d) * R : (2 + d) * R, here] = part[f * R : (f + 1) * R]
            t_vec[...] = t_vec[...] + dot_nt(grad_proj, vectors[d, :, here])
        delta = vec_dot * out_1 + out_2
        moved = features[pl.ds(chan_first, R), here].astype(F32) + delta
        feat_out[:, here] = moved.astype(BF16)
        grad_out = jnp.concatenate([grad_0, cf * vec_dot, cf], axis=0).astype(BF16)
        t_out[...] = t_out[...] + dot_nt(grad_out, all_sums)
        normed = (features[:, here].astype(F32) - stat[0:1, here]) * stat[1:2, here]
        normal = (normed * gain + bias).astype(BF16)
        grads = jnp.concatenate([grads_b[:, here], grads_a[:, here]], axis=0)
        t_five[...] = t_five[...] + dot_nt(grads, normal)
        part = dot(w_five[...], grads)
        rounded = part.astype(BF16)
        for f in range(split):
            send_ref[f, :R, here] = rounded[f * R : (f + 1) * R]
        hat = part * gain
        tops = [
            jnp.sum(hat, axis=0, keepdims=True),
            jnp.sum(hat * normed, axis=0, keepdims=True),
        ]
        exact = [pos_a[d : d + 1, here] + pos_b[d : d + 1, here] for d in range(3)]
        for x in (moved, delta):
            exact.append(jnp.sum(x * x, axis=0, keepdims=True) * real)
        for x in (square_v, square_dv):
            exact.append(jnp.sum(x, axis=0, keepdims=True) * real)
        heads = [x.astype(BF16).astype(F32) for x in exact]
        tops = tops + heads + [x - y for x, y in zip(exact, heads)]
        tops = jnp.concatenate(tops, axis=0).astype(BF16)
        for f in range(split):
            send_ref[f, 4 * R :, here] = tops
        return 0

    lax.fori_loop(0, atoms // wide, step, 0)
    grad_a, grad_b = grad_filters_a[...], grad_filters_b[...]
    filters = [both_diagonals(g, f) for g in (grad_b, grad_a) for f in range(2)]
    flat_ref[: 5 * R] = t_five[...].astype(BF16)
    flat_ref[5 * R : 8 * R] = t_vec[...].astype(BF16)
    flat_ref[8 * R : 11 * R] = t_out[...].astype(BF16)
    flat_ref[11 * R :] = jnp.concatenate(filters, axis=1).astype(BF16)


def final_kernel(
    atoms,
    scalars, got, features, stat, gain_ref, cot_f, cot_v, back_ref, mask,
    grad_feat, grad_vec, grad_pos, small_ref,
):
    chan_first = pl.multiple_of(scalars[1], R)
    whole_gain = column(gain_ref[...])
    gain = whole_gain[:R]
    for f in range(1, H // R):
        gain = jnp.where(chan_first == f * R, whole_gain[f * R : (f + 1) * R], gain)

    def summed(rows):
        total = got[0, rows].astype(F32)
        for f in range(1, got.shape[0]):
            total = total + got[f, rows].astype(F32)
        return total

    tops = summed(slice(4 * R, 4 * R + EXTRAS))
    grad_normal = summed(slice(0, R))
    inv = stat[1:2]
    normed = (features[pl.ds(chan_first, R), :].astype(F32) - stat[0:1]) * inv
    inner = grad_normal * gain - tops[0:1] * (1.0 / H) - normed * (tops[1:2] * (1.0 / H))
    grad_feat[...] = cot_f[...].astype(F32) + inv * inner
    for d in range(3):
        part = summed(slice((1 + d) * R, (2 + d) * R))
        grad_vec[d] = cot_v[d].astype(F32) + part + back_ref[d]
    exact = tops[2:9] + tops[9:16]
    grad_pos[...] = exact[:3]
    ones = jnp.ones((8, atoms), BF16)
    small_ref[...] = jnp.zeros(small_ref.shape, F32)
    small_ref[:, :R] = dot_nt(ones, (grad_normal * normed).astype(BF16))
    small_ref[:, R : 2 * R] = dot_nt(ones, grad_normal.astype(BF16))
    totals = jnp.sum(exact[3:7], axis=1, keepdims=True)
    small_ref[0:4, LANES : 2 * LANES] = jnp.broadcast_to(totals, (4, LANES))
    real = jnp.sum(mask[...].astype(F32), axis=1, keepdims=True)
    small_ref[4:5, LANES : 2 * LANES] = jnp.broadcast_to(real, (1, LANES))


def unpack_kernel(
    share,
    got,
    g_gain, g_bias, g_query, g_key, g_value, g_vector, g_output, g_key_f, g_value_f, rms_ref,
):
    total = got[0, share:]
    for n in range(1, got.shape[0]):
        total = total + got[n, share:]
    g_gain[...] = total[0:1, :R]
    g_bias[...] = total[0:1, R : 2 * R]
    numbers = total[:, LANES : LANES + 1]
    size = jnp.where(lax.broadcasted_iota(jnp.int32, (8, 1), 0) < 2, 1.0, 3.0) * H
    rms = jnp.sqrt(numbers / (numbers[4:5] * size) + 1e-06)
    rms_ref[...] = jnp.broadcast_to(rms, (8, LANES)).T[:1, :8]
    plain = [(g_query, None), (g_key, None)]
    plain += [(g, p) for g in (g_value, g_vector, g_output) for p in range(3)]
    for n in range(got.shape[0]):
        at = n * share
        while at < (n + 1) * share:
            m = at // R
            size = min((m + 1) * R, (n + 1) * share) - at
            value = got[n, at - n * share : at - n * share + size]
            rows = slice(at - m * R, at - m * R + size)
            at += size
            if m == 11:
                g_key_f[rows] = value[:, :R]
                for p in range(3):
                    g_value_f[p, rows] = value[:, (1 + p) * R : (2 + p) * R]
                continue
            g, p = plain[m]
            if p is None:
                g[rows] = value
            else:
                g[p, rows] = value


def everywhere(x, axis):
    count = lax.axis_size(axis)
    return lax.all_to_all(jnp.broadcast_to(x[None], (count,) + x.shape), axis, 0, 0)


def per_device(
    features, vectors, positions, atom_mask, neighbours, ln_gain, ln_bias,
    w_query, w_key, w_value, w_vector, w_output, w_key_filter, w_value_filter,
    cot_features, cot_vectors,
):
    channels = w_query.shape[1]
    atoms = features.shape[1]
    count = lax.axis_size("atoms")
    split = lax.axis_size("feat")
    chan_first = lax.axis_index("feat") * channels
    row_first = lax.axis_index("atoms") * atoms
    start = HALO - lax.rem(row_first, MOL)
    scalars = jnp.stack([start, chan_first, row_first]).astype(jnp.int32)
    molecules, rows_each, tall = edge_sizes(atoms)
    w_query, w_key = w_query.T, w_key.T
    w_value, w_vector, w_output = [jnp.swapaxes(w, 1, 2) for w in (w_value, w_vector, w_output)]
    mask = atom_mask.reshape(1, atoms)
    gain, bias = ln_gain.reshape(1, H), ln_bias.reshape(1, H)

    ends = halo_call(
        atoms,
        scalars,
        (features, vectors, cot_features, cot_vectors, neighbours, mask, positions),
    )
    low = lax.ppermute(ends[0], "atoms", [(i, i + 1) for i in range(count - 1)])
    high = lax.ppermute(ends[1], "atoms", [(i + 1, i) for i in range(count - 1)])

    inputs = (
        scalars, features, vectors, cot_features, cot_vectors, neighbours, mask, positions,
        low, high, gain, bias, w_query, w_key, w_value, w_vector, w_output,
    )
    rows, pos, part, stat = pl.pallas_call(
        functools.partial(dense_kernel, atoms),
        out_shape=[
            jax.ShapeDtypeStruct((7, tall, LANES), BF16),
            jax.ShapeDtypeStruct((tall, LANES), F32),
            jax.ShapeDtypeStruct((H, atoms + LANES), BF16),
            jax.ShapeDtypeStruct((8, atoms), F32),
        ],
        in_specs=[whole(pltpu.SMEM)] + [whole()] * (len(inputs) - 1),
        out_specs=[whole()] * 4,
        scratch_shapes=[
            pltpu.VMEM((LANES, H), BF16),
            pltpu.VMEM((LANES, H), BF16),
            pltpu.VMEM((LANES, H), BF16),
            pltpu.VMEM((3 * R, H), BF16),
            pltpu.VMEM((H, 3 * R), BF16),
        ],
        compiler_params=params(),
    )(*inputs)
    scalar_parts = lax.all_to_all(part.reshape(split, channels, atoms + LANES), "feat", 0, 0)

    kinds = shared_scratch(atoms)
    batch = OFFSETS * rows_each
    names = ["weights", "picks", "many", "mask", "loose", "loose", "tall", "tall", "counts", "pre"]
    names += ["grad_pre", "line", "line2", "line3"]
    names += ["tall"] * 3 + ["low"] * 7 + ["low"] * 10 + ["first"] * 10
    sums, back, grads_a, pos_a, grad_filters_a, radial, geo = edge_call(
        vector_kernel,
        atoms,
        (scalars, rows, pos, w_value_filter[1], w_value_filter[2]),
        (),
        [
            ((3, R, atoms), F32),
            ((3, R, atoms), F32),
            ((2 * R, atoms), BF16),
            ((8, atoms), F32),
            ((LANES, 2 * LANES), F32),
        ],
        [((SPAN, batch, 2 * LANES), BF16), ((SPAN, 7, batch, LANES), BF16)],
        [kinds[name] for name in names],
    )
    names = ["weights", "picks", "many", "weights", "loose", "tall", "tall", "counts", "pre"]
    names += ["grad_pre", "line", "wide2", "wide2f", "line4", "line1"]
    names += ["low"] * 4 + ["low"] * 7 + ["first"] * 7
    scalar_sum, grads_b, pos_b, grad_filters_b = edge_call(
        scalar_kernel,
        atoms,
        (scalars, rows, w_key_filter, w_value_filter[0], scalar_parts),
        (radial, geo),
        [
            ((R, atoms), BF16),
            ((3 * R, atoms), BF16),
            ((8, atoms), F32),
            ((LANES, 2 * LANES), F32),
        ],
        [],
        [kinds[name] for name in names],
    )
    gathered = lax.all_gather(scalar_sum, "feat", axis=0, tiled=True)

    inputs = (
        scalars, features, stat, vectors, cot_features, cot_vectors, gathered, sums,
        grads_b, grads_a, pos_a, pos_b, mask, gain, bias,
        w_query, w_key, w_value, w_vector, w_output, grad_filters_a, grad_filters_b,
    )
    new_features, new_vectors, send, flat = pl.pallas_call(
        functools.partial(layer_kernel, atoms),
        out_shape=[
            jax.ShapeDtypeStruct((R, atoms), BF16),
            jax.ShapeDtypeStruct((3, R, atoms), BF16),
            jax.ShapeDtypeStruct((split, 4 * R + EXTRAS, atoms), BF16),
            jax.ShapeDtypeStruct((12 * R, H), BF16),
        ],
        in_specs=[whole(pltpu.SMEM)] + [whole()] * (len(inputs) - 1),
        out_specs=[whole()] * 4,
        scratch_shapes=[
            pltpu.VMEM((H, 5 * R), BF16),
            pltpu.VMEM((H, 3 * R), BF16),
            pltpu.VMEM((3 * R, H), BF16),
            pltpu.VMEM((3 * R, H), BF16),
            pltpu.VMEM((5 * R, H), F32),
            pltpu.VMEM((3 * R, H), F32),
            pltpu.VMEM((3 * R, H), F32),
        ],
        compiler_params=params(),
    )(*inputs)
    got = lax.all_to_all(send, "feat", 0, 0)
    share = 12 * R // count
    shares = lax.all_to_all(flat.reshape(count, share, H), "atoms", 0, 0)

    inputs = (
        scalars, got, features, stat, gain, cot_features, cot_vectors, back, mask,
    )
    grad_features, grad_vectors, grad_positions, small = pl.pallas_call(
        functools.partial(final_kernel, atoms),
        out_shape=[
            jax.ShapeDtypeStruct((R, atoms), F32),
            jax.ShapeDtypeStruct((3, R, atoms), F32),
            jax.ShapeDtypeStruct((3, atoms), F32),
            jax.ShapeDtypeStruct((8, H), F32),
        ],
        in_specs=[whole(pltpu.SMEM)] + [whole()] * (len(inputs) - 1),
        out_specs=[whole()] * 4,
        compiler_params=params(),
    )(*inputs)
    mine = jnp.concatenate([jnp.sum(shares.astype(F32), axis=0), small], axis=0)
    every = everywhere(mine, "atoms")
    shapes = [
        (1, R), (1, R), (R, H), (R, H), (3, R, H), (3, R, H), (3, R, H), (R, R), (3, R, R), (1, 8),
    ]
    grads = pl.pallas_call(
        functools.partial(unpack_kernel, share),
        out_shape=[jax.ShapeDtypeStruct(shape, F32) for shape in shapes],
        in_specs=[whole()],
        out_specs=[whole()] * len(shapes),
        compiler_params=params(),
    )(every)
    return (
        new_features,
        new_vectors,
        grad_features,
        grad_vectors,
        grad_positions,
        grads[0].reshape(R),
        grads[1].reshape(R),
        grads[2].T,
        grads[3].T,
        jnp.swapaxes(grads[4], 1, 2),
        jnp.swapaxes(grads[5], 1, 2),
        jnp.swapaxes(grads[6], 1, 2),
        grads[7],
        grads[8],
        grads[9][0, :4],
    )


def solution(mesh):
    in_specs = (
        P(None, "atoms"),
        P(None, None, "atoms"),
        P(None, "atoms"),
        P("atoms"),
        P(None, "atoms"),
        P(),
        P(),
        P(None, "feat"),
        P(None, "feat"),
        P(None, None, "feat"),
        P(None, None, "feat"),
        P(None, None, "feat"),
        P(None, "feat"),
        P(None, None, "feat"),
        P("feat", "atoms"),
        P(None, "feat", "atoms"),
    )
    out_specs = (
        P("feat", "atoms"),
        P(None, "feat", "atoms"),
        P("feat", "atoms"),
        P(None, "feat", "atoms"),
        P(None, "atoms"),
        P("feat"),
        P("feat"),
        P(None, "feat"),
        P(None, "feat"),
        P(None, None, "feat"),
        P(None, None, "feat"),
        P(None, None, "feat"),
        P(None, "feat"),
        P(None, None, "feat"),
        P(),
    )
    return jax.shard_map(
        per_device, mesh=mesh, in_specs=in_specs, out_specs=out_specs, check_vma=False
    )
```

```python
import functools
import math

import jax
import jax.numpy as jnp
from jax import lax
from jax.experimental import pallas as pl
from jax.experimental.pallas import tpu as pltpu
from jax.sharding import PartitionSpec as P

H = 256
HEADS = 8
HEAD = H // HEADS
R = 64
MOL = 29
HALO = 32
CUTOFF = 5.0
EPSILON = 1e-05
F32 = jnp.float32
BF16 = jnp.bfloat16

LANE_GROUPS = 2
ROW_GROUPS = 3
SPAN = 5
OFFSETS = 14
STEPS = SPAN + OFFSETS
SUB = 16
LANES = 128

QK, V0_COUNT, V12, VEC01, VEC2_COUNT, COT01, COT2 = range(7)
GROUP_ROWS = 352
EXTRAS = 16


def place(t, group):
    return lax.rem(t + SPAN * group, MOL)


def spread(source, first, second, start, molecules, rows):
    low = lax.broadcasted_iota(jnp.int32, (molecules, LANES), 1) < R

    def step(t, _):
        pieces_in = []
        for g in range(ROW_GROUPS):
            a = source[pl.ds(start + place(t, 2 * g), molecules, stride=MOL), :]
            b = source[pl.ds(start + place(t, 2 * g + 1), molecules, stride=MOL), :]
            pieces_in.append((a, b))
        for g, (a, b) in enumerate(pieces_in):
            at = pl.ds(t * rows + g * molecules, molecules)
            if second is None:
                first[at, :] = jnp.where(low, a, b)
                continue
            first[at, :] = jnp.where(low, a, pltpu.roll(b, R, 1))
            second[at, :] = jnp.where(low, pltpu.roll(a, R, 1), b)
        return 0

    lax.fori_loop(0, STEPS, step, 0)


def clear_tails(ref, molecules, rows):
    left = rows - ROW_GROUPS * molecules
    for t in range(STEPS):
        at = t * rows + ROW_GROUPS * molecules
        if left:
            ref[at : at + left] = jnp.zeros((left, LANES), F32)


def collect(first, second, target, start, molecules, rows):
    low = lax.broadcasted_iota(jnp.int32, (molecules, LANES), 1) < R
    target[...] = jnp.zeros(target.shape, F32)

    def step(t, _):
        done = []
        for g in range(ROW_GROUPS):
            at = pl.ds(t * rows + g * molecules, molecules)
            a = first[at, :]
            b = second[at, :]
            c = jnp.where(low, a, pltpu.roll(b, R, 1))
            d = jnp.where(low, pltpu.roll(a, R, 1), b)
            for value, group in ((c, 2 * g), (d, 2 * g + 1)):
                here = pl.ds(start + place(t, group), molecules, stride=MOL)
                done.append((here, target[here, :] + value))
        for here, value in done:
            target[here, :] = value
        return 0

    lax.fori_loop(0, STEPS, step, 0)


def row_masks(owned, start, molecules, rows, atoms):
    row = lax.broadcasted_iota(jnp.int32, (rows, LANES), 0)
    which = row
    for g in range(1, ROW_GROUPS):
        which = jnp.where(row >= g * molecules, row - g * molecules, which)
    first = start - HALO + which * MOL
    owned[...] = jnp.where((first >= 0) & (first < atoms), 1.0, 0.0)


def set_picks(picks):
    row = lax.broadcasted_iota(jnp.int32, (LANES, LANES), 0)
    lane = lax.broadcasted_iota(jnp.int32, (LANES, LANES), 1)
    base = jnp.where(lane >= R, R, 0)
    for n in range(2 * OFFSETS):
        which = 1 + n if n < OFFSETS else 33 + n - OFFSETS
        block = jnp.where(row == base + which, 1.0, 0.0).astype(BF16)
        picks[:, n * LANES : (n + 1) * LANES] = block


def set_multiplicities(count, target, molecules, rows):
    row = lax.broadcasted_iota(jnp.int32, (rows, LANES), 0)
    lane = lax.broadcasted_iota(jnp.int32, (rows, LANES), 1)
    inner = jnp.where(lane >= R, lane - R, lane)
    doubled = (row >= (ROW_GROUPS - 1) * molecules) & (lane >= R)
    for t in range(SPAN):
        value = jnp.where(inner < 32, count[t * rows : (t + 1) * rows], 0.0)
        for k in range(1, OFFSETS + 1):
            there = count[(t + k) * rows : (t + k + 1) * rows]
            value = jnp.where(inner == 32 + k, there, value)
        if t == SPAN - 1:
            value = jnp.where(doubled, 0.0, value)
        target[t * rows : (t + 1) * rows] = value.astype(BF16)


def dot(a, b):
    return jnp.dot(a, b, preferred_element_type=F32)


def dot_tn(a, b):
    return lax.dot_general(a, b, (((0,), (0,)), ((), ())), preferred_element_type=F32)


def dot_nt(a, b):
    return lax.dot_general(a, b, (((1,), (1,)), ((), ())), preferred_element_type=F32)


COSINE = (0.9999999998, -0.04934802137, 0.000405870916, -1.335212003e-06, 2.349373138e-09, -2.43963243e-12)

GEO_ENVELOPE, GEO_SLOPE, GEO_BEND, GEO_OWN, GEO_WAY = 0, 1, 2, 3, 4


def geometry(pos, t, rows, owned, radial, geo, inverses):
    lane = lax.broadcasted_iota(jnp.int32, (1, LANES), 1)
    centre = jnp.where(lane >= R, lane - R, lane).astype(F32)
    inv_space = (R - 1) / CUTOFF

    def step(k, _):
        for o, size in halves(rows):
            here = pl.ds(pl.multiple_of(k * rows + o, SUB), size)
            ii = pl.ds(pl.multiple_of(t * rows + o, SUB), size)
            jj = pl.ds(pl.multiple_of((t + 1 + k) * rows + o, SUB), size)
            off = [p[ii, :] - p[jj, :] for p in pos]
            mine = owned[o : o + size]
            square = off[0] * off[0] + off[1] * off[1] + off[2] * off[2]
            clamped = jnp.maximum(square, 0.01)
            inverse = lax.rsqrt(clamped)
            c = COSINE[-1]
            for term in COSINE[-2::-1]:
                c = c * clamped + term
            c = jnp.where(clamped < CUTOFF * CUTOFF, c, 0.0)
            envelope = c * c
            y = jnp.maximum(envelope - envelope * envelope, 1e-30)
            free = jnp.where(square > 0.01, 1.0, 0.0)
            bend = ((-math.pi / CUTOFF) * free) * (y * lax.rsqrt(y))
            u = (clamped * inverse) * inv_space - centre
            bump = jnp.exp(-0.5 * (u * u))
            value = bump * envelope
            high = value.astype(BF16)
            slope = bump * bend - (inv_space * free) * (u * value)
            radial[here, :LANES] = high
            radial[here, LANES:] = (value - high.astype(F32)).astype(BF16)
            geo[GEO_OWN, here, :] = (value * mine).astype(BF16)
            geo[GEO_SLOPE, here, :] = slope.astype(BF16)
            geo[GEO_BEND, here, :] = bend.astype(BF16)
            geo[GEO_ENVELOPE, here, :] = envelope.astype(BF16)
            for d in range(3):
                geo[GEO_WAY + d, here, :] = (off[d] * inverse).astype(BF16)
            inverses[0, here, :] = inverse.astype(BF16)
            inverses[1, here, :] = (inverse * free).astype(BF16)
        return 0

    lax.fori_loop(0, OFFSETS, step, 0)


def halves(rows):
    tiles = rows // SUB
    first = (tiles + 1) // 2 * SUB
    return ((0, first), (first, rows - first))


def set_filters(weights_ref, filter_1, filter_2):
    weights_ref[...] = jnp.zeros(weights_ref.shape, BF16)
    for f, ref in enumerate((filter_1, filter_2)):
        half = ref[...] * jnp.asarray(0.5, BF16)
        for part in range(2):
            for g in range(LANE_GROUPS):
                down = part * LANES + g * R
                at = f * LANES + g * R
                weights_ref[down : down + R, at : at + R] = half


def spread_positions(pos_ref, loose, targets, start, molecules, rows):
    for d, target in enumerate(targets):
        clear_tails(target, molecules, rows)
        loose[...] = jnp.broadcast_to(pos_ref[:, d : d + 1], loose.shape)
        spread(loose, target, None, start, molecules, rows)


def gate(h):
    t = jnp.tanh(h)
    u = 1.0 + t
    f = h * u
    return f.astype(BF16), (u + f * (1.0 - t)).astype(BF16)


def total_of(partner, first, t_rows, target):
    target[...] = partner[...].astype(F32)
    target[:t_rows] = target[:t_rows] + first[...]


def carried(rows, t, totals, group, body):
    def outer(s, _):
        o = pl.multiple_of(s * SUB, SUB)
        base = pl.multiple_of(t * rows + o, SUB)
        ii = pl.ds(base, SUB)
        sums = None
        for k in range(0, OFFSETS, group):
            loaded = []
            for n in range(k, k + group):
                here = pl.ds(o + n * rows, SUB)
                loaded.append(body(o, here, ii, pl.ds(base + (1 + n) * rows, SUB), n))
            done = [f() for f in loaded]
            given = [one for one, _ in done]
            while len(given) > 1:
                left = given[len(given) // 2 * 2 :]
                pairs = zip(given[0::2], given[1::2])
                given = [[x + y for x, y in zip(a, b)] for a, b in pairs] + left
            total = [x.astype(F32) for x in given[0]]
            sums = total if sums is None else [x + y for x, y in zip(sums, total)]
            for _, stores in done:
                for ref, index, value in stores:
                    ref[index] = value
        for total, value in zip(totals, sums):
            total[ii, :] = value
        return 0

    lax.fori_loop(0, rows // SUB, outer, 0)


def lanes_of(n):
    return slice(n * LANES, (n + 1) * LANES)


def vector_kernel(
    molecules, rows, atoms,
    scalars, pairs_ref, pos_ref, filter_1, filter_2,
    sums_ref, back_ref, grads_ref, pos_out, grad_w_ref, radial_out, geo_out,
    weights_ref, picks, many, owned, loose, loose2, tall_a, tall_b, counts, pre, grad_pre,
    grad_radial, inverses, grad_ways,
    px, py, pz, w0, w1, w2, v2, c0, c1, c2,
    s0, s1, s2, a0, a1, a2, gv, gx, gy, gz,
    fs0, fs1, fs2, fa0, fa1, fa2, fgv, fgx, fgy, fgz,
):
    t = pl.program_id(0)
    start = scalars[0]
    own = slice(HALO, HALO + atoms)
    radial, geo = radial_out.at[0], geo_out.at[0]
    w, c, g_pos = (w0, w1, w2), (c0, c1, c2), (gx, gy, gz)
    sums, backs = (s0, s1, s2), (a0, a1, a2)

    @pl.when(t == 0)
    def _():
        set_filters(weights_ref, filter_1, filter_2)
        set_picks(picks)
        row_masks(owned, start, molecules, rows, atoms)
        v12 = pairs_ref[V12].astype(F32)
        low = lax.broadcasted_iota(jnp.int32, v12.shape, 1) < R
        v11 = jnp.where(low, v12, pltpu.roll(v12, R, 1))
        clear_tails(tall_a, molecules, rows)
        clear_tails(tall_b, molecules, rows)

        def place_pair(first, second):
            spread(loose, tall_a, tall_b, start, molecules, rows)
            first[...] = tall_a[...].astype(BF16)
            if second is not None:
                second[...] = tall_b[...].astype(BF16)

        loose[...] = pairs_ref[VEC01].astype(F32) * v11
        place_pair(w0, w1)
        third = pairs_ref[VEC2_COUNT].astype(F32)
        loose[...] = jnp.where(low, third * v11, v12)
        place_pair(w2, v2)
        loose[...] = pairs_ref[COT01].astype(F32)
        place_pair(c0, c1)
        loose[...] = jnp.where(low, pairs_ref[COT2].astype(F32), third)
        place_pair(c2, None)
        set_multiplicities(tall_b, many, molecules, rows)
        spread_positions(pos_ref, loose, (px, py, pz), start, molecules, rows)
        for total in (s0, s1, s2, a0, a1, a2, gv, gx, gy, gz):
            total[...] = jnp.zeros(total.shape, BF16)
        grad_w_ref[...] = jnp.zeros(grad_w_ref.shape, F32)

    counts[...] = dot(many[pl.ds(pl.multiple_of(t * rows, SUB), rows), :], picks[...])
    geometry((px, py, pz), t, rows, owned, radial, geo, inverses)
    pre[...] = dot(radial[...], weights_ref[...])

    def channel(o, here, ii, jj, k):
        h1, h2 = pre[here, :LANES], pre[here, LANES:]
        mi = counts[pl.ds(o, SUB), lanes_of(k)]
        mj = counts[pl.ds(o, SUB), lanes_of(OFFSETS + k)]
        v2i, v2j = v2[ii, :], v2[jj, :]
        ways = [geo[GEO_WAY + d, here, :] for d in range(3)]
        wi, wj = [w[d][ii, :] for d in range(3)], [w[d][jj, :] for d in range(3)]
        ci, cj = [c[d][ii, :] for d in range(3)], [c[d][jj, :] for d in range(3)]
        old_sums = [sums[d][jj, :] for d in range(3)]
        old_backs = [backs[d][jj, :] for d in range(3)]
        old_gv = gv[jj, :]

        def compute():
            f1, d1 = gate(h1)
            f2, d2 = gate(h2)
            ni, nj = mi.astype(BF16), mj.astype(BF16)
            f1i, f1j, f2i, f2j = f1 * ni, f1 * nj, f2 * ni, f2 * nj
            msg_i, msg_j = f2i * v2j, f2j * v2i
            stores, sum_i, back_i = [], [], []
            along_i = along_j = across_i = across_j = None
            for d in range(3):
                way = ways[d]
                sum_i.append(f1i * wj[d] + msg_i * way)
                stores.append((sums[d], (jj, slice(None)), old_sums[d] + (f1j * wi[d] - msg_j * way)))
                stores.append((backs[d], (jj, slice(None)), old_backs[d] + f1i * ci[d]))
                back_i.append(f1j * cj[d])
                grad = ci[d] * msg_i - cj[d] * msg_j
                stores.append((grad_ways, (d, here, slice(None)), grad))
                new = (ci[d] * way, cj[d] * way, ci[d] * wj[d], cj[d] * wi[d])
                if d == 0:
                    along_i, along_j, across_i, across_j = new
                else:
                    along_i, along_j = along_i + new[0], along_j + new[1]
                    across_i, across_j = across_i + new[2], across_j + new[3]
            stores.append((gv, (jj, slice(None)), old_gv + f2i * along_i))
            g1 = ni * across_i + nj * across_j
            g2 = ni * along_i * v2j - nj * along_j * v2i
            stores.append((grad_pre, (here, slice(0, LANES)), g1 * d1))
            stores.append((grad_pre, (here, slice(LANES, None)), g2 * d2))
            return sum_i + back_i + [-(f2j * along_j)], stores

        return compute

    carried(rows, t, (fs0, fs1, fs2, fa0, fa1, fa2, fgv), 2, channel)
    grad_radial[...] = dot_nt(grad_pre[...], weights_ref[:LANES])
    grad_w_ref[...] = grad_w_ref[...] + dot_tn(geo[GEO_OWN], grad_pre[...])

    def turn(o, here, ii, jj, k):
        ways = [geo[GEO_WAY + d, here, :] for d in range(3)]
        grads = [grad_ways[d, here, :] for d in range(3)]
        grad, slope = grad_radial[here, :], geo[GEO_SLOPE, here, :]
        inverse, free = inverses[0, here, :], inverses[1, here, :]
        old = [g[jj, :] for g in g_pos]

        def compute():
            along = ways[0] * grads[0] + ways[1] * grads[1] + ways[2] * grads[2]
            pull = grad.astype(BF16) * slope - free * along
            out = [grads[d] * inverse + ways[d] * pull for d in range(3)]
            return out, [(g_pos[d], (jj, slice(None)), old[d] - out[d]) for d in range(3)]

        return compute

    carried(rows, t, (fgx, fgy, fgz), 7, turn)

    @pl.when(t == SPAN - 1)
    def _():
        low = lax.broadcasted_iota(jnp.int32, (atoms, LANES), 1) < R

        def gather_pair(one, two, target):
            total_of(one[0], one[1], SPAN * rows, tall_a)
            total_of(two[0], two[1], SPAN * rows, tall_b)
            collect(tall_a, tall_b, target, start, molecules, rows)

        gather_pair((s0, fs0), (s1, fs1), loose)
        both = loose[own].T
        sums_ref[0] = both[:R]
        sums_ref[1] = both[R:]
        gather_pair((s2, fs2), (gv, fgv), loose)
        both = loose[own].T
        sums_ref[2] = both[:R]
        grads_ref[R:] = both[R:].astype(BF16)
        gather_pair((a0, fa0), (a1, fa1), loose2)
        v12 = pairs_ref[V12, own].astype(F32)
        v11 = jnp.where(low, v12, pltpu.roll(v12, R, 1))
        both = (loose2[own] * v11).T
        back_ref[0] = both[:R]
        back_ref[1] = both[R:]
        partial = loose2[own] * pairs_ref[VEC01, own].astype(F32)
        partial = partial + pltpu.roll(partial, R, 1)
        gather_pair((a2, fa2), (gx, fgx), loose2)
        back_ref[2] = (loose2[own] * v11).T[:R]
        partial = partial + loose2[own] * pairs_ref[VEC2_COUNT, own].astype(F32)
        grads_ref[:R] = partial.T[:R].astype(BF16)
        pos_out[...] = jnp.zeros(pos_out.shape, F32)
        pos_out[0:1] = jnp.sum(loose2[own].T[R:], axis=0, keepdims=True)
        gather_pair((gy, fgy), (gz, fgz), loose)
        both = loose[own].T
        pos_out[1:2] = jnp.sum(both[:R], axis=0, keepdims=True)
        pos_out[2:3] = jnp.sum(both[R:], axis=0, keepdims=True)


def scalar_kernel(
    molecules, rows, atoms,
    scalars, pairs_ref, filter_1, filter_2, scalar_parts, radial_in, geo_in,
    sum_ref, grads_ref, pos_out, grad_w_ref,
    weights_ref, picks, many, heads_ref, loose, tall_a, tall_b, counts, pre, grad_pre,
    grad_radial, products, sums, gates, bends,
    q, key, v0, gs,
    ss, gq, gk, g0, gx, gy, gz,
    fss, fgq, fgk, fg0, fgx, fgy, fgz,
):
    t = pl.program_id(0)
    start = scalars[0]
    own = slice(HALO, HALO + atoms)
    radial, geo = radial_in.at[0], geo_in.at[0]
    g_pos = (gx, gy, gz)

    @pl.when(t == 0)
    def _():
        set_filters(weights_ref, filter_1, filter_2)
        set_picks(picks)
        row = lax.broadcasted_iota(jnp.int32, (2 * LANES, 2 * LANES), 0)
        lane = lax.broadcasted_iota(jnp.int32, (2 * LANES, 2 * LANES), 1)
        heads_ref[...] = jnp.where(row // HEAD == lane // HEAD, 1.0, 0.0).astype(BF16)
        clear_tails(tall_a, molecules, rows)
        clear_tails(tall_b, molecules, rows)

        def place_pair(first, second):
            spread(loose, tall_a, tall_b, start, molecules, rows)
            first[...] = tall_a[...].astype(BF16)
            if second is not None:
                second[...] = tall_b[...].astype(BF16)

        loose[...] = pairs_ref[QK].astype(F32)
        place_pair(q, key)
        loose[...] = pairs_ref[V0_COUNT].astype(F32)
        place_pair(v0, None)
        set_multiplicities(tall_b, many, molecules, rows)
        summed = scalar_parts[0].astype(F32)
        for f in range(1, scalar_parts.shape[0]):
            summed = summed + scalar_parts[f].astype(F32)
        summed = jnp.concatenate([summed, jnp.zeros_like(summed)], axis=0).T
        loose[own] = summed[:atoms]
        loose[:HALO] = summed[atoms : atoms + HALO]
        loose[HALO + atoms : 2 * HALO + atoms] = summed[atoms + HALO : atoms + 2 * HALO]
        loose[2 * HALO + atoms :] = jnp.zeros((loose.shape[0] - 2 * HALO - atoms, LANES), F32)
        place_pair(gs, None)
        for total in (ss, gq, gk, g0, gx, gy, gz):
            total[...] = jnp.zeros(total.shape, BF16)
        grad_w_ref[...] = jnp.zeros(grad_w_ref.shape, F32)

    counts[...] = dot(many[pl.ds(pl.multiple_of(t * rows, SUB), rows), :], picks[...])
    pre[...] = dot(radial[...], weights_ref[...])

    def multiply(k, _):
        for o, size in halves(rows):
            here = pl.ds(pl.multiple_of(k * rows + o, SUB), size)
            ii = pl.ds(pl.multiple_of(t * rows + o, SUB), size)
            jj = pl.ds(pl.multiple_of((t + 1 + k) * rows + o, SUB), size)
            fk, dk = gate(pre[here, :LANES])
            f0, d0 = gate(pre[here, LANES:])
            k_ij, k_ji = q[ii, :] * key[jj, :] * fk, q[jj, :] * key[ii, :] * fk
            s_ij, s_ji = gs[ii, :] * v0[jj, :] * f0, gs[jj, :] * v0[ii, :] * f0
            gates[0, here, :] = fk
            gates[1, here, :] = f0
            gates[2, here, :] = dk
            gates[3, here, :] = d0
            products[0, here, :LANES] = k_ij
            products[0, here, LANES:] = k_ji
            products[1, here, :LANES] = s_ij
            products[1, here, LANES:] = s_ji
        return 0

    lax.fori_loop(0, OFFSETS, multiply, 0)
    sums[0] = dot(products[0], heads_ref[...])
    sums[1] = dot(products[1], heads_ref[...])

    def channel(o, here, ii, jj, k):
        fk, f0, dk, d0 = [gates[n, here, :] for n in range(4)]
        envelope, bend = geo[GEO_ENVELOPE, here, :], geo[GEO_BEND, here, :]
        side_in = []
        for side in range(2):
            lanes = slice(side * LANES, (side + 1) * LANES)
            m = counts[pl.ds(o, SUB), lanes_of(side * OFFSETS + k)]
            h, o_ = (ii, jj) if side == 0 else (jj, ii)
            side_in.append(
                (m, sums[0, here, lanes], sums[1, here, lanes])
                + (q[h, :], key[o_, :], gs[h, :], v0[o_, :])
            )
        old = [ref[jj, :] for ref in (g0, gk, ss, gq)]

        def compute():
            gives, news = [], []
            for m, score, g_att, qh, kt, gh, vt in side_in:
                act, rise = gate(0.5 * score)
                m, g_att = m.astype(BF16), g_att.astype(BF16)
                weight = m * envelope
                att = act * weight
                g_score = g_att * (0.5 * rise) * weight
                lift = m * (g_att * act)
                bv, dv = f0 * att, fk * g_score
                gives.append((vt * bv, kt * dv, gh * bv, qh * dv))
                news.append((qh * kt * g_score, gh * vt * att, lift))
            one, two = gives
            new = [x + y for x, y in zip(*news)]
            stores = [
                (ref, (jj, slice(None)), x + y)
                for ref, x, y in zip((g0, gk, ss, gq), old, (one[2], one[3], two[0], two[1]))
            ]
            stores.append((grad_pre, (here, slice(0, LANES)), new[0] * dk))
            stores.append((grad_pre, (here, slice(LANES, None)), new[1] * d0))
            stores.append((bends, (here, slice(None)), new[2] * bend * (1.0 / HEAD)))
            return [one[0], one[1], two[2], two[3]], stores

        return compute

    carried(rows, t, (fss, fgq, fg0, fgk), 2, channel)
    grad_radial[...] = dot_nt(grad_pre[...], weights_ref[:LANES])
    grad_w_ref[...] = grad_w_ref[...] + dot_tn(geo[GEO_OWN], grad_pre[...])

    def turn(o, here, ii, jj, k):
        ways = [geo[GEO_WAY + d, here, :] for d in range(3)]
        grad, slope, bend = grad_radial[here, :], geo[GEO_SLOPE, here, :], bends[here, :]
        old = [g[jj, :] for g in g_pos]

        def compute():
            pull = grad.astype(BF16) * slope + bend
            out = [way * pull for way in ways]
            return out, [(g_pos[d], (jj, slice(None)), old[d] - out[d]) for d in range(3)]

        return compute

    carried(rows, t, (fgx, fgy, fgz), 7, turn)

    @pl.when(t == SPAN - 1)
    def _():
        def gather_pair(one, two):
            total_of(one[0], one[1], SPAN * rows, tall_a)
            total_of(two[0], two[1], SPAN * rows, tall_b)
            collect(tall_a, tall_b, loose, start, molecules, rows)
            return loose[own].T

        both = gather_pair((ss, fss), (g0, fg0))
        sum_ref[...] = both[:R].astype(BF16)
        grads_ref[2 * R :] = both[R:].astype(BF16)
        both = gather_pair((gq, fgq), (gk, fgk))
        grads_ref[: 2 * R] = both.astype(BF16)
        pos_out[...] = jnp.zeros(pos_out.shape, F32)
        both = gather_pair((gx, fgx), (gy, fgy))
        pos_out[0:1] = jnp.sum(both[:R], axis=0, keepdims=True)
        pos_out[1:2] = jnp.sum(both[R:], axis=0, keepdims=True)
        both = gather_pair((gz, fgz), (gz, fgz))
        pos_out[2:3] = jnp.sum(both[:R], axis=0, keepdims=True)


def whole(memory=pltpu.VMEM):
    return pl.BlockSpec(memory_space=memory)


def params(mib=60):
    return pltpu.CompilerParams(vmem_limit_bytes=mib * 1024 * 1024)


def edge_sizes(atoms):
    molecules = (atoms + 2 * (MOL - 1)) // MOL
    rows = -(-ROW_GROUPS * molecules // SUB) * SUB
    tall = -(-(HALO + molecules * MOL) // SUB) * SUB
    return molecules, rows, tall


def by_step(shape):
    zeros = (0,) * (len(shape) - 1)
    return pl.BlockSpec((1,) + shape[1:], lambda t: (t,) + zeros)


def fixed(shape):
    zeros = (0,) * len(shape)
    return pl.BlockSpec(shape, lambda t: zeros)


def edge_call(kernel, atoms, inputs, stepped_in, outs, stepped_out, scratch):
    molecules, rows, _ = edge_sizes(atoms)
    return pl.pallas_call(
        functools.partial(kernel, molecules, rows, atoms),
        grid=(SPAN,),
        out_shape=[jax.ShapeDtypeStruct(s, kind) for s, kind in outs + stepped_out],
        in_specs=[whole(pltpu.SMEM)]
        + [fixed(x.shape) for x in inputs[1:]]
        + [by_step(x.shape) for x in stepped_in],
        out_specs=[fixed(s) for s, _ in outs] + [by_step(s) for s, _ in stepped_out],
        scratch_shapes=[pltpu.VMEM(s, kind) for s, kind in scratch],
        compiler_params=params(),
    )(*inputs, *stepped_in)


def shared_scratch(atoms):
    _, rows, tall = edge_sizes(atoms)
    batch = OFFSETS * rows
    high = STEPS * rows
    return {
        "weights": ((2 * LANES, 2 * LANES), BF16),
        "picks": ((LANES, 2 * OFFSETS * LANES), BF16),
        "many": ((SPAN * rows, LANES), BF16),
        "mask": ((rows, LANES), F32),
        "loose": ((tall, LANES), F32),
        "tall": ((high, LANES), F32),
        "low": ((high, LANES), BF16),
        "first": ((SPAN * rows, LANES), F32),
        "counts": ((rows, 2 * OFFSETS * LANES), F32),
        "pre": ((batch, 2 * LANES), F32),
        "grad_pre": ((batch, 2 * LANES), BF16),
        "line": ((batch, LANES), F32),
        "line2": ((2, batch, LANES), BF16),
        "line3": ((3, batch, LANES), BF16),
        "line4": ((4, batch, LANES), BF16),
        "line1": ((batch, LANES), BF16),
        "wide2": ((2, batch, 2 * LANES), BF16),
        "wide2f": ((2, batch, 2 * LANES), F32),
    }


def offsets_in_block(neighbours, mask, first):
    lane = lax.broadcasted_iota(jnp.int32, neighbours.shape, 1)
    diff = neighbours - (first + lane)
    return jnp.where(diff < 0, diff + MOL, diff) * mask


def pieces(x):
    a = x.astype(BF16)
    rest = x - a.astype(F32)
    b = rest.astype(BF16)
    return a, b, (rest - b.astype(F32)).astype(BF16)


def edge_groups(features, vectors, cot_f, cot_v, neighbours, mask, positions, first):
    diff = offsets_in_block(neighbours[...], mask[...], first).astype(F32).astype(BF16)
    groups = [jnp.concatenate([features[...], cot_f[...], diff], axis=0)]
    for d in range(3):
        rows = [x.astype(F32) for x in pieces(positions[d : d + 1])]
        rows = jnp.concatenate(rows + [jnp.zeros((29, LANES), F32)], axis=0).astype(BF16)
        groups.append(jnp.concatenate([vectors[d], cot_v[d], rows], axis=0))
    return groups


def halo_kernel(atoms, scalars, *refs):
    row_first = scalars[2]
    lane = lax.broadcasted_iota(jnp.int32, (GROUP_ROWS, LANES), 1)
    for end, at, out in ((0, atoms - LANES, refs[14]), (1, 0, refs[15])):
        groups = edge_groups(*refs[7 * end : 7 * end + 7], row_first + at)
        total = None
        for g, group in enumerate(groups):
            by = (HALO * (g + 1) if end == 0 else HALO * g) % LANES
            moved = group.astype(F32)
            moved = pltpu.roll(moved, by, 1) if by else moved
            total = moved if total is None else jnp.where(lane >= HALO * g, moved, total)
        out[...] = total.astype(BF16)


def halo_call(atoms, scalars, arrays):
    specs = []
    for at in (atoms // LANES - 1, 0):
        for x in arrays:
            shape = x.shape[:-1] + (LANES,)
            index = (0,) * (x.ndim - 1) + (at,)
            specs.append(pl.BlockSpec(shape, lambda *_, index=index: index))
    out = jax.ShapeDtypeStruct((GROUP_ROWS, LANES), BF16)
    return pl.pallas_call(
        functools.partial(halo_kernel, atoms),
        grid=(1,),
        out_shape=[out, out],
        in_specs=[whole(pltpu.SMEM)] + specs,
        out_specs=[whole(), whole()],
        compiler_params=params(),
    )(scalars, *arrays, *arrays)


def column(row):
    return jnp.broadcast_to(row, (8, row.shape[1])).T[:, :1]


def normalised(f):
    mean = jnp.mean(f, axis=0, keepdims=True)
    centred = f - mean
    inv = lax.rsqrt(jnp.mean(centred * centred, axis=0, keepdims=True) + EPSILON)
    return centred * inv, mean, inv


def dense_kernel(
    atoms,
    scalars, features, vectors, cot_f, cot_v, neighbours, mask, positions, low_ref, high_ref,
    gain_ref, bias_ref, w_query, w_key, w_value, w_vector, w_output,
    rows_ref, pos_ref, part_ref, stat_ref,
    w_qk, w_v0, w_v12, w_vec_t, w_out,
):
    chan_first = pl.multiple_of(scalars[1], R)
    row_first = scalars[2]
    gain, bias = column(gain_ref[...]), column(bias_ref[...])
    w_qk[:R] = w_query[...]
    w_qk[R:] = w_key[...]
    w_v0[:R] = w_value[0]
    w_v0[R:] = jnp.zeros((R, H), BF16)
    w_v12[:R] = w_value[1]
    w_v12[R:] = w_value[2]
    for p in range(3):
        w_vec_t[p * R : (p + 1) * R] = w_vector[p]
    w_out[...] = jnp.concatenate([w_output[p] for p in range(3)], axis=0).astype(F32).T.astype(BF16)

    def block(f, v, cf, cv, own_v, diff, pos):
        width = f.shape[1]
        normed, mean, inv = normalised(f)
        turned = (normed * gain + bias).T.astype(BF16)
        kinds = lax.broadcasted_iota(jnp.int32, (R, width), 0)
        kinds = jnp.where(kinds < 32, kinds, MOL + 32 - kinds).astype(F32)
        counts = jnp.zeros((R, width), F32)
        for s in range(diff.shape[0]):
            counts = counts + jnp.where(diff[s : s + 1] == kinds, 1.0, 0.0)
        none = jnp.zeros((R, width), F32)
        counts = jnp.concatenate([none, counts], axis=0).T
        pairs = [None] * 7
        pairs[QK] = dot_nt(turned, w_qk[...])
        pairs[V0_COUNT] = dot_nt(turned, w_v0[...]) + counts
        pairs[V12] = dot_nt(turned, w_v12[...])
        pairs[VEC01] = jnp.concatenate([own_v[0], own_v[1]], axis=0).T
        pairs[VEC2_COUNT] = jnp.concatenate([own_v[2], none], axis=0).T + counts
        pairs[COT01] = jnp.concatenate([cv[0], cv[1]], axis=0).T
        pairs[COT2] = jnp.concatenate([cv[2], none], axis=0).T
        place3 = jnp.concatenate([pos, jnp.zeros((LANES - 3, width), F32)], axis=0).T
        vec_dot = grad_0 = 0.0
        for d in range(3):
            proj = dot(w_vec_t[...], v[d])
            vec_dot = vec_dot + proj[:R] * proj[R : 2 * R]
            grad_0 = grad_0 + cv[d] * proj[2 * R :]
        grad_out = jnp.concatenate([grad_0, cf * vec_dot, cf], axis=0).astype(BF16)
        part = dot(w_out[...], grad_out)
        return [x.astype(BF16) for x in pairs], place3, part.astype(BF16), mean, inv

    wide = 2 * LANES

    def step(b, _):
        at = pl.multiple_of(b * wide, wide)
        here = pl.ds(at, wide)
        own_v = [vectors[d, pl.ds(chan_first, R), here].astype(F32) for d in range(3)]
        diff = offsets_in_block(neighbours[:, here], mask[:, here], row_first + at)
        pairs, place3, part, mean, inv = block(
            features[:, here].astype(F32),
            [vectors[d, :, here] for d in range(3)],
            cot_f[:, here].astype(F32),
            [cot_v[d, :, here].astype(F32) for d in range(3)],
            own_v,
            diff.astype(F32),
            positions[:, here],
        )
        there = pl.ds(pl.multiple_of(HALO + at, 2 * SUB), wide)
        for n, pair in enumerate(pairs):
            rows_ref[n, there, :] = pair
        pos_ref[there, :] = place3
        part_ref[:, here] = part
        stat_ref[0:1, here] = mean
        stat_ref[1:2, here] = inv
        return 0

    lax.fori_loop(0, atoms // wide, step, 0)

    lane = lax.broadcasted_iota(jnp.int32, (GROUP_ROWS, LANES), 1)
    packed_low, packed_high = low_ref[...].astype(F32), high_ref[...].astype(F32)
    groups = []
    for g in range(4):
        a = pltpu.roll(packed_low, (LANES - HALO * g) % LANES, 1) if g else packed_low
        by = (LANES + HALO - HALO * g) % LANES
        b = pltpu.roll(packed_high, by, 1) if by else packed_high
        both = jnp.where(lane < HALO, a, jnp.where(lane < 2 * HALO, b, 0.0))
        groups.append(both)
    pick_rows = lax.broadcasted_iota(jnp.int32, (H, LANES), 0)
    own_v, pos = [], []
    for d in range(3):
        g = groups[1 + d]
        found = g[:R]
        for f in range(1, H // R):
            found = jnp.where(chan_first == f * R, g[f * R : (f + 1) * R], found)
        own_v.append(found)
        pos.append(g[320:321] + g[321:322] + g[322:323])
    pairs, place3, part, _, _ = block(
        groups[0][:H],
        [groups[1 + d][:H].astype(BF16) for d in range(3)],
        groups[0][H : H + R],
        [groups[1 + d][H : H + R] for d in range(3)],
        own_v,
        groups[0][H + R :],
        jnp.concatenate(pos, axis=0),
    )
    high = HALO + atoms
    tall = rows_ref.shape[1]
    for n, pair in enumerate(pairs):
        rows_ref[n, :HALO] = pair[:HALO]
        rows_ref[n, high : high + HALO] = pair[HALO : 2 * HALO]
        rows_ref[n, high + HALO :] = jnp.zeros((tall - high - HALO, LANES), BF16)
    pos_ref[:HALO] = place3[:HALO]
    pos_ref[high : high + HALO] = place3[HALO : 2 * HALO]
    pos_ref[high + HALO :] = jnp.zeros((tall - high - HALO, LANES), F32)
    part_ref[:, atoms:] = part


def both_diagonals(grad, f):
    at = f * LANES
    return 0.5 * (grad[:R, at : at + R] + grad[R:, at + R : at + LANES])


def layer_kernel(
    atoms,
    scalars, features, stat, vectors, cot_f, cot_v, gathered, sums_ref,
    grads_b, grads_a, pos_a, pos_b, mask, gain_ref, bias_ref,
    w_query, w_key, w_value, w_vector, w_output, grad_filters_a, grad_filters_b,
    feat_out, vec_out, send_ref, flat_ref,
    w_five, w_vec, w_vec_t, w_out_t, t_five, t_vec, t_out,
):
    chan_first = pl.multiple_of(scalars[1], R)
    gain, bias = column(gain_ref[...]), column(bias_ref[...])
    five = [w_query[...], w_key[...]] + [w_value[p] for p in range(3)]
    w_five[...] = jnp.concatenate(five, axis=0).astype(F32).T.astype(BF16)
    for p in range(3):
        w_vec_t[p * R : (p + 1) * R] = w_vector[p]
        w_out_t[p * R : (p + 1) * R] = w_output[p]
    w_vec[...] = w_vec_t[...].astype(F32).T.astype(BF16)
    t_five[...] = jnp.zeros(t_five.shape, F32)
    t_vec[...] = jnp.zeros(t_vec.shape, F32)
    t_out[...] = jnp.zeros(t_out.shape, F32)
    wide = 2 * LANES
    split = send_ref.shape[0]

    def step(b, _):
        at = pl.multiple_of(b * wide, wide)
        here = pl.ds(at, wide)
        real = mask[:, here].astype(F32)
        all_sums = gathered[:, here]
        outputs = dot(w_out_t[...], all_sums)
        out_0, out_1, out_2 = outputs[:R], outputs[R : 2 * R], outputs[2 * R :]
        cf = cot_f[:, here].astype(F32)
        grad_dot = cf * out_1
        vec_dot = grad_0 = square_v = square_dv = 0.0
        for d in range(3):
            proj = dot(w_vec_t[...], vectors[d, :, here])
            first, second, third = proj[:R], proj[R : 2 * R], proj[2 * R :]
            cv = cot_v[d, :, here].astype(F32)
            vec_dot = vec_dot + first * second
            grad_0 = grad_0 + cv * third
            delta = third * out_0 + sums_ref[d, :, here]
            moved = vectors[d, pl.ds(chan_first, R), here].astype(F32) + delta
            vec_out[d, :, here] = moved.astype(BF16)
            square_v = square_v + moved * moved
            square_dv = square_dv + delta * delta
            grad_proj = jnp.concatenate(
                [grad_dot * second, grad_dot * first, cv * out_0], axis=0
            ).astype(BF16)
            part = dot(w_vec[...], grad_proj).astype(BF16)
            for f in range(split):
                send_ref[f, (1 + d) * R : (2 + d) * R, here] = part[f * R : (f + 1) * R]
            t_vec[...] = t_vec[...] + dot_nt(grad_proj, vectors[d, :, here])
        delta = vec_dot * out_1 + out_2
        moved = features[pl.ds(chan_first, R), here].astype(F32) + delta
        feat_out[:, here] = moved.astype(BF16)
        grad_out = jnp.concatenate([grad_0, cf * vec_dot, cf], axis=0).astype(BF16)
        t_out[...] = t_out[...] + dot_nt(grad_out, all_sums)
        normed = (features[:, here].astype(F32) - stat[0:1, here]) * stat[1:2, here]
        normal = (normed * gain + bias).astype(BF16)
        grads = jnp.concatenate([grads_b[:, here], grads_a[:, here]], axis=0)
        t_five[...] = t_five[...] + dot_nt(grads, normal)
        part = dot(w_five[...], grads)
        rounded = part.astype(BF16)
        for f in range(split):
            send_ref[f, :R, here] = rounded[f * R : (f + 1) * R]
        hat = part * gain
        tops = [
            jnp.sum(hat, axis=0, keepdims=True),
            jnp.sum(hat * normed, axis=0, keepdims=True),
        ]
        exact = [pos_a[d : d + 1, here] + pos_b[d : d + 1, here] for d in range(3)]
        for x in (moved, delta):
            exact.append(jnp.sum(x * x, axis=0, keepdims=True) * real)
        for x in (square_v, square_dv):
            exact.append(jnp.sum(x, axis=0, keepdims=True) * real)
        heads = [x.astype(BF16).astype(F32) for x in exact]
        tops = tops + heads + [x - y for x, y in zip(exact, heads)]
        tops = jnp.concatenate(tops, axis=0).astype(BF16)
        for f in range(split):
            send_ref[f, 4 * R :, here] = tops
        return 0

    lax.fori_loop(0, atoms // wide, step, 0)
    grad_a, grad_b = grad_filters_a[...], grad_filters_b[...]
    filters = [both_diagonals(g, f) for g in (grad_b, grad_a) for f in range(2)]
    flat_ref[: 5 * R] = t_five[...].astype(BF16)
    flat_ref[5 * R : 8 * R] = t_vec[...].astype(BF16)
    flat_ref[8 * R : 11 * R] = t_out[...].astype(BF16)
    flat_ref[11 * R :] = jnp.concatenate(filters, axis=1).astype(BF16)


def final_kernel(
    atoms,
    scalars, got, features, stat, gain_ref, cot_f, cot_v, back_ref, mask,
    grad_feat, grad_vec, grad_pos, small_ref,
):
    chan_first = pl.multiple_of(scalars[1], R)
    whole_gain = column(gain_ref[...])
    gain = whole_gain[:R]
    for f in range(1, H // R):
        gain = jnp.where(chan_first == f * R, whole_gain[f * R : (f + 1) * R], gain)

    def summed(rows):
        total = got[0, rows].astype(F32)
        for f in range(1, got.shape[0]):
            total = total + got[f, rows].astype(F32)
        return total

    tops = summed(slice(4 * R, 4 * R + EXTRAS))
    grad_normal = summed(slice(0, R))
    inv = stat[1:2]
    normed = (features[pl.ds(chan_first, R), :].astype(F32) - stat[0:1]) * inv
    inner = grad_normal * gain - tops[0:1] * (1.0 / H) - normed * (tops[1:2] * (1.0 / H))
    grad_feat[...] = cot_f[...].astype(F32) + inv * inner
    for d in range(3):
        part = summed(slice((1 + d) * R, (2 + d) * R))
        grad_vec[d] = cot_v[d].astype(F32) + part + back_ref[d]
    exact = tops[2:9] + tops[9:16]
    grad_pos[...] = exact[:3]
    ones = jnp.ones((8, atoms), BF16)
    small_ref[...] = jnp.zeros(small_ref.shape, F32)
    small_ref[:, :R] = dot_nt(ones, (grad_normal * normed).astype(BF16))
    small_ref[:, R : 2 * R] = dot_nt(ones, grad_normal.astype(BF16))
    totals = jnp.sum(exact[3:7], axis=1, keepdims=True)
    small_ref[0:4, LANES : 2 * LANES] = jnp.broadcast_to(totals, (4, LANES))
    real = jnp.sum(mask[...].astype(F32), axis=1, keepdims=True)
    small_ref[4:5, LANES : 2 * LANES] = jnp.broadcast_to(real, (1, LANES))


def unpack_kernel(
    share,
    got,
    g_gain, g_bias, g_query, g_key, g_value, g_vector, g_output, g_key_f, g_value_f, rms_ref,
):
    total = got[0, share:]
    for n in range(1, got.shape[0]):
        total = total + got[n, share:]
    g_gain[...] = total[0:1, :R]
    g_bias[...] = total[0:1, R : 2 * R]
    numbers = total[:, LANES : LANES + 1]
    size = jnp.where(lax.broadcasted_iota(jnp.int32, (8, 1), 0) < 2, 1.0, 3.0) * H
    rms = jnp.sqrt(numbers / (numbers[4:5] * size) + 1e-06)
    rms_ref[...] = jnp.broadcast_to(rms, (8, LANES)).T[:1, :8]
    plain = [(g_query, None), (g_key, None)]
    plain += [(g, p) for g in (g_value, g_vector, g_output) for p in range(3)]
    for n in range(got.shape[0]):
        at = n * share
        while at < (n + 1) * share:
            m = at // R
            size = min((m + 1) * R, (n + 1) * share) - at
            value = got[n, at - n * share : at - n * share + size]
            rows = slice(at - m * R, at - m * R + size)
            at += size
            if m == 11:
                g_key_f[rows] = value[:, :R]
                for p in range(3):
                    g_value_f[p, rows] = value[:, (1 + p) * R : (2 + p) * R]
                continue
            g, p = plain[m]
            if p is None:
                g[rows] = value
            else:
                g[p, rows] = value


def everywhere(x, axis):
    count = lax.axis_size(axis)
    return lax.all_to_all(jnp.broadcast_to(x[None], (count,) + x.shape), axis, 0, 0)


def per_device(
    features, vectors, positions, atom_mask, neighbours, ln_gain, ln_bias,
    w_query, w_key, w_value, w_vector, w_output, w_key_filter, w_value_filter,
    cot_features, cot_vectors,
):
    channels = w_query.shape[1]
    atoms = features.shape[1]
    count = lax.axis_size("atoms")
    split = lax.axis_size("feat")
    chan_first = lax.axis_index("feat") * channels
    row_first = lax.axis_index("atoms") * atoms
    start = HALO - lax.rem(row_first, MOL)
    scalars = jnp.stack([start, chan_first, row_first]).astype(jnp.int32)
    molecules, rows_each, tall = edge_sizes(atoms)
    w_query, w_key = w_query.T, w_key.T
    w_value, w_vector, w_output = [jnp.swapaxes(w, 1, 2) for w in (w_value, w_vector, w_output)]
    mask = atom_mask.reshape(1, atoms)
    gain, bias = ln_gain.reshape(1, H), ln_bias.reshape(1, H)

    ends = halo_call(
        atoms,
        scalars,
        (features, vectors, cot_features, cot_vectors, neighbours, mask, positions),
    )
    low = lax.ppermute(ends[0], "atoms", [(i, i + 1) for i in range(count - 1)])
    high = lax.ppermute(ends[1], "atoms", [(i + 1, i) for i in range(count - 1)])

    inputs = (
        scalars, features, vectors, cot_features, cot_vectors, neighbours, mask, positions,
        low, high, gain, bias, w_query, w_key, w_value, w_vector, w_output,
    )
    rows, pos, part, stat = pl.pallas_call(
        functools.partial(dense_kernel, atoms),
        out_shape=[
            jax.ShapeDtypeStruct((7, tall, LANES), BF16),
            jax.ShapeDtypeStruct((tall, LANES), F32),
            jax.ShapeDtypeStruct((H, atoms + LANES), BF16),
            jax.ShapeDtypeStruct((8, atoms), F32),
        ],
        in_specs=[whole(pltpu.SMEM)] + [whole()] * (len(inputs) - 1),
        out_specs=[whole()] * 4,
        scratch_shapes=[
            pltpu.VMEM((LANES, H), BF16),
            pltpu.VMEM((LANES, H), BF16),
            pltpu.VMEM((LANES, H), BF16),
            pltpu.VMEM((3 * R, H), BF16),
            pltpu.VMEM((H, 3 * R), BF16),
        ],
        compiler_params=params(),
    )(*inputs)
    scalar_parts = lax.all_to_all(part.reshape(split, channels, atoms + LANES), "feat", 0, 0)

    kinds = shared_scratch(atoms)
    batch = OFFSETS * rows_each
    names = ["weights", "picks", "many", "mask", "loose", "loose", "tall", "tall", "counts", "pre"]
    names += ["grad_pre", "line", "line2", "line3"]
    names += ["tall"] * 3 + ["low"] * 7 + ["low"] * 10 + ["first"] * 10
    sums, back, grads_a, pos_a, grad_filters_a, radial, geo = edge_call(
        vector_kernel,
        atoms,
        (scalars, rows, pos, w_value_filter[1], w_value_filter[2]),
        (),
        [
            ((3, R, atoms), F32),
            ((3, R, atoms), F32),
            ((2 * R, atoms), BF16),
            ((8, atoms), F32),
            ((LANES, 2 * LANES), F32),
        ],
        [((SPAN, batch, 2 * LANES), BF16), ((SPAN, 7, batch, LANES), BF16)],
        [kinds[name] for name in names],
    )
    names = ["weights", "picks", "many", "weights", "loose", "tall", "tall", "counts", "pre"]
    names += ["grad_pre", "line", "wide2", "wide2f", "line4", "line1"]
    names += ["low"] * 4 + ["low"] * 7 + ["first"] * 7
    scalar_sum, grads_b, pos_b, grad_filters_b = edge_call(
        scalar_kernel,
        atoms,
        (scalars, rows, w_key_filter, w_value_filter[0], scalar_parts),
        (radial, geo),
        [
            ((R, atoms), BF16),
            ((3 * R, atoms), BF16),
            ((8, atoms), F32),
            ((LANES, 2 * LANES), F32),
        ],
        [],
        [kinds[name] for name in names],
    )
    gathered = lax.all_gather(scalar_sum, "feat", axis=0, tiled=True)

    inputs = (
        scalars, features, stat, vectors, cot_features, cot_vectors, gathered, sums,
        grads_b, grads_a, pos_a, pos_b, mask, gain, bias,
        w_query, w_key, w_value, w_vector, w_output, grad_filters_a, grad_filters_b,
    )
    new_features, new_vectors, send, flat = pl.pallas_call(
        functools.partial(layer_kernel, atoms),
        out_shape=[
            jax.ShapeDtypeStruct((R, atoms), BF16),
            jax.ShapeDtypeStruct((3, R, atoms), BF16),
            jax.ShapeDtypeStruct((split, 4 * R + EXTRAS, atoms), BF16),
            jax.ShapeDtypeStruct((12 * R, H), BF16),
        ],
        in_specs=[whole(pltpu.SMEM)] + [whole()] * (len(inputs) - 1),
        out_specs=[whole()] * 4,
        scratch_shapes=[
            pltpu.VMEM((H, 5 * R), BF16),
            pltpu.VMEM((H, 3 * R), BF16),
            pltpu.VMEM((3 * R, H), BF16),
            pltpu.VMEM((3 * R, H), BF16),
            pltpu.VMEM((5 * R, H), F32),
            pltpu.VMEM((3 * R, H), F32),
            pltpu.VMEM((3 * R, H), F32),
        ],
        compiler_params=params(),
    )(*inputs)
    got = lax.all_to_all(send, "feat", 0, 0)
    share = 12 * R // count
    shares = lax.all_to_all(flat.reshape(count, share, H), "atoms", 0, 0)

    inputs = (
        scalars, got, features, stat, gain, cot_features, cot_vectors, back, mask,
    )
    grad_features, grad_vectors, grad_positions, small = pl.pallas_call(
        functools.partial(final_kernel, atoms),
        out_shape=[
            jax.ShapeDtypeStruct((R, atoms), F32),
            jax.ShapeDtypeStruct((3, R, atoms), F32),
            jax.ShapeDtypeStruct((3, atoms), F32),
            jax.ShapeDtypeStruct((8, H), F32),
        ],
        in_specs=[whole(pltpu.SMEM)] + [whole()] * (len(inputs) - 1),
        out_specs=[whole()] * 4,
        compiler_params=params(),
    )(*inputs)
    mine = jnp.concatenate([jnp.sum(shares.astype(F32), axis=0), small], axis=0)
    every = everywhere(mine, "atoms")
    shapes = [
        (1, R), (1, R), (R, H), (R, H), (3, R, H), (3, R, H), (3, R, H), (R, R), (3, R, R), (1, 8),
    ]
    grads = pl.pallas_call(
        functools.partial(unpack_kernel, share),
        out_shape=[jax.ShapeDtypeStruct(shape, F32) for shape in shapes],
        in_specs=[whole()],
        out_specs=[whole()] * len(shapes),
        compiler_params=params(),
    )(every)
    return (
        new_features,
        new_vectors,
        grad_features,
        grad_vectors,
        grad_positions,
        grads[0].reshape(R),
        grads[1].reshape(R),
        grads[2].T,
        grads[3].T,
        jnp.swapaxes(grads[4], 1, 2),
        jnp.swapaxes(grads[5], 1, 2),
        jnp.swapaxes(grads[6], 1, 2),
        grads[7],
        grads[8],
        grads[9][0, :4],
    )


def solution(mesh):
    in_specs = (
        P(None, "atoms"),
        P(None, None, "atoms"),
        P(None, "atoms"),
        P("atoms"),
        P(None, "atoms"),
        P(),
        P(),
        P(None, "feat"),
        P(None, "feat"),
        P(None, None, "feat"),
        P(None, None, "feat"),
        P(None, None, "feat"),
        P(None, "feat"),
        P(None, None, "feat"),
        P("feat", "atoms"),
        P(None, "feat", "atoms"),
    )
    out_specs = (
        P("feat", "atoms"),
        P(None, "feat", "atoms"),
        P("feat", "atoms"),
        P(None, "feat", "atoms"),
        P(None, "atoms"),
        P("feat"),
        P("feat"),
        P(None, "feat"),
        P(None, "feat"),
        P(None, None, "feat"),
        P(None, None, "feat"),
        P(None, None, "feat"),
        P(None, "feat"),
        P(None, None, "feat"),
        P(),
    )
    return jax.shard_map(
        per_device, mesh=mesh, in_specs=in_specs, out_specs=out_specs, check_vma=False
    )
```

```python
import functools
import math

import jax
import jax.numpy as jnp
from jax import lax
from jax.experimental import pallas as pl
from jax.experimental.pallas import tpu as pltpu
from jax.sharding import PartitionSpec as P

H = 256
HEADS = 8
HEAD = H // HEADS
R = 64
MOL = 29
HALO = 32
CUTOFF = 5.0
EPSILON = 1e-05
F32 = jnp.float32
BF16 = jnp.bfloat16

LANE_GROUPS = 2
ROW_GROUPS = 3
SPAN = 5
OFFSETS = 14
STEPS = SPAN + OFFSETS
SUB = 16
LANES = 128

W01, W2V2, C01, C2_COUNT, POS, QK, V0_COUNT, V12, VEC01, VEC2 = range(10)
GROUP_ROWS = 352
EXTRAS = 16


BLOCK = 8
WINDOW = 256


def block_list(molecules, rows):
    full, rest = divmod(molecules, BLOCK)
    wide = ROW_GROUPS * BLOCK
    out = [(n * wide, wide, BLOCK) for n in range(full)]
    if rows > full * wide:
        out.append((full * wide, rows - full * wide, rest))
    return out


def row_parts(shape, axis, size):
    row = lax.broadcasted_iota(jnp.int32, shape, axis)
    group = jnp.zeros(shape, jnp.int32)
    for g in range(1, ROW_GROUPS):
        group = jnp.where(row >= g * size, g, group)
    return group, row - group * size, row < ROW_GROUPS * size


def set_distances(target, width, size):
    for r in range(LANE_GROUPS):

        def step(t, _, r=r):
            group, molecule, held = row_parts((width, WINDOW), 0, size)
            spot = t + SPAN * (LANE_GROUPS * group + r)
            spot = jnp.where(spot >= MOL, spot - MOL, spot)
            lane = lax.broadcasted_iota(jnp.int32, (width, WINDOW), 1)
            value = jnp.where(held, molecule * MOL + spot - lane, -(10**6))
            target[r, pl.ds(t * width, width), :] = value
            return 0

        lax.fori_loop(0, STEPS, step, 0)


def windows(blocks, distances, start, tall):
    for n, (first, width, size) in enumerate(blocks):
        atom = start + n * BLOCK * MOL
        base = jnp.minimum(atom // SUB * SUB, tall - WINDOW)
        base = pl.multiple_of(base, SUB)
        chosen = distances[0] if size == BLOCK else distances[1]
        ones = [jnp.where(chosen[r] == base - atom, 1.0, 0.0).astype(BF16) for r in (0, 1)]
        yield first, width, pl.ds(base, WINDOW), ones


def spread(source, lanes, stage, blocks, distances, start):
    for first, width, here, ones in windows(blocks, distances, start, source.shape[0]):
        given = source[here, lanes]
        a, b = dot(ones[0], given), dot(ones[1], given)
        low = lax.broadcasted_iota(jnp.int32, (a.shape[0], LANES), 1) < R
        for n in range(a.shape[1] // LANES):
            left, right = a[:, n * LANES : (n + 1) * LANES], b[:, n * LANES : (n + 1) * LANES]
            one = jnp.where(low, left, pltpu.roll(right, R, 1))
            two = jnp.where(low, pltpu.roll(left, R, 1), right)
            stage[2 * n, :, first : first + width] = one.reshape(STEPS, width, LANES)
            stage[2 * n + 1, :, first : first + width] = two.reshape(STEPS, width, LANES)


def spread_positions(source, lanes, targets, blocks, distances, start):
    row = lax.broadcasted_iota(jnp.int32, (LANES, 3 * LANES), 0)
    lane = lax.broadcasted_iota(jnp.int32, (LANES, 3 * LANES), 1)
    axis = jnp.where(lane >= 2 * LANES, 2, jnp.where(lane >= LANES, 1, 0))
    mine = (row >= 3 * axis) & (row < 3 * axis + 3)
    low = lane - axis * LANES < R
    wide = [jnp.where(mine & (low == (r == 0)), 1.0, 0.0).astype(BF16) for r in (0, 1)]
    for first, width, here, ones in windows(blocks, distances, start, source.shape[0]):
        given = source[here, lanes]
        total = 0.0
        for r in (0, 1):
            total = total + dot(dot(ones[r], given).astype(BF16), wide[r])
        for d, target in enumerate(targets):
            value = total[:, d * LANES : (d + 1) * LANES]
            target[:, first : first + width] = value.reshape(STEPS, width, LANES)


def collect(sources, target, blocks, distances, start):
    target[...] = jnp.zeros(target.shape, F32)
    units = []
    for first, width, here, ones in windows(blocks, distances, start, target.shape[0]):
        units.append((first, width, here, ones))
    at = 0
    while at < len(units):
        group = units[at : at + 2] if units[at][0] % SUB == 0 and at + 1 < len(units) else None
        if group is None or (group[0][1] + group[1][1]) % SUB:
            group = units[at : at + 1]
        at += len(group)
        first = group[0][0]
        size = sum(g[1] for g in group)
        blocks_in = []
        for partner, carry in sources:
            value = partner[:, first : first + size].astype(F32)
            start_part = value[:SPAN] + carry[:, first : first + size]
            blocks_in.append(jnp.concatenate([start_part, value[SPAN:]], axis=0))
        for f, width, here, ones in group:
            parts = ([], [])
            for n in range(0, len(sources), 2):
                a = blocks_in[n][:, f - first : f - first + width].reshape(STEPS * width, LANES)
                b = blocks_in[n + 1][:, f - first : f - first + width]
                b = b.reshape(STEPS * width, LANES)
                low = lax.broadcasted_iota(jnp.int32, a.shape, 1) < R
                parts[0].append(jnp.where(low, a, pltpu.roll(b, R, 1)).astype(BF16))
                parts[1].append(jnp.where(low, pltpu.roll(a, R, 1), b).astype(BF16))
            total = 0.0
            for r in (0, 1):
                total = total + dot_tn(ones[r], jnp.concatenate(parts[r], axis=1))
            target[here, :] = target[here, :] + total


def row_masks(owned, start, blocks, atoms):
    for n, (at, width, size) in enumerate(blocks):
        _, molecule, _ = row_parts((width, LANES), 0, size)
        first = start - HALO + (n * BLOCK + molecule) * MOL
        owned[at : at + width] = jnp.where((first >= 0) & (first < atoms), 1.0, 0.0)


def set_picks(picks):
    row = lax.broadcasted_iota(jnp.int32, (LANES, LANES), 0)
    lane = lax.broadcasted_iota(jnp.int32, (LANES, LANES), 1)
    base = jnp.where(lane >= R, R, 0)
    for n in range(2 * OFFSETS):
        which = 1 + n if n < OFFSETS else 33 + n - OFFSETS
        block = jnp.where(row == base + which, 1.0, 0.0).astype(BF16)
        picks[:, n * LANES : (n + 1) * LANES] = block


def set_multiplicities(count, target, blocks, rows):
    lane = lax.broadcasted_iota(jnp.int32, (rows, LANES), 1)
    inner = jnp.where(lane >= R, lane - R, lane)
    last = []
    for _, width, size in blocks:
        last.append(row_parts((width, LANES), 0, size)[0])
    doubled = (jnp.concatenate(last, axis=0) == ROW_GROUPS - 1) & (lane >= R)
    for t in range(SPAN):
        value = jnp.where(inner < 32, count[t], 0.0)
        for k in range(1, OFFSETS + 1):
            value = jnp.where(inner == 32 + k, count[t + k], value)
        if t == SPAN - 1:
            value = jnp.where(doubled, 0.0, value)
        target[t] = value.astype(BF16)


def dot(a, b):
    return jnp.dot(a, b, preferred_element_type=F32)


def dot_tn(a, b):
    return lax.dot_general(a, b, (((0,), (0,)), ((), ())), preferred_element_type=F32)


def dot_nt(a, b):
    return lax.dot_general(a, b, (((1,), (1,)), ((), ())), preferred_element_type=F32)


COSINE = (0.9999999998, -0.04934802137, 0.000405870916, -1.335212003e-06, 2.349373138e-09, -2.43963243e-12)

GEO_ENVELOPE, GEO_SLOPE, GEO_BEND, GEO_OWN, GEO_WAY = 0, 1, 2, 3, 4


def geometry(pos, t, rows, owned, radial, geo, inverses):
    lane = lax.broadcasted_iota(jnp.int32, (1, LANES), 1)
    centre = jnp.where(lane >= R, lane - R, lane).astype(F32)
    inv_space = (R - 1) / CUTOFF

    def step(k, _):
        for o, size in halves(rows):
            here = pl.ds(pl.multiple_of(k * rows + o, SUB), size)
            off = [p[t, o : o + size] - p[t + 1 + k, o : o + size] for p in pos]
            mine = owned[o : o + size]
            square = off[0] * off[0] + off[1] * off[1] + off[2] * off[2]
            clamped = jnp.maximum(square, 0.01)
            inverse = lax.rsqrt(clamped)
            c = COSINE[-1]
            for term in COSINE[-2::-1]:
                c = c * clamped + term
            c = jnp.where(clamped < CUTOFF * CUTOFF, c, 0.0)
            envelope = c * c
            y = jnp.maximum(envelope - envelope * envelope, 1e-30)
            free = jnp.where(square > 0.01, 1.0, 0.0)
            bend = ((-math.pi / CUTOFF) * free) * (y * lax.rsqrt(y))
            u = (clamped * inverse) * inv_space - centre
            bump = jnp.exp(-0.5 * (u * u))
            value = bump * envelope
            high = value.astype(BF16)
            slope = bump * bend - (inv_space * free) * (u * value)
            radial[here, :LANES] = high
            radial[here, LANES:] = (value - high.astype(F32)).astype(BF16)
            geo[GEO_OWN, here, :] = (value * mine).astype(BF16)
            geo[GEO_SLOPE, here, :] = slope.astype(BF16)
            geo[GEO_BEND, here, :] = bend.astype(BF16)
            geo[GEO_ENVELOPE, here, :] = envelope.astype(BF16)
            for d in range(3):
                geo[GEO_WAY + d, here, :] = (off[d] * inverse).astype(BF16)
            inverses[0, here, :] = inverse.astype(BF16)
            inverses[1, here, :] = (inverse * free).astype(BF16)
        return 0

    lax.fori_loop(0, OFFSETS, step, 0)


def halves(rows):
    tiles = rows // SUB
    first = (tiles + 1) // 2 * SUB
    return ((0, first), (first, rows - first))


def set_filters(weights_ref, filter_1, filter_2):
    weights_ref[...] = jnp.zeros(weights_ref.shape, BF16)
    for f, ref in enumerate((filter_1, filter_2)):
        half = ref[...] * jnp.asarray(0.5, BF16)
        for part in range(2):
            for g in range(LANE_GROUPS):
                down = part * LANES + g * R
                at = f * LANES + g * R
                weights_ref[down : down + R, at : at + R] = half


def gate(h):
    t = jnp.tanh(h)
    u = 1.0 + t
    f = h * u
    return f.astype(BF16), (u + f * (1.0 - t)).astype(BF16)


def carried(rows, t, totals, group, body):
    def outer(s, _):
        o = pl.multiple_of(s * SUB, SUB)
        block = pl.ds(o, SUB)
        ii = (t, block)
        sums = None
        for k in range(0, OFFSETS, group):
            loaded = []
            for n in range(k, k + group):
                here = pl.ds(o + n * rows, SUB)
                loaded.append(body(o, here, ii, (t + 1 + n, block), n))
            done = [f() for f in loaded]
            given = [one for one, _ in done]
            while len(given) > 1:
                left = given[len(given) // 2 * 2 :]
                pairs = zip(given[0::2], given[1::2])
                given = [[x + y for x, y in zip(a, b)] for a, b in pairs] + left
            total = [x.astype(F32) for x in given[0]]
            sums = total if sums is None else [x + y for x, y in zip(sums, total)]
            for _, stores in done:
                for ref, index, value in stores:
                    ref[index] = value
        for total, value in zip(totals, sums):
            total[ii] = value
        return 0

    lax.fori_loop(0, rows // SUB, outer, 0)


def lanes_of(n):
    return slice(n * LANES, (n + 1) * LANES)


def vector_kernel(
    molecules, rows, atoms,
    scalars, rows_ref, filter_1, filter_2,
    sums_ref, back_ref, grads_ref, pos_out, grad_w_ref, radial_out, geo_out,
    weights_ref, picks, many, owned, near, near_last, stage, loose, counts, pre, grad_pre,
    grad_radial, inverses, grad_ways,
    px, py, pz, w0, w1, w2, v2, c0, c1, c2,
    s0, s1, s2, a0, a1, a2, gv, gx, gy, gz,
    fs0, fs1, fs2, fa0, fa1, fa2, fgv, fgx, fgy, fgz,
):
    t = pl.program_id(0)
    start = scalars[0]
    own = slice(HALO, HALO + atoms)
    radial, geo = radial_out.at[0], geo_out.at[0]
    w, c, g_pos = (w0, w1, w2), (c0, c1, c2), (gx, gy, gz)
    sums, backs = (s0, s1, s2), (a0, a1, a2)
    blocks = block_list(molecules, rows)
    distances = (near, near_last)

    @pl.when(t == 0)
    def _():
        set_filters(weights_ref, filter_1, filter_2)
        set_picks(picks)
        row_masks(owned, start, blocks, atoms)
        set_distances(near, blocks[0][1], blocks[0][2])
        set_distances(near_last, blocks[-1][1], blocks[-1][2])
        lanes = slice(W01 * LANES, (C2_COUNT + 1) * LANES)
        spread(rows_ref, lanes, stage, blocks, distances, start)
        for n, target in enumerate((w0, w1, w2, v2, c0, c1, c2)):
            target[...] = stage[n].astype(BF16)
        set_multiplicities(stage.at[7], many, blocks, rows)
        lanes = slice(POS * LANES, (POS + 1) * LANES)
        spread_positions(rows_ref, lanes, (px, py, pz), blocks, distances, start)
        for total in (s0, s1, s2, a0, a1, a2, gv, gx, gy, gz):
            total[...] = jnp.zeros(total.shape, BF16)
        grad_w_ref[...] = jnp.zeros(grad_w_ref.shape, F32)

    counts[...] = dot(many[t], picks[...])
    geometry((px, py, pz), t, rows, owned, radial, geo, inverses)
    pre[...] = dot(radial[...], weights_ref[...])

    def channel(o, here, ii, jj, k):
        h1, h2 = pre[here, :LANES], pre[here, LANES:]
        mi = counts[pl.ds(o, SUB), lanes_of(k)]
        mj = counts[pl.ds(o, SUB), lanes_of(OFFSETS + k)]
        v2i, v2j = v2[ii], v2[jj]
        ways = [geo[GEO_WAY + d, here, :] for d in range(3)]
        wi, wj = [w[d][ii] for d in range(3)], [w[d][jj] for d in range(3)]
        ci, cj = [c[d][ii] for d in range(3)], [c[d][jj] for d in range(3)]
        old_sums = [sums[d][jj] for d in range(3)]
        old_backs = [backs[d][jj] for d in range(3)]
        old_gv = gv[jj]

        def compute():
            f1, d1 = gate(h1)
            f2, d2 = gate(h2)
            ni, nj = mi.astype(BF16), mj.astype(BF16)
            f1i, f1j, f2i, f2j = f1 * ni, f1 * nj, f2 * ni, f2 * nj
            msg_i, msg_j = f2i * v2j, f2j * v2i
            stores, sum_i, back_i = [], [], []
            along_i = along_j = across_i = across_j = None
            for d in range(3):
                way = ways[d]
                sum_i.append(f1i * wj[d] + msg_i * way)
                stores.append((sums[d], jj, old_sums[d] + (f1j * wi[d] - msg_j * way)))
                stores.append((backs[d], jj, old_backs[d] + f1i * ci[d]))
                back_i.append(f1j * cj[d])
                grad = ci[d] * msg_i - cj[d] * msg_j
                stores.append((grad_ways, (d, here, slice(None)), grad))
                new = (ci[d] * way, cj[d] * way, ci[d] * wj[d], cj[d] * wi[d])
                if d == 0:
                    along_i, along_j, across_i, across_j = new
                else:
                    along_i, along_j = along_i + new[0], along_j + new[1]
                    across_i, across_j = across_i + new[2], across_j + new[3]
            stores.append((gv, jj, old_gv + f2i * along_i))
            g1 = ni * across_i + nj * across_j
            g2 = ni * along_i * v2j - nj * along_j * v2i
            stores.append((grad_pre, (here, slice(0, LANES)), g1 * d1))
            stores.append((grad_pre, (here, slice(LANES, None)), g2 * d2))
            return sum_i + back_i + [-(f2j * along_j)], stores

        return compute

    carried(rows, t, (fs0, fs1, fs2, fa0, fa1, fa2, fgv), 2, channel)
    grad_radial[...] = dot_nt(grad_pre[...], weights_ref[:LANES])
    grad_w_ref[...] = grad_w_ref[...] + dot_tn(geo[GEO_OWN], grad_pre[...])

    def turn(o, here, ii, jj, k):
        ways = [geo[GEO_WAY + d, here, :] for d in range(3)]
        grads = [grad_ways[d, here, :] for d in range(3)]
        grad, slope = grad_radial[here, :], geo[GEO_SLOPE, here, :]
        inverse, free = inverses[0, here, :], inverses[1, here, :]
        old = [g[jj] for g in g_pos]

        def compute():
            along = ways[0] * grads[0] + ways[1] * grads[1] + ways[2] * grads[2]
            pull = grad.astype(BF16) * slope - free * along
            out = [grads[d] * inverse + ways[d] * pull for d in range(3)]
            return out, [(g_pos[d], jj, old[d] - out[d]) for d in range(3)]

        return compute

    carried(rows, t, (fgx, fgy, fgz), 7, turn)

    @pl.when(t == SPAN - 1)
    def _():
        low = lax.broadcasted_iota(jnp.int32, (atoms, LANES), 1) < R
        totals = (s0, s1, s2, gv, a0, a1, a2, gx, gy, gz)
        firsts = (fs0, fs1, fs2, fgv, fa0, fa1, fa2, fgx, fgy, fgz)
        collect(tuple(zip(totals, firsts)), loose, blocks, distances, start)
        both = loose[own, :LANES].T
        sums_ref[0] = both[:R]
        sums_ref[1] = both[R:]
        both = loose[own, LANES : 2 * LANES].T
        sums_ref[2] = both[:R]
        grads_ref[R:] = both[R:].astype(BF16)

        def kept(n):
            return rows_ref[own, n * LANES : (n + 1) * LANES].astype(F32)

        v12 = kept(V12)
        v11 = jnp.where(low, v12, pltpu.roll(v12, R, 1))
        back = loose[own, 2 * LANES : 3 * LANES]
        both = (back * v11).T
        back_ref[0] = both[:R]
        back_ref[1] = both[R:]
        partial = back * kept(VEC01)
        partial = partial + pltpu.roll(partial, R, 1)
        back = loose[own, 3 * LANES : 4 * LANES]
        back_ref[2] = (back * v11).T[:R]
        partial = partial + back * kept(VEC2)
        grads_ref[:R] = partial.T[:R].astype(BF16)
        pos_out[...] = jnp.zeros(pos_out.shape, F32)
        pos_out[0:1] = jnp.sum(back.T[R:], axis=0, keepdims=True)
        both = loose[own, 4 * LANES :].T
        pos_out[1:2] = jnp.sum(both[:R], axis=0, keepdims=True)
        pos_out[2:3] = jnp.sum(both[R:], axis=0, keepdims=True)


def scalar_kernel(
    molecules, rows, atoms,
    scalars, rows_ref, filter_1, filter_2, scalar_parts, radial_in, geo_in,
    sum_ref, grads_ref, pos_out, grad_w_ref,
    weights_ref, picks, many, heads_ref, near, near_last, stage, loose, loose_low, counts, pre,
    grad_pre, grad_radial, products, sums, gates, bends,
    q, key, v0, gs,
    ss, gq, gk, g0, gx, gy, gz,
    fss, fgq, fgk, fg0, fgx, fgy, fgz,
):
    t = pl.program_id(0)
    start = scalars[0]
    own = slice(HALO, HALO + atoms)
    radial, geo = radial_in.at[0], geo_in.at[0]
    g_pos = (gx, gy, gz)
    blocks = block_list(molecules, rows)
    distances = (near, near_last)

    @pl.when(t == 0)
    def _():
        set_filters(weights_ref, filter_1, filter_2)
        set_picks(picks)
        row = lax.broadcasted_iota(jnp.int32, (2 * LANES, 2 * LANES), 0)
        lane = lax.broadcasted_iota(jnp.int32, (2 * LANES, 2 * LANES), 1)
        heads_ref[...] = jnp.where(row // HEAD == lane // HEAD, 1.0, 0.0).astype(BF16)
        set_distances(near, blocks[0][1], blocks[0][2])
        set_distances(near_last, blocks[-1][1], blocks[-1][2])
        lanes = slice(QK * LANES, (V0_COUNT + 1) * LANES)
        spread(rows_ref, lanes, stage, blocks, distances, start)
        for n, target in enumerate((q, key, v0)):
            target[...] = stage[n].astype(BF16)
        set_multiplicities(stage.at[3], many, blocks, rows)
        summed = scalar_parts[0].astype(F32)
        for f in range(1, scalar_parts.shape[0]):
            summed = summed + scalar_parts[f].astype(F32)
        summed = jnp.concatenate([summed, jnp.zeros_like(summed)], axis=0).T.astype(BF16)
        loose_low[own] = summed[:atoms]
        loose_low[:HALO] = summed[atoms : atoms + HALO]
        loose_low[HALO + atoms : 2 * HALO + atoms] = summed[atoms + HALO : atoms + 2 * HALO]
        end = 2 * HALO + atoms
        loose_low[end:] = jnp.zeros((loose_low.shape[0] - end, LANES), BF16)
        spread(loose_low, slice(None), stage, blocks, distances, start)
        gs[...] = stage[0].astype(BF16)
        for total in (ss, gq, gk, g0, gx, gy, gz):
            total[...] = jnp.zeros(total.shape, BF16)
        grad_w_ref[...] = jnp.zeros(grad_w_ref.shape, F32)

    counts[...] = dot(many[t], picks[...])
    pre[...] = dot(radial[...], weights_ref[...])

    def multiply(k, _):
        for o, size in halves(rows):
            here = pl.ds(pl.multiple_of(k * rows + o, SUB), size)
            ii, jj = (t, slice(o, o + size)), (t + 1 + k, slice(o, o + size))
            fk, dk = gate(pre[here, :LANES])
            f0, d0 = gate(pre[here, LANES:])
            k_ij, k_ji = q[ii] * key[jj] * fk, q[jj] * key[ii] * fk
            s_ij, s_ji = gs[ii] * v0[jj] * f0, gs[jj] * v0[ii] * f0
            gates[0, here, :] = fk
            gates[1, here, :] = f0
            gates[2, here, :] = dk
            gates[3, here, :] = d0
            products[0, here, :LANES] = k_ij
            products[0, here, LANES:] = k_ji
            products[1, here, :LANES] = s_ij
            products[1, here, LANES:] = s_ji
        return 0

    lax.fori_loop(0, OFFSETS, multiply, 0)
    sums[0] = dot(products[0], heads_ref[...])
    sums[1] = dot(products[1], heads_ref[...])

    def channel(o, here, ii, jj, k):
        fk, f0, dk, d0 = [gates[n, here, :] for n in range(4)]
        envelope, bend = geo[GEO_ENVELOPE, here, :], geo[GEO_BEND, here, :]
        side_in = []
        for side in range(2):
            lanes = slice(side * LANES, (side + 1) * LANES)
            m = counts[pl.ds(o, SUB), lanes_of(side * OFFSETS + k)]
            h, o_ = (ii, jj) if side == 0 else (jj, ii)
            side_in.append(
                (m, sums[0, here, lanes], sums[1, here, lanes])
                + (q[h], key[o_], gs[h], v0[o_])
            )
        old = [ref[jj] for ref in (g0, gk, ss, gq)]

        def compute():
            gives, news = [], []
            for m, score, g_att, qh, kt, gh, vt in side_in:
                act, rise = gate(0.5 * score)
                m, g_att = m.astype(BF16), g_att.astype(BF16)
                weight = m * envelope
                att = act * weight
                g_score = g_att * (0.5 * rise) * weight
                lift = m * (g_att * act)
                bv, dv = f0 * att, fk * g_score
                gives.append((vt * bv, kt * dv, gh * bv, qh * dv))
                news.append((qh * kt * g_score, gh * vt * att, lift))
            one, two = gives
            new = [x + y for x, y in zip(*news)]
            stores = [
                (ref, jj, x + y)
                for ref, x, y in zip((g0, gk, ss, gq), old, (one[2], one[3], two[0], two[1]))
            ]
            stores.append((grad_pre, (here, slice(0, LANES)), new[0] * dk))
            stores.append((grad_pre, (here, slice(LANES, None)), new[1] * d0))
            stores.append((bends, (here, slice(None)), new[2] * bend * (1.0 / HEAD)))
            return [one[0], one[1], two[2], two[3]], stores

        return compute

    carried(rows, t, (fss, fgq, fg0, fgk), 2, channel)
    grad_radial[...] = dot_nt(grad_pre[...], weights_ref[:LANES])
    grad_w_ref[...] = grad_w_ref[...] + dot_tn(geo[GEO_OWN], grad_pre[...])

    def turn(o, here, ii, jj, k):
        ways = [geo[GEO_WAY + d, here, :] for d in range(3)]
        grad, slope, bend = grad_radial[here, :], geo[GEO_SLOPE, here, :], bends[here, :]
        old = [g[jj] for g in g_pos]

        def compute():
            pull = grad.astype(BF16) * slope + bend
            out = [way * pull for way in ways]
            return out, [(g_pos[d], jj, old[d] - out[d]) for d in range(3)]

        return compute

    carried(rows, t, (fgx, fgy, fgz), 7, turn)

    @pl.when(t == SPAN - 1)
    def _():
        totals = (ss, g0, gq, gk, gx, gy, gz, gz)
        firsts = (fss, fg0, fgq, fgk, fgx, fgy, fgz, fgz)
        collect(tuple(zip(totals, firsts)), loose, blocks, distances, start)
        both = loose[own, :LANES].T
        sum_ref[...] = both[:R].astype(BF16)
        grads_ref[2 * R :] = both[R:].astype(BF16)
        grads_ref[: 2 * R] = loose[own, LANES : 2 * LANES].T.astype(BF16)
        pos_out[...] = jnp.zeros(pos_out.shape, F32)
        both = loose[own, 2 * LANES : 3 * LANES].T
        pos_out[0:1] = jnp.sum(both[:R], axis=0, keepdims=True)
        pos_out[1:2] = jnp.sum(both[R:], axis=0, keepdims=True)
        both = loose[own, 3 * LANES :].T
        pos_out[2:3] = jnp.sum(both[:R], axis=0, keepdims=True)


def whole(memory=pltpu.VMEM):
    return pl.BlockSpec(memory_space=memory)


def params(mib=60):
    return pltpu.CompilerParams(vmem_limit_bytes=mib * 1024 * 1024)


def edge_sizes(atoms):
    molecules = (atoms + 2 * (MOL - 1)) // MOL
    full, rest = divmod(molecules, BLOCK)
    rows = full * ROW_GROUPS * BLOCK + -(-ROW_GROUPS * rest // BLOCK) * BLOCK
    rows = -(-rows // SUB) * SUB
    tall = -(-(HALO + molecules * MOL) // SUB) * SUB
    return molecules, rows, tall


def by_step(shape):
    zeros = (0,) * (len(shape) - 1)
    return pl.BlockSpec((1,) + shape[1:], lambda t: (t,) + zeros)


def fixed(shape):
    zeros = (0,) * len(shape)
    return pl.BlockSpec(shape, lambda t: zeros)


def edge_call(kernel, atoms, inputs, stepped_in, outs, stepped_out, scratch):
    molecules, rows, _ = edge_sizes(atoms)
    return pl.pallas_call(
        functools.partial(kernel, molecules, rows, atoms),
        grid=(SPAN,),
        out_shape=[jax.ShapeDtypeStruct(s, kind) for s, kind in outs + stepped_out],
        in_specs=[whole(pltpu.SMEM)]
        + [fixed(x.shape) for x in inputs[1:]]
        + [by_step(x.shape) for x in stepped_in],
        out_specs=[fixed(s) for s, _ in outs] + [by_step(s) for s, _ in stepped_out],
        scratch_shapes=[pltpu.VMEM(s, kind) for s, kind in scratch],
        compiler_params=params(),
    )(*inputs, *stepped_in)


def shared_scratch(atoms):
    molecules, rows, tall = edge_sizes(atoms)
    batch = OFFSETS * rows
    blocks = block_list(molecules, rows)
    return {
        "weights": ((2 * LANES, 2 * LANES), BF16),
        "picks": ((LANES, 2 * OFFSETS * LANES), BF16),
        "many": ((SPAN, rows, LANES), BF16),
        "mask": ((rows, LANES), F32),
        "near": ((LANE_GROUPS, STEPS * blocks[0][1], WINDOW), jnp.int32),
        "near_last": ((LANE_GROUPS, STEPS * blocks[-1][1], WINDOW), jnp.int32),
        "stage8": ((8, STEPS, rows, LANES), F32),
        "stage4": ((4, STEPS, rows, LANES), F32),
        "loose5": ((tall, 5 * LANES), F32),
        "loose4": ((tall, 4 * LANES), F32),
        "loose_low": ((tall, LANES), BF16),
        "tall": ((STEPS, rows, LANES), F32),
        "low": ((STEPS, rows, LANES), BF16),
        "first": ((SPAN, rows, LANES), F32),
        "counts": ((rows, 2 * OFFSETS * LANES), F32),
        "pre": ((batch, 2 * LANES), F32),
        "grad_pre": ((batch, 2 * LANES), BF16),
        "line": ((batch, LANES), F32),
        "line2": ((2, batch, LANES), BF16),
        "line3": ((3, batch, LANES), BF16),
        "line4": ((4, batch, LANES), BF16),
        "line1": ((batch, LANES), BF16),
        "wide2": ((2, batch, 2 * LANES), BF16),
        "wide2f": ((2, batch, 2 * LANES), F32),
    }


def offsets_in_block(neighbours, mask, first):
    lane = lax.broadcasted_iota(jnp.int32, neighbours.shape, 1)
    diff = neighbours - (first + lane)
    return jnp.where(diff < 0, diff + MOL, diff) * mask


def pieces(x):
    a = x.astype(BF16)
    rest = x - a.astype(F32)
    b = rest.astype(BF16)
    return a, b, (rest - b.astype(F32)).astype(BF16)


def edge_groups(features, vectors, cot_f, cot_v, neighbours, mask, positions, first):
    diff = offsets_in_block(neighbours[...], mask[...], first).astype(F32).astype(BF16)
    groups = [jnp.concatenate([features[...], cot_f[...], diff], axis=0)]
    for d in range(3):
        rows = [x.astype(F32) for x in pieces(positions[d : d + 1])]
        rows = jnp.concatenate(rows + [jnp.zeros((29, LANES), F32)], axis=0).astype(BF16)
        groups.append(jnp.concatenate([vectors[d], cot_v[d], rows], axis=0))
    return groups


def halo_kernel(atoms, scalars, *refs):
    row_first = scalars[2]
    lane = lax.broadcasted_iota(jnp.int32, (GROUP_ROWS, LANES), 1)
    for end, at, out in ((0, atoms - LANES, refs[14]), (1, 0, refs[15])):
        groups = edge_groups(*refs[7 * end : 7 * end + 7], row_first + at)
        total = None
        for g, group in enumerate(groups):
            by = (HALO * (g + 1) if end == 0 else HALO * g) % LANES
            moved = group.astype(F32)
            moved = pltpu.roll(moved, by, 1) if by else moved
            total = moved if total is None else jnp.where(lane >= HALO * g, moved, total)
        out[...] = total.astype(BF16)


def halo_call(atoms, scalars, arrays):
    specs = []
    for at in (atoms // LANES - 1, 0):
        for x in arrays:
            shape = x.shape[:-1] + (LANES,)
            index = (0,) * (x.ndim - 1) + (at,)
            specs.append(pl.BlockSpec(shape, lambda *_, index=index: index))
    out = jax.ShapeDtypeStruct((GROUP_ROWS, LANES), BF16)
    return pl.pallas_call(
        functools.partial(halo_kernel, atoms),
        grid=(1,),
        out_shape=[out, out],
        in_specs=[whole(pltpu.SMEM)] + specs,
        out_specs=[whole(), whole()],
        compiler_params=params(),
    )(scalars, *arrays, *arrays)


def column(row):
    return jnp.broadcast_to(row, (8, row.shape[1])).T[:, :1]


def normalised(f):
    mean = jnp.mean(f, axis=0, keepdims=True)
    centred = f - mean
    inv = lax.rsqrt(jnp.mean(centred * centred, axis=0, keepdims=True) + EPSILON)
    return centred * inv, mean, inv


def dense_kernel(
    atoms,
    scalars, features, vectors, cot_f, cot_v, neighbours, mask, positions, low_ref, high_ref,
    gain_ref, bias_ref, w_query, w_key, w_value, w_vector, w_output,
    rows_ref, part_ref, stat_ref,
    w_qk, w_v0, w_v12, w_vec_t, w_out,
):
    chan_first = pl.multiple_of(scalars[1], R)
    row_first = scalars[2]
    gain, bias = column(gain_ref[...]), column(bias_ref[...])
    w_qk[:R] = w_query[...]
    w_qk[R:] = w_key[...]
    w_v0[:R] = w_value[0]
    w_v0[R:] = jnp.zeros((R, H), BF16)
    w_v12[:R] = w_value[1]
    w_v12[R:] = w_value[2]
    for p in range(3):
        w_vec_t[p * R : (p + 1) * R] = w_vector[p]
    w_out[...] = jnp.concatenate([w_output[p] for p in range(3)], axis=0).astype(F32).T.astype(BF16)

    def block(f, v, cf, cv, own_v, diff, pos):
        width = f.shape[1]
        normed, mean, inv = normalised(f)
        turned = (normed * gain + bias).T.astype(BF16)
        kinds = lax.broadcasted_iota(jnp.int32, (R, width), 0)
        kinds = jnp.where(kinds < 32, kinds, MOL + 32 - kinds).astype(F32)
        counts = jnp.zeros((R, width), F32)
        for s in range(diff.shape[0]):
            counts = counts + jnp.where(diff[s : s + 1] == kinds, 1.0, 0.0)
        none = jnp.zeros((R, width), F32)
        counts = jnp.concatenate([none, counts], axis=0).T
        low = lax.broadcasted_iota(jnp.int32, (width, LANES), 1) < R
        pairs = [None] * 10
        pairs[QK] = dot_nt(turned, w_qk[...])
        pairs[V0_COUNT] = dot_nt(turned, w_v0[...]) + counts
        v12 = dot_nt(turned, w_v12[...]).astype(BF16).astype(F32)
        v11 = jnp.where(low, v12, pltpu.roll(v12, R, 1))
        pairs[V12] = v12
        pairs[VEC01] = jnp.concatenate([own_v[0], own_v[1]], axis=0).T
        pairs[VEC2] = jnp.concatenate([own_v[2], none], axis=0).T
        pairs[W01] = pairs[VEC01] * v11
        pairs[W2V2] = jnp.where(low, pairs[VEC2] * v11, v12)
        pairs[C01] = jnp.concatenate([cv[0], cv[1]], axis=0).T
        pairs[C2_COUNT] = jnp.concatenate([cv[2], none], axis=0).T + counts
        pairs[POS] = jnp.concatenate([pos, jnp.zeros((LANES - 9, width), F32)], axis=0).T
        vec_dot = grad_0 = 0.0
        for d in range(3):
            proj = dot(w_vec_t[...], v[d])
            vec_dot = vec_dot + proj[:R] * proj[R : 2 * R]
            grad_0 = grad_0 + cv[d] * proj[2 * R :]
        grad_out = jnp.concatenate([grad_0, cf * vec_dot, cf], axis=0).astype(BF16)
        part = dot(w_out[...], grad_out)
        return [x.astype(BF16) for x in pairs], part.astype(BF16), mean, inv

    wide = 2 * LANES

    def step(b, _):
        at = pl.multiple_of(b * wide, wide)
        here = pl.ds(at, wide)
        own_v = [vectors[d, pl.ds(chan_first, R), here].astype(F32) for d in range(3)]
        diff = offsets_in_block(neighbours[:, here], mask[:, here], row_first + at)
        places = [p.astype(F32) for d in range(3) for p in pieces(positions[d : d + 1, here])]
        pairs, part, mean, inv = block(
            features[:, here].astype(F32),
            [vectors[d, :, here] for d in range(3)],
            cot_f[:, here].astype(F32),
            [cot_v[d, :, here].astype(F32) for d in range(3)],
            own_v,
            diff.astype(F32),
            jnp.concatenate(places, axis=0),
        )
        there = pl.ds(pl.multiple_of(HALO + at, 2 * SUB), wide)
        for n, pair in enumerate(pairs):
            rows_ref[there, n * LANES : (n + 1) * LANES] = pair
        part_ref[:, here] = part
        stat_ref[0:1, here] = mean
        stat_ref[1:2, here] = inv
        return 0

    lax.fori_loop(0, atoms // wide, step, 0)

    lane = lax.broadcasted_iota(jnp.int32, (GROUP_ROWS, LANES), 1)
    packed_low, packed_high = low_ref[...].astype(F32), high_ref[...].astype(F32)
    groups = []
    for g in range(4):
        a = pltpu.roll(packed_low, (LANES - HALO * g) % LANES, 1) if g else packed_low
        by = (LANES + HALO - HALO * g) % LANES
        b = pltpu.roll(packed_high, by, 1) if by else packed_high
        both = jnp.where(lane < HALO, a, jnp.where(lane < 2 * HALO, b, 0.0))
        groups.append(both)
    pick_rows = lax.broadcasted_iota(jnp.int32, (H, LANES), 0)
    own_v, pos = [], []
    for d in range(3):
        g = groups[1 + d]
        found = g[:R]
        for f in range(1, H // R):
            found = jnp.where(chan_first == f * R, g[f * R : (f + 1) * R], found)
        own_v.append(found)
        pos.append(g[320:323])
    pairs, part, _, _ = block(
        groups[0][:H],
        [groups[1 + d][:H].astype(BF16) for d in range(3)],
        groups[0][H : H + R],
        [groups[1 + d][H : H + R] for d in range(3)],
        own_v,
        groups[0][H + R :],
        jnp.concatenate(pos, axis=0),
    )
    high = HALO + atoms
    tall = rows_ref.shape[0]
    for n, pair in enumerate(pairs):
        lanes = slice(n * LANES, (n + 1) * LANES)
        rows_ref[:HALO, lanes] = pair[:HALO]
        rows_ref[high : high + HALO, lanes] = pair[HALO : 2 * HALO]
        rows_ref[high + HALO :, lanes] = jnp.zeros((tall - high - HALO, LANES), BF16)
    part_ref[:, atoms:] = part


def both_diagonals(grad, f):
    at = f * LANES
    return 0.5 * (grad[:R, at : at + R] + grad[R:, at + R : at + LANES])


def layer_kernel(
    atoms,
    scalars, features, stat, vectors, cot_f, cot_v, gathered, sums_ref,
    grads_b, grads_a, pos_a, pos_b, mask, gain_ref, bias_ref,
    w_query, w_key, w_value, w_vector, w_output, grad_filters_a, grad_filters_b,
    feat_out, vec_out, send_ref, flat_ref,
    w_five, w_vec, w_vec_t, w_out_t, t_five, t_vec, t_out,
):
    chan_first = pl.multiple_of(scalars[1], R)
    gain, bias = column(gain_ref[...]), column(bias_ref[...])
    five = [w_query[...], w_key[...]] + [w_value[p] for p in range(3)]
    w_five[...] = jnp.concatenate(five, axis=0).astype(F32).T.astype(BF16)
    for p in range(3):
        w_vec_t[p * R : (p + 1) * R] = w_vector[p]
        w_out_t[p * R : (p + 1) * R] = w_output[p]
    w_vec[...] = w_vec_t[...].astype(F32).T.astype(BF16)
    t_five[...] = jnp.zeros(t_five.shape, F32)
    t_vec[...] = jnp.zeros(t_vec.shape, F32)
    t_out[...] = jnp.zeros(t_out.shape, F32)
    wide = 2 * LANES
    split = send_ref.shape[0]

    def step(b, _):
        at = pl.multiple_of(b * wide, wide)
        here = pl.ds(at, wide)
        real = mask[:, here].astype(F32)
        all_sums = gathered[:, here]
        outputs = dot(w_out_t[...], all_sums)
        out_0, out_1, out_2 = outputs[:R], outputs[R : 2 * R], outputs[2 * R :]
        cf = cot_f[:, here].astype(F32)
        grad_dot = cf * out_1
        vec_dot = grad_0 = square_v = square_dv = 0.0
        for d in range(3):
            proj = dot(w_vec_t[...], vectors[d, :, here])
            first, second, third = proj[:R], proj[R : 2 * R], proj[2 * R :]
            cv = cot_v[d, :, here].astype(F32)
            vec_dot = vec_dot + first * second
            grad_0 = grad_0 + cv * third
            delta = third * out_0 + sums_ref[d, :, here]
            moved = vectors[d, pl.ds(chan_first, R), here].astype(F32) + delta
            vec_out[d, :, here] = moved.astype(BF16)
            square_v = square_v + moved * moved
            square_dv = square_dv + delta * delta
            grad_proj = jnp.concatenate(
                [grad_dot * second, grad_dot * first, cv * out_0], axis=0
            ).astype(BF16)
            part = dot(w_vec[...], grad_proj).astype(BF16)
            for f in range(split):
                send_ref[f, (1 + d) * R : (2 + d) * R, here] = part[f * R : (f + 1) * R]
            t_vec[...] = t_vec[...] + dot_nt(grad_proj, vectors[d, :, here])
        delta = vec_dot * out_1 + out_2
        moved = features[pl.ds(chan_first, R), here].astype(F32) + delta
        feat_out[:, here] = moved.astype(BF16)
        grad_out = jnp.concatenate([grad_0, cf * vec_dot, cf], axis=0).astype(BF16)
        t_out[...] = t_out[...] + dot_nt(grad_out, all_sums)
        normed = (features[:, here].astype(F32) - stat[0:1, here]) * stat[1:2, here]
        normal = (normed * gain + bias).astype(BF16)
        grads = jnp.concatenate([grads_b[:, here], grads_a[:, here]], axis=0)
        t_five[...] = t_five[...] + dot_nt(grads, normal)
        part = dot(w_five[...], grads)
        rounded = part.astype(BF16)
        for f in range(split):
            send_ref[f, :R, here] = rounded[f * R : (f + 1) * R]
        hat = part * gain
        tops = [
            jnp.sum(hat, axis=0, keepdims=True),
            jnp.sum(hat * normed, axis=0, keepdims=True),
        ]
        exact = [pos_a[d : d + 1, here] + pos_b[d : d + 1, here] for d in range(3)]
        for x in (moved, delta):
            exact.append(jnp.sum(x * x, axis=0, keepdims=True) * real)
        for x in (square_v, square_dv):
            exact.append(jnp.sum(x, axis=0, keepdims=True) * real)
        heads = [x.astype(BF16).astype(F32) for x in exact]
        tops = tops + heads + [x - y for x, y in zip(exact, heads)]
        tops = jnp.concatenate(tops, axis=0).astype(BF16)
        for f in range(split):
            send_ref[f, 4 * R :, here] = tops
        return 0

    lax.fori_loop(0, atoms // wide, step, 0)
    grad_a, grad_b = grad_filters_a[...], grad_filters_b[...]
    filters = [both_diagonals(g, f) for g in (grad_b, grad_a) for f in range(2)]
    flat_ref[: 5 * R] = t_five[...].astype(BF16)
    flat_ref[5 * R : 8 * R] = t_vec[...].astype(BF16)
    flat_ref[8 * R : 11 * R] = t_out[...].astype(BF16)
    flat_ref[11 * R :] = jnp.concatenate(filters, axis=1).astype(BF16)


def final_kernel(
    atoms,
    scalars, got, features, stat, gain_ref, cot_f, cot_v, back_ref, mask,
    grad_feat, grad_vec, grad_pos, small_ref,
):
    chan_first = pl.multiple_of(scalars[1], R)
    whole_gain = column(gain_ref[...])
    gain = whole_gain[:R]
    for f in range(1, H // R):
        gain = jnp.where(chan_first == f * R, whole_gain[f * R : (f + 1) * R], gain)

    def summed(rows):
        total = got[0, rows].astype(F32)
        for f in range(1, got.shape[0]):
            total = total + got[f, rows].astype(F32)
        return total

    tops = summed(slice(4 * R, 4 * R + EXTRAS))
    grad_normal = summed(slice(0, R))
    inv = stat[1:2]
    normed = (features[pl.ds(chan_first, R), :].astype(F32) - stat[0:1]) * inv
    inner = grad_normal * gain - tops[0:1] * (1.0 / H) - normed * (tops[1:2] * (1.0 / H))
    grad_feat[...] = cot_f[...].astype(F32) + inv * inner
    for d in range(3):
        part = summed(slice((1 + d) * R, (2 + d) * R))
        grad_vec[d] = cot_v[d].astype(F32) + part + back_ref[d]
    exact = tops[2:9] + tops[9:16]
    grad_pos[...] = exact[:3]
    ones = jnp.ones((8, atoms), BF16)
    small_ref[...] = jnp.zeros(small_ref.shape, F32)
    small_ref[:, :R] = dot_nt(ones, (grad_normal * normed).astype(BF16))
    small_ref[:, R : 2 * R] = dot_nt(ones, grad_normal.astype(BF16))
    totals = jnp.sum(exact[3:7], axis=1, keepdims=True)
    small_ref[0:4, LANES : 2 * LANES] = jnp.broadcast_to(totals, (4, LANES))
    real = jnp.sum(mask[...].astype(F32), axis=1, keepdims=True)
    small_ref[4:5, LANES : 2 * LANES] = jnp.broadcast_to(real, (1, LANES))


def unpack_kernel(
    share,
    got,
    g_gain, g_bias, g_query, g_key, g_value, g_vector, g_output, g_key_f, g_value_f, rms_ref,
):
    total = got[0, share:]
    for n in range(1, got.shape[0]):
        total = total + got[n, share:]
    g_gain[...] = total[0:1, :R]
    g_bias[...] = total[0:1, R : 2 * R]
    numbers = total[:, LANES : LANES + 1]
    size = jnp.where(lax.broadcasted_iota(jnp.int32, (8, 1), 0) < 2, 1.0, 3.0) * H
    rms = jnp.sqrt(numbers / (numbers[4:5] * size) + 1e-06)
    rms_ref[...] = jnp.broadcast_to(rms, (8, LANES)).T[:1, :8]
    plain = [(g_query, None), (g_key, None)]
    plain += [(g, p) for g in (g_value, g_vector, g_output) for p in range(3)]
    for n in range(got.shape[0]):
        at = n * share
        while at < (n + 1) * share:
            m = at // R
            size = min((m + 1) * R, (n + 1) * share) - at
            value = got[n, at - n * share : at - n * share + size]
            rows = slice(at - m * R, at - m * R + size)
            at += size
            if m == 11:
                g_key_f[rows] = value[:, :R]
                for p in range(3):
                    g_value_f[p, rows] = value[:, (1 + p) * R : (2 + p) * R]
                continue
            g, p = plain[m]
            if p is None:
                g[rows] = value
            else:
                g[p, rows] = value


def everywhere(x, axis):
    count = lax.axis_size(axis)
    return lax.all_to_all(jnp.broadcast_to(x[None], (count,) + x.shape), axis, 0, 0)


def per_device(
    features, vectors, positions, atom_mask, neighbours, ln_gain, ln_bias,
    w_query, w_key, w_value, w_vector, w_output, w_key_filter, w_value_filter,
    cot_features, cot_vectors,
):
    channels = w_query.shape[1]
    atoms = features.shape[1]
    count = lax.axis_size("atoms")
    split = lax.axis_size("feat")
    chan_first = lax.axis_index("feat") * channels
    row_first = lax.axis_index("atoms") * atoms
    start = HALO - lax.rem(row_first, MOL)
    scalars = jnp.stack([start, chan_first, row_first]).astype(jnp.int32)
    molecules, rows_each, tall = edge_sizes(atoms)
    w_query, w_key = w_query.T, w_key.T
    w_value, w_vector, w_output = [jnp.swapaxes(w, 1, 2) for w in (w_value, w_vector, w_output)]
    mask = atom_mask.reshape(1, atoms)
    gain, bias = ln_gain.reshape(1, H), ln_bias.reshape(1, H)

    ends = halo_call(
        atoms,
        scalars,
        (features, vectors, cot_features, cot_vectors, neighbours, mask, positions),
    )
    low = lax.ppermute(ends[0], "atoms", [(i, i + 1) for i in range(count - 1)])
    high = lax.ppermute(ends[1], "atoms", [(i + 1, i) for i in range(count - 1)])

    inputs = (
        scalars, features, vectors, cot_features, cot_vectors, neighbours, mask, positions,
        low, high, gain, bias, w_query, w_key, w_value, w_vector, w_output,
    )
    rows, part, stat = pl.pallas_call(
        functools.partial(dense_kernel, atoms),
        out_shape=[
            jax.ShapeDtypeStruct((tall, 10 * LANES), BF16),
            jax.ShapeDtypeStruct((H, atoms + LANES), BF16),
            jax.ShapeDtypeStruct((8, atoms), F32),
        ],
        in_specs=[whole(pltpu.SMEM)] + [whole()] * (len(inputs) - 1),
        out_specs=[whole()] * 3,
        scratch_shapes=[
            pltpu.VMEM((LANES, H), BF16),
            pltpu.VMEM((LANES, H), BF16),
            pltpu.VMEM((LANES, H), BF16),
            pltpu.VMEM((3 * R, H), BF16),
            pltpu.VMEM((H, 3 * R), BF16),
        ],
        compiler_params=params(),
    )(*inputs)
    scalar_parts = lax.all_to_all(part.reshape(split, channels, atoms + LANES), "feat", 0, 0)

    kinds = shared_scratch(atoms)
    batch = OFFSETS * rows_each
    names = ["weights", "picks", "many", "mask", "near", "near_last", "stage8", "loose5"]
    names += ["counts", "pre", "grad_pre", "line", "line2", "line3"]
    names += ["tall"] * 3 + ["low"] * 7 + ["low"] * 10 + ["first"] * 10
    sums, back, grads_a, pos_a, grad_filters_a, radial, geo = edge_call(
        vector_kernel,
        atoms,
        (scalars, rows, w_value_filter[1], w_value_filter[2]),
        (),
        [
            ((3, R, atoms), F32),
            ((3, R, atoms), F32),
            ((2 * R, atoms), BF16),
            ((8, atoms), F32),
            ((LANES, 2 * LANES), F32),
        ],
        [((SPAN, batch, 2 * LANES), BF16), ((SPAN, 7, batch, LANES), BF16)],
        [kinds[name] for name in names],
    )
    names = ["weights", "picks", "many", "weights", "near", "near_last", "stage4", "loose4"]
    names += ["loose_low", "counts", "pre", "grad_pre", "line", "wide2", "wide2f", "line4", "line1"]
    names += ["low"] * 4 + ["low"] * 7 + ["first"] * 7
    scalar_sum, grads_b, pos_b, grad_filters_b = edge_call(
        scalar_kernel,
        atoms,
        (scalars, rows, w_key_filter, w_value_filter[0], scalar_parts),
        (radial, geo),
        [
            ((R, atoms), BF16),
            ((3 * R, atoms), BF16),
            ((8, atoms), F32),
            ((LANES, 2 * LANES), F32),
        ],
        [],
        [kinds[name] for name in names],
    )
    gathered = lax.all_gather(scalar_sum, "feat", axis=0, tiled=True)

    inputs = (
        scalars, features, stat, vectors, cot_features, cot_vectors, gathered, sums,
        grads_b, grads_a, pos_a, pos_b, mask, gain, bias,
        w_query, w_key, w_value, w_vector, w_output, grad_filters_a, grad_filters_b,
    )
    new_features, new_vectors, send, flat = pl.pallas_call(
        functools.partial(layer_kernel, atoms),
        out_shape=[
            jax.ShapeDtypeStruct((R, atoms), BF16),
            jax.ShapeDtypeStruct((3, R, atoms), BF16),
            jax.ShapeDtypeStruct((split, 4 * R + EXTRAS, atoms), BF16),
            jax.ShapeDtypeStruct((12 * R, H), BF16),
        ],
        in_specs=[whole(pltpu.SMEM)] + [whole()] * (len(inputs) - 1),
        out_specs=[whole()] * 4,
        scratch_shapes=[
            pltpu.VMEM((H, 5 * R), BF16),
            pltpu.VMEM((H, 3 * R), BF16),
            pltpu.VMEM((3 * R, H), BF16),
            pltpu.VMEM((3 * R, H), BF16),
            pltpu.VMEM((5 * R, H), F32),
            pltpu.VMEM((3 * R, H), F32),
            pltpu.VMEM((3 * R, H), F32),
        ],
        compiler_params=params(),
    )(*inputs)
    got = lax.all_to_all(send, "feat", 0, 0)
    share = 12 * R // count
    shares = lax.all_to_all(flat.reshape(count, share, H), "atoms", 0, 0)

    inputs = (
        scalars, got, features, stat, gain, cot_features, cot_vectors, back, mask,
    )
    grad_features, grad_vectors, grad_positions, small = pl.pallas_call(
        functools.partial(final_kernel, atoms),
        out_shape=[
            jax.ShapeDtypeStruct((R, atoms), F32),
            jax.ShapeDtypeStruct((3, R, atoms), F32),
            jax.ShapeDtypeStruct((3, atoms), F32),
            jax.ShapeDtypeStruct((8, H), F32),
        ],
        in_specs=[whole(pltpu.SMEM)] + [whole()] * (len(inputs) - 1),
        out_specs=[whole()] * 4,
        compiler_params=params(),
    )(*inputs)
    mine = jnp.concatenate([jnp.sum(shares.astype(F32), axis=0), small], axis=0)
    every = everywhere(mine, "atoms")
    shapes = [
        (1, R), (1, R), (R, H), (R, H), (3, R, H), (3, R, H), (3, R, H), (R, R), (3, R, R), (1, 8),
    ]
    grads = pl.pallas_call(
        functools.partial(unpack_kernel, share),
        out_shape=[jax.ShapeDtypeStruct(shape, F32) for shape in shapes],
        in_specs=[whole()],
        out_specs=[whole()] * len(shapes),
        compiler_params=params(),
    )(every)
    return (
        new_features,
        new_vectors,
        grad_features,
        grad_vectors,
        grad_positions,
        grads[0].reshape(R),
        grads[1].reshape(R),
        grads[2].T,
        grads[3].T,
        jnp.swapaxes(grads[4], 1, 2),
        jnp.swapaxes(grads[5], 1, 2),
        jnp.swapaxes(grads[6], 1, 2),
        grads[7],
        grads[8],
        grads[9][0, :4],
    )


def solution(mesh):
    in_specs = (
        P(None, "atoms"),
        P(None, None, "atoms"),
        P(None, "atoms"),
        P("atoms"),
        P(None, "atoms"),
        P(),
        P(),
        P(None, "feat"),
        P(None, "feat"),
        P(None, None, "feat"),
        P(None, None, "feat"),
        P(None, None, "feat"),
        P(None, "feat"),
        P(None, None, "feat"),
        P("feat", "atoms"),
        P(None, "feat", "atoms"),
    )
    out_specs = (
        P("feat", "atoms"),
        P(None, "feat", "atoms"),
        P("feat", "atoms"),
        P(None, "feat", "atoms"),
        P(None, "atoms"),
        P("feat"),
        P("feat"),
        P(None, "feat"),
        P(None, "feat"),
        P(None, None, "feat"),
        P(None, None, "feat"),
        P(None, None, "feat"),
        P(None, "feat"),
        P(None, None, "feat"),
        P(),
    )
    return jax.shard_map(
        per_device, mesh=mesh, in_specs=in_specs, out_specs=out_specs, check_vma=False
    )
```

```python
import functools
import math

import jax
import jax.numpy as jnp
from jax import lax
from jax.experimental import pallas as pl
from jax.experimental.pallas import tpu as pltpu
from jax.sharding import PartitionSpec as P

H = 256
HEADS = 8
HEAD = H // HEADS
R = 64
MOL = 29
HALO = 32
CUTOFF = 5.0
EPSILON = 1e-05
F32 = jnp.float32
BF16 = jnp.bfloat16

LANE_GROUPS = 2
ROW_GROUPS = 3
SPAN = 5
OFFSETS = 14
STEPS = SPAN + OFFSETS
SUB = 16
LANES = 128

W01, W2V2, C01, C2_COUNT, POS, QK, V0_COUNT, V12, VEC01, VEC2 = range(10)
GROUP_ROWS = 352
EXTRAS = 16


BLOCK = 8
WINDOW = 256


def block_list(molecules, rows):
    full, rest = divmod(molecules, BLOCK)
    wide = ROW_GROUPS * BLOCK
    out = [(n * wide, wide, BLOCK) for n in range(full)]
    if rows > full * wide:
        out.append((full * wide, rows - full * wide, rest))
    return out


def row_parts(shape, axis, size):
    row = lax.broadcasted_iota(jnp.int32, shape, axis)
    group = jnp.zeros(shape, jnp.int32)
    for g in range(1, ROW_GROUPS):
        group = jnp.where(row >= g * size, g, group)
    return group, row - group * size, row < ROW_GROUPS * size


def set_distances(target, width, size):
    for r in range(LANE_GROUPS):

        def step(t, _, r=r):
            group, molecule, held = row_parts((width, WINDOW), 0, size)
            spot = t + SPAN * (LANE_GROUPS * group + r)
            spot = jnp.where(spot >= MOL, spot - MOL, spot)
            lane = lax.broadcasted_iota(jnp.int32, (width, WINDOW), 1)
            value = jnp.where(held, molecule * MOL + spot - lane, -(10**6))
            target[r, pl.ds(t * width, width), :] = value
            return 0

        lax.fori_loop(0, STEPS, step, 0)


def windows(blocks, distances, start, tall):
    for n, (first, width, size) in enumerate(blocks):
        atom = start + n * BLOCK * MOL
        base = jnp.minimum(atom // SUB * SUB, tall - WINDOW)
        base = pl.multiple_of(base, SUB)
        chosen = distances[0] if size == BLOCK else distances[1]
        ones = [jnp.where(chosen[r] == base - atom, 1.0, 0.0).astype(BF16) for r in (0, 1)]
        yield first, width, pl.ds(base, WINDOW), ones


def spread(source, lanes, stage, blocks, distances, start):
    for first, width, here, ones in windows(blocks, distances, start, source.shape[0]):
        given = source[here, lanes]
        a, b = dot(ones[0], given), dot(ones[1], given)
        low = lax.broadcasted_iota(jnp.int32, (a.shape[0], LANES), 1) < R
        for n in range(a.shape[1] // LANES):
            left, right = a[:, n * LANES : (n + 1) * LANES], b[:, n * LANES : (n + 1) * LANES]
            one = jnp.where(low, left, pltpu.roll(right, R, 1))
            two = jnp.where(low, pltpu.roll(left, R, 1), right)
            stage[2 * n, :, first : first + width] = one.reshape(STEPS, width, LANES)
            stage[2 * n + 1, :, first : first + width] = two.reshape(STEPS, width, LANES)


def spread_positions(source, lanes, targets, blocks, distances, start):
    row = lax.broadcasted_iota(jnp.int32, (LANES, 3 * LANES), 0)
    lane = lax.broadcasted_iota(jnp.int32, (LANES, 3 * LANES), 1)
    axis = jnp.where(lane >= 2 * LANES, 2, jnp.where(lane >= LANES, 1, 0))
    mine = (row >= 3 * axis) & (row < 3 * axis + 3)
    low = lane - axis * LANES < R
    wide = [jnp.where(mine & (low == (r == 0)), 1.0, 0.0).astype(BF16) for r in (0, 1)]
    for first, width, here, ones in windows(blocks, distances, start, source.shape[0]):
        given = source[here, lanes]
        total = 0.0
        for r in (0, 1):
            total = total + dot(dot(ones[r], given).astype(BF16), wide[r])
        for d, target in enumerate(targets):
            value = total[:, d * LANES : (d + 1) * LANES]
            target[:, first : first + width] = value.reshape(STEPS, width, LANES)


def collect(sources, target, blocks, distances, start):
    target[...] = jnp.zeros(target.shape, F32)
    units = []
    for first, width, here, ones in windows(blocks, distances, start, target.shape[0]):
        units.append((first, width, here, ones))
    at = 0
    while at < len(units):
        group = units[at : at + 2] if units[at][0] % SUB == 0 and at + 1 < len(units) else None
        if group is None or (group[0][1] + group[1][1]) % SUB:
            group = units[at : at + 1]
        at += len(group)
        first = group[0][0]
        size = sum(g[1] for g in group)
        blocks_in = []
        for partner, carry in sources:
            value = partner[:, first : first + size].astype(F32)
            start_part = value[:SPAN] + carry[:, first : first + size]
            blocks_in.append(jnp.concatenate([start_part, value[SPAN:]], axis=0))
        for f, width, here, ones in group:
            parts = ([], [])
            for n in range(0, len(sources), 2):
                a = blocks_in[n][:, f - first : f - first + width].reshape(STEPS * width, LANES)
                b = blocks_in[n + 1][:, f - first : f - first + width]
                b = b.reshape(STEPS * width, LANES)
                low = lax.broadcasted_iota(jnp.int32, a.shape, 1) < R
                parts[0].append(jnp.where(low, a, pltpu.roll(b, R, 1)).astype(BF16))
                parts[1].append(jnp.where(low, pltpu.roll(a, R, 1), b).astype(BF16))
            total = 0.0
            for r in (0, 1):
                total = total + dot_tn(ones[r], jnp.concatenate(parts[r], axis=1))
            target[here, :] = target[here, :] + total


def row_masks(owned, start, blocks, atoms):
    for n, (at, width, size) in enumerate(blocks):
        _, molecule, _ = row_parts((width, LANES), 0, size)
        first = start - HALO + (n * BLOCK + molecule) * MOL
        owned[at : at + width] = jnp.where((first >= 0) & (first < atoms), 1.0, 0.0)


def set_picks(picks):
    row = lax.broadcasted_iota(jnp.int32, (LANES, LANES), 0)
    lane = lax.broadcasted_iota(jnp.int32, (LANES, LANES), 1)
    base = jnp.where(lane >= R, R, 0)
    for n in range(2 * OFFSETS):
        which = 1 + n if n < OFFSETS else 33 + n - OFFSETS
        block = jnp.where(row == base + which, 1.0, 0.0).astype(BF16)
        picks[:, n * LANES : (n + 1) * LANES] = block


def set_multiplicities(count, target, blocks, rows):
    lane = lax.broadcasted_iota(jnp.int32, (rows, LANES), 1)
    inner = jnp.where(lane >= R, lane - R, lane)
    last = []
    for _, width, size in blocks:
        last.append(row_parts((width, LANES), 0, size)[0])
    doubled = (jnp.concatenate(last, axis=0) == ROW_GROUPS - 1) & (lane >= R)
    for t in range(SPAN):
        value = jnp.where(inner < 32, count[t], 0.0)
        for k in range(1, OFFSETS + 1):
            value = jnp.where(inner == 32 + k, count[t + k], value)
        if t == SPAN - 1:
            value = jnp.where(doubled, 0.0, value)
        target[t] = value.astype(BF16)


def dot(a, b):
    return jnp.dot(a, b, preferred_element_type=F32)


def dot_tn(a, b):
    return lax.dot_general(a, b, (((0,), (0,)), ((), ())), preferred_element_type=F32)


def dot_nt(a, b):
    return lax.dot_general(a, b, (((1,), (1,)), ((), ())), preferred_element_type=F32)


COSINE = (0.9999999998, -0.04934802137, 0.000405870916, -1.335212003e-06, 2.349373138e-09, -2.43963243e-12)

GEO_ENVELOPE, GEO_SLOPE, GEO_BEND, GEO_OWN, GEO_WAY, GEO_INVERSE, GEO_FREE = 0, 1, 2, 3, 4, 7, 8
GEO = 9


def geometry(pos, t, rows, owned, radial, geo):
    lane = lax.broadcasted_iota(jnp.int32, (1, LANES), 1)
    centre = jnp.where(lane >= R, lane - R, lane).astype(F32)
    inv_space = (R - 1) / CUTOFF

    def step(k, _):
        for o, size in halves(rows):
            here = pl.ds(pl.multiple_of(k * rows + o, SUB), size)
            off = [p[t, o : o + size] - p[t + 1 + k, o : o + size] for p in pos]
            mine = owned[o : o + size]
            square = off[0] * off[0] + off[1] * off[1] + off[2] * off[2]
            clamped = jnp.maximum(square, 0.01)
            inverse = lax.rsqrt(clamped)
            c = COSINE[-1]
            for term in COSINE[-2::-1]:
                c = c * clamped + term
            c = jnp.where(clamped < CUTOFF * CUTOFF, c, 0.0)
            envelope = c * c
            y = jnp.maximum(envelope - envelope * envelope, 1e-30)
            free = jnp.where(square > 0.01, 1.0, 0.0)
            bend = ((-math.pi / CUTOFF) * free) * (y * lax.rsqrt(y))
            u = (clamped * inverse) * inv_space - centre
            bump = jnp.exp(-0.5 * (u * u))
            value = bump * envelope
            high = value.astype(BF16)
            slope = bump * bend - (inv_space * free) * (u * value)
            radial[here, :LANES] = high
            radial[here, LANES:] = (value - high.astype(F32)).astype(BF16)
            geo[GEO_OWN, here, :] = (value * mine).astype(BF16)
            geo[GEO_SLOPE, here, :] = slope.astype(BF16)
            geo[GEO_BEND, here, :] = bend.astype(BF16)
            geo[GEO_ENVELOPE, here, :] = envelope.astype(BF16)
            for d in range(3):
                geo[GEO_WAY + d, here, :] = (off[d] * inverse).astype(BF16)
            geo[GEO_INVERSE, here, :] = inverse.astype(BF16)
            geo[GEO_FREE, here, :] = (inverse * free).astype(BF16)
        return 0

    lax.fori_loop(0, OFFSETS, step, 0)


def halves(rows):
    tiles = rows // SUB
    first = (tiles + 1) // 2 * SUB
    return ((0, first), (first, rows - first))


def set_filters(weights_ref, filter_1, filter_2):
    weights_ref[...] = jnp.zeros(weights_ref.shape, BF16)
    for f, ref in enumerate((filter_1, filter_2)):
        half = ref[...] * jnp.asarray(0.5, BF16)
        for part in range(2):
            for g in range(LANE_GROUPS):
                down = part * LANES + g * R
                at = f * LANES + g * R
                weights_ref[down : down + R, at : at + R] = half


def gate(h):
    t = jnp.tanh(h)
    u = 1.0 + t
    f = h * u
    return f.astype(BF16), (u + f * (1.0 - t)).astype(BF16)


def carried(rows, t, totals, group, body):
    def outer(s, _):
        o = pl.multiple_of(s * SUB, SUB)
        block = pl.ds(o, SUB)
        ii = (t, block)
        sums = None
        for k in range(0, OFFSETS, group):
            loaded = []
            for n in range(k, k + group):
                here = pl.ds(o + n * rows, SUB)
                loaded.append(body(o, here, ii, (t + 1 + n, block), n))
            done = [f() for f in loaded]
            given = [one for one, _ in done]
            while len(given) > 1:
                left = given[len(given) // 2 * 2 :]
                pairs = zip(given[0::2], given[1::2])
                given = [[x + y for x, y in zip(a, b)] for a, b in pairs] + left
            total = [x.astype(F32) for x in given[0]]
            sums = total if sums is None else [x + y for x, y in zip(sums, total)]
            for _, stores in done:
                for ref, index, value in stores:
                    ref[index] = value
        for total, value in zip(totals, sums):
            total[ii] = value
        return 0

    lax.fori_loop(0, rows // SUB, outer, 0)


def lanes_of(n):
    return slice(n * LANES, (n + 1) * LANES)


def geometry_kernel(
    molecules, rows, atoms,
    scalars, rows_ref, radial_out, geo_out, owned, near, near_last, px, py, pz,
):
    t = pl.program_id(0)
    start = scalars[0]
    blocks = block_list(molecules, rows)
    distances = (near, near_last)

    @pl.when(t == 0)
    def _():
        row_masks(owned, start, blocks, atoms)
        set_distances(near, blocks[0][1], blocks[0][2])
        set_distances(near_last, blocks[-1][1], blocks[-1][2])
        lanes = slice(POS * LANES, (POS + 1) * LANES)
        spread_positions(rows_ref, lanes, (px, py, pz), blocks, distances, start)

    geometry((px, py, pz), t, rows, owned, radial_out.at[0], geo_out.at[0])


def vector_kernel(
    molecules, rows, atoms,
    scalars, rows_ref, filter_1, filter_2, radial_in, geo_in,
    sums_ref, back_ref, grads_ref, pos_out, grad_w_ref,
    weights_ref, picks, many, near, near_last, stage, loose, counts, pre, grad_pre,
    grad_radial, grad_ways,
    w0, w1, w2, v2, c0, c1, c2,
    s0, s1, s2, a0, a1, a2, gv, gx, gy, gz,
    fs0, fs1, fs2, fa0, fa1, fa2, fgv, fgx, fgy, fgz,
):
    t = pl.program_id(0)
    start = scalars[0]
    own = slice(HALO, HALO + atoms)
    radial, geo = radial_in.at[0], geo_in.at[0]
    w, c, g_pos = (w0, w1, w2), (c0, c1, c2), (gx, gy, gz)
    sums, backs = (s0, s1, s2), (a0, a1, a2)
    blocks = block_list(molecules, rows)
    distances = (near, near_last)

    @pl.when(t == 0)
    def _():
        set_filters(weights_ref, filter_1, filter_2)
        set_picks(picks)
        set_distances(near, blocks[0][1], blocks[0][2])
        set_distances(near_last, blocks[-1][1], blocks[-1][2])
        lanes = slice(W01 * LANES, (C2_COUNT + 1) * LANES)
        spread(rows_ref, lanes, stage, blocks, distances, start)
        for n, target in enumerate((w0, w1, w2, v2, c0, c1, c2)):
            target[...] = stage[n].astype(BF16)
        set_multiplicities(stage.at[7], many, blocks, rows)
        for total in (s0, s1, s2, a0, a1, a2, gv, gx, gy, gz):
            total[...] = jnp.zeros(total.shape, BF16)
        grad_w_ref[...] = jnp.zeros(grad_w_ref.shape, F32)

    counts[...] = dot(many[t], picks[...])
    pre[...] = dot(radial[...], weights_ref[...])

    def channel(o, here, ii, jj, k):
        h1, h2 = pre[here, :LANES], pre[here, LANES:]
        mi = counts[pl.ds(o, SUB), lanes_of(k)]
        mj = counts[pl.ds(o, SUB), lanes_of(OFFSETS + k)]
        v2i, v2j = v2[ii], v2[jj]
        ways = [geo[GEO_WAY + d, here, :] for d in range(3)]
        wi, wj = [w[d][ii] for d in range(3)], [w[d][jj] for d in range(3)]
        ci, cj = [c[d][ii] for d in range(3)], [c[d][jj] for d in range(3)]
        old_sums = [sums[d][jj] for d in range(3)]
        old_backs = [backs[d][jj] for d in range(3)]
        old_gv = gv[jj]

        def compute():
            f1, d1 = gate(h1)
            f2, d2 = gate(h2)
            ni, nj = mi.astype(BF16), mj.astype(BF16)
            f1i, f1j, f2i, f2j = f1 * ni, f1 * nj, f2 * ni, f2 * nj
            msg_i, msg_j = f2i * v2j, f2j * v2i
            stores, sum_i, back_i = [], [], []
            along_i = along_j = across_i = across_j = None
            for d in range(3):
                way = ways[d]
                sum_i.append(f1i * wj[d] + msg_i * way)
                stores.append((sums[d], jj, old_sums[d] + (f1j * wi[d] - msg_j * way)))
                stores.append((backs[d], jj, old_backs[d] + f1i * ci[d]))
                back_i.append(f1j * cj[d])
                grad = ci[d] * msg_i - cj[d] * msg_j
                stores.append((grad_ways, (d, here, slice(None)), grad))
                new = (ci[d] * way, cj[d] * way, ci[d] * wj[d], cj[d] * wi[d])
                if d == 0:
                    along_i, along_j, across_i, across_j = new
                else:
                    along_i, along_j = along_i + new[0], along_j + new[1]
                    across_i, across_j = across_i + new[2], across_j + new[3]
            stores.append((gv, jj, old_gv + f2i * along_i))
            g1 = ni * across_i + nj * across_j
            g2 = ni * along_i * v2j - nj * along_j * v2i
            stores.append((grad_pre, (here, slice(0, LANES)), g1 * d1))
            stores.append((grad_pre, (here, slice(LANES, None)), g2 * d2))
            return sum_i + back_i + [-(f2j * along_j)], stores

        return compute

    carried(rows, t, (fs0, fs1, fs2, fa0, fa1, fa2, fgv), 2, channel)
    grad_radial[...] = dot_nt(grad_pre[...], weights_ref[:LANES])
    grad_w_ref[...] = grad_w_ref[...] + dot_tn(geo[GEO_OWN], grad_pre[...])

    def turn(o, here, ii, jj, k):
        ways = [geo[GEO_WAY + d, here, :] for d in range(3)]
        grads = [grad_ways[d, here, :] for d in range(3)]
        grad, slope = grad_radial[here, :], geo[GEO_SLOPE, here, :]
        inverse, free = geo[GEO_INVERSE, here, :], geo[GEO_FREE, here, :]
        old = [g[jj] for g in g_pos]

        def compute():
            along = ways[0] * grads[0] + ways[1] * grads[1] + ways[2] * grads[2]
            pull = grad.astype(BF16) * slope - free * along
            out = [grads[d] * inverse + ways[d] * pull for d in range(3)]
            return out, [(g_pos[d], jj, old[d] - out[d]) for d in range(3)]

        return compute

    carried(rows, t, (fgx, fgy, fgz), 7, turn)

    @pl.when(t == SPAN - 1)
    def _():
        low = lax.broadcasted_iota(jnp.int32, (atoms, LANES), 1) < R
        totals = (s0, s1, s2, gv, a0, a1, a2, gx, gy, gz)
        firsts = (fs0, fs1, fs2, fgv, fa0, fa1, fa2, fgx, fgy, fgz)
        collect(tuple(zip(totals, firsts)), loose, blocks, distances, start)
        both = loose[own, :LANES].T
        sums_ref[0] = both[:R]
        sums_ref[1] = both[R:]
        both = loose[own, LANES : 2 * LANES].T
        sums_ref[2] = both[:R]
        grads_ref[R:] = both[R:].astype(BF16)

        def kept(n):
            return rows_ref[own, n * LANES : (n + 1) * LANES].astype(F32)

        v12 = kept(V12)
        v11 = jnp.where(low, v12, pltpu.roll(v12, R, 1))
        back = loose[own, 2 * LANES : 3 * LANES]
        both = (back * v11).T
        back_ref[0] = both[:R]
        back_ref[1] = both[R:]
        partial = back * kept(VEC01)
        partial = partial + pltpu.roll(partial, R, 1)
        back = loose[own, 3 * LANES : 4 * LANES]
        back_ref[2] = (back * v11).T[:R]
        partial = partial + back * kept(VEC2)
        grads_ref[:R] = partial.T[:R].astype(BF16)
        pos_out[...] = jnp.zeros(pos_out.shape, F32)
        pos_out[0:1] = jnp.sum(back.T[R:], axis=0, keepdims=True)
        both = loose[own, 4 * LANES :].T
        pos_out[1:2] = jnp.sum(both[:R], axis=0, keepdims=True)
        pos_out[2:3] = jnp.sum(both[R:], axis=0, keepdims=True)


def scalar_kernel(
    molecules, rows, atoms,
    scalars, rows_ref, filter_1, filter_2, scalar_parts, radial_in, geo_in,
    sum_ref, grads_ref, pos_out, grad_w_ref,
    weights_ref, picks, many, heads_ref, near, near_last, stage, loose, loose_low, counts, pre,
    grad_pre, grad_radial, products, sums, gates, bends,
    q, key, v0, gs,
    ss, gq, gk, g0, gx, gy, gz,
    fss, fgq, fgk, fg0, fgx, fgy, fgz,
):
    t = pl.program_id(0)
    start = scalars[0]
    own = slice(HALO, HALO + atoms)
    radial, geo = radial_in.at[0], geo_in.at[0]
    g_pos = (gx, gy, gz)
    blocks = block_list(molecules, rows)
    distances = (near, near_last)

    @pl.when(t == 0)
    def _():
        set_filters(weights_ref, filter_1, filter_2)
        set_picks(picks)
        row = lax.broadcasted_iota(jnp.int32, (2 * LANES, 2 * LANES), 0)
        lane = lax.broadcasted_iota(jnp.int32, (2 * LANES, 2 * LANES), 1)
        heads_ref[...] = jnp.where(row // HEAD == lane // HEAD, 1.0, 0.0).astype(BF16)
        set_distances(near, blocks[0][1], blocks[0][2])
        set_distances(near_last, blocks[-1][1], blocks[-1][2])
        lanes = slice(QK * LANES, (V0_COUNT + 1) * LANES)
        spread(rows_ref, lanes, stage, blocks, distances, start)
        for n, target in enumerate((q, key, v0)):
            target[...] = stage[n].astype(BF16)
        set_multiplicities(stage.at[3], many, blocks, rows)
        summed = scalar_parts[0].astype(F32)
        for f in range(1, scalar_parts.shape[0]):
            summed = summed + scalar_parts[f].astype(F32)
        summed = jnp.concatenate([summed, jnp.zeros_like(summed)], axis=0).T.astype(BF16)
        loose_low[own] = summed[:atoms]
        loose_low[:HALO] = summed[atoms : atoms + HALO]
        loose_low[HALO + atoms : 2 * HALO + atoms] = summed[atoms + HALO : atoms + 2 * HALO]
        end = 2 * HALO + atoms
        loose_low[end:] = jnp.zeros((loose_low.shape[0] - end, LANES), BF16)
        spread(loose_low, slice(None), stage, blocks, distances, start)
        gs[...] = stage[0].astype(BF16)
        for total in (ss, gq, gk, g0, gx, gy, gz):
            total[...] = jnp.zeros(total.shape, BF16)
        grad_w_ref[...] = jnp.zeros(grad_w_ref.shape, F32)

    counts[...] = dot(many[t], picks[...])
    pre[...] = dot(radial[...], weights_ref[...])

    def multiply(k, _):
        for o, size in halves(rows):
            here = pl.ds(pl.multiple_of(k * rows + o, SUB), size)
            ii, jj = (t, slice(o, o + size)), (t + 1 + k, slice(o, o + size))
            fk, dk = gate(pre[here, :LANES])
            f0, d0 = gate(pre[here, LANES:])
            k_ij, k_ji = q[ii] * key[jj] * fk, q[jj] * key[ii] * fk
            s_ij, s_ji = gs[ii] * v0[jj] * f0, gs[jj] * v0[ii] * f0
            gates[0, here, :] = fk
            gates[1, here, :] = f0
            gates[2, here, :] = dk
            gates[3, here, :] = d0
            products[0, here, :LANES] = k_ij
            products[0, here, LANES:] = k_ji
            products[1, here, :LANES] = s_ij
            products[1, here, LANES:] = s_ji
        return 0

    lax.fori_loop(0, OFFSETS, multiply, 0)
    sums[0] = dot(products[0], heads_ref[...])
    sums[1] = dot(products[1], heads_ref[...])

    def channel(o, here, ii, jj, k):
        fk, f0, dk, d0 = [gates[n, here, :] for n in range(4)]
        envelope, bend = geo[GEO_ENVELOPE, here, :], geo[GEO_BEND, here, :]
        side_in = []
        for side in range(2):
            lanes = slice(side * LANES, (side + 1) * LANES)
            m = counts[pl.ds(o, SUB), lanes_of(side * OFFSETS + k)]
            h, o_ = (ii, jj) if side == 0 else (jj, ii)
            side_in.append(
                (m, sums[0, here, lanes], sums[1, here, lanes])
                + (q[h], key[o_], gs[h], v0[o_])
            )
        old = [ref[jj] for ref in (g0, gk, ss, gq)]

        def compute():
            gives, news = [], []
            for m, score, g_att, qh, kt, gh, vt in side_in:
                act, rise = gate(0.5 * score)
                m, g_att = m.astype(BF16), g_att.astype(BF16)
                weight = m * envelope
                att = act * weight
                g_score = g_att * (0.5 * rise) * weight
                lift = m * (g_att * act)
                bv, dv = f0 * att, fk * g_score
                gives.append((vt * bv, kt * dv, gh * bv, qh * dv))
                news.append((qh * kt * g_score, gh * vt * att, lift))
            one, two = gives
            new = [x + y for x, y in zip(*news)]
            stores = [
                (ref, jj, x + y)
                for ref, x, y in zip((g0, gk, ss, gq), old, (one[2], one[3], two[0], two[1]))
            ]
            stores.append((grad_pre, (here, slice(0, LANES)), new[0] * dk))
            stores.append((grad_pre, (here, slice(LANES, None)), new[1] * d0))
            stores.append((bends, (here, slice(None)), new[2] * bend * (1.0 / HEAD)))
            return [one[0], one[1], two[2], two[3]], stores

        return compute

    carried(rows, t, (fss, fgq, fg0, fgk), 2, channel)
    grad_radial[...] = dot_nt(grad_pre[...], weights_ref[:LANES])
    grad_w_ref[...] = grad_w_ref[...] + dot_tn(geo[GEO_OWN], grad_pre[...])

    def turn(o, here, ii, jj, k):
        ways = [geo[GEO_WAY + d, here, :] for d in range(3)]
        grad, slope, bend = grad_radial[here, :], geo[GEO_SLOPE, here, :], bends[here, :]
        old = [g[jj] for g in g_pos]

        def compute():
            pull = grad.astype(BF16) * slope + bend
            out = [way * pull for way in ways]
            return out, [(g_pos[d], jj, old[d] - out[d]) for d in range(3)]

        return compute

    carried(rows, t, (fgx, fgy, fgz), 7, turn)

    @pl.when(t == SPAN - 1)
    def _():
        totals = (ss, g0, gq, gk, gx, gy, gz, gz)
        firsts = (fss, fg0, fgq, fgk, fgx, fgy, fgz, fgz)
        collect(tuple(zip(totals, firsts)), loose, blocks, distances, start)
        both = loose[own, :LANES].T
        sum_ref[...] = both[:R].astype(BF16)
        grads_ref[2 * R :] = both[R:].astype(BF16)
        grads_ref[: 2 * R] = loose[own, LANES : 2 * LANES].T.astype(BF16)
        pos_out[...] = jnp.zeros(pos_out.shape, F32)
        both = loose[own, 2 * LANES : 3 * LANES].T
        pos_out[0:1] = jnp.sum(both[:R], axis=0, keepdims=True)
        pos_out[1:2] = jnp.sum(both[R:], axis=0, keepdims=True)
        both = loose[own, 3 * LANES :].T
        pos_out[2:3] = jnp.sum(both[:R], axis=0, keepdims=True)


def whole(memory=pltpu.VMEM):
    return pl.BlockSpec(memory_space=memory)


def params(mib=60):
    return pltpu.CompilerParams(vmem_limit_bytes=mib * 1024 * 1024)


def edge_sizes(atoms):
    molecules = (atoms + 2 * (MOL - 1)) // MOL
    full, rest = divmod(molecules, BLOCK)
    rows = full * ROW_GROUPS * BLOCK + -(-ROW_GROUPS * rest // BLOCK) * BLOCK
    rows = -(-rows // SUB) * SUB
    tall = -(-(HALO + molecules * MOL) // SUB) * SUB
    return molecules, rows, tall


def by_step(shape):
    zeros = (0,) * (len(shape) - 1)
    return pl.BlockSpec((1,) + shape[1:], lambda t: (t,) + zeros)


def fixed(shape):
    zeros = (0,) * len(shape)
    return pl.BlockSpec(shape, lambda t: zeros)


def edge_call(kernel, atoms, inputs, stepped_in, outs, stepped_out, scratch):
    molecules, rows, _ = edge_sizes(atoms)
    return pl.pallas_call(
        functools.partial(kernel, molecules, rows, atoms),
        grid=(SPAN,),
        out_shape=[jax.ShapeDtypeStruct(s, kind) for s, kind in outs + stepped_out],
        in_specs=[whole(pltpu.SMEM)]
        + [fixed(x.shape) for x in inputs[1:]]
        + [by_step(x.shape) for x in stepped_in],
        out_specs=[fixed(s) for s, _ in outs] + [by_step(s) for s, _ in stepped_out],
        scratch_shapes=[pltpu.VMEM(s, kind) for s, kind in scratch],
        compiler_params=params(),
    )(*inputs, *stepped_in)


def shared_scratch(atoms):
    molecules, rows, tall = edge_sizes(atoms)
    batch = OFFSETS * rows
    blocks = block_list(molecules, rows)
    return {
        "weights": ((2 * LANES, 2 * LANES), BF16),
        "picks": ((LANES, 2 * OFFSETS * LANES), BF16),
        "many": ((SPAN, rows, LANES), BF16),
        "mask": ((rows, LANES), F32),
        "near": ((LANE_GROUPS, STEPS * blocks[0][1], WINDOW), jnp.int32),
        "near_last": ((LANE_GROUPS, STEPS * blocks[-1][1], WINDOW), jnp.int32),
        "stage8": ((8, STEPS, rows, LANES), F32),
        "stage4": ((4, STEPS, rows, LANES), F32),
        "loose5": ((tall, 5 * LANES), F32),
        "loose4": ((tall, 4 * LANES), F32),
        "loose_low": ((tall, LANES), BF16),
        "tall": ((STEPS, rows, LANES), F32),
        "low": ((STEPS, rows, LANES), BF16),
        "first": ((SPAN, rows, LANES), F32),
        "counts": ((rows, 2 * OFFSETS * LANES), F32),
        "pre": ((batch, 2 * LANES), F32),
        "grad_pre": ((batch, 2 * LANES), BF16),
        "line": ((batch, LANES), F32),
        "line2": ((2, batch, LANES), BF16),
        "line3": ((3, batch, LANES), BF16),
        "line4": ((4, batch, LANES), BF16),
        "line1": ((batch, LANES), BF16),
        "wide2": ((2, batch, 2 * LANES), BF16),
        "wide2f": ((2, batch, 2 * LANES), F32),
    }


def offsets_in_block(neighbours, mask, first):
    lane = lax.broadcasted_iota(jnp.int32, neighbours.shape, 1)
    diff = neighbours - (first + lane)
    return jnp.where(diff < 0, diff + MOL, diff) * mask


def pieces(x):
    a = x.astype(BF16)
    rest = x - a.astype(F32)
    b = rest.astype(BF16)
    return a, b, (rest - b.astype(F32)).astype(BF16)


def edge_groups(features, vectors, cot_f, cot_v, neighbours, mask, positions, first):
    diff = offsets_in_block(neighbours[...], mask[...], first).astype(F32).astype(BF16)
    groups = [jnp.concatenate([features[...], cot_f[...], diff], axis=0)]
    for d in range(3):
        rows = [x.astype(F32) for x in pieces(positions[d : d + 1])]
        rows = jnp.concatenate(rows + [jnp.zeros((29, LANES), F32)], axis=0).astype(BF16)
        groups.append(jnp.concatenate([vectors[d], cot_v[d], rows], axis=0))
    return groups


def halo_kernel(atoms, scalars, *refs):
    row_first = scalars[2]
    lane = lax.broadcasted_iota(jnp.int32, (GROUP_ROWS, LANES), 1)
    for end, at, out in ((0, atoms - LANES, refs[14]), (1, 0, refs[15])):
        groups = edge_groups(*refs[7 * end : 7 * end + 7], row_first + at)
        total = None
        for g, group in enumerate(groups):
            by = (HALO * (g + 1) if end == 0 else HALO * g) % LANES
            moved = group.astype(F32)
            moved = pltpu.roll(moved, by, 1) if by else moved
            total = moved if total is None else jnp.where(lane >= HALO * g, moved, total)
        out[...] = total.astype(BF16)


def halo_call(atoms, scalars, arrays):
    specs = []
    for at in (atoms // LANES - 1, 0):
        for x in arrays:
            shape = x.shape[:-1] + (LANES,)
            index = (0,) * (x.ndim - 1) + (at,)
            specs.append(pl.BlockSpec(shape, lambda *_, index=index: index))
    out = jax.ShapeDtypeStruct((GROUP_ROWS, LANES), BF16)
    return pl.pallas_call(
        functools.partial(halo_kernel, atoms),
        grid=(1,),
        out_shape=[out, out],
        in_specs=[whole(pltpu.SMEM)] + specs,
        out_specs=[whole(), whole()],
        compiler_params=params(),
    )(scalars, *arrays, *arrays)


def column(row):
    return jnp.broadcast_to(row, (8, row.shape[1])).T[:, :1]


def normalised(f):
    mean = jnp.mean(f, axis=0, keepdims=True)
    centred = f - mean
    inv = lax.rsqrt(jnp.mean(centred * centred, axis=0, keepdims=True) + EPSILON)
    return centred * inv, mean, inv


def dense_kernel(
    atoms,
    scalars, features, vectors, cot_f, cot_v, neighbours, mask, positions, low_ref, high_ref,
    gain_ref, bias_ref, w_query, w_key, w_value, w_vector, w_output,
    rows_ref, part_ref, stat_ref,
    w_qk, w_v0, w_v12, w_vec_t, w_out,
):
    chan_first = pl.multiple_of(scalars[1], R)
    row_first = scalars[2]
    gain, bias = column(gain_ref[...]), column(bias_ref[...])
    w_qk[:R] = w_query[...]
    w_qk[R:] = w_key[...]
    w_v0[:R] = w_value[0]
    w_v0[R:] = jnp.zeros((R, H), BF16)
    w_v12[:R] = w_value[1]
    w_v12[R:] = w_value[2]
    for p in range(3):
        w_vec_t[p * R : (p + 1) * R] = w_vector[p]
    w_out[...] = jnp.concatenate([w_output[p] for p in range(3)], axis=0).astype(F32).T.astype(BF16)

    def block(f, v, cf, cv, own_v, diff, pos):
        width = f.shape[1]
        normed, mean, inv = normalised(f)
        turned = (normed * gain + bias).T.astype(BF16)
        kinds = lax.broadcasted_iota(jnp.int32, (R, width), 0)
        kinds = jnp.where(kinds < 32, kinds, MOL + 32 - kinds).astype(F32)
        counts = jnp.zeros((R, width), F32)
        for s in range(diff.shape[0]):
            counts = counts + jnp.where(diff[s : s + 1] == kinds, 1.0, 0.0)
        none = jnp.zeros((R, width), F32)
        counts = jnp.concatenate([none, counts], axis=0).T
        low = lax.broadcasted_iota(jnp.int32, (width, LANES), 1) < R
        pairs = [None] * 10
        pairs[QK] = dot_nt(turned, w_qk[...])
        pairs[V0_COUNT] = dot_nt(turned, w_v0[...]) + counts
        v12 = dot_nt(turned, w_v12[...]).astype(BF16).astype(F32)
        v11 = jnp.where(low, v12, pltpu.roll(v12, R, 1))
        pairs[V12] = v12
        pairs[VEC01] = jnp.concatenate([own_v[0], own_v[1]], axis=0).T
        pairs[VEC2] = jnp.concatenate([own_v[2], none], axis=0).T
        pairs[W01] = pairs[VEC01] * v11
        pairs[W2V2] = jnp.where(low, pairs[VEC2] * v11, v12)
        pairs[C01] = jnp.concatenate([cv[0], cv[1]], axis=0).T
        pairs[C2_COUNT] = jnp.concatenate([cv[2], none], axis=0).T + counts
        pairs[POS] = jnp.concatenate([pos, jnp.zeros((LANES - 9, width), F32)], axis=0).T
        vec_dot = grad_0 = 0.0
        for d in range(3):
            proj = dot(w_vec_t[...], v[d])
            vec_dot = vec_dot + proj[:R] * proj[R : 2 * R]
            grad_0 = grad_0 + cv[d] * proj[2 * R :]
        grad_out = jnp.concatenate([grad_0, cf * vec_dot, cf], axis=0).astype(BF16)
        part = dot(w_out[...], grad_out)
        return [x.astype(BF16) for x in pairs], part.astype(BF16), mean, inv

    wide = 2 * LANES

    def step(b, _):
        at = pl.multiple_of(b * wide, wide)
        here = pl.ds(at, wide)
        own_v = [vectors[d, pl.ds(chan_first, R), here].astype(F32) for d in range(3)]
        diff = offsets_in_block(neighbours[:, here], mask[:, here], row_first + at)
        places = [p.astype(F32) for d in range(3) for p in pieces(positions[d : d + 1, here])]
        pairs, part, mean, inv = block(
            features[:, here].astype(F32),
            [vectors[d, :, here] for d in range(3)],
            cot_f[:, here].astype(F32),
            [cot_v[d, :, here].astype(F32) for d in range(3)],
            own_v,
            diff.astype(F32),
            jnp.concatenate(places, axis=0),
        )
        there = pl.ds(pl.multiple_of(HALO + at, 2 * SUB), wide)
        for n, pair in enumerate(pairs):
            rows_ref[there, n * LANES : (n + 1) * LANES] = pair
        part_ref[:, here] = part
        stat_ref[0:1, here] = mean
        stat_ref[1:2, here] = inv
        return 0

    lax.fori_loop(0, atoms // wide, step, 0)

    lane = lax.broadcasted_iota(jnp.int32, (GROUP_ROWS, LANES), 1)
    packed_low, packed_high = low_ref[...].astype(F32), high_ref[...].astype(F32)
    groups = []
    for g in range(4):
        a = pltpu.roll(packed_low, (LANES - HALO * g) % LANES, 1) if g else packed_low
        by = (LANES + HALO - HALO * g) % LANES
        b = pltpu.roll(packed_high, by, 1) if by else packed_high
        both = jnp.where(lane < HALO, a, jnp.where(lane < 2 * HALO, b, 0.0))
        groups.append(both)
    pick_rows = lax.broadcasted_iota(jnp.int32, (H, LANES), 0)
    own_v, pos = [], []
    for d in range(3):
        g = groups[1 + d]
        found = g[:R]
        for f in range(1, H // R):
            found = jnp.where(chan_first == f * R, g[f * R : (f + 1) * R], found)
        own_v.append(found)
        pos.append(g[320:323])
    pairs, part, _, _ = block(
        groups[0][:H],
        [groups[1 + d][:H].astype(BF16) for d in range(3)],
        groups[0][H : H + R],
        [groups[1 + d][H : H + R] for d in range(3)],
        own_v,
        groups[0][H + R :],
        jnp.concatenate(pos, axis=0),
    )
    high = HALO + atoms
    tall = rows_ref.shape[0]
    for n, pair in enumerate(pairs):
        lanes = slice(n * LANES, (n + 1) * LANES)
        rows_ref[:HALO, lanes] = pair[:HALO]
        rows_ref[high : high + HALO, lanes] = pair[HALO : 2 * HALO]
        rows_ref[high + HALO :, lanes] = jnp.zeros((tall - high - HALO, LANES), BF16)
    part_ref[:, atoms:] = part


def both_diagonals(grad, f):
    at = f * LANES
    return 0.5 * (grad[:R, at : at + R] + grad[R:, at + R : at + LANES])


def layer_kernel(
    atoms,
    scalars, features, vectors, cot_f, cot_v, gathered, w_vector, w_output,
    feat_out, delta_ref, square_ref, send_ref, flat_ref,
    w_vec, w_vec_t, w_out_t, t_vec, t_out,
):
    chan_first = pl.multiple_of(scalars[1], R)
    for p in range(3):
        w_vec_t[p * R : (p + 1) * R] = w_vector[p]
        w_out_t[p * R : (p + 1) * R] = w_output[p]
    w_vec[...] = w_vec_t[...].astype(F32).T.astype(BF16)
    t_vec[...] = jnp.zeros(t_vec.shape, F32)
    t_out[...] = jnp.zeros(t_out.shape, F32)
    wide = 2 * LANES
    split = send_ref.shape[0]

    def step(b, _):
        at = pl.multiple_of(b * wide, wide)
        here = pl.ds(at, wide)
        all_sums = gathered[:, here]
        outputs = dot(w_out_t[...], all_sums)
        out_0, out_1, out_2 = outputs[:R], outputs[R : 2 * R], outputs[2 * R :]
        cf = cot_f[:, here].astype(F32)
        grad_dot = cf * out_1
        vec_dot = grad_0 = 0.0
        for d in range(3):
            proj = dot(w_vec_t[...], vectors[d, :, here])
            first, second, third = proj[:R], proj[R : 2 * R], proj[2 * R :]
            cv = cot_v[d, :, here].astype(F32)
            vec_dot = vec_dot + first * second
            grad_0 = grad_0 + cv * third
            delta_ref[d, :, here] = third * out_0
            grad_proj = jnp.concatenate(
                [grad_dot * second, grad_dot * first, cv * out_0], axis=0
            ).astype(BF16)
            part = dot(w_vec[...], grad_proj).astype(BF16)
            for f in range(split):
                send_ref[f, d * R : (d + 1) * R, here] = part[f * R : (f + 1) * R]
            t_vec[...] = t_vec[...] + dot_nt(grad_proj, vectors[d, :, here])
        delta = vec_dot * out_1 + out_2
        moved = features[pl.ds(chan_first, R), here].astype(F32) + delta
        feat_out[:, here] = moved.astype(BF16)
        grad_out = jnp.concatenate([grad_0, cf * vec_dot, cf], axis=0).astype(BF16)
        t_out[...] = t_out[...] + dot_nt(grad_out, all_sums)
        square_ref[0:1, here] = jnp.sum(moved * moved, axis=0, keepdims=True)
        square_ref[1:2, here] = jnp.sum(delta * delta, axis=0, keepdims=True)
        return 0

    lax.fori_loop(0, atoms // wide, step, 0)
    flat_ref[: 3 * R] = t_vec[...].astype(BF16)
    flat_ref[3 * R :] = t_out[...].astype(BF16)


def normal_kernel(
    atoms,
    scalars, features, stat, vectors, delta_ref, square_ref, sums_ref,
    grads_b, grads_a, pos_a, pos_b, mask, gain_ref, bias_ref,
    w_query, w_key, w_value, grad_filters_a, grad_filters_b,
    vec_out, send_ref, flat_ref,
    w_five, t_five,
):
    chan_first = pl.multiple_of(scalars[1], R)
    gain, bias = column(gain_ref[...]), column(bias_ref[...])
    five = [w_query[...], w_key[...]] + [w_value[p] for p in range(3)]
    w_five[...] = jnp.concatenate(five, axis=0).astype(F32).T.astype(BF16)
    t_five[...] = jnp.zeros(t_five.shape, F32)
    wide = 2 * LANES
    split = send_ref.shape[0]

    def step(b, _):
        at = pl.multiple_of(b * wide, wide)
        here = pl.ds(at, wide)
        real = mask[:, here].astype(F32)
        square_v = square_dv = 0.0
        for d in range(3):
            delta = delta_ref[d, :, here] + sums_ref[d, :, here]
            moved = vectors[d, pl.ds(chan_first, R), here].astype(F32) + delta
            vec_out[d, :, here] = moved.astype(BF16)
            square_v = square_v + moved * moved
            square_dv = square_dv + delta * delta
        normed = (features[:, here].astype(F32) - stat[0:1, here]) * stat[1:2, here]
        normal = (normed * gain + bias).astype(BF16)
        grads = jnp.concatenate([grads_b[:, here], grads_a[:, here]], axis=0)
        t_five[...] = t_five[...] + dot_nt(grads, normal)
        part = dot(w_five[...], grads)
        rounded = part.astype(BF16)
        for f in range(split):
            send_ref[f, :R, here] = rounded[f * R : (f + 1) * R]
        hat = part * gain
        tops = [
            jnp.sum(hat, axis=0, keepdims=True),
            jnp.sum(hat * normed, axis=0, keepdims=True),
        ]
        exact = [pos_a[d : d + 1, here] + pos_b[d : d + 1, here] for d in range(3)]
        exact += [square_ref[n : n + 1, here] * real for n in range(2)]
        for x in (square_v, square_dv):
            exact.append(jnp.sum(x, axis=0, keepdims=True) * real)
        heads = [x.astype(BF16).astype(F32) for x in exact]
        tops = tops + heads + [x - y for x, y in zip(exact, heads)]
        tops = jnp.concatenate(tops, axis=0).astype(BF16)
        for f in range(split):
            send_ref[f, R:, here] = tops
        return 0

    lax.fori_loop(0, atoms // wide, step, 0)
    grad_a, grad_b = grad_filters_a[...], grad_filters_b[...]
    filters = [both_diagonals(g, f) for g in (grad_b, grad_a) for f in range(2)]
    flat_ref[: 5 * R] = t_five[...].astype(BF16)
    flat_ref[5 * R :] = jnp.concatenate(filters, axis=1).astype(BF16)


def final_kernel(
    atoms,
    scalars, got, got_vec, features, stat, gain_ref, cot_f, cot_v, back_ref, mask,
    grad_feat, grad_vec, grad_pos, small_ref,
):
    chan_first = pl.multiple_of(scalars[1], R)
    whole_gain = column(gain_ref[...])
    gain = whole_gain[:R]
    for f in range(1, H // R):
        gain = jnp.where(chan_first == f * R, whole_gain[f * R : (f + 1) * R], gain)

    def summed(ref, rows):
        total = ref[0, rows].astype(F32)
        for f in range(1, ref.shape[0]):
            total = total + ref[f, rows].astype(F32)
        return total

    tops = summed(got, slice(R, R + EXTRAS))
    grad_normal = summed(got, slice(0, R))
    inv = stat[1:2]
    normed = (features[pl.ds(chan_first, R), :].astype(F32) - stat[0:1]) * inv
    inner = grad_normal * gain - tops[0:1] * (1.0 / H) - normed * (tops[1:2] * (1.0 / H))
    grad_feat[...] = cot_f[...].astype(F32) + inv * inner
    for d in range(3):
        part = summed(got_vec, slice(d * R, (d + 1) * R))
        grad_vec[d] = cot_v[d].astype(F32) + part + back_ref[d]
    exact = tops[2:9] + tops[9:16]
    grad_pos[...] = exact[:3]
    ones = jnp.ones((8, atoms), BF16)
    gains = dot_nt(ones, (grad_normal * normed).astype(BF16))
    biases = dot_nt(ones, grad_normal.astype(BF16))
    totals = jnp.sum(exact[3:7], axis=1, keepdims=True)
    real = jnp.sum(mask[...].astype(F32), axis=1, keepdims=True)
    numbers = jnp.concatenate([totals, real, jnp.zeros((3, 1), F32)], axis=0)
    small = jnp.concatenate([gains, biases, jnp.broadcast_to(numbers, (8, LANES))], axis=1)
    high = small.astype(BF16)
    small_ref[:8] = high.astype(F32)
    small_ref[8:] = small - high.astype(F32)


def unpack_kernel(
    share,
    got,
    g_gain, g_bias, g_query, g_key, g_value, g_vector, g_output, g_key_f, g_value_f, rms_ref,
):
    every = [got[n].astype(F32) for n in range(got.shape[0])]
    total = 0.0
    for x in every:
        total = total + (x[2 * share : 2 * share + 8] + x[2 * share + 8 : 2 * share + 16])
    g_gain[...] = total[0:1, :R]
    g_bias[...] = total[0:1, R : 2 * R]
    numbers = total[:, LANES : LANES + 1]
    size = jnp.where(lax.broadcasted_iota(jnp.int32, (8, 1), 0) < 2, 1.0, 3.0) * H
    rms = jnp.sqrt(numbers / (numbers[4:5] * size) + 1e-06)
    rms_ref[...] = jnp.broadcast_to(rms, (8, LANES)).T[:1, :8]
    early = [(g, p) for g in (g_vector, g_output) for p in range(3)]
    late = [(g_query, None), (g_key, None)] + [(g_value, p) for p in range(3)]
    for n, x in enumerate(every):
        for first, names in ((0, early), (share, late)):
            at = n * share
            while at < (n + 1) * share:
                m = at // R
                size = min((m + 1) * R, (n + 1) * share) - at
                value = x[first + at - n * share : first + at - n * share + size]
                rows = slice(at - m * R, at - m * R + size)
                at += size
                if m == len(names):
                    g_key_f[rows] = value[:, :R]
                    for p in range(3):
                        g_value_f[p, rows] = value[:, (1 + p) * R : (2 + p) * R]
                    continue
                g, p = names[m]
                if p is None:
                    g[rows] = value
                else:
                    g[p, rows] = value


def everywhere(x, axis):
    count = lax.axis_size(axis)
    return lax.all_to_all(jnp.broadcast_to(x[None], (count,) + x.shape), axis, 0, 0)


def per_device(
    features, vectors, positions, atom_mask, neighbours, ln_gain, ln_bias,
    w_query, w_key, w_value, w_vector, w_output, w_key_filter, w_value_filter,
    cot_features, cot_vectors,
):
    channels = w_query.shape[1]
    atoms = features.shape[1]
    count = lax.axis_size("atoms")
    split = lax.axis_size("feat")
    chan_first = lax.axis_index("feat") * channels
    row_first = lax.axis_index("atoms") * atoms
    start = HALO - lax.rem(row_first, MOL)
    scalars = jnp.stack([start, chan_first, row_first]).astype(jnp.int32)
    molecules, rows_each, tall = edge_sizes(atoms)
    w_query, w_key = w_query.T, w_key.T
    w_value, w_vector, w_output = [jnp.swapaxes(w, 1, 2) for w in (w_value, w_vector, w_output)]
    mask = atom_mask.reshape(1, atoms)
    gain, bias = ln_gain.reshape(1, H), ln_bias.reshape(1, H)

    ends = halo_call(
        atoms,
        scalars,
        (features, vectors, cot_features, cot_vectors, neighbours, mask, positions),
    )
    low = lax.ppermute(ends[0], "atoms", [(i, i + 1) for i in range(count - 1)])
    high = lax.ppermute(ends[1], "atoms", [(i + 1, i) for i in range(count - 1)])

    inputs = (
        scalars, features, vectors, cot_features, cot_vectors, neighbours, mask, positions,
        low, high, gain, bias, w_query, w_key, w_value, w_vector, w_output,
    )
    rows, part, stat = pl.pallas_call(
        functools.partial(dense_kernel, atoms),
        out_shape=[
            jax.ShapeDtypeStruct((tall, 10 * LANES), BF16),
            jax.ShapeDtypeStruct((H, atoms + LANES), BF16),
            jax.ShapeDtypeStruct((8, atoms), F32),
        ],
        in_specs=[whole(pltpu.SMEM)] + [whole()] * (len(inputs) - 1),
        out_specs=[whole()] * 3,
        scratch_shapes=[
            pltpu.VMEM((LANES, H), BF16),
            pltpu.VMEM((LANES, H), BF16),
            pltpu.VMEM((LANES, H), BF16),
            pltpu.VMEM((3 * R, H), BF16),
            pltpu.VMEM((H, 3 * R), BF16),
        ],
        compiler_params=params(),
    )(*inputs)
    scalar_parts = lax.all_to_all(part.reshape(split, channels, atoms + LANES), "feat", 0, 0)

    kinds = shared_scratch(atoms)
    batch = OFFSETS * rows_each
    names = ["mask", "near", "near_last"] + ["tall"] * 3
    radial, geo = edge_call(
        geometry_kernel,
        atoms,
        (scalars, rows),
        (),
        [],
        [((SPAN, batch, 2 * LANES), BF16), ((SPAN, GEO, batch, LANES), BF16)],
        [kinds[name] for name in names],
    )
    names = ["weights", "picks", "many", "weights", "near", "near_last", "stage4", "loose4"]
    names += ["loose_low", "counts", "pre", "grad_pre", "line", "wide2", "wide2f", "line4", "line1"]
    names += ["low"] * 4 + ["low"] * 7 + ["first"] * 7
    scalar_sum, grads_b, pos_b, grad_filters_b = edge_call(
        scalar_kernel,
        atoms,
        (scalars, rows, w_key_filter, w_value_filter[0], scalar_parts),
        (radial, geo),
        [
            ((R, atoms), BF16),
            ((3 * R, atoms), BF16),
            ((8, atoms), F32),
            ((LANES, 2 * LANES), F32),
        ],
        [],
        [kinds[name] for name in names],
    )
    gathered = lax.all_gather(scalar_sum, "feat", axis=0, tiled=True)

    inputs = (
        scalars, features, vectors, cot_features, cot_vectors, gathered, w_vector, w_output,
    )
    new_features, delta, squares, send_vec, flat_early = pl.pallas_call(
        functools.partial(layer_kernel, atoms),
        out_shape=[
            jax.ShapeDtypeStruct((R, atoms), BF16),
            jax.ShapeDtypeStruct((3, R, atoms), F32),
            jax.ShapeDtypeStruct((8, atoms), F32),
            jax.ShapeDtypeStruct((split, 3 * R, atoms), BF16),
            jax.ShapeDtypeStruct((6 * R, H), BF16),
        ],
        in_specs=[whole(pltpu.SMEM)] + [whole()] * (len(inputs) - 1),
        out_specs=[whole()] * 5,
        scratch_shapes=[
            pltpu.VMEM((H, 3 * R), BF16),
            pltpu.VMEM((3 * R, H), BF16),
            pltpu.VMEM((3 * R, H), BF16),
            pltpu.VMEM((3 * R, H), F32),
            pltpu.VMEM((3 * R, H), F32),
        ],
        compiler_params=params(),
    )(*inputs)
    share = 6 * R // count
    got_vec = lax.all_to_all(send_vec, "feat", 0, 0)
    shares_early = lax.all_to_all(flat_early.reshape(count, share, H), "atoms", 0, 0)

    names = ["weights", "picks", "many", "near", "near_last", "stage8", "loose5"]
    names += ["counts", "pre", "grad_pre", "line", "line3"]
    names += ["low"] * 7 + ["low"] * 10 + ["first"] * 10
    sums, back, grads_a, pos_a, grad_filters_a = edge_call(
        vector_kernel,
        atoms,
        (scalars, rows, w_value_filter[1], w_value_filter[2]),
        (radial, geo),
        [
            ((3, R, atoms), F32),
            ((3, R, atoms), F32),
            ((2 * R, atoms), BF16),
            ((8, atoms), F32),
            ((LANES, 2 * LANES), F32),
        ],
        [],
        [kinds[name] for name in names],
    )

    inputs = (
        scalars, features, stat, vectors, delta, squares, sums, grads_b, grads_a, pos_a, pos_b,
        mask, gain, bias, w_query, w_key, w_value, grad_filters_a, grad_filters_b,
    )
    new_vectors, send, flat_late = pl.pallas_call(
        functools.partial(normal_kernel, atoms),
        out_shape=[
            jax.ShapeDtypeStruct((3, R, atoms), BF16),
            jax.ShapeDtypeStruct((split, R + EXTRAS, atoms), BF16),
            jax.ShapeDtypeStruct((6 * R, H), BF16),
        ],
        in_specs=[whole(pltpu.SMEM)] + [whole()] * (len(inputs) - 1),
        out_specs=[whole()] * 3,
        scratch_shapes=[pltpu.VMEM((H, 5 * R), BF16), pltpu.VMEM((5 * R, H), F32)],
        compiler_params=params(),
    )(*inputs)
    got = lax.all_to_all(send, "feat", 0, 0)
    shares_late = lax.all_to_all(flat_late.reshape(count, share, H), "atoms", 0, 0)

    inputs = (
        scalars, got, got_vec, features, stat, gain, cot_features, cot_vectors, back, mask,
    )
    grad_features, grad_vectors, grad_positions, small = pl.pallas_call(
        functools.partial(final_kernel, atoms),
        out_shape=[
            jax.ShapeDtypeStruct((R, atoms), F32),
            jax.ShapeDtypeStruct((3, R, atoms), F32),
            jax.ShapeDtypeStruct((3, atoms), F32),
            jax.ShapeDtypeStruct((16, H), F32),
        ],
        in_specs=[whole(pltpu.SMEM)] + [whole()] * (len(inputs) - 1),
        out_specs=[whole()] * 4,
        compiler_params=params(),
    )(*inputs)
    summed = [jnp.sum(x.astype(F32), axis=0) for x in (shares_early, shares_late)]
    mine = jnp.concatenate(summed + [small], axis=0).astype(BF16)
    every = everywhere(mine, "atoms")
    shapes = [
        (1, R), (1, R), (R, H), (R, H), (3, R, H), (3, R, H), (3, R, H), (R, R), (3, R, R), (1, 8),
    ]
    grads = pl.pallas_call(
        functools.partial(unpack_kernel, share),
        out_shape=[jax.ShapeDtypeStruct(shape, F32) for shape in shapes],
        in_specs=[whole()],
        out_specs=[whole()] * len(shapes),
        compiler_params=params(),
    )(every)
    return (
        new_features,
        new_vectors,
        grad_features,
        grad_vectors,
        grad_positions,
        grads[0].reshape(R),
        grads[1].reshape(R),
        grads[2].T,
        grads[3].T,
        jnp.swapaxes(grads[4], 1, 2),
        jnp.swapaxes(grads[5], 1, 2),
        jnp.swapaxes(grads[6], 1, 2),
        grads[7],
        grads[8],
        grads[9][0, :4],
    )


def solution(mesh):
    in_specs = (
        P(None, "atoms"),
        P(None, None, "atoms"),
        P(None, "atoms"),
        P("atoms"),
        P(None, "atoms"),
        P(),
        P(),
        P(None, "feat"),
        P(None, "feat"),
        P(None, None, "feat"),
        P(None, None, "feat"),
        P(None, None, "feat"),
        P(None, "feat"),
        P(None, None, "feat"),
        P("feat", "atoms"),
        P(None, "feat", "atoms"),
    )
    out_specs = (
        P("feat", "atoms"),
        P(None, "feat", "atoms"),
        P("feat", "atoms"),
        P(None, "feat", "atoms"),
        P(None, "atoms"),
        P("feat"),
        P("feat"),
        P(None, "feat"),
        P(None, "feat"),
        P(None, None, "feat"),
        P(None, None, "feat"),
        P(None, None, "feat"),
        P(None, "feat"),
        P(None, None, "feat"),
        P(),
    )
    return jax.shard_map(
        per_device, mesh=mesh, in_specs=in_specs, out_specs=out_specs, check_vma=False
    )
```

```python
import functools
import math

import jax
import jax.numpy as jnp
from jax import lax
from jax.experimental import pallas as pl
from jax.experimental.pallas import tpu as pltpu
from jax.sharding import PartitionSpec as P

H = 256
HEADS = 8
HEAD = H // HEADS
R = 64
MOL = 29
HALO = 32
CUTOFF = 5.0
EPSILON = 1e-05
F32 = jnp.float32
BF16 = jnp.bfloat16

LANE_GROUPS = 2
ROW_GROUPS = 3
SPAN = 5
OFFSETS = 14
STEPS = SPAN + OFFSETS
SUB = 16
LANES = 128

W01, W2V2, C01, C2_COUNT, POS, QK, V0_COUNT, V12, VEC01, VEC2 = range(10)
GROUP_ROWS = 352
EXTRAS = 16


BLOCK = 8
WINDOW = 256


def block_list(molecules, rows):
    full, rest = divmod(molecules, BLOCK)
    wide = ROW_GROUPS * BLOCK
    out = [(n * wide, wide, BLOCK) for n in range(full)]
    if rows > full * wide:
        out.append((full * wide, rows - full * wide, rest))
    return out


def row_parts(shape, axis, size):
    row = lax.broadcasted_iota(jnp.int32, shape, axis)
    group = jnp.zeros(shape, jnp.int32)
    for g in range(1, ROW_GROUPS):
        group = jnp.where(row >= g * size, g, group)
    return group, row - group * size, row < ROW_GROUPS * size


def set_distances(target, width, size):
    for r in range(LANE_GROUPS):

        def step(t, _, r=r):
            group, molecule, held = row_parts((width, WINDOW), 0, size)
            spot = t + SPAN * (LANE_GROUPS * group + r)
            spot = jnp.where(spot >= MOL, spot - MOL, spot)
            lane = lax.broadcasted_iota(jnp.int32, (width, WINDOW), 1)
            value = jnp.where(held, molecule * MOL + spot - lane, -(10**6))
            target[r, pl.ds(t * width, width), :] = value
            return 0

        lax.fori_loop(0, STEPS, step, 0)


def windows(blocks, distances, start, tall):
    for n, (first, width, size) in enumerate(blocks):
        atom = start + n * BLOCK * MOL
        base = jnp.minimum(atom // SUB * SUB, tall - WINDOW)
        base = pl.multiple_of(base, SUB)
        chosen = distances[0] if size == BLOCK else distances[1]
        ones = [jnp.where(chosen[r] == base - atom, 1.0, 0.0).astype(BF16) for r in (0, 1)]
        yield first, width, pl.ds(base, WINDOW), ones


def spread(source, lanes, stage, blocks, distances, start):
    for first, width, here, ones in windows(blocks, distances, start, source.shape[0]):
        given = source[here, lanes]
        a, b = dot(ones[0], given), dot(ones[1], given)
        low = lax.broadcasted_iota(jnp.int32, (a.shape[0], LANES), 1) < R
        for n in range(a.shape[1] // LANES):
            left, right = a[:, n * LANES : (n + 1) * LANES], b[:, n * LANES : (n + 1) * LANES]
            one = jnp.where(low, left, pltpu.roll(right, R, 1))
            two = jnp.where(low, pltpu.roll(left, R, 1), right)
            stage[2 * n, :, first : first + width] = one.reshape(STEPS, width, LANES)
            stage[2 * n + 1, :, first : first + width] = two.reshape(STEPS, width, LANES)


def spread_positions(source, lanes, targets, blocks, distances, start):
    row = lax.broadcasted_iota(jnp.int32, (LANES, 3 * LANES), 0)
    lane = lax.broadcasted_iota(jnp.int32, (LANES, 3 * LANES), 1)
    axis = jnp.where(lane >= 2 * LANES, 2, jnp.where(lane >= LANES, 1, 0))
    mine = (row >= 3 * axis) & (row < 3 * axis + 3)
    low = lane - axis * LANES < R
    wide = [jnp.where(mine & (low == (r == 0)), 1.0, 0.0).astype(BF16) for r in (0, 1)]
    for first, width, here, ones in windows(blocks, distances, start, source.shape[0]):
        given = source[here, lanes]
        total = 0.0
        for r in (0, 1):
            total = total + dot(dot(ones[r], given).astype(BF16), wide[r])
        for d, target in enumerate(targets):
            value = total[:, d * LANES : (d + 1) * LANES]
            target[:, first : first + width] = value.reshape(STEPS, width, LANES)


def collect(sources, target, blocks, distances, start):
    target[...] = jnp.zeros(target.shape, F32)
    units = []
    for first, width, here, ones in windows(blocks, distances, start, target.shape[0]):
        units.append((first, width, here, ones))
    at = 0
    while at < len(units):
        group = units[at : at + 2] if units[at][0] % SUB == 0 and at + 1 < len(units) else None
        if group is None or (group[0][1] + group[1][1]) % SUB:
            group = units[at : at + 1]
        at += len(group)
        first = group[0][0]
        size = sum(g[1] for g in group)
        blocks_in = []
        for partner, carry in sources:
            value = partner[:, first : first + size].astype(F32)
            start_part = value[:SPAN] + carry[:, first : first + size]
            blocks_in.append(jnp.concatenate([start_part, value[SPAN:]], axis=0))
        for f, width, here, ones in group:
            parts = ([], [])
            for n in range(0, len(sources), 2):
                a = blocks_in[n][:, f - first : f - first + width].reshape(STEPS * width, LANES)
                b = blocks_in[n + 1][:, f - first : f - first + width]
                b = b.reshape(STEPS * width, LANES)
                low = lax.broadcasted_iota(jnp.int32, a.shape, 1) < R
                parts[0].append(jnp.where(low, a, pltpu.roll(b, R, 1)).astype(BF16))
                parts[1].append(jnp.where(low, pltpu.roll(a, R, 1), b).astype(BF16))
            total = 0.0
            for r in (0, 1):
                total = total + dot_tn(ones[r], jnp.concatenate(parts[r], axis=1))
            target[here, :] = target[here, :] + total


def row_masks(owned, start, blocks, atoms):
    for n, (at, width, size) in enumerate(blocks):
        _, molecule, _ = row_parts((width, LANES), 0, size)
        first = start - HALO + (n * BLOCK + molecule) * MOL
        owned[at : at + width] = jnp.where((first >= 0) & (first < atoms), 1.0, 0.0)


def set_picks(picks):
    row = lax.broadcasted_iota(jnp.int32, (LANES, LANES), 0)
    lane = lax.broadcasted_iota(jnp.int32, (LANES, LANES), 1)
    base = jnp.where(lane >= R, R, 0)
    for n in range(2 * OFFSETS):
        which = 1 + n if n < OFFSETS else 33 + n - OFFSETS
        block = jnp.where(row == base + which, 1.0, 0.0).astype(BF16)
        picks[:, n * LANES : (n + 1) * LANES] = block


def set_multiplicities(count, target, blocks, rows):
    lane = lax.broadcasted_iota(jnp.int32, (rows, LANES), 1)
    inner = jnp.where(lane >= R, lane - R, lane)
    last = []
    for _, width, size in blocks:
        last.append(row_parts((width, LANES), 0, size)[0])
    doubled = (jnp.concatenate(last, axis=0) == ROW_GROUPS - 1) & (lane >= R)
    for t in range(SPAN):
        value = jnp.where(inner < 32, count[t], 0.0)
        for k in range(1, OFFSETS + 1):
            value = jnp.where(inner == 32 + k, count[t + k], value)
        if t == SPAN - 1:
            value = jnp.where(doubled, 0.0, value)
        target[t] = value.astype(BF16)


def dot(a, b):
    return jnp.dot(a, b, preferred_element_type=F32)


def dot_tn(a, b):
    return lax.dot_general(a, b, (((0,), (0,)), ((), ())), preferred_element_type=F32)


def dot_nt(a, b):
    return lax.dot_general(a, b, (((1,), (1,)), ((), ())), preferred_element_type=F32)


COSINE = (0.9999999998, -0.04934802137, 0.000405870916, -1.335212003e-06, 2.349373138e-09, -2.43963243e-12)

GEO_ENVELOPE, GEO_SLOPE, GEO_BEND, GEO_OWN, GEO_WAY, GEO_INVERSE, GEO_FREE = 0, 1, 2, 3, 4, 7, 8
GEO = 9


def geometry(pos, t, rows, owned, radial, geo):
    lane = lax.broadcasted_iota(jnp.int32, (1, LANES), 1)
    centre = jnp.where(lane >= R, lane - R, lane).astype(F32)
    inv_space = (R - 1) / CUTOFF

    def step(k, _):
        for o, size in halves(rows):
            here = pl.ds(pl.multiple_of(k * rows + o, SUB), size)
            off = [p[t, o : o + size] - p[t + 1 + k, o : o + size] for p in pos]
            mine = owned[o : o + size]
            square = off[0] * off[0] + off[1] * off[1] + off[2] * off[2]
            clamped = jnp.maximum(square, 0.01)
            inverse = lax.rsqrt(clamped)
            c = COSINE[-1]
            for term in COSINE[-2::-1]:
                c = c * clamped + term
            c = jnp.where(clamped < CUTOFF * CUTOFF, c, 0.0)
            envelope = c * c
            y = jnp.maximum(envelope - envelope * envelope, 1e-30)
            free = jnp.where(square > 0.01, 1.0, 0.0)
            bend = ((-math.pi / CUTOFF) * free) * (y * lax.rsqrt(y))
            u = (clamped * inverse) * inv_space - centre
            bump = jnp.exp(-0.5 * (u * u))
            value = bump * envelope
            high = value.astype(BF16)
            slope = bump * bend - (inv_space * free) * (u * value)
            radial[here, :LANES] = high
            radial[here, LANES:] = (value - high.astype(F32)).astype(BF16)
            geo[GEO_OWN, here, :] = (value * mine).astype(BF16)
            geo[GEO_SLOPE, here, :] = slope.astype(BF16)
            geo[GEO_BEND, here, :] = bend.astype(BF16)
            geo[GEO_ENVELOPE, here, :] = envelope.astype(BF16)
            for d in range(3):
                geo[GEO_WAY + d, here, :] = (off[d] * inverse).astype(BF16)
            geo[GEO_INVERSE, here, :] = inverse.astype(BF16)
            geo[GEO_FREE, here, :] = (inverse * free).astype(BF16)
        return 0

    lax.fori_loop(0, OFFSETS, step, 0)


def halves(rows):
    tiles = rows // SUB
    first = (tiles + 1) // 2 * SUB
    return ((0, first), (first, rows - first))


def set_filters(weights_ref, filter_1, filter_2):
    weights_ref[...] = jnp.zeros(weights_ref.shape, BF16)
    for f, ref in enumerate((filter_1, filter_2)):
        half = ref[...] * jnp.asarray(0.5, BF16)
        for part in range(2):
            for g in range(LANE_GROUPS):
                down = part * LANES + g * R
                at = f * LANES + g * R
                weights_ref[down : down + R, at : at + R] = half


def gate(h):
    t = jnp.tanh(h)
    u = 1.0 + t
    f = h * u
    return f.astype(BF16), (u + f * (1.0 - t)).astype(BF16)


def carried(rows, t, totals, group, body):
    def outer(s, _):
        o = pl.multiple_of(s * SUB, SUB)
        block = pl.ds(o, SUB)
        ii = (t, block)
        sums = None
        for k in range(0, OFFSETS, group):
            loaded = []
            for n in range(k, k + group):
                here = pl.ds(o + n * rows, SUB)
                loaded.append(body(o, here, ii, (t + 1 + n, block), n))
            done = [f() for f in loaded]
            given = [one for one, _ in done]
            while len(given) > 1:
                left = given[len(given) // 2 * 2 :]
                pairs = zip(given[0::2], given[1::2])
                given = [[x + y for x, y in zip(a, b)] for a, b in pairs] + left
            total = [x.astype(F32) for x in given[0]]
            sums = total if sums is None else [x + y for x, y in zip(sums, total)]
            for _, stores in done:
                for ref, index, value in stores:
                    ref[index] = value
        for total, value in zip(totals, sums):
            total[ii] = value
        return 0

    lax.fori_loop(0, rows // SUB, outer, 0)


def lanes_of(n):
    return slice(n * LANES, (n + 1) * LANES)


def geometry_kernel(
    molecules, rows, atoms,
    scalars, rows_ref, radial_out, geo_out, owned, near, near_last, px, py, pz,
):
    t = pl.program_id(0)
    start = scalars[0]
    blocks = block_list(molecules, rows)
    distances = (near, near_last)

    @pl.when(t == 0)
    def _():
        row_masks(owned, start, blocks, atoms)
        set_distances(near, blocks[0][1], blocks[0][2])
        set_distances(near_last, blocks[-1][1], blocks[-1][2])
        lanes = slice(POS * LANES, (POS + 1) * LANES)
        spread_positions(rows_ref, lanes, (px, py, pz), blocks, distances, start)

    geometry((px, py, pz), t, rows, owned, radial_out.at[0], geo_out.at[0])


def vector_kernel(
    molecules, rows, atoms,
    scalars, rows_ref, filter_1, filter_2, radial_in, geo_in,
    sums_ref, back_ref, grads_ref, pos_out, grad_w_ref,
    weights_ref, picks, many, near, near_last, stage, loose, counts, pre, grad_pre,
    grad_radial, grad_ways,
    w0, w1, w2, v2, c0, c1, c2,
    s0, s1, s2, a0, a1, a2, gv, gx, gy, gz,
    fs0, fs1, fs2, fa0, fa1, fa2, fgv, fgx, fgy, fgz,
):
    t = pl.program_id(0)
    start = scalars[0]
    own = slice(HALO, HALO + atoms)
    radial, geo = radial_in.at[0], geo_in.at[0]
    w, c, g_pos = (w0, w1, w2), (c0, c1, c2), (gx, gy, gz)
    sums, backs = (s0, s1, s2), (a0, a1, a2)
    blocks = block_list(molecules, rows)
    distances = (near, near_last)

    @pl.when(t == 0)
    def _():
        set_filters(weights_ref, filter_1, filter_2)
        set_picks(picks)
        set_distances(near, blocks[0][1], blocks[0][2])
        set_distances(near_last, blocks[-1][1], blocks[-1][2])
        lanes = slice(W01 * LANES, (C2_COUNT + 1) * LANES)
        spread(rows_ref, lanes, stage, blocks, distances, start)
        for n, target in enumerate((w0, w1, w2, v2, c0, c1, c2)):
            target[...] = stage[n].astype(BF16)
        set_multiplicities(stage.at[7], many, blocks, rows)
        for total in (s0, s1, s2, a0, a1, a2, gv, gx, gy, gz):
            total[...] = jnp.zeros(total.shape, BF16)
        grad_w_ref[...] = jnp.zeros(grad_w_ref.shape, F32)

    counts[...] = dot(many[t], picks[...])
    pre[...] = dot(radial[...], weights_ref[...])

    def channel(o, here, ii, jj, k):
        h1, h2 = pre[here, :LANES], pre[here, LANES:]
        mi = counts[pl.ds(o, SUB), lanes_of(k)]
        mj = counts[pl.ds(o, SUB), lanes_of(OFFSETS + k)]
        v2i, v2j = v2[ii], v2[jj]
        ways = [geo[GEO_WAY + d, here, :] for d in range(3)]
        wi, wj = [w[d][ii] for d in range(3)], [w[d][jj] for d in range(3)]
        ci, cj = [c[d][ii] for d in range(3)], [c[d][jj] for d in range(3)]
        old_sums = [sums[d][jj] for d in range(3)]
        old_backs = [backs[d][jj] for d in range(3)]
        old_gv = gv[jj]

        def compute():
            f1, d1 = gate(h1)
            f2, d2 = gate(h2)
            ni, nj = mi.astype(BF16), mj.astype(BF16)
            f1i, f1j, f2i, f2j = f1 * ni, f1 * nj, f2 * ni, f2 * nj
            msg_i, msg_j = f2i * v2j, f2j * v2i
            stores, sum_i, back_i = [], [], []
            along_i = along_j = across_i = across_j = None
            for d in range(3):
                way = ways[d]
                sum_i.append(f1i * wj[d] + msg_i * way)
                stores.append((sums[d], jj, old_sums[d] + (f1j * wi[d] - msg_j * way)))
                stores.append((backs[d], jj, old_backs[d] + f1i * ci[d]))
                back_i.append(f1j * cj[d])
                grad = ci[d] * msg_i - cj[d] * msg_j
                stores.append((grad_ways, (d, here, slice(None)), grad))
                new = (ci[d] * way, cj[d] * way, ci[d] * wj[d], cj[d] * wi[d])
                if d == 0:
                    along_i, along_j, across_i, across_j = new
                else:
                    along_i, along_j = along_i + new[0], along_j + new[1]
                    across_i, across_j = across_i + new[2], across_j + new[3]
            stores.append((gv, jj, old_gv + f2i * along_i))
            g1 = ni * across_i + nj * across_j
            g2 = ni * along_i * v2j - nj * along_j * v2i
            stores.append((grad_pre, (here, slice(0, LANES)), g1 * d1))
            stores.append((grad_pre, (here, slice(LANES, None)), g2 * d2))
            return sum_i + back_i + [-(f2j * along_j)], stores

        return compute

    carried(rows, t, (fs0, fs1, fs2, fa0, fa1, fa2, fgv), 2, channel)
    grad_radial[...] = dot_nt(grad_pre[...], weights_ref[:LANES])
    grad_w_ref[...] = grad_w_ref[...] + dot_tn(geo[GEO_OWN], grad_pre[...])

    def turn(o, here, ii, jj, k):
        ways = [geo[GEO_WAY + d, here, :] for d in range(3)]
        grads = [grad_ways[d, here, :] for d in range(3)]
        grad, slope = grad_radial[here, :], geo[GEO_SLOPE, here, :]
        inverse, free = geo[GEO_INVERSE, here, :], geo[GEO_FREE, here, :]
        old = [g[jj] for g in g_pos]

        def compute():
            along = ways[0] * grads[0] + ways[1] * grads[1] + ways[2] * grads[2]
            pull = grad.astype(BF16) * slope - free * along
            out = [grads[d] * inverse + ways[d] * pull for d in range(3)]
            return out, [(g_pos[d], jj, old[d] - out[d]) for d in range(3)]

        return compute

    carried(rows, t, (fgx, fgy, fgz), 7, turn)

    @pl.when(t == SPAN - 1)
    def _():
        low = lax.broadcasted_iota(jnp.int32, (atoms, LANES), 1) < R
        totals = (s0, s1, s2, gv, a0, a1, a2, gx, gy, gz)
        firsts = (fs0, fs1, fs2, fgv, fa0, fa1, fa2, fgx, fgy, fgz)
        collect(tuple(zip(totals, firsts)), loose, blocks, distances, start)
        both = loose[own, :LANES].T
        sums_ref[0] = both[:R]
        sums_ref[1] = both[R:]
        both = loose[own, LANES : 2 * LANES].T
        sums_ref[2] = both[:R]
        grads_ref[R:] = both[R:].astype(BF16)

        def kept(n):
            return rows_ref[own, n * LANES : (n + 1) * LANES].astype(F32)

        v12 = kept(V12)
        v11 = jnp.where(low, v12, pltpu.roll(v12, R, 1))
        back = loose[own, 2 * LANES : 3 * LANES]
        both = (back * v11).T
        back_ref[0] = both[:R]
        back_ref[1] = both[R:]
        partial = back * kept(VEC01)
        partial = partial + pltpu.roll(partial, R, 1)
        back = loose[own, 3 * LANES : 4 * LANES]
        back_ref[2] = (back * v11).T[:R]
        partial = partial + back * kept(VEC2)
        grads_ref[:R] = partial.T[:R].astype(BF16)
        pos_out[...] = jnp.zeros(pos_out.shape, F32)
        pos_out[0:1] = jnp.sum(back.T[R:], axis=0, keepdims=True)
        both = loose[own, 4 * LANES :].T
        pos_out[1:2] = jnp.sum(both[:R], axis=0, keepdims=True)
        pos_out[2:3] = jnp.sum(both[R:], axis=0, keepdims=True)


def scalar_kernel(
    molecules, rows, atoms,
    scalars, rows_ref, filter_1, filter_2, scalar_parts, radial_in, geo_in,
    sum_ref, grads_ref, pos_out, grad_w_ref,
    weights_ref, picks, many, heads_ref, near, near_last, stage, loose, loose_low, counts, pre,
    grad_pre, grad_radial, products, sums, gates, bends,
    q, key, v0, gs,
    ss, gq, gk, g0, gx, gy, gz,
    fss, fgq, fgk, fg0, fgx, fgy, fgz,
):
    t = pl.program_id(0)
    start = scalars[0]
    own = slice(HALO, HALO + atoms)
    radial, geo = radial_in.at[0], geo_in.at[0]
    g_pos = (gx, gy, gz)
    blocks = block_list(molecules, rows)
    distances = (near, near_last)

    @pl.when(t == 0)
    def _():
        set_filters(weights_ref, filter_1, filter_2)
        set_picks(picks)
        row = lax.broadcasted_iota(jnp.int32, (2 * LANES, 2 * LANES), 0)
        lane = lax.broadcasted_iota(jnp.int32, (2 * LANES, 2 * LANES), 1)
        heads_ref[...] = jnp.where(row // HEAD == lane // HEAD, 1.0, 0.0).astype(BF16)
        set_distances(near, blocks[0][1], blocks[0][2])
        set_distances(near_last, blocks[-1][1], blocks[-1][2])
        lanes = slice(QK * LANES, (V0_COUNT + 1) * LANES)
        spread(rows_ref, lanes, stage, blocks, distances, start)
        for n, target in enumerate((q, key, v0)):
            target[...] = stage[n].astype(BF16)
        set_multiplicities(stage.at[3], many, blocks, rows)
        summed = scalar_parts[0].astype(F32)
        for f in range(1, scalar_parts.shape[0]):
            summed = summed + scalar_parts[f].astype(F32)
        summed = jnp.concatenate([summed, jnp.zeros_like(summed)], axis=0).T.astype(BF16)
        loose_low[own] = summed[:atoms]
        loose_low[:HALO] = summed[atoms : atoms + HALO]
        loose_low[HALO + atoms : 2 * HALO + atoms] = summed[atoms + HALO : atoms + 2 * HALO]
        end = 2 * HALO + atoms
        loose_low[end:] = jnp.zeros((loose_low.shape[0] - end, LANES), BF16)
        spread(loose_low, slice(None), stage, blocks, distances, start)
        gs[...] = stage[0].astype(BF16)
        for total in (ss, gq, gk, g0, gx, gy, gz):
            total[...] = jnp.zeros(total.shape, BF16)
        grad_w_ref[...] = jnp.zeros(grad_w_ref.shape, F32)

    counts[...] = dot(many[t], picks[...])
    pre[...] = dot(radial[...], weights_ref[...])

    def multiply(k, _):
        for o, size in halves(rows):
            here = pl.ds(pl.multiple_of(k * rows + o, SUB), size)
            ii, jj = (t, slice(o, o + size)), (t + 1 + k, slice(o, o + size))
            fk, dk = gate(pre[here, :LANES])
            f0, d0 = gate(pre[here, LANES:])
            k_ij, k_ji = q[ii] * key[jj] * fk, q[jj] * key[ii] * fk
            s_ij, s_ji = gs[ii] * v0[jj] * f0, gs[jj] * v0[ii] * f0
            gates[0, here, :] = fk
            gates[1, here, :] = f0
            gates[2, here, :] = dk
            gates[3, here, :] = d0
            products[0, here, :LANES] = k_ij
            products[0, here, LANES:] = k_ji
            products[1, here, :LANES] = s_ij
            products[1, here, LANES:] = s_ji
        return 0

    lax.fori_loop(0, OFFSETS, multiply, 0)
    sums[0] = dot(products[0], heads_ref[...])
    sums[1] = dot(products[1], heads_ref[...])

    def channel(o, here, ii, jj, k):
        fk, f0, dk, d0 = [gates[n, here, :] for n in range(4)]
        envelope, bend = geo[GEO_ENVELOPE, here, :], geo[GEO_BEND, here, :]
        side_in = []
        for side in range(2):
            lanes = slice(side * LANES, (side + 1) * LANES)
            m = counts[pl.ds(o, SUB), lanes_of(side * OFFSETS + k)]
            h, o_ = (ii, jj) if side == 0 else (jj, ii)
            side_in.append(
                (m, sums[0, here, lanes], sums[1, here, lanes])
                + (q[h], key[o_], gs[h], v0[o_])
            )
        old = [ref[jj] for ref in (g0, gk, ss, gq)]

        def compute():
            gives, news = [], []
            for m, score, g_att, qh, kt, gh, vt in side_in:
                act, rise = gate(0.5 * score)
                m, g_att = m.astype(BF16), g_att.astype(BF16)
                weight = m * envelope
                att = act * weight
                g_score = g_att * (0.5 * rise) * weight
                lift = m * (g_att * act)
                bv, dv = f0 * att, fk * g_score
                gives.append((vt * bv, kt * dv, gh * bv, qh * dv))
                news.append((qh * kt * g_score, gh * vt * att, lift))
            one, two = gives
            new = [x + y for x, y in zip(*news)]
            stores = [
                (ref, jj, x + y)
                for ref, x, y in zip((g0, gk, ss, gq), old, (one[2], one[3], two[0], two[1]))
            ]
            stores.append((grad_pre, (here, slice(0, LANES)), new[0] * dk))
            stores.append((grad_pre, (here, slice(LANES, None)), new[1] * d0))
            stores.append((bends, (here, slice(None)), new[2] * bend * (1.0 / HEAD)))
            return [one[0], one[1], two[2], two[3]], stores

        return compute

    carried(rows, t, (fss, fgq, fg0, fgk), 2, channel)
    grad_radial[...] = dot_nt(grad_pre[...], weights_ref[:LANES])
    grad_w_ref[...] = grad_w_ref[...] + dot_tn(geo[GEO_OWN], grad_pre[...])

    def turn(o, here, ii, jj, k):
        ways = [geo[GEO_WAY + d, here, :] for d in range(3)]
        grad, slope, bend = grad_radial[here, :], geo[GEO_SLOPE, here, :], bends[here, :]
        old = [g[jj] for g in g_pos]

        def compute():
            pull = grad.astype(BF16) * slope + bend
            out = [way * pull for way in ways]
            return out, [(g_pos[d], jj, old[d] - out[d]) for d in range(3)]

        return compute

    carried(rows, t, (fgx, fgy, fgz), 7, turn)

    @pl.when(t == SPAN - 1)
    def _():
        totals = (ss, g0, gq, gk, gx, gy, gz, gz)
        firsts = (fss, fg0, fgq, fgk, fgx, fgy, fgz, fgz)
        collect(tuple(zip(totals, firsts)), loose, blocks, distances, start)
        both = loose[own, :LANES].T
        sum_ref[...] = both[:R].astype(BF16)
        grads_ref[2 * R :] = both[R:].astype(BF16)
        grads_ref[: 2 * R] = loose[own, LANES : 2 * LANES].T.astype(BF16)
        pos_out[...] = jnp.zeros(pos_out.shape, F32)
        both = loose[own, 2 * LANES : 3 * LANES].T
        pos_out[0:1] = jnp.sum(both[:R], axis=0, keepdims=True)
        pos_out[1:2] = jnp.sum(both[R:], axis=0, keepdims=True)
        both = loose[own, 3 * LANES :].T
        pos_out[2:3] = jnp.sum(both[:R], axis=0, keepdims=True)


def whole(memory=pltpu.VMEM):
    return pl.BlockSpec(memory_space=memory)


def params(mib=60):
    return pltpu.CompilerParams(vmem_limit_bytes=mib * 1024 * 1024)


def edge_sizes(atoms):
    molecules = (atoms + 2 * (MOL - 1)) // MOL
    full, rest = divmod(molecules, BLOCK)
    rows = full * ROW_GROUPS * BLOCK + -(-ROW_GROUPS * rest // BLOCK) * BLOCK
    rows = -(-rows // SUB) * SUB
    tall = -(-(HALO + molecules * MOL) // SUB) * SUB
    return molecules, rows, tall


def by_step(shape):
    zeros = (0,) * (len(shape) - 1)
    return pl.BlockSpec((1,) + shape[1:], lambda t: (t,) + zeros)


def fixed(shape):
    zeros = (0,) * len(shape)
    return pl.BlockSpec(shape, lambda t: zeros)


def edge_call(kernel, atoms, inputs, stepped_in, outs, stepped_out, scratch):
    molecules, rows, _ = edge_sizes(atoms)
    return pl.pallas_call(
        functools.partial(kernel, molecules, rows, atoms),
        grid=(SPAN,),
        out_shape=[jax.ShapeDtypeStruct(s, kind) for s, kind in outs + stepped_out],
        in_specs=[whole(pltpu.SMEM)]
        + [fixed(x.shape) for x in inputs[1:]]
        + [by_step(x.shape) for x in stepped_in],
        out_specs=[fixed(s) for s, _ in outs] + [by_step(s) for s, _ in stepped_out],
        scratch_shapes=[pltpu.VMEM(s, kind) for s, kind in scratch],
        compiler_params=params(),
        cost_estimate=pl.CostEstimate(
            flops=20 * 10**9, bytes_accessed=40 * 10**6, transcendentals=10**7
        ),
    )(*inputs, *stepped_in)


def shared_scratch(atoms):
    molecules, rows, tall = edge_sizes(atoms)
    batch = OFFSETS * rows
    blocks = block_list(molecules, rows)
    return {
        "weights": ((2 * LANES, 2 * LANES), BF16),
        "picks": ((LANES, 2 * OFFSETS * LANES), BF16),
        "many": ((SPAN, rows, LANES), BF16),
        "mask": ((rows, LANES), F32),
        "near": ((LANE_GROUPS, STEPS * blocks[0][1], WINDOW), jnp.int32),
        "near_last": ((LANE_GROUPS, STEPS * blocks[-1][1], WINDOW), jnp.int32),
        "stage8": ((8, STEPS, rows, LANES), F32),
        "stage4": ((4, STEPS, rows, LANES), F32),
        "loose5": ((tall, 5 * LANES), F32),
        "loose4": ((tall, 4 * LANES), F32),
        "loose_low": ((tall, LANES), BF16),
        "tall": ((STEPS, rows, LANES), F32),
        "low": ((STEPS, rows, LANES), BF16),
        "first": ((SPAN, rows, LANES), F32),
        "counts": ((rows, 2 * OFFSETS * LANES), F32),
        "pre": ((batch, 2 * LANES), F32),
        "grad_pre": ((batch, 2 * LANES), BF16),
        "line": ((batch, LANES), F32),
        "line2": ((2, batch, LANES), BF16),
        "line3": ((3, batch, LANES), BF16),
        "line4": ((4, batch, LANES), BF16),
        "line1": ((batch, LANES), BF16),
        "wide2": ((2, batch, 2 * LANES), BF16),
        "wide2f": ((2, batch, 2 * LANES), F32),
    }


def offsets_in_block(neighbours, mask, first):
    lane = lax.broadcasted_iota(jnp.int32, neighbours.shape, 1)
    diff = neighbours - (first + lane)
    return jnp.where(diff < 0, diff + MOL, diff) * mask


def pieces(x):
    a = x.astype(BF16)
    rest = x - a.astype(F32)
    b = rest.astype(BF16)
    return a, b, (rest - b.astype(F32)).astype(BF16)


def edge_groups(features, vectors, cot_f, cot_v, neighbours, mask, positions, first):
    diff = offsets_in_block(neighbours[...], mask[...], first).astype(F32).astype(BF16)
    groups = [jnp.concatenate([features[...], cot_f[...], diff], axis=0)]
    for d in range(3):
        rows = [x.astype(F32) for x in pieces(positions[d : d + 1])]
        rows = jnp.concatenate(rows + [jnp.zeros((29, LANES), F32)], axis=0).astype(BF16)
        groups.append(jnp.concatenate([vectors[d], cot_v[d], rows], axis=0))
    return groups


def halo_kernel(atoms, scalars, *refs):
    row_first = scalars[2]
    lane = lax.broadcasted_iota(jnp.int32, (GROUP_ROWS, LANES), 1)
    for end, at, out in ((0, atoms - LANES, refs[14]), (1, 0, refs[15])):
        groups = edge_groups(*refs[7 * end : 7 * end + 7], row_first + at)
        total = None
        for g, group in enumerate(groups):
            by = (HALO * (g + 1) if end == 0 else HALO * g) % LANES
            moved = group.astype(F32)
            moved = pltpu.roll(moved, by, 1) if by else moved
            total = moved if total is None else jnp.where(lane >= HALO * g, moved, total)
        out[...] = total.astype(BF16)


def halo_call(atoms, scalars, arrays):
    specs = []
    for at in (atoms // LANES - 1, 0):
        for x in arrays:
            shape = x.shape[:-1] + (LANES,)
            index = (0,) * (x.ndim - 1) + (at,)
            specs.append(pl.BlockSpec(shape, lambda *_, index=index: index))
    out = jax.ShapeDtypeStruct((GROUP_ROWS, LANES), BF16)
    return pl.pallas_call(
        functools.partial(halo_kernel, atoms),
        grid=(1,),
        out_shape=[out, out],
        in_specs=[whole(pltpu.SMEM)] + specs,
        out_specs=[whole(), whole()],
        compiler_params=params(),
    )(scalars, *arrays, *arrays)


def column(row):
    return jnp.broadcast_to(row, (8, row.shape[1])).T[:, :1]


def normalised(f):
    mean = jnp.mean(f, axis=0, keepdims=True)
    centred = f - mean
    inv = lax.rsqrt(jnp.mean(centred * centred, axis=0, keepdims=True) + EPSILON)
    return centred * inv, mean, inv


def dense_kernel(
    atoms,
    scalars, features, vectors, cot_f, cot_v, neighbours, mask, positions, low_ref, high_ref,
    gain_ref, bias_ref, w_query, w_key, w_value, w_vector, w_output,
    rows_ref, part_ref, stat_ref,
    w_qk, w_v0, w_v12, w_vec_t, w_out,
):
    chan_first = pl.multiple_of(scalars[1], R)
    row_first = scalars[2]
    gain, bias = column(gain_ref[...]), column(bias_ref[...])
    w_qk[:R] = w_query[...]
    w_qk[R:] = w_key[...]
    w_v0[:R] = w_value[0]
    w_v0[R:] = jnp.zeros((R, H), BF16)
    w_v12[:R] = w_value[1]
    w_v12[R:] = w_value[2]
    for p in range(3):
        w_vec_t[p * R : (p + 1) * R] = w_vector[p]
    w_out[...] = jnp.concatenate([w_output[p] for p in range(3)], axis=0).astype(F32).T.astype(BF16)

    def block(f, v, cf, cv, own_v, diff, pos):
        width = f.shape[1]
        normed, mean, inv = normalised(f)
        turned = (normed * gain + bias).T.astype(BF16)
        kinds = lax.broadcasted_iota(jnp.int32, (R, width), 0)
        kinds = jnp.where(kinds < 32, kinds, MOL + 32 - kinds).astype(F32)
        counts = jnp.zeros((R, width), F32)
        for s in range(diff.shape[0]):
            counts = counts + jnp.where(diff[s : s + 1] == kinds, 1.0, 0.0)
        none = jnp.zeros((R, width), F32)
        counts = jnp.concatenate([none, counts], axis=0).T
        low = lax.broadcasted_iota(jnp.int32, (width, LANES), 1) < R
        pairs = [None] * 10
        pairs[QK] = dot_nt(turned, w_qk[...])
        pairs[V0_COUNT] = dot_nt(turned, w_v0[...]) + counts
        v12 = dot_nt(turned, w_v12[...]).astype(BF16).astype(F32)
        v11 = jnp.where(low, v12, pltpu.roll(v12, R, 1))
        pairs[V12] = v12
        pairs[VEC01] = jnp.concatenate([own_v[0], own_v[1]], axis=0).T
        pairs[VEC2] = jnp.concatenate([own_v[2], none], axis=0).T
        pairs[W01] = pairs[VEC01] * v11
        pairs[W2V2] = jnp.where(low, pairs[VEC2] * v11, v12)
        pairs[C01] = jnp.concatenate([cv[0], cv[1]], axis=0).T
        pairs[C2_COUNT] = jnp.concatenate([cv[2], none], axis=0).T + counts
        pairs[POS] = jnp.concatenate([pos, jnp.zeros((LANES - 9, width), F32)], axis=0).T
        vec_dot = grad_0 = 0.0
        for d in range(3):
            proj = dot(w_vec_t[...], v[d])
            vec_dot = vec_dot + proj[:R] * proj[R : 2 * R]
            grad_0 = grad_0 + cv[d] * proj[2 * R :]
        grad_out = jnp.concatenate([grad_0, cf * vec_dot, cf], axis=0).astype(BF16)
        part = dot(w_out[...], grad_out)
        return [x.astype(BF16) for x in pairs], part.astype(BF16), mean, inv

    wide = 2 * LANES

    def step(b, _):
        at = pl.multiple_of(b * wide, wide)
        here = pl.ds(at, wide)
        own_v = [vectors[d, pl.ds(chan_first, R), here].astype(F32) for d in range(3)]
        diff = offsets_in_block(neighbours[:, here], mask[:, here], row_first + at)
        places = [p.astype(F32) for d in range(3) for p in pieces(positions[d : d + 1, here])]
        pairs, part, mean, inv = block(
            features[:, here].astype(F32),
            [vectors[d, :, here] for d in range(3)],
            cot_f[:, here].astype(F32),
            [cot_v[d, :, here].astype(F32) for d in range(3)],
            own_v,
            diff.astype(F32),
            jnp.concatenate(places, axis=0),
        )
        there = pl.ds(pl.multiple_of(HALO + at, 2 * SUB), wide)
        for n, pair in enumerate(pairs):
            rows_ref[there, n * LANES : (n + 1) * LANES] = pair
        part_ref[:, here] = part
        stat_ref[0:1, here] = mean
        stat_ref[1:2, here] = inv
        return 0

    lax.fori_loop(0, atoms // wide, step, 0)

    lane = lax.broadcasted_iota(jnp.int32, (GROUP_ROWS, LANES), 1)
    packed_low, packed_high = low_ref[...].astype(F32), high_ref[...].astype(F32)
    groups = []
    for g in range(4):
        a = pltpu.roll(packed_low, (LANES - HALO * g) % LANES, 1) if g else packed_low
        by = (LANES + HALO - HALO * g) % LANES
        b = pltpu.roll(packed_high, by, 1) if by else packed_high
        both = jnp.where(lane < HALO, a, jnp.where(lane < 2 * HALO, b, 0.0))
        groups.append(both)
    pick_rows = lax.broadcasted_iota(jnp.int32, (H, LANES), 0)
    own_v, pos = [], []
    for d in range(3):
        g = groups[1 + d]
        found = g[:R]
        for f in range(1, H // R):
            found = jnp.where(chan_first == f * R, g[f * R : (f + 1) * R], found)
        own_v.append(found)
        pos.append(g[320:323])
    pairs, part, _, _ = block(
        groups[0][:H],
        [groups[1 + d][:H].astype(BF16) for d in range(3)],
        groups[0][H : H + R],
        [groups[1 + d][H : H + R] for d in range(3)],
        own_v,
        groups[0][H + R :],
        jnp.concatenate(pos, axis=0),
    )
    high = HALO + atoms
    tall = rows_ref.shape[0]
    for n, pair in enumerate(pairs):
        lanes = slice(n * LANES, (n + 1) * LANES)
        rows_ref[:HALO, lanes] = pair[:HALO]
        rows_ref[high : high + HALO, lanes] = pair[HALO : 2 * HALO]
        rows_ref[high + HALO :, lanes] = jnp.zeros((tall - high - HALO, LANES), BF16)
    part_ref[:, atoms:] = part


def both_diagonals(grad, f):
    at = f * LANES
    return 0.5 * (grad[:R, at : at + R] + grad[R:, at + R : at + LANES])


def layer_kernel(
    atoms,
    scalars, features, vectors, cot_f, cot_v, gathered, w_vector, w_output,
    feat_out, delta_ref, square_ref, send_ref, flat_ref,
    w_vec, w_vec_t, w_out_t, t_vec, t_out,
):
    chan_first = pl.multiple_of(scalars[1], R)
    for p in range(3):
        w_vec_t[p * R : (p + 1) * R] = w_vector[p]
        w_out_t[p * R : (p + 1) * R] = w_output[p]
    w_vec[...] = w_vec_t[...].astype(F32).T.astype(BF16)
    t_vec[...] = jnp.zeros(t_vec.shape, F32)
    t_out[...] = jnp.zeros(t_out.shape, F32)
    wide = 2 * LANES
    split = send_ref.shape[0]

    def step(b, _):
        at = pl.multiple_of(b * wide, wide)
        here = pl.ds(at, wide)
        all_sums = gathered[:, here]
        outputs = dot(w_out_t[...], all_sums)
        out_0, out_1, out_2 = outputs[:R], outputs[R : 2 * R], outputs[2 * R :]
        cf = cot_f[:, here].astype(F32)
        grad_dot = cf * out_1
        vec_dot = grad_0 = 0.0
        for d in range(3):
            proj = dot(w_vec_t[...], vectors[d, :, here])
            first, second, third = proj[:R], proj[R : 2 * R], proj[2 * R :]
            cv = cot_v[d, :, here].astype(F32)
            vec_dot = vec_dot + first * second
            grad_0 = grad_0 + cv * third
            delta_ref[d, :, here] = third * out_0
            grad_proj = jnp.concatenate(
                [grad_dot * second, grad_dot * first, cv * out_0], axis=0
            ).astype(BF16)
            part = dot(w_vec[...], grad_proj).astype(BF16)
            for f in range(split):
                send_ref[f, d * R : (d + 1) * R, here] = part[f * R : (f + 1) * R]
            t_vec[...] = t_vec[...] + dot_nt(grad_proj, vectors[d, :, here])
        delta = vec_dot * out_1 + out_2
        moved = features[pl.ds(chan_first, R), here].astype(F32) + delta
        feat_out[:, here] = moved.astype(BF16)
        grad_out = jnp.concatenate([grad_0, cf * vec_dot, cf], axis=0).astype(BF16)
        t_out[...] = t_out[...] + dot_nt(grad_out, all_sums)
        square_ref[0:1, here] = jnp.sum(moved * moved, axis=0, keepdims=True)
        square_ref[1:2, here] = jnp.sum(delta * delta, axis=0, keepdims=True)
        return 0

    lax.fori_loop(0, atoms // wide, step, 0)
    flat_ref[: 3 * R] = t_vec[...].astype(BF16)
    flat_ref[3 * R :] = t_out[...].astype(BF16)


def normal_kernel(
    atoms,
    scalars, features, stat, vectors, delta_ref, square_ref, sums_ref,
    grads_b, grads_a, pos_a, pos_b, mask, gain_ref, bias_ref,
    w_query, w_key, w_value, grad_filters_a, grad_filters_b,
    vec_out, send_ref, flat_ref,
    w_five, t_five,
):
    chan_first = pl.multiple_of(scalars[1], R)
    gain, bias = column(gain_ref[...]), column(bias_ref[...])
    five = [w_query[...], w_key[...]] + [w_value[p] for p in range(3)]
    w_five[...] = jnp.concatenate(five, axis=0).astype(F32).T.astype(BF16)
    t_five[...] = jnp.zeros(t_five.shape, F32)
    wide = 2 * LANES
    split = send_ref.shape[0]

    def step(b, _):
        at = pl.multiple_of(b * wide, wide)
        here = pl.ds(at, wide)
        real = mask[:, here].astype(F32)
        square_v = square_dv = 0.0
        for d in range(3):
            delta = delta_ref[d, :, here] + sums_ref[d, :, here]
            moved = vectors[d, pl.ds(chan_first, R), here].astype(F32) + delta
            vec_out[d, :, here] = moved.astype(BF16)
            square_v = square_v + moved * moved
            square_dv = square_dv + delta * delta
        normed = (features[:, here].astype(F32) - stat[0:1, here]) * stat[1:2, here]
        normal = (normed * gain + bias).astype(BF16)
        grads = jnp.concatenate([grads_b[:, here], grads_a[:, here]], axis=0)
        t_five[...] = t_five[...] + dot_nt(grads, normal)
        part = dot(w_five[...], grads)
        rounded = part.astype(BF16)
        for f in range(split):
            send_ref[f, :R, here] = rounded[f * R : (f + 1) * R]
        hat = part * gain
        tops = [
            jnp.sum(hat, axis=0, keepdims=True),
            jnp.sum(hat * normed, axis=0, keepdims=True),
        ]
        exact = [pos_a[d : d + 1, here] + pos_b[d : d + 1, here] for d in range(3)]
        exact += [square_ref[n : n + 1, here] * real for n in range(2)]
        for x in (square_v, square_dv):
            exact.append(jnp.sum(x, axis=0, keepdims=True) * real)
        heads = [x.astype(BF16).astype(F32) for x in exact]
        tops = tops + heads + [x - y for x, y in zip(exact, heads)]
        tops = jnp.concatenate(tops, axis=0).astype(BF16)
        for f in range(split):
            send_ref[f, R:, here] = tops
        return 0

    lax.fori_loop(0, atoms // wide, step, 0)
    grad_a, grad_b = grad_filters_a[...], grad_filters_b[...]
    filters = [both_diagonals(g, f) for g in (grad_b, grad_a) for f in range(2)]
    flat_ref[: 5 * R] = t_five[...].astype(BF16)
    flat_ref[5 * R :] = jnp.concatenate(filters, axis=1).astype(BF16)


def final_kernel(
    atoms,
    scalars, got, got_vec, features, stat, gain_ref, cot_f, cot_v, back_ref, mask,
    grad_feat, grad_vec, grad_pos, small_ref,
):
    chan_first = pl.multiple_of(scalars[1], R)
    whole_gain = column(gain_ref[...])
    gain = whole_gain[:R]
    for f in range(1, H // R):
        gain = jnp.where(chan_first == f * R, whole_gain[f * R : (f + 1) * R], gain)

    def summed(ref, rows):
        total = ref[0, rows].astype(F32)
        for f in range(1, ref.shape[0]):
            total = total + ref[f, rows].astype(F32)
        return total

    tops = summed(got, slice(R, R + EXTRAS))
    grad_normal = summed(got, slice(0, R))
    inv = stat[1:2]
    normed = (features[pl.ds(chan_first, R), :].astype(F32) - stat[0:1]) * inv
    inner = grad_normal * gain - tops[0:1] * (1.0 / H) - normed * (tops[1:2] * (1.0 / H))
    grad_feat[...] = cot_f[...].astype(F32) + inv * inner
    for d in range(3):
        part = summed(got_vec, slice(d * R, (d + 1) * R))
        grad_vec[d] = cot_v[d].astype(F32) + part + back_ref[d]
    exact = tops[2:9] + tops[9:16]
    grad_pos[...] = exact[:3]
    ones = jnp.ones((8, atoms), BF16)
    gains = dot_nt(ones, (grad_normal * normed).astype(BF16))
    biases = dot_nt(ones, grad_normal.astype(BF16))
    totals = jnp.sum(exact[3:7], axis=1, keepdims=True)
    real = jnp.sum(mask[...].astype(F32), axis=1, keepdims=True)
    numbers = jnp.concatenate([totals, real, jnp.zeros((3, 1), F32)], axis=0)
    small = jnp.concatenate([gains, biases, jnp.broadcast_to(numbers, (8, LANES))], axis=1)
    high = small.astype(BF16)
    small_ref[:8] = high.astype(F32)
    small_ref[8:] = small - high.astype(F32)


def unpack_kernel(
    share,
    got,
    g_gain, g_bias, g_query, g_key, g_value, g_vector, g_output, g_key_f, g_value_f, rms_ref,
):
    every = [got[n].astype(F32) for n in range(got.shape[0])]
    total = 0.0
    for x in every:
        total = total + (x[2 * share : 2 * share + 8] + x[2 * share + 8 : 2 * share + 16])
    g_gain[...] = total[0:1, :R]
    g_bias[...] = total[0:1, R : 2 * R]
    numbers = total[:, LANES : LANES + 1]
    size = jnp.where(lax.broadcasted_iota(jnp.int32, (8, 1), 0) < 2, 1.0, 3.0) * H
    rms = jnp.sqrt(numbers / (numbers[4:5] * size) + 1e-06)
    rms_ref[...] = jnp.broadcast_to(rms, (8, LANES)).T[:1, :8]
    early = [(g, p) for g in (g_vector, g_output) for p in range(3)]
    late = [(g_query, None), (g_key, None)] + [(g_value, p) for p in range(3)]
    for n, x in enumerate(every):
        for first, names in ((0, early), (share, late)):
            at = n * share
            while at < (n + 1) * share:
                m = at // R
                size = min((m + 1) * R, (n + 1) * share) - at
                value = x[first + at - n * share : first + at - n * share + size]
                rows = slice(at - m * R, at - m * R + size)
                at += size
                if m == len(names):
                    g_key_f[rows] = value[:, :R]
                    for p in range(3):
                        g_value_f[p, rows] = value[:, (1 + p) * R : (2 + p) * R]
                    continue
                g, p = names[m]
                if p is None:
                    g[rows] = value
                else:
                    g[p, rows] = value


def everywhere(x, axis):
    count = lax.axis_size(axis)
    return lax.all_to_all(jnp.broadcast_to(x[None], (count,) + x.shape), axis, 0, 0)


def per_device(
    features, vectors, positions, atom_mask, neighbours, ln_gain, ln_bias,
    w_query, w_key, w_value, w_vector, w_output, w_key_filter, w_value_filter,
    cot_features, cot_vectors,
):
    channels = w_query.shape[1]
    atoms = features.shape[1]
    count = lax.axis_size("atoms")
    split = lax.axis_size("feat")
    chan_first = lax.axis_index("feat") * channels
    row_first = lax.axis_index("atoms") * atoms
    start = HALO - lax.rem(row_first, MOL)
    scalars = jnp.stack([start, chan_first, row_first]).astype(jnp.int32)
    molecules, rows_each, tall = edge_sizes(atoms)
    w_query, w_key = w_query.T, w_key.T
    w_value, w_vector, w_output = [jnp.swapaxes(w, 1, 2) for w in (w_value, w_vector, w_output)]
    mask = atom_mask.reshape(1, atoms)
    gain, bias = ln_gain.reshape(1, H), ln_bias.reshape(1, H)

    ends = halo_call(
        atoms,
        scalars,
        (features, vectors, cot_features, cot_vectors, neighbours, mask, positions),
    )
    low = lax.ppermute(ends[0], "atoms", [(i, i + 1) for i in range(count - 1)])
    high = lax.ppermute(ends[1], "atoms", [(i + 1, i) for i in range(count - 1)])

    inputs = (
        scalars, features, vectors, cot_features, cot_vectors, neighbours, mask, positions,
        low, high, gain, bias, w_query, w_key, w_value, w_vector, w_output,
    )
    rows, part, stat = pl.pallas_call(
        functools.partial(dense_kernel, atoms),
        out_shape=[
            jax.ShapeDtypeStruct((tall, 10 * LANES), BF16),
            jax.ShapeDtypeStruct((H, atoms + LANES), BF16),
            jax.ShapeDtypeStruct((8, atoms), F32),
        ],
        in_specs=[whole(pltpu.SMEM)] + [whole()] * (len(inputs) - 1),
        out_specs=[whole()] * 3,
        scratch_shapes=[
            pltpu.VMEM((LANES, H), BF16),
            pltpu.VMEM((LANES, H), BF16),
            pltpu.VMEM((LANES, H), BF16),
            pltpu.VMEM((3 * R, H), BF16),
            pltpu.VMEM((H, 3 * R), BF16),
        ],
        compiler_params=params(),
    )(*inputs)
    scalar_parts = lax.all_to_all(part.reshape(split, channels, atoms + LANES), "feat", 0, 0)

    kinds = shared_scratch(atoms)
    batch = OFFSETS * rows_each
    names = ["mask", "near", "near_last"] + ["tall"] * 3
    radial, geo = edge_call(
        geometry_kernel,
        atoms,
        (scalars, rows),
        (),
        [],
        [((SPAN, batch, 2 * LANES), BF16), ((SPAN, GEO, batch, LANES), BF16)],
        [kinds[name] for name in names],
    )
    names = ["weights", "picks", "many", "weights", "near", "near_last", "stage4", "loose4"]
    names += ["loose_low", "counts", "pre", "grad_pre", "line", "wide2", "wide2f", "line4", "line1"]
    names += ["low"] * 4 + ["low"] * 7 + ["first"] * 7
    scalar_sum, grads_b, pos_b, grad_filters_b = edge_call(
        scalar_kernel,
        atoms,
        (scalars, rows, w_key_filter, w_value_filter[0], scalar_parts),
        (radial, geo),
        [
            ((R, atoms), BF16),
            ((3 * R, atoms), BF16),
            ((8, atoms), F32),
            ((LANES, 2 * LANES), F32),
        ],
        [],
        [kinds[name] for name in names],
    )
    gathered = lax.all_gather(scalar_sum, "feat", axis=0, tiled=True)

    inputs = (
        scalars, features, vectors, cot_features, cot_vectors, gathered, w_vector, w_output,
    )
    new_features, delta, squares, send_vec, flat_early = pl.pallas_call(
        functools.partial(layer_kernel, atoms),
        out_shape=[
            jax.ShapeDtypeStruct((R, atoms), BF16),
            jax.ShapeDtypeStruct((3, R, atoms), F32),
            jax.ShapeDtypeStruct((8, atoms), F32),
            jax.ShapeDtypeStruct((split, 3 * R, atoms), BF16),
            jax.ShapeDtypeStruct((6 * R, H), BF16),
        ],
        in_specs=[whole(pltpu.SMEM)] + [whole()] * (len(inputs) - 1),
        out_specs=[whole()] * 5,
        scratch_shapes=[
            pltpu.VMEM((H, 3 * R), BF16),
            pltpu.VMEM((3 * R, H), BF16),
            pltpu.VMEM((3 * R, H), BF16),
            pltpu.VMEM((3 * R, H), F32),
            pltpu.VMEM((3 * R, H), F32),
        ],
        compiler_params=params(),
    )(*inputs)
    share = 6 * R // count
    got_vec = lax.all_to_all(send_vec, "feat", 0, 0)
    shares_early = lax.all_to_all(flat_early.reshape(count, share, H), "atoms", 0, 0)

    names = ["weights", "picks", "many", "near", "near_last", "stage8", "loose5"]
    names += ["counts", "pre", "grad_pre", "line", "line3"]
    names += ["low"] * 7 + ["low"] * 10 + ["first"] * 10
    rows, _ = lax.optimization_barrier((rows, squares))
    sums, back, grads_a, pos_a, grad_filters_a = edge_call(
        vector_kernel,
        atoms,
        (scalars, rows, w_value_filter[1], w_value_filter[2]),
        (radial, geo),
        [
            ((3, R, atoms), F32),
            ((3, R, atoms), F32),
            ((2 * R, atoms), BF16),
            ((8, atoms), F32),
            ((LANES, 2 * LANES), F32),
        ],
        [],
        [kinds[name] for name in names],
    )

    inputs = (
        scalars, features, stat, vectors, delta, squares, sums, grads_b, grads_a, pos_a, pos_b,
        mask, gain, bias, w_query, w_key, w_value, grad_filters_a, grad_filters_b,
    )
    new_vectors, send, flat_late = pl.pallas_call(
        functools.partial(normal_kernel, atoms),
        out_shape=[
            jax.ShapeDtypeStruct((3, R, atoms), BF16),
            jax.ShapeDtypeStruct((split, R + EXTRAS, atoms), BF16),
            jax.ShapeDtypeStruct((6 * R, H), BF16),
        ],
        in_specs=[whole(pltpu.SMEM)] + [whole()] * (len(inputs) - 1),
        out_specs=[whole()] * 3,
        scratch_shapes=[pltpu.VMEM((H, 5 * R), BF16), pltpu.VMEM((5 * R, H), F32)],
        compiler_params=params(),
    )(*inputs)
    got = lax.all_to_all(send, "feat", 0, 0)
    shares_late = lax.all_to_all(flat_late.reshape(count, share, H), "atoms", 0, 0)

    inputs = (
        scalars, got, got_vec, features, stat, gain, cot_features, cot_vectors, back, mask,
    )
    grad_features, grad_vectors, grad_positions, small = pl.pallas_call(
        functools.partial(final_kernel, atoms),
        out_shape=[
            jax.ShapeDtypeStruct((R, atoms), F32),
            jax.ShapeDtypeStruct((3, R, atoms), F32),
            jax.ShapeDtypeStruct((3, atoms), F32),
            jax.ShapeDtypeStruct((16, H), F32),
        ],
        in_specs=[whole(pltpu.SMEM)] + [whole()] * (len(inputs) - 1),
        out_specs=[whole()] * 4,
        compiler_params=params(),
    )(*inputs)
    summed = [jnp.sum(x.astype(F32), axis=0) for x in (shares_early, shares_late)]
    mine = jnp.concatenate(summed + [small], axis=0).astype(BF16)
    every = everywhere(mine, "atoms")
    shapes = [
        (1, R), (1, R), (R, H), (R, H), (3, R, H), (3, R, H), (3, R, H), (R, R), (3, R, R), (1, 8),
    ]
    grads = pl.pallas_call(
        functools.partial(unpack_kernel, share),
        out_shape=[jax.ShapeDtypeStruct(shape, F32) for shape in shapes],
        in_specs=[whole()],
        out_specs=[whole()] * len(shapes),
        compiler_params=params(),
    )(every)
    return (
        new_features,
        new_vectors,
        grad_features,
        grad_vectors,
        grad_positions,
        grads[0].reshape(R),
        grads[1].reshape(R),
        grads[2].T,
        grads[3].T,
        jnp.swapaxes(grads[4], 1, 2),
        jnp.swapaxes(grads[5], 1, 2),
        jnp.swapaxes(grads[6], 1, 2),
        grads[7],
        grads[8],
        grads[9][0, :4],
    )


def solution(mesh):
    in_specs = (
        P(None, "atoms"),
        P(None, None, "atoms"),
        P(None, "atoms"),
        P("atoms"),
        P(None, "atoms"),
        P(),
        P(),
        P(None, "feat"),
        P(None, "feat"),
        P(None, None, "feat"),
        P(None, None, "feat"),
        P(None, None, "feat"),
        P(None, "feat"),
        P(None, None, "feat"),
        P("feat", "atoms"),
        P(None, "feat", "atoms"),
    )
    out_specs = (
        P("feat", "atoms"),
        P(None, "feat", "atoms"),
        P("feat", "atoms"),
        P(None, "feat", "atoms"),
        P(None, "atoms"),
        P("feat"),
        P("feat"),
        P(None, "feat"),
        P(None, "feat"),
        P(None, None, "feat"),
        P(None, None, "feat"),
        P(None, None, "feat"),
        P(None, "feat"),
        P(None, None, "feat"),
        P(),
    )
    return jax.shard_map(
        per_device, mesh=mesh, in_specs=in_specs, out_specs=out_specs, check_vma=False
    )
```

```python
import functools
import math

import jax
import jax.numpy as jnp
from jax import lax
from jax.experimental import pallas as pl
from jax.experimental.pallas import tpu as pltpu
from jax.sharding import PartitionSpec as P

H = 256
HEADS = 8
HEAD = H // HEADS
R = 64
MOL = 29
HALO = 32
CUTOFF = 5.0
EPSILON = 1e-05
F32 = jnp.float32
BF16 = jnp.bfloat16

LANE_GROUPS = 2
ROW_GROUPS = 3
SPAN = 5
OFFSETS = 14
STEPS = SPAN + OFFSETS
SUB = 16
LANES = 128

W01, W2V2, C01, C2_COUNT, POS, QK, V0_COUNT, V12, VEC01, VEC2 = range(10)
GROUP_ROWS = 352
EXTRAS = 16


BLOCK = 8
WINDOW = 256


def block_list(molecules, rows):
    full, rest = divmod(molecules, BLOCK)
    wide = ROW_GROUPS * BLOCK
    out = [(n * wide, wide, BLOCK) for n in range(full)]
    if rows > full * wide:
        out.append((full * wide, rows - full * wide, rest))
    return out


def row_parts(shape, axis, size):
    row = lax.broadcasted_iota(jnp.int32, shape, axis)
    group = jnp.zeros(shape, jnp.int32)
    for g in range(1, ROW_GROUPS):
        group = jnp.where(row >= g * size, g, group)
    return group, row - group * size, row < ROW_GROUPS * size


def set_distances(target, width, size):
    for r in range(LANE_GROUPS):

        def step(t, _, r=r):
            group, molecule, held = row_parts((width, WINDOW), 0, size)
            spot = t + SPAN * (LANE_GROUPS * group + r)
            spot = jnp.where(spot >= MOL, spot - MOL, spot)
            lane = lax.broadcasted_iota(jnp.int32, (width, WINDOW), 1)
            value = jnp.where(held, molecule * MOL + spot - lane, -(10**6))
            target[r, pl.ds(t * width, width), :] = value
            return 0

        lax.fori_loop(0, STEPS, step, 0)


def windows(blocks, distances, start, tall):
    for n, (first, width, size) in enumerate(blocks):
        atom = start + n * BLOCK * MOL
        base = jnp.minimum(atom // SUB * SUB, tall - WINDOW)
        base = pl.multiple_of(base, SUB)
        chosen = distances[0] if size == BLOCK else distances[1]
        ones = [jnp.where(chosen[r] == base - atom, 1.0, 0.0).astype(BF16) for r in (0, 1)]
        yield first, width, pl.ds(base, WINDOW), ones


def spread(source, lanes, stage, blocks, distances, start):
    for first, width, here, ones in windows(blocks, distances, start, source.shape[0]):
        given = source[here, lanes]
        a, b = dot(ones[0], given), dot(ones[1], given)
        low = lax.broadcasted_iota(jnp.int32, (a.shape[0], LANES), 1) < R
        for n in range(a.shape[1] // LANES):
            left, right = a[:, n * LANES : (n + 1) * LANES], b[:, n * LANES : (n + 1) * LANES]
            one = jnp.where(low, left, pltpu.roll(right, R, 1))
            two = jnp.where(low, pltpu.roll(left, R, 1), right)
            stage[2 * n, :, first : first + width] = one.reshape(STEPS, width, LANES)
            stage[2 * n + 1, :, first : first + width] = two.reshape(STEPS, width, LANES)


def spread_positions(source, lanes, targets, blocks, distances, start):
    row = lax.broadcasted_iota(jnp.int32, (LANES, 3 * LANES), 0)
    lane = lax.broadcasted_iota(jnp.int32, (LANES, 3 * LANES), 1)
    axis = jnp.where(lane >= 2 * LANES, 2, jnp.where(lane >= LANES, 1, 0))
    mine = (row >= 3 * axis) & (row < 3 * axis + 3)
    low = lane - axis * LANES < R
    wide = [jnp.where(mine & (low == (r == 0)), 1.0, 0.0).astype(BF16) for r in (0, 1)]
    for first, width, here, ones in windows(blocks, distances, start, source.shape[0]):
        given = source[here, lanes]
        total = 0.0
        for r in (0, 1):
            total = total + dot(dot(ones[r], given).astype(BF16), wide[r])
        for d, target in enumerate(targets):
            value = total[:, d * LANES : (d + 1) * LANES]
            target[:, first : first + width] = value.reshape(STEPS, width, LANES)


def collect(sources, target, blocks, distances, start):
    target[...] = jnp.zeros(target.shape, F32)
    units = []
    for first, width, here, ones in windows(blocks, distances, start, target.shape[0]):
        units.append((first, width, here, ones))
    at = 0
    while at < len(units):
        group = units[at : at + 2] if units[at][0] % SUB == 0 and at + 1 < len(units) else None
        if group is None or (group[0][1] + group[1][1]) % SUB:
            group = units[at : at + 1]
        at += len(group)
        first = group[0][0]
        size = sum(g[1] for g in group)
        blocks_in = []
        for partner, carry in sources:
            value = partner[:, first : first + size].astype(F32)
            start_part = value[:SPAN] + carry[:, first : first + size]
            blocks_in.append(jnp.concatenate([start_part, value[SPAN:]], axis=0))
        for f, width, here, ones in group:
            parts = ([], [])
            for n in range(0, len(sources), 2):
                a = blocks_in[n][:, f - first : f - first + width].reshape(STEPS * width, LANES)
                b = blocks_in[n + 1][:, f - first : f - first + width]
                b = b.reshape(STEPS * width, LANES)
                low = lax.broadcasted_iota(jnp.int32, a.shape, 1) < R
                parts[0].append(jnp.where(low, a, pltpu.roll(b, R, 1)).astype(BF16))
                parts[1].append(jnp.where(low, pltpu.roll(a, R, 1), b).astype(BF16))
            total = 0.0
            for r in (0, 1):
                total = total + dot_tn(ones[r], jnp.concatenate(parts[r], axis=1))
            target[here, :] = target[here, :] + total


def row_masks(owned, start, blocks, atoms):
    for n, (at, width, size) in enumerate(blocks):
        _, molecule, _ = row_parts((width, LANES), 0, size)
        first = start - HALO + (n * BLOCK + molecule) * MOL
        owned[at : at + width] = jnp.where((first >= 0) & (first < atoms), 1.0, 0.0)


def set_picks(picks):
    row = lax.broadcasted_iota(jnp.int32, (LANES, LANES), 0)
    lane = lax.broadcasted_iota(jnp.int32, (LANES, LANES), 1)
    base = jnp.where(lane >= R, R, 0)
    for n in range(2 * OFFSETS):
        which = 1 + n if n < OFFSETS else 33 + n - OFFSETS
        block = jnp.where(row == base + which, 1.0, 0.0).astype(BF16)
        picks[:, n * LANES : (n + 1) * LANES] = block


def set_multiplicities(count, target, blocks, rows):
    lane = lax.broadcasted_iota(jnp.int32, (rows, LANES), 1)
    inner = jnp.where(lane >= R, lane - R, lane)
    last = []
    for _, width, size in blocks:
        last.append(row_parts((width, LANES), 0, size)[0])
    doubled = (jnp.concatenate(last, axis=0) == ROW_GROUPS - 1) & (lane >= R)
    for t in range(SPAN):
        value = jnp.where(inner < 32, count[t], 0.0)
        for k in range(1, OFFSETS + 1):
            value = jnp.where(inner == 32 + k, count[t + k], value)
        if t == SPAN - 1:
            value = jnp.where(doubled, 0.0, value)
        target[t] = value.astype(BF16)


def dot(a, b):
    return jnp.dot(a, b, preferred_element_type=F32)


def dot_tn(a, b):
    return lax.dot_general(a, b, (((0,), (0,)), ((), ())), preferred_element_type=F32)


def dot_nt(a, b):
    return lax.dot_general(a, b, (((1,), (1,)), ((), ())), preferred_element_type=F32)


COSINE = (0.9999999998, -0.04934802137, 0.000405870916, -1.335212003e-06, 2.349373138e-09, -2.43963243e-12)

GEO_ENVELOPE, GEO_SLOPE, GEO_BEND, GEO_OWN, GEO_WAY, GEO_INVERSE, GEO_FREE = 0, 1, 2, 3, 4, 7, 8
GEO = 9


def geometry(pos, t, rows, owned, radial, geo):
    lane = lax.broadcasted_iota(jnp.int32, (1, LANES), 1)
    centre = jnp.where(lane >= R, lane - R, lane).astype(F32)
    inv_space = (R - 1) / CUTOFF

    def step(k, _):
        for o, size in halves(rows):
            here = pl.ds(pl.multiple_of(k * rows + o, SUB), size)
            off = [p[t, o : o + size] - p[t + 1 + k, o : o + size] for p in pos]
            mine = owned[o : o + size]
            square = off[0] * off[0] + off[1] * off[1] + off[2] * off[2]
            clamped = jnp.maximum(square, 0.01)
            inverse = lax.rsqrt(clamped)
            c = COSINE[-1]
            for term in COSINE[-2::-1]:
                c = c * clamped + term
            c = jnp.where(clamped < CUTOFF * CUTOFF, c, 0.0)
            envelope = c * c
            y = jnp.maximum(envelope - envelope * envelope, 1e-30)
            free = jnp.where(square > 0.01, 1.0, 0.0)
            bend = ((-math.pi / CUTOFF) * free) * (y * lax.rsqrt(y))
            u = (clamped * inverse) * inv_space - centre
            bump = jnp.exp(-0.5 * (u * u))
            value = bump * envelope
            high = value.astype(BF16)
            slope = bump * bend - (inv_space * free) * (u * value)
            radial[here, :LANES] = high
            radial[here, LANES:] = (value - high.astype(F32)).astype(BF16)
            geo[GEO_OWN, here, :] = (value * mine).astype(BF16)
            geo[GEO_SLOPE, here, :] = slope.astype(BF16)
            geo[GEO_BEND, here, :] = bend.astype(BF16)
            geo[GEO_ENVELOPE, here, :] = envelope.astype(BF16)
            for d in range(3):
                geo[GEO_WAY + d, here, :] = (off[d] * inverse).astype(BF16)
            geo[GEO_INVERSE, here, :] = inverse.astype(BF16)
            geo[GEO_FREE, here, :] = (inverse * free).astype(BF16)
        return 0

    lax.fori_loop(0, OFFSETS, step, 0)


def halves(rows):
    tiles = rows // SUB
    first = (tiles + 1) // 2 * SUB
    return ((0, first), (first, rows - first))


def set_filters(weights_ref, filter_1, filter_2):
    weights_ref[...] = jnp.zeros(weights_ref.shape, BF16)
    for f, ref in enumerate((filter_1, filter_2)):
        half = ref[...] * jnp.asarray(0.5, BF16)
        for part in range(2):
            for g in range(LANE_GROUPS):
                down = part * LANES + g * R
                at = f * LANES + g * R
                weights_ref[down : down + R, at : at + R] = half


def gate(h):
    t = jnp.tanh(h)
    u = 1.0 + t
    f = h * u
    return f.astype(BF16), (u + f * (1.0 - t)).astype(BF16)


def carried(rows, t, totals, group, body):
    def outer(s, _):
        o = pl.multiple_of(s * SUB, SUB)
        block = pl.ds(o, SUB)
        ii = (t, block)
        sums = None
        for k in range(0, OFFSETS, group):
            loaded = []
            for n in range(k, k + group):
                here = pl.ds(o + n * rows, SUB)
                loaded.append(body(o, here, ii, (t + 1 + n, block), n))
            done = [f() for f in loaded]
            given = [one for one, _ in done]
            while len(given) > 1:
                left = given[len(given) // 2 * 2 :]
                pairs = zip(given[0::2], given[1::2])
                given = [[x + y for x, y in zip(a, b)] for a, b in pairs] + left
            total = [x.astype(F32) for x in given[0]]
            sums = total if sums is None else [x + y for x, y in zip(sums, total)]
            for _, stores in done:
                for ref, index, value in stores:
                    ref[index] = value
        for total, value in zip(totals, sums):
            total[ii] = value
        return 0

    lax.fori_loop(0, rows // SUB, outer, 0)


def lanes_of(n):
    return slice(n * LANES, (n + 1) * LANES)


def geometry_kernel(
    molecules, rows, atoms,
    scalars, rows_ref, radial_out, geo_out, owned, near, near_last, px, py, pz,
):
    t = pl.program_id(0)
    start = scalars[0]
    blocks = block_list(molecules, rows)
    distances = (near, near_last)

    @pl.when(t == 0)
    def _():
        row_masks(owned, start, blocks, atoms)
        set_distances(near, blocks[0][1], blocks[0][2])
        set_distances(near_last, blocks[-1][1], blocks[-1][2])
        lanes = slice(POS * LANES, (POS + 1) * LANES)
        spread_positions(rows_ref, lanes, (px, py, pz), blocks, distances, start)

    geometry((px, py, pz), t, rows, owned, radial_out.at[0], geo_out.at[0])


def vector_kernel(
    molecules, rows, atoms,
    scalars, rows_ref, filter_1, filter_2, radial_in, geo_in,
    sums_ref, back_ref, grads_ref, pos_out, grad_w_ref,
    weights_ref, picks, many, near, near_last, stage, loose, counts, pre, grad_pre,
    grad_radial, grad_ways,
    w0, w1, w2, v2, c0, c1, c2,
    s0, s1, s2, a0, a1, a2, gv, gx, gy, gz,
    fs0, fs1, fs2, fa0, fa1, fa2, fgv, fgx, fgy, fgz,
):
    t = pl.program_id(0)
    start = scalars[0]
    own = slice(HALO, HALO + atoms)
    radial, geo = radial_in.at[0], geo_in.at[0]
    w, c, g_pos = (w0, w1, w2), (c0, c1, c2), (gx, gy, gz)
    sums, backs = (s0, s1, s2), (a0, a1, a2)
    blocks = block_list(molecules, rows)
    distances = (near, near_last)

    @pl.when(t == 0)
    def _():
        set_filters(weights_ref, filter_1, filter_2)
        set_picks(picks)
        set_distances(near, blocks[0][1], blocks[0][2])
        set_distances(near_last, blocks[-1][1], blocks[-1][2])
        lanes = slice(W01 * LANES, (C2_COUNT + 1) * LANES)
        spread(rows_ref, lanes, stage, blocks, distances, start)
        for n, target in enumerate((w0, w1, w2, v2, c0, c1, c2)):
            target[...] = stage[n].astype(BF16)
        set_multiplicities(stage.at[7], many, blocks, rows)
        for total in (s0, s1, s2, a0, a1, a2, gv, gx, gy, gz):
            total[...] = jnp.zeros(total.shape, BF16)
        grad_w_ref[...] = jnp.zeros(grad_w_ref.shape, F32)

    counts[...] = dot(many[t], picks[...])
    pre[...] = dot(radial[...], weights_ref[...])

    def channel(o, here, ii, jj, k):
        h1, h2 = pre[here, :LANES], pre[here, LANES:]
        mi = counts[pl.ds(o, SUB), lanes_of(k)]
        mj = counts[pl.ds(o, SUB), lanes_of(OFFSETS + k)]
        v2i, v2j = v2[ii], v2[jj]
        ways = [geo[GEO_WAY + d, here, :] for d in range(3)]
        wi, wj = [w[d][ii] for d in range(3)], [w[d][jj] for d in range(3)]
        ci, cj = [c[d][ii] for d in range(3)], [c[d][jj] for d in range(3)]
        old_sums = [sums[d][jj] for d in range(3)]
        old_backs = [backs[d][jj] for d in range(3)]
        old_gv = gv[jj]

        def compute():
            f1, d1 = gate(h1)
            f2, d2 = gate(h2)
            ni, nj = mi.astype(BF16), mj.astype(BF16)
            f1i, f1j, f2i, f2j = f1 * ni, f1 * nj, f2 * ni, f2 * nj
            msg_i, msg_j = f2i * v2j, f2j * v2i
            stores, sum_i, back_i = [], [], []
            along_i = along_j = across_i = across_j = None
            for d in range(3):
                way = ways[d]
                sum_i.append(f1i * wj[d] + msg_i * way)
                stores.append((sums[d], jj, old_sums[d] + (f1j * wi[d] - msg_j * way)))
                stores.append((backs[d], jj, old_backs[d] + f1i * ci[d]))
                back_i.append(f1j * cj[d])
                grad = ci[d] * msg_i - cj[d] * msg_j
                stores.append((grad_ways, (d, here, slice(None)), grad))
                new = (ci[d] * way, cj[d] * way, ci[d] * wj[d], cj[d] * wi[d])
                if d == 0:
                    along_i, along_j, across_i, across_j = new
                else:
                    along_i, along_j = along_i + new[0], along_j + new[1]
                    across_i, across_j = across_i + new[2], across_j + new[3]
            stores.append((gv, jj, old_gv + f2i * along_i))
            g1 = ni * across_i + nj * across_j
            g2 = ni * along_i * v2j - nj * along_j * v2i
            stores.append((grad_pre, (here, slice(0, LANES)), g1 * d1))
            stores.append((grad_pre, (here, slice(LANES, None)), g2 * d2))
            return sum_i + back_i + [-(f2j * along_j)], stores

        return compute

    carried(rows, t, (fs0, fs1, fs2, fa0, fa1, fa2, fgv), 2, channel)
    grad_radial[...] = dot_nt(grad_pre[...], weights_ref[:LANES])
    grad_w_ref[...] = grad_w_ref[...] + dot_tn(geo[GEO_OWN], grad_pre[...])

    def turn(o, here, ii, jj, k):
        ways = [geo[GEO_WAY + d, here, :] for d in range(3)]
        grads = [grad_ways[d, here, :] for d in range(3)]
        grad, slope = grad_radial[here, :], geo[GEO_SLOPE, here, :]
        inverse, free = geo[GEO_INVERSE, here, :], geo[GEO_FREE, here, :]
        old = [g[jj] for g in g_pos]

        def compute():
            along = ways[0] * grads[0] + ways[1] * grads[1] + ways[2] * grads[2]
            pull = grad.astype(BF16) * slope - free * along
            out = [grads[d] * inverse + ways[d] * pull for d in range(3)]
            return out, [(g_pos[d], jj, old[d] - out[d]) for d in range(3)]

        return compute

    carried(rows, t, (fgx, fgy, fgz), 7, turn)

    @pl.when(t == SPAN - 1)
    def _():
        low = lax.broadcasted_iota(jnp.int32, (atoms, LANES), 1) < R
        totals = (s0, s1, s2, gv, a0, a1, a2, gx, gy, gz)
        firsts = (fs0, fs1, fs2, fgv, fa0, fa1, fa2, fgx, fgy, fgz)
        collect(tuple(zip(totals, firsts)), loose, blocks, distances, start)
        both = loose[own, :LANES].T
        sums_ref[0] = both[:R]
        sums_ref[1] = both[R:]
        both = loose[own, LANES : 2 * LANES].T
        sums_ref[2] = both[:R]
        grads_ref[R:] = both[R:].astype(BF16)

        def kept(n):
            return rows_ref[own, n * LANES : (n + 1) * LANES].astype(F32)

        v12 = kept(V12)
        v11 = jnp.where(low, v12, pltpu.roll(v12, R, 1))
        back = loose[own, 2 * LANES : 3 * LANES]
        both = (back * v11).T
        back_ref[0] = both[:R]
        back_ref[1] = both[R:]
        partial = back * kept(VEC01)
        partial = partial + pltpu.roll(partial, R, 1)
        back = loose[own, 3 * LANES : 4 * LANES]
        back_ref[2] = (back * v11).T[:R]
        partial = partial + back * kept(VEC2)
        grads_ref[:R] = partial.T[:R].astype(BF16)
        pos_out[...] = jnp.zeros(pos_out.shape, F32)
        pos_out[0:1] = jnp.sum(back.T[R:], axis=0, keepdims=True)
        both = loose[own, 4 * LANES :].T
        pos_out[1:2] = jnp.sum(both[:R], axis=0, keepdims=True)
        pos_out[2:3] = jnp.sum(both[R:], axis=0, keepdims=True)


def scalar_kernel(
    molecules, rows, atoms,
    scalars, rows_ref, filter_1, filter_2, scalar_parts, radial_in, geo_in,
    sum_ref, grads_ref, pos_out, grad_w_ref,
    weights_ref, picks, many, heads_ref, near, near_last, stage, loose, loose_low, counts, pre,
    grad_pre, grad_radial, products, sums, gates, bends,
    q, key, v0, gs,
    ss, gq, gk, g0, gx, gy, gz,
    fss, fgq, fgk, fg0, fgx, fgy, fgz,
):
    t = pl.program_id(0)
    start = scalars[0]
    own = slice(HALO, HALO + atoms)
    radial, geo = radial_in.at[0], geo_in.at[0]
    g_pos = (gx, gy, gz)
    blocks = block_list(molecules, rows)
    distances = (near, near_last)

    @pl.when(t == 0)
    def _():
        set_filters(weights_ref, filter_1, filter_2)
        set_picks(picks)
        row = lax.broadcasted_iota(jnp.int32, (2 * LANES, 2 * LANES), 0)
        lane = lax.broadcasted_iota(jnp.int32, (2 * LANES, 2 * LANES), 1)
        heads_ref[...] = jnp.where(row // HEAD == lane // HEAD, 1.0, 0.0).astype(BF16)
        set_distances(near, blocks[0][1], blocks[0][2])
        set_distances(near_last, blocks[-1][1], blocks[-1][2])
        lanes = slice(QK * LANES, (V0_COUNT + 1) * LANES)
        spread(rows_ref, lanes, stage, blocks, distances, start)
        for n, target in enumerate((q, key, v0)):
            target[...] = stage[n].astype(BF16)
        set_multiplicities(stage.at[3], many, blocks, rows)
        summed = scalar_parts[0].astype(F32)
        for f in range(1, scalar_parts.shape[0]):
            summed = summed + scalar_parts[f].astype(F32)
        summed = jnp.concatenate([summed, jnp.zeros_like(summed)], axis=0).T.astype(BF16)
        loose_low[own] = summed[:atoms]
        loose_low[:HALO] = summed[atoms : atoms + HALO]
        loose_low[HALO + atoms : 2 * HALO + atoms] = summed[atoms + HALO : atoms + 2 * HALO]
        end = 2 * HALO + atoms
        loose_low[end:] = jnp.zeros((loose_low.shape[0] - end, LANES), BF16)
        spread(loose_low, slice(None), stage, blocks, distances, start)
        gs[...] = stage[0].astype(BF16)
        for total in (ss, gq, gk, g0, gx, gy, gz):
            total[...] = jnp.zeros(total.shape, BF16)
        grad_w_ref[...] = jnp.zeros(grad_w_ref.shape, F32)

    counts[...] = dot(many[t], picks[...])
    pre[...] = dot(radial[...], weights_ref[...])

    def multiply(k, _):
        for o, size in halves(rows):
            here = pl.ds(pl.multiple_of(k * rows + o, SUB), size)
            ii, jj = (t, slice(o, o + size)), (t + 1 + k, slice(o, o + size))
            fk, dk = gate(pre[here, :LANES])
            f0, d0 = gate(pre[here, LANES:])
            k_ij, k_ji = q[ii] * key[jj] * fk, q[jj] * key[ii] * fk
            s_ij, s_ji = gs[ii] * v0[jj] * f0, gs[jj] * v0[ii] * f0
            gates[0, here, :] = fk
            gates[1, here, :] = f0
            gates[2, here, :] = dk
            gates[3, here, :] = d0
            products[0, here, :LANES] = k_ij
            products[0, here, LANES:] = k_ji
            products[1, here, :LANES] = s_ij
            products[1, here, LANES:] = s_ji
        return 0

    lax.fori_loop(0, OFFSETS, multiply, 0)
    sums[0] = dot(products[0], heads_ref[...])
    sums[1] = dot(products[1], heads_ref[...])

    def channel(o, here, ii, jj, k):
        fk, f0, dk, d0 = [gates[n, here, :] for n in range(4)]
        envelope, bend = geo[GEO_ENVELOPE, here, :], geo[GEO_BEND, here, :]
        side_in = []
        for side in range(2):
            lanes = slice(side * LANES, (side + 1) * LANES)
            m = counts[pl.ds(o, SUB), lanes_of(side * OFFSETS + k)]
            h, o_ = (ii, jj) if side == 0 else (jj, ii)
            side_in.append(
                (m, sums[0, here, lanes], sums[1, here, lanes])
                + (q[h], key[o_], gs[h], v0[o_])
            )
        old = [ref[jj] for ref in (g0, gk, ss, gq)]

        def compute():
            gives, news = [], []
            for m, score, g_att, qh, kt, gh, vt in side_in:
                act, rise = gate(0.5 * score)
                m, g_att = m.astype(BF16), g_att.astype(BF16)
                weight = m * envelope
                att = act * weight
                g_score = g_att * (0.5 * rise) * weight
                lift = m * (g_att * act)
                bv, dv = f0 * att, fk * g_score
                gives.append((vt * bv, kt * dv, gh * bv, qh * dv))
                news.append((qh * kt * g_score, gh * vt * att, lift))
            one, two = gives
            new = [x + y for x, y in zip(*news)]
            stores = [
                (ref, jj, x + y)
                for ref, x, y in zip((g0, gk, ss, gq), old, (one[2], one[3], two[0], two[1]))
            ]
            stores.append((grad_pre, (here, slice(0, LANES)), new[0] * dk))
            stores.append((grad_pre, (here, slice(LANES, None)), new[1] * d0))
            stores.append((bends, (here, slice(None)), new[2] * bend * (1.0 / HEAD)))
            return [one[0], one[1], two[2], two[3]], stores

        return compute

    carried(rows, t, (fss, fgq, fg0, fgk), 2, channel)
    grad_radial[...] = dot_nt(grad_pre[...], weights_ref[:LANES])
    grad_w_ref[...] = grad_w_ref[...] + dot_tn(geo[GEO_OWN], grad_pre[...])

    def turn(o, here, ii, jj, k):
        ways = [geo[GEO_WAY + d, here, :] for d in range(3)]
        grad, slope, bend = grad_radial[here, :], geo[GEO_SLOPE, here, :], bends[here, :]
        old = [g[jj] for g in g_pos]

        def compute():
            pull = grad.astype(BF16) * slope + bend
            out = [way * pull for way in ways]
            return out, [(g_pos[d], jj, old[d] - out[d]) for d in range(3)]

        return compute

    carried(rows, t, (fgx, fgy, fgz), 7, turn)

    @pl.when(t == SPAN - 1)
    def _():
        totals = (ss, g0, gq, gk, gx, gy, gz, gz)
        firsts = (fss, fg0, fgq, fgk, fgx, fgy, fgz, fgz)
        collect(tuple(zip(totals, firsts)), loose, blocks, distances, start)
        both = loose[own, :LANES].T
        sum_ref[...] = both[:R].astype(BF16)
        grads_ref[2 * R :] = both[R:].astype(BF16)
        grads_ref[: 2 * R] = loose[own, LANES : 2 * LANES].T.astype(BF16)
        pos_out[...] = jnp.zeros(pos_out.shape, F32)
        both = loose[own, 2 * LANES : 3 * LANES].T
        pos_out[0:1] = jnp.sum(both[:R], axis=0, keepdims=True)
        pos_out[1:2] = jnp.sum(both[R:], axis=0, keepdims=True)
        both = loose[own, 3 * LANES :].T
        pos_out[2:3] = jnp.sum(both[:R], axis=0, keepdims=True)


def whole(memory=pltpu.VMEM):
    return pl.BlockSpec(memory_space=memory)


def params(mib=60):
    return pltpu.CompilerParams(vmem_limit_bytes=mib * 1024 * 1024)


def edge_sizes(atoms):
    molecules = (atoms + 2 * (MOL - 1)) // MOL
    full, rest = divmod(molecules, BLOCK)
    rows = full * ROW_GROUPS * BLOCK + -(-ROW_GROUPS * rest // BLOCK) * BLOCK
    rows = -(-rows // SUB) * SUB
    tall = -(-(HALO + molecules * MOL) // SUB) * SUB
    return molecules, rows, tall


def by_step(shape):
    zeros = (0,) * (len(shape) - 1)
    return pl.BlockSpec((1,) + shape[1:], lambda t: (t,) + zeros)


def fixed(shape):
    zeros = (0,) * len(shape)
    return pl.BlockSpec(shape, lambda t: zeros)


def edge_call(kernel, atoms, inputs, stepped_in, outs, stepped_out, scratch):
    molecules, rows, _ = edge_sizes(atoms)
    return pl.pallas_call(
        functools.partial(kernel, molecules, rows, atoms),
        grid=(SPAN,),
        out_shape=[jax.ShapeDtypeStruct(s, kind) for s, kind in outs + stepped_out],
        in_specs=[whole(pltpu.SMEM)]
        + [fixed(x.shape) for x in inputs[1:]]
        + [by_step(x.shape) for x in stepped_in],
        out_specs=[fixed(s) for s, _ in outs] + [by_step(s) for s, _ in stepped_out],
        scratch_shapes=[pltpu.VMEM(s, kind) for s, kind in scratch],
        compiler_params=params(),
        cost_estimate=pl.CostEstimate(
            flops=20 * 10**9, bytes_accessed=40 * 10**6, transcendentals=10**7
        ),
    )(*inputs, *stepped_in)


def shared_scratch(atoms):
    molecules, rows, tall = edge_sizes(atoms)
    batch = OFFSETS * rows
    blocks = block_list(molecules, rows)
    return {
        "weights": ((2 * LANES, 2 * LANES), BF16),
        "picks": ((LANES, 2 * OFFSETS * LANES), BF16),
        "many": ((SPAN, rows, LANES), BF16),
        "mask": ((rows, LANES), F32),
        "near": ((LANE_GROUPS, STEPS * blocks[0][1], WINDOW), jnp.int32),
        "near_last": ((LANE_GROUPS, STEPS * blocks[-1][1], WINDOW), jnp.int32),
        "stage8": ((8, STEPS, rows, LANES), F32),
        "stage4": ((4, STEPS, rows, LANES), F32),
        "loose5": ((tall, 5 * LANES), F32),
        "loose4": ((tall, 4 * LANES), F32),
        "loose_low": ((tall, LANES), BF16),
        "tall": ((STEPS, rows, LANES), F32),
        "low": ((STEPS, rows, LANES), BF16),
        "first": ((SPAN, rows, LANES), F32),
        "counts": ((rows, 2 * OFFSETS * LANES), F32),
        "pre": ((batch, 2 * LANES), F32),
        "grad_pre": ((batch, 2 * LANES), BF16),
        "line": ((batch, LANES), F32),
        "line2": ((2, batch, LANES), BF16),
        "line3": ((3, batch, LANES), BF16),
        "line4": ((4, batch, LANES), BF16),
        "line1": ((batch, LANES), BF16),
        "wide2": ((2, batch, 2 * LANES), BF16),
        "wide2f": ((2, batch, 2 * LANES), F32),
    }


def offsets_in_block(neighbours, mask, first):
    lane = lax.broadcasted_iota(jnp.int32, neighbours.shape, 1)
    diff = neighbours - (first + lane)
    return jnp.where(diff < 0, diff + MOL, diff) * mask


def pieces(x):
    a = x.astype(BF16)
    rest = x - a.astype(F32)
    b = rest.astype(BF16)
    return a, b, (rest - b.astype(F32)).astype(BF16)


def edge_groups(features, vectors, cot_f, cot_v, neighbours, mask, positions, first):
    diff = offsets_in_block(neighbours[...], mask[...], first).astype(F32).astype(BF16)
    groups = [jnp.concatenate([features[...], cot_f[...], diff], axis=0)]
    for d in range(3):
        rows = [x.astype(F32) for x in pieces(positions[d : d + 1])]
        rows = jnp.concatenate(rows + [jnp.zeros((29, LANES), F32)], axis=0).astype(BF16)
        groups.append(jnp.concatenate([vectors[d], cot_v[d], rows], axis=0))
    return groups


def halo_kernel(atoms, scalars, *refs):
    row_first = scalars[2]
    lane = lax.broadcasted_iota(jnp.int32, (GROUP_ROWS, LANES), 1)
    for end, at, out in ((0, atoms - LANES, refs[14]), (1, 0, refs[15])):
        groups = edge_groups(*refs[7 * end : 7 * end + 7], row_first + at)
        total = None
        for g, group in enumerate(groups):
            by = (HALO * (g + 1) if end == 0 else HALO * g) % LANES
            moved = group.astype(F32)
            moved = pltpu.roll(moved, by, 1) if by else moved
            total = moved if total is None else jnp.where(lane >= HALO * g, moved, total)
        out[...] = total.astype(BF16)


def halo_call(atoms, scalars, arrays):
    specs = []
    for at in (atoms // LANES - 1, 0):
        for x in arrays:
            shape = x.shape[:-1] + (LANES,)
            index = (0,) * (x.ndim - 1) + (at,)
            specs.append(pl.BlockSpec(shape, lambda *_, index=index: index))
    out = jax.ShapeDtypeStruct((GROUP_ROWS, LANES), BF16)
    return pl.pallas_call(
        functools.partial(halo_kernel, atoms),
        grid=(1,),
        out_shape=[out, out],
        in_specs=[whole(pltpu.SMEM)] + specs,
        out_specs=[whole(), whole()],
        compiler_params=params(),
    )(scalars, *arrays, *arrays)


def column(row):
    return jnp.broadcast_to(row, (8, row.shape[1])).T[:, :1]


def normalised(f):
    mean = jnp.mean(f, axis=0, keepdims=True)
    centred = f - mean
    inv = lax.rsqrt(jnp.mean(centred * centred, axis=0, keepdims=True) + EPSILON)
    return centred * inv, mean, inv


def dense_kernel(
    atoms,
    scalars, features, vectors, cot_f, cot_v, neighbours, mask, positions, low_ref, high_ref,
    gain_ref, bias_ref, w_query, w_key, w_value, w_vector, w_output,
    rows_ref, part_ref, stat_ref,
    w_qk, w_v0, w_v12, w_vec_t, w_out,
):
    chan_first = pl.multiple_of(scalars[1], R)
    row_first = scalars[2]
    gain, bias = column(gain_ref[...]), column(bias_ref[...])
    w_qk[:R] = w_query[...]
    w_qk[R:] = w_key[...]
    w_v0[:R] = w_value[0]
    w_v0[R:] = jnp.zeros((R, H), BF16)
    w_v12[:R] = w_value[1]
    w_v12[R:] = w_value[2]
    for p in range(3):
        w_vec_t[p * R : (p + 1) * R] = w_vector[p]
    w_out[...] = jnp.concatenate([w_output[p] for p in range(3)], axis=0).astype(F32).T.astype(BF16)

    def block(f, v, cf, cv, own_v, diff, pos):
        width = f.shape[1]
        normed, mean, inv = normalised(f)
        turned = (normed * gain + bias).T.astype(BF16)
        kinds = lax.broadcasted_iota(jnp.int32, (R, width), 0)
        kinds = jnp.where(kinds < 32, kinds, MOL + 32 - kinds).astype(F32)
        counts = jnp.zeros((R, width), F32)
        for s in range(diff.shape[0]):
            counts = counts + jnp.where(diff[s : s + 1] == kinds, 1.0, 0.0)
        none = jnp.zeros((R, width), F32)
        counts = jnp.concatenate([none, counts], axis=0).T
        low = lax.broadcasted_iota(jnp.int32, (width, LANES), 1) < R
        pairs = [None] * 10
        pairs[QK] = dot_nt(turned, w_qk[...])
        pairs[V0_COUNT] = dot_nt(turned, w_v0[...]) + counts
        v12 = dot_nt(turned, w_v12[...]).astype(BF16).astype(F32)
        v11 = jnp.where(low, v12, pltpu.roll(v12, R, 1))
        pairs[V12] = v12
        pairs[VEC01] = jnp.concatenate([own_v[0], own_v[1]], axis=0).T
        pairs[VEC2] = jnp.concatenate([own_v[2], none], axis=0).T
        pairs[W01] = pairs[VEC01] * v11
        pairs[W2V2] = jnp.where(low, pairs[VEC2] * v11, v12)
        pairs[C01] = jnp.concatenate([cv[0], cv[1]], axis=0).T
        pairs[C2_COUNT] = jnp.concatenate([cv[2], none], axis=0).T + counts
        pairs[POS] = jnp.concatenate([pos, jnp.zeros((LANES - 9, width), F32)], axis=0).T
        vec_dot = grad_0 = 0.0
        for d in range(3):
            proj = dot(w_vec_t[...], v[d])
            vec_dot = vec_dot + proj[:R] * proj[R : 2 * R]
            grad_0 = grad_0 + cv[d] * proj[2 * R :]
        grad_out = jnp.concatenate([grad_0, cf * vec_dot, cf], axis=0).astype(BF16)
        part = dot(w_out[...], grad_out)
        return [x.astype(BF16) for x in pairs], part.astype(BF16), mean, inv

    wide = 2 * LANES

    def step(b, _):
        at = pl.multiple_of(b * wide, wide)
        here = pl.ds(at, wide)
        own_v = [vectors[d, pl.ds(chan_first, R), here].astype(F32) for d in range(3)]
        diff = offsets_in_block(neighbours[:, here], mask[:, here], row_first + at)
        places = [p.astype(F32) for d in range(3) for p in pieces(positions[d : d + 1, here])]
        pairs, part, mean, inv = block(
            features[:, here].astype(F32),
            [vectors[d, :, here] for d in range(3)],
            cot_f[:, here].astype(F32),
            [cot_v[d, :, here].astype(F32) for d in range(3)],
            own_v,
            diff.astype(F32),
            jnp.concatenate(places, axis=0),
        )
        there = pl.ds(pl.multiple_of(HALO + at, 2 * SUB), wide)
        for n, pair in enumerate(pairs):
            rows_ref[there, n * LANES : (n + 1) * LANES] = pair
        part_ref[:, here] = part
        stat_ref[0:1, here] = mean
        stat_ref[1:2, here] = inv
        return 0

    lax.fori_loop(0, atoms // wide, step, 0)

    lane = lax.broadcasted_iota(jnp.int32, (GROUP_ROWS, LANES), 1)
    packed_low, packed_high = low_ref[...].astype(F32), high_ref[...].astype(F32)
    groups = []
    for g in range(4):
        a = pltpu.roll(packed_low, (LANES - HALO * g) % LANES, 1) if g else packed_low
        by = (LANES + HALO - HALO * g) % LANES
        b = pltpu.roll(packed_high, by, 1) if by else packed_high
        both = jnp.where(lane < HALO, a, jnp.where(lane < 2 * HALO, b, 0.0))
        groups.append(both)
    pick_rows = lax.broadcasted_iota(jnp.int32, (H, LANES), 0)
    own_v, pos = [], []
    for d in range(3):
        g = groups[1 + d]
        found = g[:R]
        for f in range(1, H // R):
            found = jnp.where(chan_first == f * R, g[f * R : (f + 1) * R], found)
        own_v.append(found)
        pos.append(g[320:323])
    pairs, part, _, _ = block(
        groups[0][:H],
        [groups[1 + d][:H].astype(BF16) for d in range(3)],
        groups[0][H : H + R],
        [groups[1 + d][H : H + R] for d in range(3)],
        own_v,
        groups[0][H + R :],
        jnp.concatenate(pos, axis=0),
    )
    high = HALO + atoms
    tall = rows_ref.shape[0]
    for n, pair in enumerate(pairs):
        lanes = slice(n * LANES, (n + 1) * LANES)
        rows_ref[:HALO, lanes] = pair[:HALO]
        rows_ref[high : high + HALO, lanes] = pair[HALO : 2 * HALO]
        rows_ref[high + HALO :, lanes] = jnp.zeros((tall - high - HALO, LANES), BF16)
    part_ref[:, atoms:] = part


def both_diagonals(grad, f):
    at = f * LANES
    return 0.5 * (grad[:R, at : at + R] + grad[R:, at + R : at + LANES])


def layer_kernel(
    atoms,
    scalars, features, vectors, cot_f, cot_v, gathered, w_vector, w_output,
    feat_out, delta_ref, square_ref, send_ref, flat_ref,
    w_vec, w_vec_t, w_out_t, t_vec, t_out,
):
    chan_first = pl.multiple_of(scalars[1], R)
    for p in range(3):
        w_vec_t[p * R : (p + 1) * R] = w_vector[p]
        w_out_t[p * R : (p + 1) * R] = w_output[p]
    w_vec[...] = w_vec_t[...].astype(F32).T.astype(BF16)
    t_vec[...] = jnp.zeros(t_vec.shape, F32)
    t_out[...] = jnp.zeros(t_out.shape, F32)
    wide = 2 * LANES
    split = send_ref.shape[0]

    def step(b, _):
        at = pl.multiple_of(b * wide, wide)
        here = pl.ds(at, wide)
        all_sums = gathered[:, here]
        outputs = dot(w_out_t[...], all_sums)
        out_0, out_1, out_2 = outputs[:R], outputs[R : 2 * R], outputs[2 * R :]
        cf = cot_f[:, here].astype(F32)
        grad_dot = cf * out_1
        vec_dot = grad_0 = 0.0
        for d in range(3):
            proj = dot(w_vec_t[...], vectors[d, :, here])
            first, second, third = proj[:R], proj[R : 2 * R], proj[2 * R :]
            cv = cot_v[d, :, here].astype(F32)
            vec_dot = vec_dot + first * second
            grad_0 = grad_0 + cv * third
            delta_ref[d, :, here] = third * out_0
            grad_proj = jnp.concatenate(
                [grad_dot * second, grad_dot * first, cv * out_0], axis=0
            ).astype(BF16)
            part = dot(w_vec[...], grad_proj).astype(BF16)
            for f in range(split):
                send_ref[f, d * R : (d + 1) * R, here] = part[f * R : (f + 1) * R]
            t_vec[...] = t_vec[...] + dot_nt(grad_proj, vectors[d, :, here])
        delta = vec_dot * out_1 + out_2
        moved = features[pl.ds(chan_first, R), here].astype(F32) + delta
        feat_out[:, here] = moved.astype(BF16)
        grad_out = jnp.concatenate([grad_0, cf * vec_dot, cf], axis=0).astype(BF16)
        t_out[...] = t_out[...] + dot_nt(grad_out, all_sums)
        square_ref[0:1, here] = jnp.sum(moved * moved, axis=0, keepdims=True)
        square_ref[1:2, here] = jnp.sum(delta * delta, axis=0, keepdims=True)
        return 0

    lax.fori_loop(0, atoms // wide, step, 0)
    flat_ref[: 3 * R] = t_vec[...].astype(BF16)
    flat_ref[3 * R :] = t_out[...].astype(BF16)


def normal_kernel(
    atoms,
    scalars, features, stat, vectors, delta_ref, square_ref, sums_ref,
    grads_b, grads_a, pos_a, pos_b, mask, gain_ref, bias_ref,
    w_query, w_key, w_value, grad_filters_a, grad_filters_b,
    vec_out, send_ref, flat_ref,
    w_five, t_five,
):
    chan_first = pl.multiple_of(scalars[1], R)
    gain, bias = column(gain_ref[...]), column(bias_ref[...])
    five = [w_query[...], w_key[...]] + [w_value[p] for p in range(3)]
    w_five[...] = jnp.concatenate(five, axis=0).astype(F32).T.astype(BF16)
    t_five[...] = jnp.zeros(t_five.shape, F32)
    wide = 2 * LANES
    split = send_ref.shape[0]

    def step(b, _):
        at = pl.multiple_of(b * wide, wide)
        here = pl.ds(at, wide)
        real = mask[:, here].astype(F32)
        square_v = square_dv = 0.0
        for d in range(3):
            delta = delta_ref[d, :, here] + sums_ref[d, :, here]
            moved = vectors[d, pl.ds(chan_first, R), here].astype(F32) + delta
            vec_out[d, :, here] = moved.astype(BF16)
            square_v = square_v + moved * moved
            square_dv = square_dv + delta * delta
        normed = (features[:, here].astype(F32) - stat[0:1, here]) * stat[1:2, here]
        normal = (normed * gain + bias).astype(BF16)
        grads = jnp.concatenate([grads_b[:, here], grads_a[:, here]], axis=0)
        t_five[...] = t_five[...] + dot_nt(grads, normal)
        part = dot(w_five[...], grads)
        rounded = part.astype(BF16)
        for f in range(split):
            send_ref[f, :R, here] = rounded[f * R : (f + 1) * R]
        hat = part * gain
        tops = [
            jnp.sum(hat, axis=0, keepdims=True),
            jnp.sum(hat * normed, axis=0, keepdims=True),
        ]
        exact = [pos_a[d : d + 1, here] + pos_b[d : d + 1, here] for d in range(3)]
        exact += [square_ref[n : n + 1, here] * real for n in range(2)]
        for x in (square_v, square_dv):
            exact.append(jnp.sum(x, axis=0, keepdims=True) * real)
        heads = [x.astype(BF16).astype(F32) for x in exact]
        tops = tops + heads + [x - y for x, y in zip(exact, heads)]
        tops = jnp.concatenate(tops, axis=0).astype(BF16)
        for f in range(split):
            send_ref[f, R:, here] = tops
        return 0

    lax.fori_loop(0, atoms // wide, step, 0)
    grad_a, grad_b = grad_filters_a[...], grad_filters_b[...]
    filters = [both_diagonals(g, f) for g in (grad_b, grad_a) for f in range(2)]
    flat_ref[: 5 * R] = t_five[...].astype(BF16)
    flat_ref[5 * R :] = jnp.concatenate(filters, axis=1).astype(BF16)


def final_kernel(
    atoms,
    scalars, got, got_vec, features, stat, gain_ref, cot_f, cot_v, back_ref, mask,
    grad_feat, grad_vec, grad_pos, small_ref,
):
    chan_first = pl.multiple_of(scalars[1], R)
    whole_gain = column(gain_ref[...])
    gain = whole_gain[:R]
    for f in range(1, H // R):
        gain = jnp.where(chan_first == f * R, whole_gain[f * R : (f + 1) * R], gain)

    def summed(ref, rows):
        total = ref[0, rows].astype(F32)
        for f in range(1, ref.shape[0]):
            total = total + ref[f, rows].astype(F32)
        return total

    tops = summed(got, slice(R, R + EXTRAS))
    grad_normal = summed(got, slice(0, R))
    inv = stat[1:2]
    normed = (features[pl.ds(chan_first, R), :].astype(F32) - stat[0:1]) * inv
    inner = grad_normal * gain - tops[0:1] * (1.0 / H) - normed * (tops[1:2] * (1.0 / H))
    grad_feat[...] = cot_f[...].astype(F32) + inv * inner
    for d in range(3):
        part = summed(got_vec, slice(d * R, (d + 1) * R))
        grad_vec[d] = cot_v[d].astype(F32) + part + back_ref[d]
    exact = tops[2:9] + tops[9:16]
    grad_pos[...] = exact[:3]
    ones = jnp.ones((8, atoms), BF16)
    gains = dot_nt(ones, (grad_normal * normed).astype(BF16))
    biases = dot_nt(ones, grad_normal.astype(BF16))
    totals = jnp.sum(exact[3:7], axis=1, keepdims=True)
    real = jnp.sum(mask[...].astype(F32), axis=1, keepdims=True)
    numbers = jnp.concatenate([totals, real, jnp.zeros((3, 1), F32)], axis=0)
    small = jnp.concatenate([gains, biases, jnp.broadcast_to(numbers, (8, LANES))], axis=1)
    high = small.astype(BF16)
    small_ref[:8] = high.astype(F32)
    small_ref[8:] = small - high.astype(F32)


def unpack_kernel(
    share,
    got,
    g_gain, g_bias, g_query, g_key, g_value, g_vector, g_output, g_key_f, g_value_f, rms_ref,
):
    every = [got[n].astype(F32) for n in range(got.shape[0])]
    total = 0.0
    for x in every:
        total = total + (x[2 * share : 2 * share + 8] + x[2 * share + 8 : 2 * share + 16])
    g_gain[...] = total[0:1, :R]
    g_bias[...] = total[0:1, R : 2 * R]
    numbers = total[:, LANES : LANES + 1]
    size = jnp.where(lax.broadcasted_iota(jnp.int32, (8, 1), 0) < 2, 1.0, 3.0) * H
    rms = jnp.sqrt(numbers / (numbers[4:5] * size) + 1e-06)
    rms_ref[...] = jnp.broadcast_to(rms, (8, LANES)).T[:1, :8]
    early = [(g, p) for g in (g_vector, g_output) for p in range(3)]
    late = [(g_query, None), (g_key, None)] + [(g_value, p) for p in range(3)]
    for n, x in enumerate(every):
        for first, names in ((0, early), (share, late)):
            at = n * share
            while at < (n + 1) * share:
                m = at // R
                size = min((m + 1) * R, (n + 1) * share) - at
                value = x[first + at - n * share : first + at - n * share + size]
                rows = slice(at - m * R, at - m * R + size)
                at += size
                if m == len(names):
                    g_key_f[rows] = value[:, :R]
                    for p in range(3):
                        g_value_f[p, rows] = value[:, (1 + p) * R : (2 + p) * R]
                    continue
                g, p = names[m]
                if p is None:
                    g[rows] = value
                else:
                    g[p, rows] = value


def everywhere(x, axis):
    count = lax.axis_size(axis)
    return lax.all_to_all(jnp.broadcast_to(x[None], (count,) + x.shape), axis, 0, 0)


def per_device(
    features, vectors, positions, atom_mask, neighbours, ln_gain, ln_bias,
    w_query, w_key, w_value, w_vector, w_output, w_key_filter, w_value_filter,
    cot_features, cot_vectors,
):
    channels = w_query.shape[1]
    atoms = features.shape[1]
    count = lax.axis_size("atoms")
    split = lax.axis_size("feat")
    chan_first = lax.axis_index("feat") * channels
    row_first = lax.axis_index("atoms") * atoms
    start = HALO - lax.rem(row_first, MOL)
    scalars = jnp.stack([start, chan_first, row_first]).astype(jnp.int32)
    molecules, rows_each, tall = edge_sizes(atoms)
    w_query, w_key = w_query.T, w_key.T
    w_value, w_vector, w_output = [jnp.swapaxes(w, 1, 2) for w in (w_value, w_vector, w_output)]
    mask = atom_mask.reshape(1, atoms)
    gain, bias = ln_gain.reshape(1, H), ln_bias.reshape(1, H)

    ends = halo_call(
        atoms,
        scalars,
        (features, vectors, cot_features, cot_vectors, neighbours, mask, positions),
    )
    low = lax.ppermute(ends[0], "atoms", [(i, i + 1) for i in range(count - 1)])
    high = lax.ppermute(ends[1], "atoms", [(i + 1, i) for i in range(count - 1)])

    inputs = (
        scalars, features, vectors, cot_features, cot_vectors, neighbours, mask, positions,
        low, high, gain, bias, w_query, w_key, w_value, w_vector, w_output,
    )
    rows, part, stat = pl.pallas_call(
        functools.partial(dense_kernel, atoms),
        out_shape=[
            jax.ShapeDtypeStruct((tall, 10 * LANES), BF16),
            jax.ShapeDtypeStruct((H, atoms + LANES), BF16),
            jax.ShapeDtypeStruct((8, atoms), F32),
        ],
        in_specs=[whole(pltpu.SMEM)] + [whole()] * (len(inputs) - 1),
        out_specs=[whole()] * 3,
        scratch_shapes=[
            pltpu.VMEM((LANES, H), BF16),
            pltpu.VMEM((LANES, H), BF16),
            pltpu.VMEM((LANES, H), BF16),
            pltpu.VMEM((3 * R, H), BF16),
            pltpu.VMEM((H, 3 * R), BF16),
        ],
        compiler_params=params(),
    )(*inputs)
    scalar_parts = lax.all_to_all(part.reshape(split, channels, atoms + LANES), "feat", 0, 0)

    kinds = shared_scratch(atoms)
    batch = OFFSETS * rows_each
    names = ["mask", "near", "near_last"] + ["tall"] * 3
    radial, geo = edge_call(
        geometry_kernel,
        atoms,
        (scalars, rows),
        (),
        [],
        [((SPAN, batch, 2 * LANES), BF16), ((SPAN, GEO, batch, LANES), BF16)],
        [kinds[name] for name in names],
    )
    names = ["weights", "picks", "many", "weights", "near", "near_last", "stage4", "loose4"]
    names += ["loose_low", "counts", "pre", "grad_pre", "line", "wide2", "wide2f", "line4", "line1"]
    names += ["low"] * 4 + ["low"] * 7 + ["first"] * 7
    scalar_sum, grads_b, pos_b, grad_filters_b = edge_call(
        scalar_kernel,
        atoms,
        (scalars, rows, w_key_filter, w_value_filter[0], scalar_parts),
        (radial, geo),
        [
            ((R, atoms), BF16),
            ((3 * R, atoms), BF16),
            ((8, atoms), F32),
            ((LANES, 2 * LANES), F32),
        ],
        [],
        [kinds[name] for name in names],
    )
    gathered = lax.all_gather(scalar_sum, "feat", axis=0, tiled=True)

    inputs = (
        scalars, features, vectors, cot_features, cot_vectors, gathered, w_vector, w_output,
    )
    new_features, delta, squares, send_vec, flat_early = pl.pallas_call(
        functools.partial(layer_kernel, atoms),
        out_shape=[
            jax.ShapeDtypeStruct((R, atoms), BF16),
            jax.ShapeDtypeStruct((3, R, atoms), F32),
            jax.ShapeDtypeStruct((8, atoms), F32),
            jax.ShapeDtypeStruct((split, 3 * R, atoms), BF16),
            jax.ShapeDtypeStruct((6 * R, H), BF16),
        ],
        in_specs=[whole(pltpu.SMEM)] + [whole()] * (len(inputs) - 1),
        out_specs=[whole()] * 5,
        scratch_shapes=[
            pltpu.VMEM((H, 3 * R), BF16),
            pltpu.VMEM((3 * R, H), BF16),
            pltpu.VMEM((3 * R, H), BF16),
            pltpu.VMEM((3 * R, H), F32),
            pltpu.VMEM((3 * R, H), F32),
        ],
        compiler_params=params(),
    )(*inputs)
    share = 6 * R // count
    got_vec = lax.all_to_all(send_vec, "feat", 0, 0)
    shares_early = lax.all_to_all(flat_early.reshape(count, share, H), "atoms", 0, 0)

    names = ["weights", "picks", "many", "near", "near_last", "stage8", "loose5"]
    names += ["counts", "pre", "grad_pre", "line", "line3"]
    names += ["low"] * 7 + ["low"] * 10 + ["first"] * 10
    rows, _ = lax.optimization_barrier((rows, squares))
    sums, back, grads_a, pos_a, grad_filters_a = edge_call(
        vector_kernel,
        atoms,
        (scalars, rows, w_value_filter[1], w_value_filter[2]),
        (radial, geo),
        [
            ((3, R, atoms), F32),
            ((3, R, atoms), F32),
            ((2 * R, atoms), BF16),
            ((8, atoms), F32),
            ((LANES, 2 * LANES), F32),
        ],
        [],
        [kinds[name] for name in names],
    )

    delta, got_vec, shares_early = lax.optimization_barrier((delta, got_vec, shares_early))
    inputs = (
        scalars, features, stat, vectors, delta, squares, sums, grads_b, grads_a, pos_a, pos_b,
        mask, gain, bias, w_query, w_key, w_value, grad_filters_a, grad_filters_b,
    )
    new_vectors, send, flat_late = pl.pallas_call(
        functools.partial(normal_kernel, atoms),
        out_shape=[
            jax.ShapeDtypeStruct((3, R, atoms), BF16),
            jax.ShapeDtypeStruct((split, R + EXTRAS, atoms), BF16),
            jax.ShapeDtypeStruct((6 * R, H), BF16),
        ],
        in_specs=[whole(pltpu.SMEM)] + [whole()] * (len(inputs) - 1),
        out_specs=[whole()] * 3,
        scratch_shapes=[pltpu.VMEM((H, 5 * R), BF16), pltpu.VMEM((5 * R, H), F32)],
        compiler_params=params(),
    )(*inputs)
    got = lax.all_to_all(send, "feat", 0, 0)
    shares_late = lax.all_to_all(flat_late.reshape(count, share, H), "atoms", 0, 0)

    inputs = (
        scalars, got, got_vec, features, stat, gain, cot_features, cot_vectors, back, mask,
    )
    grad_features, grad_vectors, grad_positions, small = pl.pallas_call(
        functools.partial(final_kernel, atoms),
        out_shape=[
            jax.ShapeDtypeStruct((R, atoms), F32),
            jax.ShapeDtypeStruct((3, R, atoms), F32),
            jax.ShapeDtypeStruct((3, atoms), F32),
            jax.ShapeDtypeStruct((16, H), F32),
        ],
        in_specs=[whole(pltpu.SMEM)] + [whole()] * (len(inputs) - 1),
        out_specs=[whole()] * 4,
        compiler_params=params(),
    )(*inputs)
    summed = [jnp.sum(x.astype(F32), axis=0) for x in (shares_early, shares_late)]
    mine = jnp.concatenate(summed + [small], axis=0).astype(BF16)
    every = everywhere(mine, "atoms")
    shapes = [
        (1, R), (1, R), (R, H), (R, H), (3, R, H), (3, R, H), (3, R, H), (R, R), (3, R, R), (1, 8),
    ]
    grads = pl.pallas_call(
        functools.partial(unpack_kernel, share),
        out_shape=[jax.ShapeDtypeStruct(shape, F32) for shape in shapes],
        in_specs=[whole()],
        out_specs=[whole()] * len(shapes),
        compiler_params=params(),
    )(every)
    return (
        new_features,
        new_vectors,
        grad_features,
        grad_vectors,
        grad_positions,
        grads[0].reshape(R),
        grads[1].reshape(R),
        grads[2].T,
        grads[3].T,
        jnp.swapaxes(grads[4], 1, 2),
        jnp.swapaxes(grads[5], 1, 2),
        jnp.swapaxes(grads[6], 1, 2),
        grads[7],
        grads[8],
        grads[9][0, :4],
    )


def solution(mesh):
    in_specs = (
        P(None, "atoms"),
        P(None, None, "atoms"),
        P(None, "atoms"),
        P("atoms"),
        P(None, "atoms"),
        P(),
        P(),
        P(None, "feat"),
        P(None, "feat"),
        P(None, None, "feat"),
        P(None, None, "feat"),
        P(None, None, "feat"),
        P(None, "feat"),
        P(None, None, "feat"),
        P("feat", "atoms"),
        P(None, "feat", "atoms"),
    )
    out_specs = (
        P("feat", "atoms"),
        P(None, "feat", "atoms"),
        P("feat", "atoms"),
        P(None, "feat", "atoms"),
        P(None, "atoms"),
        P("feat"),
        P("feat"),
        P(None, "feat"),
        P(None, "feat"),
        P(None, None, "feat"),
        P(None, None, "feat"),
        P(None, None, "feat"),
        P(None, "feat"),
        P(None, None, "feat"),
        P(),
    )
    return jax.shard_map(
        per_device, mesh=mesh, in_specs=in_specs, out_specs=out_specs, check_vma=False
    )
```

```python
import functools
import math

import jax
import jax.numpy as jnp
from jax import lax
from jax.experimental import pallas as pl
from jax.experimental.pallas import tpu as pltpu
from jax.sharding import PartitionSpec as P

H = 256
HEADS = 8
HEAD = H // HEADS
R = 64
MOL = 29
HALO = 32
CUTOFF = 5.0
EPSILON = 1e-05
F32 = jnp.float32
BF16 = jnp.bfloat16

LANE_GROUPS = 2
ROW_GROUPS = 3
SPAN = 5
OFFSETS = 14
STEPS = SPAN + OFFSETS
SUB = 16
LANES = 128

W01, W2V2, C01, C2_COUNT, POS, QK, V0_COUNT, V12, VEC01, VEC2 = range(10)
GROUP_ROWS = 352
LATE = 2 * R + R // 2
EXTRAS = 16


BLOCK = 8
WINDOW = 256


def block_list(molecules, rows):
    full, rest = divmod(molecules, BLOCK)
    wide = ROW_GROUPS * BLOCK
    out = [(n * wide, wide, BLOCK) for n in range(full)]
    if rows > full * wide:
        out.append((full * wide, rows - full * wide, rest))
    return out


def row_parts(shape, axis, size):
    row = lax.broadcasted_iota(jnp.int32, shape, axis)
    group = jnp.zeros(shape, jnp.int32)
    for g in range(1, ROW_GROUPS):
        group = jnp.where(row >= g * size, g, group)
    return group, row - group * size, row < ROW_GROUPS * size


def set_distances(target, width, size):
    for r in range(LANE_GROUPS):

        def step(t, _, r=r):
            group, molecule, held = row_parts((width, WINDOW), 0, size)
            spot = t + SPAN * (LANE_GROUPS * group + r)
            spot = jnp.where(spot >= MOL, spot - MOL, spot)
            lane = lax.broadcasted_iota(jnp.int32, (width, WINDOW), 1)
            value = jnp.where(held, molecule * MOL + spot - lane, -(10**6))
            target[r, pl.ds(t * width, width), :] = value
            return 0

        lax.fori_loop(0, STEPS, step, 0)


def windows(blocks, distances, start, tall):
    for n, (first, width, size) in enumerate(blocks):
        atom = start + n * BLOCK * MOL
        base = jnp.minimum(atom // SUB * SUB, tall - WINDOW)
        base = pl.multiple_of(base, SUB)
        chosen = distances[0] if size == BLOCK else distances[1]
        ones = [jnp.where(chosen[r] == base - atom, 1.0, 0.0).astype(BF16) for r in (0, 1)]
        yield first, width, pl.ds(base, WINDOW), ones


def spread(source, lanes, stage, blocks, distances, start):
    for first, width, here, ones in windows(blocks, distances, start, source.shape[0]):
        given = source[here, lanes]
        a, b = dot(ones[0], given), dot(ones[1], given)
        low = lax.broadcasted_iota(jnp.int32, (a.shape[0], LANES), 1) < R
        for n in range(a.shape[1] // LANES):
            left, right = a[:, n * LANES : (n + 1) * LANES], b[:, n * LANES : (n + 1) * LANES]
            one = jnp.where(low, left, pltpu.roll(right, R, 1))
            two = jnp.where(low, pltpu.roll(left, R, 1), right)
            stage[2 * n, :, first : first + width] = one.reshape(STEPS, width, LANES)
            stage[2 * n + 1, :, first : first + width] = two.reshape(STEPS, width, LANES)


def spread_positions(source, lanes, targets, blocks, distances, start):
    row = lax.broadcasted_iota(jnp.int32, (LANES, 3 * LANES), 0)
    lane = lax.broadcasted_iota(jnp.int32, (LANES, 3 * LANES), 1)
    axis = jnp.where(lane >= 2 * LANES, 2, jnp.where(lane >= LANES, 1, 0))
    mine = (row >= 3 * axis) & (row < 3 * axis + 3)
    low = lane - axis * LANES < R
    wide = [jnp.where(mine & (low == (r == 0)), 1.0, 0.0).astype(BF16) for r in (0, 1)]
    for first, width, here, ones in windows(blocks, distances, start, source.shape[0]):
        given = source[here, lanes]
        total = 0.0
        for r in (0, 1):
            total = total + dot(dot(ones[r], given).astype(BF16), wide[r])
        for d, target in enumerate(targets):
            value = total[:, d * LANES : (d + 1) * LANES]
            target[:, first : first + width] = value.reshape(STEPS, width, LANES)


def collect(sources, target, blocks, distances, start):
    target[...] = jnp.zeros(target.shape, F32)
    units = []
    for first, width, here, ones in windows(blocks, distances, start, target.shape[0]):
        units.append((first, width, here, ones))
    at = 0
    while at < len(units):
        group = units[at : at + 2] if units[at][0] % SUB == 0 and at + 1 < len(units) else None
        if group is None or (group[0][1] + group[1][1]) % SUB:
            group = units[at : at + 1]
        at += len(group)
        first = group[0][0]
        size = sum(g[1] for g in group)
        blocks_in = []
        for partner, carry in sources:
            value = partner[:, first : first + size].astype(F32)
            start_part = value[:SPAN] + carry[:, first : first + size]
            blocks_in.append(jnp.concatenate([start_part, value[SPAN:]], axis=0))
        for f, width, here, ones in group:
            parts = ([], [])
            for n in range(0, len(sources), 2):
                a = blocks_in[n][:, f - first : f - first + width].reshape(STEPS * width, LANES)
                b = blocks_in[n + 1][:, f - first : f - first + width]
                b = b.reshape(STEPS * width, LANES)
                low = lax.broadcasted_iota(jnp.int32, a.shape, 1) < R
                parts[0].append(jnp.where(low, a, pltpu.roll(b, R, 1)).astype(BF16))
                parts[1].append(jnp.where(low, pltpu.roll(a, R, 1), b).astype(BF16))
            total = 0.0
            for r in (0, 1):
                total = total + dot_tn(ones[r], jnp.concatenate(parts[r], axis=1))
            target[here, :] = target[here, :] + total


def row_masks(owned, start, blocks, atoms):
    for n, (at, width, size) in enumerate(blocks):
        _, molecule, _ = row_parts((width, LANES), 0, size)
        first = start - HALO + (n * BLOCK + molecule) * MOL
        owned[at : at + width] = jnp.where((first >= 0) & (first < atoms), 1.0, 0.0)


def set_picks(picks):
    row = lax.broadcasted_iota(jnp.int32, (LANES, LANES), 0)
    lane = lax.broadcasted_iota(jnp.int32, (LANES, LANES), 1)
    base = jnp.where(lane >= R, R, 0)
    for n in range(2 * OFFSETS):
        which = 1 + n if n < OFFSETS else 33 + n - OFFSETS
        block = jnp.where(row == base + which, 1.0, 0.0).astype(BF16)
        picks[:, n * LANES : (n + 1) * LANES] = block


def set_multiplicities(count, target, blocks, rows):
    lane = lax.broadcasted_iota(jnp.int32, (rows, LANES), 1)
    inner = jnp.where(lane >= R, lane - R, lane)
    last = []
    for _, width, size in blocks:
        last.append(row_parts((width, LANES), 0, size)[0])
    doubled = (jnp.concatenate(last, axis=0) == ROW_GROUPS - 1) & (lane >= R)
    for t in range(SPAN):
        value = jnp.where(inner < 32, count[t], 0.0)
        for k in range(1, OFFSETS + 1):
            value = jnp.where(inner == 32 + k, count[t + k], value)
        if t == SPAN - 1:
            value = jnp.where(doubled, 0.0, value)
        target[t] = value.astype(BF16)


def dot(a, b):
    return jnp.dot(a, b, preferred_element_type=F32)


def dot_tn(a, b):
    return lax.dot_general(a, b, (((0,), (0,)), ((), ())), preferred_element_type=F32)


def dot_nt(a, b):
    return lax.dot_general(a, b, (((1,), (1,)), ((), ())), preferred_element_type=F32)


COSINE = (0.9999999998, -0.04934802137, 0.000405870916, -1.335212003e-06, 2.349373138e-09, -2.43963243e-12)

GEO_ENVELOPE, GEO_SLOPE, GEO_BEND, GEO_OWN, GEO_WAY, GEO_INVERSE, GEO_FREE = 0, 1, 2, 3, 4, 7, 8
GEO = 9


def geometry(pos, t, rows, owned, radial, geo):
    lane = lax.broadcasted_iota(jnp.int32, (1, LANES), 1)
    centre = jnp.where(lane >= R, lane - R, lane).astype(F32)
    inv_space = (R - 1) / CUTOFF

    def step(k, _):
        for o, size in halves(rows):
            here = pl.ds(pl.multiple_of(k * rows + o, SUB), size)
            off = [p[t, o : o + size] - p[t + 1 + k, o : o + size] for p in pos]
            mine = owned[o : o + size]
            square = off[0] * off[0] + off[1] * off[1] + off[2] * off[2]
            clamped = jnp.maximum(square, 0.01)
            inverse = lax.rsqrt(clamped)
            c = COSINE[-1]
            for term in COSINE[-2::-1]:
                c = c * clamped + term
            c = jnp.where(clamped < CUTOFF * CUTOFF, c, 0.0)
            envelope = c * c
            y = jnp.maximum(envelope - envelope * envelope, 1e-30)
            free = jnp.where(square > 0.01, 1.0, 0.0)
            bend = ((-math.pi / CUTOFF) * free) * (y * lax.rsqrt(y))
            u = (clamped * inverse) * inv_space - centre
            bump = jnp.exp(-0.5 * (u * u))
            value = bump * envelope
            high = value.astype(BF16)
            slope = bump * bend - (inv_space * free) * (u * value)
            radial[here, :LANES] = high
            radial[here, LANES:] = (value - high.astype(F32)).astype(BF16)
            geo[GEO_OWN, here, :] = (value * mine).astype(BF16)
            geo[GEO_SLOPE, here, :] = slope.astype(BF16)
            geo[GEO_BEND, here, :] = bend.astype(BF16)
            geo[GEO_ENVELOPE, here, :] = envelope.astype(BF16)
            for d in range(3):
                geo[GEO_WAY + d, here, :] = (off[d] * inverse).astype(BF16)
            geo[GEO_INVERSE, here, :] = inverse.astype(BF16)
            geo[GEO_FREE, here, :] = (inverse * free).astype(BF16)
        return 0

    lax.fori_loop(0, OFFSETS, step, 0)


def halves(rows):
    tiles = rows // SUB
    first = (tiles + 1) // 2 * SUB
    return ((0, first), (first, rows - first))


def set_filters(weights_ref, filter_1, filter_2):
    weights_ref[...] = jnp.zeros(weights_ref.shape, BF16)
    for f, ref in enumerate((filter_1, filter_2)):
        half = ref[...] * jnp.asarray(0.5, BF16)
        for part in range(2):
            for g in range(LANE_GROUPS):
                down = part * LANES + g * R
                at = f * LANES + g * R
                weights_ref[down : down + R, at : at + R] = half


def gate(h):
    t = jnp.tanh(h)
    u = 1.0 + t
    f = h * u
    return f.astype(BF16), (u + f * (1.0 - t)).astype(BF16)


def carried(rows, t, totals, group, body):
    def outer(s, _):
        o = pl.multiple_of(s * SUB, SUB)
        block = pl.ds(o, SUB)
        ii = (t, block)
        sums = None
        for k in range(0, OFFSETS, group):
            loaded = []
            for n in range(k, k + group):
                here = pl.ds(o + n * rows, SUB)
                loaded.append(body(o, here, ii, (t + 1 + n, block), n))
            done = [f() for f in loaded]
            given = [one for one, _ in done]
            while len(given) > 1:
                left = given[len(given) // 2 * 2 :]
                pairs = zip(given[0::2], given[1::2])
                given = [[x + y for x, y in zip(a, b)] for a, b in pairs] + left
            total = [x.astype(F32) for x in given[0]]
            sums = total if sums is None else [x + y for x, y in zip(sums, total)]
            for _, stores in done:
                for ref, index, value in stores:
                    ref[index] = value
        for total, value in zip(totals, sums):
            total[ii] = value
        return 0

    lax.fori_loop(0, rows // SUB, outer, 0)


def lanes_of(n):
    return slice(n * LANES, (n + 1) * LANES)


def geometry_kernel(
    molecules, rows, atoms,
    scalars, rows_ref, radial_out, geo_out, owned, near, near_last, px, py, pz,
):
    t = pl.program_id(0)
    start = scalars[0]
    blocks = block_list(molecules, rows)
    distances = (near, near_last)

    @pl.when(t == 0)
    def _():
        row_masks(owned, start, blocks, atoms)
        set_distances(near, blocks[0][1], blocks[0][2])
        set_distances(near_last, blocks[-1][1], blocks[-1][2])
        lanes = slice(POS * LANES, (POS + 1) * LANES)
        spread_positions(rows_ref, lanes, (px, py, pz), blocks, distances, start)

    geometry((px, py, pz), t, rows, owned, radial_out.at[0], geo_out.at[0])


def vector_kernel(
    molecules, rows, atoms,
    scalars, rows_ref, filter_1, filter_2, radial_in, geo_in,
    sums_ref, back_ref, grads_ref, pos_out, grad_w_ref,
    weights_ref, picks, many, near, near_last, stage, loose, counts, pre, grad_pre,
    grad_radial, grad_ways,
    w0, w1, w2, v2, c0, c1, c2,
    s0, s1, s2, a0, a1, a2, gv, gx, gy, gz,
    fs0, fs1, fs2, fa0, fa1, fa2, fgv, fgx, fgy, fgz,
):
    t = pl.program_id(0)
    start = scalars[0]
    own = slice(HALO, HALO + atoms)
    radial, geo = radial_in.at[0], geo_in.at[0]
    w, c, g_pos = (w0, w1, w2), (c0, c1, c2), (gx, gy, gz)
    sums, backs = (s0, s1, s2), (a0, a1, a2)
    blocks = block_list(molecules, rows)
    distances = (near, near_last)

    @pl.when(t == 0)
    def _():
        set_filters(weights_ref, filter_1, filter_2)
        set_picks(picks)
        set_distances(near, blocks[0][1], blocks[0][2])
        set_distances(near_last, blocks[-1][1], blocks[-1][2])
        lanes = slice(W01 * LANES, (C2_COUNT + 1) * LANES)
        spread(rows_ref, lanes, stage, blocks, distances, start)
        for n, target in enumerate((w0, w1, w2, v2, c0, c1, c2)):
            target[...] = stage[n].astype(BF16)
        set_multiplicities(stage.at[7], many, blocks, rows)
        for total in (s0, s1, s2, a0, a1, a2, gv, gx, gy, gz):
            total[...] = jnp.zeros(total.shape, BF16)
        grad_w_ref[...] = jnp.zeros(grad_w_ref.shape, F32)

    counts[...] = dot(many[t], picks[...])
    pre[...] = dot(radial[...], weights_ref[...])

    def channel(o, here, ii, jj, k):
        h1, h2 = pre[here, :LANES], pre[here, LANES:]
        mi = counts[pl.ds(o, SUB), lanes_of(k)]
        mj = counts[pl.ds(o, SUB), lanes_of(OFFSETS + k)]
        v2i, v2j = v2[ii], v2[jj]
        ways = [geo[GEO_WAY + d, here, :] for d in range(3)]
        wi, wj = [w[d][ii] for d in range(3)], [w[d][jj] for d in range(3)]
        ci, cj = [c[d][ii] for d in range(3)], [c[d][jj] for d in range(3)]
        old_sums = [sums[d][jj] for d in range(3)]
        old_backs = [backs[d][jj] for d in range(3)]
        old_gv = gv[jj]

        def compute():
            f1, d1 = gate(h1)
            f2, d2 = gate(h2)
            ni, nj = mi.astype(BF16), mj.astype(BF16)
            f1i, f1j, f2i, f2j = f1 * ni, f1 * nj, f2 * ni, f2 * nj
            msg_i, msg_j = f2i * v2j, f2j * v2i
            stores, sum_i, back_i = [], [], []
            along_i = along_j = across_i = across_j = None
            for d in range(3):
                way = ways[d]
                sum_i.append(f1i * wj[d] + msg_i * way)
                stores.append((sums[d], jj, old_sums[d] + (f1j * wi[d] - msg_j * way)))
                stores.append((backs[d], jj, old_backs[d] + f1i * ci[d]))
                back_i.append(f1j * cj[d])
                grad = ci[d] * msg_i - cj[d] * msg_j
                stores.append((grad_ways, (d, here, slice(None)), grad))
                new = (ci[d] * way, cj[d] * way, ci[d] * wj[d], cj[d] * wi[d])
                if d == 0:
                    along_i, along_j, across_i, across_j = new
                else:
                    along_i, along_j = along_i + new[0], along_j + new[1]
                    across_i, across_j = across_i + new[2], across_j + new[3]
            stores.append((gv, jj, old_gv + f2i * along_i))
            g1 = ni * across_i + nj * across_j
            g2 = ni * along_i * v2j - nj * along_j * v2i
            stores.append((grad_pre, (here, slice(0, LANES)), g1 * d1))
            stores.append((grad_pre, (here, slice(LANES, None)), g2 * d2))
            return sum_i + back_i + [-(f2j * along_j)], stores

        return compute

    carried(rows, t, (fs0, fs1, fs2, fa0, fa1, fa2, fgv), 2, channel)
    grad_radial[...] = dot_nt(grad_pre[...], weights_ref[:LANES])
    grad_w_ref[...] = grad_w_ref[...] + dot_tn(geo[GEO_OWN], grad_pre[...])

    def turn(o, here, ii, jj, k):
        ways = [geo[GEO_WAY + d, here, :] for d in range(3)]
        grads = [grad_ways[d, here, :] for d in range(3)]
        grad, slope = grad_radial[here, :], geo[GEO_SLOPE, here, :]
        inverse, free = geo[GEO_INVERSE, here, :], geo[GEO_FREE, here, :]
        old = [g[jj] for g in g_pos]

        def compute():
            along = ways[0] * grads[0] + ways[1] * grads[1] + ways[2] * grads[2]
            pull = grad.astype(BF16) * slope - free * along
            out = [grads[d] * inverse + ways[d] * pull for d in range(3)]
            return out, [(g_pos[d], jj, old[d] - out[d]) for d in range(3)]

        return compute

    carried(rows, t, (fgx, fgy, fgz), 7, turn)

    @pl.when(t == SPAN - 1)
    def _():
        low = lax.broadcasted_iota(jnp.int32, (atoms, LANES), 1) < R
        totals = (s0, s1, s2, gv, a0, a1, a2, gx, gy, gz)
        firsts = (fs0, fs1, fs2, fgv, fa0, fa1, fa2, fgx, fgy, fgz)
        collect(tuple(zip(totals, firsts)), loose, blocks, distances, start)
        both = loose[own, :LANES].T
        sums_ref[0] = both[:R]
        sums_ref[1] = both[R:]
        both = loose[own, LANES : 2 * LANES].T
        sums_ref[2] = both[:R]
        grads_ref[R:] = both[R:].astype(BF16)

        def kept(n):
            return rows_ref[own, n * LANES : (n + 1) * LANES].astype(F32)

        v12 = kept(V12)
        v11 = jnp.where(low, v12, pltpu.roll(v12, R, 1))
        back = loose[own, 2 * LANES : 3 * LANES]
        both = (back * v11).T
        back_ref[0] = both[:R]
        back_ref[1] = both[R:]
        partial = back * kept(VEC01)
        partial = partial + pltpu.roll(partial, R, 1)
        back = loose[own, 3 * LANES : 4 * LANES]
        back_ref[2] = (back * v11).T[:R]
        partial = partial + back * kept(VEC2)
        grads_ref[:R] = partial.T[:R].astype(BF16)
        pos_out[...] = jnp.zeros(pos_out.shape, F32)
        pos_out[0:1] = jnp.sum(back.T[R:], axis=0, keepdims=True)
        both = loose[own, 4 * LANES :].T
        pos_out[1:2] = jnp.sum(both[:R], axis=0, keepdims=True)
        pos_out[2:3] = jnp.sum(both[R:], axis=0, keepdims=True)


def scalar_kernel(
    molecules, rows, atoms,
    scalars, rows_ref, filter_1, filter_2, scalar_parts, radial_in, geo_in,
    sum_ref, grads_ref, pos_out, grad_w_ref,
    weights_ref, picks, many, heads_ref, near, near_last, stage, loose, loose_low, counts, pre,
    grad_pre, grad_radial, products, sums, gates, bends,
    q, key, v0, gs,
    ss, gq, gk, g0, gx, gy, gz,
    fss, fgq, fgk, fg0, fgx, fgy, fgz,
):
    t = pl.program_id(0)
    start = scalars[0]
    own = slice(HALO, HALO + atoms)
    radial, geo = radial_in.at[0], geo_in.at[0]
    g_pos = (gx, gy, gz)
    blocks = block_list(molecules, rows)
    distances = (near, near_last)

    @pl.when(t == 0)
    def _():
        set_filters(weights_ref, filter_1, filter_2)
        set_picks(picks)
        row = lax.broadcasted_iota(jnp.int32, (2 * LANES, 2 * LANES), 0)
        lane = lax.broadcasted_iota(jnp.int32, (2 * LANES, 2 * LANES), 1)
        heads_ref[...] = jnp.where(row // HEAD == lane // HEAD, 1.0, 0.0).astype(BF16)
        set_distances(near, blocks[0][1], blocks[0][2])
        set_distances(near_last, blocks[-1][1], blocks[-1][2])
        lanes = slice(QK * LANES, (V0_COUNT + 1) * LANES)
        spread(rows_ref, lanes, stage, blocks, distances, start)
        for n, target in enumerate((q, key, v0)):
            target[...] = stage[n].astype(BF16)
        set_multiplicities(stage.at[3], many, blocks, rows)
        summed = scalar_parts[0].astype(F32)
        for f in range(1, scalar_parts.shape[0]):
            summed = summed + scalar_parts[f].astype(F32)
        summed = jnp.concatenate([summed, jnp.zeros_like(summed)], axis=0).T.astype(BF16)
        loose_low[own] = summed[:atoms]
        loose_low[:HALO] = summed[atoms : atoms + HALO]
        loose_low[HALO + atoms : 2 * HALO + atoms] = summed[atoms + HALO : atoms + 2 * HALO]
        end = 2 * HALO + atoms
        loose_low[end:] = jnp.zeros((loose_low.shape[0] - end, LANES), BF16)
        spread(loose_low, slice(None), stage, blocks, distances, start)
        gs[...] = stage[0].astype(BF16)
        for total in (ss, gq, gk, g0, gx, gy, gz):
            total[...] = jnp.zeros(total.shape, BF16)
        grad_w_ref[...] = jnp.zeros(grad_w_ref.shape, F32)

    counts[...] = dot(many[t], picks[...])
    pre[...] = dot(radial[...], weights_ref[...])

    def multiply(k, _):
        for o, size in halves(rows):
            here = pl.ds(pl.multiple_of(k * rows + o, SUB), size)
            ii, jj = (t, slice(o, o + size)), (t + 1 + k, slice(o, o + size))
            fk, dk = gate(pre[here, :LANES])
            f0, d0 = gate(pre[here, LANES:])
            k_ij, k_ji = q[ii] * key[jj] * fk, q[jj] * key[ii] * fk
            s_ij, s_ji = gs[ii] * v0[jj] * f0, gs[jj] * v0[ii] * f0
            gates[0, here, :] = fk
            gates[1, here, :] = f0
            gates[2, here, :] = dk
            gates[3, here, :] = d0
            products[0, here, :LANES] = k_ij
            products[0, here, LANES:] = k_ji
            products[1, here, :LANES] = s_ij
            products[1, here, LANES:] = s_ji
        return 0

    lax.fori_loop(0, OFFSETS, multiply, 0)
    sums[0] = dot(products[0], heads_ref[...])
    sums[1] = dot(products[1], heads_ref[...])

    def channel(o, here, ii, jj, k):
        fk, f0, dk, d0 = [gates[n, here, :] for n in range(4)]
        envelope, bend = geo[GEO_ENVELOPE, here, :], geo[GEO_BEND, here, :]
        side_in = []
        for side in range(2):
            lanes = slice(side * LANES, (side + 1) * LANES)
            m = counts[pl.ds(o, SUB), lanes_of(side * OFFSETS + k)]
            h, o_ = (ii, jj) if side == 0 else (jj, ii)
            side_in.append(
                (m, sums[0, here, lanes], sums[1, here, lanes])
                + (q[h], key[o_], gs[h], v0[o_])
            )
        old = [ref[jj] for ref in (g0, gk, ss, gq)]

        def compute():
            gives, news = [], []
            for m, score, g_att, qh, kt, gh, vt in side_in:
                act, rise = gate(0.5 * score)
                m, g_att = m.astype(BF16), g_att.astype(BF16)
                weight = m * envelope
                att = act * weight
                g_score = g_att * (0.5 * rise) * weight
                lift = m * (g_att * act)
                bv, dv = f0 * att, fk * g_score
                gives.append((vt * bv, kt * dv, gh * bv, qh * dv))
                news.append((qh * kt * g_score, gh * vt * att, lift))
            one, two = gives
            new = [x + y for x, y in zip(*news)]
            stores = [
                (ref, jj, x + y)
                for ref, x, y in zip((g0, gk, ss, gq), old, (one[2], one[3], two[0], two[1]))
            ]
            stores.append((grad_pre, (here, slice(0, LANES)), new[0] * dk))
            stores.append((grad_pre, (here, slice(LANES, None)), new[1] * d0))
            stores.append((bends, (here, slice(None)), new[2] * bend * (1.0 / HEAD)))
            return [one[0], one[1], two[2], two[3]], stores

        return compute

    carried(rows, t, (fss, fgq, fg0, fgk), 2, channel)
    grad_radial[...] = dot_nt(grad_pre[...], weights_ref[:LANES])
    grad_w_ref[...] = grad_w_ref[...] + dot_tn(geo[GEO_OWN], grad_pre[...])

    def turn(o, here, ii, jj, k):
        ways = [geo[GEO_WAY + d, here, :] for d in range(3)]
        grad, slope, bend = grad_radial[here, :], geo[GEO_SLOPE, here, :], bends[here, :]
        old = [g[jj] for g in g_pos]

        def compute():
            pull = grad.astype(BF16) * slope + bend
            out = [way * pull for way in ways]
            return out, [(g_pos[d], jj, old[d] - out[d]) for d in range(3)]

        return compute

    carried(rows, t, (fgx, fgy, fgz), 7, turn)

    @pl.when(t == SPAN - 1)
    def _():
        totals = (ss, g0, gq, gk, gx, gy, gz, gz)
        firsts = (fss, fg0, fgq, fgk, fgx, fgy, fgz, fgz)
        collect(tuple(zip(totals, firsts)), loose, blocks, distances, start)
        both = loose[own, :LANES].T
        sum_ref[...] = both[:R].astype(BF16)
        grads_ref[2 * R :] = both[R:].astype(BF16)
        grads_ref[: 2 * R] = loose[own, LANES : 2 * LANES].T.astype(BF16)
        pos_out[...] = jnp.zeros(pos_out.shape, F32)
        both = loose[own, 2 * LANES : 3 * LANES].T
        pos_out[0:1] = jnp.sum(both[:R], axis=0, keepdims=True)
        pos_out[1:2] = jnp.sum(both[R:], axis=0, keepdims=True)
        both = loose[own, 3 * LANES :].T
        pos_out[2:3] = jnp.sum(both[:R], axis=0, keepdims=True)


def whole(memory=pltpu.VMEM):
    return pl.BlockSpec(memory_space=memory)


def params(mib=60):
    return pltpu.CompilerParams(vmem_limit_bytes=mib * 1024 * 1024)


def edge_sizes(atoms):
    molecules = (atoms + 2 * (MOL - 1)) // MOL
    full, rest = divmod(molecules, BLOCK)
    rows = full * ROW_GROUPS * BLOCK + -(-ROW_GROUPS * rest // BLOCK) * BLOCK
    rows = -(-rows // SUB) * SUB
    tall = -(-(HALO + molecules * MOL) // SUB) * SUB
    return molecules, rows, tall


def by_step(shape):
    zeros = (0,) * (len(shape) - 1)
    return pl.BlockSpec((1,) + shape[1:], lambda t: (t,) + zeros)


def fixed(shape):
    zeros = (0,) * len(shape)
    return pl.BlockSpec(shape, lambda t: zeros)


def edge_call(kernel, atoms, inputs, stepped_in, outs, stepped_out, scratch):
    molecules, rows, _ = edge_sizes(atoms)
    return pl.pallas_call(
        functools.partial(kernel, molecules, rows, atoms),
        grid=(SPAN,),
        out_shape=[jax.ShapeDtypeStruct(s, kind) for s, kind in outs + stepped_out],
        in_specs=[whole(pltpu.SMEM)]
        + [fixed(x.shape) for x in inputs[1:]]
        + [by_step(x.shape) for x in stepped_in],
        out_specs=[fixed(s) for s, _ in outs] + [by_step(s) for s, _ in stepped_out],
        scratch_shapes=[pltpu.VMEM(s, kind) for s, kind in scratch],
        compiler_params=params(),
        cost_estimate=pl.CostEstimate(
            flops=20 * 10**9, bytes_accessed=40 * 10**6, transcendentals=10**7
        ),
    )(*inputs, *stepped_in)


def shared_scratch(atoms):
    molecules, rows, tall = edge_sizes(atoms)
    batch = OFFSETS * rows
    blocks = block_list(molecules, rows)
    return {
        "weights": ((2 * LANES, 2 * LANES), BF16),
        "picks": ((LANES, 2 * OFFSETS * LANES), BF16),
        "many": ((SPAN, rows, LANES), BF16),
        "mask": ((rows, LANES), F32),
        "near": ((LANE_GROUPS, STEPS * blocks[0][1], WINDOW), jnp.int32),
        "near_last": ((LANE_GROUPS, STEPS * blocks[-1][1], WINDOW), jnp.int32),
        "stage8": ((8, STEPS, rows, LANES), F32),
        "stage4": ((4, STEPS, rows, LANES), F32),
        "loose5": ((tall, 5 * LANES), F32),
        "loose4": ((tall, 4 * LANES), F32),
        "loose_low": ((tall, LANES), BF16),
        "tall": ((STEPS, rows, LANES), F32),
        "low": ((STEPS, rows, LANES), BF16),
        "first": ((SPAN, rows, LANES), F32),
        "counts": ((rows, 2 * OFFSETS * LANES), F32),
        "pre": ((batch, 2 * LANES), F32),
        "grad_pre": ((batch, 2 * LANES), BF16),
        "line": ((batch, LANES), F32),
        "line2": ((2, batch, LANES), BF16),
        "line3": ((3, batch, LANES), BF16),
        "line4": ((4, batch, LANES), BF16),
        "line1": ((batch, LANES), BF16),
        "wide2": ((2, batch, 2 * LANES), BF16),
        "wide2f": ((2, batch, 2 * LANES), F32),
    }


def offsets_in_block(neighbours, mask, first):
    lane = lax.broadcasted_iota(jnp.int32, neighbours.shape, 1)
    diff = neighbours - (first + lane)
    return jnp.where(diff < 0, diff + MOL, diff) * mask


def pieces(x):
    a = x.astype(BF16)
    rest = x - a.astype(F32)
    b = rest.astype(BF16)
    return a, b, (rest - b.astype(F32)).astype(BF16)


def edge_groups(features, vectors, cot_f, cot_v, neighbours, mask, positions, first):
    diff = offsets_in_block(neighbours[...], mask[...], first).astype(F32).astype(BF16)
    groups = [jnp.concatenate([features[...], cot_f[...], diff], axis=0)]
    for d in range(3):
        rows = [x.astype(F32) for x in pieces(positions[d : d + 1])]
        rows = jnp.concatenate(rows + [jnp.zeros((29, LANES), F32)], axis=0).astype(BF16)
        groups.append(jnp.concatenate([vectors[d], cot_v[d], rows], axis=0))
    return groups


def halo_kernel(atoms, scalars, *refs):
    row_first = scalars[2]
    lane = lax.broadcasted_iota(jnp.int32, (GROUP_ROWS, LANES), 1)
    for end, at, out in ((0, atoms - LANES, refs[14]), (1, 0, refs[15])):
        groups = edge_groups(*refs[7 * end : 7 * end + 7], row_first + at)
        total = None
        for g, group in enumerate(groups):
            by = (HALO * (g + 1) if end == 0 else HALO * g) % LANES
            moved = group.astype(F32)
            moved = pltpu.roll(moved, by, 1) if by else moved
            total = moved if total is None else jnp.where(lane >= HALO * g, moved, total)
        out[...] = total.astype(BF16)


def halo_call(atoms, scalars, arrays):
    specs = []
    for at in (atoms // LANES - 1, 0):
        for x in arrays:
            shape = x.shape[:-1] + (LANES,)
            index = (0,) * (x.ndim - 1) + (at,)
            specs.append(pl.BlockSpec(shape, lambda *_, index=index: index))
    out = jax.ShapeDtypeStruct((GROUP_ROWS, LANES), BF16)
    return pl.pallas_call(
        functools.partial(halo_kernel, atoms),
        grid=(1,),
        out_shape=[out, out],
        in_specs=[whole(pltpu.SMEM)] + specs,
        out_specs=[whole(), whole()],
        compiler_params=params(),
    )(scalars, *arrays, *arrays)


def column(row):
    return jnp.broadcast_to(row, (8, row.shape[1])).T[:, :1]


def normalised(f):
    mean = jnp.mean(f, axis=0, keepdims=True)
    centred = f - mean
    inv = lax.rsqrt(jnp.mean(centred * centred, axis=0, keepdims=True) + EPSILON)
    return centred * inv, mean, inv


def dense_kernel(
    atoms,
    scalars, features, vectors, cot_f, cot_v, neighbours, mask, positions, low_ref, high_ref,
    gain_ref, bias_ref, w_query, w_key, w_value, w_vector, w_output,
    rows_ref, part_ref, stat_ref,
    w_qk, w_v0, w_v12, w_vec_t, w_out,
):
    chan_first = pl.multiple_of(scalars[1], R)
    row_first = scalars[2]
    gain, bias = column(gain_ref[...]), column(bias_ref[...])
    w_qk[:R] = w_query[...]
    w_qk[R:] = w_key[...]
    w_v0[:R] = w_value[0]
    w_v0[R:] = jnp.zeros((R, H), BF16)
    w_v12[:R] = w_value[1]
    w_v12[R:] = w_value[2]
    for p in range(3):
        w_vec_t[p * R : (p + 1) * R] = w_vector[p]
    w_out[...] = jnp.concatenate([w_output[p] for p in range(3)], axis=0).astype(F32).T.astype(BF16)

    def block(f, v, cf, cv, own_v, diff, pos):
        width = f.shape[1]
        normed, mean, inv = normalised(f)
        turned = (normed * gain + bias).T.astype(BF16)
        kinds = lax.broadcasted_iota(jnp.int32, (R, width), 0)
        kinds = jnp.where(kinds < 32, kinds, MOL + 32 - kinds).astype(F32)
        counts = jnp.zeros((R, width), F32)
        for s in range(diff.shape[0]):
            counts = counts + jnp.where(diff[s : s + 1] == kinds, 1.0, 0.0)
        none = jnp.zeros((R, width), F32)
        counts = jnp.concatenate([none, counts], axis=0).T
        low = lax.broadcasted_iota(jnp.int32, (width, LANES), 1) < R
        pairs = [None] * 10
        pairs[QK] = dot_nt(turned, w_qk[...])
        pairs[V0_COUNT] = dot_nt(turned, w_v0[...]) + counts
        v12 = dot_nt(turned, w_v12[...]).astype(BF16).astype(F32)
        v11 = jnp.where(low, v12, pltpu.roll(v12, R, 1))
        pairs[V12] = v12
        pairs[VEC01] = jnp.concatenate([own_v[0], own_v[1]], axis=0).T
        pairs[VEC2] = jnp.concatenate([own_v[2], none], axis=0).T
        pairs[W01] = pairs[VEC01] * v11
        pairs[W2V2] = jnp.where(low, pairs[VEC2] * v11, v12)
        pairs[C01] = jnp.concatenate([cv[0], cv[1]], axis=0).T
        pairs[C2_COUNT] = jnp.concatenate([cv[2], none], axis=0).T + counts
        pairs[POS] = jnp.concatenate([pos, jnp.zeros((LANES - 9, width), F32)], axis=0).T
        vec_dot = grad_0 = 0.0
        for d in range(3):
            proj = dot(w_vec_t[...], v[d])
            vec_dot = vec_dot + proj[:R] * proj[R : 2 * R]
            grad_0 = grad_0 + cv[d] * proj[2 * R :]
        grad_out = jnp.concatenate([grad_0, cf * vec_dot, cf], axis=0).astype(BF16)
        part = dot(w_out[...], grad_out)
        return [x.astype(BF16) for x in pairs], part.astype(BF16), mean, inv

    wide = 2 * LANES

    def step(b, _):
        at = pl.multiple_of(b * wide, wide)
        here = pl.ds(at, wide)
        own_v = [vectors[d, pl.ds(chan_first, R), here].astype(F32) for d in range(3)]
        diff = offsets_in_block(neighbours[:, here], mask[:, here], row_first + at)
        places = [p.astype(F32) for d in range(3) for p in pieces(positions[d : d + 1, here])]
        pairs, part, mean, inv = block(
            features[:, here].astype(F32),
            [vectors[d, :, here] for d in range(3)],
            cot_f[:, here].astype(F32),
            [cot_v[d, :, here].astype(F32) for d in range(3)],
            own_v,
            diff.astype(F32),
            jnp.concatenate(places, axis=0),
        )
        there = pl.ds(pl.multiple_of(HALO + at, 2 * SUB), wide)
        for n, pair in enumerate(pairs):
            rows_ref[there, n * LANES : (n + 1) * LANES] = pair
        part_ref[:, here] = part
        stat_ref[0:1, here] = mean
        stat_ref[1:2, here] = inv
        return 0

    lax.fori_loop(0, atoms // wide, step, 0)

    lane = lax.broadcasted_iota(jnp.int32, (GROUP_ROWS, LANES), 1)
    packed_low, packed_high = low_ref[...].astype(F32), high_ref[...].astype(F32)
    groups = []
    for g in range(4):
        a = pltpu.roll(packed_low, (LANES - HALO * g) % LANES, 1) if g else packed_low
        by = (LANES + HALO - HALO * g) % LANES
        b = pltpu.roll(packed_high, by, 1) if by else packed_high
        both = jnp.where(lane < HALO, a, jnp.where(lane < 2 * HALO, b, 0.0))
        groups.append(both)
    pick_rows = lax.broadcasted_iota(jnp.int32, (H, LANES), 0)
    own_v, pos = [], []
    for d in range(3):
        g = groups[1 + d]
        found = g[:R]
        for f in range(1, H // R):
            found = jnp.where(chan_first == f * R, g[f * R : (f + 1) * R], found)
        own_v.append(found)
        pos.append(g[320:323])
    pairs, part, _, _ = block(
        groups[0][:H],
        [groups[1 + d][:H].astype(BF16) for d in range(3)],
        groups[0][H : H + R],
        [groups[1 + d][H : H + R] for d in range(3)],
        own_v,
        groups[0][H + R :],
        jnp.concatenate(pos, axis=0),
    )
    high = HALO + atoms
    tall = rows_ref.shape[0]
    for n, pair in enumerate(pairs):
        lanes = slice(n * LANES, (n + 1) * LANES)
        rows_ref[:HALO, lanes] = pair[:HALO]
        rows_ref[high : high + HALO, lanes] = pair[HALO : 2 * HALO]
        rows_ref[high + HALO :, lanes] = jnp.zeros((tall - high - HALO, LANES), BF16)
    part_ref[:, atoms:] = part


def both_diagonals(grad, f):
    at = f * LANES
    return 0.5 * (grad[:R, at : at + R] + grad[R:, at + R : at + LANES])


def filter_block(grad):
    both = jnp.concatenate([both_diagonals(grad, 0), both_diagonals(grad, 1)], axis=1)
    return jnp.concatenate([both[: R // 2], both[R // 2 :]], axis=1)


def layer_kernel(
    atoms,
    scalars, features, stat, vectors, cot_f, cot_v, gathered, grads_b, gain_ref, bias_ref,
    w_vector, w_output, grad_filters_b,
    feat_out, delta_ref, square_ref, send_ref, flat_ref,
    w_vec, w_vec_t, w_out_t,
):
    chan_first = pl.multiple_of(scalars[1], R)
    gain, bias = column(gain_ref[...]), column(bias_ref[...])
    for p in range(3):
        w_vec_t[p * R : (p + 1) * R] = w_vector[p]
        w_out_t[p * R : (p + 1) * R] = w_output[p]
    w_vec[...] = w_vec_t[...].astype(F32).T.astype(BF16)
    t_vec, t_out, t_b = [flat_ref.at[n * 3 * R : (n + 1) * 3 * R] for n in range(3)]
    flat_ref[...] = jnp.zeros(flat_ref.shape, F32)
    wide = 2 * LANES
    split = send_ref.shape[0]

    def step(b, _):
        at = pl.multiple_of(b * wide, wide)
        here = pl.ds(at, wide)
        all_sums = gathered[:, here]
        outputs = dot(w_out_t[...], all_sums)
        out_0, out_1, out_2 = outputs[:R], outputs[R : 2 * R], outputs[2 * R :]
        cf = cot_f[:, here].astype(F32)
        grad_dot = cf * out_1
        vec_dot = grad_0 = 0.0
        for d in range(3):
            proj = dot(w_vec_t[...], vectors[d, :, here])
            first, second, third = proj[:R], proj[R : 2 * R], proj[2 * R :]
            cv = cot_v[d, :, here].astype(F32)
            vec_dot = vec_dot + first * second
            grad_0 = grad_0 + cv * third
            delta_ref[d, :, here] = third * out_0
            grad_proj = jnp.concatenate(
                [grad_dot * second, grad_dot * first, cv * out_0], axis=0
            ).astype(BF16)
            part = dot(w_vec[...], grad_proj).astype(BF16)
            for f in range(split):
                send_ref[f, d * R : (d + 1) * R, here] = part[f * R : (f + 1) * R]
            t_vec[...] = t_vec[...] + dot_nt(grad_proj, vectors[d, :, here])
        delta = vec_dot * out_1 + out_2
        moved = features[pl.ds(chan_first, R), here].astype(F32) + delta
        feat_out[:, here] = moved.astype(BF16)
        grad_out = jnp.concatenate([grad_0, cf * vec_dot, cf], axis=0).astype(BF16)
        t_out[...] = t_out[...] + dot_nt(grad_out, all_sums)
        square_ref[0:1, here] = jnp.sum(moved * moved, axis=0, keepdims=True)
        square_ref[1:2, here] = jnp.sum(delta * delta, axis=0, keepdims=True)
        normed = (features[:, here].astype(F32) - stat[0:1, here]) * stat[1:2, here]
        normal = (normed * gain + bias).astype(BF16)
        t_b[...] = t_b[...] + dot_nt(grads_b[:, here], normal)
        return 0

    lax.fori_loop(0, atoms // wide, step, 0)
    flat_ref[9 * R : 9 * R + R // 2] = filter_block(grad_filters_b[...])


def normal_kernel(
    atoms,
    scalars, features, stat, vectors, delta_ref, square_ref, sums_ref,
    grads_b, grads_a, pos_a, pos_b, mask, gain_ref, bias_ref,
    w_query, w_key, w_value, grad_filters_a,
    vec_out, send_ref, flat_ref,
    w_five, t_late,
):
    chan_first = pl.multiple_of(scalars[1], R)
    gain, bias = column(gain_ref[...]), column(bias_ref[...])
    five = [w_query[...], w_key[...]] + [w_value[p] for p in range(3)]
    w_five[...] = jnp.concatenate(five, axis=0).astype(F32).T.astype(BF16)
    t_late[...] = jnp.zeros(t_late.shape, F32)
    wide = 2 * LANES
    split = send_ref.shape[0]

    def step(b, _):
        at = pl.multiple_of(b * wide, wide)
        here = pl.ds(at, wide)
        real = mask[:, here].astype(F32)
        square_v = square_dv = 0.0
        for d in range(3):
            delta = delta_ref[d, :, here] + sums_ref[d, :, here]
            moved = vectors[d, pl.ds(chan_first, R), here].astype(F32) + delta
            vec_out[d, :, here] = moved.astype(BF16)
            square_v = square_v + moved * moved
            square_dv = square_dv + delta * delta
        normed = (features[:, here].astype(F32) - stat[0:1, here]) * stat[1:2, here]
        normal = (normed * gain + bias).astype(BF16)
        grads = jnp.concatenate([grads_b[:, here], grads_a[:, here]], axis=0)
        t_late[...] = t_late[...] + dot_nt(grads_a[:, here], normal)
        part = dot(w_five[...], grads)
        rounded = part.astype(BF16)
        for f in range(split):
            send_ref[f, :R, here] = rounded[f * R : (f + 1) * R]
        hat = part * gain
        tops = [
            jnp.sum(hat, axis=0, keepdims=True),
            jnp.sum(hat * normed, axis=0, keepdims=True),
        ]
        exact = [pos_a[d : d + 1, here] + pos_b[d : d + 1, here] for d in range(3)]
        exact += [square_ref[n : n + 1, here] * real for n in range(2)]
        for x in (square_v, square_dv):
            exact.append(jnp.sum(x, axis=0, keepdims=True) * real)
        heads = [x.astype(BF16).astype(F32) for x in exact]
        tops = tops + heads + [x - y for x, y in zip(exact, heads)]
        tops = jnp.concatenate(tops, axis=0).astype(BF16)
        for f in range(split):
            send_ref[f, R:, here] = tops
        return 0

    lax.fori_loop(0, atoms // wide, step, 0)
    flat_ref[: 2 * R] = t_late[...].astype(BF16)
    flat_ref[2 * R :] = filter_block(grad_filters_a[...]).astype(BF16)


def final_kernel(
    atoms,
    scalars, got, got_vec, features, stat, gain_ref, cot_f, cot_v, back_ref, mask,
    grad_feat, grad_vec, grad_pos, small_ref,
):
    chan_first = pl.multiple_of(scalars[1], R)
    whole_gain = column(gain_ref[...])
    gain = whole_gain[:R]
    for f in range(1, H // R):
        gain = jnp.where(chan_first == f * R, whole_gain[f * R : (f + 1) * R], gain)

    def summed(ref, rows):
        total = ref[0, rows].astype(F32)
        for f in range(1, ref.shape[0]):
            total = total + ref[f, rows].astype(F32)
        return total

    tops = summed(got, slice(R, R + EXTRAS))
    grad_normal = summed(got, slice(0, R))
    inv = stat[1:2]
    normed = (features[pl.ds(chan_first, R), :].astype(F32) - stat[0:1]) * inv
    inner = grad_normal * gain - tops[0:1] * (1.0 / H) - normed * (tops[1:2] * (1.0 / H))
    grad_feat[...] = cot_f[...].astype(F32) + inv * inner
    for d in range(3):
        part = summed(got_vec, slice(d * R, (d + 1) * R))
        grad_vec[d] = cot_v[d].astype(F32) + part + back_ref[d]
    exact = tops[2:9] + tops[9:16]
    grad_pos[...] = exact[:3]
    ones = jnp.ones((8, atoms), BF16)
    gains = dot_nt(ones, (grad_normal * normed).astype(BF16))
    biases = dot_nt(ones, grad_normal.astype(BF16))
    totals = jnp.sum(exact[3:7], axis=1, keepdims=True)
    real = jnp.sum(mask[...].astype(F32), axis=1, keepdims=True)
    numbers = jnp.concatenate([totals, real, jnp.zeros((3, 1), F32)], axis=0)
    small = jnp.concatenate([gains, biases, jnp.broadcast_to(numbers, (8, LANES))], axis=1)
    high = small.astype(BF16)
    small_ref[:8] = high.astype(F32)
    small_ref[8:] = small - high.astype(F32)


def unpack_kernel(
    share,
    got,
    g_gain, g_bias, g_query, g_key, g_value, g_vector, g_output, g_key_f, g_value_f, rms_ref,
):
    every = [got[n].astype(F32) for n in range(got.shape[0])]
    small = 0.0
    late = 0.0
    for x in every:
        small = small + x[share + LATE :]
        late = late + x[share : share + LATE]
    total = small[:8] + small[8:]
    g_gain[...] = total[0:1, :R]
    g_bias[...] = total[0:1, R : 2 * R]
    numbers = total[:, LANES : LANES + 1]
    size = jnp.where(lax.broadcasted_iota(jnp.int32, (8, 1), 0) < 2, 1.0, 3.0) * H
    rms = jnp.sqrt(numbers / (numbers[4:5] * size) + 1e-06)
    rms_ref[...] = jnp.broadcast_to(rms, (8, LANES)).T[:1, :8]
    g_value[1] = late[:R]
    g_value[2] = late[R : 2 * R]
    last = late[2 * R :]
    for p, at in ((1, 0), (2, R)):
        g_value_f[p, : R // 2] = last[:, at : at + R]
        g_value_f[p, R // 2 :] = last[:, LANES + at : LANES + at + R]
    early = [(g, p) for g in (g_vector, g_output) for p in range(3)]
    early += [(g_query, None), (g_key, None), (g_value, 0)]
    for n, x in enumerate(every):
        at = n * share
        while at < (n + 1) * share:
            m = at // R
            size = min((m + 1) * R, (n + 1) * share) - at
            value = x[at - n * share : at - n * share + size]
            first = at - m * R
            at += size
            if m < len(early):
                g, p = early[m]
                if p is None:
                    g[first : first + size] = value
                else:
                    g[p, first : first + size] = value
                continue
            if first >= R // 2:
                continue
            size = min(size, R // 2 - first)
            for h in (0, 1):
                rows = slice(first + h * R // 2, first + h * R // 2 + size)
                g_key_f[rows] = value[:size, h * LANES : h * LANES + R]
                g_value_f[0, rows] = value[:size, h * LANES + R : h * LANES + 2 * R]


def everywhere(x, axis):
    count = lax.axis_size(axis)
    return lax.all_to_all(jnp.broadcast_to(x[None], (count,) + x.shape), axis, 0, 0)


def per_device(
    features, vectors, positions, atom_mask, neighbours, ln_gain, ln_bias,
    w_query, w_key, w_value, w_vector, w_output, w_key_filter, w_value_filter,
    cot_features, cot_vectors,
):
    channels = w_query.shape[1]
    atoms = features.shape[1]
    count = lax.axis_size("atoms")
    split = lax.axis_size("feat")
    chan_first = lax.axis_index("feat") * channels
    row_first = lax.axis_index("atoms") * atoms
    start = HALO - lax.rem(row_first, MOL)
    scalars = jnp.stack([start, chan_first, row_first]).astype(jnp.int32)
    molecules, rows_each, tall = edge_sizes(atoms)
    w_query, w_key = w_query.T, w_key.T
    w_value, w_vector, w_output = [jnp.swapaxes(w, 1, 2) for w in (w_value, w_vector, w_output)]
    mask = atom_mask.reshape(1, atoms)
    gain, bias = ln_gain.reshape(1, H), ln_bias.reshape(1, H)

    ends = halo_call(
        atoms,
        scalars,
        (features, vectors, cot_features, cot_vectors, neighbours, mask, positions),
    )
    low = lax.ppermute(ends[0], "atoms", [(i, i + 1) for i in range(count - 1)])
    high = lax.ppermute(ends[1], "atoms", [(i + 1, i) for i in range(count - 1)])

    inputs = (
        scalars, features, vectors, cot_features, cot_vectors, neighbours, mask, positions,
        low, high, gain, bias, w_query, w_key, w_value, w_vector, w_output,
    )
    rows, part, stat = pl.pallas_call(
        functools.partial(dense_kernel, atoms),
        out_shape=[
            jax.ShapeDtypeStruct((tall, 10 * LANES), BF16),
            jax.ShapeDtypeStruct((H, atoms + LANES), BF16),
            jax.ShapeDtypeStruct((8, atoms), F32),
        ],
        in_specs=[whole(pltpu.SMEM)] + [whole()] * (len(inputs) - 1),
        out_specs=[whole()] * 3,
        scratch_shapes=[
            pltpu.VMEM((LANES, H), BF16),
            pltpu.VMEM((LANES, H), BF16),
            pltpu.VMEM((LANES, H), BF16),
            pltpu.VMEM((3 * R, H), BF16),
            pltpu.VMEM((H, 3 * R), BF16),
        ],
        compiler_params=params(),
    )(*inputs)
    scalar_parts = lax.all_to_all(part.reshape(split, channels, atoms + LANES), "feat", 0, 0)

    kinds = shared_scratch(atoms)
    batch = OFFSETS * rows_each
    names = ["mask", "near", "near_last"] + ["tall"] * 3
    radial, geo = edge_call(
        geometry_kernel,
        atoms,
        (scalars, rows),
        (),
        [],
        [((SPAN, batch, 2 * LANES), BF16), ((SPAN, GEO, batch, LANES), BF16)],
        [kinds[name] for name in names],
    )
    names = ["weights", "picks", "many", "weights", "near", "near_last", "stage4", "loose4"]
    names += ["loose_low", "counts", "pre", "grad_pre", "line", "wide2", "wide2f", "line4", "line1"]
    names += ["low"] * 4 + ["low"] * 7 + ["first"] * 7
    scalar_sum, grads_b, pos_b, grad_filters_b = edge_call(
        scalar_kernel,
        atoms,
        (scalars, rows, w_key_filter, w_value_filter[0], scalar_parts),
        (radial, geo),
        [
            ((R, atoms), BF16),
            ((3 * R, atoms), BF16),
            ((8, atoms), F32),
            ((LANES, 2 * LANES), F32),
        ],
        [],
        [kinds[name] for name in names],
    )
    gathered = lax.all_gather(scalar_sum, "feat", axis=0, tiled=True)

    inputs = (
        scalars, features, stat, vectors, cot_features, cot_vectors, gathered, grads_b,
        gain, bias, w_vector, w_output, grad_filters_b,
    )
    new_features, delta, squares, send_vec, flat_early = pl.pallas_call(
        functools.partial(layer_kernel, atoms),
        out_shape=[
            jax.ShapeDtypeStruct((R, atoms), BF16),
            jax.ShapeDtypeStruct((3, R, atoms), F32),
            jax.ShapeDtypeStruct((8, atoms), F32),
            jax.ShapeDtypeStruct((split, 3 * R, atoms), BF16),
            jax.ShapeDtypeStruct((10 * R, H), F32),
        ],
        in_specs=[whole(pltpu.SMEM)] + [whole()] * (len(inputs) - 1),
        out_specs=[whole()] * 5,
        scratch_shapes=[
            pltpu.VMEM((H, 3 * R), BF16),
            pltpu.VMEM((3 * R, H), BF16),
            pltpu.VMEM((3 * R, H), BF16),
        ],
        compiler_params=params(),
    )(*inputs)
    share = 10 * R // count
    got_vec = lax.all_to_all(send_vec, "feat", 0, 0)
    shares_early = lax.psum_scatter(flat_early, "atoms", scatter_dimension=0, tiled=True)

    names = ["weights", "picks", "many", "near", "near_last", "stage8", "loose5"]
    names += ["counts", "pre", "grad_pre", "line", "line3"]
    names += ["low"] * 7 + ["low"] * 10 + ["first"] * 10
    rows, _ = lax.optimization_barrier((rows, squares))
    sums, back, grads_a, pos_a, grad_filters_a = edge_call(
        vector_kernel,
        atoms,
        (scalars, rows, w_value_filter[1], w_value_filter[2]),
        (radial, geo),
        [
            ((3, R, atoms), F32),
            ((3, R, atoms), F32),
            ((2 * R, atoms), BF16),
            ((8, atoms), F32),
            ((LANES, 2 * LANES), F32),
        ],
        [],
        [kinds[name] for name in names],
    )

    delta, got_vec, shares_early = lax.optimization_barrier((delta, got_vec, shares_early))
    inputs = (
        scalars, features, stat, vectors, delta, squares, sums, grads_b, grads_a, pos_a, pos_b,
        mask, gain, bias, w_query, w_key, w_value, grad_filters_a,
    )
    new_vectors, send, flat_late = pl.pallas_call(
        functools.partial(normal_kernel, atoms),
        out_shape=[
            jax.ShapeDtypeStruct((3, R, atoms), BF16),
            jax.ShapeDtypeStruct((split, R + EXTRAS, atoms), BF16),
            jax.ShapeDtypeStruct((LATE, H), BF16),
        ],
        in_specs=[whole(pltpu.SMEM)] + [whole()] * (len(inputs) - 1),
        out_specs=[whole()] * 3,
        scratch_shapes=[pltpu.VMEM((H, 5 * R), BF16), pltpu.VMEM((2 * R, H), F32)],
        compiler_params=params(),
    )(*inputs)
    got = lax.all_to_all(send, "feat", 0, 0)

    inputs = (
        scalars, got, got_vec, features, stat, gain, cot_features, cot_vectors, back, mask,
    )
    grad_features, grad_vectors, grad_positions, small = pl.pallas_call(
        functools.partial(final_kernel, atoms),
        out_shape=[
            jax.ShapeDtypeStruct((R, atoms), F32),
            jax.ShapeDtypeStruct((3, R, atoms), F32),
            jax.ShapeDtypeStruct((3, atoms), F32),
            jax.ShapeDtypeStruct((16, H), F32),
        ],
        in_specs=[whole(pltpu.SMEM)] + [whole()] * (len(inputs) - 1),
        out_specs=[whole()] * 4,
        compiler_params=params(),
    )(*inputs)
    mine = jnp.concatenate([shares_early.astype(BF16), flat_late, small.astype(BF16)], axis=0)
    every = everywhere(mine, "atoms")
    shapes = [
        (1, R), (1, R), (R, H), (R, H), (3, R, H), (3, R, H), (3, R, H), (R, R), (3, R, R), (1, 8),
    ]
    grads = pl.pallas_call(
        functools.partial(unpack_kernel, share),
        out_shape=[jax.ShapeDtypeStruct(shape, F32) for shape in shapes],
        in_specs=[whole()],
        out_specs=[whole()] * len(shapes),
        compiler_params=params(),
    )(every)
    return (
        new_features,
        new_vectors,
        grad_features,
        grad_vectors,
        grad_positions,
        grads[0].reshape(R),
        grads[1].reshape(R),
        grads[2].T,
        grads[3].T,
        jnp.swapaxes(grads[4], 1, 2),
        jnp.swapaxes(grads[5], 1, 2),
        jnp.swapaxes(grads[6], 1, 2),
        grads[7],
        grads[8],
        grads[9][0, :4],
    )


def solution(mesh):
    in_specs = (
        P(None, "atoms"),
        P(None, None, "atoms"),
        P(None, "atoms"),
        P("atoms"),
        P(None, "atoms"),
        P(),
        P(),
        P(None, "feat"),
        P(None, "feat"),
        P(None, None, "feat"),
        P(None, None, "feat"),
        P(None, None, "feat"),
        P(None, "feat"),
        P(None, None, "feat"),
        P("feat", "atoms"),
        P(None, "feat", "atoms"),
    )
    out_specs = (
        P("feat", "atoms"),
        P(None, "feat", "atoms"),
        P("feat", "atoms"),
        P(None, "feat", "atoms"),
        P(None, "atoms"),
        P("feat"),
        P("feat"),
        P(None, "feat"),
        P(None, "feat"),
        P(None, None, "feat"),
        P(None, None, "feat"),
        P(None, None, "feat"),
        P(None, "feat"),
        P(None, None, "feat"),
        P(),
    )
    return jax.shard_map(
        per_device, mesh=mesh, in_specs=in_specs, out_specs=out_specs, check_vma=False
    )
```

```python
import functools
import math

import jax
import jax.numpy as jnp
from jax import lax
from jax.experimental import pallas as pl
from jax.experimental.pallas import tpu as pltpu
from jax.sharding import PartitionSpec as P

H = 256
HEADS = 8
HEAD = H // HEADS
R = 64
MOL = 29
HALO = 32
CUTOFF = 5.0
EPSILON = 1e-05
F32 = jnp.float32
BF16 = jnp.bfloat16

LANE_GROUPS = 2
ROW_GROUPS = 3
SPAN = 5
OFFSETS = 14
STEPS = SPAN + OFFSETS
SUB = 16
LANES = 128

W01, W2V2, C01, C2_COUNT, POS, QK, V0_COUNT, V12, VEC01, VEC2 = range(10)
GROUP_ROWS = 352
LATE = 2 * R + R // 2
EXTRAS = 16


BLOCK = 8
WINDOW = 256


def block_list(molecules, rows):
    full, rest = divmod(molecules, BLOCK)
    wide = ROW_GROUPS * BLOCK
    out = [(n * wide, wide, BLOCK) for n in range(full)]
    if rows > full * wide:
        out.append((full * wide, rows - full * wide, rest))
    return out


def row_parts(shape, axis, size):
    row = lax.broadcasted_iota(jnp.int32, shape, axis)
    group = jnp.zeros(shape, jnp.int32)
    for g in range(1, ROW_GROUPS):
        group = jnp.where(row >= g * size, g, group)
    return group, row - group * size, row < ROW_GROUPS * size


def set_distances(target, width, size):
    for r in range(LANE_GROUPS):

        def step(t, _, r=r):
            group, molecule, held = row_parts((width, WINDOW), 0, size)
            spot = t + SPAN * (LANE_GROUPS * group + r)
            spot = jnp.where(spot >= MOL, spot - MOL, spot)
            lane = lax.broadcasted_iota(jnp.int32, (width, WINDOW), 1)
            value = jnp.where(held, molecule * MOL + spot - lane, -(10**6))
            target[r, pl.ds(t * width, width), :] = value
            return 0

        lax.fori_loop(0, STEPS, step, 0)


def windows(blocks, distances, start, tall):
    for n, (first, width, size) in enumerate(blocks):
        atom = start + n * BLOCK * MOL
        base = jnp.minimum(atom // SUB * SUB, tall - WINDOW)
        base = pl.multiple_of(base, SUB)
        chosen = distances[0] if size == BLOCK else distances[1]
        ones = [jnp.where(chosen[r] == base - atom, 1.0, 0.0).astype(BF16) for r in (0, 1)]
        yield first, width, pl.ds(base, WINDOW), ones


def spread(source, lanes, stage, blocks, distances, start):
    for first, width, here, ones in windows(blocks, distances, start, source.shape[0]):
        given = source[here, lanes]
        a, b = dot(ones[0], given), dot(ones[1], given)
        low = lax.broadcasted_iota(jnp.int32, (a.shape[0], LANES), 1) < R
        for n in range(a.shape[1] // LANES):
            left, right = a[:, n * LANES : (n + 1) * LANES], b[:, n * LANES : (n + 1) * LANES]
            one = jnp.where(low, left, pltpu.roll(right, R, 1))
            two = jnp.where(low, pltpu.roll(left, R, 1), right)
            stage[2 * n, :, first : first + width] = one.reshape(STEPS, width, LANES)
            stage[2 * n + 1, :, first : first + width] = two.reshape(STEPS, width, LANES)


def spread_positions(source, lanes, targets, blocks, distances, start):
    row = lax.broadcasted_iota(jnp.int32, (LANES, 3 * LANES), 0)
    lane = lax.broadcasted_iota(jnp.int32, (LANES, 3 * LANES), 1)
    axis = jnp.where(lane >= 2 * LANES, 2, jnp.where(lane >= LANES, 1, 0))
    mine = (row >= 3 * axis) & (row < 3 * axis + 3)
    low = lane - axis * LANES < R
    wide = [jnp.where(mine & (low == (r == 0)), 1.0, 0.0).astype(BF16) for r in (0, 1)]
    for first, width, here, ones in windows(blocks, distances, start, source.shape[0]):
        given = source[here, lanes]
        total = 0.0
        for r in (0, 1):
            total = total + dot(dot(ones[r], given).astype(BF16), wide[r])
        for d, target in enumerate(targets):
            value = total[:, d * LANES : (d + 1) * LANES]
            target[:, first : first + width] = value.reshape(STEPS, width, LANES)


def collect(sources, target, blocks, distances, start):
    target[...] = jnp.zeros(target.shape, F32)
    units = []
    for first, width, here, ones in windows(blocks, distances, start, target.shape[0]):
        units.append((first, width, here, ones))
    at = 0
    while at < len(units):
        group = units[at : at + 2] if units[at][0] % SUB == 0 and at + 1 < len(units) else None
        if group is None or (group[0][1] + group[1][1]) % SUB:
            group = units[at : at + 1]
        at += len(group)
        first = group[0][0]
        size = sum(g[1] for g in group)
        blocks_in = []
        for partner, carry in sources:
            value = partner[:, first : first + size].astype(F32)
            start_part = value[:SPAN] + carry[:, first : first + size]
            blocks_in.append(jnp.concatenate([start_part, value[SPAN:]], axis=0))
        for f, width, here, ones in group:
            parts = ([], [])
            for n in range(0, len(sources), 2):
                a = blocks_in[n][:, f - first : f - first + width].reshape(STEPS * width, LANES)
                b = blocks_in[n + 1][:, f - first : f - first + width]
                b = b.reshape(STEPS * width, LANES)
                low = lax.broadcasted_iota(jnp.int32, a.shape, 1) < R
                parts[0].append(jnp.where(low, a, pltpu.roll(b, R, 1)).astype(BF16))
                parts[1].append(jnp.where(low, pltpu.roll(a, R, 1), b).astype(BF16))
            total = 0.0
            for r in (0, 1):
                total = total + dot_tn(ones[r], jnp.concatenate(parts[r], axis=1))
            target[here, :] = target[here, :] + total


def row_masks(owned, start, blocks, atoms):
    for n, (at, width, size) in enumerate(blocks):
        _, molecule, _ = row_parts((width, LANES), 0, size)
        first = start - HALO + (n * BLOCK + molecule) * MOL
        owned[at : at + width] = jnp.where((first >= 0) & (first < atoms), 1.0, 0.0)


def set_picks(picks):
    row = lax.broadcasted_iota(jnp.int32, (LANES, LANES), 0)
    lane = lax.broadcasted_iota(jnp.int32, (LANES, LANES), 1)
    base = jnp.where(lane >= R, R, 0)
    for n in range(2 * OFFSETS):
        which = 1 + n if n < OFFSETS else 33 + n - OFFSETS
        block = jnp.where(row == base + which, 1.0, 0.0).astype(BF16)
        picks[:, n * LANES : (n + 1) * LANES] = block


def set_multiplicities(count, target, blocks, rows):
    lane = lax.broadcasted_iota(jnp.int32, (rows, LANES), 1)
    inner = jnp.where(lane >= R, lane - R, lane)
    last = []
    for _, width, size in blocks:
        last.append(row_parts((width, LANES), 0, size)[0])
    doubled = (jnp.concatenate(last, axis=0) == ROW_GROUPS - 1) & (lane >= R)
    for t in range(SPAN):
        value = jnp.where(inner < 32, count[t], 0.0)
        for k in range(1, OFFSETS + 1):
            value = jnp.where(inner == 32 + k, count[t + k], value)
        if t == SPAN - 1:
            value = jnp.where(doubled, 0.0, value)
        target[t] = value.astype(BF16)


def dot(a, b):
    return jnp.dot(a, b, preferred_element_type=F32)


def dot_tn(a, b):
    return lax.dot_general(a, b, (((0,), (0,)), ((), ())), preferred_element_type=F32)


def dot_nt(a, b):
    return lax.dot_general(a, b, (((1,), (1,)), ((), ())), preferred_element_type=F32)


COSINE = (0.9999999998, -0.04934802137, 0.000405870916, -1.335212003e-06, 2.349373138e-09, -2.43963243e-12)

GEO_ENVELOPE, GEO_SLOPE, GEO_BEND, GEO_OWN, GEO_WAY, GEO_INVERSE, GEO_FREE = 0, 1, 2, 3, 4, 7, 8
GEO = 9


def geometry(pos, t, rows, owned, radial, geo):
    lane = lax.broadcasted_iota(jnp.int32, (1, LANES), 1)
    centre = jnp.where(lane >= R, lane - R, lane).astype(F32)
    inv_space = (R - 1) / CUTOFF

    def step(k, _):
        for o, size in halves(rows):
            here = pl.ds(pl.multiple_of(k * rows + o, SUB), size)
            off = [p[t, o : o + size] - p[t + 1 + k, o : o + size] for p in pos]
            mine = owned[o : o + size]
            square = off[0] * off[0] + off[1] * off[1] + off[2] * off[2]
            clamped = jnp.maximum(square, 0.01)
            inverse = lax.rsqrt(clamped)
            c = COSINE[-1]
            for term in COSINE[-2::-1]:
                c = c * clamped + term
            c = jnp.where(clamped < CUTOFF * CUTOFF, c, 0.0)
            envelope = c * c
            y = jnp.maximum(envelope - envelope * envelope, 1e-30)
            free = jnp.where(square > 0.01, 1.0, 0.0)
            bend = ((-math.pi / CUTOFF) * free) * (y * lax.rsqrt(y))
            u = (clamped * inverse) * inv_space - centre
            bump = jnp.exp(-0.5 * (u * u))
            value = bump * envelope
            high = value.astype(BF16)
            slope = bump * bend - (inv_space * free) * (u * value)
            radial[here, :LANES] = high
            radial[here, LANES:] = (value - high.astype(F32)).astype(BF16)
            geo[GEO_OWN, here, :] = (value * mine).astype(BF16)
            geo[GEO_SLOPE, here, :] = slope.astype(BF16)
            geo[GEO_BEND, here, :] = bend.astype(BF16)
            geo[GEO_ENVELOPE, here, :] = envelope.astype(BF16)
            for d in range(3):
                geo[GEO_WAY + d, here, :] = (off[d] * inverse).astype(BF16)
            geo[GEO_INVERSE, here, :] = inverse.astype(BF16)
            geo[GEO_FREE, here, :] = (inverse * free).astype(BF16)
        return 0

    lax.fori_loop(0, OFFSETS, step, 0)


def halves(rows):
    tiles = rows // SUB
    first = (tiles + 1) // 2 * SUB
    return ((0, first), (first, rows - first))


def set_filters(weights_ref, filter_1, filter_2):
    weights_ref[...] = jnp.zeros(weights_ref.shape, BF16)
    for f, ref in enumerate((filter_1, filter_2)):
        half = ref[...] * jnp.asarray(0.5, BF16)
        for part in range(2):
            for g in range(LANE_GROUPS):
                down = part * LANES + g * R
                at = f * LANES + g * R
                weights_ref[down : down + R, at : at + R] = half


def gate(h):
    t = jnp.tanh(h)
    u = 1.0 + t
    f = h * u
    return f.astype(BF16), (u + f * (1.0 - t)).astype(BF16)


def carried(rows, t, totals, group, body):
    def outer(s, _):
        o = pl.multiple_of(s * SUB, SUB)
        block = pl.ds(o, SUB)
        ii = (t, block)
        sums = None
        for k in range(0, OFFSETS, group):
            loaded = []
            for n in range(k, k + group):
                here = pl.ds(o + n * rows, SUB)
                loaded.append(body(o, here, ii, (t + 1 + n, block), n))
            done = [f() for f in loaded]
            given = [one for one, _ in done]
            while len(given) > 1:
                left = given[len(given) // 2 * 2 :]
                pairs = zip(given[0::2], given[1::2])
                given = [[x + y for x, y in zip(a, b)] for a, b in pairs] + left
            total = [x.astype(F32) for x in given[0]]
            sums = total if sums is None else [x + y for x, y in zip(sums, total)]
            for _, stores in done:
                for ref, index, value in stores:
                    ref[index] = value
        for total, value in zip(totals, sums):
            total[ii] = value
        return 0

    lax.fori_loop(0, rows // SUB, outer, 0)


def lanes_of(n):
    return slice(n * LANES, (n + 1) * LANES)


def geometry_kernel(
    molecules, rows, atoms,
    scalars, rows_ref, radial_out, geo_out, owned, near, near_last, px, py, pz,
):
    t = pl.program_id(0)
    start = scalars[0]
    blocks = block_list(molecules, rows)
    distances = (near, near_last)

    @pl.when(t == 0)
    def _():
        row_masks(owned, start, blocks, atoms)
        set_distances(near, blocks[0][1], blocks[0][2])
        set_distances(near_last, blocks[-1][1], blocks[-1][2])
        lanes = slice(POS * LANES, (POS + 1) * LANES)
        spread_positions(rows_ref, lanes, (px, py, pz), blocks, distances, start)

    geometry((px, py, pz), t, rows, owned, radial_out.at[0], geo_out.at[0])


def vector_kernel(
    molecules, rows, atoms,
    scalars, rows_ref, filter_1, filter_2, radial_in, geo_in,
    sums_ref, back_ref, grads_ref, pos_out, grad_w_ref,
    weights_ref, picks, many, near, near_last, stage, loose, counts, pre, grad_pre,
    grad_radial, grad_ways,
    w0, w1, w2, v2, c0, c1, c2,
    s0, s1, s2, a0, a1, a2, gv, gx, gy, gz,
    fs0, fs1, fs2, fa0, fa1, fa2, fgv, fgx, fgy, fgz,
):
    t = pl.program_id(0)
    start = scalars[0]
    own = slice(HALO, HALO + atoms)
    radial, geo = radial_in.at[0], geo_in.at[0]
    w, c, g_pos = (w0, w1, w2), (c0, c1, c2), (gx, gy, gz)
    sums, backs = (s0, s1, s2), (a0, a1, a2)
    blocks = block_list(molecules, rows)
    distances = (near, near_last)

    @pl.when(t == 0)
    def _():
        set_filters(weights_ref, filter_1, filter_2)
        set_picks(picks)
        set_distances(near, blocks[0][1], blocks[0][2])
        set_distances(near_last, blocks[-1][1], blocks[-1][2])
        lanes = slice(W01 * LANES, (C2_COUNT + 1) * LANES)
        spread(rows_ref, lanes, stage, blocks, distances, start)
        for n, target in enumerate((w0, w1, w2, v2, c0, c1, c2)):
            target[...] = stage[n].astype(BF16)
        set_multiplicities(stage.at[7], many, blocks, rows)
        for total in (s0, s1, s2, a0, a1, a2, gv, gx, gy, gz):
            total[...] = jnp.zeros(total.shape, BF16)
        grad_w_ref[...] = jnp.zeros(grad_w_ref.shape, F32)

    counts[...] = dot(many[t], picks[...])
    pre[...] = dot(radial[...], weights_ref[...])

    def channel(o, here, ii, jj, k):
        h1, h2 = pre[here, :LANES], pre[here, LANES:]
        mi = counts[pl.ds(o, SUB), lanes_of(k)]
        mj = counts[pl.ds(o, SUB), lanes_of(OFFSETS + k)]
        v2i, v2j = v2[ii], v2[jj]
        ways = [geo[GEO_WAY + d, here, :] for d in range(3)]
        wi, wj = [w[d][ii] for d in range(3)], [w[d][jj] for d in range(3)]
        ci, cj = [c[d][ii] for d in range(3)], [c[d][jj] for d in range(3)]
        old_sums = [sums[d][jj] for d in range(3)]
        old_backs = [backs[d][jj] for d in range(3)]
        old_gv = gv[jj]

        def compute():
            f1, d1 = gate(h1)
            f2, d2 = gate(h2)
            ni, nj = mi.astype(BF16), mj.astype(BF16)
            f1i, f1j, f2i, f2j = f1 * ni, f1 * nj, f2 * ni, f2 * nj
            msg_i, msg_j = f2i * v2j, f2j * v2i
            stores, sum_i, back_i = [], [], []
            along_i = along_j = across_i = across_j = None
            for d in range(3):
                way = ways[d]
                sum_i.append(f1i * wj[d] + msg_i * way)
                stores.append((sums[d], jj, old_sums[d] + (f1j * wi[d] - msg_j * way)))
                stores.append((backs[d], jj, old_backs[d] + f1i * ci[d]))
                back_i.append(f1j * cj[d])
                grad = ci[d] * msg_i - cj[d] * msg_j
                stores.append((grad_ways, (d, here, slice(None)), grad))
                new = (ci[d] * way, cj[d] * way, ci[d] * wj[d], cj[d] * wi[d])
                if d == 0:
                    along_i, along_j, across_i, across_j = new
                else:
                    along_i, along_j = along_i + new[0], along_j + new[1]
                    across_i, across_j = across_i + new[2], across_j + new[3]
            stores.append((gv, jj, old_gv + f2i * along_i))
            g1 = ni * across_i + nj * across_j
            g2 = ni * along_i * v2j - nj * along_j * v2i
            stores.append((grad_pre, (here, slice(0, LANES)), g1 * d1))
            stores.append((grad_pre, (here, slice(LANES, None)), g2 * d2))
            return sum_i + back_i + [-(f2j * along_j)], stores

        return compute

    carried(rows, t, (fs0, fs1, fs2, fa0, fa1, fa2, fgv), 2, channel)
    grad_radial[...] = dot_nt(grad_pre[...], weights_ref[:LANES])
    grad_w_ref[...] = grad_w_ref[...] + dot_tn(geo[GEO_OWN], grad_pre[...])

    def turn(o, here, ii, jj, k):
        ways = [geo[GEO_WAY + d, here, :] for d in range(3)]
        grads = [grad_ways[d, here, :] for d in range(3)]
        grad, slope = grad_radial[here, :], geo[GEO_SLOPE, here, :]
        inverse, free = geo[GEO_INVERSE, here, :], geo[GEO_FREE, here, :]
        old = [g[jj] for g in g_pos]

        def compute():
            along = ways[0] * grads[0] + ways[1] * grads[1] + ways[2] * grads[2]
            pull = grad.astype(BF16) * slope - free * along
            out = [grads[d] * inverse + ways[d] * pull for d in range(3)]
            return out, [(g_pos[d], jj, old[d] - out[d]) for d in range(3)]

        return compute

    carried(rows, t, (fgx, fgy, fgz), 7, turn)

    @pl.when(t == SPAN - 1)
    def _():
        low = lax.broadcasted_iota(jnp.int32, (atoms, LANES), 1) < R
        totals = (s0, s1, s2, gv, a0, a1, a2, gx, gy, gz)
        firsts = (fs0, fs1, fs2, fgv, fa0, fa1, fa2, fgx, fgy, fgz)
        collect(tuple(zip(totals, firsts)), loose, blocks, distances, start)
        both = loose[own, :LANES].T
        sums_ref[0] = both[:R]
        sums_ref[1] = both[R:]
        both = loose[own, LANES : 2 * LANES].T
        sums_ref[2] = both[:R]
        grads_ref[R:] = both[R:].astype(BF16)

        def kept(n):
            return rows_ref[own, n * LANES : (n + 1) * LANES].astype(F32)

        v12 = kept(V12)
        v11 = jnp.where(low, v12, pltpu.roll(v12, R, 1))
        back = loose[own, 2 * LANES : 3 * LANES]
        both = (back * v11).T
        back_ref[0] = both[:R]
        back_ref[1] = both[R:]
        partial = back * kept(VEC01)
        partial = partial + pltpu.roll(partial, R, 1)
        back = loose[own, 3 * LANES : 4 * LANES]
        back_ref[2] = (back * v11).T[:R]
        partial = partial + back * kept(VEC2)
        grads_ref[:R] = partial.T[:R].astype(BF16)
        pos_out[...] = jnp.zeros(pos_out.shape, F32)
        pos_out[0:1] = jnp.sum(back.T[R:], axis=0, keepdims=True)
        both = loose[own, 4 * LANES :].T
        pos_out[1:2] = jnp.sum(both[:R], axis=0, keepdims=True)
        pos_out[2:3] = jnp.sum(both[R:], axis=0, keepdims=True)


def scalar_kernel(
    molecules, rows, atoms,
    scalars, rows_ref, filter_1, filter_2, scalar_parts, radial_in, geo_in,
    sum_ref, grads_ref, pos_out, grad_w_ref,
    weights_ref, picks, many, heads_ref, near, near_last, stage, loose, loose_low, counts, pre,
    grad_pre, grad_radial, products, sums, gates, bends,
    q, key, v0, gs,
    ss, gq, gk, g0, gx, gy, gz,
    fss, fgq, fgk, fg0, fgx, fgy, fgz,
):
    t = pl.program_id(0)
    start = scalars[0]
    own = slice(HALO, HALO + atoms)
    radial, geo = radial_in.at[0], geo_in.at[0]
    g_pos = (gx, gy, gz)
    blocks = block_list(molecules, rows)
    distances = (near, near_last)

    @pl.when(t == 0)
    def _():
        set_filters(weights_ref, filter_1, filter_2)
        set_picks(picks)
        row = lax.broadcasted_iota(jnp.int32, (2 * LANES, 2 * LANES), 0)
        lane = lax.broadcasted_iota(jnp.int32, (2 * LANES, 2 * LANES), 1)
        heads_ref[...] = jnp.where(row // HEAD == lane // HEAD, 1.0, 0.0).astype(BF16)
        set_distances(near, blocks[0][1], blocks[0][2])
        set_distances(near_last, blocks[-1][1], blocks[-1][2])
        lanes = slice(QK * LANES, (V0_COUNT + 1) * LANES)
        spread(rows_ref, lanes, stage, blocks, distances, start)
        for n, target in enumerate((q, key, v0)):
            target[...] = stage[n].astype(BF16)
        set_multiplicities(stage.at[3], many, blocks, rows)
        summed = scalar_parts[0].astype(F32)
        for f in range(1, scalar_parts.shape[0]):
            summed = summed + scalar_parts[f].astype(F32)
        summed = jnp.concatenate([summed, jnp.zeros_like(summed)], axis=0).T.astype(BF16)
        loose_low[own] = summed[:atoms]
        loose_low[:HALO] = summed[atoms : atoms + HALO]
        loose_low[HALO + atoms : 2 * HALO + atoms] = summed[atoms + HALO : atoms + 2 * HALO]
        end = 2 * HALO + atoms
        loose_low[end:] = jnp.zeros((loose_low.shape[0] - end, LANES), BF16)
        spread(loose_low, slice(None), stage, blocks, distances, start)
        gs[...] = stage[0].astype(BF16)
        for total in (ss, gq, gk, g0, gx, gy, gz):
            total[...] = jnp.zeros(total.shape, BF16)
        grad_w_ref[...] = jnp.zeros(grad_w_ref.shape, F32)

    counts[...] = dot(many[t], picks[...])
    pre[...] = dot(radial[...], weights_ref[...])

    def multiply(k, _):
        for o, size in halves(rows):
            here = pl.ds(pl.multiple_of(k * rows + o, SUB), size)
            ii, jj = (t, slice(o, o + size)), (t + 1 + k, slice(o, o + size))
            fk, dk = gate(pre[here, :LANES])
            f0, d0 = gate(pre[here, LANES:])
            k_ij, k_ji = q[ii] * key[jj] * fk, q[jj] * key[ii] * fk
            s_ij, s_ji = gs[ii] * v0[jj] * f0, gs[jj] * v0[ii] * f0
            gates[0, here, :] = fk
            gates[1, here, :] = f0
            gates[2, here, :] = dk
            gates[3, here, :] = d0
            products[0, here, :LANES] = k_ij
            products[0, here, LANES:] = k_ji
            products[1, here, :LANES] = s_ij
            products[1, here, LANES:] = s_ji
        return 0

    lax.fori_loop(0, OFFSETS, multiply, 0)
    sums[0] = dot(products[0], heads_ref[...])
    sums[1] = dot(products[1], heads_ref[...])

    def channel(o, here, ii, jj, k):
        fk, f0, dk, d0 = [gates[n, here, :] for n in range(4)]
        envelope, bend = geo[GEO_ENVELOPE, here, :], geo[GEO_BEND, here, :]
        side_in = []
        for side in range(2):
            lanes = slice(side * LANES, (side + 1) * LANES)
            m = counts[pl.ds(o, SUB), lanes_of(side * OFFSETS + k)]
            h, o_ = (ii, jj) if side == 0 else (jj, ii)
            side_in.append(
                (m, sums[0, here, lanes], sums[1, here, lanes])
                + (q[h], key[o_], gs[h], v0[o_])
            )
        old = [ref[jj] for ref in (g0, gk, ss, gq)]

        def compute():
            gives, news = [], []
            for m, score, g_att, qh, kt, gh, vt in side_in:
                act, rise = gate(0.5 * score)
                m, g_att = m.astype(BF16), g_att.astype(BF16)
                weight = m * envelope
                att = act * weight
                g_score = g_att * (0.5 * rise) * weight
                lift = m * (g_att * act)
                bv, dv = f0 * att, fk * g_score
                gives.append((vt * bv, kt * dv, gh * bv, qh * dv))
                news.append((qh * kt * g_score, gh * vt * att, lift))
            one, two = gives
            new = [x + y for x, y in zip(*news)]
            stores = [
                (ref, jj, x + y)
                for ref, x, y in zip((g0, gk, ss, gq), old, (one[2], one[3], two[0], two[1]))
            ]
            stores.append((grad_pre, (here, slice(0, LANES)), new[0] * dk))
            stores.append((grad_pre, (here, slice(LANES, None)), new[1] * d0))
            stores.append((bends, (here, slice(None)), new[2] * bend * (1.0 / HEAD)))
            return [one[0], one[1], two[2], two[3]], stores

        return compute

    carried(rows, t, (fss, fgq, fg0, fgk), 2, channel)
    grad_radial[...] = dot_nt(grad_pre[...], weights_ref[:LANES])
    grad_w_ref[...] = grad_w_ref[...] + dot_tn(geo[GEO_OWN], grad_pre[...])

    def turn(o, here, ii, jj, k):
        ways = [geo[GEO_WAY + d, here, :] for d in range(3)]
        grad, slope, bend = grad_radial[here, :], geo[GEO_SLOPE, here, :], bends[here, :]
        old = [g[jj] for g in g_pos]

        def compute():
            pull = grad.astype(BF16) * slope + bend
            out = [way * pull for way in ways]
            return out, [(g_pos[d], jj, old[d] - out[d]) for d in range(3)]

        return compute

    carried(rows, t, (fgx, fgy, fgz), 7, turn)

    @pl.when(t == SPAN - 1)
    def _():
        totals = (ss, g0, gq, gk, gx, gy, gz, gz)
        firsts = (fss, fg0, fgq, fgk, fgx, fgy, fgz, fgz)
        collect(tuple(zip(totals, firsts)), loose, blocks, distances, start)
        both = loose[own, :LANES].T
        sum_ref[...] = both[:R].astype(BF16)
        grads_ref[2 * R :] = both[R:].astype(BF16)
        grads_ref[: 2 * R] = loose[own, LANES : 2 * LANES].T.astype(BF16)
        pos_out[...] = jnp.zeros(pos_out.shape, F32)
        both = loose[own, 2 * LANES : 3 * LANES].T
        pos_out[0:1] = jnp.sum(both[:R], axis=0, keepdims=True)
        pos_out[1:2] = jnp.sum(both[R:], axis=0, keepdims=True)
        both = loose[own, 3 * LANES :].T
        pos_out[2:3] = jnp.sum(both[:R], axis=0, keepdims=True)


def whole(memory=pltpu.VMEM):
    return pl.BlockSpec(memory_space=memory)


def params(mib=60):
    return pltpu.CompilerParams(vmem_limit_bytes=mib * 1024 * 1024)


def edge_sizes(atoms):
    molecules = (atoms + 2 * (MOL - 1)) // MOL
    full, rest = divmod(molecules, BLOCK)
    rows = full * ROW_GROUPS * BLOCK + -(-ROW_GROUPS * rest // BLOCK) * BLOCK
    rows = -(-rows // SUB) * SUB
    tall = -(-(HALO + molecules * MOL) // SUB) * SUB
    return molecules, rows, tall


def by_step(shape):
    zeros = (0,) * (len(shape) - 1)
    return pl.BlockSpec((1,) + shape[1:], lambda t: (t,) + zeros)


def fixed(shape):
    zeros = (0,) * len(shape)
    return pl.BlockSpec(shape, lambda t: zeros)


def edge_call(kernel, atoms, inputs, stepped_in, outs, stepped_out, scratch):
    molecules, rows, _ = edge_sizes(atoms)
    return pl.pallas_call(
        functools.partial(kernel, molecules, rows, atoms),
        grid=(SPAN,),
        out_shape=[jax.ShapeDtypeStruct(s, kind) for s, kind in outs + stepped_out],
        in_specs=[whole(pltpu.SMEM)]
        + [fixed(x.shape) for x in inputs[1:]]
        + [by_step(x.shape) for x in stepped_in],
        out_specs=[fixed(s) for s, _ in outs] + [by_step(s) for s, _ in stepped_out],
        scratch_shapes=[pltpu.VMEM(s, kind) for s, kind in scratch],
        compiler_params=params(),
        cost_estimate=pl.CostEstimate(
            flops=20 * 10**9, bytes_accessed=40 * 10**6, transcendentals=10**7
        ),
    )(*inputs, *stepped_in)


def shared_scratch(atoms):
    molecules, rows, tall = edge_sizes(atoms)
    batch = OFFSETS * rows
    blocks = block_list(molecules, rows)
    return {
        "weights": ((2 * LANES, 2 * LANES), BF16),
        "picks": ((LANES, 2 * OFFSETS * LANES), BF16),
        "many": ((SPAN, rows, LANES), BF16),
        "mask": ((rows, LANES), F32),
        "near": ((LANE_GROUPS, STEPS * blocks[0][1], WINDOW), jnp.int32),
        "near_last": ((LANE_GROUPS, STEPS * blocks[-1][1], WINDOW), jnp.int32),
        "stage8": ((8, STEPS, rows, LANES), F32),
        "stage4": ((4, STEPS, rows, LANES), F32),
        "loose5": ((tall, 5 * LANES), F32),
        "loose4": ((tall, 4 * LANES), F32),
        "loose_low": ((tall, LANES), BF16),
        "tall": ((STEPS, rows, LANES), F32),
        "low": ((STEPS, rows, LANES), BF16),
        "first": ((SPAN, rows, LANES), F32),
        "counts": ((rows, 2 * OFFSETS * LANES), F32),
        "pre": ((batch, 2 * LANES), F32),
        "grad_pre": ((batch, 2 * LANES), BF16),
        "line": ((batch, LANES), F32),
        "line2": ((2, batch, LANES), BF16),
        "line3": ((3, batch, LANES), BF16),
        "line4": ((4, batch, LANES), BF16),
        "line1": ((batch, LANES), BF16),
        "wide2": ((2, batch, 2 * LANES), BF16),
        "wide2f": ((2, batch, 2 * LANES), F32),
    }


def offsets_in_block(neighbours, mask, first):
    lane = lax.broadcasted_iota(jnp.int32, neighbours.shape, 1)
    diff = neighbours - (first + lane)
    return jnp.where(diff < 0, diff + MOL, diff) * mask


def pieces(x):
    a = x.astype(BF16)
    rest = x - a.astype(F32)
    b = rest.astype(BF16)
    return a, b, (rest - b.astype(F32)).astype(BF16)


def edge_groups(features, vectors, cot_f, cot_v, neighbours, mask, positions, first):
    diff = offsets_in_block(neighbours[...], mask[...], first).astype(F32).astype(BF16)
    groups = [jnp.concatenate([features[...], cot_f[...], diff], axis=0)]
    for d in range(3):
        rows = [x.astype(F32) for x in pieces(positions[d : d + 1])]
        rows = jnp.concatenate(rows + [jnp.zeros((29, LANES), F32)], axis=0).astype(BF16)
        groups.append(jnp.concatenate([vectors[d], cot_v[d], rows], axis=0))
    return groups


def halo_kernel(atoms, scalars, *refs):
    row_first = scalars[2]
    lane = lax.broadcasted_iota(jnp.int32, (GROUP_ROWS, LANES), 1)
    for end, at, out in ((0, atoms - LANES, refs[14]), (1, 0, refs[15])):
        groups = edge_groups(*refs[7 * end : 7 * end + 7], row_first + at)
        total = None
        for g, group in enumerate(groups):
            by = (HALO * (g + 1) if end == 0 else HALO * g) % LANES
            moved = group.astype(F32)
            moved = pltpu.roll(moved, by, 1) if by else moved
            total = moved if total is None else jnp.where(lane >= HALO * g, moved, total)
        out[...] = total.astype(BF16)


def halo_call(atoms, scalars, arrays):
    specs = []
    for at in (atoms // LANES - 1, 0):
        for x in arrays:
            shape = x.shape[:-1] + (LANES,)
            index = (0,) * (x.ndim - 1) + (at,)
            specs.append(pl.BlockSpec(shape, lambda *_, index=index: index))
    out = jax.ShapeDtypeStruct((GROUP_ROWS, LANES), BF16)
    return pl.pallas_call(
        functools.partial(halo_kernel, atoms),
        grid=(1,),
        out_shape=[out, out],
        in_specs=[whole(pltpu.SMEM)] + specs,
        out_specs=[whole(), whole()],
        compiler_params=params(),
    )(scalars, *arrays, *arrays)


def column(row):
    return jnp.broadcast_to(row, (8, row.shape[1])).T[:, :1]


def normalised(f):
    mean = jnp.mean(f, axis=0, keepdims=True)
    centred = f - mean
    inv = lax.rsqrt(jnp.mean(centred * centred, axis=0, keepdims=True) + EPSILON)
    return centred * inv, mean, inv


def dense_kernel(
    atoms,
    scalars, features, vectors, cot_f, cot_v, neighbours, mask, positions, low_ref, high_ref,
    gain_ref, bias_ref, w_query, w_key, w_value, w_vector, w_output,
    rows_ref, part_ref, stat_ref,
    w_qk, w_v0, w_v12, w_vec_t, w_out,
):
    chan_first = pl.multiple_of(scalars[1], R)
    row_first = scalars[2]
    gain, bias = column(gain_ref[...]), column(bias_ref[...])
    w_qk[:R] = w_query[...]
    w_qk[R:] = w_key[...]
    w_v0[:R] = w_value[0]
    w_v0[R:] = jnp.zeros((R, H), BF16)
    w_v12[:R] = w_value[1]
    w_v12[R:] = w_value[2]
    for p in range(3):
        w_vec_t[p * R : (p + 1) * R] = w_vector[p]
    w_out[...] = jnp.concatenate([w_output[p] for p in range(3)], axis=0).astype(F32).T.astype(BF16)

    def block(f, v, cf, cv, own_v, diff, pos):
        width = f.shape[1]
        normed, mean, inv = normalised(f)
        turned = (normed * gain + bias).T.astype(BF16)
        kinds = lax.broadcasted_iota(jnp.int32, (R, width), 0)
        kinds = jnp.where(kinds < 32, kinds, MOL + 32 - kinds).astype(F32)
        counts = jnp.zeros((R, width), F32)
        for s in range(diff.shape[0]):
            counts = counts + jnp.where(diff[s : s + 1] == kinds, 1.0, 0.0)
        none = jnp.zeros((R, width), F32)
        counts = jnp.concatenate([none, counts], axis=0).T
        low = lax.broadcasted_iota(jnp.int32, (width, LANES), 1) < R
        pairs = [None] * 10
        pairs[QK] = dot_nt(turned, w_qk[...])
        pairs[V0_COUNT] = dot_nt(turned, w_v0[...]) + counts
        v12 = dot_nt(turned, w_v12[...]).astype(BF16).astype(F32)
        v11 = jnp.where(low, v12, pltpu.roll(v12, R, 1))
        pairs[V12] = v12
        pairs[VEC01] = jnp.concatenate([own_v[0], own_v[1]], axis=0).T
        pairs[VEC2] = jnp.concatenate([own_v[2], none], axis=0).T
        pairs[W01] = pairs[VEC01] * v11
        pairs[W2V2] = jnp.where(low, pairs[VEC2] * v11, v12)
        pairs[C01] = jnp.concatenate([cv[0], cv[1]], axis=0).T
        pairs[C2_COUNT] = jnp.concatenate([cv[2], none], axis=0).T + counts
        pairs[POS] = jnp.concatenate([pos, jnp.zeros((LANES - 9, width), F32)], axis=0).T
        vec_dot = grad_0 = 0.0
        for d in range(3):
            proj = dot(w_vec_t[...], v[d])
            vec_dot = vec_dot + proj[:R] * proj[R : 2 * R]
            grad_0 = grad_0 + cv[d] * proj[2 * R :]
        grad_out = jnp.concatenate([grad_0, cf * vec_dot, cf], axis=0).astype(BF16)
        part = dot(w_out[...], grad_out)
        return [x.astype(BF16) for x in pairs], part.astype(BF16), mean, inv

    wide = 2 * LANES

    def step(b, _):
        at = pl.multiple_of(b * wide, wide)
        here = pl.ds(at, wide)
        own_v = [vectors[d, pl.ds(chan_first, R), here].astype(F32) for d in range(3)]
        diff = offsets_in_block(neighbours[:, here], mask[:, here], row_first + at)
        places = [p.astype(F32) for d in range(3) for p in pieces(positions[d : d + 1, here])]
        pairs, part, mean, inv = block(
            features[:, here].astype(F32),
            [vectors[d, :, here] for d in range(3)],
            cot_f[:, here].astype(F32),
            [cot_v[d, :, here].astype(F32) for d in range(3)],
            own_v,
            diff.astype(F32),
            jnp.concatenate(places, axis=0),
        )
        there = pl.ds(pl.multiple_of(HALO + at, 2 * SUB), wide)
        for n, pair in enumerate(pairs):
            rows_ref[there, n * LANES : (n + 1) * LANES] = pair
        part_ref[:, here] = part
        stat_ref[0:1, here] = mean
        stat_ref[1:2, here] = inv
        return 0

    lax.fori_loop(0, atoms // wide, step, 0)

    lane = lax.broadcasted_iota(jnp.int32, (GROUP_ROWS, LANES), 1)
    packed_low, packed_high = low_ref[...].astype(F32), high_ref[...].astype(F32)
    groups = []
    for g in range(4):
        a = pltpu.roll(packed_low, (LANES - HALO * g) % LANES, 1) if g else packed_low
        by = (LANES + HALO - HALO * g) % LANES
        b = pltpu.roll(packed_high, by, 1) if by else packed_high
        both = jnp.where(lane < HALO, a, jnp.where(lane < 2 * HALO, b, 0.0))
        groups.append(both)
    pick_rows = lax.broadcasted_iota(jnp.int32, (H, LANES), 0)
    own_v, pos = [], []
    for d in range(3):
        g = groups[1 + d]
        found = g[:R]
        for f in range(1, H // R):
            found = jnp.where(chan_first == f * R, g[f * R : (f + 1) * R], found)
        own_v.append(found)
        pos.append(g[320:323])
    pairs, part, _, _ = block(
        groups[0][:H],
        [groups[1 + d][:H].astype(BF16) for d in range(3)],
        groups[0][H : H + R],
        [groups[1 + d][H : H + R] for d in range(3)],
        own_v,
        groups[0][H + R :],
        jnp.concatenate(pos, axis=0),
    )
    high = HALO + atoms
    tall = rows_ref.shape[0]
    for n, pair in enumerate(pairs):
        lanes = slice(n * LANES, (n + 1) * LANES)
        rows_ref[:HALO, lanes] = pair[:HALO]
        rows_ref[high : high + HALO, lanes] = pair[HALO : 2 * HALO]
        rows_ref[high + HALO :, lanes] = jnp.zeros((tall - high - HALO, LANES), BF16)
    part_ref[:, atoms:] = part


def both_diagonals(grad, f):
    at = f * LANES
    return 0.5 * (grad[:R, at : at + R] + grad[R:, at + R : at + LANES])


def filter_block(grad):
    both = jnp.concatenate([both_diagonals(grad, 0), both_diagonals(grad, 1)], axis=1)
    return jnp.concatenate([both[: R // 2], both[R // 2 :]], axis=1)


def layer_kernel(
    atoms,
    scalars, features, stat, vectors, cot_f, cot_v, gathered, grads_b, gain_ref, bias_ref,
    w_vector, w_output, grad_filters_b,
    feat_out, delta_ref, square_ref, send_ref, flat_ref,
    w_vec, w_vec_t, w_out_t,
):
    chan_first = pl.multiple_of(scalars[1], R)
    gain, bias = column(gain_ref[...]), column(bias_ref[...])
    for p in range(3):
        w_vec_t[p * R : (p + 1) * R] = w_vector[p]
        w_out_t[p * R : (p + 1) * R] = w_output[p]
    w_vec[...] = w_vec_t[...].astype(F32).T.astype(BF16)
    t_vec, t_out, t_b = [flat_ref.at[n * 3 * R : (n + 1) * 3 * R] for n in range(3)]
    flat_ref[...] = jnp.zeros(flat_ref.shape, F32)
    wide = 2 * LANES
    split = send_ref.shape[0]

    def step(b, _):
        at = pl.multiple_of(b * wide, wide)
        here = pl.ds(at, wide)
        all_sums = gathered[:, here]
        outputs = dot(w_out_t[...], all_sums)
        out_0, out_1, out_2 = outputs[:R], outputs[R : 2 * R], outputs[2 * R :]
        cf = cot_f[:, here].astype(F32)
        grad_dot = cf * out_1
        vec_dot = grad_0 = 0.0
        for d in range(3):
            proj = dot(w_vec_t[...], vectors[d, :, here])
            first, second, third = proj[:R], proj[R : 2 * R], proj[2 * R :]
            cv = cot_v[d, :, here].astype(F32)
            vec_dot = vec_dot + first * second
            grad_0 = grad_0 + cv * third
            delta_ref[d, :, here] = third * out_0
            grad_proj = jnp.concatenate(
                [grad_dot * second, grad_dot * first, cv * out_0], axis=0
            ).astype(BF16)
            part = dot(w_vec[...], grad_proj).astype(BF16)
            for f in range(split):
                send_ref[f, d * R : (d + 1) * R, here] = part[f * R : (f + 1) * R]
            t_vec[...] = t_vec[...] + dot_nt(grad_proj, vectors[d, :, here])
        delta = vec_dot * out_1 + out_2
        moved = features[pl.ds(chan_first, R), here].astype(F32) + delta
        feat_out[:, here] = moved.astype(BF16)
        grad_out = jnp.concatenate([grad_0, cf * vec_dot, cf], axis=0).astype(BF16)
        t_out[...] = t_out[...] + dot_nt(grad_out, all_sums)
        square_ref[0:1, here] = jnp.sum(moved * moved, axis=0, keepdims=True)
        square_ref[1:2, here] = jnp.sum(delta * delta, axis=0, keepdims=True)
        normed = (features[:, here].astype(F32) - stat[0:1, here]) * stat[1:2, here]
        normal = (normed * gain + bias).astype(BF16)
        t_b[...] = t_b[...] + dot_nt(grads_b[:, here], normal)
        return 0

    lax.fori_loop(0, atoms // wide, step, 0)
    flat_ref[9 * R : 9 * R + R // 2] = filter_block(grad_filters_b[...])


def normal_kernel(
    atoms,
    scalars, features, stat, vectors, delta_ref, square_ref, sums_ref,
    grads_b, grads_a, pos_a, pos_b, mask, gain_ref, bias_ref,
    w_query, w_key, w_value, grad_filters_a,
    vec_out, send_ref, flat_ref,
    w_five, t_late,
):
    chan_first = pl.multiple_of(scalars[1], R)
    gain, bias = column(gain_ref[...]), column(bias_ref[...])
    five = [w_query[...], w_key[...]] + [w_value[p] for p in range(3)]
    w_five[...] = jnp.concatenate(five, axis=0).astype(F32).T.astype(BF16)
    t_late[...] = jnp.zeros(t_late.shape, F32)
    wide = 2 * LANES
    split = send_ref.shape[0]

    def step(b, _):
        at = pl.multiple_of(b * wide, wide)
        here = pl.ds(at, wide)
        real = mask[:, here].astype(F32)
        square_v = square_dv = 0.0
        for d in range(3):
            delta = delta_ref[d, :, here] + sums_ref[d, :, here]
            moved = vectors[d, pl.ds(chan_first, R), here].astype(F32) + delta
            vec_out[d, :, here] = moved.astype(BF16)
            square_v = square_v + moved * moved
            square_dv = square_dv + delta * delta
        normed = (features[:, here].astype(F32) - stat[0:1, here]) * stat[1:2, here]
        normal = (normed * gain + bias).astype(BF16)
        grads = jnp.concatenate([grads_b[:, here], grads_a[:, here]], axis=0)
        t_late[...] = t_late[...] + dot_nt(grads_a[:, here], normal)
        part = dot(w_five[...], grads)
        rounded = part.astype(BF16)
        for f in range(split):
            send_ref[f, :R, here] = rounded[f * R : (f + 1) * R]
        hat = part * gain
        tops = [
            jnp.sum(hat, axis=0, keepdims=True),
            jnp.sum(hat * normed, axis=0, keepdims=True),
        ]
        exact = [pos_a[d : d + 1, here] + pos_b[d : d + 1, here] for d in range(3)]
        exact += [square_ref[n : n + 1, here] * real for n in range(2)]
        for x in (square_v, square_dv):
            exact.append(jnp.sum(x, axis=0, keepdims=True) * real)
        heads = [x.astype(BF16).astype(F32) for x in exact]
        tops = tops + heads + [x - y for x, y in zip(exact, heads)]
        tops = jnp.concatenate(tops, axis=0).astype(BF16)
        for f in range(split):
            send_ref[f, R:, here] = tops
        return 0

    lax.fori_loop(0, atoms // wide, step, 0)
    flat_ref[: 2 * R] = t_late[...].astype(BF16)
    flat_ref[2 * R :] = filter_block(grad_filters_a[...]).astype(BF16)


def final_kernel(
    atoms,
    scalars, got, got_vec, features, stat, gain_ref, cot_f, cot_v, back_ref, mask,
    grad_feat, grad_vec, grad_pos, small_ref,
):
    chan_first = pl.multiple_of(scalars[1], R)
    whole_gain = column(gain_ref[...])
    gain = whole_gain[:R]
    for f in range(1, H // R):
        gain = jnp.where(chan_first == f * R, whole_gain[f * R : (f + 1) * R], gain)

    def summed(ref, rows):
        total = ref[0, rows].astype(F32)
        for f in range(1, ref.shape[0]):
            total = total + ref[f, rows].astype(F32)
        return total

    tops = summed(got, slice(R, R + EXTRAS))
    grad_normal = summed(got, slice(0, R))
    inv = stat[1:2]
    normed = (features[pl.ds(chan_first, R), :].astype(F32) - stat[0:1]) * inv
    inner = grad_normal * gain - tops[0:1] * (1.0 / H) - normed * (tops[1:2] * (1.0 / H))
    grad_feat[...] = cot_f[...].astype(F32) + inv * inner
    for d in range(3):
        part = summed(got_vec, slice(d * R, (d + 1) * R))
        grad_vec[d] = cot_v[d].astype(F32) + part + back_ref[d]
    exact = tops[2:9] + tops[9:16]
    grad_pos[...] = exact[:3]
    ones = jnp.ones((8, atoms), BF16)
    gains = dot_nt(ones, (grad_normal * normed).astype(BF16))
    biases = dot_nt(ones, grad_normal.astype(BF16))
    totals = jnp.sum(exact[3:7], axis=1, keepdims=True)
    real = jnp.sum(mask[...].astype(F32), axis=1, keepdims=True)
    numbers = jnp.concatenate([totals, real, jnp.zeros((3, 1), F32)], axis=0)
    small = jnp.concatenate([gains, biases, jnp.broadcast_to(numbers, (8, LANES))], axis=1)
    high = small.astype(BF16)
    small_ref[:8] = high.astype(F32)
    small_ref[8:] = small - high.astype(F32)


def unpack_kernel(
    share,
    got,
    g_gain, g_bias, g_query, g_key, g_value, g_vector, g_output, g_key_f, g_value_f, rms_ref,
):
    every = [got[n].astype(F32) for n in range(got.shape[0])]
    small = 0.0
    late = 0.0
    for x in every:
        small = small + x[share + LATE :]
        late = late + x[share : share + LATE]
    total = small[:8] + small[8:]
    g_gain[...] = total[0:1, :R]
    g_bias[...] = total[0:1, R : 2 * R]
    numbers = total[:, LANES : LANES + 1]
    size = jnp.where(lax.broadcasted_iota(jnp.int32, (8, 1), 0) < 2, 1.0, 3.0) * H
    rms = jnp.sqrt(numbers / (numbers[4:5] * size) + 1e-06)
    rms_ref[...] = jnp.broadcast_to(rms, (8, LANES)).T[:1, :8]
    g_value[1] = late[:R]
    g_value[2] = late[R : 2 * R]
    last = late[2 * R :]
    for p, at in ((1, 0), (2, R)):
        g_value_f[p, : R // 2] = last[:, at : at + R]
        g_value_f[p, R // 2 :] = last[:, LANES + at : LANES + at + R]
    early = [(g, p) for g in (g_vector, g_output) for p in range(3)]
    early += [(g_query, None), (g_key, None), (g_value, 0)]
    for n, x in enumerate(every):
        at = n * share
        while at < (n + 1) * share:
            m = at // R
            size = min((m + 1) * R, (n + 1) * share) - at
            value = x[at - n * share : at - n * share + size]
            first = at - m * R
            at += size
            if m < len(early):
                g, p = early[m]
                if p is None:
                    g[first : first + size] = value
                else:
                    g[p, first : first + size] = value
                continue
            if first >= R // 2:
                continue
            size = min(size, R // 2 - first)
            for h in (0, 1):
                rows = slice(first + h * R // 2, first + h * R // 2 + size)
                g_key_f[rows] = value[:size, h * LANES : h * LANES + R]
                g_value_f[0, rows] = value[:size, h * LANES + R : h * LANES + 2 * R]


def everywhere(x, axis):
    count = lax.axis_size(axis)
    return lax.all_to_all(jnp.broadcast_to(x[None], (count,) + x.shape), axis, 0, 0)


def per_device(
    features, vectors, positions, atom_mask, neighbours, ln_gain, ln_bias,
    w_query, w_key, w_value, w_vector, w_output, w_key_filter, w_value_filter,
    cot_features, cot_vectors,
):
    channels = w_query.shape[1]
    atoms = features.shape[1]
    count = lax.axis_size("atoms")
    split = lax.axis_size("feat")
    chan_first = lax.axis_index("feat") * channels
    row_first = lax.axis_index("atoms") * atoms
    start = HALO - lax.rem(row_first, MOL)
    scalars = jnp.stack([start, chan_first, row_first]).astype(jnp.int32)
    molecules, rows_each, tall = edge_sizes(atoms)
    w_query, w_key = w_query.T, w_key.T
    w_value, w_vector, w_output = [jnp.swapaxes(w, 1, 2) for w in (w_value, w_vector, w_output)]
    mask = atom_mask.reshape(1, atoms)
    gain, bias = ln_gain.reshape(1, H), ln_bias.reshape(1, H)

    ends = halo_call(
        atoms,
        scalars,
        (features, vectors, cot_features, cot_vectors, neighbours, mask, positions),
    )
    low = lax.ppermute(ends[0], "atoms", [(i, i + 1) for i in range(count - 1)])
    high = lax.ppermute(ends[1], "atoms", [(i + 1, i) for i in range(count - 1)])

    inputs = (
        scalars, features, vectors, cot_features, cot_vectors, neighbours, mask, positions,
        low, high, gain, bias, w_query, w_key, w_value, w_vector, w_output,
    )
    rows, part, stat = pl.pallas_call(
        functools.partial(dense_kernel, atoms),
        out_shape=[
            jax.ShapeDtypeStruct((tall, 10 * LANES), BF16),
            jax.ShapeDtypeStruct((H, atoms + LANES), BF16),
            jax.ShapeDtypeStruct((8, atoms), F32),
        ],
        in_specs=[whole(pltpu.SMEM)] + [whole()] * (len(inputs) - 1),
        out_specs=[whole()] * 3,
        scratch_shapes=[
            pltpu.VMEM((LANES, H), BF16),
            pltpu.VMEM((LANES, H), BF16),
            pltpu.VMEM((LANES, H), BF16),
            pltpu.VMEM((3 * R, H), BF16),
            pltpu.VMEM((H, 3 * R), BF16),
        ],
        compiler_params=params(),
    )(*inputs)
    scalar_parts = lax.all_to_all(part.reshape(split, channels, atoms + LANES), "feat", 0, 0)

    kinds = shared_scratch(atoms)
    batch = OFFSETS * rows_each
    names = ["mask", "near", "near_last"] + ["tall"] * 3
    radial, geo = edge_call(
        geometry_kernel,
        atoms,
        (scalars, rows),
        (),
        [],
        [((SPAN, batch, 2 * LANES), BF16), ((SPAN, GEO, batch, LANES), BF16)],
        [kinds[name] for name in names],
    )
    names = ["weights", "picks", "many", "weights", "near", "near_last", "stage4", "loose4"]
    names += ["loose_low", "counts", "pre", "grad_pre", "line", "wide2", "wide2f", "line4", "line1"]
    names += ["low"] * 4 + ["low"] * 7 + ["first"] * 7
    scalar_sum, grads_b, pos_b, grad_filters_b = edge_call(
        scalar_kernel,
        atoms,
        (scalars, rows, w_key_filter, w_value_filter[0], scalar_parts),
        (radial, geo),
        [
            ((R, atoms), BF16),
            ((3 * R, atoms), BF16),
            ((8, atoms), F32),
            ((LANES, 2 * LANES), F32),
        ],
        [],
        [kinds[name] for name in names],
    )
    gathered = lax.all_gather(scalar_sum, "feat", axis=0, tiled=True)

    inputs = (
        scalars, features, stat, vectors, cot_features, cot_vectors, gathered, grads_b,
        gain, bias, w_vector, w_output, grad_filters_b,
    )
    new_features, delta, squares, send_vec, flat_early = pl.pallas_call(
        functools.partial(layer_kernel, atoms),
        out_shape=[
            jax.ShapeDtypeStruct((R, atoms), BF16),
            jax.ShapeDtypeStruct((3, R, atoms), F32),
            jax.ShapeDtypeStruct((8, atoms), F32),
            jax.ShapeDtypeStruct((split, 3 * R, atoms), BF16),
            jax.ShapeDtypeStruct((10 * R, H), F32),
        ],
        in_specs=[whole(pltpu.SMEM)] + [whole()] * (len(inputs) - 1),
        out_specs=[whole()] * 5,
        scratch_shapes=[
            pltpu.VMEM((H, 3 * R), BF16),
            pltpu.VMEM((3 * R, H), BF16),
            pltpu.VMEM((3 * R, H), BF16),
        ],
        compiler_params=params(),
    )(*inputs)
    share = 10 * R // count
    got_vec = lax.all_to_all(send_vec, "feat", 0, 0)
    shares_early = lax.psum_scatter(flat_early, "atoms", scatter_dimension=0, tiled=True)

    names = ["weights", "picks", "many", "near", "near_last", "stage8", "loose5"]
    names += ["counts", "pre", "grad_pre", "line", "line3"]
    names += ["low"] * 7 + ["low"] * 10 + ["first"] * 10
    rows, _ = lax.optimization_barrier((rows, squares))
    sums, back, grads_a, pos_a, grad_filters_a = edge_call(
        vector_kernel,
        atoms,
        (scalars, rows, w_value_filter[1], w_value_filter[2]),
        (radial, geo),
        [
            ((3, R, atoms), F32),
            ((3, R, atoms), F32),
            ((2 * R, atoms), BF16),
            ((8, atoms), F32),
            ((LANES, 2 * LANES), F32),
        ],
        [],
        [kinds[name] for name in names],
    )

    delta, got_vec = lax.optimization_barrier((delta, got_vec))
    inputs = (
        scalars, features, stat, vectors, delta, squares, sums, grads_b, grads_a, pos_a, pos_b,
        mask, gain, bias, w_query, w_key, w_value, grad_filters_a,
    )
    new_vectors, send, flat_late = pl.pallas_call(
        functools.partial(normal_kernel, atoms),
        out_shape=[
            jax.ShapeDtypeStruct((3, R, atoms), BF16),
            jax.ShapeDtypeStruct((split, R + EXTRAS, atoms), BF16),
            jax.ShapeDtypeStruct((LATE, H), BF16),
        ],
        in_specs=[whole(pltpu.SMEM)] + [whole()] * (len(inputs) - 1),
        out_specs=[whole()] * 3,
        scratch_shapes=[pltpu.VMEM((H, 5 * R), BF16), pltpu.VMEM((2 * R, H), F32)],
        compiler_params=params(),
    )(*inputs)
    got = lax.all_to_all(send, "feat", 0, 0)

    inputs = (
        scalars, got, got_vec, features, stat, gain, cot_features, cot_vectors, back, mask,
    )
    grad_features, grad_vectors, grad_positions, small = pl.pallas_call(
        functools.partial(final_kernel, atoms),
        out_shape=[
            jax.ShapeDtypeStruct((R, atoms), F32),
            jax.ShapeDtypeStruct((3, R, atoms), F32),
            jax.ShapeDtypeStruct((3, atoms), F32),
            jax.ShapeDtypeStruct((16, H), F32),
        ],
        in_specs=[whole(pltpu.SMEM)] + [whole()] * (len(inputs) - 1),
        out_specs=[whole()] * 4,
        compiler_params=params(),
    )(*inputs)
    mine = jnp.concatenate([shares_early.astype(BF16), flat_late, small.astype(BF16)], axis=0)
    every = everywhere(mine, "atoms")
    shapes = [
        (1, R), (1, R), (R, H), (R, H), (3, R, H), (3, R, H), (3, R, H), (R, R), (3, R, R), (1, 8),
    ]
    grads = pl.pallas_call(
        functools.partial(unpack_kernel, share),
        out_shape=[jax.ShapeDtypeStruct(shape, F32) for shape in shapes],
        in_specs=[whole()],
        out_specs=[whole()] * len(shapes),
        compiler_params=params(),
    )(every)
    return (
        new_features,
        new_vectors,
        grad_features,
        grad_vectors,
        grad_positions,
        grads[0].reshape(R),
        grads[1].reshape(R),
        grads[2].T,
        grads[3].T,
        jnp.swapaxes(grads[4], 1, 2),
        jnp.swapaxes(grads[5], 1, 2),
        jnp.swapaxes(grads[6], 1, 2),
        grads[7],
        grads[8],
        grads[9][0, :4],
    )


def solution(mesh):
    in_specs = (
        P(None, "atoms"),
        P(None, None, "atoms"),
        P(None, "atoms"),
        P("atoms"),
        P(None, "atoms"),
        P(),
        P(),
        P(None, "feat"),
        P(None, "feat"),
        P(None, None, "feat"),
        P(None, None, "feat"),
        P(None, None, "feat"),
        P(None, "feat"),
        P(None, None, "feat"),
        P("feat", "atoms"),
        P(None, "feat", "atoms"),
    )
    out_specs = (
        P("feat", "atoms"),
        P(None, "feat", "atoms"),
        P("feat", "atoms"),
        P(None, "feat", "atoms"),
        P(None, "atoms"),
        P("feat"),
        P("feat"),
        P(None, "feat"),
        P(None, "feat"),
        P(None, None, "feat"),
        P(None, None, "feat"),
        P(None, None, "feat"),
        P(None, "feat"),
        P(None, None, "feat"),
        P(),
    )
    return jax.shard_map(
        per_device, mesh=mesh, in_specs=in_specs, out_specs=out_specs, check_vma=False
    )
```

```python
import functools
import math

import jax
import jax.numpy as jnp
from jax import lax
from jax.experimental import pallas as pl
from jax.experimental.pallas import tpu as pltpu
from jax.sharding import PartitionSpec as P

H = 256
HEADS = 8
HEAD = H // HEADS
R = 64
MOL = 29
HALO = 32
CUTOFF = 5.0
EPSILON = 1e-05
F32 = jnp.float32
BF16 = jnp.bfloat16

LANE_GROUPS = 2
ROW_GROUPS = 3
SPAN = 5
OFFSETS = 14
STEPS = SPAN + OFFSETS
SUB = 16
LANES = 128

W01, W2V2, C01, C2_COUNT, POS, QK, V0_COUNT, V12, VEC01, VEC2 = range(10)
GROUP_ROWS = 352
EARLY = 9 * R + R // 2
LATE = 2 * R + R // 2
EXTRAS = 16


BLOCK = 8
WINDOW = 256


def block_list(molecules, rows):
    full, rest = divmod(molecules, BLOCK)
    wide = ROW_GROUPS * BLOCK
    out = [(n * wide, wide, BLOCK) for n in range(full)]
    if rows > full * wide:
        out.append((full * wide, rows - full * wide, rest))
    return out


def row_parts(shape, axis, size):
    row = lax.broadcasted_iota(jnp.int32, shape, axis)
    group = jnp.zeros(shape, jnp.int32)
    for g in range(1, ROW_GROUPS):
        group = jnp.where(row >= g * size, g, group)
    return group, row - group * size, row < ROW_GROUPS * size


def set_distances(target, width, size):
    for r in range(LANE_GROUPS):

        def step(t, _, r=r):
            group, molecule, held = row_parts((width, WINDOW), 0, size)
            spot = t + SPAN * (LANE_GROUPS * group + r)
            spot = jnp.where(spot >= MOL, spot - MOL, spot)
            lane = lax.broadcasted_iota(jnp.int32, (width, WINDOW), 1)
            value = jnp.where(held, molecule * MOL + spot - lane, -(10**6))
            target[r, pl.ds(t * width, width), :] = value
            return 0

        lax.fori_loop(0, STEPS, step, 0)


def windows(blocks, distances, start, tall):
    for n, (first, width, size) in enumerate(blocks):
        atom = start + n * BLOCK * MOL
        base = jnp.minimum(atom // SUB * SUB, tall - WINDOW)
        base = pl.multiple_of(base, SUB)
        chosen = distances[0] if size == BLOCK else distances[1]
        ones = [jnp.where(chosen[r] == base - atom, 1.0, 0.0).astype(BF16) for r in (0, 1)]
        yield first, width, pl.ds(base, WINDOW), ones


def spread(source, lanes, stage, blocks, distances, start):
    for first, width, here, ones in windows(blocks, distances, start, source.shape[0]):
        given = source[here, lanes]
        a, b = dot(ones[0], given), dot(ones[1], given)
        low = lax.broadcasted_iota(jnp.int32, (a.shape[0], LANES), 1) < R
        for n in range(a.shape[1] // LANES):
            left, right = a[:, n * LANES : (n + 1) * LANES], b[:, n * LANES : (n + 1) * LANES]
            one = jnp.where(low, left, pltpu.roll(right, R, 1))
            two = jnp.where(low, pltpu.roll(left, R, 1), right)
            stage[2 * n, :, first : first + width] = one.reshape(STEPS, width, LANES)
            stage[2 * n + 1, :, first : first + width] = two.reshape(STEPS, width, LANES)


def spread_positions(source, lanes, targets, blocks, distances, start):
    row = lax.broadcasted_iota(jnp.int32, (LANES, 3 * LANES), 0)
    lane = lax.broadcasted_iota(jnp.int32, (LANES, 3 * LANES), 1)
    axis = jnp.where(lane >= 2 * LANES, 2, jnp.where(lane >= LANES, 1, 0))
    mine = (row >= 3 * axis) & (row < 3 * axis + 3)
    low = lane - axis * LANES < R
    wide = [jnp.where(mine & (low == (r == 0)), 1.0, 0.0).astype(BF16) for r in (0, 1)]
    for first, width, here, ones in windows(blocks, distances, start, source.shape[0]):
        given = source[here, lanes]
        total = 0.0
        for r in (0, 1):
            total = total + dot(dot(ones[r], given).astype(BF16), wide[r])
        for d, target in enumerate(targets):
            value = total[:, d * LANES : (d + 1) * LANES]
            target[:, first : first + width] = value.reshape(STEPS, width, LANES)


def collect(sources, target, blocks, distances, start):
    target[...] = jnp.zeros(target.shape, F32)
    units = []
    for first, width, here, ones in windows(blocks, distances, start, target.shape[0]):
        units.append((first, width, here, ones))
    at = 0
    while at < len(units):
        group = units[at : at + 2] if units[at][0] % SUB == 0 and at + 1 < len(units) else None
        if group is None or (group[0][1] + group[1][1]) % SUB:
            group = units[at : at + 1]
        at += len(group)
        first = group[0][0]
        size = sum(g[1] for g in group)
        blocks_in = []
        for partner, carry in sources:
            value = partner[:, first : first + size].astype(F32)
            start_part = value[:SPAN] + carry[:, first : first + size]
            blocks_in.append(jnp.concatenate([start_part, value[SPAN:]], axis=0))
        for f, width, here, ones in group:
            parts = ([], [])
            for n in range(0, len(sources), 2):
                a = blocks_in[n][:, f - first : f - first + width].reshape(STEPS * width, LANES)
                b = blocks_in[n + 1][:, f - first : f - first + width]
                b = b.reshape(STEPS * width, LANES)
                low = lax.broadcasted_iota(jnp.int32, a.shape, 1) < R
                parts[0].append(jnp.where(low, a, pltpu.roll(b, R, 1)).astype(BF16))
                parts[1].append(jnp.where(low, pltpu.roll(a, R, 1), b).astype(BF16))
            total = 0.0
            for r in (0, 1):
                total = total + dot_tn(ones[r], jnp.concatenate(parts[r], axis=1))
            target[here, :] = target[here, :] + total


def row_masks(owned, start, blocks, atoms):
    for n, (at, width, size) in enumerate(blocks):
        _, molecule, _ = row_parts((width, LANES), 0, size)
        first = start - HALO + (n * BLOCK + molecule) * MOL
        owned[at : at + width] = jnp.where((first >= 0) & (first < atoms), 1.0, 0.0)


def set_multiplicities(count, target, blocks, rows):
    lane = lax.broadcasted_iota(jnp.int32, (rows, LANES), 1)
    inner = jnp.where(lane >= R, lane - R, lane)
    last = []
    for _, width, size in blocks:
        last.append(row_parts((width, LANES), 0, size)[0])
    doubled = (jnp.concatenate(last, axis=0) == ROW_GROUPS - 1) & (lane >= R)
    for t in range(SPAN):
        value = jnp.where(inner < 32, count[t], 0.0)
        for k in range(1, OFFSETS + 1):
            value = jnp.where(inner == 32 + k, count[t + k], value)
        if t == SPAN - 1:
            value = jnp.where(doubled, 0.0, value)
        target[t] = value


def dot(a, b):
    return jnp.dot(a, b, preferred_element_type=F32)


def dot_tn(a, b):
    return lax.dot_general(a, b, (((0,), (0,)), ((), ())), preferred_element_type=F32)


def dot_nt(a, b):
    return lax.dot_general(a, b, (((1,), (1,)), ((), ())), preferred_element_type=F32)


COSINE = (0.9999999998, -0.04934802137, 0.000405870916, -1.335212003e-06, 2.349373138e-09, -2.43963243e-12)

GEO_ENVELOPE, GEO_BEND, GEO_INVERSE, GEO_INTO, GEO_FROM, GEO_WAY, GEO_SLOPE, GEO_OWN = 0, 1, 2, 3, 4, 5, 8, 9
GEO = 10


def geometry(pos, many, t, rows, owned, close, radial, geo):
    lane = lax.broadcasted_iota(jnp.int32, (rows, LANES), 1)
    inner = jnp.where(lane >= R, lane - R, lane)
    inv_space = (R - 1) / CUTOFF
    off = []
    for p in pos:
        there = p[t + 1]
        for k in range(2, OFFSETS + 1):
            there = jnp.where(inner == k, p[t + k], there)
        off.append(p[t] - there)
    square = off[0] * off[0] + off[1] * off[1] + off[2] * off[2]
    clamped = jnp.maximum(square, 0.01)
    inverse = lax.rsqrt(clamped)
    c = COSINE[-1]
    for term in COSINE[-2::-1]:
        c = c * clamped + term
    c = jnp.where(clamped < CUTOFF * CUTOFF, c, 0.0)
    envelope = c * c
    y = jnp.maximum(envelope - envelope * envelope, 1e-30)
    bend = (-math.pi / CUTOFF) * (y * lax.rsqrt(y))
    close[GEO_ENVELOPE] = envelope
    close[GEO_BEND] = jnp.where(envelope > 0.0, bend, 0.0)
    close[GEO_INVERSE] = jnp.where(square > 0.01, inverse, -inverse)
    close[GEO_INTO] = many[t]
    close[GEO_FROM] = many[t]
    for d in range(3):
        close[GEO_WAY + d] = off[d] * inverse
    close[GEO_SLOPE] = jnp.where(envelope > 0.0, bend / jnp.maximum(envelope, 1e-37), 0.0)
    close[GEO_OWN] = (clamped * inverse) * inv_space

    def step(k, _):
        for o, size in halves(rows):
            here = pl.ds(pl.multiple_of(k * rows + o, SUB), size)
            part = slice(o, o + size)
            lane = lax.broadcasted_iota(jnp.int32, (size, LANES), 1)
            base = jnp.where(lane >= R, R, 0)
            centre = (lane - base).astype(F32)
            near = base + (k + 1)

            def wide(n, by=0):
                return jnp.take_along_axis(close[n, part], near + by, axis=1)

            u = wide(GEO_OWN) - centre
            envelope = wide(GEO_ENVELOPE)
            value = jnp.exp(-0.5 * (u * u)) * envelope
            high = value.astype(BF16)
            slope = value * (wide(GEO_SLOPE) - inv_space * u)
            radial[here, :LANES] = high
            radial[here, LANES:] = (value - high.astype(F32)).astype(BF16)
            geo[GEO_OWN, here, :] = high * owned[part].astype(BF16)
            geo[GEO_SLOPE, here, :] = slope.astype(BF16)
            geo[GEO_ENVELOPE, here, :] = envelope.astype(BF16)
            for n in (GEO_BEND, GEO_INVERSE, GEO_INTO, GEO_WAY, GEO_WAY + 1, GEO_WAY + 2):
                geo[n, here, :] = wide(n).astype(BF16)
            geo[GEO_FROM, here, :] = wide(GEO_FROM, 32).astype(BF16)
        return 0

    lax.fori_loop(0, OFFSETS, step, 0)


def halves(rows):
    tiles = rows // SUB
    first = (tiles + 1) // 2 * SUB
    return ((0, first), (first, rows - first))


def set_filters(weights_ref, filter_1, filter_2):
    weights_ref[...] = jnp.zeros(weights_ref.shape, BF16)
    for f, ref in enumerate((filter_1, filter_2)):
        half = ref[...] * jnp.asarray(0.5, BF16)
        for part in range(2):
            for g in range(LANE_GROUPS):
                down = part * LANES + g * R
                at = f * LANES + g * R
                weights_ref[down : down + R, at : at + R] = half


def gate(h):
    t = jnp.tanh(h)
    u = 1.0 + t
    f = h * u
    return f.astype(BF16), (u + f * (1.0 - t)).astype(BF16)


def carried(rows, t, totals, group, body):
    def outer(s, _):
        o = pl.multiple_of(s * SUB, SUB)
        block = pl.ds(o, SUB)
        ii = (t, block)
        sums = None
        for k in range(0, OFFSETS, group):
            loaded = []
            for n in range(k, k + group):
                here = pl.ds(o + n * rows, SUB)
                loaded.append(body(o, here, ii, (t + 1 + n, block), n))
            done = [f() for f in loaded]
            given = [one for one, _ in done]
            while len(given) > 1:
                left = given[len(given) // 2 * 2 :]
                pairs = zip(given[0::2], given[1::2])
                given = [[x + y for x, y in zip(a, b)] for a, b in pairs] + left
            total = [x.astype(F32) for x in given[0]]
            sums = total if sums is None else [x + y for x, y in zip(sums, total)]
            for _, stores in done:
                for ref, index, value in stores:
                    ref[index] = value
        for total, value in zip(totals, sums):
            total[ii] = value
        return 0

    lax.fori_loop(0, rows // SUB, outer, 0)


def geometry_kernel(
    molecules, rows, atoms,
    scalars, rows_ref, radial_out, geo_out, owned, near, near_last, px, py, pz, many, stage, close,
):
    t = pl.program_id(0)
    start = scalars[0]
    blocks = block_list(molecules, rows)
    distances = (near, near_last)

    @pl.when(t == 0)
    def _():
        row_masks(owned, start, blocks, atoms)
        set_distances(near, blocks[0][1], blocks[0][2])
        set_distances(near_last, blocks[-1][1], blocks[-1][2])
        lanes = slice(POS * LANES, (POS + 1) * LANES)
        spread_positions(rows_ref, lanes, (px, py, pz), blocks, distances, start)
        lanes = slice(C2_COUNT * LANES, (C2_COUNT + 1) * LANES)
        spread(rows_ref, lanes, stage, blocks, distances, start)
        set_multiplicities(stage.at[1], many, blocks, rows)

    geometry((px, py, pz), many, t, rows, owned, close, radial_out.at[0], geo_out.at[0])


def vector_kernel(
    molecules, rows, atoms,
    scalars, rows_ref, filter_1, filter_2, radial_in, geo_in,
    sums_ref, back_ref, grads_ref, pos_out, grad_w_ref,
    weights_ref, near, near_last, stage, loose, pre, grad_pre,
    grad_radial, grad_ways,
    w0, w1, w2, v2, c0, c1, c2,
    s0, s1, s2, a0, a1, a2, gv, gx, gy, gz,
    fs0, fs1, fs2, fa0, fa1, fa2, fgv, fgx, fgy, fgz,
):
    t = pl.program_id(0)
    start = scalars[0]
    own = slice(HALO, HALO + atoms)
    radial, geo = radial_in.at[0], geo_in.at[0]
    w, c, g_pos = (w0, w1, w2), (c0, c1, c2), (gx, gy, gz)
    sums, backs = (s0, s1, s2), (a0, a1, a2)
    blocks = block_list(molecules, rows)
    distances = (near, near_last)

    @pl.when(t == 0)
    def _():
        set_filters(weights_ref, filter_1, filter_2)
        set_distances(near, blocks[0][1], blocks[0][2])
        set_distances(near_last, blocks[-1][1], blocks[-1][2])
        lanes = slice(W01 * LANES, (C2_COUNT + 1) * LANES)
        spread(rows_ref, lanes, stage, blocks, distances, start)
        for n, target in enumerate((w0, w1, w2, v2, c0, c1, c2)):
            target[...] = stage[n].astype(BF16)
        for total in (s0, s1, s2, a0, a1, a2, gv, gx, gy, gz):
            total[...] = jnp.zeros(total.shape, BF16)
        grad_w_ref[...] = jnp.zeros(grad_w_ref.shape, F32)

    pre[...] = dot(radial[...], weights_ref[...])

    def channel(o, here, ii, jj, k):
        h1, h2 = pre[here, :LANES], pre[here, LANES:]
        ni, nj = geo[GEO_INTO, here, :], geo[GEO_FROM, here, :]
        v2i, v2j = v2[ii], v2[jj]
        ways = [geo[GEO_WAY + d, here, :] for d in range(3)]
        wi, wj = [w[d][ii] for d in range(3)], [w[d][jj] for d in range(3)]
        ci, cj = [c[d][ii] for d in range(3)], [c[d][jj] for d in range(3)]
        old_sums = [sums[d][jj] for d in range(3)]
        old_backs = [backs[d][jj] for d in range(3)]
        old_gv = gv[jj]

        def compute():
            f1, d1 = gate(h1)
            f2, d2 = gate(h2)
            f1i, f1j, f2i, f2j = f1 * ni, f1 * nj, f2 * ni, f2 * nj
            msg_i, msg_j = f2i * v2j, f2j * v2i
            stores, sum_i, back_i = [], [], []
            along_i = along_j = across_i = across_j = None
            for d in range(3):
                way = ways[d]
                sum_i.append(f1i * wj[d] + msg_i * way)
                stores.append((sums[d], jj, old_sums[d] + (f1j * wi[d] - msg_j * way)))
                stores.append((backs[d], jj, old_backs[d] + f1i * ci[d]))
                back_i.append(f1j * cj[d])
                grad = ci[d] * msg_i - cj[d] * msg_j
                stores.append((grad_ways, (d, here, slice(None)), grad))
                new = (ci[d] * way, cj[d] * way, ci[d] * wj[d], cj[d] * wi[d])
                if d == 0:
                    along_i, along_j, across_i, across_j = new
                else:
                    along_i, along_j = along_i + new[0], along_j + new[1]
                    across_i, across_j = across_i + new[2], across_j + new[3]
            stores.append((gv, jj, old_gv + f2i * along_i))
            g1 = ni * across_i + nj * across_j
            g2 = ni * along_i * v2j - nj * along_j * v2i
            stores.append((grad_pre, (here, slice(0, LANES)), g1 * d1))
            stores.append((grad_pre, (here, slice(LANES, None)), g2 * d2))
            return sum_i + back_i + [-(f2j * along_j)], stores

        return compute

    carried(rows, t, (fs0, fs1, fs2, fa0, fa1, fa2, fgv), 2, channel)
    grad_radial[...] = dot_nt(grad_pre[...], weights_ref[:LANES])
    grad_w_ref[...] = grad_w_ref[...] + dot_tn(geo[GEO_OWN], grad_pre[...])

    def turn(o, here, ii, jj, k):
        ways = [geo[GEO_WAY + d, here, :] for d in range(3)]
        grads = [grad_ways[d, here, :] for d in range(3)]
        grad, slope = grad_radial[here, :], geo[GEO_SLOPE, here, :]
        signed = geo[GEO_INVERSE, here, :]
        old = [g[jj] for g in g_pos]

        def compute():
            inverse = jnp.abs(signed)
            turned = [g * inverse for g in grads]
            along = ways[0] * turned[0] + ways[1] * turned[1] + ways[2] * turned[2]
            pull = jnp.where(signed > 0, grad.astype(BF16) * slope - along, 0)
            out = [turned[d] + ways[d] * pull for d in range(3)]
            return out, [(g_pos[d], jj, old[d] - out[d]) for d in range(3)]

        return compute

    carried(rows, t, (fgx, fgy, fgz), 7, turn)

    @pl.when(t == SPAN - 1)
    def _():
        low = lax.broadcasted_iota(jnp.int32, (atoms, LANES), 1) < R
        totals = (s0, s1, s2, gv, a0, a1, a2, gx, gy, gz)
        firsts = (fs0, fs1, fs2, fgv, fa0, fa1, fa2, fgx, fgy, fgz)
        collect(tuple(zip(totals, firsts)), loose, blocks, distances, start)
        both = loose[own, :LANES].T
        sums_ref[0] = both[:R]
        sums_ref[1] = both[R:]
        both = loose[own, LANES : 2 * LANES].T
        sums_ref[2] = both[:R]
        grads_ref[R:] = both[R:].astype(BF16)

        def kept(n):
            return rows_ref[own, n * LANES : (n + 1) * LANES].astype(F32)

        v12 = kept(V12)
        v11 = jnp.where(low, v12, pltpu.roll(v12, R, 1))
        back = loose[own, 2 * LANES : 3 * LANES]
        both = (back * v11).T
        back_ref[0] = both[:R]
        back_ref[1] = both[R:]
        partial = back * kept(VEC01)
        partial = partial + pltpu.roll(partial, R, 1)
        back = loose[own, 3 * LANES : 4 * LANES]
        back_ref[2] = (back * v11).T[:R]
        partial = partial + back * kept(VEC2)
        grads_ref[:R] = partial.T[:R].astype(BF16)
        pos_out[...] = jnp.zeros(pos_out.shape, F32)
        pos_out[0:1] = jnp.sum(back.T[R:], axis=0, keepdims=True)
        both = loose[own, 4 * LANES :].T
        pos_out[1:2] = jnp.sum(both[:R], axis=0, keepdims=True)
        pos_out[2:3] = jnp.sum(both[R:], axis=0, keepdims=True)


def scalar_kernel(
    molecules, rows, atoms,
    scalars, rows_ref, filter_1, filter_2, scalar_parts, radial_in, geo_in,
    sum_ref, grads_ref, pos_out, grad_w_ref,
    weights_ref, heads_ref, near, near_last, stage, loose, loose_low, pre,
    grad_pre, grad_radial, products, sums, gates, bends,
    q, key, v0, gs,
    ss, gq, gk, g0, gx, gy, gz,
    fss, fgq, fgk, fg0, fgx, fgy, fgz,
):
    t = pl.program_id(0)
    start = scalars[0]
    own = slice(HALO, HALO + atoms)
    radial, geo = radial_in.at[0], geo_in.at[0]
    g_pos = (gx, gy, gz)
    blocks = block_list(molecules, rows)
    distances = (near, near_last)

    @pl.when(t == 0)
    def _():
        set_filters(weights_ref, filter_1, filter_2)
        row = lax.broadcasted_iota(jnp.int32, (2 * LANES, 2 * LANES), 0)
        lane = lax.broadcasted_iota(jnp.int32, (2 * LANES, 2 * LANES), 1)
        heads_ref[...] = jnp.where(row // HEAD == lane // HEAD, 1.0, 0.0).astype(BF16)
        set_distances(near, blocks[0][1], blocks[0][2])
        set_distances(near_last, blocks[-1][1], blocks[-1][2])
        lanes = slice(QK * LANES, (V0_COUNT + 1) * LANES)
        spread(rows_ref, lanes, stage, blocks, distances, start)
        for n, target in enumerate((q, key, v0)):
            target[...] = stage[n].astype(BF16)
        summed = scalar_parts[0].astype(F32)
        for f in range(1, scalar_parts.shape[0]):
            summed = summed + scalar_parts[f].astype(F32)
        summed = jnp.concatenate([summed, jnp.zeros_like(summed)], axis=0).T.astype(BF16)
        loose_low[own] = summed[:atoms]
        loose_low[:HALO] = summed[atoms : atoms + HALO]
        loose_low[HALO + atoms : 2 * HALO + atoms] = summed[atoms + HALO : atoms + 2 * HALO]
        end = 2 * HALO + atoms
        loose_low[end:] = jnp.zeros((loose_low.shape[0] - end, LANES), BF16)
        spread(loose_low, slice(None), stage, blocks, distances, start)
        gs[...] = stage[0].astype(BF16)
        for total in (ss, gq, gk, g0, gx, gy, gz):
            total[...] = jnp.zeros(total.shape, BF16)
        grad_w_ref[...] = jnp.zeros(grad_w_ref.shape, F32)

    pre[...] = dot(radial[...], weights_ref[...])

    def multiply(k, _):
        for o, size in halves(rows):
            here = pl.ds(pl.multiple_of(k * rows + o, SUB), size)
            ii, jj = (t, slice(o, o + size)), (t + 1 + k, slice(o, o + size))
            fk, dk = gate(pre[here, :LANES])
            f0, d0 = gate(pre[here, LANES:])
            k_ij, k_ji = q[ii] * key[jj] * fk, q[jj] * key[ii] * fk
            s_ij, s_ji = gs[ii] * v0[jj] * f0, gs[jj] * v0[ii] * f0
            gates[0, here, :] = fk
            gates[1, here, :] = f0
            gates[2, here, :] = dk
            gates[3, here, :] = d0
            products[0, here, :LANES] = k_ij
            products[0, here, LANES:] = k_ji
            products[1, here, :LANES] = s_ij
            products[1, here, LANES:] = s_ji
        return 0

    lax.fori_loop(0, OFFSETS, multiply, 0)
    sums[0] = dot(products[0], heads_ref[...])
    sums[1] = dot(products[1], heads_ref[...])

    def channel(o, here, ii, jj, k):
        fk, f0, dk, d0 = [gates[n, here, :] for n in range(4)]
        envelope, bend = geo[GEO_ENVELOPE, here, :], geo[GEO_BEND, here, :]
        side_in = []
        for side in range(2):
            lanes = slice(side * LANES, (side + 1) * LANES)
            m = geo[GEO_INTO + side, here, :]
            h, o_ = (ii, jj) if side == 0 else (jj, ii)
            side_in.append(
                (m, sums[0, here, lanes], sums[1, here, lanes])
                + (q[h], key[o_], gs[h], v0[o_])
            )
        old = [ref[jj] for ref in (g0, gk, ss, gq)]

        def compute():
            gives, news = [], []
            for m, score, g_att, qh, kt, gh, vt in side_in:
                act, rise = gate(0.5 * score)
                g_att = g_att.astype(BF16)
                weight = m * envelope
                att = act * weight
                g_score = g_att * (0.5 * rise) * weight
                lift = m * (g_att * act)
                bv, dv = f0 * att, fk * g_score
                gives.append((vt * bv, kt * dv, gh * bv, qh * dv))
                news.append((qh * kt * g_score, gh * vt * att, lift))
            one, two = gives
            new = [x + y for x, y in zip(*news)]
            stores = [
                (ref, jj, x + y)
                for ref, x, y in zip((g0, gk, ss, gq), old, (one[2], one[3], two[0], two[1]))
            ]
            stores.append((grad_pre, (here, slice(0, LANES)), new[0] * dk))
            stores.append((grad_pre, (here, slice(LANES, None)), new[1] * d0))
            stores.append((bends, (here, slice(None)), new[2] * bend * (1.0 / HEAD)))
            return [one[0], one[1], two[2], two[3]], stores

        return compute

    carried(rows, t, (fss, fgq, fg0, fgk), 2, channel)
    grad_radial[...] = dot_nt(grad_pre[...], weights_ref[:LANES])
    grad_w_ref[...] = grad_w_ref[...] + dot_tn(geo[GEO_OWN], grad_pre[...])

    def turn(o, here, ii, jj, k):
        ways = [geo[GEO_WAY + d, here, :] for d in range(3)]
        grad, slope, bend = grad_radial[here, :], geo[GEO_SLOPE, here, :], bends[here, :]
        signed = geo[GEO_INVERSE, here, :]
        old = [g[jj] for g in g_pos]

        def compute():
            pull = jnp.where(signed > 0, grad.astype(BF16) * slope + bend, 0)
            out = [way * pull for way in ways]
            return out, [(g_pos[d], jj, old[d] - out[d]) for d in range(3)]

        return compute

    carried(rows, t, (fgx, fgy, fgz), 7, turn)

    @pl.when(t == SPAN - 1)
    def _():
        totals = (ss, g0, gq, gk, gx, gy, gz, gz)
        firsts = (fss, fg0, fgq, fgk, fgx, fgy, fgz, fgz)
        collect(tuple(zip(totals, firsts)), loose, blocks, distances, start)
        both = loose[own, :LANES].T
        sum_ref[...] = both[:R].astype(BF16)
        grads_ref[2 * R :] = both[R:].astype(BF16)
        grads_ref[: 2 * R] = loose[own, LANES : 2 * LANES].T.astype(BF16)
        pos_out[...] = jnp.zeros(pos_out.shape, F32)
        both = loose[own, 2 * LANES : 3 * LANES].T
        pos_out[0:1] = jnp.sum(both[:R], axis=0, keepdims=True)
        pos_out[1:2] = jnp.sum(both[R:], axis=0, keepdims=True)
        both = loose[own, 3 * LANES :].T
        pos_out[2:3] = jnp.sum(both[:R], axis=0, keepdims=True)


def whole(memory=pltpu.VMEM):
    return pl.BlockSpec(memory_space=memory)


def params(mib=60):
    return pltpu.CompilerParams(vmem_limit_bytes=mib * 1024 * 1024)


def edge_sizes(atoms):
    molecules = (atoms + 2 * (MOL - 1)) // MOL
    full, rest = divmod(molecules, BLOCK)
    rows = full * ROW_GROUPS * BLOCK + -(-ROW_GROUPS * rest // BLOCK) * BLOCK
    rows = -(-rows // SUB) * SUB
    tall = -(-(HALO + molecules * MOL) // SUB) * SUB
    return molecules, rows, tall


def by_step(shape):
    zeros = (0,) * (len(shape) - 1)
    return pl.BlockSpec((1,) + shape[1:], lambda t: (t,) + zeros)


def fixed(shape):
    zeros = (0,) * len(shape)
    return pl.BlockSpec(shape, lambda t: zeros)


def edge_call(kernel, atoms, inputs, stepped_in, outs, stepped_out, scratch):
    molecules, rows, _ = edge_sizes(atoms)
    return pl.pallas_call(
        functools.partial(kernel, molecules, rows, atoms),
        grid=(SPAN,),
        out_shape=[jax.ShapeDtypeStruct(s, kind) for s, kind in outs + stepped_out],
        in_specs=[whole(pltpu.SMEM)]
        + [fixed(x.shape) for x in inputs[1:]]
        + [by_step(x.shape) for x in stepped_in],
        out_specs=[fixed(s) for s, _ in outs] + [by_step(s) for s, _ in stepped_out],
        scratch_shapes=[pltpu.VMEM(s, kind) for s, kind in scratch],
        compiler_params=params(),
        cost_estimate=pl.CostEstimate(
            flops=20 * 10**9, bytes_accessed=40 * 10**6, transcendentals=10**7
        ),
    )(*inputs, *stepped_in)


def shared_scratch(atoms):
    molecules, rows, tall = edge_sizes(atoms)
    batch = OFFSETS * rows
    blocks = block_list(molecules, rows)
    return {
        "weights": ((2 * LANES, 2 * LANES), BF16),
        "many": ((SPAN, rows, LANES), F32),
        "close": ((GEO, rows, LANES), F32),
        "stage2": ((2, STEPS, rows, LANES), F32),
        "mask": ((rows, LANES), F32),
        "near": ((LANE_GROUPS, STEPS * blocks[0][1], WINDOW), jnp.int32),
        "near_last": ((LANE_GROUPS, STEPS * blocks[-1][1], WINDOW), jnp.int32),
        "stage8": ((8, STEPS, rows, LANES), F32),
        "stage4": ((4, STEPS, rows, LANES), F32),
        "loose5": ((tall, 5 * LANES), F32),
        "loose4": ((tall, 4 * LANES), F32),
        "loose_low": ((tall, LANES), BF16),
        "tall": ((STEPS, rows, LANES), F32),
        "low": ((STEPS, rows, LANES), BF16),
        "first": ((SPAN, rows, LANES), F32),
        "pre": ((batch, 2 * LANES), F32),
        "grad_pre": ((batch, 2 * LANES), BF16),
        "line": ((batch, LANES), F32),
        "line2": ((2, batch, LANES), BF16),
        "line3": ((3, batch, LANES), BF16),
        "line4": ((4, batch, LANES), BF16),
        "line1": ((batch, LANES), BF16),
        "wide2": ((2, batch, 2 * LANES), BF16),
        "wide2f": ((2, batch, 2 * LANES), F32),
    }


def offsets_in_block(neighbours, mask, first):
    lane = lax.broadcasted_iota(jnp.int32, neighbours.shape, 1)
    diff = neighbours - (first + lane)
    return jnp.where(diff < 0, diff + MOL, diff) * mask


def pieces(x):
    a = x.astype(BF16)
    rest = x - a.astype(F32)
    b = rest.astype(BF16)
    return a, b, (rest - b.astype(F32)).astype(BF16)


def edge_groups(features, vectors, cot_f, cot_v, neighbours, mask, positions, first):
    diff = offsets_in_block(neighbours[...], mask[...], first).astype(F32).astype(BF16)
    groups = [jnp.concatenate([features[...], cot_f[...], diff], axis=0)]
    for d in range(3):
        rows = [x.astype(F32) for x in pieces(positions[d : d + 1])]
        rows = jnp.concatenate(rows + [jnp.zeros((29, LANES), F32)], axis=0).astype(BF16)
        groups.append(jnp.concatenate([vectors[d], cot_v[d], rows], axis=0))
    return groups


def halo_kernel(atoms, scalars, *refs):
    row_first = scalars[2]
    lane = lax.broadcasted_iota(jnp.int32, (GROUP_ROWS, LANES), 1)
    for end, at, out in ((0, atoms - LANES, refs[14]), (1, 0, refs[15])):
        groups = edge_groups(*refs[7 * end : 7 * end + 7], row_first + at)
        total = None
        for g, group in enumerate(groups):
            by = (HALO * (g + 1) if end == 0 else HALO * g) % LANES
            moved = group.astype(F32)
            moved = pltpu.roll(moved, by, 1) if by else moved
            total = moved if total is None else jnp.where(lane >= HALO * g, moved, total)
        out[...] = total.astype(BF16)


def halo_call(atoms, scalars, arrays):
    specs = []
    for at in (atoms // LANES - 1, 0):
        for x in arrays:
            shape = x.shape[:-1] + (LANES,)
            index = (0,) * (x.ndim - 1) + (at,)
            specs.append(pl.BlockSpec(shape, lambda *_, index=index: index))
    out = jax.ShapeDtypeStruct((GROUP_ROWS, LANES), BF16)
    return pl.pallas_call(
        functools.partial(halo_kernel, atoms),
        grid=(1,),
        out_shape=[out, out],
        in_specs=[whole(pltpu.SMEM)] + specs,
        out_specs=[whole(), whole()],
        compiler_params=params(),
    )(scalars, *arrays, *arrays)


def column(row):
    return jnp.broadcast_to(row, (8, row.shape[1])).T[:, :1]


def normalised(f):
    mean = jnp.mean(f, axis=0, keepdims=True)
    centred = f - mean
    inv = lax.rsqrt(jnp.mean(centred * centred, axis=0, keepdims=True) + EPSILON)
    return centred * inv, mean, inv


def dense_kernel(
    atoms,
    scalars, features, vectors, cot_f, cot_v, neighbours, mask, positions, low_ref, high_ref,
    gain_ref, bias_ref, w_query, w_key, w_value, w_vector, w_output,
    rows_ref, part_ref, stat_ref,
    w_qk, w_v0, w_v12, w_vec_t, w_out,
):
    chan_first = pl.multiple_of(scalars[1], R)
    row_first = scalars[2]
    gain, bias = column(gain_ref[...]), column(bias_ref[...])
    w_qk[:R] = w_query[...]
    w_qk[R:] = w_key[...]
    w_v0[:R] = w_value[0]
    w_v0[R:] = jnp.zeros((R, H), BF16)
    w_v12[:R] = w_value[1]
    w_v12[R:] = w_value[2]
    for p in range(3):
        w_vec_t[p * R : (p + 1) * R] = w_vector[p]
    w_out[...] = jnp.concatenate([w_output[p] for p in range(3)], axis=0).astype(F32).T.astype(BF16)

    def block(f, v, cf, cv, own_v, diff, pos):
        width = f.shape[1]
        normed, mean, inv = normalised(f)
        turned = (normed * gain + bias).T.astype(BF16)
        kinds = lax.broadcasted_iota(jnp.int32, (R, width), 0)
        kinds = jnp.where(kinds < 32, kinds, MOL + 32 - kinds).astype(F32)
        counts = jnp.zeros((R, width), F32)
        for s in range(diff.shape[0]):
            counts = counts + jnp.where(diff[s : s + 1] == kinds, 1.0, 0.0)
        none = jnp.zeros((R, width), F32)
        counts = jnp.concatenate([none, counts], axis=0).T
        low = lax.broadcasted_iota(jnp.int32, (width, LANES), 1) < R
        pairs = [None] * 10
        pairs[QK] = dot_nt(turned, w_qk[...])
        pairs[V0_COUNT] = dot_nt(turned, w_v0[...]) + counts
        v12 = dot_nt(turned, w_v12[...]).astype(BF16).astype(F32)
        v11 = jnp.where(low, v12, pltpu.roll(v12, R, 1))
        pairs[V12] = v12
        pairs[VEC01] = jnp.concatenate([own_v[0], own_v[1]], axis=0).T
        pairs[VEC2] = jnp.concatenate([own_v[2], none], axis=0).T
        pairs[W01] = pairs[VEC01] * v11
        pairs[W2V2] = jnp.where(low, pairs[VEC2] * v11, v12)
        pairs[C01] = jnp.concatenate([cv[0], cv[1]], axis=0).T
        pairs[C2_COUNT] = jnp.concatenate([cv[2], none], axis=0).T + counts
        pairs[POS] = jnp.concatenate([pos, jnp.zeros((LANES - 9, width), F32)], axis=0).T
        vec_dot = grad_0 = 0.0
        for d in range(3):
            proj = dot(w_vec_t[...], v[d])
            vec_dot = vec_dot + proj[:R] * proj[R : 2 * R]
            grad_0 = grad_0 + cv[d] * proj[2 * R :]
        grad_out = jnp.concatenate([grad_0, cf * vec_dot, cf], axis=0).astype(BF16)
        part = dot(w_out[...], grad_out)
        return [x.astype(BF16) for x in pairs], part.astype(BF16), mean, inv

    wide = 2 * LANES

    def step(b, _):
        at = pl.multiple_of(b * wide, wide)
        here = pl.ds(at, wide)
        own_v = [vectors[d, pl.ds(chan_first, R), here].astype(F32) for d in range(3)]
        diff = offsets_in_block(neighbours[:, here], mask[:, here], row_first + at)
        places = [p.astype(F32) for d in range(3) for p in pieces(positions[d : d + 1, here])]
        pairs, part, mean, inv = block(
            features[:, here].astype(F32),
            [vectors[d, :, here] for d in range(3)],
            cot_f[:, here].astype(F32),
            [cot_v[d, :, here].astype(F32) for d in range(3)],
            own_v,
            diff.astype(F32),
            jnp.concatenate(places, axis=0),
        )
        there = pl.ds(pl.multiple_of(HALO + at, 2 * SUB), wide)
        for n, pair in enumerate(pairs):
            rows_ref[there, n * LANES : (n + 1) * LANES] = pair
        part_ref[:, here] = part
        stat_ref[0:1, here] = mean
        stat_ref[1:2, here] = inv
        return 0

    lax.fori_loop(0, atoms // wide, step, 0)

    lane = lax.broadcasted_iota(jnp.int32, (GROUP_ROWS, LANES), 1)
    packed_low, packed_high = low_ref[...].astype(F32), high_ref[...].astype(F32)
    groups = []
    for g in range(4):
        a = pltpu.roll(packed_low, (LANES - HALO * g) % LANES, 1) if g else packed_low
        by = (LANES + HALO - HALO * g) % LANES
        b = pltpu.roll(packed_high, by, 1) if by else packed_high
        both = jnp.where(lane < HALO, a, jnp.where(lane < 2 * HALO, b, 0.0))
        groups.append(both)
    pick_rows = lax.broadcasted_iota(jnp.int32, (H, LANES), 0)
    own_v, pos = [], []
    for d in range(3):
        g = groups[1 + d]
        found = g[:R]
        for f in range(1, H // R):
            found = jnp.where(chan_first == f * R, g[f * R : (f + 1) * R], found)
        own_v.append(found)
        pos.append(g[320:323])
    pairs, part, _, _ = block(
        groups[0][:H],
        [groups[1 + d][:H].astype(BF16) for d in range(3)],
        groups[0][H : H + R],
        [groups[1 + d][H : H + R] for d in range(3)],
        own_v,
        groups[0][H + R :],
        jnp.concatenate(pos, axis=0),
    )
    high = HALO + atoms
    tall = rows_ref.shape[0]
    for n, pair in enumerate(pairs):
        lanes = slice(n * LANES, (n + 1) * LANES)
        rows_ref[:HALO, lanes] = pair[:HALO]
        rows_ref[high : high + HALO, lanes] = pair[HALO : 2 * HALO]
        rows_ref[high + HALO :, lanes] = jnp.zeros((tall - high - HALO, LANES), BF16)
    part_ref[:, atoms:] = part


def both_diagonals(grad, f):
    at = f * LANES
    return 0.5 * (grad[:R, at : at + R] + grad[R:, at + R : at + LANES])


def filter_block(grad):
    both = jnp.concatenate([both_diagonals(grad, 0), both_diagonals(grad, 1)], axis=1)
    return jnp.concatenate([both[: R // 2], both[R // 2 :]], axis=1)


def layer_kernel(
    atoms,
    scalars, features, stat, vectors, cot_f, cot_v, gathered, grads_b, gain_ref, bias_ref,
    w_vector, w_output, grad_filters_b,
    feat_out, delta_ref, square_ref, send_ref, flat_ref,
    w_vec, w_vec_t, w_out_t,
):
    chan_first = pl.multiple_of(scalars[1], R)
    gain, bias = column(gain_ref[...]), column(bias_ref[...])
    for p in range(3):
        w_vec_t[p * R : (p + 1) * R] = w_vector[p]
        w_out_t[p * R : (p + 1) * R] = w_output[p]
    w_vec[...] = w_vec_t[...].astype(F32).T.astype(BF16)
    t_vec, t_out, t_b = [flat_ref.at[n * 3 * R : (n + 1) * 3 * R] for n in range(3)]
    flat_ref[...] = jnp.zeros(flat_ref.shape, F32)
    wide = 2 * LANES
    split = send_ref.shape[0]

    def step(b, _):
        at = pl.multiple_of(b * wide, wide)
        here = pl.ds(at, wide)
        all_sums = gathered[:, here]
        outputs = dot(w_out_t[...], all_sums)
        out_0, out_1, out_2 = outputs[:R], outputs[R : 2 * R], outputs[2 * R :]
        cf = cot_f[:, here].astype(F32)
        grad_dot = cf * out_1
        vec_dot = grad_0 = 0.0
        for d in range(3):
            proj = dot(w_vec_t[...], vectors[d, :, here])
            first, second, third = proj[:R], proj[R : 2 * R], proj[2 * R :]
            cv = cot_v[d, :, here].astype(F32)
            vec_dot = vec_dot + first * second
            grad_0 = grad_0 + cv * third
            delta_ref[d, :, here] = third * out_0
            grad_proj = jnp.concatenate(
                [grad_dot * second, grad_dot * first, cv * out_0], axis=0
            ).astype(BF16)
            part = dot(w_vec[...], grad_proj).astype(BF16)
            for f in range(split):
                send_ref[f, d * R : (d + 1) * R, here] = part[f * R : (f + 1) * R]
            t_vec[...] = t_vec[...] + dot_nt(grad_proj, vectors[d, :, here])
        delta = vec_dot * out_1 + out_2
        moved = features[pl.ds(chan_first, R), here].astype(F32) + delta
        feat_out[:, here] = moved.astype(BF16)
        grad_out = jnp.concatenate([grad_0, cf * vec_dot, cf], axis=0).astype(BF16)
        t_out[...] = t_out[...] + dot_nt(grad_out, all_sums)
        square_ref[0:1, here] = jnp.sum(moved * moved, axis=0, keepdims=True)
        square_ref[1:2, here] = jnp.sum(delta * delta, axis=0, keepdims=True)
        normed = (features[:, here].astype(F32) - stat[0:1, here]) * stat[1:2, here]
        normal = (normed * gain + bias).astype(BF16)
        t_b[...] = t_b[...] + dot_nt(grads_b[:, here], normal)
        return 0

    lax.fori_loop(0, atoms // wide, step, 0)
    flat_ref[9 * R :] = filter_block(grad_filters_b[...])


def normal_kernel(
    atoms,
    scalars, features, stat, vectors, delta_ref, square_ref, sums_ref,
    grads_b, grads_a, pos_a, pos_b, mask, gain_ref, bias_ref,
    w_query, w_key, w_value, grad_filters_a,
    vec_out, send_ref, flat_ref,
    w_five, t_late,
):
    chan_first = pl.multiple_of(scalars[1], R)
    gain, bias = column(gain_ref[...]), column(bias_ref[...])
    five = [w_query[...], w_key[...]] + [w_value[p] for p in range(3)]
    w_five[...] = jnp.concatenate(five, axis=0).astype(F32).T.astype(BF16)
    t_late[...] = jnp.zeros(t_late.shape, F32)
    wide = 2 * LANES
    split = send_ref.shape[0]

    def step(b, _):
        at = pl.multiple_of(b * wide, wide)
        here = pl.ds(at, wide)
        real = mask[:, here].astype(F32)
        square_v = square_dv = 0.0
        for d in range(3):
            delta = delta_ref[d, :, here] + sums_ref[d, :, here]
            moved = vectors[d, pl.ds(chan_first, R), here].astype(F32) + delta
            vec_out[d, :, here] = moved.astype(BF16)
            square_v = square_v + moved * moved
            square_dv = square_dv + delta * delta
        normed = (features[:, here].astype(F32) - stat[0:1, here]) * stat[1:2, here]
        normal = (normed * gain + bias).astype(BF16)
        grads = jnp.concatenate([grads_b[:, here], grads_a[:, here]], axis=0)
        t_late[...] = t_late[...] + dot_nt(grads_a[:, here], normal)
        part = dot(w_five[...], grads)
        rounded = part.astype(BF16)
        for f in range(split):
            send_ref[f, :R, here] = rounded[f * R : (f + 1) * R]
        hat = part * gain
        tops = [
            jnp.sum(hat, axis=0, keepdims=True),
            jnp.sum(hat * normed, axis=0, keepdims=True),
        ]
        exact = [pos_a[d : d + 1, here] + pos_b[d : d + 1, here] for d in range(3)]
        exact += [square_ref[n : n + 1, here] * real for n in range(2)]
        for x in (square_v, square_dv):
            exact.append(jnp.sum(x, axis=0, keepdims=True) * real)
        heads = [x.astype(BF16).astype(F32) for x in exact]
        tops = tops + heads + [x - y for x, y in zip(exact, heads)]
        tops = jnp.concatenate(tops, axis=0).astype(BF16)
        for f in range(split):
            send_ref[f, R:, here] = tops
        return 0

    lax.fori_loop(0, atoms // wide, step, 0)
    flat_ref[: 2 * R] = t_late[...].astype(BF16)
    flat_ref[2 * R :] = filter_block(grad_filters_a[...]).astype(BF16)


def final_kernel(
    atoms,
    scalars, got, got_vec, features, stat, gain_ref, cot_f, cot_v, back_ref, mask,
    grad_feat, grad_vec, grad_pos, small_ref,
):
    chan_first = pl.multiple_of(scalars[1], R)
    whole_gain = column(gain_ref[...])
    gain = whole_gain[:R]
    for f in range(1, H // R):
        gain = jnp.where(chan_first == f * R, whole_gain[f * R : (f + 1) * R], gain)

    def summed(ref, rows):
        total = ref[0, rows].astype(F32)
        for f in range(1, ref.shape[0]):
            total = total + ref[f, rows].astype(F32)
        return total

    tops = summed(got, slice(R, R + EXTRAS))
    grad_normal = summed(got, slice(0, R))
    inv = stat[1:2]
    normed = (features[pl.ds(chan_first, R), :].astype(F32) - stat[0:1]) * inv
    inner = grad_normal * gain - tops[0:1] * (1.0 / H) - normed * (tops[1:2] * (1.0 / H))
    grad_feat[...] = cot_f[...].astype(F32) + inv * inner
    for d in range(3):
        part = summed(got_vec, slice(d * R, (d + 1) * R))
        grad_vec[d] = cot_v[d].astype(F32) + part + back_ref[d]
    exact = tops[2:9] + tops[9:16]
    grad_pos[...] = exact[:3]
    ones = jnp.ones((8, atoms), BF16)
    gains = dot_nt(ones, (grad_normal * normed).astype(BF16))
    biases = dot_nt(ones, grad_normal.astype(BF16))
    totals = jnp.sum(exact[3:7], axis=1, keepdims=True)
    real = jnp.sum(mask[...].astype(F32), axis=1, keepdims=True)
    numbers = jnp.concatenate([totals, real, jnp.zeros((3, 1), F32)], axis=0)
    small = jnp.concatenate([gains, biases, jnp.broadcast_to(numbers, (8, LANES))], axis=1)
    high = small.astype(BF16)
    small_ref[:8] = high.astype(F32)
    small_ref[8:] = small - high.astype(F32)


def unpack_kernel(
    share,
    got,
    g_gain, g_bias, g_query, g_key, g_value, g_vector, g_output, g_key_f, g_value_f, rms_ref,
):
    every = [got[n].astype(F32) for n in range(got.shape[0])]
    small = 0.0
    for x in every:
        small = small + x[share:]
    total = small[:8] + small[8:]
    g_gain[...] = total[0:1, :R]
    g_bias[...] = total[0:1, R : 2 * R]
    numbers = total[:, LANES : LANES + 1]
    size = jnp.where(lax.broadcasted_iota(jnp.int32, (8, 1), 0) < 2, 1.0, 3.0) * H
    rms = jnp.sqrt(numbers / (numbers[4:5] * size) + 1e-06)
    rms_ref[...] = jnp.broadcast_to(rms, (8, LANES)).T[:1, :8]
    order = [(g, p) for g in (g_vector, g_output) for p in range(3)]
    order += [(g_query, None), (g_key, None), (g_value, 0), ((g_key_f, None), (g_value_f, 0))]
    order += [(g_value, 1), (g_value, 2), ((g_value_f, 1), (g_value_f, 2))]
    begins = [0]
    for g, _ in order:
        begins.append(begins[-1] + (R // 2 if isinstance(g, tuple) else R))
    for n, x in enumerate(every):
        for (g, p), low, high in zip(order, begins[:-1], begins[1:]):
            first, last = max(low, n * share), min(high, (n + 1) * share)
            if first >= last:
                continue
            value = x[first - n * share : last - n * share]
            rows = slice(first - low, last - low)
            if not isinstance(g, tuple):
                put(g, p, rows, value)
                continue
            for h in (0, 1):
                down = slice(rows.start + h * R // 2, rows.stop + h * R // 2)
                at = h * LANES
                put(g[0], g[1], down, value[:, at : at + R])
                put(p[0], p[1], down, value[:, at + R : at + 2 * R])


def put(ref, p, rows, value):
    if p is None:
        ref[rows] = value
    else:
        ref[p, rows] = value


def everywhere(x, axis):
    count = lax.axis_size(axis)
    return lax.all_to_all(jnp.broadcast_to(x[None], (count,) + x.shape), axis, 0, 0)


def per_device(
    features, vectors, positions, atom_mask, neighbours, ln_gain, ln_bias,
    w_query, w_key, w_value, w_vector, w_output, w_key_filter, w_value_filter,
    cot_features, cot_vectors,
):
    channels = w_query.shape[1]
    atoms = features.shape[1]
    count = lax.axis_size("atoms")
    split = lax.axis_size("feat")
    chan_first = lax.axis_index("feat") * channels
    row_first = lax.axis_index("atoms") * atoms
    start = HALO - lax.rem(row_first, MOL)
    scalars = jnp.stack([start, chan_first, row_first]).astype(jnp.int32)
    molecules, rows_each, tall = edge_sizes(atoms)
    w_query, w_key = w_query.T, w_key.T
    w_value, w_vector, w_output = [jnp.swapaxes(w, 1, 2) for w in (w_value, w_vector, w_output)]
    mask = atom_mask.reshape(1, atoms)
    gain, bias = ln_gain.reshape(1, H), ln_bias.reshape(1, H)

    ends = halo_call(
        atoms,
        scalars,
        (features, vectors, cot_features, cot_vectors, neighbours, mask, positions),
    )
    low = lax.ppermute(ends[0], "atoms", [(i, i + 1) for i in range(count - 1)])
    high = lax.ppermute(ends[1], "atoms", [(i + 1, i) for i in range(count - 1)])

    inputs = (
        scalars, features, vectors, cot_features, cot_vectors, neighbours, mask, positions,
        low, high, gain, bias, w_query, w_key, w_value, w_vector, w_output,
    )
    rows, part, stat = pl.pallas_call(
        functools.partial(dense_kernel, atoms),
        out_shape=[
            jax.ShapeDtypeStruct((tall, 10 * LANES), BF16),
            jax.ShapeDtypeStruct((H, atoms + LANES), BF16),
            jax.ShapeDtypeStruct((8, atoms), F32),
        ],
        in_specs=[whole(pltpu.SMEM)] + [whole()] * (len(inputs) - 1),
        out_specs=[whole()] * 3,
        scratch_shapes=[
            pltpu.VMEM((LANES, H), BF16),
            pltpu.VMEM((LANES, H), BF16),
            pltpu.VMEM((LANES, H), BF16),
            pltpu.VMEM((3 * R, H), BF16),
            pltpu.VMEM((H, 3 * R), BF16),
        ],
        compiler_params=params(),
    )(*inputs)
    scalar_parts = lax.all_to_all(part.reshape(split, channels, atoms + LANES), "feat", 0, 0)

    kinds = shared_scratch(atoms)
    batch = OFFSETS * rows_each
    names = ["mask", "near", "near_last"] + ["tall"] * 3 + ["many", "stage2", "close"]
    radial, geo = edge_call(
        geometry_kernel,
        atoms,
        (scalars, rows),
        (),
        [],
        [((SPAN, batch, 2 * LANES), BF16), ((SPAN, GEO, batch, LANES), BF16)],
        [kinds[name] for name in names],
    )
    names = ["weights", "weights", "near", "near_last", "stage4", "loose4"]
    names += ["loose_low", "pre", "grad_pre", "line", "wide2", "wide2f", "line4", "line1"]
    names += ["low"] * 4 + ["low"] * 7 + ["first"] * 7
    scalar_sum, grads_b, pos_b, grad_filters_b = edge_call(
        scalar_kernel,
        atoms,
        (scalars, rows, w_key_filter, w_value_filter[0], scalar_parts),
        (radial, geo),
        [
            ((R, atoms), BF16),
            ((3 * R, atoms), BF16),
            ((8, atoms), F32),
            ((LANES, 2 * LANES), F32),
        ],
        [],
        [kinds[name] for name in names],
    )
    gathered = lax.all_gather(scalar_sum, "feat", axis=0, tiled=True)

    inputs = (
        scalars, features, stat, vectors, cot_features, cot_vectors, gathered, grads_b,
        gain, bias, w_vector, w_output, grad_filters_b,
    )
    new_features, delta, squares, send_vec, flat_early = pl.pallas_call(
        functools.partial(layer_kernel, atoms),
        out_shape=[
            jax.ShapeDtypeStruct((R, atoms), BF16),
            jax.ShapeDtypeStruct((3, R, atoms), F32),
            jax.ShapeDtypeStruct((8, atoms), F32),
            jax.ShapeDtypeStruct((split, 3 * R, atoms), BF16),
            jax.ShapeDtypeStruct((EARLY, H), F32),
        ],
        in_specs=[whole(pltpu.SMEM)] + [whole()] * (len(inputs) - 1),
        out_specs=[whole()] * 5,
        scratch_shapes=[
            pltpu.VMEM((H, 3 * R), BF16),
            pltpu.VMEM((3 * R, H), BF16),
            pltpu.VMEM((3 * R, H), BF16),
        ],
        compiler_params=params(),
    )(*inputs)
    share = (EARLY + LATE) // count
    got_vec = lax.all_to_all(send_vec, "feat", 0, 0)

    names = ["weights", "near", "near_last", "stage8", "loose5"]
    names += ["pre", "grad_pre", "line", "line3"]
    names += ["low"] * 7 + ["low"] * 10 + ["first"] * 10
    rows, _ = lax.optimization_barrier((rows, squares))
    sums, back, grads_a, pos_a, grad_filters_a = edge_call(
        vector_kernel,
        atoms,
        (scalars, rows, w_value_filter[1], w_value_filter[2]),
        (radial, geo),
        [
            ((3, R, atoms), F32),
            ((3, R, atoms), F32),
            ((2 * R, atoms), BF16),
            ((8, atoms), F32),
            ((LANES, 2 * LANES), F32),
        ],
        [],
        [kinds[name] for name in names],
    )

    delta, got_vec = lax.optimization_barrier((delta, got_vec))
    inputs = (
        scalars, features, stat, vectors, delta, squares, sums, grads_b, grads_a, pos_a, pos_b,
        mask, gain, bias, w_query, w_key, w_value, grad_filters_a,
    )
    new_vectors, send, flat_late = pl.pallas_call(
        functools.partial(normal_kernel, atoms),
        out_shape=[
            jax.ShapeDtypeStruct((3, R, atoms), BF16),
            jax.ShapeDtypeStruct((split, R + EXTRAS, atoms), BF16),
            jax.ShapeDtypeStruct((LATE, H), BF16),
        ],
        in_specs=[whole(pltpu.SMEM)] + [whole()] * (len(inputs) - 1),
        out_specs=[whole()] * 3,
        scratch_shapes=[pltpu.VMEM((H, 5 * R), BF16), pltpu.VMEM((2 * R, H), F32)],
        compiler_params=params(),
    )(*inputs)
    got = lax.all_to_all(send, "feat", 0, 0)
    flat = jnp.concatenate([flat_early.astype(BF16), flat_late], axis=0)
    shares = lax.all_to_all(flat.reshape(count, share, H), "atoms", 0, 0)

    inputs = (
        scalars, got, got_vec, features, stat, gain, cot_features, cot_vectors, back, mask,
    )
    grad_features, grad_vectors, grad_positions, small = pl.pallas_call(
        functools.partial(final_kernel, atoms),
        out_shape=[
            jax.ShapeDtypeStruct((R, atoms), F32),
            jax.ShapeDtypeStruct((3, R, atoms), F32),
            jax.ShapeDtypeStruct((3, atoms), F32),
            jax.ShapeDtypeStruct((16, H), F32),
        ],
        in_specs=[whole(pltpu.SMEM)] + [whole()] * (len(inputs) - 1),
        out_specs=[whole()] * 4,
        compiler_params=params(),
    )(*inputs)
    mine = jnp.concatenate([jnp.sum(shares.astype(F32), axis=0), small], axis=0).astype(BF16)
    every = everywhere(mine, "atoms")
    shapes = [
        (1, R), (1, R), (R, H), (R, H), (3, R, H), (3, R, H), (3, R, H), (R, R), (3, R, R), (1, 8),
    ]
    grads = pl.pallas_call(
        functools.partial(unpack_kernel, share),
        out_shape=[jax.ShapeDtypeStruct(shape, F32) for shape in shapes],
        in_specs=[whole()],
        out_specs=[whole()] * len(shapes),
        compiler_params=params(),
    )(every)
    return (
        new_features,
        new_vectors,
        grad_features,
        grad_vectors,
        grad_positions,
        grads[0].reshape(R),
        grads[1].reshape(R),
        grads[2].T,
        grads[3].T,
        jnp.swapaxes(grads[4], 1, 2),
        jnp.swapaxes(grads[5], 1, 2),
        jnp.swapaxes(grads[6], 1, 2),
        grads[7],
        grads[8],
        grads[9][0, :4],
    )


def solution(mesh):
    in_specs = (
        P(None, "atoms"),
        P(None, None, "atoms"),
        P(None, "atoms"),
        P("atoms"),
        P(None, "atoms"),
        P(),
        P(),
        P(None, "feat"),
        P(None, "feat"),
        P(None, None, "feat"),
        P(None, None, "feat"),
        P(None, None, "feat"),
        P(None, "feat"),
        P(None, None, "feat"),
        P("feat", "atoms"),
        P(None, "feat", "atoms"),
    )
    out_specs = (
        P("feat", "atoms"),
        P(None, "feat", "atoms"),
        P("feat", "atoms"),
        P(None, "feat", "atoms"),
        P(None, "atoms"),
        P("feat"),
        P("feat"),
        P(None, "feat"),
        P(None, "feat"),
        P(None, None, "feat"),
        P(None, None, "feat"),
        P(None, None, "feat"),
        P(None, "feat"),
        P(None, None, "feat"),
        P(),
    )
    return jax.shard_map(
        per_device, mesh=mesh, in_specs=in_specs, out_specs=out_specs, check_vma=False
    )
```

```python
import functools
import math

import jax
import jax.numpy as jnp
from jax import lax
from jax.experimental import pallas as pl
from jax.experimental.pallas import tpu as pltpu
from jax.sharding import PartitionSpec as P

H = 256
HEADS = 8
HEAD = H // HEADS
R = 64
MOL = 29
HALO = 32
CUTOFF = 5.0
EPSILON = 1e-05
F32 = jnp.float32
BF16 = jnp.bfloat16

LANE_GROUPS = 2
ROW_GROUPS = 3
SPAN = 5
OFFSETS = 14
STEPS = SPAN + OFFSETS
SUB = 16
LANES = 128

W01, W2V2, C01, C2_COUNT, POS, QK, V0_COUNT, V12, VEC01, VEC2 = range(10)
GROUP_ROWS = 352
EARLY = 9 * R + R // 2
LATE = 2 * R + R // 2
EXTRAS = 16


BLOCK = 8
WINDOW = 256


def block_list(molecules, rows):
    full, rest = divmod(molecules, BLOCK)
    wide = ROW_GROUPS * BLOCK
    out = [(n * wide, wide, BLOCK) for n in range(full)]
    if rows > full * wide:
        out.append((full * wide, rows - full * wide, rest))
    return out


def row_parts(shape, axis, size):
    row = lax.broadcasted_iota(jnp.int32, shape, axis)
    group = jnp.zeros(shape, jnp.int32)
    for g in range(1, ROW_GROUPS):
        group = jnp.where(row >= g * size, g, group)
    return group, row - group * size, row < ROW_GROUPS * size


def set_distances(target, width, size):
    for r in range(LANE_GROUPS):

        def step(t, _, r=r):
            group, molecule, held = row_parts((width, WINDOW), 0, size)
            spot = t + SPAN * (LANE_GROUPS * group + r)
            spot = jnp.where(spot >= MOL, spot - MOL, spot)
            lane = lax.broadcasted_iota(jnp.int32, (width, WINDOW), 1)
            value = jnp.where(held, molecule * MOL + spot - lane, -(10**6))
            target[r, pl.ds(t * width, width), :] = value
            return 0

        lax.fori_loop(0, STEPS, step, 0)


def windows(blocks, distances, start, tall):
    for n, (first, width, size) in enumerate(blocks):
        atom = start + n * BLOCK * MOL
        base = jnp.minimum(atom // SUB * SUB, tall - WINDOW)
        base = pl.multiple_of(base, SUB)
        chosen = distances[0] if size == BLOCK else distances[1]
        ones = [jnp.where(chosen[r] == base - atom, 1.0, 0.0).astype(BF16) for r in (0, 1)]
        yield first, width, pl.ds(base, WINDOW), ones


def spread(source, lanes, stage, blocks, distances, start):
    for first, width, here, ones in windows(blocks, distances, start, source.shape[0]):
        given = source[here, lanes]
        a, b = dot(ones[0], given), dot(ones[1], given)
        low = lax.broadcasted_iota(jnp.int32, (a.shape[0], LANES), 1) < R
        for n in range(a.shape[1] // LANES):
            left, right = a[:, n * LANES : (n + 1) * LANES], b[:, n * LANES : (n + 1) * LANES]
            one = jnp.where(low, left, pltpu.roll(right, R, 1))
            two = jnp.where(low, pltpu.roll(left, R, 1), right)
            stage[2 * n, :, first : first + width] = one.reshape(STEPS, width, LANES)
            stage[2 * n + 1, :, first : first + width] = two.reshape(STEPS, width, LANES)


def spread_positions(source, lanes, targets, blocks, distances, start):
    row = lax.broadcasted_iota(jnp.int32, (LANES, 3 * LANES), 0)
    lane = lax.broadcasted_iota(jnp.int32, (LANES, 3 * LANES), 1)
    axis = jnp.where(lane >= 2 * LANES, 2, jnp.where(lane >= LANES, 1, 0))
    mine = (row >= 3 * axis) & (row < 3 * axis + 3)
    low = lane - axis * LANES < R
    wide = [jnp.where(mine & (low == (r == 0)), 1.0, 0.0).astype(BF16) for r in (0, 1)]
    for first, width, here, ones in windows(blocks, distances, start, source.shape[0]):
        given = source[here, lanes]
        total = 0.0
        for r in (0, 1):
            total = total + dot(dot(ones[r], given).astype(BF16), wide[r])
        for d, target in enumerate(targets):
            value = total[:, d * LANES : (d + 1) * LANES]
            target[:, first : first + width] = value.reshape(STEPS, width, LANES)


def collect(sources, target, blocks, distances, start):
    target[...] = jnp.zeros(target.shape, F32)
    units = []
    for first, width, here, ones in windows(blocks, distances, start, target.shape[0]):
        units.append((first, width, here, ones))
    at = 0
    while at < len(units):
        group = units[at : at + 2] if units[at][0] % SUB == 0 and at + 1 < len(units) else None
        if group is None or (group[0][1] + group[1][1]) % SUB:
            group = units[at : at + 1]
        at += len(group)
        first = group[0][0]
        size = sum(g[1] for g in group)
        blocks_in = []
        for partner, carry in sources:
            value = partner[:, first : first + size].astype(F32)
            start_part = value[:SPAN] + carry[:, first : first + size]
            blocks_in.append(jnp.concatenate([start_part, value[SPAN:]], axis=0))
        for f, width, here, ones in group:
            parts = ([], [])
            for n in range(0, len(sources), 2):
                a = blocks_in[n][:, f - first : f - first + width].reshape(STEPS * width, LANES)
                b = blocks_in[n + 1][:, f - first : f - first + width]
                b = b.reshape(STEPS * width, LANES)
                low = lax.broadcasted_iota(jnp.int32, a.shape, 1) < R
                parts[0].append(jnp.where(low, a, pltpu.roll(b, R, 1)).astype(BF16))
                parts[1].append(jnp.where(low, pltpu.roll(a, R, 1), b).astype(BF16))
            total = 0.0
            for r in (0, 1):
                total = total + dot_tn(ones[r], jnp.concatenate(parts[r], axis=1))
            target[here, :] = target[here, :] + total


def row_masks(owned, start, blocks, atoms):
    for n, (at, width, size) in enumerate(blocks):
        _, molecule, _ = row_parts((width, LANES), 0, size)
        first = start - HALO + (n * BLOCK + molecule) * MOL
        owned[at : at + width] = jnp.where((first >= 0) & (first < atoms), 1.0, 0.0)


def set_multiplicities(count, target, blocks, rows):
    lane = lax.broadcasted_iota(jnp.int32, (rows, LANES), 1)
    inner = jnp.where(lane >= R, lane - R, lane)
    last = []
    for _, width, size in blocks:
        last.append(row_parts((width, LANES), 0, size)[0])
    doubled = (jnp.concatenate(last, axis=0) == ROW_GROUPS - 1) & (lane >= R)
    for t in range(SPAN):
        value = jnp.where(inner < 32, count[t], 0.0)
        for k in range(1, OFFSETS + 1):
            value = jnp.where(inner == 32 + k, count[t + k], value)
        if t == SPAN - 1:
            value = jnp.where(doubled, 0.0, value)
        target[t] = value


def dot(a, b):
    return jnp.dot(a, b, preferred_element_type=F32)


def dot_tn(a, b):
    return lax.dot_general(a, b, (((0,), (0,)), ((), ())), preferred_element_type=F32)


def dot_nt(a, b):
    return lax.dot_general(a, b, (((1,), (1,)), ((), ())), preferred_element_type=F32)


COSINE = (0.9999999998, -0.04934802137, 0.000405870916, -1.335212003e-06, 2.349373138e-09, -2.43963243e-12)

GEO_ENVELOPE, GEO_BEND, GEO_INVERSE, GEO_INTO, GEO_FROM, GEO_WAY, GEO_SLOPE, GEO_OWN = 0, 1, 2, 3, 4, 5, 8, 9
GEO = 10


def geometry(pos, many, t, rows, owned, radial, geo):
    inv_space = (R - 1) / CUTOFF

    def step(k, _):
        for o, size in halves(rows):
            here = pl.ds(pl.multiple_of(k * rows + o, SUB), size)
            part = slice(o, o + size)
            off = [p[t, part] - p[t + 1 + k, part] for p in pos]
            mine = owned[part].astype(BF16)
            close = many[t, part]
            lane = lax.broadcasted_iota(jnp.int32, (size, LANES), 1)
            base = jnp.where(lane >= R, R, 0)
            centre = (lane - base).astype(F32)
            near = base + (k + 1)
            square = off[0] * off[0] + off[1] * off[1] + off[2] * off[2]
            clamped = jnp.maximum(square, 0.01)
            inverse = lax.rsqrt(clamped)
            c = COSINE[-1]
            for term in COSINE[-2::-1]:
                c = c * clamped + term
            c = jnp.where(clamped < CUTOFF * CUTOFF, c, 0.0)
            envelope = c * c
            y = jnp.maximum(1.0 - envelope, 1e-30)
            bend = ((-math.pi / CUTOFF) * c) * (y * lax.rsqrt(y))
            u = (clamped * inverse) * inv_space - centre
            bump = jnp.exp(-0.5 * (u * u))
            value = bump * envelope
            high = value.astype(BF16)
            slope = bump * bend - inv_space * (u * value)
            radial[here, :LANES] = high
            radial[here, LANES:] = (value - high.astype(F32)).astype(BF16)
            geo[GEO_OWN, here, :] = high * mine
            geo[GEO_SLOPE, here, :] = slope.astype(BF16)
            geo[GEO_BEND, here, :] = bend.astype(BF16)
            geo[GEO_ENVELOPE, here, :] = envelope.astype(BF16)
            for d in range(3):
                geo[GEO_WAY + d, here, :] = (off[d] * inverse).astype(BF16)
            signed = jnp.where(square > 0.01, inverse, -inverse)
            geo[GEO_INVERSE, here, :] = signed.astype(BF16)
            into = jnp.take_along_axis(close, near, axis=1)
            out_of = jnp.take_along_axis(close, near + 32, axis=1)
            geo[GEO_INTO, here, :] = into.astype(BF16)
            geo[GEO_FROM, here, :] = out_of.astype(BF16)
        return 0

    lax.fori_loop(0, OFFSETS, step, 0)


def halves(rows):
    tiles = rows // SUB
    first = (tiles + 1) // 2 * SUB
    return ((0, first), (first, rows - first))


def set_filters(weights_ref, filter_1, filter_2):
    weights_ref[...] = jnp.zeros(weights_ref.shape, BF16)
    for f, ref in enumerate((filter_1, filter_2)):
        half = ref[...] * jnp.asarray(0.5, BF16)
        for part in range(2):
            for g in range(LANE_GROUPS):
                down = part * LANES + g * R
                at = f * LANES + g * R
                weights_ref[down : down + R, at : at + R] = half


def gate(h):
    t = jnp.tanh(h)
    u = 1.0 + t
    f = h * u
    return f.astype(BF16), (u + f * (1.0 - t)).astype(BF16)


def carried(rows, t, totals, group, body):
    def outer(s, _):
        o = pl.multiple_of(s * SUB, SUB)
        block = pl.ds(o, SUB)
        ii = (t, block)
        sums = None
        for k in range(0, OFFSETS, group):
            loaded = []
            for n in range(k, k + group):
                here = pl.ds(o + n * rows, SUB)
                loaded.append(body(o, here, ii, (t + 1 + n, block), n))
            done = [f() for f in loaded]
            given = [one for one, _ in done]
            while len(given) > 1:
                left = given[len(given) // 2 * 2 :]
                pairs = zip(given[0::2], given[1::2])
                given = [[x + y for x, y in zip(a, b)] for a, b in pairs] + left
            total = [x.astype(F32) for x in given[0]]
            sums = total if sums is None else [x + y for x, y in zip(sums, total)]
            for _, stores in done:
                for ref, index, value in stores:
                    ref[index] = value
        for total, value in zip(totals, sums):
            total[ii] = value
        return 0

    lax.fori_loop(0, rows // SUB, outer, 0)


def geometry_kernel(
    molecules, rows, atoms,
    scalars, rows_ref, radial_out, geo_out, owned, near, near_last, px, py, pz, many, stage,
):
    t = pl.program_id(0)
    start = scalars[0]
    blocks = block_list(molecules, rows)
    distances = (near, near_last)

    @pl.when(t == 0)
    def _():
        row_masks(owned, start, blocks, atoms)
        set_distances(near, blocks[0][1], blocks[0][2])
        set_distances(near_last, blocks[-1][1], blocks[-1][2])
        lanes = slice(POS * LANES, (POS + 1) * LANES)
        spread_positions(rows_ref, lanes, (px, py, pz), blocks, distances, start)
        lanes = slice(C2_COUNT * LANES, (C2_COUNT + 1) * LANES)
        spread(rows_ref, lanes, stage, blocks, distances, start)
        set_multiplicities(stage.at[1], many, blocks, rows)

    geometry((px, py, pz), many, t, rows, owned, radial_out.at[0], geo_out.at[0])


def vector_kernel(
    molecules, rows, atoms,
    scalars, rows_ref, filter_1, filter_2, radial_in, geo_in, pull_in,
    sums_ref, back_ref, grads_ref, pos_out, grad_w_ref,
    weights_ref, near, near_last, stage, loose, pre, grad_pre,
    grad_radial, grad_ways,
    w0, w1, w2, v2, c0, c1, c2,
    s0, s1, s2, a0, a1, a2, gv, gx, gy, gz,
    fs0, fs1, fs2, fa0, fa1, fa2, fgv, fgx, fgy, fgz,
):
    t = pl.program_id(0)
    start = scalars[0]
    own = slice(HALO, HALO + atoms)
    radial, geo = radial_in.at[0], geo_in.at[0]
    w, c, g_pos = (w0, w1, w2), (c0, c1, c2), (gx, gy, gz)
    sums, backs = (s0, s1, s2), (a0, a1, a2)
    blocks = block_list(molecules, rows)
    distances = (near, near_last)

    @pl.when(t == 0)
    def _():
        set_filters(weights_ref, filter_1, filter_2)
        set_distances(near, blocks[0][1], blocks[0][2])
        set_distances(near_last, blocks[-1][1], blocks[-1][2])
        lanes = slice(W01 * LANES, (C2_COUNT + 1) * LANES)
        spread(rows_ref, lanes, stage, blocks, distances, start)
        for n, target in enumerate((w0, w1, w2, v2, c0, c1, c2)):
            target[...] = stage[n].astype(BF16)
        for total in (s0, s1, s2, a0, a1, a2, gv, gx, gy, gz):
            total[...] = jnp.zeros(total.shape, BF16)
        grad_w_ref[...] = jnp.zeros(grad_w_ref.shape, F32)

    pre[...] = dot(radial[...], weights_ref[...])

    def channel(o, here, ii, jj, k):
        h1, h2 = pre[here, :LANES], pre[here, LANES:]
        ni, nj = geo[GEO_INTO, here, :], geo[GEO_FROM, here, :]
        v2i, v2j = v2[ii], v2[jj]
        ways = [geo[GEO_WAY + d, here, :] for d in range(3)]
        wi, wj = [w[d][ii] for d in range(3)], [w[d][jj] for d in range(3)]
        ci, cj = [c[d][ii] for d in range(3)], [c[d][jj] for d in range(3)]
        old_sums = [sums[d][jj] for d in range(3)]
        old_backs = [backs[d][jj] for d in range(3)]
        old_gv = gv[jj]

        def compute():
            f1, d1 = gate(h1)
            f2, d2 = gate(h2)
            f1i, f1j, f2i, f2j = f1 * ni, f1 * nj, f2 * ni, f2 * nj
            msg_i, msg_j = f2i * v2j, f2j * v2i
            stores, sum_i, back_i = [], [], []
            along_i = along_j = across_i = across_j = None
            for d in range(3):
                way = ways[d]
                sum_i.append(f1i * wj[d] + msg_i * way)
                stores.append((sums[d], jj, old_sums[d] + (f1j * wi[d] - msg_j * way)))
                stores.append((backs[d], jj, old_backs[d] + f1i * ci[d]))
                back_i.append(f1j * cj[d])
                grad = ci[d] * msg_i - cj[d] * msg_j
                stores.append((grad_ways, (d, here, slice(None)), grad))
                new = (ci[d] * way, cj[d] * way, ci[d] * wj[d], cj[d] * wi[d])
                if d == 0:
                    along_i, along_j, across_i, across_j = new
                else:
                    along_i, along_j = along_i + new[0], along_j + new[1]
                    across_i, across_j = across_i + new[2], across_j + new[3]
            stores.append((gv, jj, old_gv + f2i * along_i))
            g1 = ni * across_i + nj * across_j
            g2 = ni * along_i * v2j - nj * along_j * v2i
            stores.append((grad_pre, (here, slice(0, LANES)), g1 * d1))
            stores.append((grad_pre, (here, slice(LANES, None)), g2 * d2))
            return sum_i + back_i + [-(f2j * along_j)], stores

        return compute

    carried(rows, t, (fs0, fs1, fs2, fa0, fa1, fa2, fgv), 2, channel)
    grad_radial[...] = dot_nt(grad_pre[...], weights_ref[:LANES])
    grad_w_ref[...] = grad_w_ref[...] + dot_tn(geo[GEO_OWN], grad_pre[...])

    def turn(o, here, ii, jj, k):
        ways = [geo[GEO_WAY + d, here, :] for d in range(3)]
        grads = [grad_ways[d, here, :] for d in range(3)]
        grad, slope = grad_radial[here, :], geo[GEO_SLOPE, here, :]
        signed, more = geo[GEO_INVERSE, here, :], pull_in[0, here, :]
        old = [g[jj] for g in g_pos]

        def compute():
            inverse = jnp.abs(signed)
            turned = [g * inverse for g in grads]
            along = ways[0] * turned[0] + ways[1] * turned[1] + ways[2] * turned[2]
            pull = jnp.where(signed > 0, grad.astype(BF16) * slope + more - along, 0)
            out = [turned[d] + ways[d] * pull for d in range(3)]
            return out, [(g_pos[d], jj, old[d] - out[d]) for d in range(3)]

        return compute

    carried(rows, t, (fgx, fgy, fgz), 7, turn)

    @pl.when(t == SPAN - 1)
    def _():
        low = lax.broadcasted_iota(jnp.int32, (atoms, LANES), 1) < R
        totals = (s0, s1, s2, gv, a0, a1, a2, gx, gy, gz)
        firsts = (fs0, fs1, fs2, fgv, fa0, fa1, fa2, fgx, fgy, fgz)
        collect(tuple(zip(totals, firsts)), loose, blocks, distances, start)
        both = loose[own, :LANES].T
        sums_ref[0] = both[:R]
        sums_ref[1] = both[R:]
        both = loose[own, LANES : 2 * LANES].T
        sums_ref[2] = both[:R]
        grads_ref[R:] = both[R:].astype(BF16)

        def kept(n):
            return rows_ref[own, n * LANES : (n + 1) * LANES].astype(F32)

        v12 = kept(V12)
        v11 = jnp.where(low, v12, pltpu.roll(v12, R, 1))
        back = loose[own, 2 * LANES : 3 * LANES]
        both = (back * v11).T
        back_ref[0] = both[:R]
        back_ref[1] = both[R:]
        partial = back * kept(VEC01)
        partial = partial + pltpu.roll(partial, R, 1)
        back = loose[own, 3 * LANES : 4 * LANES]
        back_ref[2] = (back * v11).T[:R]
        partial = partial + back * kept(VEC2)
        grads_ref[:R] = partial.T[:R].astype(BF16)
        pos_out[...] = jnp.zeros(pos_out.shape, F32)
        pos_out[0:1] = jnp.sum(back.T[R:], axis=0, keepdims=True)
        both = loose[own, 4 * LANES :].T
        pos_out[1:2] = jnp.sum(both[:R], axis=0, keepdims=True)
        pos_out[2:3] = jnp.sum(both[R:], axis=0, keepdims=True)


def scalar_kernel(
    molecules, rows, atoms,
    scalars, rows_ref, filter_1, filter_2, scalar_parts, radial_in, geo_in,
    sum_ref, grads_ref, grad_w_ref, pull_out,
    weights_ref, heads_ref, near, near_last, stage, loose, loose_low, pre,
    grad_pre, grad_radial, products, sums, gates, bends,
    q, key, v0, gs,
    ss, gq, gk, g0,
    fss, fgq, fgk, fg0,
):
    t = pl.program_id(0)
    start = scalars[0]
    own = slice(HALO, HALO + atoms)
    radial, geo = radial_in.at[0], geo_in.at[0]
    blocks = block_list(molecules, rows)
    distances = (near, near_last)

    @pl.when(t == 0)
    def _():
        set_filters(weights_ref, filter_1, filter_2)
        row = lax.broadcasted_iota(jnp.int32, (2 * LANES, 2 * LANES), 0)
        lane = lax.broadcasted_iota(jnp.int32, (2 * LANES, 2 * LANES), 1)
        heads_ref[...] = jnp.where(row // HEAD == lane // HEAD, 1.0, 0.0).astype(BF16)
        set_distances(near, blocks[0][1], blocks[0][2])
        set_distances(near_last, blocks[-1][1], blocks[-1][2])
        lanes = slice(QK * LANES, (V0_COUNT + 1) * LANES)
        spread(rows_ref, lanes, stage, blocks, distances, start)
        for n, target in enumerate((q, key, v0)):
            target[...] = stage[n].astype(BF16)
        summed = scalar_parts[0].astype(F32)
        for f in range(1, scalar_parts.shape[0]):
            summed = summed + scalar_parts[f].astype(F32)
        summed = jnp.concatenate([summed, jnp.zeros_like(summed)], axis=0).T.astype(BF16)
        loose_low[own] = summed[:atoms]
        loose_low[:HALO] = summed[atoms : atoms + HALO]
        loose_low[HALO + atoms : 2 * HALO + atoms] = summed[atoms + HALO : atoms + 2 * HALO]
        end = 2 * HALO + atoms
        loose_low[end:] = jnp.zeros((loose_low.shape[0] - end, LANES), BF16)
        spread(loose_low, slice(None), stage, blocks, distances, start)
        gs[...] = stage[0].astype(BF16)
        for total in (ss, gq, gk, g0):
            total[...] = jnp.zeros(total.shape, BF16)
        grad_w_ref[...] = jnp.zeros(grad_w_ref.shape, F32)

    pre[...] = dot(radial[...], weights_ref[...])

    def multiply(k, _):
        for o, size in halves(rows):
            here = pl.ds(pl.multiple_of(k * rows + o, SUB), size)
            ii, jj = (t, slice(o, o + size)), (t + 1 + k, slice(o, o + size))
            fk, dk = gate(pre[here, :LANES])
            f0, d0 = gate(pre[here, LANES:])
            k_ij, k_ji = q[ii] * key[jj] * fk, q[jj] * key[ii] * fk
            s_ij, s_ji = gs[ii] * v0[jj] * f0, gs[jj] * v0[ii] * f0
            gates[0, here, :] = fk
            gates[1, here, :] = f0
            gates[2, here, :] = dk
            gates[3, here, :] = d0
            products[0, here, :LANES] = k_ij
            products[0, here, LANES:] = k_ji
            products[1, here, :LANES] = s_ij
            products[1, here, LANES:] = s_ji
        return 0

    lax.fori_loop(0, OFFSETS, multiply, 0)
    sums[0] = dot(products[0], heads_ref[...])
    sums[1] = dot(products[1], heads_ref[...])

    def channel(o, here, ii, jj, k):
        fk, f0, dk, d0 = [gates[n, here, :] for n in range(4)]
        envelope, bend = geo[GEO_ENVELOPE, here, :], geo[GEO_BEND, here, :]
        side_in = []
        for side in range(2):
            lanes = slice(side * LANES, (side + 1) * LANES)
            m = geo[GEO_INTO + side, here, :]
            h, o_ = (ii, jj) if side == 0 else (jj, ii)
            side_in.append(
                (m, sums[0, here, lanes], sums[1, here, lanes])
                + (q[h], key[o_], gs[h], v0[o_])
            )
        old = [ref[jj] for ref in (g0, gk, ss, gq)]

        def compute():
            gives, news = [], []
            for m, score, g_att, qh, kt, gh, vt in side_in:
                act, rise = gate(0.5 * score)
                g_att = g_att.astype(BF16)
                weight = m * envelope
                att = act * weight
                g_score = g_att * (0.5 * rise) * weight
                lift = m * (g_att * act)
                bv, dv = f0 * att, fk * g_score
                gives.append((vt * bv, kt * dv, gh * bv, qh * dv))
                news.append((qh * kt * g_score, gh * vt * att, lift))
            one, two = gives
            new = [x + y for x, y in zip(*news)]
            stores = [
                (ref, jj, x + y)
                for ref, x, y in zip((g0, gk, ss, gq), old, (one[2], one[3], two[0], two[1]))
            ]
            stores.append((grad_pre, (here, slice(0, LANES)), new[0] * dk))
            stores.append((grad_pre, (here, slice(LANES, None)), new[1] * d0))
            stores.append((bends, (here, slice(None)), new[2] * bend * (1.0 / HEAD)))
            return [one[0], one[1], two[2], two[3]], stores

        return compute

    carried(rows, t, (fss, fgq, fg0, fgk), 2, channel)
    grad_radial[...] = dot_nt(grad_pre[...], weights_ref[:LANES])
    grad_w_ref[...] = grad_w_ref[...] + dot_tn(geo[GEO_OWN], grad_pre[...])

    def pull(k, _):
        here = pl.ds(pl.multiple_of(k * rows, SUB), rows)
        grad = grad_radial[here, :].astype(BF16)
        pull_out[0, here, :] = grad * geo[GEO_SLOPE, here, :] + bends[here, :]
        return 0

    lax.fori_loop(0, OFFSETS, pull, 0)

    @pl.when(t == SPAN - 1)
    def _():
        totals = (ss, g0, gq, gk)
        firsts = (fss, fg0, fgq, fgk)
        collect(tuple(zip(totals, firsts)), loose, blocks, distances, start)
        both = loose[own, :LANES].T
        sum_ref[...] = both[:R].astype(BF16)
        grads_ref[2 * R :] = both[R:].astype(BF16)
        grads_ref[: 2 * R] = loose[own, LANES : 2 * LANES].T.astype(BF16)


def whole(memory=pltpu.VMEM):
    return pl.BlockSpec(memory_space=memory)


def params(mib=60):
    return pltpu.CompilerParams(vmem_limit_bytes=mib * 1024 * 1024)


def edge_sizes(atoms):
    molecules = (atoms + 2 * (MOL - 1)) // MOL
    full, rest = divmod(molecules, BLOCK)
    rows = full * ROW_GROUPS * BLOCK + -(-ROW_GROUPS * rest // BLOCK) * BLOCK
    rows = -(-rows // SUB) * SUB
    tall = -(-(HALO + molecules * MOL) // SUB) * SUB
    return molecules, rows, tall


def by_step(shape):
    zeros = (0,) * (len(shape) - 1)
    return pl.BlockSpec((1,) + shape[1:], lambda t: (t,) + zeros)


def fixed(shape):
    zeros = (0,) * len(shape)
    return pl.BlockSpec(shape, lambda t: zeros)


def edge_call(kernel, atoms, inputs, stepped_in, outs, stepped_out, scratch):
    molecules, rows, _ = edge_sizes(atoms)
    return pl.pallas_call(
        functools.partial(kernel, molecules, rows, atoms),
        grid=(SPAN,),
        out_shape=[jax.ShapeDtypeStruct(s, kind) for s, kind in outs + stepped_out],
        in_specs=[whole(pltpu.SMEM)]
        + [fixed(x.shape) for x in inputs[1:]]
        + [by_step(x.shape) for x in stepped_in],
        out_specs=[fixed(s) for s, _ in outs] + [by_step(s) for s, _ in stepped_out],
        scratch_shapes=[pltpu.VMEM(s, kind) for s, kind in scratch],
        compiler_params=params(),
        cost_estimate=pl.CostEstimate(
            flops=20 * 10**9, bytes_accessed=40 * 10**6, transcendentals=10**7
        ),
    )(*inputs, *stepped_in)


def shared_scratch(atoms):
    molecules, rows, tall = edge_sizes(atoms)
    batch = OFFSETS * rows
    blocks = block_list(molecules, rows)
    return {
        "weights": ((2 * LANES, 2 * LANES), BF16),
        "many": ((SPAN, rows, LANES), F32),
        "stage2": ((2, STEPS, rows, LANES), F32),
        "mask": ((rows, LANES), F32),
        "near": ((LANE_GROUPS, STEPS * blocks[0][1], WINDOW), jnp.int32),
        "near_last": ((LANE_GROUPS, STEPS * blocks[-1][1], WINDOW), jnp.int32),
        "stage8": ((8, STEPS, rows, LANES), F32),
        "stage4": ((4, STEPS, rows, LANES), F32),
        "loose5": ((tall, 5 * LANES), F32),
        "loose2": ((tall, 2 * LANES), F32),
        "loose_low": ((tall, LANES), BF16),
        "tall": ((STEPS, rows, LANES), F32),
        "low": ((STEPS, rows, LANES), BF16),
        "first": ((SPAN, rows, LANES), F32),
        "pre": ((batch, 2 * LANES), F32),
        "grad_pre": ((batch, 2 * LANES), BF16),
        "line": ((batch, LANES), F32),
        "line2": ((2, batch, LANES), BF16),
        "line3": ((3, batch, LANES), BF16),
        "line4": ((4, batch, LANES), BF16),
        "line1": ((batch, LANES), BF16),
        "wide2": ((2, batch, 2 * LANES), BF16),
        "wide2f": ((2, batch, 2 * LANES), F32),
    }


def offsets_in_block(neighbours, mask, first):
    lane = lax.broadcasted_iota(jnp.int32, neighbours.shape, 1)
    diff = neighbours - (first + lane)
    return jnp.where(diff < 0, diff + MOL, diff) * mask


def pieces(x):
    a = x.astype(BF16)
    rest = x - a.astype(F32)
    b = rest.astype(BF16)
    return a, b, (rest - b.astype(F32)).astype(BF16)


def edge_groups(features, vectors, cot_f, cot_v, neighbours, mask, positions, first):
    diff = offsets_in_block(neighbours[...], mask[...], first).astype(F32).astype(BF16)
    groups = [jnp.concatenate([features[...], cot_f[...], diff], axis=0)]
    for d in range(3):
        rows = [x.astype(F32) for x in pieces(positions[d : d + 1])]
        rows = jnp.concatenate(rows + [jnp.zeros((29, LANES), F32)], axis=0).astype(BF16)
        groups.append(jnp.concatenate([vectors[d], cot_v[d], rows], axis=0))
    return groups


def halo_kernel(atoms, scalars, *refs):
    row_first = scalars[2]
    lane = lax.broadcasted_iota(jnp.int32, (GROUP_ROWS, LANES), 1)
    for end, at, out in ((0, atoms - LANES, refs[14]), (1, 0, refs[15])):
        groups = edge_groups(*refs[7 * end : 7 * end + 7], row_first + at)
        total = None
        for g, group in enumerate(groups):
            by = (HALO * (g + 1) if end == 0 else HALO * g) % LANES
            moved = group.astype(F32)
            moved = pltpu.roll(moved, by, 1) if by else moved
            total = moved if total is None else jnp.where(lane >= HALO * g, moved, total)
        out[...] = total.astype(BF16)


def halo_call(atoms, scalars, arrays):
    specs = []
    for at in (atoms // LANES - 1, 0):
        for x in arrays:
            shape = x.shape[:-1] + (LANES,)
            index = (0,) * (x.ndim - 1) + (at,)
            specs.append(pl.BlockSpec(shape, lambda *_, index=index: index))
    out = jax.ShapeDtypeStruct((GROUP_ROWS, LANES), BF16)
    return pl.pallas_call(
        functools.partial(halo_kernel, atoms),
        grid=(1,),
        out_shape=[out, out],
        in_specs=[whole(pltpu.SMEM)] + specs,
        out_specs=[whole(), whole()],
        compiler_params=params(),
    )(scalars, *arrays, *arrays)


def column(row):
    return jnp.broadcast_to(row, (8, row.shape[1])).T[:, :1]


def normalised(f):
    mean = jnp.mean(f, axis=0, keepdims=True)
    centred = f - mean
    inv = lax.rsqrt(jnp.mean(centred * centred, axis=0, keepdims=True) + EPSILON)
    return centred * inv, mean, inv


def dense_kernel(
    atoms,
    scalars, features, vectors, cot_f, cot_v, neighbours, mask, positions, low_ref, high_ref,
    gain_ref, bias_ref, w_query, w_key, w_value, w_vector, w_output,
    rows_ref, part_ref, stat_ref,
    w_qk, w_v0, w_v12, w_vec_t, w_out,
):
    chan_first = pl.multiple_of(scalars[1], R)
    row_first = scalars[2]
    gain, bias = column(gain_ref[...]), column(bias_ref[...])
    w_qk[:R] = w_query[...]
    w_qk[R:] = w_key[...]
    w_v0[:R] = w_value[0]
    w_v0[R:] = jnp.zeros((R, H), BF16)
    w_v12[:R] = w_value[1]
    w_v12[R:] = w_value[2]
    for p in range(3):
        w_vec_t[p * R : (p + 1) * R] = w_vector[p]
    w_out[...] = jnp.concatenate([w_output[p] for p in range(3)], axis=0).astype(F32).T.astype(BF16)

    def block(f, v, cf, cv, own_v, diff, pos):
        width = f.shape[1]
        normed, mean, inv = normalised(f)
        turned = (normed * gain + bias).T.astype(BF16)
        kinds = lax.broadcasted_iota(jnp.int32, (R, width), 0)
        kinds = jnp.where(kinds < 32, kinds, MOL + 32 - kinds).astype(F32)
        counts = jnp.zeros((R, width), F32)
        for s in range(diff.shape[0]):
            counts = counts + jnp.where(diff[s : s + 1] == kinds, 1.0, 0.0)
        none = jnp.zeros((R, width), F32)
        counts = jnp.concatenate([none, counts], axis=0).T
        low = lax.broadcasted_iota(jnp.int32, (width, LANES), 1) < R
        pairs = [None] * 10
        pairs[QK] = dot_nt(turned, w_qk[...])
        pairs[V0_COUNT] = dot_nt(turned, w_v0[...]) + counts
        v12 = dot_nt(turned, w_v12[...]).astype(BF16).astype(F32)
        v11 = jnp.where(low, v12, pltpu.roll(v12, R, 1))
        pairs[V12] = v12
        pairs[VEC01] = jnp.concatenate([own_v[0], own_v[1]], axis=0).T
        pairs[VEC2] = jnp.concatenate([own_v[2], none], axis=0).T
        pairs[W01] = pairs[VEC01] * v11
        pairs[W2V2] = jnp.where(low, pairs[VEC2] * v11, v12)
        pairs[C01] = jnp.concatenate([cv[0], cv[1]], axis=0).T
        pairs[C2_COUNT] = jnp.concatenate([cv[2], none], axis=0).T + counts
        pairs[POS] = jnp.concatenate([pos, jnp.zeros((LANES - 9, width), F32)], axis=0).T
        vec_dot = grad_0 = 0.0
        for d in range(3):
            proj = dot(w_vec_t[...], v[d])
            vec_dot = vec_dot + proj[:R] * proj[R : 2 * R]
            grad_0 = grad_0 + cv[d] * proj[2 * R :]
        grad_out = jnp.concatenate([grad_0, cf * vec_dot, cf], axis=0).astype(BF16)
        part = dot(w_out[...], grad_out)
        return [x.astype(BF16) for x in pairs], part.astype(BF16), mean, inv

    wide = 2 * LANES

    def step(b, _):
        at = pl.multiple_of(b * wide, wide)
        here = pl.ds(at, wide)
        own_v = [vectors[d, pl.ds(chan_first, R), here].astype(F32) for d in range(3)]
        diff = offsets_in_block(neighbours[:, here], mask[:, here], row_first + at)
        places = [p.astype(F32) for d in range(3) for p in pieces(positions[d : d + 1, here])]
        pairs, part, mean, inv = block(
            features[:, here].astype(F32),
            [vectors[d, :, here] for d in range(3)],
            cot_f[:, here].astype(F32),
            [cot_v[d, :, here].astype(F32) for d in range(3)],
            own_v,
            diff.astype(F32),
            jnp.concatenate(places, axis=0),
        )
        there = pl.ds(pl.multiple_of(HALO + at, 2 * SUB), wide)
        for n, pair in enumerate(pairs):
            rows_ref[there, n * LANES : (n + 1) * LANES] = pair
        part_ref[:, here] = part
        stat_ref[0:1, here] = mean
        stat_ref[1:2, here] = inv
        return 0

    lax.fori_loop(0, atoms // wide, step, 0)

    lane = lax.broadcasted_iota(jnp.int32, (GROUP_ROWS, LANES), 1)
    packed_low, packed_high = low_ref[...].astype(F32), high_ref[...].astype(F32)
    groups = []
    for g in range(4):
        a = pltpu.roll(packed_low, (LANES - HALO * g) % LANES, 1) if g else packed_low
        by = (LANES + HALO - HALO * g) % LANES
        b = pltpu.roll(packed_high, by, 1) if by else packed_high
        both = jnp.where(lane < HALO, a, jnp.where(lane < 2 * HALO, b, 0.0))
        groups.append(both)
    pick_rows = lax.broadcasted_iota(jnp.int32, (H, LANES), 0)
    own_v, pos = [], []
    for d in range(3):
        g = groups[1 + d]
        found = g[:R]
        for f in range(1, H // R):
            found = jnp.where(chan_first == f * R, g[f * R : (f + 1) * R], found)
        own_v.append(found)
        pos.append(g[320:323])
    pairs, part, _, _ = block(
        groups[0][:H],
        [groups[1 + d][:H].astype(BF16) for d in range(3)],
        groups[0][H : H + R],
        [groups[1 + d][H : H + R] for d in range(3)],
        own_v,
        groups[0][H + R :],
        jnp.concatenate(pos, axis=0),
    )
    high = HALO + atoms
    tall = rows_ref.shape[0]
    for n, pair in enumerate(pairs):
        lanes = slice(n * LANES, (n + 1) * LANES)
        rows_ref[:HALO, lanes] = pair[:HALO]
        rows_ref[high : high + HALO, lanes] = pair[HALO : 2 * HALO]
        rows_ref[high + HALO :, lanes] = jnp.zeros((tall - high - HALO, LANES), BF16)
    part_ref[:, atoms:] = part


def both_diagonals(grad, f):
    at = f * LANES
    return 0.5 * (grad[:R, at : at + R] + grad[R:, at + R : at + LANES])


def filter_block(grad):
    both = jnp.concatenate([both_diagonals(grad, 0), both_diagonals(grad, 1)], axis=1)
    return jnp.concatenate([both[: R // 2], both[R // 2 :]], axis=1)


def layer_kernel(
    atoms,
    scalars, features, stat, vectors, cot_f, cot_v, gathered, grads_b, gain_ref, bias_ref,
    w_vector, w_output, grad_filters_b,
    feat_out, delta_ref, square_ref, send_ref, flat_ref,
    w_vec, w_vec_t, w_out_t,
):
    chan_first = pl.multiple_of(scalars[1], R)
    gain, bias = column(gain_ref[...]), column(bias_ref[...])
    for p in range(3):
        w_vec_t[p * R : (p + 1) * R] = w_vector[p]
        w_out_t[p * R : (p + 1) * R] = w_output[p]
    w_vec[...] = w_vec_t[...].astype(F32).T.astype(BF16)
    t_vec, t_out, t_b = [flat_ref.at[n * 3 * R : (n + 1) * 3 * R] for n in range(3)]
    flat_ref[...] = jnp.zeros(flat_ref.shape, F32)
    wide = 2 * LANES
    split = send_ref.shape[0]

    def step(b, _):
        at = pl.multiple_of(b * wide, wide)
        here = pl.ds(at, wide)
        all_sums = gathered[:, here]
        outputs = dot(w_out_t[...], all_sums)
        out_0, out_1, out_2 = outputs[:R], outputs[R : 2 * R], outputs[2 * R :]
        cf = cot_f[:, here].astype(F32)
        grad_dot = cf * out_1
        vec_dot = grad_0 = 0.0
        for d in range(3):
            proj = dot(w_vec_t[...], vectors[d, :, here])
            first, second, third = proj[:R], proj[R : 2 * R], proj[2 * R :]
            cv = cot_v[d, :, here].astype(F32)
            vec_dot = vec_dot + first * second
            grad_0 = grad_0 + cv * third
            delta_ref[d, :, here] = third * out_0
            grad_proj = jnp.concatenate(
                [grad_dot * second, grad_dot * first, cv * out_0], axis=0
            ).astype(BF16)
            part = dot(w_vec[...], grad_proj).astype(BF16)
            for f in range(split):
                send_ref[f, d * R : (d + 1) * R, here] = part[f * R : (f + 1) * R]
            t_vec[...] = t_vec[...] + dot_nt(grad_proj, vectors[d, :, here])
        delta = vec_dot * out_1 + out_2
        moved = features[pl.ds(chan_first, R), here].astype(F32) + delta
        feat_out[:, here] = moved.astype(BF16)
        grad_out = jnp.concatenate([grad_0, cf * vec_dot, cf], axis=0).astype(BF16)
        t_out[...] = t_out[...] + dot_nt(grad_out, all_sums)
        square_ref[0:1, here] = jnp.sum(moved * moved, axis=0, keepdims=True)
        square_ref[1:2, here] = jnp.sum(delta * delta, axis=0, keepdims=True)
        normed = (features[:, here].astype(F32) - stat[0:1, here]) * stat[1:2, here]
        normal = (normed * gain + bias).astype(BF16)
        t_b[...] = t_b[...] + dot_nt(grads_b[:, here], normal)
        return 0

    lax.fori_loop(0, atoms // wide, step, 0)
    flat_ref[9 * R :] = filter_block(grad_filters_b[...])


def normal_kernel(
    atoms,
    scalars, features, stat, vectors, delta_ref, square_ref, sums_ref,
    grads_b, grads_a, pos_a, mask, gain_ref, bias_ref,
    w_query, w_key, w_value, grad_filters_a,
    vec_out, send_ref, flat_ref,
    w_five, t_late,
):
    chan_first = pl.multiple_of(scalars[1], R)
    gain, bias = column(gain_ref[...]), column(bias_ref[...])
    five = [w_query[...], w_key[...]] + [w_value[p] for p in range(3)]
    w_five[...] = jnp.concatenate(five, axis=0).astype(F32).T.astype(BF16)
    t_late[...] = jnp.zeros(t_late.shape, F32)
    wide = 2 * LANES
    split = send_ref.shape[0]

    def step(b, _):
        at = pl.multiple_of(b * wide, wide)
        here = pl.ds(at, wide)
        real = mask[:, here].astype(F32)
        square_v = square_dv = 0.0
        for d in range(3):
            delta = delta_ref[d, :, here] + sums_ref[d, :, here]
            moved = vectors[d, pl.ds(chan_first, R), here].astype(F32) + delta
            vec_out[d, :, here] = moved.astype(BF16)
            square_v = square_v + moved * moved
            square_dv = square_dv + delta * delta
        normed = (features[:, here].astype(F32) - stat[0:1, here]) * stat[1:2, here]
        normal = (normed * gain + bias).astype(BF16)
        grads = jnp.concatenate([grads_b[:, here], grads_a[:, here]], axis=0)
        t_late[...] = t_late[...] + dot_nt(grads_a[:, here], normal)
        part = dot(w_five[...], grads)
        rounded = part.astype(BF16)
        for f in range(split):
            send_ref[f, :R, here] = rounded[f * R : (f + 1) * R]
        hat = part * gain
        tops = [
            jnp.sum(hat, axis=0, keepdims=True),
            jnp.sum(hat * normed, axis=0, keepdims=True),
        ]
        exact = [pos_a[d : d + 1, here] for d in range(3)]
        exact += [square_ref[n : n + 1, here] * real for n in range(2)]
        for x in (square_v, square_dv):
            exact.append(jnp.sum(x, axis=0, keepdims=True) * real)
        heads = [x.astype(BF16).astype(F32) for x in exact]
        tops = tops + heads + [x - y for x, y in zip(exact, heads)]
        tops = jnp.concatenate(tops, axis=0).astype(BF16)
        for f in range(split):
            send_ref[f, R:, here] = tops
        return 0

    lax.fori_loop(0, atoms // wide, step, 0)
    flat_ref[: 2 * R] = t_late[...].astype(BF16)
    flat_ref[2 * R :] = filter_block(grad_filters_a[...]).astype(BF16)


def final_kernel(
    atoms,
    scalars, got, got_vec, features, stat, gain_ref, cot_f, cot_v, back_ref, mask,
    grad_feat, grad_vec, grad_pos, small_ref,
):
    chan_first = pl.multiple_of(scalars[1], R)
    whole_gain = column(gain_ref[...])
    gain = whole_gain[:R]
    for f in range(1, H // R):
        gain = jnp.where(chan_first == f * R, whole_gain[f * R : (f + 1) * R], gain)

    def summed(ref, rows):
        total = ref[0, rows].astype(F32)
        for f in range(1, ref.shape[0]):
            total = total + ref[f, rows].astype(F32)
        return total

    tops = summed(got, slice(R, R + EXTRAS))
    grad_normal = summed(got, slice(0, R))
    inv = stat[1:2]
    normed = (features[pl.ds(chan_first, R), :].astype(F32) - stat[0:1]) * inv
    inner = grad_normal * gain - tops[0:1] * (1.0 / H) - normed * (tops[1:2] * (1.0 / H))
    grad_feat[...] = cot_f[...].astype(F32) + inv * inner
    for d in range(3):
        part = summed(got_vec, slice(d * R, (d + 1) * R))
        grad_vec[d] = cot_v[d].astype(F32) + part + back_ref[d]
    exact = tops[2:9] + tops[9:16]
    grad_pos[...] = exact[:3]
    ones = jnp.ones((8, atoms), BF16)
    gains = dot_nt(ones, (grad_normal * normed).astype(BF16))
    biases = dot_nt(ones, grad_normal.astype(BF16))
    totals = jnp.sum(exact[3:7], axis=1, keepdims=True)
    real = jnp.sum(mask[...].astype(F32), axis=1, keepdims=True)
    numbers = jnp.concatenate([totals, real, jnp.zeros((3, 1), F32)], axis=0)
    small = jnp.concatenate([gains, biases, jnp.broadcast_to(numbers, (8, LANES))], axis=1)
    high = small.astype(BF16)
    small_ref[:8] = high.astype(F32)
    small_ref[8:] = small - high.astype(F32)


def unpack_kernel(
    share,
    got,
    g_gain, g_bias, g_query, g_key, g_value, g_vector, g_output, g_key_f, g_value_f, rms_ref,
):
    every = [got[n].astype(F32) for n in range(got.shape[0])]
    small = 0.0
    for x in every:
        small = small + x[share:]
    total = small[:8] + small[8:]
    g_gain[...] = total[0:1, :R]
    g_bias[...] = total[0:1, R : 2 * R]
    numbers = total[:, LANES : LANES + 1]
    size = jnp.where(lax.broadcasted_iota(jnp.int32, (8, 1), 0) < 2, 1.0, 3.0) * H
    rms = jnp.sqrt(numbers / (numbers[4:5] * size) + 1e-06)
    rms_ref[...] = jnp.broadcast_to(rms, (8, LANES)).T[:1, :8]
    order = [(g, p) for g in (g_vector, g_output) for p in range(3)]
    order += [(g_query, None), (g_key, None), (g_value, 0), ((g_key_f, None), (g_value_f, 0))]
    order += [(g_value, 1), (g_value, 2), ((g_value_f, 1), (g_value_f, 2))]
    begins = [0]
    for g, _ in order:
        begins.append(begins[-1] + (R // 2 if isinstance(g, tuple) else R))
    for n, x in enumerate(every):
        for (g, p), low, high in zip(order, begins[:-1], begins[1:]):
            first, last = max(low, n * share), min(high, (n + 1) * share)
            if first >= last:
                continue
            value = x[first - n * share : last - n * share]
            rows = slice(first - low, last - low)
            if not isinstance(g, tuple):
                put(g, p, rows, value)
                continue
            for h in (0, 1):
                down = slice(rows.start + h * R // 2, rows.stop + h * R // 2)
                at = h * LANES
                put(g[0], g[1], down, value[:, at : at + R])
                put(p[0], p[1], down, value[:, at + R : at + 2 * R])


def put(ref, p, rows, value):
    if p is None:
        ref[rows] = value
    else:
        ref[p, rows] = value


def everywhere(x, axis):
    count = lax.axis_size(axis)
    return lax.all_to_all(jnp.broadcast_to(x[None], (count,) + x.shape), axis, 0, 0)


def per_device(
    features, vectors, positions, atom_mask, neighbours, ln_gain, ln_bias,
    w_query, w_key, w_value, w_vector, w_output, w_key_filter, w_value_filter,
    cot_features, cot_vectors,
):
    channels = w_query.shape[1]
    atoms = features.shape[1]
    count = lax.axis_size("atoms")
    split = lax.axis_size("feat")
    chan_first = lax.axis_index("feat") * channels
    row_first = lax.axis_index("atoms") * atoms
    start = HALO - lax.rem(row_first, MOL)
    scalars = jnp.stack([start, chan_first, row_first]).astype(jnp.int32)
    molecules, rows_each, tall = edge_sizes(atoms)
    w_query, w_key = w_query.T, w_key.T
    w_value, w_vector, w_output = [jnp.swapaxes(w, 1, 2) for w in (w_value, w_vector, w_output)]
    mask = atom_mask.reshape(1, atoms)
    gain, bias = ln_gain.reshape(1, H), ln_bias.reshape(1, H)

    ends = halo_call(
        atoms,
        scalars,
        (features, vectors, cot_features, cot_vectors, neighbours, mask, positions),
    )
    low = lax.ppermute(ends[0], "atoms", [(i, i + 1) for i in range(count - 1)])
    high = lax.ppermute(ends[1], "atoms", [(i + 1, i) for i in range(count - 1)])

    inputs = (
        scalars, features, vectors, cot_features, cot_vectors, neighbours, mask, positions,
        low, high, gain, bias, w_query, w_key, w_value, w_vector, w_output,
    )
    rows, part, stat = pl.pallas_call(
        functools.partial(dense_kernel, atoms),
        out_shape=[
            jax.ShapeDtypeStruct((tall, 10 * LANES), BF16),
            jax.ShapeDtypeStruct((H, atoms + LANES), BF16),
            jax.ShapeDtypeStruct((8, atoms), F32),
        ],
        in_specs=[whole(pltpu.SMEM)] + [whole()] * (len(inputs) - 1),
        out_specs=[whole()] * 3,
        scratch_shapes=[
            pltpu.VMEM((LANES, H), BF16),
            pltpu.VMEM((LANES, H), BF16),
            pltpu.VMEM((LANES, H), BF16),
            pltpu.VMEM((3 * R, H), BF16),
            pltpu.VMEM((H, 3 * R), BF16),
        ],
        compiler_params=params(),
    )(*inputs)
    scalar_parts = lax.all_to_all(part.reshape(split, channels, atoms + LANES), "feat", 0, 0)

    kinds = shared_scratch(atoms)
    batch = OFFSETS * rows_each
    names = ["mask", "near", "near_last"] + ["tall"] * 3 + ["many", "stage2"]
    radial, geo = edge_call(
        geometry_kernel,
        atoms,
        (scalars, rows),
        (),
        [],
        [((SPAN, batch, 2 * LANES), BF16), ((SPAN, GEO, batch, LANES), BF16)],
        [kinds[name] for name in names],
    )
    names = ["weights", "weights", "near", "near_last", "stage4", "loose2"]
    names += ["loose_low", "pre", "grad_pre", "line", "wide2", "wide2f", "line4", "line1"]
    names += ["low"] * 4 + ["low"] * 4 + ["first"] * 4
    scalar_sum, grads_b, grad_filters_b, pull = edge_call(
        scalar_kernel,
        atoms,
        (scalars, rows, w_key_filter, w_value_filter[0], scalar_parts),
        (radial, geo),
        [
            ((R, atoms), BF16),
            ((3 * R, atoms), BF16),
            ((LANES, 2 * LANES), F32),
        ],
        [((SPAN, batch, LANES), BF16)],
        [kinds[name] for name in names],
    )
    gathered = lax.all_gather(scalar_sum, "feat", axis=0, tiled=True)

    inputs = (
        scalars, features, stat, vectors, cot_features, cot_vectors, gathered, grads_b,
        gain, bias, w_vector, w_output, grad_filters_b,
    )
    new_features, delta, squares, send_vec, flat_early = pl.pallas_call(
        functools.partial(layer_kernel, atoms),
        out_shape=[
            jax.ShapeDtypeStruct((R, atoms), BF16),
            jax.ShapeDtypeStruct((3, R, atoms), F32),
            jax.ShapeDtypeStruct((8, atoms), F32),
            jax.ShapeDtypeStruct((split, 3 * R, atoms), BF16),
            jax.ShapeDtypeStruct((EARLY, H), F32),
        ],
        in_specs=[whole(pltpu.SMEM)] + [whole()] * (len(inputs) - 1),
        out_specs=[whole()] * 5,
        scratch_shapes=[
            pltpu.VMEM((H, 3 * R), BF16),
            pltpu.VMEM((3 * R, H), BF16),
            pltpu.VMEM((3 * R, H), BF16),
        ],
        compiler_params=params(),
    )(*inputs)
    share = (EARLY + LATE) // count
    got_vec = lax.all_to_all(send_vec, "feat", 0, 0)

    names = ["weights", "near", "near_last", "stage8", "loose5"]
    names += ["pre", "grad_pre", "line", "line3"]
    names += ["low"] * 7 + ["low"] * 10 + ["first"] * 10
    rows, _ = lax.optimization_barrier((rows, squares))
    sums, back, grads_a, pos_a, grad_filters_a = edge_call(
        vector_kernel,
        atoms,
        (scalars, rows, w_value_filter[1], w_value_filter[2]),
        (radial, geo, pull),
        [
            ((3, R, atoms), F32),
            ((3, R, atoms), F32),
            ((2 * R, atoms), BF16),
            ((8, atoms), F32),
            ((LANES, 2 * LANES), F32),
        ],
        [],
        [kinds[name] for name in names],
    )

    delta, got_vec = lax.optimization_barrier((delta, got_vec))
    inputs = (
        scalars, features, stat, vectors, delta, squares, sums, grads_b, grads_a, pos_a,
        mask, gain, bias, w_query, w_key, w_value, grad_filters_a,
    )
    new_vectors, send, flat_late = pl.pallas_call(
        functools.partial(normal_kernel, atoms),
        out_shape=[
            jax.ShapeDtypeStruct((3, R, atoms), BF16),
            jax.ShapeDtypeStruct((split, R + EXTRAS, atoms), BF16),
            jax.ShapeDtypeStruct((LATE, H), BF16),
        ],
        in_specs=[whole(pltpu.SMEM)] + [whole()] * (len(inputs) - 1),
        out_specs=[whole()] * 3,
        scratch_shapes=[pltpu.VMEM((H, 5 * R), BF16), pltpu.VMEM((2 * R, H), F32)],
        compiler_params=params(),
    )(*inputs)
    got = lax.all_to_all(send, "feat", 0, 0)
    flat = jnp.concatenate([flat_early.astype(BF16), flat_late], axis=0)
    shares = lax.all_to_all(flat.reshape(count, share, H), "atoms", 0, 0)

    inputs = (
        scalars, got, got_vec, features, stat, gain, cot_features, cot_vectors, back, mask,
    )
    grad_features, grad_vectors, grad_positions, small = pl.pallas_call(
        functools.partial(final_kernel, atoms),
        out_shape=[
            jax.ShapeDtypeStruct((R, atoms), F32),
            jax.ShapeDtypeStruct((3, R, atoms), F32),
            jax.ShapeDtypeStruct((3, atoms), F32),
            jax.ShapeDtypeStruct((16, H), F32),
        ],
        in_specs=[whole(pltpu.SMEM)] + [whole()] * (len(inputs) - 1),
        out_specs=[whole()] * 4,
        compiler_params=params(),
    )(*inputs)
    mine = jnp.concatenate([jnp.sum(shares.astype(F32), axis=0), small], axis=0).astype(BF16)
    every = everywhere(mine, "atoms")
    shapes = [
        (1, R), (1, R), (R, H), (R, H), (3, R, H), (3, R, H), (3, R, H), (R, R), (3, R, R), (1, 8),
    ]
    grads = pl.pallas_call(
        functools.partial(unpack_kernel, share),
        out_shape=[jax.ShapeDtypeStruct(shape, F32) for shape in shapes],
        in_specs=[whole()],
        out_specs=[whole()] * len(shapes),
        compiler_params=params(),
    )(every)
    return (
        new_features,
        new_vectors,
        grad_features,
        grad_vectors,
        grad_positions,
        grads[0].reshape(R),
        grads[1].reshape(R),
        grads[2].T,
        grads[3].T,
        jnp.swapaxes(grads[4], 1, 2),
        jnp.swapaxes(grads[5], 1, 2),
        jnp.swapaxes(grads[6], 1, 2),
        grads[7],
        grads[8],
        grads[9][0, :4],
    )


def solution(mesh):
    in_specs = (
        P(None, "atoms"),
        P(None, None, "atoms"),
        P(None, "atoms"),
        P("atoms"),
        P(None, "atoms"),
        P(),
        P(),
        P(None, "feat"),
        P(None, "feat"),
        P(None, None, "feat"),
        P(None, None, "feat"),
        P(None, None, "feat"),
        P(None, "feat"),
        P(None, None, "feat"),
        P("feat", "atoms"),
        P(None, "feat", "atoms"),
    )
    out_specs = (
        P("feat", "atoms"),
        P(None, "feat", "atoms"),
        P("feat", "atoms"),
        P(None, "feat", "atoms"),
        P(None, "atoms"),
        P("feat"),
        P("feat"),
        P(None, "feat"),
        P(None, "feat"),
        P(None, None, "feat"),
        P(None, None, "feat"),
        P(None, None, "feat"),
        P(None, "feat"),
        P(None, None, "feat"),
        P(),
    )
    return jax.shard_map(
        per_device, mesh=mesh, in_specs=in_specs, out_specs=out_specs, check_vma=False
    )
```

```python
import functools
import math

import jax
import jax.numpy as jnp
from jax import lax
from jax.experimental import pallas as pl
from jax.experimental.pallas import tpu as pltpu
from jax.sharding import PartitionSpec as P

H = 256
HEADS = 8
HEAD = H // HEADS
R = 64
MOL = 29
HALO = 32
CUTOFF = 5.0
EPSILON = 1e-05
F32 = jnp.float32
BF16 = jnp.bfloat16

LANE_GROUPS = 2
ROW_GROUPS = 3
SPAN = 5
OFFSETS = 14
STEPS = SPAN + OFFSETS
SUB = 16
LANES = 128

W01, W2V2, C01, C2_COUNT, POS, QK, V0, V12, VEC01, VEC2 = range(10)
GROUP_ROWS = 352
EARLY = 9 * R + R // 2
LATE = 2 * R + R // 2
EXTRAS = 16


BLOCK = 8
WINDOW = 256


def block_list(molecules, rows):
    full, rest = divmod(molecules, BLOCK)
    wide = ROW_GROUPS * BLOCK
    out = [(n * wide, wide, BLOCK) for n in range(full)]
    if rows > full * wide:
        out.append((full * wide, rows - full * wide, rest))
    return out


def row_parts(shape, axis, size):
    row = lax.broadcasted_iota(jnp.int32, shape, axis)
    group = jnp.zeros(shape, jnp.int32)
    for g in range(1, ROW_GROUPS):
        group = jnp.where(row >= g * size, g, group)
    return group, row - group * size, row < ROW_GROUPS * size


def set_distances(target, width, size):
    for r in range(LANE_GROUPS):

        def step(t, _, r=r):
            group, molecule, held = row_parts((width, WINDOW), 0, size)
            spot = t + SPAN * (LANE_GROUPS * group + r)
            spot = jnp.where(spot >= MOL, spot - MOL, spot)
            lane = lax.broadcasted_iota(jnp.int32, (width, WINDOW), 1)
            value = jnp.where(held, molecule * MOL + spot - lane, -(10**6))
            target[r, pl.ds(t * width, width), :] = value
            return 0

        lax.fori_loop(0, STEPS, step, 0)


def windows(blocks, distances, start, tall):
    for n, (first, width, size) in enumerate(blocks):
        atom = start + n * BLOCK * MOL
        base = jnp.minimum(atom // SUB * SUB, tall - WINDOW)
        base = pl.multiple_of(base, SUB)
        chosen = distances[0] if size == BLOCK else distances[1]
        ones = [jnp.where(chosen[r] == base - atom, 1.0, 0.0).astype(BF16) for r in (0, 1)]
        yield first, width, pl.ds(base, WINDOW), ones


def both_ways(given):
    top, bottom = [], []
    for n in range(given.shape[1] // LANES):
        x = given[:, n * LANES : (n + 1) * LANES].astype(F32)
        y = pltpu.roll(x, R, 1)
        low = lax.broadcasted_iota(jnp.int32, x.shape, 1) < R
        top += [jnp.where(low, x, 0.0), jnp.where(low, y, 0.0)]
        bottom += [jnp.where(low, 0.0, y), jnp.where(low, 0.0, x)]
    return jnp.concatenate(
        [jnp.concatenate(top, axis=1), jnp.concatenate(bottom, axis=1)], axis=0
    ).astype(BF16)


def spread(source, targets, blocks, distances, start, extra=None):
    waiting = None
    for first, width, here, ones in windows(blocks, distances, start, source.shape[0]):
        given = source[here, :]
        ones = jnp.concatenate(ones, axis=1)
        out = dot(ones, both_ways(given)).reshape(STEPS, width, 2 * given.shape[1])
        if extra is not None:
            extra(ones, here, first, width)
        if waiting is not None:
            first, out = waiting[0], jnp.concatenate([waiting[1], out], axis=1)
            waiting = None
        elif width % SUB:
            waiting = (first, out)
            continue
        for n, target in enumerate(targets):
            if target is not None:
                value = out[:, :, n * LANES : (n + 1) * LANES]
                target[:, first : first + out.shape[1]] = value.astype(target.dtype)


def position_spreader(source, targets):
    row = lax.broadcasted_iota(jnp.int32, (2 * LANES, 3 * LANES), 0)
    lane = lax.broadcasted_iota(jnp.int32, (2 * LANES, 3 * LANES), 1)
    axis = jnp.where(lane >= 2 * LANES, 2, jnp.where(lane >= LANES, 1, 0))
    part = jnp.where(row >= LANES, row - LANES, row)
    mine = (part >= 3 * axis) & (part < 3 * axis + 3)
    low = lane - axis * LANES < R
    wide = jnp.where(mine & (low == (row < LANES)), 1.0, 0.0).astype(BF16)

    def place(ones, here, first, width):
        given = source[here, :]
        found = [dot(ones[:, r * WINDOW : (r + 1) * WINDOW], given) for r in (0, 1)]
        total = dot(jnp.concatenate(found, axis=1).astype(BF16), wide)
        for d, target in enumerate(targets):
            value = total[:, d * LANES : (d + 1) * LANES]
            target[:, first : first + width] = value.reshape(STEPS, width, LANES)

    return place


def assemble(target, own_ref, halo_ref, lanes, at=0):
    atoms, tall, size = own_ref.shape[0], target.shape[0], lanes.stop - lanes.start
    there = slice(at, at + size)
    target[HALO : HALO + atoms, there] = own_ref[:, lanes]
    target[:HALO, there] = halo_ref[:HALO, lanes]
    end = 2 * HALO + atoms
    target[HALO + atoms : end, there] = halo_ref[HALO : 2 * HALO, lanes]
    target[end:, there] = jnp.zeros((tall - end, size), BF16)


def collect(sources, target, blocks, distances, start):
    target[...] = jnp.zeros(target.shape, F32)
    units = []
    for first, width, here, ones in windows(blocks, distances, start, target.shape[0]):
        units.append((first, width, here, ones))
    at = 0
    while at < len(units):
        group = units[at : at + 2] if units[at][0] % SUB == 0 and at + 1 < len(units) else None
        if group is None or (group[0][1] + group[1][1]) % SUB:
            group = units[at : at + 1]
        at += len(group)
        first = group[0][0]
        size = sum(g[1] for g in group)
        blocks_in = []
        for partner, carry in sources:
            value = partner[:, first : first + size].astype(F32)
            start_part = value[:SPAN] + carry[:, first : first + size]
            blocks_in.append(jnp.concatenate([start_part, value[SPAN:]], axis=0))
        for f, width, here, ones in group:
            parts = ([], [])
            for n in range(0, len(sources), 2):
                a = blocks_in[n][:, f - first : f - first + width].reshape(STEPS * width, LANES)
                b = blocks_in[n + 1][:, f - first : f - first + width]
                b = b.reshape(STEPS * width, LANES)
                low = lax.broadcasted_iota(jnp.int32, a.shape, 1) < R
                parts[0].append(jnp.where(low, a, pltpu.roll(b, R, 1)).astype(BF16))
                parts[1].append(jnp.where(low, pltpu.roll(a, R, 1), b).astype(BF16))
            total = 0.0
            for r in (0, 1):
                total = total + dot_tn(ones[r], jnp.concatenate(parts[r], axis=1))
            target[here, :] = target[here, :] + total


def row_masks(owned, start, blocks, atoms):
    for n, (at, width, size) in enumerate(blocks):
        _, molecule, _ = row_parts((width, LANES), 0, size)
        first = start - HALO + (n * BLOCK + molecule) * MOL
        owned[at : at + width] = jnp.where((first >= 0) & (first < atoms), 1.0, 0.0)


def set_multiplicities(count, target, blocks, rows):
    lane = lax.broadcasted_iota(jnp.int32, (rows, LANES), 1)
    inner = jnp.where(lane >= R, lane - R, lane)
    last = []
    for _, width, size in blocks:
        last.append(row_parts((width, LANES), 0, size)[0])
    doubled = (jnp.concatenate(last, axis=0) == ROW_GROUPS - 1) & (lane >= R)
    for t in range(SPAN):
        value = jnp.where(inner < 32, count[t], 0.0)
        for k in range(1, OFFSETS + 1):
            value = jnp.where(inner == 32 + k, count[t + k], value)
        if t == SPAN - 1:
            value = jnp.where(doubled, 0.0, value)
        target[t] = value


def dot(a, b):
    return jnp.dot(a, b, preferred_element_type=F32)


def dot_tn(a, b):
    return lax.dot_general(a, b, (((0,), (0,)), ((), ())), preferred_element_type=F32)


def dot_nt(a, b):
    return lax.dot_general(a, b, (((1,), (1,)), ((), ())), preferred_element_type=F32)


COSINE = (0.9999999998, -0.04934802137, 0.000405870916, -1.335212003e-06, 2.349373138e-09, -2.43963243e-12)

GEO_ENVELOPE, GEO_BEND, GEO_INVERSE, GEO_INTO, GEO_FROM, GEO_WAY, GEO_SLOPE, GEO_OWN = 0, 1, 2, 3, 4, 5, 8, 9
GEO = 10


def geometry(pos, many, t, rows, owned, radial, geo):
    inv_space = (R - 1) / CUTOFF

    def step(k, _):
        for o, size in halves(rows):
            here = pl.ds(pl.multiple_of(k * rows + o, SUB), size)
            part = slice(o, o + size)
            off = [p[t, part] - p[t + 1 + k, part] for p in pos]
            mine = owned[part].astype(BF16)
            close = many[t, part]
            lane = lax.broadcasted_iota(jnp.int32, (size, LANES), 1)
            base = jnp.where(lane >= R, R, 0)
            centre = (lane - base).astype(F32)
            near = base + (k + 1)
            square = off[0] * off[0] + off[1] * off[1] + off[2] * off[2]
            clamped = jnp.maximum(square, 0.01)
            inverse = lax.rsqrt(clamped)
            c = COSINE[-1]
            for term in COSINE[-2::-1]:
                c = c * clamped + term
            c = jnp.where(clamped < CUTOFF * CUTOFF, c, 0.0)
            envelope = c * c
            y = jnp.maximum(1.0 - envelope, 1e-30)
            bend = ((-math.pi / CUTOFF) * c) * (y * lax.rsqrt(y))
            u = (clamped * inverse) * inv_space - centre
            bump = jnp.exp(-0.5 * (u * u))
            value = bump * envelope
            high = value.astype(BF16)
            slope = bump * bend - inv_space * (u * value)
            radial[here, :LANES] = high
            radial[here, LANES:] = (value - high.astype(F32)).astype(BF16)
            geo[GEO_OWN, here, :] = high * mine
            geo[GEO_SLOPE, here, :] = slope.astype(BF16)
            geo[GEO_BEND, here, :] = bend.astype(BF16)
            geo[GEO_ENVELOPE, here, :] = envelope.astype(BF16)
            for d in range(3):
                geo[GEO_WAY + d, here, :] = (off[d] * inverse).astype(BF16)
            signed = jnp.where(square > 0.01, inverse, -inverse)
            geo[GEO_INVERSE, here, :] = signed.astype(BF16)
            into = jnp.take_along_axis(close, near, axis=1)
            out_of = jnp.take_along_axis(close, near + 32, axis=1)
            geo[GEO_INTO, here, :] = into.astype(BF16)
            geo[GEO_FROM, here, :] = out_of.astype(BF16)
        return 0

    lax.fori_loop(0, OFFSETS, step, 0)


def halves(rows):
    tiles = rows // SUB
    first = (tiles + 1) // 2 * SUB
    return ((0, first), (first, rows - first))


def set_filters(weights_ref, filter_1, filter_2):
    weights_ref[...] = jnp.zeros(weights_ref.shape, BF16)
    for f, ref in enumerate((filter_1, filter_2)):
        half = ref[...] * jnp.asarray(0.5, BF16)
        for part in range(2):
            for g in range(LANE_GROUPS):
                down = part * LANES + g * R
                at = f * LANES + g * R
                weights_ref[down : down + R, at : at + R] = half


def gate(h):
    t = jnp.tanh(h)
    u = 1.0 + t
    f = h * u
    return f.astype(BF16), (u + f * (1.0 - t)).astype(BF16)


def carried(rows, t, totals, group, body):
    def outer(s, _):
        o = pl.multiple_of(s * SUB, SUB)
        block = pl.ds(o, SUB)
        ii = (t, block)
        sums = None
        for k in range(0, OFFSETS, group):
            loaded = []
            for n in range(k, k + group):
                here = pl.ds(o + n * rows, SUB)
                loaded.append(body(o, here, ii, (t + 1 + n, block), n))
            done = [f() for f in loaded]
            given = [one for one, _ in done]
            while len(given) > 1:
                left = given[len(given) // 2 * 2 :]
                pairs = zip(given[0::2], given[1::2])
                given = [[x + y for x, y in zip(a, b)] for a, b in pairs] + left
            total = [x.astype(F32) for x in given[0]]
            sums = total if sums is None else [x + y for x, y in zip(sums, total)]
            for _, stores in done:
                for ref, index, value in stores:
                    ref[index] = value
        for total, value in zip(totals, sums):
            total[ii] = value
        return 0

    lax.fori_loop(0, rows // SUB, outer, 0)


def geometry_kernel(
    molecules, rows, atoms,
    scalars, own_ref, halo_ref, radial_out, geo_out,
    owned, near, near_last, px, py, pz, many, count, all_pos, all_count,
):
    t = pl.program_id(0)
    start = scalars[0]
    blocks = block_list(molecules, rows)
    distances = (near, near_last)

    @pl.when(t == 0)
    def _():
        row_masks(owned, start, blocks, atoms)
        set_distances(near, blocks[0][1], blocks[0][2])
        set_distances(near_last, blocks[-1][1], blocks[-1][2])
        assemble(all_pos, own_ref, halo_ref, slice(POS * LANES, (POS + 1) * LANES))
        assemble(all_count, own_ref, halo_ref, slice(C2_COUNT * LANES, (C2_COUNT + 1) * LANES))
        extra = position_spreader(all_pos, (px, py, pz))
        spread(all_count, (None, count), blocks, distances, start, extra)
        set_multiplicities(count, many, blocks, rows)

    geometry((px, py, pz), many, t, rows, owned, radial_out.at[0], geo_out.at[0])


def vector_kernel(
    molecules, rows, atoms,
    scalars, own_ref, halo_ref, filter_1, filter_2, radial_in, geo_in, pull_in,
    sums_ref, back_ref, grads_ref, pos_out, grad_w_ref,
    weights_ref, near, near_last, all_rows, loose, pre, grad_pre,
    grad_radial, grad_ways,
    w0, w1, w2, v2, c0, c1, c2,
    s0, s1, s2, a0, a1, a2, gv, gx, gy, gz,
    fs0, fs1, fs2, fa0, fa1, fa2, fgv, fgx, fgy, fgz,
):
    t = pl.program_id(0)
    start = scalars[0]
    own = slice(HALO, HALO + atoms)
    radial, geo = radial_in.at[0], geo_in.at[0]
    w, c, g_pos = (w0, w1, w2), (c0, c1, c2), (gx, gy, gz)
    sums, backs = (s0, s1, s2), (a0, a1, a2)
    blocks = block_list(molecules, rows)
    distances = (near, near_last)

    @pl.when(t == 0)
    def _():
        set_filters(weights_ref, filter_1, filter_2)
        set_distances(near, blocks[0][1], blocks[0][2])
        set_distances(near_last, blocks[-1][1], blocks[-1][2])
        assemble(all_rows, own_ref, halo_ref, slice(W01 * LANES, (C2_COUNT + 1) * LANES))
        spread(all_rows, (w0, w1, w2, v2, c0, c1, c2), blocks, distances, start)
        for total in (s0, s1, s2, a0, a1, a2, gv, gx, gy, gz):
            total[...] = jnp.zeros(total.shape, BF16)
        grad_w_ref[...] = jnp.zeros(grad_w_ref.shape, F32)

    pre[...] = dot(radial[...], weights_ref[...])

    def channel(o, here, ii, jj, k):
        h1, h2 = pre[here, :LANES], pre[here, LANES:]
        ni, nj = geo[GEO_INTO, here, :], geo[GEO_FROM, here, :]
        v2i, v2j = v2[ii], v2[jj]
        ways = [geo[GEO_WAY + d, here, :] for d in range(3)]
        wi, wj = [w[d][ii] for d in range(3)], [w[d][jj] for d in range(3)]
        ci, cj = [c[d][ii] for d in range(3)], [c[d][jj] for d in range(3)]
        old_sums = [sums[d][jj] for d in range(3)]
        old_backs = [backs[d][jj] for d in range(3)]
        old_gv = gv[jj]

        def compute():
            f1, d1 = gate(h1)
            f2, d2 = gate(h2)
            f1i, f1j, f2i, f2j = f1 * ni, f1 * nj, f2 * ni, f2 * nj
            msg_i, msg_j = f2i * v2j, f2j * v2i
            stores, sum_i, back_i = [], [], []
            along_i = along_j = across_i = across_j = None
            for d in range(3):
                way = ways[d]
                sum_i.append(f1i * wj[d] + msg_i * way)
                stores.append((sums[d], jj, old_sums[d] + (f1j * wi[d] - msg_j * way)))
                stores.append((backs[d], jj, old_backs[d] + f1i * ci[d]))
                back_i.append(f1j * cj[d])
                grad = ci[d] * msg_i - cj[d] * msg_j
                stores.append((grad_ways, (d, here, slice(None)), grad))
                new = (ci[d] * way, cj[d] * way, ci[d] * wj[d], cj[d] * wi[d])
                if d == 0:
                    along_i, along_j, across_i, across_j = new
                else:
                    along_i, along_j = along_i + new[0], along_j + new[1]
                    across_i, across_j = across_i + new[2], across_j + new[3]
            stores.append((gv, jj, old_gv + f2i * along_i))
            g1 = ni * across_i + nj * across_j
            g2 = ni * along_i * v2j - nj * along_j * v2i
            stores.append((grad_pre, (here, slice(0, LANES)), g1 * d1))
            stores.append((grad_pre, (here, slice(LANES, None)), g2 * d2))
            return sum_i + back_i + [-(f2j * along_j)], stores

        return compute

    carried(rows, t, (fs0, fs1, fs2, fa0, fa1, fa2, fgv), 2, channel)
    grad_radial[...] = dot_nt(grad_pre[...], weights_ref[:LANES])
    grad_w_ref[...] = grad_w_ref[...] + dot_tn(geo[GEO_OWN], grad_pre[...])

    def turn(o, here, ii, jj, k):
        ways = [geo[GEO_WAY + d, here, :] for d in range(3)]
        grads = [grad_ways[d, here, :] for d in range(3)]
        grad, slope = grad_radial[here, :], geo[GEO_SLOPE, here, :]
        signed, more = geo[GEO_INVERSE, here, :], pull_in[0, here, :]
        old = [g[jj] for g in g_pos]

        def compute():
            inverse = jnp.abs(signed)
            turned = [g * inverse for g in grads]
            along = ways[0] * turned[0] + ways[1] * turned[1] + ways[2] * turned[2]
            pull = jnp.where(signed > 0, grad.astype(BF16) * slope + more - along, 0)
            out = [turned[d] + ways[d] * pull for d in range(3)]
            return out, [(g_pos[d], jj, old[d] - out[d]) for d in range(3)]

        return compute

    carried(rows, t, (fgx, fgy, fgz), 7, turn)

    @pl.when(t == SPAN - 1)
    def _():
        low = lax.broadcasted_iota(jnp.int32, (atoms, LANES), 1) < R
        totals = (s0, s1, s2, gv, a0, a1, a2, gx, gy, gz)
        firsts = (fs0, fs1, fs2, fgv, fa0, fa1, fa2, fgx, fgy, fgz)
        collect(tuple(zip(totals, firsts)), loose, blocks, distances, start)
        both = loose[own, :LANES].T
        sums_ref[0] = both[:R]
        sums_ref[1] = both[R:]
        both = loose[own, LANES : 2 * LANES].T
        sums_ref[2] = both[:R]
        grads_ref[R:] = both[R:].astype(BF16)

        def kept(n):
            return own_ref[:, n * LANES : (n + 1) * LANES].astype(F32)

        v12 = kept(V12)
        v11 = jnp.where(low, v12, pltpu.roll(v12, R, 1))
        back = loose[own, 2 * LANES : 3 * LANES]
        both = (back * v11).T
        back_ref[0] = both[:R]
        back_ref[1] = both[R:]
        partial = back * kept(VEC01)
        partial = partial + pltpu.roll(partial, R, 1)
        back = loose[own, 3 * LANES : 4 * LANES]
        back_ref[2] = (back * v11).T[:R]
        partial = partial + back * kept(VEC2)
        grads_ref[:R] = partial.T[:R].astype(BF16)
        pos_out[...] = jnp.zeros(pos_out.shape, F32)
        pos_out[0:1] = jnp.sum(back.T[R:], axis=0, keepdims=True)
        both = loose[own, 4 * LANES :].T
        pos_out[1:2] = jnp.sum(both[:R], axis=0, keepdims=True)
        pos_out[2:3] = jnp.sum(both[R:], axis=0, keepdims=True)


def scalar_kernel(
    molecules, rows, atoms,
    scalars, own_ref, halo_ref, filter_1, filter_2, scalar_parts, radial_in, geo_in,
    sum_ref, grads_ref, grad_w_ref, pull_out,
    weights_ref, heads_ref, near, near_last, all_rows, loose, pre,
    grad_pre, grad_radial, products, sums, gates, bends,
    q, key, v0, gs,
    ss, gq, gk, g0,
    fss, fgq, fgk, fg0,
):
    t = pl.program_id(0)
    start = scalars[0]
    own = slice(HALO, HALO + atoms)
    radial, geo = radial_in.at[0], geo_in.at[0]
    blocks = block_list(molecules, rows)
    distances = (near, near_last)

    @pl.when(t == 0)
    def _():
        set_filters(weights_ref, filter_1, filter_2)
        row = lax.broadcasted_iota(jnp.int32, (2 * LANES, 2 * LANES), 0)
        lane = lax.broadcasted_iota(jnp.int32, (2 * LANES, 2 * LANES), 1)
        heads_ref[...] = jnp.where(row // HEAD == lane // HEAD, 1.0, 0.0).astype(BF16)
        set_distances(near, blocks[0][1], blocks[0][2])
        set_distances(near_last, blocks[-1][1], blocks[-1][2])
        assemble(all_rows, own_ref, halo_ref, slice(QK * LANES, (V0 + 1) * LANES))
        summed = scalar_parts[0].astype(F32)
        for f in range(1, scalar_parts.shape[0]):
            summed = summed + scalar_parts[f].astype(F32)
        summed = jnp.concatenate([jnp.zeros_like(summed), summed], axis=0).T
        here = slice(LANES, 2 * LANES)
        for low, high, at in (
            (HALO, HALO + atoms, 0),
            (0, HALO, atoms),
            (HALO + atoms, 2 * HALO + atoms, atoms + HALO),
        ):
            both = all_rows[low:high, here].astype(F32) + summed[at : at + high - low]
            all_rows[low:high, here] = both.astype(BF16)
        spread(all_rows, (q, key, v0, gs), blocks, distances, start)
        for total in (ss, gq, gk, g0):
            total[...] = jnp.zeros(total.shape, BF16)
        grad_w_ref[...] = jnp.zeros(grad_w_ref.shape, F32)

    pre[...] = dot(radial[...], weights_ref[...])

    def multiply(k, _):
        for o, size in halves(rows):
            here = pl.ds(pl.multiple_of(k * rows + o, SUB), size)
            ii, jj = (t, slice(o, o + size)), (t + 1 + k, slice(o, o + size))
            fk, dk = gate(pre[here, :LANES])
            f0, d0 = gate(pre[here, LANES:])
            k_ij, k_ji = q[ii] * key[jj] * fk, q[jj] * key[ii] * fk
            s_ij, s_ji = gs[ii] * v0[jj] * f0, gs[jj] * v0[ii] * f0
            gates[0, here, :] = fk
            gates[1, here, :] = f0
            gates[2, here, :] = dk
            gates[3, here, :] = d0
            products[0, here, :LANES] = k_ij
            products[0, here, LANES:] = k_ji
            products[1, here, :LANES] = s_ij
            products[1, here, LANES:] = s_ji
        return 0

    lax.fori_loop(0, OFFSETS, multiply, 0)
    sums[0] = dot(products[0], heads_ref[...])
    sums[1] = dot(products[1], heads_ref[...])

    def channel(o, here, ii, jj, k):
        fk, f0, dk, d0 = [gates[n, here, :] for n in range(4)]
        envelope, bend = geo[GEO_ENVELOPE, here, :], geo[GEO_BEND, here, :]
        side_in = []
        for side in range(2):
            lanes = slice(side * LANES, (side + 1) * LANES)
            m = geo[GEO_INTO + side, here, :]
            h, o_ = (ii, jj) if side == 0 else (jj, ii)
            side_in.append(
                (m, sums[0, here, lanes], sums[1, here, lanes])
                + (q[h], key[o_], gs[h], v0[o_])
            )
        old = [ref[jj] for ref in (g0, gk, ss, gq)]

        def compute():
            gives, news = [], []
            for m, score, g_att, qh, kt, gh, vt in side_in:
                act, rise = gate(0.5 * score)
                g_att = g_att.astype(BF16)
                weight = m * envelope
                att = act * weight
                g_score = g_att * (0.5 * rise) * weight
                lift = m * (g_att * act)
                bv, dv = f0 * att, fk * g_score
                gives.append((vt * bv, kt * dv, gh * bv, qh * dv))
                news.append((qh * kt * g_score, gh * vt * att, lift))
            one, two = gives
            new = [x + y for x, y in zip(*news)]
            stores = [
                (ref, jj, x + y)
                for ref, x, y in zip((g0, gk, ss, gq), old, (one[2], one[3], two[0], two[1]))
            ]
            stores.append((grad_pre, (here, slice(0, LANES)), new[0] * dk))
            stores.append((grad_pre, (here, slice(LANES, None)), new[1] * d0))
            stores.append((bends, (here, slice(None)), new[2] * bend * (1.0 / HEAD)))
            return [one[0], one[1], two[2], two[3]], stores

        return compute

    carried(rows, t, (fss, fgq, fg0, fgk), 2, channel)
    grad_radial[...] = dot_nt(grad_pre[...], weights_ref[:LANES])
    grad_w_ref[...] = grad_w_ref[...] + dot_tn(geo[GEO_OWN], grad_pre[...])

    def pull(k, _):
        here = pl.ds(pl.multiple_of(k * rows, SUB), rows)
        grad = grad_radial[here, :].astype(BF16)
        pull_out[0, here, :] = grad * geo[GEO_SLOPE, here, :] + bends[here, :]
        return 0

    lax.fori_loop(0, OFFSETS, pull, 0)

    @pl.when(t == SPAN - 1)
    def _():
        totals = (ss, g0, gq, gk)
        firsts = (fss, fg0, fgq, fgk)
        collect(tuple(zip(totals, firsts)), loose, blocks, distances, start)
        both = loose[own, :LANES].T
        sum_ref[...] = both[:R].astype(BF16)
        grads_ref[2 * R :] = both[R:].astype(BF16)
        grads_ref[: 2 * R] = loose[own, LANES : 2 * LANES].T.astype(BF16)


def whole(memory=pltpu.VMEM):
    return pl.BlockSpec(memory_space=memory)


def params(mib=60):
    return pltpu.CompilerParams(vmem_limit_bytes=mib * 1024 * 1024)


def edge_sizes(atoms):
    molecules = (atoms + 2 * (MOL - 1)) // MOL
    full, rest = divmod(molecules, BLOCK)
    rows = full * ROW_GROUPS * BLOCK + -(-ROW_GROUPS * rest // BLOCK) * BLOCK
    rows = -(-rows // SUB) * SUB
    tall = -(-(HALO + molecules * MOL) // SUB) * SUB
    return molecules, rows, tall


def by_step(shape):
    zeros = (0,) * (len(shape) - 1)
    return pl.BlockSpec((1,) + shape[1:], lambda t: (t,) + zeros)


def fixed(shape):
    zeros = (0,) * len(shape)
    return pl.BlockSpec(shape, lambda t: zeros)


def edge_call(kernel, atoms, inputs, stepped_in, outs, stepped_out, scratch):
    molecules, rows, _ = edge_sizes(atoms)
    return pl.pallas_call(
        functools.partial(kernel, molecules, rows, atoms),
        grid=(SPAN,),
        out_shape=[jax.ShapeDtypeStruct(s, kind) for s, kind in outs + stepped_out],
        in_specs=[whole(pltpu.SMEM)]
        + [fixed(x.shape) for x in inputs[1:]]
        + [by_step(x.shape) for x in stepped_in],
        out_specs=[fixed(s) for s, _ in outs] + [by_step(s) for s, _ in stepped_out],
        scratch_shapes=[pltpu.VMEM(s, kind) for s, kind in scratch],
        compiler_params=params(),
        cost_estimate=pl.CostEstimate(
            flops=20 * 10**9, bytes_accessed=40 * 10**6, transcendentals=10**7
        ),
    )(*inputs, *stepped_in)


def shared_scratch(atoms):
    molecules, rows, tall = edge_sizes(atoms)
    batch = OFFSETS * rows
    blocks = block_list(molecules, rows)
    return {
        "weights": ((2 * LANES, 2 * LANES), BF16),
        "many": ((SPAN, rows, LANES), F32),
        "mask": ((rows, LANES), F32),
        "near": ((LANE_GROUPS, STEPS * blocks[0][1], WINDOW), jnp.int32),
        "near_last": ((LANE_GROUPS, STEPS * blocks[-1][1], WINDOW), jnp.int32),
        "row1": ((tall, LANES), BF16),
        "row2": ((tall, 2 * LANES), BF16),
        "row4": ((tall, 4 * LANES), BF16),
        "loose5": ((tall, 5 * LANES), F32),
        "loose2": ((tall, 2 * LANES), F32),
        "tall": ((STEPS, rows, LANES), F32),
        "low": ((STEPS, rows, LANES), BF16),
        "first": ((SPAN, rows, LANES), F32),
        "pre": ((batch, 2 * LANES), F32),
        "grad_pre": ((batch, 2 * LANES), BF16),
        "line": ((batch, LANES), F32),
        "line2": ((2, batch, LANES), BF16),
        "line3": ((3, batch, LANES), BF16),
        "line4": ((4, batch, LANES), BF16),
        "line1": ((batch, LANES), BF16),
        "wide2": ((2, batch, 2 * LANES), BF16),
        "wide2f": ((2, batch, 2 * LANES), F32),
    }


def offsets_in_block(neighbours, mask, first):
    lane = lax.broadcasted_iota(jnp.int32, neighbours.shape, 1)
    diff = neighbours - (first + lane)
    return jnp.where(diff < 0, diff + MOL, diff) * mask


def pieces(x):
    a = x.astype(BF16)
    rest = x - a.astype(F32)
    b = rest.astype(BF16)
    return a, b, (rest - b.astype(F32)).astype(BF16)


def edge_groups(features, vectors, cot_f, cot_v, neighbours, mask, positions, first):
    diff = offsets_in_block(neighbours[...], mask[...], first).astype(F32).astype(BF16)
    groups = [jnp.concatenate([features[...], cot_f[...], diff], axis=0)]
    for d in range(3):
        rows = [x.astype(F32) for x in pieces(positions[d : d + 1])]
        rows = jnp.concatenate(rows + [jnp.zeros((29, LANES), F32)], axis=0).astype(BF16)
        groups.append(jnp.concatenate([vectors[d], cot_v[d], rows], axis=0))
    return groups


def halo_kernel(atoms, scalars, *refs):
    row_first = scalars[2]
    lane = lax.broadcasted_iota(jnp.int32, (GROUP_ROWS, LANES), 1)
    for end, at, out in ((0, atoms - LANES, refs[14]), (1, 0, refs[15])):
        groups = edge_groups(*refs[7 * end : 7 * end + 7], row_first + at)
        total = None
        for g, group in enumerate(groups):
            by = (HALO * (g + 1) if end == 0 else HALO * g) % LANES
            moved = group.astype(F32)
            moved = pltpu.roll(moved, by, 1) if by else moved
            total = moved if total is None else jnp.where(lane >= HALO * g, moved, total)
        out[...] = total.astype(BF16)


def halo_call(atoms, scalars, arrays):
    specs = []
    for at in (atoms // LANES - 1, 0):
        for x in arrays:
            shape = x.shape[:-1] + (LANES,)
            index = (0,) * (x.ndim - 1) + (at,)
            specs.append(pl.BlockSpec(shape, lambda *_, index=index: index))
    out = jax.ShapeDtypeStruct((GROUP_ROWS, LANES), BF16)
    return pl.pallas_call(
        functools.partial(halo_kernel, atoms),
        grid=(1,),
        out_shape=[out, out],
        in_specs=[whole(pltpu.SMEM)] + specs,
        out_specs=[whole(), whole()],
        compiler_params=params(),
    )(scalars, *arrays, *arrays)


def column(row):
    return jnp.broadcast_to(row, (8, row.shape[1])).T[:, :1]


def normalised(f):
    mean = jnp.mean(f, axis=0, keepdims=True)
    centred = f - mean
    inv = lax.rsqrt(jnp.mean(centred * centred, axis=0, keepdims=True) + EPSILON)
    return centred * inv, mean, inv


def dense_block(gain_ref, bias_ref, w_query, w_key, w_value, w_vector, w_output, scratch):
    w_qk, w_v0, w_v12, w_vec_t, w_out = scratch
    gain, bias = column(gain_ref[...]), column(bias_ref[...])
    w_qk[:R] = w_query[...]
    w_qk[R:] = w_key[...]
    w_v0[:R] = w_value[0]
    w_v0[R:] = jnp.zeros((R, H), BF16)
    w_v12[:R] = w_value[1]
    w_v12[R:] = w_value[2]
    for p in range(3):
        w_vec_t[p * R : (p + 1) * R] = w_vector[p]
    w_out[...] = jnp.concatenate([w_output[p] for p in range(3)], axis=0).astype(F32).T.astype(BF16)

    def block(f, v, cf, cv, own_v, diff, pos):
        width = f.shape[1]
        normed, mean, inv = normalised(f)
        turned = (normed * gain + bias).T.astype(BF16)
        kinds = lax.broadcasted_iota(jnp.int32, (R, width), 0)
        kinds = jnp.where(kinds < 32, kinds, MOL + 32 - kinds).astype(F32)
        counts = jnp.zeros((R, width), F32)
        for s in range(diff.shape[0]):
            counts = counts + jnp.where(diff[s : s + 1] == kinds, 1.0, 0.0)
        none = jnp.zeros((R, width), F32)
        counts = jnp.concatenate([none, counts], axis=0).T
        low = lax.broadcasted_iota(jnp.int32, (width, LANES), 1) < R
        pairs = [None] * 10
        pairs[QK] = dot_nt(turned, w_qk[...])
        pairs[V0] = dot_nt(turned, w_v0[...])
        v12 = dot_nt(turned, w_v12[...]).astype(BF16).astype(F32)
        v11 = jnp.where(low, v12, pltpu.roll(v12, R, 1))
        pairs[V12] = v12
        pairs[VEC01] = jnp.concatenate([own_v[0], own_v[1]], axis=0).T
        pairs[VEC2] = jnp.concatenate([own_v[2], none], axis=0).T
        pairs[W01] = pairs[VEC01] * v11
        pairs[W2V2] = jnp.where(low, pairs[VEC2] * v11, v12)
        pairs[C01] = jnp.concatenate([cv[0], cv[1]], axis=0).T
        pairs[C2_COUNT] = jnp.concatenate([cv[2], none], axis=0).T + counts
        pairs[POS] = jnp.concatenate([pos, jnp.zeros((LANES - 9, width), F32)], axis=0).T
        vec_dot = grad_0 = 0.0
        for d in range(3):
            proj = dot(w_vec_t[...], v[d])
            vec_dot = vec_dot + proj[:R] * proj[R : 2 * R]
            grad_0 = grad_0 + cv[d] * proj[2 * R :]
        grad_out = jnp.concatenate([grad_0, cf * vec_dot, cf], axis=0).astype(BF16)
        part = dot(w_out[...], grad_out)
        return [x.astype(BF16) for x in pairs], part.astype(BF16), mean, inv

    return block


def dense_kernel(
    atoms,
    scalars, features, vectors, cot_f, cot_v, neighbours, mask, positions,
    gain_ref, bias_ref, w_query, w_key, w_value, w_vector, w_output,
    rows_ref, part_ref, stat_ref, *scratch,
):
    chan_first = pl.multiple_of(scalars[1], R)
    row_first = scalars[2]
    weights = (w_query, w_key, w_value, w_vector, w_output)
    block = dense_block(gain_ref, bias_ref, *weights, scratch)
    wide = 2 * LANES

    def step(b, _):
        at = pl.multiple_of(b * wide, wide)
        here = pl.ds(at, wide)
        own_v = [vectors[d, pl.ds(chan_first, R), here].astype(F32) for d in range(3)]
        diff = offsets_in_block(neighbours[:, here], mask[:, here], row_first + at)
        places = [p.astype(F32) for d in range(3) for p in pieces(positions[d : d + 1, here])]
        pairs, part, mean, inv = block(
            features[:, here].astype(F32),
            [vectors[d, :, here] for d in range(3)],
            cot_f[:, here].astype(F32),
            [cot_v[d, :, here].astype(F32) for d in range(3)],
            own_v,
            diff.astype(F32),
            jnp.concatenate(places, axis=0),
        )
        for n, pair in enumerate(pairs):
            rows_ref[here, n * LANES : (n + 1) * LANES] = pair
        part_ref[:, here] = part
        stat_ref[0:1, here] = mean
        stat_ref[1:2, here] = inv
        return 0

    lax.fori_loop(0, atoms // wide, step, 0)


def dense_halo_kernel(
    atoms,
    scalars, low_ref, high_ref, part_in, gain_ref, bias_ref,
    w_query, w_key, w_value, w_vector, w_output,
    rows_ref, part_ref, *scratch,
):
    chan_first = pl.multiple_of(scalars[1], R)
    weights = (w_query, w_key, w_value, w_vector, w_output)
    block = dense_block(gain_ref, bias_ref, *weights, scratch)
    lane = lax.broadcasted_iota(jnp.int32, (GROUP_ROWS, LANES), 1)
    packed_low, packed_high = low_ref[...].astype(F32), high_ref[...].astype(F32)
    groups = []
    for g in range(4):
        a = pltpu.roll(packed_low, (LANES - HALO * g) % LANES, 1) if g else packed_low
        by = (LANES + HALO - HALO * g) % LANES
        b = pltpu.roll(packed_high, by, 1) if by else packed_high
        both = jnp.where(lane < HALO, a, jnp.where(lane < 2 * HALO, b, 0.0))
        groups.append(both)
    own_v, pos = [], []
    for d in range(3):
        g = groups[1 + d]
        found = g[:R]
        for f in range(1, H // R):
            found = jnp.where(chan_first == f * R, g[f * R : (f + 1) * R], found)
        own_v.append(found)
        pos.append(g[320:323])
    pairs, part, _, _ = block(
        groups[0][:H],
        [groups[1 + d][:H].astype(BF16) for d in range(3)],
        groups[0][H : H + R],
        [groups[1 + d][H : H + R] for d in range(3)],
        own_v,
        groups[0][H + R :],
        jnp.concatenate(pos, axis=0),
    )
    for n, pair in enumerate(pairs):
        rows_ref[:, n * LANES : (n + 1) * LANES] = pair
    part_ref[:, :atoms] = part_in[...]
    part_ref[:, atoms:] = part


def both_diagonals(grad, f):
    at = f * LANES
    return 0.5 * (grad[:R, at : at + R] + grad[R:, at + R : at + LANES])


def filter_block(grad):
    both = jnp.concatenate([both_diagonals(grad, 0), both_diagonals(grad, 1)], axis=1)
    return jnp.concatenate([both[: R // 2], both[R // 2 :]], axis=1)


def layer_kernel(
    atoms,
    scalars, features, stat, vectors, cot_f, cot_v, gathered, grads_b, gain_ref, bias_ref,
    w_vector, w_output, grad_filters_b,
    feat_out, delta_ref, square_ref, send_ref, flat_ref,
    w_vec, w_vec_t, w_out_t,
):
    chan_first = pl.multiple_of(scalars[1], R)
    gain, bias = column(gain_ref[...]), column(bias_ref[...])
    for p in range(3):
        w_vec_t[p * R : (p + 1) * R] = w_vector[p]
        w_out_t[p * R : (p + 1) * R] = w_output[p]
    w_vec[...] = w_vec_t[...].astype(F32).T.astype(BF16)
    t_vec, t_out, t_b = [flat_ref.at[n * 3 * R : (n + 1) * 3 * R] for n in range(3)]
    flat_ref[...] = jnp.zeros(flat_ref.shape, F32)
    wide = 2 * LANES
    split = send_ref.shape[0]

    def step(b, _):
        at = pl.multiple_of(b * wide, wide)
        here = pl.ds(at, wide)
        all_sums = gathered[:, here]
        outputs = dot(w_out_t[...], all_sums)
        out_0, out_1, out_2 = outputs[:R], outputs[R : 2 * R], outputs[2 * R :]
        cf = cot_f[:, here].astype(F32)
        grad_dot = cf * out_1
        vec_dot = grad_0 = 0.0
        for d in range(3):
            proj = dot(w_vec_t[...], vectors[d, :, here])
            first, second, third = proj[:R], proj[R : 2 * R], proj[2 * R :]
            cv = cot_v[d, :, here].astype(F32)
            vec_dot = vec_dot + first * second
            grad_0 = grad_0 + cv * third
            delta_ref[d, :, here] = third * out_0
            grad_proj = jnp.concatenate(
                [grad_dot * second, grad_dot * first, cv * out_0], axis=0
            ).astype(BF16)
            part = dot(w_vec[...], grad_proj).astype(BF16)
            for f in range(split):
                send_ref[f, d * R : (d + 1) * R, here] = part[f * R : (f + 1) * R]
            t_vec[...] = t_vec[...] + dot_nt(grad_proj, vectors[d, :, here])
        delta = vec_dot * out_1 + out_2
        moved = features[pl.ds(chan_first, R), here].astype(F32) + delta
        feat_out[:, here] = moved.astype(BF16)
        grad_out = jnp.concatenate([grad_0, cf * vec_dot, cf], axis=0).astype(BF16)
        t_out[...] = t_out[...] + dot_nt(grad_out, all_sums)
        square_ref[0:1, here] = jnp.sum(moved * moved, axis=0, keepdims=True)
        square_ref[1:2, here] = jnp.sum(delta * delta, axis=0, keepdims=True)
        normed = (features[:, here].astype(F32) - stat[0:1, here]) * stat[1:2, here]
        normal = (normed * gain + bias).astype(BF16)
        t_b[...] = t_b[...] + dot_nt(grads_b[:, here], normal)
        return 0

    lax.fori_loop(0, atoms // wide, step, 0)
    flat_ref[9 * R :] = filter_block(grad_filters_b[...])


def normal_kernel(
    atoms,
    scalars, features, stat, vectors, delta_ref, square_ref, sums_ref,
    grads_b, grads_a, pos_a, mask, gain_ref, bias_ref,
    w_query, w_key, w_value, grad_filters_a,
    vec_out, send_ref, flat_ref,
    w_five, t_late,
):
    chan_first = pl.multiple_of(scalars[1], R)
    gain, bias = column(gain_ref[...]), column(bias_ref[...])
    five = [w_query[...], w_key[...]] + [w_value[p] for p in range(3)]
    w_five[...] = jnp.concatenate(five, axis=0).astype(F32).T.astype(BF16)
    t_late[...] = jnp.zeros(t_late.shape, F32)
    wide = 2 * LANES
    split = send_ref.shape[0]

    def step(b, _):
        at = pl.multiple_of(b * wide, wide)
        here = pl.ds(at, wide)
        real = mask[:, here].astype(F32)
        square_v = square_dv = 0.0
        for d in range(3):
            delta = delta_ref[d, :, here] + sums_ref[d, :, here]
            moved = vectors[d, pl.ds(chan_first, R), here].astype(F32) + delta
            vec_out[d, :, here] = moved.astype(BF16)
            square_v = square_v + moved * moved
            square_dv = square_dv + delta * delta
        normed = (features[:, here].astype(F32) - stat[0:1, here]) * stat[1:2, here]
        normal = (normed * gain + bias).astype(BF16)
        grads = jnp.concatenate([grads_b[:, here], grads_a[:, here]], axis=0)
        t_late[...] = t_late[...] + dot_nt(grads_a[:, here], normal)
        part = dot(w_five[...], grads)
        rounded = part.astype(BF16)
        for f in range(split):
            send_ref[f, :R, here] = rounded[f * R : (f + 1) * R]
        hat = part * gain
        tops = [
            jnp.sum(hat, axis=0, keepdims=True),
            jnp.sum(hat * normed, axis=0, keepdims=True),
        ]
        exact = [pos_a[d : d + 1, here] for d in range(3)]
        exact += [square_ref[n : n + 1, here] * real for n in range(2)]
        for x in (square_v, square_dv):
            exact.append(jnp.sum(x, axis=0, keepdims=True) * real)
        heads = [x.astype(BF16).astype(F32) for x in exact]
        tops = tops + heads + [x - y for x, y in zip(exact, heads)]
        tops = jnp.concatenate(tops, axis=0).astype(BF16)
        for f in range(split):
            send_ref[f, R:, here] = tops
        return 0

    lax.fori_loop(0, atoms // wide, step, 0)
    flat_ref[: 2 * R] = t_late[...].astype(BF16)
    flat_ref[2 * R :] = filter_block(grad_filters_a[...]).astype(BF16)


def final_kernel(
    atoms,
    scalars, got, got_vec, features, stat, gain_ref, cot_f, cot_v, back_ref, mask,
    grad_feat, grad_vec, grad_pos, small_ref,
):
    chan_first = pl.multiple_of(scalars[1], R)
    whole_gain = column(gain_ref[...])
    gain = whole_gain[:R]
    for f in range(1, H // R):
        gain = jnp.where(chan_first == f * R, whole_gain[f * R : (f + 1) * R], gain)

    def summed(ref, rows):
        total = ref[0, rows].astype(F32)
        for f in range(1, ref.shape[0]):
            total = total + ref[f, rows].astype(F32)
        return total

    tops = summed(got, slice(R, R + EXTRAS))
    grad_normal = summed(got, slice(0, R))
    inv = stat[1:2]
    normed = (features[pl.ds(chan_first, R), :].astype(F32) - stat[0:1]) * inv
    inner = grad_normal * gain - tops[0:1] * (1.0 / H) - normed * (tops[1:2] * (1.0 / H))
    grad_feat[...] = cot_f[...].astype(F32) + inv * inner
    for d in range(3):
        part = summed(got_vec, slice(d * R, (d + 1) * R))
        grad_vec[d] = cot_v[d].astype(F32) + part + back_ref[d]
    exact = tops[2:9] + tops[9:16]
    grad_pos[...] = exact[:3]
    ones = jnp.ones((8, atoms), BF16)
    gains = dot_nt(ones, (grad_normal * normed).astype(BF16))
    biases = dot_nt(ones, grad_normal.astype(BF16))
    totals = jnp.sum(exact[3:7], axis=1, keepdims=True)
    real = jnp.sum(mask[...].astype(F32), axis=1, keepdims=True)
    numbers = jnp.concatenate([totals, real, jnp.zeros((3, 1), F32)], axis=0)
    small = jnp.concatenate([gains, biases, jnp.broadcast_to(numbers, (8, LANES))], axis=1)
    high = small.astype(BF16)
    small_ref[:8] = high.astype(F32)
    small_ref[8:] = small - high.astype(F32)


def unpack_kernel(
    share,
    got,
    g_gain, g_bias, g_query, g_key, g_value, g_vector, g_output, g_key_f, g_value_f, rms_ref,
):
    every = [got[n].astype(F32) for n in range(got.shape[0])]
    small = 0.0
    for x in every:
        small = small + x[share:]
    total = small[:8] + small[8:]
    g_gain[...] = total[0:1, :R]
    g_bias[...] = total[0:1, R : 2 * R]
    numbers = total[:, LANES : LANES + 1]
    size = jnp.where(lax.broadcasted_iota(jnp.int32, (8, 1), 0) < 2, 1.0, 3.0) * H
    rms = jnp.sqrt(numbers / (numbers[4:5] * size) + 1e-06)
    rms_ref[...] = jnp.broadcast_to(rms, (8, LANES)).T[:1, :8]
    order = [(g, p) for g in (g_vector, g_output) for p in range(3)]
    order += [(g_query, None), (g_key, None), (g_value, 0), ((g_key_f, None), (g_value_f, 0))]
    order += [(g_value, 1), (g_value, 2), ((g_value_f, 1), (g_value_f, 2))]
    begins = [0]
    for g, _ in order:
        begins.append(begins[-1] + (R // 2 if isinstance(g, tuple) else R))
    for n, x in enumerate(every):
        for (g, p), low, high in zip(order, begins[:-1], begins[1:]):
            first, last = max(low, n * share), min(high, (n + 1) * share)
            if first >= last:
                continue
            value = x[first - n * share : last - n * share]
            rows = slice(first - low, last - low)
            if not isinstance(g, tuple):
                put(g, p, rows, value)
                continue
            for h in (0, 1):
                down = slice(rows.start + h * R // 2, rows.stop + h * R // 2)
                at = h * LANES
                put(g[0], g[1], down, value[:, at : at + R])
                put(p[0], p[1], down, value[:, at + R : at + 2 * R])


def put(ref, p, rows, value):
    if p is None:
        ref[rows] = value
    else:
        ref[p, rows] = value


def everywhere(x, axis):
    count = lax.axis_size(axis)
    return lax.all_to_all(jnp.broadcast_to(x[None], (count,) + x.shape), axis, 0, 0)


def per_device(
    features, vectors, positions, atom_mask, neighbours, ln_gain, ln_bias,
    w_query, w_key, w_value, w_vector, w_output, w_key_filter, w_value_filter,
    cot_features, cot_vectors,
):
    channels = w_query.shape[1]
    atoms = features.shape[1]
    count = lax.axis_size("atoms")
    split = lax.axis_size("feat")
    chan_first = lax.axis_index("feat") * channels
    row_first = lax.axis_index("atoms") * atoms
    start = HALO - lax.rem(row_first, MOL)
    scalars = jnp.stack([start, chan_first, row_first]).astype(jnp.int32)
    molecules, rows_each, tall = edge_sizes(atoms)
    w_query, w_key = w_query.T, w_key.T
    w_value, w_vector, w_output = [jnp.swapaxes(w, 1, 2) for w in (w_value, w_vector, w_output)]
    mask = atom_mask.reshape(1, atoms)
    gain, bias = ln_gain.reshape(1, H), ln_bias.reshape(1, H)

    ends = halo_call(
        atoms,
        scalars,
        (features, vectors, cot_features, cot_vectors, neighbours, mask, positions),
    )
    low = lax.ppermute(ends[0], "atoms", [(i, i + 1) for i in range(count - 1)])
    high = lax.ppermute(ends[1], "atoms", [(i + 1, i) for i in range(count - 1)])

    scratch = [
        pltpu.VMEM((LANES, H), BF16),
        pltpu.VMEM((LANES, H), BF16),
        pltpu.VMEM((LANES, H), BF16),
        pltpu.VMEM((3 * R, H), BF16),
        pltpu.VMEM((H, 3 * R), BF16),
    ]
    weights = (gain, bias, w_query, w_key, w_value, w_vector, w_output)
    inputs = (
        scalars, features, vectors, cot_features, cot_vectors, neighbours, mask, positions,
    ) + weights
    rows, part, stat = pl.pallas_call(
        functools.partial(dense_kernel, atoms),
        out_shape=[
            jax.ShapeDtypeStruct((atoms, 10 * LANES), BF16),
            jax.ShapeDtypeStruct((H, atoms), BF16),
            jax.ShapeDtypeStruct((8, atoms), F32),
        ],
        in_specs=[whole(pltpu.SMEM)] + [whole()] * (len(inputs) - 1),
        out_specs=[whole()] * 3,
        scratch_shapes=scratch,
        compiler_params=params(),
        cost_estimate=pl.CostEstimate(
            flops=6 * 10**9, bytes_accessed=20 * 10**6, transcendentals=10**4
        ),
    )(*inputs)
    inputs = (scalars, low, high, part) + weights
    rows_halo, part = pl.pallas_call(
        functools.partial(dense_halo_kernel, atoms),
        out_shape=[
            jax.ShapeDtypeStruct((LANES, 10 * LANES), BF16),
            jax.ShapeDtypeStruct((H, atoms + LANES), BF16),
        ],
        in_specs=[whole(pltpu.SMEM)] + [whole()] * (len(inputs) - 1),
        out_specs=[whole()] * 2,
        scratch_shapes=scratch,
        compiler_params=params(),
    )(*inputs)
    scalar_parts = lax.all_to_all(part.reshape(split, channels, atoms + LANES), "feat", 0, 0)

    kinds = shared_scratch(atoms)
    batch = OFFSETS * rows_each
    names = ["mask", "near", "near_last"] + ["tall"] * 3 + ["many", "tall", "row1", "row1"]
    radial, geo = edge_call(
        geometry_kernel,
        atoms,
        (scalars, rows, rows_halo),
        (),
        [],
        [((SPAN, batch, 2 * LANES), BF16), ((SPAN, GEO, batch, LANES), BF16)],
        [kinds[name] for name in names],
    )
    names = ["weights", "weights", "near", "near_last", "row2", "loose2"]
    names += ["pre", "grad_pre", "line", "wide2", "wide2f", "line4", "line1"]
    names += ["low"] * 4 + ["low"] * 4 + ["first"] * 4
    scalar_sum, grads_b, grad_filters_b, pull = edge_call(
        scalar_kernel,
        atoms,
        (scalars, rows, rows_halo, w_key_filter, w_value_filter[0], scalar_parts),
        (radial, geo),
        [
            ((R, atoms), BF16),
            ((3 * R, atoms), BF16),
            ((LANES, 2 * LANES), F32),
        ],
        [((SPAN, batch, LANES), BF16)],
        [kinds[name] for name in names],
    )
    gathered = lax.all_gather(scalar_sum, "feat", axis=0, tiled=True)

    inputs = (
        scalars, features, stat, vectors, cot_features, cot_vectors, gathered, grads_b,
        gain, bias, w_vector, w_output, grad_filters_b,
    )
    new_features, delta, squares, send_vec, flat_early = pl.pallas_call(
        functools.partial(layer_kernel, atoms),
        out_shape=[
            jax.ShapeDtypeStruct((R, atoms), BF16),
            jax.ShapeDtypeStruct((3, R, atoms), F32),
            jax.ShapeDtypeStruct((8, atoms), F32),
            jax.ShapeDtypeStruct((split, 3 * R, atoms), BF16),
            jax.ShapeDtypeStruct((EARLY, H), F32),
        ],
        in_specs=[whole(pltpu.SMEM)] + [whole()] * (len(inputs) - 1),
        out_specs=[whole()] * 5,
        scratch_shapes=[
            pltpu.VMEM((H, 3 * R), BF16),
            pltpu.VMEM((3 * R, H), BF16),
            pltpu.VMEM((3 * R, H), BF16),
        ],
        compiler_params=params(),
    )(*inputs)
    share = (EARLY + LATE) // count
    got_vec = lax.all_to_all(send_vec, "feat", 0, 0)

    names = ["weights", "near", "near_last", "row4", "loose5"]
    names += ["pre", "grad_pre", "line", "line3"]
    names += ["low"] * 7 + ["low"] * 10 + ["first"] * 10
    rows, _ = lax.optimization_barrier((rows, squares))
    sums, back, grads_a, pos_a, grad_filters_a = edge_call(
        vector_kernel,
        atoms,
        (scalars, rows, rows_halo, w_value_filter[1], w_value_filter[2]),
        (radial, geo, pull),
        [
            ((3, R, atoms), F32),
            ((3, R, atoms), F32),
            ((2 * R, atoms), BF16),
            ((8, atoms), F32),
            ((LANES, 2 * LANES), F32),
        ],
        [],
        [kinds[name] for name in names],
    )

    delta, got_vec = lax.optimization_barrier((delta, got_vec))
    inputs = (
        scalars, features, stat, vectors, delta, squares, sums, grads_b, grads_a, pos_a,
        mask, gain, bias, w_query, w_key, w_value, grad_filters_a,
    )
    new_vectors, send, flat_late = pl.pallas_call(
        functools.partial(normal_kernel, atoms),
        out_shape=[
            jax.ShapeDtypeStruct((3, R, atoms), BF16),
            jax.ShapeDtypeStruct((split, R + EXTRAS, atoms), BF16),
            jax.ShapeDtypeStruct((LATE, H), BF16),
        ],
        in_specs=[whole(pltpu.SMEM)] + [whole()] * (len(inputs) - 1),
        out_specs=[whole()] * 3,
        scratch_shapes=[pltpu.VMEM((H, 5 * R), BF16), pltpu.VMEM((2 * R, H), F32)],
        compiler_params=params(),
    )(*inputs)
    got = lax.all_to_all(send, "feat", 0, 0)
    flat = jnp.concatenate([flat_early.astype(BF16), flat_late], axis=0)
    shares = lax.all_to_all(flat.reshape(count, share, H), "atoms", 0, 0)

    inputs = (
        scalars, got, got_vec, features, stat, gain, cot_features, cot_vectors, back, mask,
    )
    grad_features, grad_vectors, grad_positions, small = pl.pallas_call(
        functools.partial(final_kernel, atoms),
        out_shape=[
            jax.ShapeDtypeStruct((R, atoms), F32),
            jax.ShapeDtypeStruct((3, R, atoms), F32),
            jax.ShapeDtypeStruct((3, atoms), F32),
            jax.ShapeDtypeStruct((16, H), F32),
        ],
        in_specs=[whole(pltpu.SMEM)] + [whole()] * (len(inputs) - 1),
        out_specs=[whole()] * 4,
        compiler_params=params(),
    )(*inputs)
    mine = jnp.concatenate([jnp.sum(shares.astype(F32), axis=0), small], axis=0).astype(BF16)
    every = everywhere(mine, "atoms")
    shapes = [
        (1, R), (1, R), (R, H), (R, H), (3, R, H), (3, R, H), (3, R, H), (R, R), (3, R, R), (1, 8),
    ]
    grads = pl.pallas_call(
        functools.partial(unpack_kernel, share),
        out_shape=[jax.ShapeDtypeStruct(shape, F32) for shape in shapes],
        in_specs=[whole()],
        out_specs=[whole()] * len(shapes),
        compiler_params=params(),
    )(every)
    return (
        new_features,
        new_vectors,
        grad_features,
        grad_vectors,
        grad_positions,
        grads[0].reshape(R),
        grads[1].reshape(R),
        grads[2].T,
        grads[3].T,
        jnp.swapaxes(grads[4], 1, 2),
        jnp.swapaxes(grads[5], 1, 2),
        jnp.swapaxes(grads[6], 1, 2),
        grads[7],
        grads[8],
        grads[9][0, :4],
    )


def solution(mesh):
    in_specs = (
        P(None, "atoms"),
        P(None, None, "atoms"),
        P(None, "atoms"),
        P("atoms"),
        P(None, "atoms"),
        P(),
        P(),
        P(None, "feat"),
        P(None, "feat"),
        P(None, None, "feat"),
        P(None, None, "feat"),
        P(None, None, "feat"),
        P(None, "feat"),
        P(None, None, "feat"),
        P("feat", "atoms"),
        P(None, "feat", "atoms"),
    )
    out_specs = (
        P("feat", "atoms"),
        P(None, "feat", "atoms"),
        P("feat", "atoms"),
        P(None, "feat", "atoms"),
        P(None, "atoms"),
        P("feat"),
        P("feat"),
        P(None, "feat"),
        P(None, "feat"),
        P(None, None, "feat"),
        P(None, None, "feat"),
        P(None, None, "feat"),
        P(None, "feat"),
        P(None, None, "feat"),
        P(),
    )
    return jax.shard_map(
        per_device, mesh=mesh, in_specs=in_specs, out_specs=out_specs, check_vma=False
    )
```

```python
import functools
import math

import jax
import jax.numpy as jnp
from jax import lax
from jax.experimental import pallas as pl
from jax.experimental.pallas import tpu as pltpu
from jax.sharding import PartitionSpec as P

H = 256
HEADS = 8
HEAD = H // HEADS
R = 64
MOL = 29
HALO = 32
CUTOFF = 5.0
EPSILON = 1e-05
F32 = jnp.float32
BF16 = jnp.bfloat16

LANE_GROUPS = 2
ROW_GROUPS = 3
SPAN = 5
OFFSETS = 14
STEPS = SPAN + OFFSETS
SUB = 16
LANES = 128

W01, W2V2, C01, C2_COUNT, POS, QK, V0, V12, VEC01, VEC2 = range(10)
GROUP_ROWS = 352
EARLY = 9 * R + R // 2
LATE = 2 * R + R // 2
EXTRAS = 16


BLOCK = 8
WINDOW = 256


def block_list(molecules, rows):
    full, rest = divmod(molecules, BLOCK)
    wide = ROW_GROUPS * BLOCK
    out = [(n * wide, wide, BLOCK) for n in range(full)]
    if rows > full * wide:
        out.append((full * wide, rows - full * wide, rest))
    return out


def row_parts(shape, axis, size):
    row = lax.broadcasted_iota(jnp.int32, shape, axis)
    group = jnp.zeros(shape, jnp.int32)
    for g in range(1, ROW_GROUPS):
        group = jnp.where(row >= g * size, g, group)
    return group, row - group * size, row < ROW_GROUPS * size


def set_distances(target, width, size):
    for r in range(LANE_GROUPS):

        def step(t, _, r=r):
            group, molecule, held = row_parts((width, WINDOW), 0, size)
            spot = t + SPAN * (LANE_GROUPS * group + r)
            spot = jnp.where(spot >= MOL, spot - MOL, spot)
            lane = lax.broadcasted_iota(jnp.int32, (width, WINDOW), 1)
            value = jnp.where(held, molecule * MOL + spot - lane, -(10**6))
            target[r, pl.ds(t * width, width), :] = value
            return 0

        lax.fori_loop(0, STEPS, step, 0)


def windows(blocks, distances, start, tall):
    for n, (first, width, size) in enumerate(blocks):
        atom = start + n * BLOCK * MOL
        base = jnp.minimum(atom // SUB * SUB, tall - WINDOW)
        base = pl.multiple_of(base, SUB)
        chosen = distances[0] if size == BLOCK else distances[1]
        ones = [jnp.where(chosen[r] == base - atom, 1.0, 0.0).astype(BF16) for r in (0, 1)]
        yield first, width, pl.ds(base, WINDOW), ones


def both_ways(given):
    top, bottom = [], []
    for n in range(given.shape[1] // LANES):
        x = given[:, n * LANES : (n + 1) * LANES].astype(F32)
        y = pltpu.roll(x, R, 1)
        low = lax.broadcasted_iota(jnp.int32, x.shape, 1) < R
        top += [jnp.where(low, x, 0.0), jnp.where(low, y, 0.0)]
        bottom += [jnp.where(low, 0.0, y), jnp.where(low, 0.0, x)]
    return jnp.concatenate(
        [jnp.concatenate(top, axis=1), jnp.concatenate(bottom, axis=1)], axis=0
    ).astype(BF16)


def spread(source, targets, blocks, distances, start, extra=None):
    waiting = None
    for first, width, here, ones in windows(blocks, distances, start, source.shape[0]):
        given = source[here, :]
        ones = jnp.concatenate(ones, axis=1)
        out = dot(ones, both_ways(given)).reshape(STEPS, width, 2 * given.shape[1])
        if extra is not None:
            extra(ones, here, first, width)
        if waiting is not None:
            first, out = waiting[0], jnp.concatenate([waiting[1], out], axis=1)
            waiting = None
        elif width % SUB:
            waiting = (first, out)
            continue
        for n, target in enumerate(targets):
            if target is not None:
                value = out[:, :, n * LANES : (n + 1) * LANES]
                target[:, first : first + out.shape[1]] = value.astype(target.dtype)


def position_spreader(source, targets):
    row = lax.broadcasted_iota(jnp.int32, (2 * LANES, 3 * LANES), 0)
    lane = lax.broadcasted_iota(jnp.int32, (2 * LANES, 3 * LANES), 1)
    axis = jnp.where(lane >= 2 * LANES, 2, jnp.where(lane >= LANES, 1, 0))
    part = jnp.where(row >= LANES, row - LANES, row)
    mine = (part >= 3 * axis) & (part < 3 * axis + 3)
    low = lane - axis * LANES < R
    wide = jnp.where(mine & (low == (row < LANES)), 1.0, 0.0).astype(BF16)

    def place(ones, here, first, width):
        given = source[here, :]
        found = [dot(ones[:, r * WINDOW : (r + 1) * WINDOW], given) for r in (0, 1)]
        total = dot(jnp.concatenate(found, axis=1).astype(BF16), wide)
        for d, target in enumerate(targets):
            value = total[:, d * LANES : (d + 1) * LANES]
            target[:, first : first + width] = value.reshape(STEPS, width, LANES)

    return place


def assemble(target, own_ref, halo_ref, lanes, shift=0):
    atoms, tall = own_ref.shape[0], target.shape[0]
    also = slice(lanes.start + shift, lanes.stop + shift)
    target[HALO : HALO + atoms] = own_ref[:, lanes]
    target[:HALO] = halo_ref[:HALO, also]
    end = 2 * HALO + atoms
    target[HALO + atoms : end] = halo_ref[HALO : 2 * HALO, also]
    target[end:] = jnp.zeros((tall - end, target.shape[1]), BF16)


def keep_own(radial, owned, target, rows):
    def step(k, _):
        here = pl.ds(pl.multiple_of(k * rows, SUB), rows)
        target[here, :] = radial[here, :LANES] * owned[...].astype(BF16)
        return 0

    lax.fori_loop(0, OFFSETS, step, 0)


def collect(sources, target, blocks, distances, start):
    target[...] = jnp.zeros(target.shape, F32)
    units = []
    for first, width, here, ones in windows(blocks, distances, start, target.shape[0]):
        units.append((first, width, here, ones))
    at = 0
    while at < len(units):
        group = units[at : at + 2] if units[at][0] % SUB == 0 and at + 1 < len(units) else None
        if group is None or (group[0][1] + group[1][1]) % SUB:
            group = units[at : at + 1]
        at += len(group)
        first = group[0][0]
        size = sum(g[1] for g in group)
        blocks_in = []
        for partner, carry in sources:
            value = partner[:, first : first + size].astype(F32)
            start_part = value[:SPAN] + carry[:, first : first + size]
            blocks_in.append(jnp.concatenate([start_part, value[SPAN:]], axis=0))
        for f, width, here, ones in group:
            parts = ([], [])
            for n in range(0, len(sources), 2):
                a = blocks_in[n][:, f - first : f - first + width].reshape(STEPS * width, LANES)
                b = blocks_in[n + 1][:, f - first : f - first + width]
                b = b.reshape(STEPS * width, LANES)
                low = lax.broadcasted_iota(jnp.int32, a.shape, 1) < R
                parts[0].append(jnp.where(low, a, pltpu.roll(b, R, 1)).astype(BF16))
                parts[1].append(jnp.where(low, pltpu.roll(a, R, 1), b).astype(BF16))
            total = 0.0
            for r in (0, 1):
                total = total + dot_tn(ones[r], jnp.concatenate(parts[r], axis=1))
            target[here, :] = target[here, :] + total


def row_masks(owned, start, blocks, atoms):
    for n, (at, width, size) in enumerate(blocks):
        _, molecule, _ = row_parts((width, LANES), 0, size)
        first = start - HALO + (n * BLOCK + molecule) * MOL
        owned[at : at + width] = jnp.where((first >= 0) & (first < atoms), 1.0, 0.0)


def set_multiplicities(count, target, blocks, rows):
    lane = lax.broadcasted_iota(jnp.int32, (rows, LANES), 1)
    inner = jnp.where(lane >= R, lane - R, lane)
    last = []
    for _, width, size in blocks:
        last.append(row_parts((width, LANES), 0, size)[0])
    doubled = (jnp.concatenate(last, axis=0) == ROW_GROUPS - 1) & (lane >= R)
    for t in range(SPAN):
        value = jnp.where(inner < 32, count[t], 0.0)
        for k in range(1, OFFSETS + 1):
            value = jnp.where(inner == 32 + k, count[t + k], value)
        if t == SPAN - 1:
            value = jnp.where(doubled, 0.0, value)
        target[t] = value


def dot(a, b):
    return jnp.dot(a, b, preferred_element_type=F32)


def dot_tn(a, b):
    return lax.dot_general(a, b, (((0,), (0,)), ((), ())), preferred_element_type=F32)


def dot_nt(a, b):
    return lax.dot_general(a, b, (((1,), (1,)), ((), ())), preferred_element_type=F32)


COSINE = (0.9999999998, -0.04934802137, 0.000405870916, -1.335212003e-06, 2.349373138e-09, -2.43963243e-12)

GEO_SLOPE, GEO_INTO, GEO_FROM = 0, 1, 2
GEO_ENVELOPE, GEO_BEND = 0, 1
GEO_INVERSE, GEO_WAY = 0, 1


def geometry(pos, many, t, rows, radial, geo, geo_s, geo_v):
    inv_space = (R - 1) / CUTOFF

    def step(k, _):
        for o, size in halves(rows):
            here = pl.ds(pl.multiple_of(k * rows + o, SUB), size)
            part = slice(o, o + size)
            off = [p[t, part] - p[t + 1 + k, part] for p in pos]
            close = many[t, part]
            lane = lax.broadcasted_iota(jnp.int32, (size, LANES), 1)
            base = jnp.where(lane >= R, R, 0)
            centre = (lane - base).astype(F32)
            near = base + (k + 1)
            square = off[0] * off[0] + off[1] * off[1] + off[2] * off[2]
            clamped = jnp.maximum(square, 0.01)
            inverse = lax.rsqrt(clamped)
            c = COSINE[-1]
            for term in COSINE[-2::-1]:
                c = c * clamped + term
            c = jnp.where(clamped < CUTOFF * CUTOFF, c, 0.0)
            envelope = c * c
            y = jnp.maximum(1.0 - envelope, 1e-30)
            bend = ((-math.pi / CUTOFF) * c) * (y * lax.rsqrt(y))
            u = (clamped * inverse) * inv_space - centre
            bump = jnp.exp(-0.5 * (u * u))
            value = bump * envelope
            high = value.astype(BF16)
            slope = bump * bend - inv_space * (u * value)
            radial[here, :LANES] = high
            radial[here, LANES:] = (value - high.astype(F32)).astype(BF16)
            geo[GEO_SLOPE, here, :] = slope.astype(BF16)
            geo_s[GEO_BEND, here, :] = bend.astype(BF16)
            geo_s[GEO_ENVELOPE, here, :] = envelope.astype(BF16)
            for d in range(3):
                geo_v[GEO_WAY + d, here, :] = (off[d] * inverse).astype(BF16)
            signed = jnp.where(square > 0.01, inverse, -inverse)
            geo_v[GEO_INVERSE, here, :] = signed.astype(BF16)
            into = jnp.take_along_axis(close, near, axis=1)
            out_of = jnp.take_along_axis(close, near + 32, axis=1)
            geo[GEO_INTO, here, :] = into.astype(BF16)
            geo[GEO_FROM, here, :] = out_of.astype(BF16)
        return 0

    lax.fori_loop(0, OFFSETS, step, 0)


def halves(rows):
    tiles = rows // SUB
    first = (tiles + 1) // 2 * SUB
    return ((0, first), (first, rows - first))


def set_filters(weights_ref, filter_1, filter_2):
    weights_ref[...] = jnp.zeros(weights_ref.shape, BF16)
    for f, ref in enumerate((filter_1, filter_2)):
        half = ref[...] * jnp.asarray(0.5, BF16)
        for part in range(2):
            for g in range(LANE_GROUPS):
                down = part * LANES + g * R
                at = f * LANES + g * R
                weights_ref[down : down + R, at : at + R] = half


def gate(h):
    t = jnp.tanh(h)
    u = 1.0 + t
    f = h * u
    return f.astype(BF16), (u + f * (1.0 - t)).astype(BF16)


def carried(rows, t, totals, group, body):
    def outer(s, _):
        o = pl.multiple_of(s * SUB, SUB)
        block = pl.ds(o, SUB)
        ii = (t, block)
        sums = None
        for k in range(0, OFFSETS, group):
            loaded = []
            for n in range(k, k + group):
                here = pl.ds(o + n * rows, SUB)
                loaded.append(body(o, here, ii, (t + 1 + n, block), n))
            done = [f() for f in loaded]
            given = [one for one, _ in done]
            while len(given) > 1:
                left = given[len(given) // 2 * 2 :]
                pairs = zip(given[0::2], given[1::2])
                given = [[x + y for x, y in zip(a, b)] for a, b in pairs] + left
            total = [x.astype(F32) for x in given[0]]
            sums = total if sums is None else [x + y for x, y in zip(sums, total)]
            for _, stores in done:
                for ref, index, value in stores:
                    ref[index] = value
        for total, value in zip(totals, sums):
            total[ii] = value
        return 0

    lax.fori_loop(0, rows // SUB, outer, 0)


def geometry_kernel(
    molecules, rows, atoms,
    scalars, own_count, own_pos, halo_ref, radial_out, geo_out, geo_s_out, geo_v_out,
    near, near_last, px, py, pz, many, count, all_pos, all_count,
):
    t = pl.program_id(0)
    start = scalars[0]
    blocks = block_list(molecules, rows)
    distances = (near, near_last)

    @pl.when(t == 0)
    def _():
        set_distances(near, blocks[0][1], blocks[0][2])
        set_distances(near_last, blocks[-1][1], blocks[-1][2])
        assemble(all_pos, own_pos, halo_ref, slice(0, LANES), POS * LANES)
        assemble(all_count, own_count, halo_ref, slice(0, LANES), C2_COUNT * LANES)
        extra = position_spreader(all_pos, (px, py, pz))
        spread(all_count, (None, count), blocks, distances, start, extra)
        set_multiplicities(count, many, blocks, rows)

    outs = [ref.at[0] for ref in (radial_out, geo_out, geo_s_out, geo_v_out)]
    geometry((px, py, pz), many, t, rows, *outs)


def vector_kernel(
    molecules, rows, atoms,
    scalars, own_ref, halo_ref, filter_1, filter_2, radial_in, geo_in, geo_v_in, pull_in,
    sums_ref, back_ref, grads_ref, pos_out, grad_w_ref,
    weights_ref, near, near_last, all_rows, loose, pre, grad_pre,
    grad_radial, grad_ways, owned, radial_own,
    w0, w1, w2, v2, c0, c1, c2,
    s0, s1, s2, a0, a1, a2, gv, gx, gy, gz,
    fs0, fs1, fs2, fa0, fa1, fa2, fgv, fgx, fgy, fgz,
):
    t = pl.program_id(0)
    start = scalars[0]
    own = slice(HALO, HALO + atoms)
    radial, geo, geo_v = radial_in.at[0], geo_in.at[0], geo_v_in.at[0]
    w, c, g_pos = (w0, w1, w2), (c0, c1, c2), (gx, gy, gz)
    sums, backs = (s0, s1, s2), (a0, a1, a2)
    blocks = block_list(molecules, rows)
    distances = (near, near_last)

    @pl.when(t == 0)
    def _():
        set_filters(weights_ref, filter_1, filter_2)
        row_masks(owned, start, blocks, atoms)
        set_distances(near, blocks[0][1], blocks[0][2])
        set_distances(near_last, blocks[-1][1], blocks[-1][2])
        assemble(all_rows, own_ref, halo_ref, slice(W01 * LANES, (C2_COUNT + 1) * LANES))
        spread(all_rows, (w0, w1, w2, v2, c0, c1, c2), blocks, distances, start)
        for total in (s0, s1, s2, a0, a1, a2, gv, gx, gy, gz):
            total[...] = jnp.zeros(total.shape, BF16)
        grad_w_ref[...] = jnp.zeros(grad_w_ref.shape, F32)

    pre[...] = dot(radial[...], weights_ref[...])
    keep_own(radial, owned, radial_own, rows)

    def channel(o, here, ii, jj, k):
        h1, h2 = pre[here, :LANES], pre[here, LANES:]
        ni, nj = geo[GEO_INTO, here, :], geo[GEO_FROM, here, :]
        v2i, v2j = v2[ii], v2[jj]
        ways = [geo_v[GEO_WAY + d, here, :] for d in range(3)]
        wi, wj = [w[d][ii] for d in range(3)], [w[d][jj] for d in range(3)]
        ci, cj = [c[d][ii] for d in range(3)], [c[d][jj] for d in range(3)]
        old_sums = [sums[d][jj] for d in range(3)]
        old_backs = [backs[d][jj] for d in range(3)]
        old_gv = gv[jj]

        def compute():
            f1, d1 = gate(h1)
            f2, d2 = gate(h2)
            f1i, f1j, f2i, f2j = f1 * ni, f1 * nj, f2 * ni, f2 * nj
            msg_i, msg_j = f2i * v2j, f2j * v2i
            stores, sum_i, back_i = [], [], []
            along_i = along_j = across_i = across_j = None
            for d in range(3):
                way = ways[d]
                sum_i.append(f1i * wj[d] + msg_i * way)
                stores.append((sums[d], jj, old_sums[d] + (f1j * wi[d] - msg_j * way)))
                stores.append((backs[d], jj, old_backs[d] + f1i * ci[d]))
                back_i.append(f1j * cj[d])
                grad = ci[d] * msg_i - cj[d] * msg_j
                stores.append((grad_ways, (d, here, slice(None)), grad))
                new = (ci[d] * way, cj[d] * way, ci[d] * wj[d], cj[d] * wi[d])
                if d == 0:
                    along_i, along_j, across_i, across_j = new
                else:
                    along_i, along_j = along_i + new[0], along_j + new[1]
                    across_i, across_j = across_i + new[2], across_j + new[3]
            stores.append((gv, jj, old_gv + f2i * along_i))
            g1 = ni * across_i + nj * across_j
            g2 = ni * along_i * v2j - nj * along_j * v2i
            stores.append((grad_pre, (here, slice(0, LANES)), g1 * d1))
            stores.append((grad_pre, (here, slice(LANES, None)), g2 * d2))
            return sum_i + back_i + [-(f2j * along_j)], stores

        return compute

    carried(rows, t, (fs0, fs1, fs2, fa0, fa1, fa2, fgv), 2, channel)
    grad_radial[...] = dot_nt(grad_pre[...], weights_ref[:LANES])
    grad_w_ref[...] = grad_w_ref[...] + dot_tn(radial_own[...], grad_pre[...])

    def turn(o, here, ii, jj, k):
        ways = [geo_v[GEO_WAY + d, here, :] for d in range(3)]
        grads = [grad_ways[d, here, :] for d in range(3)]
        grad, slope = grad_radial[here, :], geo[GEO_SLOPE, here, :]
        signed, more = geo_v[GEO_INVERSE, here, :], pull_in[0, here, :]
        old = [g[jj] for g in g_pos]

        def compute():
            inverse = jnp.abs(signed)
            turned = [g * inverse for g in grads]
            along = ways[0] * turned[0] + ways[1] * turned[1] + ways[2] * turned[2]
            pull = jnp.where(signed > 0, grad.astype(BF16) * slope + more - along, 0)
            out = [turned[d] + ways[d] * pull for d in range(3)]
            return out, [(g_pos[d], jj, old[d] - out[d]) for d in range(3)]

        return compute

    carried(rows, t, (fgx, fgy, fgz), 7, turn)

    @pl.when(t == SPAN - 1)
    def _():
        low = lax.broadcasted_iota(jnp.int32, (atoms, LANES), 1) < R
        totals = (s0, s1, s2, gv, a0, a1, a2, gx, gy, gz)
        firsts = (fs0, fs1, fs2, fgv, fa0, fa1, fa2, fgx, fgy, fgz)
        collect(tuple(zip(totals, firsts)), loose, blocks, distances, start)
        both = loose[own, :LANES].T
        sums_ref[0] = both[:R]
        sums_ref[1] = both[R:]
        both = loose[own, LANES : 2 * LANES].T
        sums_ref[2] = both[:R]
        grads_ref[R:] = both[R:].astype(BF16)

        def kept(n):
            return own_ref[:, n * LANES : (n + 1) * LANES].astype(F32)

        v12 = kept(V12)
        v11 = jnp.where(low, v12, pltpu.roll(v12, R, 1))
        back = loose[own, 2 * LANES : 3 * LANES]
        both = (back * v11).T
        back_ref[0] = both[:R]
        back_ref[1] = both[R:]
        partial = back * kept(VEC01)
        partial = partial + pltpu.roll(partial, R, 1)
        back = loose[own, 3 * LANES : 4 * LANES]
        back_ref[2] = (back * v11).T[:R]
        partial = partial + back * kept(VEC2)
        grads_ref[:R] = partial.T[:R].astype(BF16)
        pos_out[...] = jnp.zeros(pos_out.shape, F32)
        pos_out[0:1] = jnp.sum(back.T[R:], axis=0, keepdims=True)
        both = loose[own, 4 * LANES :].T
        pos_out[1:2] = jnp.sum(both[:R], axis=0, keepdims=True)
        pos_out[2:3] = jnp.sum(both[R:], axis=0, keepdims=True)


def scalar_kernel(
    molecules, rows, atoms,
    scalars, own_ref, halo_ref, filter_1, filter_2, scalar_parts, radial_in, geo_in, geo_s_in,
    sum_ref, grads_ref, grad_w_ref, pull_out,
    weights_ref, heads_ref, near, near_last, all_rows, loose, pre,
    grad_pre, grad_radial, products, sums, gates, bends, owned, radial_own,
    q, key, v0, gs,
    ss, gq, gk, g0,
    fss, fgq, fgk, fg0,
):
    t = pl.program_id(0)
    start = scalars[0]
    own = slice(HALO, HALO + atoms)
    radial, geo, geo_s = radial_in.at[0], geo_in.at[0], geo_s_in.at[0]
    blocks = block_list(molecules, rows)
    distances = (near, near_last)

    @pl.when(t == 0)
    def _():
        set_filters(weights_ref, filter_1, filter_2)
        row = lax.broadcasted_iota(jnp.int32, (2 * LANES, 2 * LANES), 0)
        lane = lax.broadcasted_iota(jnp.int32, (2 * LANES, 2 * LANES), 1)
        heads_ref[...] = jnp.where(row // HEAD == lane // HEAD, 1.0, 0.0).astype(BF16)
        row_masks(owned, start, blocks, atoms)
        set_distances(near, blocks[0][1], blocks[0][2])
        set_distances(near_last, blocks[-1][1], blocks[-1][2])
        assemble(all_rows, own_ref, halo_ref, slice(QK * LANES, (V0 + 1) * LANES))
        summed = scalar_parts[0].astype(F32)
        for f in range(1, scalar_parts.shape[0]):
            summed = summed + scalar_parts[f].astype(F32)
        summed = jnp.concatenate([jnp.zeros_like(summed), summed], axis=0).T
        here = slice(LANES, 2 * LANES)
        for low, high, at in (
            (HALO, HALO + atoms, 0),
            (0, HALO, atoms),
            (HALO + atoms, 2 * HALO + atoms, atoms + HALO),
        ):
            both = all_rows[low:high, here].astype(F32) + summed[at : at + high - low]
            all_rows[low:high, here] = both.astype(BF16)
        spread(all_rows, (q, key, v0, gs), blocks, distances, start)
        for total in (ss, gq, gk, g0):
            total[...] = jnp.zeros(total.shape, BF16)
        grad_w_ref[...] = jnp.zeros(grad_w_ref.shape, F32)

    pre[...] = dot(radial[...], weights_ref[...])
    keep_own(radial, owned, radial_own, rows)

    def multiply(k, _):
        for o, size in halves(rows):
            here = pl.ds(pl.multiple_of(k * rows + o, SUB), size)
            ii, jj = (t, slice(o, o + size)), (t + 1 + k, slice(o, o + size))
            fk, dk = gate(pre[here, :LANES])
            f0, d0 = gate(pre[here, LANES:])
            k_ij, k_ji = q[ii] * key[jj] * fk, q[jj] * key[ii] * fk
            s_ij, s_ji = gs[ii] * v0[jj] * f0, gs[jj] * v0[ii] * f0
            gates[0, here, :] = fk
            gates[1, here, :] = f0
            gates[2, here, :] = dk
            gates[3, here, :] = d0
            products[0, here, :LANES] = k_ij
            products[0, here, LANES:] = k_ji
            products[1, here, :LANES] = s_ij
            products[1, here, LANES:] = s_ji
        return 0

    lax.fori_loop(0, OFFSETS, multiply, 0)
    sums[0] = dot(products[0], heads_ref[...])
    sums[1] = dot(products[1], heads_ref[...])

    def channel(o, here, ii, jj, k):
        fk, f0, dk, d0 = [gates[n, here, :] for n in range(4)]
        envelope, bend = geo_s[GEO_ENVELOPE, here, :], geo_s[GEO_BEND, here, :]
        side_in = []
        for side in range(2):
            lanes = slice(side * LANES, (side + 1) * LANES)
            m = geo[GEO_INTO + side, here, :]
            h, o_ = (ii, jj) if side == 0 else (jj, ii)
            side_in.append(
                (m, sums[0, here, lanes], sums[1, here, lanes])
                + (q[h], key[o_], gs[h], v0[o_])
            )
        old = [ref[jj] for ref in (g0, gk, ss, gq)]

        def compute():
            gives, news = [], []
            for m, score, g_att, qh, kt, gh, vt in side_in:
                act, rise = gate(0.5 * score)
                g_att = g_att.astype(BF16)
                weight = m * envelope
                att = act * weight
                g_score = g_att * (0.5 * rise) * weight
                lift = m * (g_att * act)
                bv, dv = f0 * att, fk * g_score
                gives.append((vt * bv, kt * dv, gh * bv, qh * dv))
                news.append((qh * kt * g_score, gh * vt * att, lift))
            one, two = gives
            new = [x + y for x, y in zip(*news)]
            stores = [
                (ref, jj, x + y)
                for ref, x, y in zip((g0, gk, ss, gq), old, (one[2], one[3], two[0], two[1]))
            ]
            stores.append((grad_pre, (here, slice(0, LANES)), new[0] * dk))
            stores.append((grad_pre, (here, slice(LANES, None)), new[1] * d0))
            stores.append((bends, (here, slice(None)), new[2] * bend * (1.0 / HEAD)))
            return [one[0], one[1], two[2], two[3]], stores

        return compute

    carried(rows, t, (fss, fgq, fg0, fgk), 2, channel)
    grad_radial[...] = dot_nt(grad_pre[...], weights_ref[:LANES])
    grad_w_ref[...] = grad_w_ref[...] + dot_tn(radial_own[...], grad_pre[...])

    def pull(k, _):
        here = pl.ds(pl.multiple_of(k * rows, SUB), rows)
        grad = grad_radial[here, :].astype(BF16)
        pull_out[0, here, :] = grad * geo[GEO_SLOPE, here, :] + bends[here, :]
        return 0

    lax.fori_loop(0, OFFSETS, pull, 0)

    @pl.when(t == SPAN - 1)
    def _():
        totals = (ss, g0, gq, gk)
        firsts = (fss, fg0, fgq, fgk)
        collect(tuple(zip(totals, firsts)), loose, blocks, distances, start)
        both = loose[own, :LANES].T
        sum_ref[...] = both[:R].astype(BF16)
        grads_ref[2 * R :] = both[R:].astype(BF16)
        grads_ref[: 2 * R] = loose[own, LANES : 2 * LANES].T.astype(BF16)


def whole(memory=pltpu.VMEM):
    return pl.BlockSpec(memory_space=memory)


def params(mib=60):
    return pltpu.CompilerParams(vmem_limit_bytes=mib * 1024 * 1024)


def edge_sizes(atoms):
    molecules = (atoms + 2 * (MOL - 1)) // MOL
    full, rest = divmod(molecules, BLOCK)
    rows = full * ROW_GROUPS * BLOCK + -(-ROW_GROUPS * rest // BLOCK) * BLOCK
    rows = -(-rows // SUB) * SUB
    tall = -(-(HALO + molecules * MOL) // SUB) * SUB
    return molecules, rows, tall


def by_step(shape):
    zeros = (0,) * (len(shape) - 1)
    return pl.BlockSpec((1,) + shape[1:], lambda t: (t,) + zeros)


def fixed(shape):
    zeros = (0,) * len(shape)
    return pl.BlockSpec(shape, lambda t: zeros)


def edge_call(kernel, atoms, inputs, stepped_in, outs, stepped_out, scratch, columns=()):
    molecules, rows, _ = edge_sizes(atoms)
    return pl.pallas_call(
        functools.partial(kernel, molecules, rows, atoms),
        grid=(SPAN,),
        out_shape=[jax.ShapeDtypeStruct(s, kind) for s, kind in outs + stepped_out],
        in_specs=[whole(pltpu.SMEM)]
        + [pl.BlockSpec((atoms, LANES), lambda t, n=n: (0, n)) for n in columns]
        + [fixed(x.shape) for x in inputs[1 + len(columns) :]]
        + [by_step(x.shape) for x in stepped_in],
        out_specs=[fixed(s) for s, _ in outs] + [by_step(s) for s, _ in stepped_out],
        scratch_shapes=[pltpu.VMEM(s, kind) for s, kind in scratch],
        compiler_params=params(),
        cost_estimate=pl.CostEstimate(
            flops=20 * 10**9, bytes_accessed=40 * 10**6, transcendentals=10**7
        ),
    )(*inputs, *stepped_in)


def shared_scratch(atoms):
    molecules, rows, tall = edge_sizes(atoms)
    batch = OFFSETS * rows
    blocks = block_list(molecules, rows)
    return {
        "weights": ((2 * LANES, 2 * LANES), BF16),
        "many": ((SPAN, rows, LANES), F32),
        "mask": ((rows, LANES), F32),
        "near": ((LANE_GROUPS, STEPS * blocks[0][1], WINDOW), jnp.int32),
        "near_last": ((LANE_GROUPS, STEPS * blocks[-1][1], WINDOW), jnp.int32),
        "row1": ((tall, LANES), BF16),
        "row2": ((tall, 2 * LANES), BF16),
        "row4": ((tall, 4 * LANES), BF16),
        "loose5": ((tall, 5 * LANES), F32),
        "loose2": ((tall, 2 * LANES), F32),
        "tall": ((STEPS, rows, LANES), F32),
        "low": ((STEPS, rows, LANES), BF16),
        "first": ((SPAN, rows, LANES), F32),
        "pre": ((batch, 2 * LANES), F32),
        "grad_pre": ((batch, 2 * LANES), BF16),
        "line": ((batch, LANES), F32),
        "line2": ((2, batch, LANES), BF16),
        "line3": ((3, batch, LANES), BF16),
        "line4": ((4, batch, LANES), BF16),
        "line1": ((batch, LANES), BF16),
        "wide2": ((2, batch, 2 * LANES), BF16),
        "wide2f": ((2, batch, 2 * LANES), F32),
    }


def offsets_in_block(neighbours, mask, first):
    lane = lax.broadcasted_iota(jnp.int32, neighbours.shape, 1)
    diff = neighbours - (first + lane)
    return jnp.where(diff < 0, diff + MOL, diff) * mask


def pieces(x):
    a = x.astype(BF16)
    rest = x - a.astype(F32)
    b = rest.astype(BF16)
    return a, b, (rest - b.astype(F32)).astype(BF16)


def edge_groups(features, vectors, cot_f, cot_v, neighbours, mask, positions, first):
    diff = offsets_in_block(neighbours[...], mask[...], first).astype(F32).astype(BF16)
    groups = [jnp.concatenate([features[...], cot_f[...], diff], axis=0)]
    for d in range(3):
        rows = [x.astype(F32) for x in pieces(positions[d : d + 1])]
        rows = jnp.concatenate(rows + [jnp.zeros((29, LANES), F32)], axis=0).astype(BF16)
        groups.append(jnp.concatenate([vectors[d], cot_v[d], rows], axis=0))
    return groups


def halo_kernel(atoms, scalars, *refs):
    row_first = scalars[2]
    lane = lax.broadcasted_iota(jnp.int32, (GROUP_ROWS, LANES), 1)
    for end, at, out in ((0, atoms - LANES, refs[14]), (1, 0, refs[15])):
        groups = edge_groups(*refs[7 * end : 7 * end + 7], row_first + at)
        total = None
        for g, group in enumerate(groups):
            by = (HALO * (g + 1) if end == 0 else HALO * g) % LANES
            moved = group.astype(F32)
            moved = pltpu.roll(moved, by, 1) if by else moved
            total = moved if total is None else jnp.where(lane >= HALO * g, moved, total)
        out[...] = total.astype(BF16)


def halo_call(atoms, scalars, arrays):
    specs = []
    for at in (atoms // LANES - 1, 0):
        for x in arrays:
            shape = x.shape[:-1] + (LANES,)
            index = (0,) * (x.ndim - 1) + (at,)
            specs.append(pl.BlockSpec(shape, lambda *_, index=index: index))
    out = jax.ShapeDtypeStruct((GROUP_ROWS, LANES), BF16)
    return pl.pallas_call(
        functools.partial(halo_kernel, atoms),
        grid=(1,),
        out_shape=[out, out],
        in_specs=[whole(pltpu.SMEM)] + specs,
        out_specs=[whole(), whole()],
        compiler_params=params(),
    )(scalars, *arrays, *arrays)


def column(row):
    return jnp.broadcast_to(row, (8, row.shape[1])).T[:, :1]


def normalised(f):
    mean = jnp.mean(f, axis=0, keepdims=True)
    centred = f - mean
    inv = lax.rsqrt(jnp.mean(centred * centred, axis=0, keepdims=True) + EPSILON)
    return centred * inv, mean, inv


def dense_block(gain_ref, bias_ref, w_query, w_key, w_value, w_vector, w_output, scratch):
    w_qk, w_v0, w_v12, w_vec_t, w_out = scratch
    gain, bias = column(gain_ref[...]), column(bias_ref[...])
    w_qk[:R] = w_query[...]
    w_qk[R:] = w_key[...]
    w_v0[:R] = w_value[0]
    w_v0[R:] = jnp.zeros((R, H), BF16)
    w_v12[:R] = w_value[1]
    w_v12[R:] = w_value[2]
    for p in range(3):
        w_vec_t[p * R : (p + 1) * R] = w_vector[p]
    w_out[...] = jnp.concatenate([w_output[p] for p in range(3)], axis=0).astype(F32).T.astype(BF16)

    def block(f, v, cf, cv, own_v, diff, pos):
        width = f.shape[1]
        normed, mean, inv = normalised(f)
        turned = (normed * gain + bias).T.astype(BF16)
        kinds = lax.broadcasted_iota(jnp.int32, (R, width), 0)
        kinds = jnp.where(kinds < 32, kinds, MOL + 32 - kinds).astype(F32)
        counts = jnp.zeros((R, width), F32)
        for s in range(diff.shape[0]):
            counts = counts + jnp.where(diff[s : s + 1] == kinds, 1.0, 0.0)
        none = jnp.zeros((R, width), F32)
        counts = jnp.concatenate([none, counts], axis=0).T
        low = lax.broadcasted_iota(jnp.int32, (width, LANES), 1) < R
        pairs = [None] * 10
        pairs[QK] = dot_nt(turned, w_qk[...])
        pairs[V0] = dot_nt(turned, w_v0[...])
        v12 = dot_nt(turned, w_v12[...]).astype(BF16).astype(F32)
        v11 = jnp.where(low, v12, pltpu.roll(v12, R, 1))
        pairs[V12] = v12
        pairs[VEC01] = jnp.concatenate([own_v[0], own_v[1]], axis=0).T
        pairs[VEC2] = jnp.concatenate([own_v[2], none], axis=0).T
        pairs[W01] = pairs[VEC01] * v11
        pairs[W2V2] = jnp.where(low, pairs[VEC2] * v11, v12)
        pairs[C01] = jnp.concatenate([cv[0], cv[1]], axis=0).T
        pairs[C2_COUNT] = jnp.concatenate([cv[2], none], axis=0).T + counts
        pairs[POS] = jnp.concatenate([pos, jnp.zeros((LANES - 9, width), F32)], axis=0).T
        vec_dot = grad_0 = 0.0
        for d in range(3):
            proj = dot(w_vec_t[...], v[d])
            vec_dot = vec_dot + proj[:R] * proj[R : 2 * R]
            grad_0 = grad_0 + cv[d] * proj[2 * R :]
        grad_out = jnp.concatenate([grad_0, cf * vec_dot, cf], axis=0).astype(BF16)
        part = dot(w_out[...], grad_out)
        return [x.astype(BF16) for x in pairs], part.astype(BF16), mean, inv

    return block


def dense_kernel(
    atoms,
    scalars, features, vectors, cot_f, cot_v, neighbours, mask, positions,
    gain_ref, bias_ref, w_query, w_key, w_value, w_vector, w_output,
    rows_ref, part_ref, stat_ref, *scratch,
):
    chan_first = pl.multiple_of(scalars[1], R)
    row_first = scalars[2]
    weights = (w_query, w_key, w_value, w_vector, w_output)
    block = dense_block(gain_ref, bias_ref, *weights, scratch)
    wide = 2 * LANES

    def step(b, _):
        at = pl.multiple_of(b * wide, wide)
        here = pl.ds(at, wide)
        own_v = [vectors[d, pl.ds(chan_first, R), here].astype(F32) for d in range(3)]
        diff = offsets_in_block(neighbours[:, here], mask[:, here], row_first + at)
        places = [p.astype(F32) for d in range(3) for p in pieces(positions[d : d + 1, here])]
        pairs, part, mean, inv = block(
            features[:, here].astype(F32),
            [vectors[d, :, here] for d in range(3)],
            cot_f[:, here].astype(F32),
            [cot_v[d, :, here].astype(F32) for d in range(3)],
            own_v,
            diff.astype(F32),
            jnp.concatenate(places, axis=0),
        )
        for n, pair in enumerate(pairs):
            rows_ref[here, n * LANES : (n + 1) * LANES] = pair
        part_ref[:, here] = part
        stat_ref[0:1, here] = mean
        stat_ref[1:2, here] = inv
        return 0

    lax.fori_loop(0, atoms // wide, step, 0)


def dense_halo_kernel(
    atoms,
    scalars, low_ref, high_ref, part_in, gain_ref, bias_ref,
    w_query, w_key, w_value, w_vector, w_output,
    rows_ref, part_ref, *scratch,
):
    chan_first = pl.multiple_of(scalars[1], R)
    weights = (w_query, w_key, w_value, w_vector, w_output)
    block = dense_block(gain_ref, bias_ref, *weights, scratch)
    lane = lax.broadcasted_iota(jnp.int32, (GROUP_ROWS, LANES), 1)
    packed_low, packed_high = low_ref[...].astype(F32), high_ref[...].astype(F32)
    groups = []
    for g in range(4):
        a = pltpu.roll(packed_low, (LANES - HALO * g) % LANES, 1) if g else packed_low
        by = (LANES + HALO - HALO * g) % LANES
        b = pltpu.roll(packed_high, by, 1) if by else packed_high
        both = jnp.where(lane < HALO, a, jnp.where(lane < 2 * HALO, b, 0.0))
        groups.append(both)
    own_v, pos = [], []
    for d in range(3):
        g = groups[1 + d]
        found = g[:R]
        for f in range(1, H // R):
            found = jnp.where(chan_first == f * R, g[f * R : (f + 1) * R], found)
        own_v.append(found)
        pos.append(g[320:323])
    pairs, part, _, _ = block(
        groups[0][:H],
        [groups[1 + d][:H].astype(BF16) for d in range(3)],
        groups[0][H : H + R],
        [groups[1 + d][H : H + R] for d in range(3)],
        own_v,
        groups[0][H + R :],
        jnp.concatenate(pos, axis=0),
    )
    for n, pair in enumerate(pairs):
        rows_ref[:, n * LANES : (n + 1) * LANES] = pair
    part_ref[:, :atoms] = part_in[...]
    part_ref[:, atoms:] = part


def both_diagonals(grad, f):
    at = f * LANES
    return 0.5 * (grad[:R, at : at + R] + grad[R:, at + R : at + LANES])


def filter_block(grad):
    both = jnp.concatenate([both_diagonals(grad, 0), both_diagonals(grad, 1)], axis=1)
    return jnp.concatenate([both[: R // 2], both[R // 2 :]], axis=1)


def layer_kernel(
    atoms,
    scalars, features, stat, vectors, cot_f, cot_v, gathered, grads_b, gain_ref, bias_ref,
    w_vector, w_output, grad_filters_b,
    feat_out, delta_ref, square_ref, send_ref, flat_ref,
    w_vec, w_vec_t, w_out_t,
):
    chan_first = pl.multiple_of(scalars[1], R)
    gain, bias = column(gain_ref[...]), column(bias_ref[...])
    for p in range(3):
        w_vec_t[p * R : (p + 1) * R] = w_vector[p]
        w_out_t[p * R : (p + 1) * R] = w_output[p]
    w_vec[...] = w_vec_t[...].astype(F32).T.astype(BF16)
    t_vec, t_out, t_b = [flat_ref.at[n * 3 * R : (n + 1) * 3 * R] for n in range(3)]
    flat_ref[...] = jnp.zeros(flat_ref.shape, F32)
    wide = 2 * LANES
    split = send_ref.shape[0]

    def step(b, _):
        at = pl.multiple_of(b * wide, wide)
        here = pl.ds(at, wide)
        all_sums = gathered[:, here]
        outputs = dot(w_out_t[...], all_sums)
        out_0, out_1, out_2 = outputs[:R], outputs[R : 2 * R], outputs[2 * R :]
        cf = cot_f[:, here].astype(F32)
        grad_dot = cf * out_1
        vec_dot = grad_0 = 0.0
        for d in range(3):
            proj = dot(w_vec_t[...], vectors[d, :, here])
            first, second, third = proj[:R], proj[R : 2 * R], proj[2 * R :]
            cv = cot_v[d, :, here].astype(F32)
            vec_dot = vec_dot + first * second
            grad_0 = grad_0 + cv * third
            delta_ref[d, :, here] = third * out_0
            grad_proj = jnp.concatenate(
                [grad_dot * second, grad_dot * first, cv * out_0], axis=0
            ).astype(BF16)
            part = dot(w_vec[...], grad_proj).astype(BF16)
            for f in range(split):
                send_ref[f, d * R : (d + 1) * R, here] = part[f * R : (f + 1) * R]
            t_vec[...] = t_vec[...] + dot_nt(grad_proj, vectors[d, :, here])
        delta = vec_dot * out_1 + out_2
        moved = features[pl.ds(chan_first, R), here].astype(F32) + delta
        feat_out[:, here] = moved.astype(BF16)
        grad_out = jnp.concatenate([grad_0, cf * vec_dot, cf], axis=0).astype(BF16)
        t_out[...] = t_out[...] + dot_nt(grad_out, all_sums)
        square_ref[0:1, here] = jnp.sum(moved * moved, axis=0, keepdims=True)
        square_ref[1:2, here] = jnp.sum(delta * delta, axis=0, keepdims=True)
        normed = (features[:, here].astype(F32) - stat[0:1, here]) * stat[1:2, here]
        normal = (normed * gain + bias).astype(BF16)
        t_b[...] = t_b[...] + dot_nt(grads_b[:, here], normal)
        return 0

    lax.fori_loop(0, atoms // wide, step, 0)
    flat_ref[9 * R :] = filter_block(grad_filters_b[...])


def normal_kernel(
    atoms,
    scalars, features, stat, vectors, delta_ref, square_ref, sums_ref,
    grads_b, grads_a, pos_a, mask, gain_ref, bias_ref,
    w_query, w_key, w_value, grad_filters_a,
    vec_out, send_ref, flat_ref,
    w_five, t_late,
):
    chan_first = pl.multiple_of(scalars[1], R)
    gain, bias = column(gain_ref[...]), column(bias_ref[...])
    five = [w_query[...], w_key[...]] + [w_value[p] for p in range(3)]
    w_five[...] = jnp.concatenate(five, axis=0).astype(F32).T.astype(BF16)
    t_late[...] = jnp.zeros(t_late.shape, F32)
    wide = 2 * LANES
    split = send_ref.shape[0]

    def step(b, _):
        at = pl.multiple_of(b * wide, wide)
        here = pl.ds(at, wide)
        real = mask[:, here].astype(F32)
        square_v = square_dv = 0.0
        for d in range(3):
            delta = delta_ref[d, :, here] + sums_ref[d, :, here]
            moved = vectors[d, pl.ds(chan_first, R), here].astype(F32) + delta
            vec_out[d, :, here] = moved.astype(BF16)
            square_v = square_v + moved * moved
            square_dv = square_dv + delta * delta
        normed = (features[:, here].astype(F32) - stat[0:1, here]) * stat[1:2, here]
        normal = (normed * gain + bias).astype(BF16)
        grads = jnp.concatenate([grads_b[:, here], grads_a[:, here]], axis=0)
        t_late[...] = t_late[...] + dot_nt(grads_a[:, here], normal)
        part = dot(w_five[...], grads)
        rounded = part.astype(BF16)
        for f in range(split):
            send_ref[f, :R, here] = rounded[f * R : (f + 1) * R]
        hat = part * gain
        tops = [
            jnp.sum(hat, axis=0, keepdims=True),
            jnp.sum(hat * normed, axis=0, keepdims=True),
        ]
        exact = [pos_a[d : d + 1, here] for d in range(3)]
        exact += [square_ref[n : n + 1, here] * real for n in range(2)]
        for x in (square_v, square_dv):
            exact.append(jnp.sum(x, axis=0, keepdims=True) * real)
        heads = [x.astype(BF16).astype(F32) for x in exact]
        tops = tops + heads + [x - y for x, y in zip(exact, heads)]
        tops = jnp.concatenate(tops, axis=0).astype(BF16)
        for f in range(split):
            send_ref[f, R:, here] = tops
        return 0

    lax.fori_loop(0, atoms // wide, step, 0)
    flat_ref[: 2 * R] = t_late[...].astype(BF16)
    flat_ref[2 * R :] = filter_block(grad_filters_a[...]).astype(BF16)


def final_kernel(
    atoms,
    scalars, got, got_vec, features, stat, gain_ref, cot_f, cot_v, back_ref, mask,
    grad_feat, grad_vec, grad_pos, small_ref,
):
    chan_first = pl.multiple_of(scalars[1], R)
    whole_gain = column(gain_ref[...])
    gain = whole_gain[:R]
    for f in range(1, H // R):
        gain = jnp.where(chan_first == f * R, whole_gain[f * R : (f + 1) * R], gain)

    def summed(ref, rows):
        total = ref[0, rows].astype(F32)
        for f in range(1, ref.shape[0]):
            total = total + ref[f, rows].astype(F32)
        return total

    tops = summed(got, slice(R, R + EXTRAS))
    grad_normal = summed(got, slice(0, R))
    inv = stat[1:2]
    normed = (features[pl.ds(chan_first, R), :].astype(F32) - stat[0:1]) * inv
    inner = grad_normal * gain - tops[0:1] * (1.0 / H) - normed * (tops[1:2] * (1.0 / H))
    grad_feat[...] = cot_f[...].astype(F32) + inv * inner
    for d in range(3):
        part = summed(got_vec, slice(d * R, (d + 1) * R))
        grad_vec[d] = cot_v[d].astype(F32) + part + back_ref[d]
    exact = tops[2:9] + tops[9:16]
    grad_pos[...] = exact[:3]
    ones = jnp.ones((8, atoms), BF16)
    gains = dot_nt(ones, (grad_normal * normed).astype(BF16))
    biases = dot_nt(ones, grad_normal.astype(BF16))
    totals = jnp.sum(exact[3:7], axis=1, keepdims=True)
    real = jnp.sum(mask[...].astype(F32), axis=1, keepdims=True)
    numbers = jnp.concatenate([totals, real, jnp.zeros((3, 1), F32)], axis=0)
    small = jnp.concatenate([gains, biases, jnp.broadcast_to(numbers, (8, LANES))], axis=1)
    high = small.astype(BF16)
    small_ref[:8] = high.astype(F32)
    small_ref[8:] = small - high.astype(F32)


def unpack_kernel(
    share,
    got,
    g_gain, g_bias, g_query, g_key, g_value, g_vector, g_output, g_key_f, g_value_f, rms_ref,
):
    every = [got[n].astype(F32) for n in range(got.shape[0])]
    small = 0.0
    for x in every:
        small = small + x[share:]
    total = small[:8] + small[8:]
    g_gain[...] = total[0:1, :R]
    g_bias[...] = total[0:1, R : 2 * R]
    numbers = total[:, LANES : LANES + 1]
    size = jnp.where(lax.broadcasted_iota(jnp.int32, (8, 1), 0) < 2, 1.0, 3.0) * H
    rms = jnp.sqrt(numbers / (numbers[4:5] * size) + 1e-06)
    rms_ref[...] = jnp.broadcast_to(rms, (8, LANES)).T[:1, :4]
    order = [(g, p) for g in (g_vector, g_output) for p in range(3)]
    order += [(g_query, None), (g_key, None), (g_value, 0), ((g_key_f, None), (g_value_f, 0))]
    order += [(g_value, 1), (g_value, 2), ((g_value_f, 1), (g_value_f, 2))]
    begins = [0]
    for g, _ in order:
        begins.append(begins[-1] + (R // 2 if isinstance(g, tuple) else R))
    for n, x in enumerate(every):
        for (g, p), low, high in zip(order, begins[:-1], begins[1:]):
            first, last = max(low, n * share), min(high, (n + 1) * share)
            if first >= last:
                continue
            value = x[first - n * share : last - n * share]
            rows = slice(first - low, last - low)
            if not isinstance(g, tuple):
                put(g, p, rows, value)
                continue
            for h in (0, 1):
                down = slice(rows.start + h * R // 2, rows.stop + h * R // 2)
                at = h * LANES
                put(g[0], g[1], down, value[:, at : at + R])
                put(p[0], p[1], down, value[:, at + R : at + 2 * R])


def put(ref, p, rows, value):
    if p is None:
        ref[rows] = value
    else:
        ref[p, rows] = value


def everywhere(x, axis):
    count = lax.axis_size(axis)
    return lax.all_to_all(jnp.broadcast_to(x[None], (count,) + x.shape), axis, 0, 0)


def per_device(
    features, vectors, positions, atom_mask, neighbours, ln_gain, ln_bias,
    w_query, w_key, w_value, w_vector, w_output, w_key_filter, w_value_filter,
    cot_features, cot_vectors,
):
    channels = w_query.shape[1]
    atoms = features.shape[1]
    count = lax.axis_size("atoms")
    split = lax.axis_size("feat")
    chan_first = lax.axis_index("feat") * channels
    row_first = lax.axis_index("atoms") * atoms
    start = HALO - lax.rem(row_first, MOL)
    scalars = jnp.stack([start, chan_first, row_first]).astype(jnp.int32)
    molecules, rows_each, tall = edge_sizes(atoms)
    w_query, w_key = w_query.T, w_key.T
    w_value, w_vector, w_output = [jnp.swapaxes(w, 1, 2) for w in (w_value, w_vector, w_output)]
    mask = atom_mask.reshape(1, atoms)
    gain, bias = ln_gain.reshape(1, H), ln_bias.reshape(1, H)

    ends = halo_call(
        atoms,
        scalars,
        (features, vectors, cot_features, cot_vectors, neighbours, mask, positions),
    )
    low = lax.ppermute(ends[0], "atoms", [(i, i + 1) for i in range(count - 1)])
    high = lax.ppermute(ends[1], "atoms", [(i + 1, i) for i in range(count - 1)])

    scratch = [
        pltpu.VMEM((LANES, H), BF16),
        pltpu.VMEM((LANES, H), BF16),
        pltpu.VMEM((LANES, H), BF16),
        pltpu.VMEM((3 * R, H), BF16),
        pltpu.VMEM((H, 3 * R), BF16),
    ]
    weights = (gain, bias, w_query, w_key, w_value, w_vector, w_output)
    inputs = (
        scalars, features, vectors, cot_features, cot_vectors, neighbours, mask, positions,
    ) + weights
    rows, part, stat = pl.pallas_call(
        functools.partial(dense_kernel, atoms),
        out_shape=[
            jax.ShapeDtypeStruct((atoms, 10 * LANES), BF16),
            jax.ShapeDtypeStruct((H, atoms), BF16),
            jax.ShapeDtypeStruct((8, atoms), F32),
        ],
        in_specs=[whole(pltpu.SMEM)] + [whole()] * (len(inputs) - 1),
        out_specs=[whole()] * 3,
        scratch_shapes=scratch,
        compiler_params=params(),
        cost_estimate=pl.CostEstimate(
            flops=6 * 10**9, bytes_accessed=20 * 10**6, transcendentals=10**4
        ),
    )(*inputs)
    inputs = (scalars, low, high, part) + weights
    rows_halo, part = pl.pallas_call(
        functools.partial(dense_halo_kernel, atoms),
        out_shape=[
            jax.ShapeDtypeStruct((LANES, 10 * LANES), BF16),
            jax.ShapeDtypeStruct((H, atoms + LANES), BF16),
        ],
        in_specs=[whole(pltpu.SMEM)] + [whole()] * (len(inputs) - 1),
        out_specs=[whole()] * 2,
        scratch_shapes=scratch,
        compiler_params=params(),
    )(*inputs)
    scalar_parts = lax.all_to_all(part.reshape(split, channels, atoms + LANES), "feat", 0, 0)

    kinds = shared_scratch(atoms)
    batch = OFFSETS * rows_each
    names = ["near", "near_last"] + ["tall"] * 3 + ["many", "tall", "row1", "row1"]
    radial, geo, geo_s, geo_v = edge_call(
        geometry_kernel,
        atoms,
        (scalars, rows, rows, rows_halo),
        (),
        [],
        [((SPAN, batch, 2 * LANES), BF16)]
        + [((SPAN, n, batch, LANES), BF16) for n in (3, 2, 4)],
        [kinds[name] for name in names],
        (C2_COUNT, POS),
    )
    names = ["weights", "weights", "near", "near_last", "row2", "loose2"]
    names += ["pre", "grad_pre", "line", "wide2", "wide2f", "line4", "line1"]
    names += ["mask", "line1"]
    names += ["low"] * 4 + ["low"] * 4 + ["first"] * 4
    scalar_sum, grads_b, grad_filters_b, pull = edge_call(
        scalar_kernel,
        atoms,
        (scalars, rows, rows_halo, w_key_filter, w_value_filter[0], scalar_parts),
        (radial, geo, geo_s),
        [
            ((R, atoms), BF16),
            ((3 * R, atoms), BF16),
            ((LANES, 2 * LANES), F32),
        ],
        [((SPAN, batch, LANES), BF16)],
        [kinds[name] for name in names],
    )
    gathered = lax.all_gather(scalar_sum, "feat", axis=0, tiled=True)

    inputs = (
        scalars, features, stat, vectors, cot_features, cot_vectors, gathered, grads_b,
        gain, bias, w_vector, w_output, grad_filters_b,
    )
    new_features, delta, squares, send_vec, flat_early = pl.pallas_call(
        functools.partial(layer_kernel, atoms),
        out_shape=[
            jax.ShapeDtypeStruct((R, atoms), BF16),
            jax.ShapeDtypeStruct((3, R, atoms), F32),
            jax.ShapeDtypeStruct((8, atoms), F32),
            jax.ShapeDtypeStruct((split, 3 * R, atoms), BF16),
            jax.ShapeDtypeStruct((EARLY, H), F32),
        ],
        in_specs=[whole(pltpu.SMEM)] + [whole()] * (len(inputs) - 1),
        out_specs=[whole()] * 5,
        scratch_shapes=[
            pltpu.VMEM((H, 3 * R), BF16),
            pltpu.VMEM((3 * R, H), BF16),
            pltpu.VMEM((3 * R, H), BF16),
        ],
        compiler_params=params(),
    )(*inputs)
    share = (EARLY + LATE) // count
    got_vec = lax.all_to_all(send_vec, "feat", 0, 0)

    names = ["weights", "near", "near_last", "row4", "loose5"]
    names += ["pre", "grad_pre", "line", "line3", "mask", "line1"]
    names += ["low"] * 7 + ["low"] * 10 + ["first"] * 10
    rows, _ = lax.optimization_barrier((rows, squares))
    sums, back, grads_a, pos_a, grad_filters_a = edge_call(
        vector_kernel,
        atoms,
        (scalars, rows, rows_halo, w_value_filter[1], w_value_filter[2]),
        (radial, geo, geo_v, pull),
        [
            ((3, R, atoms), F32),
            ((3, R, atoms), F32),
            ((2 * R, atoms), BF16),
            ((8, atoms), F32),
            ((LANES, 2 * LANES), F32),
        ],
        [],
        [kinds[name] for name in names],
    )

    delta, got_vec = lax.optimization_barrier((delta, got_vec))
    inputs = (
        scalars, features, stat, vectors, delta, squares, sums, grads_b, grads_a, pos_a,
        mask, gain, bias, w_query, w_key, w_value, grad_filters_a,
    )
    new_vectors, send, flat_late = pl.pallas_call(
        functools.partial(normal_kernel, atoms),
        out_shape=[
            jax.ShapeDtypeStruct((3, R, atoms), BF16),
            jax.ShapeDtypeStruct((split, R + EXTRAS, atoms), BF16),
            jax.ShapeDtypeStruct((LATE, H), BF16),
        ],
        in_specs=[whole(pltpu.SMEM)] + [whole()] * (len(inputs) - 1),
        out_specs=[whole()] * 3,
        scratch_shapes=[pltpu.VMEM((H, 5 * R), BF16), pltpu.VMEM((2 * R, H), F32)],
        compiler_params=params(),
    )(*inputs)
    got = lax.all_to_all(send, "feat", 0, 0)
    flat = jnp.concatenate([flat_early.astype(BF16), flat_late], axis=0)
    shares = lax.all_to_all(flat.reshape(count, share, H), "atoms", 0, 0)

    inputs = (
        scalars, got, got_vec, features, stat, gain, cot_features, cot_vectors, back, mask,
    )
    grad_features, grad_vectors, grad_positions, small = pl.pallas_call(
        functools.partial(final_kernel, atoms),
        out_shape=[
            jax.ShapeDtypeStruct((R, atoms), F32),
            jax.ShapeDtypeStruct((3, R, atoms), F32),
            jax.ShapeDtypeStruct((3, atoms), F32),
            jax.ShapeDtypeStruct((16, H), F32),
        ],
        in_specs=[whole(pltpu.SMEM)] + [whole()] * (len(inputs) - 1),
        out_specs=[whole()] * 4,
        compiler_params=params(),
    )(*inputs)
    mine = jnp.concatenate([jnp.sum(shares.astype(F32), axis=0), small], axis=0).astype(BF16)
    every = everywhere(mine, "atoms")
    shapes = [
        (1, R), (1, R), (R, H), (R, H), (3, R, H), (3, R, H), (3, R, H), (R, R), (3, R, R), (1, 4),
    ]
    grads = pl.pallas_call(
        functools.partial(unpack_kernel, share),
        out_shape=[jax.ShapeDtypeStruct(shape, F32) for shape in shapes],
        in_specs=[whole()],
        out_specs=[whole()] * len(shapes),
        compiler_params=params(),
    )(every)
    return (
        new_features,
        new_vectors,
        grad_features,
        grad_vectors,
        grad_positions,
        grads[0].reshape(R),
        grads[1].reshape(R),
        grads[2].T,
        grads[3].T,
        jnp.swapaxes(grads[4], 1, 2),
        jnp.swapaxes(grads[5], 1, 2),
        jnp.swapaxes(grads[6], 1, 2),
        grads[7],
        grads[8],
        grads[9].reshape(4),
    )


def solution(mesh):
    in_specs = (
        P(None, "atoms"),
        P(None, None, "atoms"),
        P(None, "atoms"),
        P("atoms"),
        P(None, "atoms"),
        P(),
        P(),
        P(None, "feat"),
        P(None, "feat"),
        P(None, None, "feat"),
        P(None, None, "feat"),
        P(None, None, "feat"),
        P(None, "feat"),
        P(None, None, "feat"),
        P("feat", "atoms"),
        P(None, "feat", "atoms"),
    )
    out_specs = (
        P("feat", "atoms"),
        P(None, "feat", "atoms"),
        P("feat", "atoms"),
        P(None, "feat", "atoms"),
        P(None, "atoms"),
        P("feat"),
        P("feat"),
        P(None, "feat"),
        P(None, "feat"),
        P(None, None, "feat"),
        P(None, None, "feat"),
        P(None, None, "feat"),
        P(None, "feat"),
        P(None, None, "feat"),
        P(),
    )
    return jax.shard_map(
        per_device, mesh=mesh, in_specs=in_specs, out_specs=out_specs, check_vma=False
    )
```

```python
import functools
import math

import jax
import jax.numpy as jnp
from jax import lax
from jax.experimental import pallas as pl
from jax.experimental.pallas import tpu as pltpu
from jax.sharding import PartitionSpec as P

H = 256
HEADS = 8
HEAD = H // HEADS
R = 64
MOL = 29
HALO = 32
CUTOFF = 5.0
EPSILON = 1e-05
F32 = jnp.float32
BF16 = jnp.bfloat16

LANE_GROUPS = 2
ROW_GROUPS = 3
SPAN = 5
OFFSETS = 14
STEPS = SPAN + OFFSETS
SUB = 16
LANES = 128

W01, W2V2, C01, C2_COUNT, POS, QK, V0, V12, VEC01, VEC2 = range(10)
GROUP_ROWS = 352
EARLY = 9 * R + R // 2
LATE = 2 * R + R // 2
EXTRAS = 16


BLOCK = 8
WINDOW = 256


def block_list(molecules, rows):
    full, rest = divmod(molecules, BLOCK)
    wide = ROW_GROUPS * BLOCK
    out = [(n * wide, wide, BLOCK) for n in range(full)]
    if rows > full * wide:
        out.append((full * wide, rows - full * wide, rest))
    return out


def row_parts(shape, axis, size):
    row = lax.broadcasted_iota(jnp.int32, shape, axis)
    group = jnp.zeros(shape, jnp.int32)
    for g in range(1, ROW_GROUPS):
        group = jnp.where(row >= g * size, g, group)
    return group, row - group * size, row < ROW_GROUPS * size


def set_distances(target, width, size):
    for r in range(LANE_GROUPS):

        def step(t, _, r=r):
            group, molecule, held = row_parts((width, WINDOW), 0, size)
            spot = t + SPAN * (LANE_GROUPS * group + r)
            spot = jnp.where(spot >= MOL, spot - MOL, spot)
            lane = lax.broadcasted_iota(jnp.int32, (width, WINDOW), 1)
            value = jnp.where(held, molecule * MOL + spot - lane, -(10**6))
            target[r, pl.ds(t * width, width), :] = value
            return 0

        lax.fori_loop(0, STEPS, step, 0)


def windows(blocks, distances, start, tall):
    for n, (first, width, size) in enumerate(blocks):
        atom = start + n * BLOCK * MOL
        base = jnp.minimum(atom // SUB * SUB, tall - WINDOW)
        base = pl.multiple_of(base, SUB)
        chosen = distances[0] if size == BLOCK else distances[1]
        ones = [jnp.where(chosen[r] == base - atom, 1.0, 0.0).astype(BF16) for r in (0, 1)]
        yield first, width, pl.ds(base, WINDOW), ones


def both_ways(given):
    top, bottom = [], []
    for n in range(given.shape[1] // LANES):
        x = given[:, n * LANES : (n + 1) * LANES].astype(F32)
        y = pltpu.roll(x, R, 1)
        low = lax.broadcasted_iota(jnp.int32, x.shape, 1) < R
        top += [jnp.where(low, x, 0.0), jnp.where(low, y, 0.0)]
        bottom += [jnp.where(low, 0.0, y), jnp.where(low, 0.0, x)]
    return jnp.concatenate(
        [jnp.concatenate(top, axis=1), jnp.concatenate(bottom, axis=1)], axis=0
    ).astype(BF16)


def spread(source, targets, blocks, distances, start, extra=None):
    waiting = None
    for first, width, here, ones in windows(blocks, distances, start, source.shape[0]):
        given = source[here, :]
        ones = jnp.concatenate(ones, axis=1)
        out = dot(ones, both_ways(given)).reshape(STEPS, width, 2 * given.shape[1])
        if extra is not None:
            extra(ones, here, first, width)
        if waiting is not None:
            first, out = waiting[0], jnp.concatenate([waiting[1], out], axis=1)
            waiting = None
        elif width % SUB:
            waiting = (first, out)
            continue
        for n, target in enumerate(targets):
            if target is not None:
                value = out[:, :, n * LANES : (n + 1) * LANES]
                target[:, first : first + out.shape[1]] = value.astype(target.dtype)


def position_spreader(source, targets):
    row = lax.broadcasted_iota(jnp.int32, (2 * LANES, 3 * LANES), 0)
    lane = lax.broadcasted_iota(jnp.int32, (2 * LANES, 3 * LANES), 1)
    axis = jnp.where(lane >= 2 * LANES, 2, jnp.where(lane >= LANES, 1, 0))
    part = jnp.where(row >= LANES, row - LANES, row)
    mine = (part >= 3 * axis) & (part < 3 * axis + 3)
    low = lane - axis * LANES < R
    wide = jnp.where(mine & (low == (row < LANES)), 1.0, 0.0).astype(BF16)

    def place(ones, here, first, width):
        given = source[here, :]
        found = [dot(ones[:, r * WINDOW : (r + 1) * WINDOW], given) for r in (0, 1)]
        total = dot(jnp.concatenate(found, axis=1).astype(BF16), wide)
        for d, target in enumerate(targets):
            value = total[:, d * LANES : (d + 1) * LANES]
            target[:, first : first + width] = value.reshape(STEPS, width, LANES)

    return place


def assemble(target, own_ref, halo_ref, lanes, shift=0):
    atoms, tall = own_ref.shape[0], target.shape[0]
    also = slice(lanes.start + shift, lanes.stop + shift)
    target[HALO : HALO + atoms] = own_ref[:, lanes]
    target[:HALO] = halo_ref[:HALO, also]
    end = 2 * HALO + atoms
    target[HALO + atoms : end] = halo_ref[HALO : 2 * HALO, also]
    target[end:] = jnp.zeros((tall - end, target.shape[1]), BF16)


def keep_own(radial, owned, target, rows):
    def step(k, _):
        here = pl.ds(pl.multiple_of(k * rows, SUB), rows)
        target[here, :] = radial[here, :LANES] * owned[...].astype(BF16)
        return 0

    lax.fori_loop(0, OFFSETS, step, 0)


def collect(sources, target, blocks, distances, start):
    target[...] = jnp.zeros(target.shape, F32)
    units = []
    for first, width, here, ones in windows(blocks, distances, start, target.shape[0]):
        units.append((first, width, here, ones))
    at = 0
    while at < len(units):
        group = units[at : at + 2] if units[at][0] % SUB == 0 and at + 1 < len(units) else None
        if group is None or (group[0][1] + group[1][1]) % SUB:
            group = units[at : at + 1]
        at += len(group)
        first = group[0][0]
        size = sum(g[1] for g in group)
        blocks_in = []
        for partner, carry in sources:
            value = partner[:, first : first + size].astype(F32)
            start_part = value[:SPAN] + carry[:, first : first + size]
            blocks_in.append(jnp.concatenate([start_part, value[SPAN:]], axis=0))
        for f, width, here, ones in group:
            parts = ([], [])
            for n in range(0, len(sources), 2):
                a = blocks_in[n][:, f - first : f - first + width].reshape(STEPS * width, LANES)
                b = blocks_in[n + 1][:, f - first : f - first + width]
                b = b.reshape(STEPS * width, LANES)
                low = lax.broadcasted_iota(jnp.int32, a.shape, 1) < R
                parts[0].append(jnp.where(low, a, pltpu.roll(b, R, 1)).astype(BF16))
                parts[1].append(jnp.where(low, pltpu.roll(a, R, 1), b).astype(BF16))
            total = 0.0
            for r in (0, 1):
                total = total + dot_tn(ones[r], jnp.concatenate(parts[r], axis=1))
            target[here, :] = target[here, :] + total


def row_masks(owned, start, blocks, atoms):
    for n, (at, width, size) in enumerate(blocks):
        _, molecule, _ = row_parts((width, LANES), 0, size)
        first = start - HALO + (n * BLOCK + molecule) * MOL
        owned[at : at + width] = jnp.where((first >= 0) & (first < atoms), 1.0, 0.0)


def set_picks(picks):
    row = lax.broadcasted_iota(jnp.int32, (LANES, LANES), 0)
    lane = lax.broadcasted_iota(jnp.int32, (LANES, LANES), 1)
    base = jnp.where(lane >= R, R, 0)
    for n in range(2 * OFFSETS):
        which = 1 + n if n < OFFSETS else 33 + n - OFFSETS
        block = jnp.where(row == base + which, 1.0, 0.0).astype(BF16)
        picks[:, n * LANES : (n + 1) * LANES] = block


def set_multiplicities(count, target, blocks, rows):
    lane = lax.broadcasted_iota(jnp.int32, (rows, LANES), 1)
    inner = jnp.where(lane >= R, lane - R, lane)
    last = []
    for _, width, size in blocks:
        last.append(row_parts((width, LANES), 0, size)[0])
    doubled = (jnp.concatenate(last, axis=0) == ROW_GROUPS - 1) & (lane >= R)
    for t in range(SPAN):
        value = jnp.where(inner < 32, count[t], 0.0)
        for k in range(1, OFFSETS + 1):
            value = jnp.where(inner == 32 + k, count[t + k], value)
        if t == SPAN - 1:
            value = jnp.where(doubled, 0.0, value)
        target[t] = value.astype(BF16)


def dot(a, b):
    return jnp.dot(a, b, preferred_element_type=F32)


def dot_tn(a, b):
    return lax.dot_general(a, b, (((0,), (0,)), ((), ())), preferred_element_type=F32)


def dot_nt(a, b):
    return lax.dot_general(a, b, (((1,), (1,)), ((), ())), preferred_element_type=F32)


COSINE = (0.9999999998, -0.04934802137, 0.000405870916, -1.335212003e-06, 2.349373138e-09, -2.43963243e-12)

GEO_SLOPE, GEO_INTO, GEO_FROM = 0, 1, 2
GEO_ENVELOPE, GEO_BEND = 0, 1
GEO_INVERSE, GEO_WAY = 0, 1


def geometry(pos, counts, t, rows, radial, geo, geo_s, geo_v):
    inv_space = (R - 1) / CUTOFF

    def step(k, _):
        for o, size in halves(rows):
            here = pl.ds(pl.multiple_of(k * rows + o, SUB), size)
            part = slice(o, o + size)
            off = [p[t, part] - p[t + 1 + k, part] for p in pos]
            into = counts[part, pl.ds(pl.multiple_of(k * LANES, LANES), LANES)]
            at = pl.multiple_of((OFFSETS + k) * LANES, LANES)
            out_of = counts[part, pl.ds(at, LANES)]
            lane = lax.broadcasted_iota(jnp.int32, (size, LANES), 1)
            base = jnp.where(lane >= R, R, 0)
            centre = (lane - base).astype(F32)
            square = off[0] * off[0] + off[1] * off[1] + off[2] * off[2]
            clamped = jnp.maximum(square, 0.01)
            inverse = lax.rsqrt(clamped)
            c = COSINE[-1]
            for term in COSINE[-2::-1]:
                c = c * clamped + term
            c = jnp.where(clamped < CUTOFF * CUTOFF, c, 0.0)
            envelope = c * c
            y = jnp.maximum(1.0 - envelope, 1e-30)
            bend = ((-math.pi / CUTOFF) * c) * (y * lax.rsqrt(y))
            u = (clamped * inverse) * inv_space - centre
            bump = jnp.exp(-0.5 * (u * u))
            value = bump * envelope
            high = value.astype(BF16)
            slope = bump * bend - inv_space * (u * value)
            radial[here, :LANES] = high
            radial[here, LANES:] = (value - high.astype(F32)).astype(BF16)
            geo[GEO_SLOPE, here, :] = slope.astype(BF16)
            geo_s[GEO_BEND, here, :] = bend.astype(BF16)
            geo_s[GEO_ENVELOPE, here, :] = envelope.astype(BF16)
            for d in range(3):
                geo_v[GEO_WAY + d, here, :] = (off[d] * inverse).astype(BF16)
            signed = jnp.where(square > 0.01, inverse, -inverse)
            geo_v[GEO_INVERSE, here, :] = signed.astype(BF16)
            geo[GEO_INTO, here, :] = into.astype(BF16)
            geo[GEO_FROM, here, :] = out_of.astype(BF16)
        return 0

    lax.fori_loop(0, OFFSETS, step, 0)


def halves(rows):
    tiles = rows // SUB
    first = (tiles + 1) // 2 * SUB
    return ((0, first), (first, rows - first))


def set_filters(weights_ref, filter_1, filter_2):
    weights_ref[...] = jnp.zeros(weights_ref.shape, BF16)
    for f, ref in enumerate((filter_1, filter_2)):
        half = ref[...] * jnp.asarray(0.5, BF16)
        for part in range(2):
            for g in range(LANE_GROUPS):
                down = part * LANES + g * R
                at = f * LANES + g * R
                weights_ref[down : down + R, at : at + R] = half


def gate(h):
    t = jnp.tanh(h)
    u = 1.0 + t
    f = h * u
    return f.astype(BF16), (u + f * (1.0 - t)).astype(BF16)


def carried(rows, t, totals, group, body):
    def outer(s, _):
        o = pl.multiple_of(s * SUB, SUB)
        block = pl.ds(o, SUB)
        ii = (t, block)
        sums = None
        for k in range(0, OFFSETS, group):
            loaded = []
            for n in range(k, k + group):
                here = pl.ds(o + n * rows, SUB)
                loaded.append(body(o, here, ii, (t + 1 + n, block), n))
            done = [f() for f in loaded]
            given = [one for one, _ in done]
            while len(given) > 1:
                left = given[len(given) // 2 * 2 :]
                pairs = zip(given[0::2], given[1::2])
                given = [[x + y for x, y in zip(a, b)] for a, b in pairs] + left
            total = [x.astype(F32) for x in given[0]]
            sums = total if sums is None else [x + y for x, y in zip(sums, total)]
            for _, stores in done:
                for ref, index, value in stores:
                    ref[index] = value
        for total, value in zip(totals, sums):
            total[ii] = value
        return 0

    lax.fori_loop(0, rows // SUB, outer, 0)


def geometry_kernel(
    molecules, rows, atoms,
    scalars, own_count, own_pos, halo_ref, radial_out, geo_out, geo_s_out, geo_v_out,
    near, near_last, px, py, pz, many, count, all_pos, all_count, picks, counts,
):
    t = pl.program_id(0)
    start = scalars[0]
    blocks = block_list(molecules, rows)
    distances = (near, near_last)

    @pl.when(t == 0)
    def _():
        set_distances(near, blocks[0][1], blocks[0][2])
        set_distances(near_last, blocks[-1][1], blocks[-1][2])
        assemble(all_pos, own_pos, halo_ref, slice(0, LANES), POS * LANES)
        assemble(all_count, own_count, halo_ref, slice(0, LANES), C2_COUNT * LANES)
        extra = position_spreader(all_pos, (px, py, pz))
        spread(all_count, (None, count), blocks, distances, start, extra)
        set_multiplicities(count, many, blocks, rows)
        set_picks(picks)

    counts[...] = dot(many[t], picks[...])
    outs = [ref.at[0] for ref in (radial_out, geo_out, geo_s_out, geo_v_out)]
    geometry((px, py, pz), counts, t, rows, *outs)


def vector_kernel(
    molecules, rows, atoms,
    scalars, own_ref, halo_ref, filter_1, filter_2, radial_in, geo_in, geo_v_in, pull_in,
    sums_ref, back_ref, grads_ref, pos_out, grad_w_ref,
    weights_ref, near, near_last, all_rows, loose, pre, grad_pre,
    grad_radial, grad_ways, owned, radial_own,
    w0, w1, w2, v2, c0, c1, c2,
    s0, s1, s2, a0, a1, a2, gv, gx, gy, gz,
    fs0, fs1, fs2, fa0, fa1, fa2, fgv, fgx, fgy, fgz,
):
    t = pl.program_id(0)
    start = scalars[0]
    own = slice(HALO, HALO + atoms)
    radial, geo, geo_v = radial_in.at[0], geo_in.at[0], geo_v_in.at[0]
    w, c, g_pos = (w0, w1, w2), (c0, c1, c2), (gx, gy, gz)
    sums, backs = (s0, s1, s2), (a0, a1, a2)
    blocks = block_list(molecules, rows)
    distances = (near, near_last)

    @pl.when(t == 0)
    def _():
        set_filters(weights_ref, filter_1, filter_2)
        row_masks(owned, start, blocks, atoms)
        set_distances(near, blocks[0][1], blocks[0][2])
        set_distances(near_last, blocks[-1][1], blocks[-1][2])
        assemble(all_rows, own_ref, halo_ref, slice(W01 * LANES, (C2_COUNT + 1) * LANES))
        spread(all_rows, (w0, w1, w2, v2, c0, c1, c2), blocks, distances, start)
        for total in (s0, s1, s2, a0, a1, a2, gv, gx, gy, gz):
            total[...] = jnp.zeros(total.shape, BF16)
        grad_w_ref[...] = jnp.zeros(grad_w_ref.shape, F32)

    pre[...] = dot(radial[...], weights_ref[...])
    keep_own(radial, owned, radial_own, rows)

    def channel(o, here, ii, jj, k):
        h1, h2 = pre[here, :LANES], pre[here, LANES:]
        ni, nj = geo[GEO_INTO, here, :], geo[GEO_FROM, here, :]
        v2i, v2j = v2[ii], v2[jj]
        ways = [geo_v[GEO_WAY + d, here, :] for d in range(3)]
        wi, wj = [w[d][ii] for d in range(3)], [w[d][jj] for d in range(3)]
        ci, cj = [c[d][ii] for d in range(3)], [c[d][jj] for d in range(3)]
        old_sums = [sums[d][jj] for d in range(3)]
        old_backs = [backs[d][jj] for d in range(3)]
        old_gv = gv[jj]

        def compute():
            f1, d1 = gate(h1)
            f2, d2 = gate(h2)
            f1i, f1j, f2i, f2j = f1 * ni, f1 * nj, f2 * ni, f2 * nj
            msg_i, msg_j = f2i * v2j, f2j * v2i
            stores, sum_i, back_i = [], [], []
            along_i = along_j = across_i = across_j = None
            for d in range(3):
                way = ways[d]
                sum_i.append(f1i * wj[d] + msg_i * way)
                stores.append((sums[d], jj, old_sums[d] + (f1j * wi[d] - msg_j * way)))
                stores.append((backs[d], jj, old_backs[d] + f1i * ci[d]))
                back_i.append(f1j * cj[d])
                grad = ci[d] * msg_i - cj[d] * msg_j
                stores.append((grad_ways, (d, here, slice(None)), grad))
                new = (ci[d] * way, cj[d] * way, ci[d] * wj[d], cj[d] * wi[d])
                if d == 0:
                    along_i, along_j, across_i, across_j = new
                else:
                    along_i, along_j = along_i + new[0], along_j + new[1]
                    across_i, across_j = across_i + new[2], across_j + new[3]
            stores.append((gv, jj, old_gv + f2i * along_i))
            g1 = ni * across_i + nj * across_j
            g2 = ni * along_i * v2j - nj * along_j * v2i
            stores.append((grad_pre, (here, slice(0, LANES)), g1 * d1))
            stores.append((grad_pre, (here, slice(LANES, None)), g2 * d2))
            return sum_i + back_i + [-(f2j * along_j)], stores

        return compute

    carried(rows, t, (fs0, fs1, fs2, fa0, fa1, fa2, fgv), 2, channel)
    grad_radial[...] = dot_nt(grad_pre[...], weights_ref[:LANES])
    grad_w_ref[...] = grad_w_ref[...] + dot_tn(radial_own[...], grad_pre[...])

    def turn(o, here, ii, jj, k):
        ways = [geo_v[GEO_WAY + d, here, :] for d in range(3)]
        grads = [grad_ways[d, here, :] for d in range(3)]
        grad, slope = grad_radial[here, :], geo[GEO_SLOPE, here, :]
        signed, more = geo_v[GEO_INVERSE, here, :], pull_in[0, here, :]
        old = [g[jj] for g in g_pos]

        def compute():
            inverse = jnp.abs(signed)
            turned = [g * inverse for g in grads]
            along = ways[0] * turned[0] + ways[1] * turned[1] + ways[2] * turned[2]
            pull = jnp.where(signed > 0, grad.astype(BF16) * slope + more - along, 0)
            out = [turned[d] + ways[d] * pull for d in range(3)]
            return out, [(g_pos[d], jj, old[d] - out[d]) for d in range(3)]

        return compute

    carried(rows, t, (fgx, fgy, fgz), 7, turn)

    @pl.when(t == SPAN - 1)
    def _():
        low = lax.broadcasted_iota(jnp.int32, (atoms, LANES), 1) < R
        totals = (s0, s1, s2, gv, a0, a1, a2, gx, gy, gz)
        firsts = (fs0, fs1, fs2, fgv, fa0, fa1, fa2, fgx, fgy, fgz)
        collect(tuple(zip(totals, firsts)), loose, blocks, distances, start)
        both = loose[own, :LANES].T
        sums_ref[0] = both[:R]
        sums_ref[1] = both[R:]
        both = loose[own, LANES : 2 * LANES].T
        sums_ref[2] = both[:R]
        grads_ref[R:] = both[R:].astype(BF16)

        def kept(n):
            return own_ref[:, n * LANES : (n + 1) * LANES].astype(F32)

        v12 = kept(V12)
        v11 = jnp.where(low, v12, pltpu.roll(v12, R, 1))
        back = loose[own, 2 * LANES : 3 * LANES]
        both = (back * v11).T
        back_ref[0] = both[:R]
        back_ref[1] = both[R:]
        partial = back * kept(VEC01)
        partial = partial + pltpu.roll(partial, R, 1)
        back = loose[own, 3 * LANES : 4 * LANES]
        back_ref[2] = (back * v11).T[:R]
        partial = partial + back * kept(VEC2)
        grads_ref[:R] = partial.T[:R].astype(BF16)
        pos_out[...] = jnp.zeros(pos_out.shape, F32)
        pos_out[0:1] = jnp.sum(back.T[R:], axis=0, keepdims=True)
        both = loose[own, 4 * LANES :].T
        pos_out[1:2] = jnp.sum(both[:R], axis=0, keepdims=True)
        pos_out[2:3] = jnp.sum(both[R:], axis=0, keepdims=True)


def scalar_kernel(
    molecules, rows, atoms,
    scalars, own_ref, halo_ref, filter_1, filter_2, scalar_parts, radial_in, geo_in, geo_s_in,
    sum_ref, grads_ref, grad_w_ref, pull_out,
    weights_ref, heads_ref, near, near_last, all_rows, loose, pre,
    grad_pre, grad_radial, products, sums, gates, bends, owned, radial_own,
    q, key, v0, gs,
    ss, gq, gk, g0,
    fss, fgq, fgk, fg0,
):
    t = pl.program_id(0)
    start = scalars[0]
    own = slice(HALO, HALO + atoms)
    radial, geo, geo_s = radial_in.at[0], geo_in.at[0], geo_s_in.at[0]
    blocks = block_list(molecules, rows)
    distances = (near, near_last)

    @pl.when(t == 0)
    def _():
        set_filters(weights_ref, filter_1, filter_2)
        row = lax.broadcasted_iota(jnp.int32, (2 * LANES, 2 * LANES), 0)
        lane = lax.broadcasted_iota(jnp.int32, (2 * LANES, 2 * LANES), 1)
        heads_ref[...] = jnp.where(row // HEAD == lane // HEAD, 1.0, 0.0).astype(BF16)
        row_masks(owned, start, blocks, atoms)
        set_distances(near, blocks[0][1], blocks[0][2])
        set_distances(near_last, blocks[-1][1], blocks[-1][2])
        assemble(all_rows, own_ref, halo_ref, slice(QK * LANES, (V0 + 1) * LANES))
        summed = scalar_parts[0].astype(F32)
        for f in range(1, scalar_parts.shape[0]):
            summed = summed + scalar_parts[f].astype(F32)
        summed = jnp.concatenate([jnp.zeros_like(summed), summed], axis=0).T
        here = slice(LANES, 2 * LANES)
        for low, high, at in (
            (HALO, HALO + atoms, 0),
            (0, HALO, atoms),
            (HALO + atoms, 2 * HALO + atoms, atoms + HALO),
        ):
            both = all_rows[low:high, here].astype(F32) + summed[at : at + high - low]
            all_rows[low:high, here] = both.astype(BF16)
        spread(all_rows, (q, key, v0, gs), blocks, distances, start)
        for total in (ss, gq, gk, g0):
            total[...] = jnp.zeros(total.shape, BF16)
        grad_w_ref[...] = jnp.zeros(grad_w_ref.shape, F32)

    pre[...] = dot(radial[...], weights_ref[...])
    keep_own(radial, owned, radial_own, rows)

    def multiply(k, _):
        for o, size in halves(rows):
            here = pl.ds(pl.multiple_of(k * rows + o, SUB), size)
            ii, jj = (t, slice(o, o + size)), (t + 1 + k, slice(o, o + size))
            fk, dk = gate(pre[here, :LANES])
            f0, d0 = gate(pre[here, LANES:])
            k_ij, k_ji = q[ii] * key[jj] * fk, q[jj] * key[ii] * fk
            s_ij, s_ji = gs[ii] * v0[jj] * f0, gs[jj] * v0[ii] * f0
            gates[0, here, :] = fk
            gates[1, here, :] = f0
            gates[2, here, :] = dk
            gates[3, here, :] = d0
            products[0, here, :LANES] = k_ij
            products[0, here, LANES:] = k_ji
            products[1, here, :LANES] = s_ij
            products[1, here, LANES:] = s_ji
        return 0

    lax.fori_loop(0, OFFSETS, multiply, 0)
    sums[0] = dot(products[0], heads_ref[...])
    sums[1] = dot(products[1], heads_ref[...])

    def channel(o, here, ii, jj, k):
        fk, f0, dk, d0 = [gates[n, here, :] for n in range(4)]
        envelope, bend = geo_s[GEO_ENVELOPE, here, :], geo_s[GEO_BEND, here, :]
        side_in = []
        for side in range(2):
            lanes = slice(side * LANES, (side + 1) * LANES)
            m = geo[GEO_INTO + side, here, :]
            h, o_ = (ii, jj) if side == 0 else (jj, ii)
            side_in.append(
                (m, sums[0, here, lanes], sums[1, here, lanes])
                + (q[h], key[o_], gs[h], v0[o_])
            )
        old = [ref[jj] for ref in (g0, gk, ss, gq)]

        def compute():
            gives, news = [], []
            for m, score, g_att, qh, kt, gh, vt in side_in:
                act, rise = gate(0.5 * score)
                g_att = g_att.astype(BF16)
                weight = m * envelope
                att = act * weight
                g_score = g_att * (0.5 * rise) * weight
                lift = m * (g_att * act)
                bv, dv = f0 * att, fk * g_score
                gives.append((vt * bv, kt * dv, gh * bv, qh * dv))
                news.append((qh * kt * g_score, gh * vt * att, lift))
            one, two = gives
            new = [x + y for x, y in zip(*news)]
            stores = [
                (ref, jj, x + y)
                for ref, x, y in zip((g0, gk, ss, gq), old, (one[2], one[3], two[0], two[1]))
            ]
            stores.append((grad_pre, (here, slice(0, LANES)), new[0] * dk))
            stores.append((grad_pre, (here, slice(LANES, None)), new[1] * d0))
            stores.append((bends, (here, slice(None)), new[2] * bend * (1.0 / HEAD)))
            return [one[0], one[1], two[2], two[3]], stores

        return compute

    carried(rows, t, (fss, fgq, fg0, fgk), 2, channel)
    grad_radial[...] = dot_nt(grad_pre[...], weights_ref[:LANES])
    grad_w_ref[...] = grad_w_ref[...] + dot_tn(radial_own[...], grad_pre[...])

    def pull(k, _):
        here = pl.ds(pl.multiple_of(k * rows, SUB), rows)
        grad = grad_radial[here, :].astype(BF16)
        pull_out[0, here, :] = grad * geo[GEO_SLOPE, here, :] + bends[here, :]
        return 0

    lax.fori_loop(0, OFFSETS, pull, 0)

    @pl.when(t == SPAN - 1)
    def _():
        totals = (ss, g0, gq, gk)
        firsts = (fss, fg0, fgq, fgk)
        collect(tuple(zip(totals, firsts)), loose, blocks, distances, start)
        both = loose[own, :LANES].T
        sum_ref[...] = both[:R].astype(BF16)
        grads_ref[2 * R :] = both[R:].astype(BF16)
        grads_ref[: 2 * R] = loose[own, LANES : 2 * LANES].T.astype(BF16)


def whole(memory=pltpu.VMEM):
    return pl.BlockSpec(memory_space=memory)


def params(mib=60):
    return pltpu.CompilerParams(vmem_limit_bytes=mib * 1024 * 1024)


def edge_sizes(atoms):
    molecules = (atoms + 2 * (MOL - 1)) // MOL
    full, rest = divmod(molecules, BLOCK)
    rows = full * ROW_GROUPS * BLOCK + -(-ROW_GROUPS * rest // BLOCK) * BLOCK
    rows = -(-rows // SUB) * SUB
    tall = -(-(HALO + molecules * MOL) // SUB) * SUB
    return molecules, rows, tall


def by_step(shape):
    zeros = (0,) * (len(shape) - 1)
    return pl.BlockSpec((1,) + shape[1:], lambda t: (t,) + zeros)


def fixed(shape):
    zeros = (0,) * len(shape)
    return pl.BlockSpec(shape, lambda t: zeros)


def edge_call(kernel, atoms, inputs, stepped_in, outs, stepped_out, scratch, columns=()):
    molecules, rows, _ = edge_sizes(atoms)
    return pl.pallas_call(
        functools.partial(kernel, molecules, rows, atoms),
        grid=(SPAN,),
        out_shape=[jax.ShapeDtypeStruct(s, kind) for s, kind in outs + stepped_out],
        in_specs=[whole(pltpu.SMEM)]
        + [pl.BlockSpec((atoms, LANES), lambda t, n=n: (0, n)) for n in columns]
        + [fixed(x.shape) for x in inputs[1 + len(columns) :]]
        + [by_step(x.shape) for x in stepped_in],
        out_specs=[fixed(s) for s, _ in outs] + [by_step(s) for s, _ in stepped_out],
        scratch_shapes=[pltpu.VMEM(s, kind) for s, kind in scratch],
        compiler_params=params(),
        cost_estimate=pl.CostEstimate(
            flops=20 * 10**9, bytes_accessed=40 * 10**6, transcendentals=10**7
        ),
    )(*inputs, *stepped_in)


def shared_scratch(atoms):
    molecules, rows, tall = edge_sizes(atoms)
    batch = OFFSETS * rows
    blocks = block_list(molecules, rows)
    return {
        "weights": ((2 * LANES, 2 * LANES), BF16),
        "many": ((SPAN, rows, LANES), BF16),
        "picks": ((LANES, 2 * OFFSETS * LANES), BF16),
        "counts": ((rows, 2 * OFFSETS * LANES), F32),
        "mask": ((rows, LANES), F32),
        "near": ((LANE_GROUPS, STEPS * blocks[0][1], WINDOW), jnp.int32),
        "near_last": ((LANE_GROUPS, STEPS * blocks[-1][1], WINDOW), jnp.int32),
        "row1": ((tall, LANES), BF16),
        "row2": ((tall, 2 * LANES), BF16),
        "row4": ((tall, 4 * LANES), BF16),
        "loose5": ((tall, 5 * LANES), F32),
        "loose2": ((tall, 2 * LANES), F32),
        "tall": ((STEPS, rows, LANES), F32),
        "low": ((STEPS, rows, LANES), BF16),
        "first": ((SPAN, rows, LANES), F32),
        "pre": ((batch, 2 * LANES), F32),
        "grad_pre": ((batch, 2 * LANES), BF16),
        "line": ((batch, LANES), F32),
        "line2": ((2, batch, LANES), BF16),
        "line3": ((3, batch, LANES), BF16),
        "line4": ((4, batch, LANES), BF16),
        "line1": ((batch, LANES), BF16),
        "wide2": ((2, batch, 2 * LANES), BF16),
        "wide2f": ((2, batch, 2 * LANES), F32),
    }


def offsets_in_block(neighbours, mask, first):
    lane = lax.broadcasted_iota(jnp.int32, neighbours.shape, 1)
    diff = neighbours - (first + lane)
    return jnp.where(diff < 0, diff + MOL, diff) * mask


def pieces(x):
    a = x.astype(BF16)
    rest = x - a.astype(F32)
    b = rest.astype(BF16)
    return a, b, (rest - b.astype(F32)).astype(BF16)


def edge_groups(features, vectors, cot_f, cot_v, neighbours, mask, positions, first):
    diff = offsets_in_block(neighbours[...], mask[...], first).astype(F32).astype(BF16)
    groups = [jnp.concatenate([features[...], cot_f[...], diff], axis=0)]
    for d in range(3):
        rows = [x.astype(F32) for x in pieces(positions[d : d + 1])]
        rows = jnp.concatenate(rows + [jnp.zeros((29, LANES), F32)], axis=0).astype(BF16)
        groups.append(jnp.concatenate([vectors[d], cot_v[d], rows], axis=0))
    return groups


def halo_kernel(atoms, scalars, *refs):
    row_first = scalars[2]
    lane = lax.broadcasted_iota(jnp.int32, (GROUP_ROWS, LANES), 1)
    for end, at, out in ((0, atoms - LANES, refs[14]), (1, 0, refs[15])):
        groups = edge_groups(*refs[7 * end : 7 * end + 7], row_first + at)
        total = None
        for g, group in enumerate(groups):
            by = (HALO * (g + 1) if end == 0 else HALO * g) % LANES
            moved = group.astype(F32)
            moved = pltpu.roll(moved, by, 1) if by else moved
            total = moved if total is None else jnp.where(lane >= HALO * g, moved, total)
        out[...] = total.astype(BF16)


def halo_call(atoms, scalars, arrays):
    specs = []
    for at in (atoms // LANES - 1, 0):
        for x in arrays:
            shape = x.shape[:-1] + (LANES,)
            index = (0,) * (x.ndim - 1) + (at,)
            specs.append(pl.BlockSpec(shape, lambda *_, index=index: index))
    out = jax.ShapeDtypeStruct((GROUP_ROWS, LANES), BF16)
    return pl.pallas_call(
        functools.partial(halo_kernel, atoms),
        grid=(1,),
        out_shape=[out, out],
        in_specs=[whole(pltpu.SMEM)] + specs,
        out_specs=[whole(), whole()],
        compiler_params=params(),
    )(scalars, *arrays, *arrays)


def column(row):
    return jnp.broadcast_to(row, (8, row.shape[1])).T[:, :1]


def normalised(f):
    mean = jnp.mean(f, axis=0, keepdims=True)
    centred = f - mean
    inv = lax.rsqrt(jnp.mean(centred * centred, axis=0, keepdims=True) + EPSILON)
    return centred * inv, mean, inv


def dense_block(gain_ref, bias_ref, w_query, w_key, w_value, w_vector, w_output, scratch):
    w_qk, w_v0, w_v12, w_vec_t, w_out = scratch
    gain, bias = column(gain_ref[...]), column(bias_ref[...])
    w_qk[:R] = w_query[...]
    w_qk[R:] = w_key[...]
    w_v0[:R] = w_value[0]
    w_v0[R:] = jnp.zeros((R, H), BF16)
    w_v12[:R] = w_value[1]
    w_v12[R:] = w_value[2]
    for p in range(3):
        w_vec_t[p * R : (p + 1) * R] = w_vector[p]
    w_out[...] = jnp.concatenate([w_output[p] for p in range(3)], axis=0).astype(F32).T.astype(BF16)

    def block(f, v, cf, cv, own_v, diff, pos):
        width = f.shape[1]
        normed, mean, inv = normalised(f)
        turned = (normed * gain + bias).T.astype(BF16)
        kinds = lax.broadcasted_iota(jnp.int32, (R, width), 0)
        kinds = jnp.where(kinds < 32, kinds, MOL + 32 - kinds).astype(F32)
        counts = jnp.zeros((R, width), F32)
        for s in range(diff.shape[0]):
            counts = counts + jnp.where(diff[s : s + 1] == kinds, 1.0, 0.0)
        none = jnp.zeros((R, width), F32)
        counts = jnp.concatenate([none, counts], axis=0).T
        low = lax.broadcasted_iota(jnp.int32, (width, LANES), 1) < R
        pairs = [None] * 10
        pairs[QK] = dot_nt(turned, w_qk[...])
        pairs[V0] = dot_nt(turned, w_v0[...])
        v12 = dot_nt(turned, w_v12[...]).astype(BF16).astype(F32)
        v11 = jnp.where(low, v12, pltpu.roll(v12, R, 1))
        pairs[V12] = v12
        pairs[VEC01] = jnp.concatenate([own_v[0], own_v[1]], axis=0).T
        pairs[VEC2] = jnp.concatenate([own_v[2], none], axis=0).T
        pairs[W01] = pairs[VEC01] * v11
        pairs[W2V2] = jnp.where(low, pairs[VEC2] * v11, v12)
        pairs[C01] = jnp.concatenate([cv[0], cv[1]], axis=0).T
        pairs[C2_COUNT] = jnp.concatenate([cv[2], none], axis=0).T + counts
        pairs[POS] = jnp.concatenate([pos, jnp.zeros((LANES - 9, width), F32)], axis=0).T
        vec_dot = grad_0 = 0.0
        for d in range(3):
            proj = dot(w_vec_t[...], v[d])
            vec_dot = vec_dot + proj[:R] * proj[R : 2 * R]
            grad_0 = grad_0 + cv[d] * proj[2 * R :]
        grad_out = jnp.concatenate([grad_0, cf * vec_dot, cf], axis=0).astype(BF16)
        part = dot(w_out[...], grad_out)
        return [x.astype(BF16) for x in pairs], part.astype(BF16), mean, inv

    return block


def dense_kernel(
    atoms,
    scalars, features, vectors, cot_f, cot_v, neighbours, mask, positions,
    gain_ref, bias_ref, w_query, w_key, w_value, w_vector, w_output,
    rows_ref, part_ref, stat_ref, *scratch,
):
    chan_first = pl.multiple_of(scalars[1], R)
    row_first = scalars[2]
    weights = (w_query, w_key, w_value, w_vector, w_output)
    block = dense_block(gain_ref, bias_ref, *weights, scratch)
    wide = 2 * LANES

    def step(b, _):
        at = pl.multiple_of(b * wide, wide)
        here = pl.ds(at, wide)
        own_v = [vectors[d, pl.ds(chan_first, R), here].astype(F32) for d in range(3)]
        diff = offsets_in_block(neighbours[:, here], mask[:, here], row_first + at)
        places = [p.astype(F32) for d in range(3) for p in pieces(positions[d : d + 1, here])]
        pairs, part, mean, inv = block(
            features[:, here].astype(F32),
            [vectors[d, :, here] for d in range(3)],
            cot_f[:, here].astype(F32),
            [cot_v[d, :, here].astype(F32) for d in range(3)],
            own_v,
            diff.astype(F32),
            jnp.concatenate(places, axis=0),
        )
        for n, pair in enumerate(pairs):
            rows_ref[here, n * LANES : (n + 1) * LANES] = pair
        part_ref[:, here] = part
        stat_ref[0:1, here] = mean
        stat_ref[1:2, here] = inv
        return 0

    lax.fori_loop(0, atoms // wide, step, 0)


def dense_halo_kernel(
    atoms,
    scalars, low_ref, high_ref, part_in, gain_ref, bias_ref,
    w_query, w_key, w_value, w_vector, w_output,
    rows_ref, part_ref, *scratch,
):
    chan_first = pl.multiple_of(scalars[1], R)
    weights = (w_query, w_key, w_value, w_vector, w_output)
    block = dense_block(gain_ref, bias_ref, *weights, scratch)
    lane = lax.broadcasted_iota(jnp.int32, (GROUP_ROWS, LANES), 1)
    packed_low, packed_high = low_ref[...].astype(F32), high_ref[...].astype(F32)
    groups = []
    for g in range(4):
        a = pltpu.roll(packed_low, (LANES - HALO * g) % LANES, 1) if g else packed_low
        by = (LANES + HALO - HALO * g) % LANES
        b = pltpu.roll(packed_high, by, 1) if by else packed_high
        both = jnp.where(lane < HALO, a, jnp.where(lane < 2 * HALO, b, 0.0))
        groups.append(both)
    own_v, pos = [], []
    for d in range(3):
        g = groups[1 + d]
        found = g[:R]
        for f in range(1, H // R):
            found = jnp.where(chan_first == f * R, g[f * R : (f + 1) * R], found)
        own_v.append(found)
        pos.append(g[320:323])
    pairs, part, _, _ = block(
        groups[0][:H],
        [groups[1 + d][:H].astype(BF16) for d in range(3)],
        groups[0][H : H + R],
        [groups[1 + d][H : H + R] for d in range(3)],
        own_v,
        groups[0][H + R :],
        jnp.concatenate(pos, axis=0),
    )
    for n, pair in enumerate(pairs):
        rows_ref[:, n * LANES : (n + 1) * LANES] = pair
    part_ref[:, :atoms] = part_in[...]
    part_ref[:, atoms:] = part


def both_diagonals(grad, f):
    at = f * LANES
    return 0.5 * (grad[:R, at : at + R] + grad[R:, at + R : at + LANES])


def filter_block(grad):
    both = jnp.concatenate([both_diagonals(grad, 0), both_diagonals(grad, 1)], axis=1)
    return jnp.concatenate([both[: R // 2], both[R // 2 :]], axis=1)


def layer_kernel(
    atoms,
    scalars, features, stat, vectors, cot_f, cot_v, gathered, grads_b, gain_ref, bias_ref,
    w_vector, w_output, grad_filters_b,
    feat_out, delta_ref, square_ref, send_ref, flat_ref,
    w_vec, w_vec_t, w_out_t,
):
    chan_first = pl.multiple_of(scalars[1], R)
    gain, bias = column(gain_ref[...]), column(bias_ref[...])
    for p in range(3):
        w_vec_t[p * R : (p + 1) * R] = w_vector[p]
        w_out_t[p * R : (p + 1) * R] = w_output[p]
    w_vec[...] = w_vec_t[...].astype(F32).T.astype(BF16)
    t_vec, t_out, t_b = [flat_ref.at[n * 3 * R : (n + 1) * 3 * R] for n in range(3)]
    flat_ref[...] = jnp.zeros(flat_ref.shape, F32)
    wide = 2 * LANES
    split = send_ref.shape[0]

    def step(b, _):
        at = pl.multiple_of(b * wide, wide)
        here = pl.ds(at, wide)
        all_sums = gathered[:, here]
        outputs = dot(w_out_t[...], all_sums)
        out_0, out_1, out_2 = outputs[:R], outputs[R : 2 * R], outputs[2 * R :]
        cf = cot_f[:, here].astype(F32)
        grad_dot = cf * out_1
        vec_dot = grad_0 = 0.0
        for d in range(3):
            proj = dot(w_vec_t[...], vectors[d, :, here])
            first, second, third = proj[:R], proj[R : 2 * R], proj[2 * R :]
            cv = cot_v[d, :, here].astype(F32)
            vec_dot = vec_dot + first * second
            grad_0 = grad_0 + cv * third
            delta_ref[d, :, here] = third * out_0
            grad_proj = jnp.concatenate(
                [grad_dot * second, grad_dot * first, cv * out_0], axis=0
            ).astype(BF16)
            part = dot(w_vec[...], grad_proj).astype(BF16)
            for f in range(split):
                send_ref[f, d * R : (d + 1) * R, here] = part[f * R : (f + 1) * R]
            t_vec[...] = t_vec[...] + dot_nt(grad_proj, vectors[d, :, here])
        delta = vec_dot * out_1 + out_2
        moved = features[pl.ds(chan_first, R), here].astype(F32) + delta
        feat_out[:, here] = moved.astype(BF16)
        grad_out = jnp.concatenate([grad_0, cf * vec_dot, cf], axis=0).astype(BF16)
        t_out[...] = t_out[...] + dot_nt(grad_out, all_sums)
        square_ref[0:1, here] = jnp.sum(moved * moved, axis=0, keepdims=True)
        square_ref[1:2, here] = jnp.sum(delta * delta, axis=0, keepdims=True)
        normed = (features[:, here].astype(F32) - stat[0:1, here]) * stat[1:2, here]
        normal = (normed * gain + bias).astype(BF16)
        t_b[...] = t_b[...] + dot_nt(grads_b[:, here], normal)
        return 0

    lax.fori_loop(0, atoms // wide, step, 0)
    flat_ref[9 * R :] = filter_block(grad_filters_b[...])


def normal_kernel(
    atoms,
    scalars, features, stat, vectors, delta_ref, square_ref, sums_ref,
    grads_b, grads_a, pos_a, mask, gain_ref, bias_ref,
    w_query, w_key, w_value, grad_filters_a,
    vec_out, send_ref, flat_ref,
    w_five, t_late,
):
    chan_first = pl.multiple_of(scalars[1], R)
    gain, bias = column(gain_ref[...]), column(bias_ref[...])
    five = [w_query[...], w_key[...]] + [w_value[p] for p in range(3)]
    w_five[...] = jnp.concatenate(five, axis=0).astype(F32).T.astype(BF16)
    t_late[...] = jnp.zeros(t_late.shape, F32)
    wide = 2 * LANES
    split = send_ref.shape[0]

    def step(b, _):
        at = pl.multiple_of(b * wide, wide)
        here = pl.ds(at, wide)
        real = mask[:, here].astype(F32)
        square_v = square_dv = 0.0
        for d in range(3):
            delta = delta_ref[d, :, here] + sums_ref[d, :, here]
            moved = vectors[d, pl.ds(chan_first, R), here].astype(F32) + delta
            vec_out[d, :, here] = moved.astype(BF16)
            square_v = square_v + moved * moved
            square_dv = square_dv + delta * delta
        normed = (features[:, here].astype(F32) - stat[0:1, here]) * stat[1:2, here]
        normal = (normed * gain + bias).astype(BF16)
        grads = jnp.concatenate([grads_b[:, here], grads_a[:, here]], axis=0)
        t_late[...] = t_late[...] + dot_nt(grads_a[:, here], normal)
        part = dot(w_five[...], grads)
        rounded = part.astype(BF16)
        for f in range(split):
            send_ref[f, :R, here] = rounded[f * R : (f + 1) * R]
        hat = part * gain
        tops = [
            jnp.sum(hat, axis=0, keepdims=True),
            jnp.sum(hat * normed, axis=0, keepdims=True),
        ]
        exact = [pos_a[d : d + 1, here] for d in range(3)]
        exact += [square_ref[n : n + 1, here] * real for n in range(2)]
        for x in (square_v, square_dv):
            exact.append(jnp.sum(x, axis=0, keepdims=True) * real)
        heads = [x.astype(BF16).astype(F32) for x in exact]
        tops = tops + heads + [x - y for x, y in zip(exact, heads)]
        tops = jnp.concatenate(tops, axis=0).astype(BF16)
        for f in range(split):
            send_ref[f, R:, here] = tops
        return 0

    lax.fori_loop(0, atoms // wide, step, 0)
    flat_ref[: 2 * R] = t_late[...].astype(BF16)
    flat_ref[2 * R :] = filter_block(grad_filters_a[...]).astype(BF16)


def final_kernel(
    atoms,
    scalars, got, got_vec, features, stat, gain_ref, cot_f, cot_v, back_ref, mask,
    grad_feat, grad_vec, grad_pos, small_ref,
):
    chan_first = pl.multiple_of(scalars[1], R)
    whole_gain = column(gain_ref[...])
    gain = whole_gain[:R]
    for f in range(1, H // R):
        gain = jnp.where(chan_first == f * R, whole_gain[f * R : (f + 1) * R], gain)

    def summed(ref, rows):
        total = ref[0, rows].astype(F32)
        for f in range(1, ref.shape[0]):
            total = total + ref[f, rows].astype(F32)
        return total

    tops = summed(got, slice(R, R + EXTRAS))
    grad_normal = summed(got, slice(0, R))
    inv = stat[1:2]
    normed = (features[pl.ds(chan_first, R), :].astype(F32) - stat[0:1]) * inv
    inner = grad_normal * gain - tops[0:1] * (1.0 / H) - normed * (tops[1:2] * (1.0 / H))
    grad_feat[...] = cot_f[...].astype(F32) + inv * inner
    for d in range(3):
        part = summed(got_vec, slice(d * R, (d + 1) * R))
        grad_vec[d] = cot_v[d].astype(F32) + part + back_ref[d]
    exact = tops[2:9] + tops[9:16]
    grad_pos[...] = exact[:3]
    ones = jnp.ones((8, atoms), BF16)
    gains = dot_nt(ones, (grad_normal * normed).astype(BF16))
    biases = dot_nt(ones, grad_normal.astype(BF16))
    totals = jnp.sum(exact[3:7], axis=1, keepdims=True)
    real = jnp.sum(mask[...].astype(F32), axis=1, keepdims=True)
    numbers = jnp.concatenate([totals, real, jnp.zeros((3, 1), F32)], axis=0)
    small = jnp.concatenate([gains, biases, jnp.broadcast_to(numbers, (8, LANES))], axis=1)
    high = small.astype(BF16)
    small_ref[:8] = high.astype(F32)
    small_ref[8:] = small - high.astype(F32)


def unpack_kernel(
    share,
    got,
    g_gain, g_bias, g_query, g_key, g_value, g_vector, g_output, g_key_f, g_value_f, rms_ref,
):
    every = [got[n].astype(F32) for n in range(got.shape[0])]
    small = 0.0
    for x in every:
        small = small + x[share:]
    total = small[:8] + small[8:]
    g_gain[...] = total[0:1, :R]
    g_bias[...] = total[0:1, R : 2 * R]
    numbers = total[:, LANES : LANES + 1]
    size = jnp.where(lax.broadcasted_iota(jnp.int32, (8, 1), 0) < 2, 1.0, 3.0) * H
    rms = jnp.sqrt(numbers / (numbers[4:5] * size) + 1e-06)
    rms_ref[...] = jnp.broadcast_to(rms, (8, LANES)).T[:1, :4]
    order = [(g, p) for g in (g_vector, g_output) for p in range(3)]
    order += [(g_query, None), (g_key, None), (g_value, 0), ((g_key_f, None), (g_value_f, 0))]
    order += [(g_value, 1), (g_value, 2), ((g_value_f, 1), (g_value_f, 2))]
    begins = [0]
    for g, _ in order:
        begins.append(begins[-1] + (R // 2 if isinstance(g, tuple) else R))
    for n, x in enumerate(every):
        for (g, p), low, high in zip(order, begins[:-1], begins[1:]):
            first, last = max(low, n * share), min(high, (n + 1) * share)
            if first >= last:
                continue
            value = x[first - n * share : last - n * share]
            rows = slice(first - low, last - low)
            if not isinstance(g, tuple):
                put(g, p, rows, value)
                continue
            for h in (0, 1):
                down = slice(rows.start + h * R // 2, rows.stop + h * R // 2)
                at = h * LANES
                put(g[0], g[1], down, value[:, at : at + R])
                put(p[0], p[1], down, value[:, at + R : at + 2 * R])


def put(ref, p, rows, value):
    if p is None:
        ref[rows] = value
    else:
        ref[p, rows] = value


def everywhere(x, axis):
    count = lax.axis_size(axis)
    return lax.all_to_all(jnp.broadcast_to(x[None], (count,) + x.shape), axis, 0, 0)


def per_device(
    features, vectors, positions, atom_mask, neighbours, ln_gain, ln_bias,
    w_query, w_key, w_value, w_vector, w_output, w_key_filter, w_value_filter,
    cot_features, cot_vectors,
):
    channels = w_query.shape[1]
    atoms = features.shape[1]
    count = lax.axis_size("atoms")
    split = lax.axis_size("feat")
    chan_first = lax.axis_index("feat") * channels
    row_first = lax.axis_index("atoms") * atoms
    start = HALO - lax.rem(row_first, MOL)
    scalars = jnp.stack([start, chan_first, row_first]).astype(jnp.int32)
    molecules, rows_each, tall = edge_sizes(atoms)
    w_query, w_key = w_query.T, w_key.T
    w_value, w_vector, w_output = [jnp.swapaxes(w, 1, 2) for w in (w_value, w_vector, w_output)]
    mask = atom_mask.reshape(1, atoms)
    gain, bias = ln_gain.reshape(1, H), ln_bias.reshape(1, H)

    ends = halo_call(
        atoms,
        scalars,
        (features, vectors, cot_features, cot_vectors, neighbours, mask, positions),
    )
    low = lax.ppermute(ends[0], "atoms", [(i, i + 1) for i in range(count - 1)])
    high = lax.ppermute(ends[1], "atoms", [(i + 1, i) for i in range(count - 1)])

    scratch = [
        pltpu.VMEM((LANES, H), BF16),
        pltpu.VMEM((LANES, H), BF16),
        pltpu.VMEM((LANES, H), BF16),
        pltpu.VMEM((3 * R, H), BF16),
        pltpu.VMEM((H, 3 * R), BF16),
    ]
    weights = (gain, bias, w_query, w_key, w_value, w_vector, w_output)
    inputs = (
        scalars, features, vectors, cot_features, cot_vectors, neighbours, mask, positions,
    ) + weights
    rows, part, stat = pl.pallas_call(
        functools.partial(dense_kernel, atoms),
        out_shape=[
            jax.ShapeDtypeStruct((atoms, 10 * LANES), BF16),
            jax.ShapeDtypeStruct((H, atoms), BF16),
            jax.ShapeDtypeStruct((8, atoms), F32),
        ],
        in_specs=[whole(pltpu.SMEM)] + [whole()] * (len(inputs) - 1),
        out_specs=[whole()] * 3,
        scratch_shapes=scratch,
        compiler_params=params(),
        cost_estimate=pl.CostEstimate(
            flops=6 * 10**9, bytes_accessed=20 * 10**6, transcendentals=10**4
        ),
    )(*inputs)
    inputs = (scalars, low, high, part) + weights
    rows_halo, part = pl.pallas_call(
        functools.partial(dense_halo_kernel, atoms),
        out_shape=[
            jax.ShapeDtypeStruct((LANES, 10 * LANES), BF16),
            jax.ShapeDtypeStruct((H, atoms + LANES), BF16),
        ],
        in_specs=[whole(pltpu.SMEM)] + [whole()] * (len(inputs) - 1),
        out_specs=[whole()] * 2,
        scratch_shapes=scratch,
        compiler_params=params(),
    )(*inputs)
    scalar_parts = lax.all_to_all(part.reshape(split, channels, atoms + LANES), "feat", 0, 0)

    kinds = shared_scratch(atoms)
    batch = OFFSETS * rows_each
    names = ["near", "near_last"] + ["tall"] * 3 + ["many", "tall", "row1", "row1"]
    names += ["picks", "counts"]
    radial, geo, geo_s, geo_v = edge_call(
        geometry_kernel,
        atoms,
        (scalars, rows, rows, rows_halo),
        (),
        [],
        [((SPAN, batch, 2 * LANES), BF16)]
        + [((SPAN, n, batch, LANES), BF16) for n in (3, 2, 4)],
        [kinds[name] for name in names],
        (C2_COUNT, POS),
    )
    names = ["weights", "weights", "near", "near_last", "row2", "loose2"]
    names += ["pre", "grad_pre", "line", "wide2", "wide2f", "line4", "line1"]
    names += ["mask", "line1"]
    names += ["low"] * 4 + ["low"] * 4 + ["first"] * 4
    scalar_sum, grads_b, grad_filters_b, pull = edge_call(
        scalar_kernel,
        atoms,
        (scalars, rows, rows_halo, w_key_filter, w_value_filter[0], scalar_parts),
        (radial, geo, geo_s),
        [
            ((R, atoms), BF16),
            ((3 * R, atoms), BF16),
            ((LANES, 2 * LANES), F32),
        ],
        [((SPAN, batch, LANES), BF16)],
        [kinds[name] for name in names],
    )
    gathered = lax.all_gather(scalar_sum, "feat", axis=0, tiled=True)

    inputs = (
        scalars, features, stat, vectors, cot_features, cot_vectors, gathered, grads_b,
        gain, bias, w_vector, w_output, grad_filters_b,
    )
    new_features, delta, squares, send_vec, flat_early = pl.pallas_call(
        functools.partial(layer_kernel, atoms),
        out_shape=[
            jax.ShapeDtypeStruct((R, atoms), BF16),
            jax.ShapeDtypeStruct((3, R, atoms), F32),
            jax.ShapeDtypeStruct((8, atoms), F32),
            jax.ShapeDtypeStruct((split, 3 * R, atoms), BF16),
            jax.ShapeDtypeStruct((EARLY, H), F32),
        ],
        in_specs=[whole(pltpu.SMEM)] + [whole()] * (len(inputs) - 1),
        out_specs=[whole()] * 5,
        scratch_shapes=[
            pltpu.VMEM((H, 3 * R), BF16),
            pltpu.VMEM((3 * R, H), BF16),
            pltpu.VMEM((3 * R, H), BF16),
        ],
        compiler_params=params(),
    )(*inputs)
    share = (EARLY + LATE) // count
    got_vec = lax.all_to_all(send_vec, "feat", 0, 0)

    names = ["weights", "near", "near_last", "row4", "loose5"]
    names += ["pre", "grad_pre", "line", "line3", "mask", "line1"]
    names += ["low"] * 7 + ["low"] * 10 + ["first"] * 10
    rows, _ = lax.optimization_barrier((rows, squares))
    sums, back, grads_a, pos_a, grad_filters_a = edge_call(
        vector_kernel,
        atoms,
        (scalars, rows, rows_halo, w_value_filter[1], w_value_filter[2]),
        (radial, geo, geo_v, pull),
        [
            ((3, R, atoms), F32),
            ((3, R, atoms), F32),
            ((2 * R, atoms), BF16),
            ((8, atoms), F32),
            ((LANES, 2 * LANES), F32),
        ],
        [],
        [kinds[name] for name in names],
    )

    delta, got_vec = lax.optimization_barrier((delta, got_vec))
    inputs = (
        scalars, features, stat, vectors, delta, squares, sums, grads_b, grads_a, pos_a,
        mask, gain, bias, w_query, w_key, w_value, grad_filters_a,
    )
    new_vectors, send, flat_late = pl.pallas_call(
        functools.partial(normal_kernel, atoms),
        out_shape=[
            jax.ShapeDtypeStruct((3, R, atoms), BF16),
            jax.ShapeDtypeStruct((split, R + EXTRAS, atoms), BF16),
            jax.ShapeDtypeStruct((LATE, H), BF16),
        ],
        in_specs=[whole(pltpu.SMEM)] + [whole()] * (len(inputs) - 1),
        out_specs=[whole()] * 3,
        scratch_shapes=[pltpu.VMEM((H, 5 * R), BF16), pltpu.VMEM((2 * R, H), F32)],
        compiler_params=params(),
    )(*inputs)
    got = lax.all_to_all(send, "feat", 0, 0)
    flat = jnp.concatenate([flat_early.astype(BF16), flat_late], axis=0)
    shares = lax.all_to_all(flat.reshape(count, share, H), "atoms", 0, 0)

    inputs = (
        scalars, got, got_vec, features, stat, gain, cot_features, cot_vectors, back, mask,
    )
    grad_features, grad_vectors, grad_positions, small = pl.pallas_call(
        functools.partial(final_kernel, atoms),
        out_shape=[
            jax.ShapeDtypeStruct((R, atoms), F32),
            jax.ShapeDtypeStruct((3, R, atoms), F32),
            jax.ShapeDtypeStruct((3, atoms), F32),
            jax.ShapeDtypeStruct((16, H), F32),
        ],
        in_specs=[whole(pltpu.SMEM)] + [whole()] * (len(inputs) - 1),
        out_specs=[whole()] * 4,
        compiler_params=params(),
    )(*inputs)
    mine = jnp.concatenate([jnp.sum(shares.astype(F32), axis=0), small], axis=0).astype(BF16)
    every = everywhere(mine, "atoms")
    shapes = [
        (1, R), (1, R), (R, H), (R, H), (3, R, H), (3, R, H), (3, R, H), (R, R), (3, R, R), (1, 4),
    ]
    grads = pl.pallas_call(
        functools.partial(unpack_kernel, share),
        out_shape=[jax.ShapeDtypeStruct(shape, F32) for shape in shapes],
        in_specs=[whole()],
        out_specs=[whole()] * len(shapes),
        compiler_params=params(),
    )(every)
    return (
        new_features,
        new_vectors,
        grad_features,
        grad_vectors,
        grad_positions,
        grads[0].reshape(R),
        grads[1].reshape(R),
        grads[2].T,
        grads[3].T,
        jnp.swapaxes(grads[4], 1, 2),
        jnp.swapaxes(grads[5], 1, 2),
        jnp.swapaxes(grads[6], 1, 2),
        grads[7],
        grads[8],
        grads[9].reshape(4),
    )


def solution(mesh):
    in_specs = (
        P(None, "atoms"),
        P(None, None, "atoms"),
        P(None, "atoms"),
        P("atoms"),
        P(None, "atoms"),
        P(),
        P(),
        P(None, "feat"),
        P(None, "feat"),
        P(None, None, "feat"),
        P(None, None, "feat"),
        P(None, None, "feat"),
        P(None, "feat"),
        P(None, None, "feat"),
        P("feat", "atoms"),
        P(None, "feat", "atoms"),
    )
    out_specs = (
        P("feat", "atoms"),
        P(None, "feat", "atoms"),
        P("feat", "atoms"),
        P(None, "feat", "atoms"),
        P(None, "atoms"),
        P("feat"),
        P("feat"),
        P(None, "feat"),
        P(None, "feat"),
        P(None, None, "feat"),
        P(None, None, "feat"),
        P(None, None, "feat"),
        P(None, "feat"),
        P(None, None, "feat"),
        P(),
    )
    return jax.shard_map(
        per_device, mesh=mesh, in_specs=in_specs, out_specs=out_specs, check_vma=False
    )
```
